32 devices in a mesh: section: 2 (over x), dp: 16 (over z, y, core).
Axes of the slice: x: 2, y: 2, z: 4, core: 2. Of those that a mesh axis runs over, the one named last changes fastest.
Arguments:
- visible_tokens: float32 [32, 256, 768], P('dp'), may hold values from -100 to 100
- cotangent: float32 [32, 1024, 512], P('dp'), may hold values from -6 to 6
- chip_sizes: int32 [32, 4], P('dp'), may hold values from 0 to 1024, as said below
- ground_distance: int32 [32, 4], P('dp'), may hold values from 1 to 32
- visible_slots: int32 [32, 256], P('dp'), may hold values from -1 to 1023, as said below
- encoder_gains: float32 [2, 768], replicated, may hold values from 0.5 to 1.5
- encoder_shifts: float32 [2, 768], replicated, may hold values from -4 to 4
- encoder_biases: float32 [2, 768], replicated, may hold values from -4 to 4
- encoder_attend: bfloat16 [768, 2304], replicated, may hold values from -0.21875 to 0.21875
- encoder_merge: bfloat16 [768, 768], replicated, may hold values from -1.75 to 1.75
- encoder_expand: bfloat16 [768, 3072], replicated, may hold values from -0.21875 to 0.21875
- encoder_inner: float32 [3072], replicated, may hold values from -4 to 4
- encoder_shrink: bfloat16 [3072, 768], replicated, may hold values from -0.109375 to 0.109375
- decoder_entry: bfloat16 [768, 512], replicated, may hold values from -0.21875 to 0.21875
- decoder_biases: float32 [3, 512], replicated, may hold values from -4 to 4
- mask_token: float32 [512], replicated, may hold values from -5 to 5
- decoder_gains: float32 [2, 512], replicated, may hold values from 0.5 to 1.5
- decoder_shifts: float32 [2, 512], replicated, may hold values from -4 to 4
- decoder_attend: bfloat16 [512, 768], replicated, may hold values from -0.25 to 0.25
- decoder_merge: bfloat16 [256, 512], replicated, may hold values from -4 to 4
- decoder_widen_weight: bfloat16 [512, 2048], replicated, may hold values from -0.25 to 0.25
- decoder_inner: float32 [2048], replicated, may hold values from -4 to 4
- decoder_shrink: bfloat16 [2048, 512], replicated, may hold values from -0.125 to 0.125
Outputs:
- boundary_grads: float32 [2, 32, 256, 768], P('section', 'dp')
- statistics: float32 [8], replicated
- encoder_gains_grad: float32 [2, 768], P(None, ('section', 'dp'))
- encoder_shifts_grad: float32 [2, 768], P(None, ('section', 'dp'))
- encoder_biases_grad: float32 [2, 768], P(None, ('section', 'dp'))
- encoder_attend_grad: float32 [768, 2304], P(('section', 'dp'))
- encoder_merge_grad: float32 [768, 768], P(None, ('section', 'dp'))
- encoder_expand_grad: float32 [768, 3072], P(('section', 'dp'))
- encoder_inner_grad: float32 [3072], P(('section', 'dp'))
- encoder_shrink_grad: float32 [3072, 768], P(('section', 'dp'))
- decoder_entry_grad: float32 [768, 512], P(('section', 'dp'))
- decoder_biases_grad: float32 [3, 512], P(None, ('section', 'dp'))
- mask_token_grad: float32 [512], P(('section', 'dp'))
- decoder_gains_grad: float32 [2, 512], P(None, ('section', 'dp'))
- decoder_shifts_grad: float32 [2, 512], P(None, ('section', 'dp'))
- decoder_attend_grad: float32 [512, 768], P(('section', 'dp'))
- decoder_merge_grad: float32 [256, 512], P(None, ('section', 'dp'))
- decoder_expand_grad: float32 [512, 2048], P(('section', 'dp'))
- decoder_inner_grad: float32 [2048], P(('section', 'dp'))
- decoder_shrink_grad: float32 [2048, 512], P(('section', 'dp'))
The draws below stay inside these ranges and needn't reach their ends.
Inputs may be any that keep to these rules, and one draw needn't show every extreme that they name: `chip_sizes`: each pack's slots hold, in order, either one chip of 1024 patches or two to 4 chips of 256 patches, then zeros. The first pack holds one chip of 1024, the second 4 chips of 256. `visible_slots`: encoder slots follow the pack's chips in order: a chip of n patches owns n / 4 consecutive slots, each naming a different decoder slot of that chip; the slots after the last chip hold -1.
All inputs are finite; a program needn't handle non-finite values.
Results may differ from the reference program's by a relative error of at most 0.017.
Values may be sent and summed in bfloat16 or wider, within the bound.
A program may use at most 320 MiB of HBM per device.

```python
import jax
import jax.numpy as jnp
from jax import lax

DE = 768
HE = 12
HD = 64
FE = 3072
DD = 512
HDEC = 4
FD = 2048
SMALL_SIDE = 16
BIG_SIDE = 32
SMALL_CHIP = 256
DPACK = 1024
EPACK = 256
SLOTS = 4
PACKS = 32


def chip_plan(key):
    plan_key = jax.random.fold_in(key, 101)
    first_key, second_key = jax.random.split(plan_key)
    pack_index = jnp.arange(PACKS, dtype=jnp.int32)
    large_pick = jax.random.randint(first_key, (PACKS,), 0, 2).astype(jnp.int32)
    small_count = jax.random.randint(second_key, (PACKS,), 2, SLOTS + 1).astype(jnp.int32)
    large_pick = jnp.where(pack_index == 0, 1, jnp.where(pack_index == 1, 0, large_pick))
    small_count = jnp.where(pack_index == 1, SLOTS, small_count)
    slot_index = jnp.arange(SLOTS, dtype=jnp.int32)
    small_rows = jnp.where(slot_index[None, :] < small_count[:, None], SMALL_CHIP, 0)
    large_rows = jnp.where(slot_index[None, :] == 0, DPACK, 0)
    return jnp.where(large_pick[:, None] == 1, large_rows, small_rows).astype(jnp.int32)


def draw_chip_sizes(key, part):
    return chip_plan(key)


def draw_visible_slots(key, part):
    extents = chip_plan(key)
    key = jax.random.fold_in(key, 7)
    chip_ends = jnp.cumsum(extents, axis=1).astype(jnp.int32)
    chip_starts = chip_ends - extents
    places = jnp.arange(DPACK, dtype=jnp.int32)
    slot_chip = jnp.sum((places[None, :, None] >= chip_ends[:, None, :]).astype(jnp.int32), axis=2)
    ranks = jax.vmap(lambda single: jax.random.permutation(single, DPACK))(jax.random.split(key, PACKS)).astype(jnp.int32)
    order = jnp.argsort(slot_chip * DPACK + ranks, axis=1).astype(jnp.int32)
    token_places = 4 * jnp.arange(EPACK, dtype=jnp.int32)
    token_chip = jnp.sum((token_places[None, :, None] >= chip_ends[:, None, :]).astype(jnp.int32), axis=2)
    member = (token_chip[:, :, None] == jnp.arange(SLOTS, dtype=jnp.int32)[None, None, :]).astype(jnp.int32)
    first_slot = jnp.sum(member * chip_starts[:, None, :], axis=2)
    position = first_slot + jnp.arange(EPACK, dtype=jnp.int32)[None, :] - first_slot // 4
    position = jnp.clip(position, 0, DPACK - 1)
    picked = jnp.take_along_axis(order, position, axis=1)
    return jnp.where(token_chip < SLOTS, picked, -1).astype(jnp.int32)


def draw_visible_tokens(key, part):
    key = jax.random.fold_in(key, 3)
    base_key, row_key, col_key = jax.random.split(key, 3)
    shape = (PACKS, EPACK, DE)
    base = jnp.clip(jax.random.normal(base_key, shape, jnp.float32), -5.0, 5.0)
    ramp = 1.0 + 2.0 * jnp.arange(PACKS, dtype=jnp.float32) / (PACKS - 1)
    rows = jnp.exp(jax.random.uniform(row_key, (PACKS, EPACK, 1), jnp.float32, -0.8, 0.8))
    cols = jnp.exp(jax.random.uniform(col_key, (1, 1, DE), jnp.float32, -0.5, 0.5))
    return base * ramp[:, None, None] * rows * cols


def with_ends(entries, own_key, smallest, top_value):
    longest = entries.shape.index(max(entries.shape))
    spots = []
    for shift in (0, 1):
        where = [jax.random.randint(jax.random.fold_in(own_key, axis), (), 0, length) for axis, length in enumerate(entries.shape)]
        where[longest] = (where[longest] + shift) % entries.shape[longest]
        spots.append(tuple(where))
    return entries.at[spots[0]].set(smallest).at[spots[1]].set(top_value)


def shard_levels(rng, shape, cuts, smallest, high):
    gain, own = 1.0, jax.random.fold_in(rng, 6)
    for dim, blocks in cuts:
        steps = jnp.exp(jax.random.uniform(jax.random.fold_in(own, dim), (blocks,), jnp.float32, smallest / len(cuts), high / len(cuts)))
        gain = gain * jnp.repeat(steps, shape[dim] // blocks).reshape([-1 if axis == dim else 1 for axis in range(len(shape))])
    return gain


def centred(rng, dims, deviation, bound, cuts=(), held_as=jnp.bfloat16):
    loudness = shard_levels(rng, dims, cuts, -0.22, 0.18) if cuts else 1.0
    result = jax.random.normal(rng, dims, jnp.float32) * deviation * loudness
    return jnp.minimum(jnp.maximum(result, -bound), bound).astype(held_as)


def setup_inputs(seed: int = 0) -> dict:
    seeds = jax.random.split(jax.random.key(seed), 24)
    visible_tokens = draw_visible_tokens(jax.random.fold_in(seeds[23], 71), 0)
    cotangent = centred(seeds[1], (PACKS, DPACK, DD), 1.0, 6.0, ((0, 16),), jnp.float32)
    chip_sizes = draw_chip_sizes(jax.random.fold_in(seeds[23], 71), 0)
    ground_distance = with_ends(jax.random.randint(seeds[3], (PACKS, SLOTS), 1, 33), jax.random.fold_in(seeds[3], 1), 1, 32).astype(jnp.int32)
    visible_slots = draw_visible_slots(jax.random.fold_in(seeds[23], 71), 0)
    encoder_gains = jnp.clip(1.0 + 0.1 * jax.random.normal(seeds[5], (2, DE), jnp.float32), 0.5, 1.5)
    encoder_shifts = centred(seeds[6], (2, DE), 0.3, 4.0, (), jnp.float32)
    encoder_biases = centred(seeds[7], (2, DE), 0.3, 4.0, (), jnp.float32)
    encoder_attend = centred(seeds[8], (DE, 3 * HE * HD), DE ** -0.5, 0.21875)
    encoder_merge = centred(seeds[9], (HE * HD, DE), (max(1, HE * HD // 64)) ** -0.5, 1.75)
    encoder_expand = centred(seeds[10], (DE, FE), DE ** -0.5, 0.21875)
    encoder_inner = centred(seeds[11], (FE,), 0.3, 4.0, (), jnp.float32)
    encoder_shrink = centred(seeds[12], (FE, DE), FE ** -0.5, 0.109375)
    decoder_entry = centred(seeds[13], (DE, DD), DE ** -0.5, 0.21875)
    decoder_biases = centred(seeds[14], (3, DD), 0.3, 4.0, (), jnp.float32)
    mask_token = centred(seeds[15], (DD,), 1.0, 5.0, (), jnp.float32)
    decoder_gains = jnp.clip(1.0 + 0.1 * jax.random.normal(seeds[16], (2, DD), jnp.float32), 0.5, 1.5)
    decoder_shifts = centred(seeds[17], (2, DD), 0.3, 4.0, (), jnp.float32)
    decoder_attend = centred(seeds[18], (DD, 3 * HDEC * HD), DD ** -0.5, 0.25)
    decoder_merge = centred(seeds[19], (HDEC * HD, DD), (max(1, HDEC * HD // 128)) ** -0.5, 4.0)
    decoder_widen_weight = centred(seeds[20], (DD, FD), DD ** -0.5, 0.25)
    decoder_inner = centred(seeds[21], (FD,), 0.3, 4.0, (), jnp.float32)
    decoder_shrink = centred(seeds[22], (FD, DD), FD ** -0.5, 0.125)
    return dict(visible_tokens=visible_tokens, cotangent=cotangent, chip_sizes=chip_sizes, ground_distance=ground_distance, visible_slots=visible_slots, encoder_gains=encoder_gains, encoder_shifts=encoder_shifts, encoder_biases=encoder_biases, encoder_attend=encoder_attend, encoder_merge=encoder_merge, encoder_expand=encoder_expand, encoder_inner=encoder_inner, encoder_shrink=encoder_shrink, decoder_entry=decoder_entry, decoder_biases=decoder_biases, mask_token=mask_token, decoder_gains=decoder_gains, decoder_shifts=decoder_shifts, decoder_attend=decoder_attend, decoder_merge=decoder_merge, decoder_widen_weight=decoder_widen_weight, decoder_inner=decoder_inner, decoder_shrink=decoder_shrink)


@jax.custom_vjp
def low(v):
    return lax.optimization_barrier(v.astype(jnp.bfloat16)).astype(jnp.float32)

@jax.custom_vjp
def low_back(v):
    return v

def low_keep(v):
    return (low(v), None)

def low_pass(kept, grad):
    return (grad,)

def back_keep(v):
    return (v, None)

def back_low(kept, grad):
    return (low(grad),)
low.defvjp(low_keep, low_pass)
low_back.defvjp(back_keep, back_low)
HIGHEST = lax.Precision.HIGHEST

def pack_layout(extents, distance, visible):
    slot_count = extents.shape[0]
    chip_ends = jnp.cumsum(extents).astype(jnp.int32)
    chip_starts = (chip_ends - extents).astype(jnp.int32)
    places = jnp.arange(DPACK, dtype=jnp.int32)
    slot_chip = lax.optimization_barrier(jnp.sum((places[:, None] >= chip_ends[None, :]).astype(jnp.int32), axis=1))
    token_places = 4 * jnp.arange(EPACK, dtype=jnp.int32)
    token_chip = lax.optimization_barrier(jnp.sum((token_places[:, None] >= chip_ends[None, :]).astype(jnp.int32), axis=1))
    member = (slot_chip[:, None] == jnp.arange(slot_count, dtype=jnp.int32)[None, :]).astype(jnp.int32)
    first_slot = lax.optimization_barrier(jnp.sum(member * chip_starts[None, :], axis=1))
    extent = lax.optimization_barrier(jnp.sum(member * extents[None, :], axis=1))
    spacing = lax.optimization_barrier(jnp.sum(member * distance[None, :], axis=1))
    within = places - first_slot
    side_cells = jnp.where(extent == DPACK, BIG_SIDE, SMALL_SIDE).astype(jnp.int32)
    row_index = (within // side_cells).astype(jnp.float32)
    column_position = (within % side_cells).astype(jnp.float32)
    slot_valid = (slot_chip < slot_count).astype(jnp.float32)
    token_valid = (token_chip < slot_count).astype(jnp.float32)
    quarter = DD // 4
    frequency = jnp.exp(-jnp.log(10000.0) * jnp.arange(quarter, dtype=jnp.float32) / quarter)
    scaled = (spacing.astype(jnp.float32) / 16.0)[:, None] * frequency[None, :]
    angle_rows = row_index[:, None] * scaled
    angle_cols = column_position[:, None] * scaled
    encoding = jnp.concatenate([jnp.sin(angle_rows), jnp.cos(angle_rows), jnp.sin(angle_cols), jnp.cos(angle_cols)], axis=1) * slot_valid[:, None]
    scatter = (visible[None, :] == places[:, None]).astype(jnp.float32)
    covered = lax.optimization_barrier(jnp.sum(scatter, axis=1))
    fill_weight = slot_valid * (1.0 - covered)
    return (token_chip, slot_chip, token_valid, slot_valid, scatter, fill_weight, encoding)

def norm_rows(values, gain_row, shift_row):
    centered = values - lax.optimization_barrier(jnp.mean(values, axis=-1, keepdims=True))
    variance = lax.optimization_barrier(jnp.mean(centered * centered, axis=-1, keepdims=True))
    return centered * lax.rsqrt(variance + 1e-05) * gain_row + shift_row

def exact_dot(matrix_a, matrix_b):
    return jnp.dot(matrix_a, matrix_b, precision=HIGHEST)

def layer_unit_block(hidden, chip_ids, gain_rows, shift_rows, bias_rows, attend, merging, expand, inner_bias, shrink, head_count):
    length, width = hidden.shape
    head_size = HD
    inner_width = head_count * HD
    normed = low(norm_rows(hidden, gain_rows[0], shift_rows[0]))
    mixed = low(low_back(exact_dot(normed, attend)))
    pieces = mixed.reshape(length, 3, head_count, head_size)
    queries = pieces[:, 0]
    key_rows = pieces[:, 1]
    values = pieces[:, 2]
    raw_scores = low_back(jnp.einsum('qhd,khd->hqk', queries, key_rows, precision=HIGHEST))
    allowed = chip_ids[:, None] == chip_ids[None, :]
    scores = jnp.where(allowed[None], raw_scores * head_size ** (-0.5), -1e+30)
    weights = low(jax.nn.softmax(scores, axis=-1))
    context = jnp.einsum('hqk,khd->qhd', weights, values, precision=HIGHEST).reshape(length, inner_width)
    context = low(low_back(context))
    attention = low_back(exact_dot(context, merging)) + bias_rows[0]
    middle = hidden + attention
    normed_two = low(norm_rows(middle, gain_rows[1], shift_rows[1]))
    before = low_back(exact_dot(normed_two, expand) + inner_bias)
    active = low(jax.nn.gelu(before, approximate=False))
    feed = low_back(exact_dot(active, shrink)) + bias_rows[1]
    return (middle + feed, attention, feed)

def square_sums(valid_rows, members):
    return jnp.stack([jnp.sum(valid_rows[..., None] * member * member) for member in members])

def reference(visible_tokens, cotangent, chip_sizes, ground_distance, visible_slots, encoder_gains, encoder_shifts, encoder_biases, encoder_attend, encoder_merge, encoder_expand, encoder_inner, encoder_shrink, decoder_entry, decoder_biases, mask_token, decoder_gains, decoder_shifts, decoder_attend, decoder_merge, decoder_widen_weight, decoder_inner, decoder_shrink):
    token_chip, slot_chip, token_valid, slot_valid, scatter, fill_weight, encoding = jax.vmap(pack_layout)(chip_sizes, ground_distance, visible_slots)
    encoder_params = tuple((member.astype(jnp.float32) for member in (encoder_gains, encoder_shifts, encoder_biases, encoder_attend, encoder_merge, encoder_expand, encoder_inner, encoder_shrink)))
    decoder_params = tuple((member.astype(jnp.float32) for member in (decoder_entry, decoder_biases, mask_token, decoder_gains, decoder_shifts, decoder_attend, decoder_merge, decoder_widen_weight, decoder_inner, decoder_shrink)))

    def encode(tokens, params):

        def one_pack(inputs):
            pack_tokens, chip_ids, valid_rows = inputs
            output, attention, feed = layer_unit_block(pack_tokens, chip_ids, *params, HE)
            return (output, square_sums(valid_rows, (pack_tokens, attention, feed, output)))
        outputs, squares = lax.map(jax.checkpoint(one_pack), (tokens, token_chip, token_valid))
        return (outputs, squares)
    encoded, encode_back, encoder_squares = jax.vjp(encode, visible_tokens.astype(jnp.float32), encoder_params, has_aux=True)

    def decode(arrived, params):
        entry_weight, bias_rows, mask_row, gain_rows, shift_rows, attend, merging, expand, inner_bias, shrink = params

        def one_pack(inputs):
            pack_arrived, chip_ids, valid_rows, scatter_rows, fill_rows, encoded_rows, target = inputs
            sent = low(low_back(pack_arrived))
            entry_record = low(low_back(exact_dot(sent, entry_weight)) + bias_rows[0])
            inserted = low_back(exact_dot(scatter_rows, entry_record))
            start = inserted + fill_rows[:, None] * mask_row[None, :] + encoded_rows
            output, attention, feed = layer_unit_block(start, chip_ids, gain_rows, shift_rows, bias_rows[1:], attend, merging, expand, inner_bias, shrink, HDEC)
            loss_part = jnp.sum(output * target * valid_rows[:, None])
            return (loss_part, square_sums(valid_rows, (start, attention, feed, output)))
        losses, squares = lax.map(jax.checkpoint(one_pack), (arrived, slot_chip, slot_valid, scatter, fill_weight, encoding, cotangent))
        return (jnp.sum(losses), squares)
    total_loss, decode_back, decoder_squares = jax.vjp(decode, encoded, decoder_params, has_aux=True)
    arrived_grad, decoder_grads = decode_back(jnp.ones_like(total_loss))
    token_grad, encoder_grads = encode_back(arrived_grad)
    boundary = jnp.stack([token_grad, arrived_grad])
    totals = jnp.concatenate([lax.optimization_barrier(jnp.sum(encoder_squares, axis=0)), lax.optimization_barrier(jnp.sum(decoder_squares, axis=0))])
    counts = jnp.concatenate([jnp.full((4,), jnp.sum(token_valid) * DE), jnp.full((4,), jnp.sum(slot_valid) * DD)])
    statistics = jnp.sqrt(totals / counts)
    return (boundary, statistics, encoder_grads[0], encoder_grads[1], encoder_grads[2], encoder_grads[3], encoder_grads[4], encoder_grads[5], encoder_grads[6], encoder_grads[7], decoder_grads[0], decoder_grads[1], decoder_grads[2], decoder_grads[3], decoder_grads[4], decoder_grads[5], decoder_grads[6], decoder_grads[7], decoder_grads[8], decoder_grads[9])
```

```python
import jax
import jax.numpy as jnp
import numpy as np
from jax import lax
from jax.sharding import PartitionSpec as P

DE = 768
HE = 12
HD = 64
DD = 512
HDEC = 4
SMALL_SIDE = 16
BIG_SIDE = 32
MICRO = 2
DPACK = 1024
EPACK = 256


def pack_layout(extents, distance, visible):
    slot_count = extents.shape[0]
    chip_ends = jnp.cumsum(extents)
    chip_starts = chip_ends - extents
    places = jnp.arange(DPACK, dtype=jnp.int32)
    slot_chip = jnp.sum((places[:, None] >= chip_ends[None, :]).astype(jnp.int32), axis=1)
    token_places = 4 * jnp.arange(EPACK, dtype=jnp.int32)
    token_chip = jnp.sum((token_places[:, None] >= chip_ends[None, :]).astype(jnp.int32), axis=1)
    member = (slot_chip[:, None] == jnp.arange(slot_count, dtype=jnp.int32)[None, :]).astype(
        jnp.int32
    )
    first_slot = jnp.sum(member * chip_starts[None, :], axis=1)
    extent = jnp.sum(member * extents[None, :], axis=1)
    spacing = jnp.sum(member * distance[None, :], axis=1)
    within = places - first_slot
    side_cells = jnp.where(extent == DPACK, BIG_SIDE, SMALL_SIDE).astype(jnp.int32)
    row_index = (within // side_cells).astype(jnp.float32)
    column_position = (within % side_cells).astype(jnp.float32)
    slot_valid = (slot_chip < slot_count).astype(jnp.float32)
    token_valid = (token_chip < slot_count).astype(jnp.float32)
    quarter = DD // 4
    frequency = jnp.exp(-jnp.log(10000.0) * jnp.arange(quarter, dtype=jnp.float32) / quarter)
    scaled = (spacing.astype(jnp.float32) / 16.0)[:, None] * frequency[None, :]
    angle_rows = row_index[:, None] * scaled
    angle_cols = column_position[:, None] * scaled
    encoding = (
        jnp.concatenate(
            [jnp.sin(angle_rows), jnp.cos(angle_rows), jnp.sin(angle_cols), jnp.cos(angle_cols)],
            axis=1,
        )
        * slot_valid[:, None]
    )
    scatter = (visible[None, :] == places[:, None]).astype(jnp.float32)
    covered = jnp.sum(scatter, axis=1)
    fill_weight = slot_valid * (1.0 - covered)
    return (token_chip, slot_chip, token_valid, slot_valid, scatter, fill_weight, encoding)


def norm_rows(values, gain_row, shift_row):
    centered = values - jnp.mean(values, axis=-1, keepdims=True)
    variance = jnp.mean(centered * centered, axis=-1, keepdims=True)
    return centered * lax.rsqrt(variance + 1e-05) * gain_row + shift_row


def score_block(queries, key_rows, allowed, scale):
    raw_scores = jnp.einsum(
        "bqhd,bkhd->bhqk", queries, key_rows, preferred_element_type=jnp.float32
    )
    return jnp.where(allowed, raw_scores * scale, -1e30)


def square_sums(valid_rows, members):
    return jnp.stack([jnp.sum(valid_rows[..., None] * member * member) for member in members])


def block_forward(
    hidden,
    chip_ids,
    gain_rows,
    shift_rows,
    bias_rows,
    attend,
    merging,
    expand,
    inner_bias,
    shrink,
    head_count,
):
    batch, length, width = hidden.shape
    head_size = HD
    inner_width = head_count * HD
    scale = head_size ** (-0.5)
    normed = norm_rows(hidden, gain_rows[0], shift_rows[0]).astype(jnp.bfloat16)
    mixed = jnp.einsum("bld,df->blf", normed, attend, preferred_element_type=jnp.float32).astype(
        jnp.bfloat16
    )
    pieces = mixed.reshape(batch, length, 3, head_count, head_size)
    queries = pieces[:, :, 0]
    key_rows = pieces[:, :, 1]
    values = pieces[:, :, 2]
    allowed = (chip_ids[:, :, None] == chip_ids[:, None, :])[:, None]
    scores = score_block(queries, key_rows, allowed, scale)
    highest = jnp.max(scores, axis=-1, keepdims=True)
    expos = jnp.exp(scores - highest)
    totals = jnp.sum(expos, axis=-1, keepdims=True)
    weights = (expos / totals).astype(jnp.bfloat16)
    log_total = highest + jnp.log(totals)
    context = jnp.einsum("bhqk,bkhd->bqhd", weights, values, preferred_element_type=jnp.float32)
    context = context.reshape(batch, length, inner_width).astype(jnp.bfloat16)
    attention = (
        jnp.einsum("bld,de->ble", context, merging, preferred_element_type=jnp.float32)
        + bias_rows[0]
    )
    middle = hidden + attention
    normed_two = norm_rows(middle, gain_rows[1], shift_rows[1]).astype(jnp.bfloat16)
    before = (
        jnp.einsum("bld,df->blf", normed_two, expand, preferred_element_type=jnp.float32)
        + inner_bias
    )
    active = jax.nn.gelu(before, approximate=False).astype(jnp.bfloat16)
    feed = (
        jnp.einsum("blf,fd->bld", active, shrink, preferred_element_type=jnp.float32) + bias_rows[1]
    )
    kept = (
        hidden,
        normed,
        queries,
        key_rows,
        values,
        allowed,
        log_total,
        context,
        middle,
        normed_two,
        before,
        active,
    )
    return (middle + feed, attention, feed, kept)


def block_backward(
    grad_out, kept, gain_rows, shift_rows, attend, merging, expand, shrink, head_count
):
    (
        hidden,
        normed,
        queries,
        key_rows,
        values,
        allowed,
        log_total,
        context,
        middle,
        normed_two,
        before,
        active,
    ) = kept
    batch, length, width = hidden.shape
    head_size = HD
    inner_width = head_count * HD
    scale = head_size ** (-0.5)
    grad_feed = grad_out.astype(jnp.bfloat16)
    feed_bias = jnp.sum(grad_out, axis=(0, 1))
    shrink_grad = jnp.einsum("blf,bld->fd", active, grad_feed, preferred_element_type=jnp.float32)
    active_grad = jnp.einsum("bld,fd->blf", grad_feed, shrink, preferred_element_type=jnp.float32)
    unused, gelu_back = jax.vjp(lambda inputs: jax.nn.gelu(inputs, approximate=False), before)
    before_grad = gelu_back(active_grad)[0].astype(jnp.bfloat16)
    inner_grad = jnp.sum(before_grad, axis=(0, 1), dtype=jnp.float32)
    expand_grad = jnp.einsum(
        "bld,blf->df", normed_two, before_grad, preferred_element_type=jnp.float32
    )
    normed_two_grad = jnp.einsum(
        "blf,df->bld", before_grad, expand, preferred_element_type=jnp.float32
    )
    unused, second_back = jax.vjp(norm_rows, middle, gain_rows[1], shift_rows[1])
    middle_part, gain_two, shift_two = second_back(normed_two_grad)
    middle_grad = grad_out + middle_part
    attention_bias = jnp.sum(middle_grad, axis=(0, 1))
    attention_low = middle_grad.astype(jnp.bfloat16)
    merge_grad = jnp.einsum(
        "bld,ble->de", context, attention_low, preferred_element_type=jnp.float32
    )
    context_grad = jnp.einsum(
        "ble,de->bld", attention_low, merging, preferred_element_type=jnp.float32
    )
    context_grad = context_grad.astype(jnp.bfloat16).reshape(batch, length, head_count, head_size)
    scores = score_block(queries, key_rows, allowed, scale)
    probs = jnp.exp(scores - log_total)
    probs_low = probs.astype(jnp.bfloat16)
    probs_grad = jnp.einsum(
        "bqhd,bkhd->bhqk", context_grad, values, preferred_element_type=jnp.float32
    )
    values_grad = jnp.einsum(
        "bhqk,bqhd->bkhd", probs_low, context_grad, preferred_element_type=jnp.float32
    )
    score_grad = probs * (probs_grad - jnp.sum(probs * probs_grad, axis=-1, keepdims=True))
    raw_grad = jnp.where(allowed, score_grad * scale, 0.0).astype(jnp.bfloat16)
    query_grad = jnp.einsum(
        "bhqk,bkhd->bqhd", raw_grad, key_rows, preferred_element_type=jnp.float32
    )
    key_grad = jnp.einsum("bhqk,bqhd->bkhd", raw_grad, queries, preferred_element_type=jnp.float32)
    mixed_grad = (
        jnp.stack([query_grad, key_grad, values_grad], axis=2)
        .reshape(batch, length, 3 * inner_width)
        .astype(jnp.bfloat16)
    )
    attend_grad = jnp.einsum("bld,blf->df", normed, mixed_grad, preferred_element_type=jnp.float32)
    normed_grad = jnp.einsum("blf,df->bld", mixed_grad, attend, preferred_element_type=jnp.float32)
    unused, first_back = jax.vjp(norm_rows, hidden, gain_rows[0], shift_rows[0])
    hidden_part, gain_one, shift_one = first_back(normed_grad)
    input_grad = middle_grad + hidden_part
    grads = (
        jnp.stack([gain_one, gain_two]),
        jnp.stack([shift_one, shift_two]),
        jnp.stack([attention_bias, feed_bias]),
        attend_grad,
        merge_grad,
        expand_grad,
        inner_grad,
        shrink_grad,
    )
    return (input_grad, grads)


def scatter_sum(member, share_dim):
    return lax.psum_scatter(
        member, ("section", "dp"), scatter_dimension=share_dim, tiled=True
    )


def body(
    visible_tokens,
    cotangent,
    chip_sizes,
    ground_distance,
    visible_slots,
    encoder_gains,
    encoder_shifts,
    encoder_biases,
    encoder_attend,
    encoder_merge,
    encoder_expand,
    encoder_inner,
    encoder_shrink,
    decoder_entry,
    decoder_biases,
    mask_token,
    decoder_gains,
    decoder_shifts,
    decoder_attend,
    decoder_merge,
    decoder_widen_weight,
    decoder_inner,
    decoder_shrink,
):
    section = lax.axis_index("section")
    section_count = lax.axis_size("section")
    own = visible_tokens.shape[0] // section_count

    def mine(values):
        return lax.dynamic_slice_in_dim(values, section * own, own, 0)

    tokens = mine(visible_tokens)
    target = mine(cotangent)
    token_chip, slot_chip, token_valid, slot_valid, scatter, fill_weight, encoding = jax.vmap(
        pack_layout
    )(mine(chip_sizes), mine(ground_distance), mine(visible_slots))
    spread = scatter.astype(jnp.bfloat16)
    encoded, attention, feed, kept_encoder = block_forward(
        tokens,
        token_chip,
        encoder_gains,
        encoder_shifts,
        encoder_biases,
        encoder_attend,
        encoder_merge,
        encoder_expand,
        encoder_inner,
        encoder_shrink,
        HE,
    )
    encoder_squares = square_sums(token_valid, (tokens, attention, feed, encoded))
    sent = encoded.astype(jnp.bfloat16)
    entry = (
        jnp.einsum("bex,xd->bed", sent, decoder_entry, preferred_element_type=jnp.float32)
        + decoder_biases[0]
    ).astype(jnp.bfloat16)
    start = (
        jnp.einsum("kjw,kwi->kji", spread, entry, preferred_element_type=jnp.float32)
        + fill_weight[..., None] * mask_token
        + encoding
    )
    decoded, attention, feed, kept_decoder = block_forward(
        start,
        slot_chip,
        decoder_gains,
        decoder_shifts,
        decoder_biases[1:],
        decoder_attend,
        decoder_merge,
        decoder_widen_weight,
        decoder_inner,
        decoder_shrink,
        HDEC,
    )
    decoder_squares = square_sums(slot_valid, (start, attention, feed, decoded))
    start_grad, decoder_grads = block_backward(
        target * slot_valid[..., None],
        kept_decoder,
        decoder_gains,
        decoder_shifts,
        decoder_attend,
        decoder_merge,
        decoder_widen_weight,
        decoder_shrink,
        HDEC,
    )
    mask_grad = jnp.sum(fill_weight[..., None] * start_grad, axis=(0, 1))
    entry_grad = jnp.einsum(
        "ujc,ujr->ucr",
        spread,
        start_grad.astype(jnp.bfloat16),
        preferred_element_type=jnp.float32,
    )
    entry_low = entry_grad.astype(jnp.bfloat16)
    entry_bias = jnp.sum(entry_grad, axis=(0, 1))
    entry_weight = jnp.einsum("bex,bed->xd", sent, entry_low, preferred_element_type=jnp.float32)
    encoded_grad = jnp.einsum(
        "bed,xd->bex", entry_low, decoder_entry, preferred_element_type=jnp.float32
    ).astype(jnp.bfloat16)
    tokens_grad, encoder_grads = block_backward(
        encoded_grad.astype(jnp.float32),
        kept_encoder,
        encoder_gains,
        encoder_shifts,
        encoder_attend,
        encoder_merge,
        encoder_expand,
        encoder_shrink,
        HE,
    )
    swap = [(0, 1), (1, 0)]
    other_encoded = lax.ppermute(encoded_grad, "section", swap).astype(jnp.float32)
    other_tokens = lax.ppermute(tokens_grad, "section", swap)
    boundary = jnp.where(
        section == 0,
        jnp.concatenate([tokens_grad, other_tokens], axis=0),
        jnp.concatenate([other_encoded, encoded_grad.astype(jnp.float32)], axis=0),
    )
    counts = jnp.stack([jnp.sum(token_valid), jnp.sum(slot_valid)])
    totals, numbers = lax.psum(
        (jnp.concatenate([encoder_squares, decoder_squares]), counts), ("section", "dp")
    )
    denominators = jnp.concatenate(
        [jnp.full((4,), numbers[0] * DE), jnp.full((4,), numbers[1] * DD)]
    )
    statistics = jnp.sqrt(totals / denominators)
    gains, shifts, biases, attend, merge, expand, inner, shrink = decoder_grads
    biases = jnp.concatenate([entry_bias[None], biases], axis=0)
    decoder_grads = (entry_weight, biases, mask_grad, gains, shifts, attend, merge, expand, inner, shrink)
    reduced = [
        scatter_sum(member, share_dim)
        for member, share_dim in zip(
            encoder_grads + decoder_grads,
            (1, 1, 1, 0, 1, 0, 0, 0) + (0, 1, 0, 1, 1, 0, 1, 0, 0, 0),
        )
    ]
    return (boundary[None], statistics) + tuple(reduced)


def solution(mesh):
    in_specs = (
        P("dp", None, None),
        P("dp", None, None),
        P("dp", None),
        P("dp", None),
        P("dp", None),
        P(),
        P(),
        P(),
        P(),
        P(),
        P(),
        P(),
        P(),
        P(),
        P(),
        P(),
        P(),
        P(),
        P(),
        P(),
        P(),
        P(),
        P(),
    )
    out_specs = (
        P("section", "dp", None, None),
        P(),
        P(None, ("section", "dp")),
        P(None, ("section", "dp")),
        P(None, ("section", "dp")),
        P(("section", "dp"), None),
        P(None, ("section", "dp")),
        P(("section", "dp"), None),
        P(("section", "dp")),
        P(("section", "dp"), None),
        P(("section", "dp"), None),
        P(None, ("section", "dp")),
        P(("section", "dp")),
        P(None, ("section", "dp")),
        P(None, ("section", "dp")),
        P(("section", "dp"), None),
        P(None, ("section", "dp")),
        P(("section", "dp"), None),
        P(("section", "dp")),
        P(("section", "dp"), None),
    )
    return jax.shard_map(body, mesh=mesh, in_specs=in_specs, out_specs=out_specs, check_vma=False)
```

```python
import jax
import jax.numpy as jnp
from jax import lax
from jax.experimental import pallas as pl
from jax.experimental.pallas import tpu as pltpu
from jax.sharding import PartitionSpec as P

DE = 768
HE = 12
HD = 64
DD = 512
HDEC = 4
SMALL_SIDE = 16
BIG_SIDE = 32
MICRO = 2
DPACK = 1024
EPACK = 256


def pack_layout(extents, distance, visible):
    slot_count = extents.shape[0]
    chip_ends = jnp.cumsum(extents)
    chip_starts = chip_ends - extents
    places = jnp.arange(DPACK, dtype=jnp.int32)
    slot_chip = jnp.sum((places[:, None] >= chip_ends[None, :]).astype(jnp.int32), axis=1)
    token_places = 4 * jnp.arange(EPACK, dtype=jnp.int32)
    token_chip = jnp.sum((token_places[:, None] >= chip_ends[None, :]).astype(jnp.int32), axis=1)
    member = (slot_chip[:, None] == jnp.arange(slot_count, dtype=jnp.int32)[None, :]).astype(
        jnp.int32
    )
    first_slot = jnp.sum(member * chip_starts[None, :], axis=1)
    extent = jnp.sum(member * extents[None, :], axis=1)
    spacing = jnp.sum(member * distance[None, :], axis=1)
    within = places - first_slot
    side_cells = jnp.where(extent == DPACK, BIG_SIDE, SMALL_SIDE).astype(jnp.int32)
    row_index = (within // side_cells).astype(jnp.float32)
    column_position = (within % side_cells).astype(jnp.float32)
    slot_valid = (slot_chip < slot_count).astype(jnp.float32)
    token_valid = (token_chip < slot_count).astype(jnp.float32)
    quarter = DD // 4
    frequency = jnp.exp(-jnp.log(10000.0) * jnp.arange(quarter, dtype=jnp.float32) / quarter)
    scaled = (spacing.astype(jnp.float32) / 16.0)[:, None] * frequency[None, :]
    angle_rows = row_index[:, None] * scaled
    angle_cols = column_position[:, None] * scaled
    encoding = (
        jnp.concatenate(
            [jnp.sin(angle_rows), jnp.cos(angle_rows), jnp.sin(angle_cols), jnp.cos(angle_cols)],
            axis=1,
        )
        * slot_valid[:, None]
    )
    scatter = (visible[None, :] == places[:, None]).astype(jnp.float32)
    covered = jnp.sum(scatter, axis=1)
    fill_weight = slot_valid * (1.0 - covered)
    return (token_chip, slot_chip, token_valid, slot_valid, scatter, fill_weight, encoding)


def norm_rows(values, gain_row, shift_row):
    centered = values - jnp.mean(values, axis=-1, keepdims=True)
    variance = jnp.mean(centered * centered, axis=-1, keepdims=True)
    return centered * lax.rsqrt(variance + 1e-05) * gain_row + shift_row


def score_block(queries, key_rows, allowed, scale):
    raw_scores = jnp.einsum(
        "bqhd,bkhd->bhqk", queries, key_rows, preferred_element_type=jnp.float32
    )
    return jnp.where(allowed, raw_scores * scale, -1e30)


def square_sums(valid_rows, members):
    return jnp.stack([jnp.sum(valid_rows[..., None] * member * member) for member in members])


def block_forward(
    hidden,
    chip_ids,
    gain_rows,
    shift_rows,
    bias_rows,
    attend,
    merging,
    expand,
    inner_bias,
    shrink,
    head_count,
):
    batch, length, width = hidden.shape
    head_size = HD
    inner_width = head_count * HD
    scale = head_size ** (-0.5)
    normed = norm_rows(hidden, gain_rows[0], shift_rows[0]).astype(jnp.bfloat16)
    mixed = jnp.einsum("bld,df->blf", normed, attend, preferred_element_type=jnp.float32).astype(
        jnp.bfloat16
    )
    pieces = mixed.reshape(batch, length, 3, head_count, head_size)
    queries = pieces[:, :, 0]
    key_rows = pieces[:, :, 1]
    values = pieces[:, :, 2]
    allowed = (chip_ids[:, :, None] == chip_ids[:, None, :])[:, None]
    scores = score_block(queries, key_rows, allowed, scale)
    highest = jnp.max(scores, axis=-1, keepdims=True)
    expos = jnp.exp(scores - highest)
    totals = jnp.sum(expos, axis=-1, keepdims=True)
    weights = (expos / totals).astype(jnp.bfloat16)
    log_total = highest + jnp.log(totals)
    context = jnp.einsum("bhqk,bkhd->bqhd", weights, values, preferred_element_type=jnp.float32)
    context = context.reshape(batch, length, inner_width).astype(jnp.bfloat16)
    attention = (
        jnp.einsum("bld,de->ble", context, merging, preferred_element_type=jnp.float32)
        + bias_rows[0]
    )
    middle = hidden + attention
    normed_two = norm_rows(middle, gain_rows[1], shift_rows[1]).astype(jnp.bfloat16)
    before = (
        jnp.einsum("bld,df->blf", normed_two, expand, preferred_element_type=jnp.float32)
        + inner_bias
    )
    active = jax.nn.gelu(before, approximate=False).astype(jnp.bfloat16)
    feed = (
        jnp.einsum("blf,fd->bld", active, shrink, preferred_element_type=jnp.float32) + bias_rows[1]
    )
    kept = (
        hidden,
        normed,
        queries,
        key_rows,
        values,
        allowed,
        log_total,
        context,
        middle,
        normed_two,
        before,
        active,
    )
    return (middle + feed, attention, feed, kept)


def block_backward(
    grad_out, kept, gain_rows, shift_rows, attend, merging, expand, shrink, head_count
):
    (
        hidden,
        normed,
        queries,
        key_rows,
        values,
        allowed,
        log_total,
        context,
        middle,
        normed_two,
        before,
        active,
    ) = kept
    batch, length, width = hidden.shape
    head_size = HD
    inner_width = head_count * HD
    scale = head_size ** (-0.5)
    grad_feed = grad_out.astype(jnp.bfloat16)
    feed_bias = jnp.sum(grad_out, axis=(0, 1))
    shrink_grad = jnp.einsum("blf,bld->fd", active, grad_feed, preferred_element_type=jnp.float32)
    active_grad = jnp.einsum("bld,fd->blf", grad_feed, shrink, preferred_element_type=jnp.float32)
    unused, gelu_back = jax.vjp(lambda inputs: jax.nn.gelu(inputs, approximate=False), before)
    before_grad = gelu_back(active_grad)[0].astype(jnp.bfloat16)
    inner_grad = jnp.sum(before_grad, axis=(0, 1), dtype=jnp.float32)
    expand_grad = jnp.einsum(
        "bld,blf->df", normed_two, before_grad, preferred_element_type=jnp.float32
    )
    normed_two_grad = jnp.einsum(
        "blf,df->bld", before_grad, expand, preferred_element_type=jnp.float32
    )
    unused, second_back = jax.vjp(norm_rows, middle, gain_rows[1], shift_rows[1])
    middle_part, gain_two, shift_two = second_back(normed_two_grad)
    middle_grad = grad_out + middle_part
    attention_bias = jnp.sum(middle_grad, axis=(0, 1))
    attention_low = middle_grad.astype(jnp.bfloat16)
    merge_grad = jnp.einsum(
        "bld,ble->de", context, attention_low, preferred_element_type=jnp.float32
    )
    context_grad = jnp.einsum(
        "ble,de->bld", attention_low, merging, preferred_element_type=jnp.float32
    )
    context_grad = context_grad.astype(jnp.bfloat16).reshape(batch, length, head_count, head_size)
    scores = score_block(queries, key_rows, allowed, scale)
    probs = jnp.exp(scores - log_total)
    probs_low = probs.astype(jnp.bfloat16)
    probs_grad = jnp.einsum(
        "bqhd,bkhd->bhqk", context_grad, values, preferred_element_type=jnp.float32
    )
    values_grad = jnp.einsum(
        "bhqk,bqhd->bkhd", probs_low, context_grad, preferred_element_type=jnp.float32
    )
    score_grad = probs * (probs_grad - jnp.sum(probs * probs_grad, axis=-1, keepdims=True))
    raw_grad = jnp.where(allowed, score_grad * scale, 0.0).astype(jnp.bfloat16)
    query_grad = jnp.einsum(
        "bhqk,bkhd->bqhd", raw_grad, key_rows, preferred_element_type=jnp.float32
    )
    key_grad = jnp.einsum("bhqk,bqhd->bkhd", raw_grad, queries, preferred_element_type=jnp.float32)
    mixed_grad = (
        jnp.stack([query_grad, key_grad, values_grad], axis=2)
        .reshape(batch, length, 3 * inner_width)
        .astype(jnp.bfloat16)
    )
    attend_grad = jnp.einsum("bld,blf->df", normed, mixed_grad, preferred_element_type=jnp.float32)
    normed_grad = jnp.einsum("blf,df->bld", mixed_grad, attend, preferred_element_type=jnp.float32)
    unused, first_back = jax.vjp(norm_rows, hidden, gain_rows[0], shift_rows[0])
    hidden_part, gain_one, shift_one = first_back(normed_grad)
    input_grad = middle_grad + hidden_part
    grads = (
        jnp.stack([gain_one, gain_two]),
        jnp.stack([shift_one, shift_two]),
        jnp.stack([attention_bias, feed_bias]),
        attend_grad,
        merge_grad,
        expand_grad,
        inner_grad,
        shrink_grad,
    )
    return (input_grad, grads)


MESH_ID = pl.DeviceIdType.MESH
CANON = ("x", "z2", "z1", "y")
ROUTES = (("x", "y", "z1", "z2"), ("y", "x", "z1", "z2"), ("z1", "z2", "x", "y"))
WIDTHS = (5, 6, 3)
CHUNKS = 11
STRIDE = sum(WIDTHS)
COLUMNS = CHUNKS * STRIDE * 128
OFFSETS = (0, WIDTHS[0], WIDTHS[0] + WIDTHS[1])


def place(names, bits):
    index = 0
    for name in names:
        index = index * 2 + bits[name]
    return index


def left_after(route, stage):
    return tuple(name for name in CANON if name not in route[:stage])


def choices(names):
    for number in range(2 ** len(names)):
        yield {name: (number >> (len(names) - 1 - i)) & 1 for i, name in enumerate(names)}


def reduce_kernel(packed, small, payload, out, small_out, payload_out, *scratch):
    own, first = scratch[0], scratch[1]
    sent, got = scratch[2:14], scratch[14:26]
    small_own, small_sent, small_got = scratch[26:29]
    own_sem, first_send, first_recv, send_sem, recv_sem, small_sem, small_send, small_recv, pay_send, pay_recv = scratch[29:]
    section = lax.axis_index("section")
    data = lax.axis_index("dp")
    mine = {"x": section, "c": data % 2, "y": data // 2 % 2, "z1": data // 4 % 2, "z2": data // 8 % 2}
    weight = {"c": 1, "y": 2, "z1": 4, "z2": 8}
    partner = {"x": (1 - section, data)}
    for name, step in weight.items():
        partner[name] = (section, data + step * (1 - 2 * mine[name]))

    barrier = pltpu.get_barrier_semaphore()
    for name in ("c",) + CANON:
        pl.semaphore_signal(barrier, inc=1, device_id=partner[name], device_id_type=MESH_ID)
    pl.semaphore_wait(barrier, 5)

    def remote(source, target, send, recv, name):
        return pltpu.make_async_remote_copy(
            src_ref=source,
            dst_ref=target,
            send_sem=send,
            recv_sem=recv,
            device_id=partner[name],
            device_id_type=MESH_ID,
        )

    def wide(chunk):
        return pl.ds(pl.multiple_of(chunk * (STRIDE * 128), 128), STRIDE * 128)

    def own_copy(chunk):
        return pltpu.make_async_copy(
            packed.at[:, mine["c"], :, wide(chunk)], own.at[:, :, wide(chunk)], own_sem.at[chunk]
        )

    def first_copy(chunk):
        return remote(
            packed.at[:, 1 - mine["c"], :, wide(chunk)],
            first.at[:, :, wide(chunk)],
            first_send.at[chunk],
            first_recv.at[chunk],
            "c",
        )

    def columns(route, chunk):
        width = WIDTHS[route] * 128
        return pl.ds(pl.multiple_of(chunk * width, 128), width)

    def whole_columns(route, chunk):
        start = chunk * (STRIDE * 128) + OFFSETS[route] * 128
        return pl.ds(pl.multiple_of(start, 128), WIDTHS[route] * 128)

    def stage_copy(route, stage, chunk):
        cols = columns(route, chunk)
        return remote(
            sent[route * 4 + stage].at[:, :, cols],
            got[route * 4 + stage].at[:, :, cols],
            send_sem.at[route, stage, chunk],
            recv_sem.at[route, stage, chunk],
            ROUTES[route][stage],
        )

    def total(route, stage, chunk, bits):
        cols = whole_columns(route, chunk)
        spot = place(CANON, bits)
        value = own[spot, :, cols].astype(jnp.float32) + first[spot, :, cols].astype(jnp.float32)
        for earlier in range(stage):
            names = left_after(ROUTES[route], earlier + 1)
            piece = got[route * 4 + earlier][place(names, bits), :, columns(route, chunk)]
            value = value + piece.astype(jnp.float32)
        return value

    def advance(route, stage, chunk):
        path = ROUTES[route]
        if stage == 0:
            pass
        else:
            stage_copy(route, stage - 1, chunk).wait_recv()
        if stage == 4:
            out[:, whole_columns(route, chunk)] = total(route, 4, chunk, mine)
            return
        names = left_after(path, stage + 1)
        for free in choices(names):
            bits = dict(mine)
            bits[path[stage]] = 1 - mine[path[stage]]
            bits.update(free)
            sent[route * 4 + stage][place(names, free), :, columns(route, chunk)] = total(
                route, stage, chunk, bits
            ).astype(jnp.bfloat16)
        stage_copy(route, stage, chunk).start()

    small_route = ("c",) + ROUTES[0]

    def small_copy(stage):
        count = 16 >> stage
        return remote(
            small_sent.at[stage, pl.ds(0, count)],
            small_got.at[stage, pl.ds(0, count)],
            small_send.at[stage],
            small_recv.at[stage],
            small_route[stage],
        )

    every = CANON + ("c",)

    def small_left(stage):
        return tuple(name for name in every if name not in small_route[:stage])

    def small_total(stage, bits):
        value = small_own[place(every, bits)]
        for earlier in range(stage):
            value = value + small_got[earlier, place(small_left(earlier + 1), bits)]
        return value

    def small_advance(stage):
        if stage > 0:
            small_copy(stage - 1).wait_recv()
        if stage == 5:
            small_out[...] = small_total(5, mine)
            return
        names = small_left(stage + 1)
        for free in choices(names):
            bits = dict(mine)
            bits[small_route[stage]] = 1 - mine[small_route[stage]]
            bits.update(free)
            small_sent[stage, place(names, free)] = small_total(stage, bits)
        small_copy(stage).start()

    ahead = 2
    for chunk in range(ahead):
        own_copy(chunk).start()
        first_copy(chunk).start()
    small_fetch = pltpu.make_async_copy(small, small_own, small_sem)
    small_fetch.start()
    exchange = remote(payload, payload_out, pay_send, pay_recv, "x")
    exchange.start()
    small_fetch.wait()

    @pl.loop(0, CHUNKS + 4)
    def _(turn):
        @pl.when(turn + ahead < CHUNKS)
        def _():
            own_copy(turn + ahead).start()
            first_copy(turn + ahead).start()

        for stage in range(4, -1, -1):
            chunk = turn - stage

            @pl.when((chunk >= 0) & (chunk < CHUNKS))
            def _(stage=stage, chunk=chunk):
                if stage == 0:
                    own_copy(chunk).wait()
                    first_copy(chunk).wait_recv()
                for route in range(3):
                    advance(route, stage, chunk)

        for stage in range(6):

            @pl.when(turn == stage)
            def _(stage=stage):
                small_advance(stage)

    @pl.loop(0, CHUNKS)
    def _(chunk):
        first_copy(chunk).wait_send()
        for route in range(3):
            for stage in range(4):
                stage_copy(route, stage, chunk).wait_send()

    for stage in range(5):
        small_copy(stage).wait_send()
    exchange.wait()


def reduce_call(packed, small, payload):
    blocks = [8, 4, 2, 1]
    buffers = [
        pltpu.VMEM((block, 16, CHUNKS * width * 128), jnp.bfloat16)
        for width in WIDTHS
        for block in blocks
    ]
    return pl.pallas_call(
        reduce_kernel,
        out_shape=(
            jax.ShapeDtypeStruct((16, COLUMNS), jnp.float32),
            jax.ShapeDtypeStruct((8, 128), jnp.float32),
            jax.ShapeDtypeStruct(payload.shape, payload.dtype),
        ),
        in_specs=[pl.BlockSpec(memory_space=pl.ANY)] * 3,
        out_specs=(
            pl.BlockSpec(memory_space=pltpu.VMEM),
            pl.BlockSpec(memory_space=pltpu.VMEM),
            pl.BlockSpec(memory_space=pl.ANY),
        ),
        scratch_shapes=[pltpu.VMEM((16, 16, COLUMNS), jnp.bfloat16)] * 2
        + buffers
        + buffers
        + [
            pltpu.VMEM((32, 8, 128), jnp.float32),
            pltpu.VMEM((5, 16, 8, 128), jnp.float32),
            pltpu.VMEM((5, 16, 8, 128), jnp.float32),
            pltpu.SemaphoreType.DMA((CHUNKS,)),
            pltpu.SemaphoreType.DMA((CHUNKS,)),
            pltpu.SemaphoreType.DMA((CHUNKS,)),
            pltpu.SemaphoreType.DMA((3, 4, CHUNKS)),
            pltpu.SemaphoreType.DMA((3, 4, CHUNKS)),
            pltpu.SemaphoreType.DMA,
            pltpu.SemaphoreType.DMA((5,)),
            pltpu.SemaphoreType.DMA((5,)),
            pltpu.SemaphoreType.DMA,
            pltpu.SemaphoreType.DMA,
        ],
        compiler_params=pltpu.CompilerParams(
            collective_id=0, has_side_effects=True, vmem_limit_bytes=58 * 2**20
        ),
        cost_estimate=pl.CostEstimate(
            flops=3 * 16 * COLUMNS * 32, bytes_accessed=4 * 16 * COLUMNS * 32, transcendentals=0
        ),
        name="reduce_gradients",
    )(packed, small, payload)


def pack_rows(member):
    rows, width = member.shape
    count = rows // 32
    groups = member.astype(jnp.bfloat16).reshape(32, count // 8, 8, width)
    pairs = count // 16
    pieces = [groups[:, 2 * i : 2 * i + 2].reshape(32, 16, width) for i in range(pairs)]
    if count % 16:
        rest = groups[:, -1].reshape(32, 8, 2, width // 2)
        pieces.append(jnp.swapaxes(rest, 1, 2).reshape(32, 16, width // 2))
    return pieces


def unpack_rows(packed, offset, count, width):
    pairs = count // 16
    pieces = [packed[:, offset + i * width : offset + (i + 1) * width] for i in range(pairs)]
    offset = offset + pairs * width
    if count % 16:
        half = width // 2
        rest = packed[:, offset : offset + half]
        pieces.append(jnp.concatenate([rest[:8], rest[8:]], axis=1))
        offset = offset + half
    return jnp.concatenate(pieces, axis=0), offset


def shard_columns(member):
    lines = member.reshape(-1, member.shape[-1])
    count = lines.shape[1] // 32
    return jnp.swapaxes(lines.reshape(-1, 32, count), 0, 1).reshape(32, -1)


def reduce_all(wide, vectors, sums, payload):
    packed = jnp.concatenate([piece for member in wide for piece in pack_rows(member)], axis=2)
    lines = jnp.concatenate([shard_columns(member) for member in vectors], axis=1)
    lines = jnp.concatenate(
        [
            jnp.pad(lines, ((0, 0), (0, 512 - lines.shape[1]))),
            jnp.broadcast_to(jnp.pad(sums, (0, 512 - sums.shape[0])), (32, 512)),
        ],
        axis=1,
    ).reshape(32, 8, 128)
    out, small, arrived = reduce_call(packed.reshape(16, 2, 16, COLUMNS), lines, payload)
    small = small.reshape(1024)
    wide_out = []
    offset = 0
    for member in wide:
        piece, offset = unpack_rows(out, offset, member.shape[0] // 32, member.shape[1])
        wide_out.append(piece)
    vectors_out = []
    offset = 0
    for member in vectors:
        count = member.size // 32
        vectors_out.append(
            small[offset : offset + count].reshape(member.shape[:-1] + (member.shape[-1] // 32,))
        )
        offset += count
    return wide_out, vectors_out, small[512 : 512 + sums.shape[0]], arrived


def scatter_sum(member, share_dim):
    return lax.psum_scatter(
        member, ("section", "dp"), scatter_dimension=share_dim, tiled=True
    )


def body(
    visible_tokens,
    cotangent,
    chip_sizes,
    ground_distance,
    visible_slots,
    encoder_gains,
    encoder_shifts,
    encoder_biases,
    encoder_attend,
    encoder_merge,
    encoder_expand,
    encoder_inner,
    encoder_shrink,
    decoder_entry,
    decoder_biases,
    mask_token,
    decoder_gains,
    decoder_shifts,
    decoder_attend,
    decoder_merge,
    decoder_widen_weight,
    decoder_inner,
    decoder_shrink,
):
    section = lax.axis_index("section")
    section_count = lax.axis_size("section")
    own = visible_tokens.shape[0] // section_count

    def mine(values):
        return lax.dynamic_slice_in_dim(values, section * own, own, 0)

    tokens = mine(visible_tokens)
    target = mine(cotangent)
    token_chip, slot_chip, token_valid, slot_valid, scatter, fill_weight, encoding = jax.vmap(
        pack_layout
    )(mine(chip_sizes), mine(ground_distance), mine(visible_slots))
    spread = scatter.astype(jnp.bfloat16)
    encoded, attention, feed, kept_encoder = block_forward(
        tokens,
        token_chip,
        encoder_gains,
        encoder_shifts,
        encoder_biases,
        encoder_attend,
        encoder_merge,
        encoder_expand,
        encoder_inner,
        encoder_shrink,
        HE,
    )
    encoder_squares = square_sums(token_valid, (tokens, attention, feed, encoded))
    sent = encoded.astype(jnp.bfloat16)
    entry = (
        jnp.einsum("bex,xd->bed", sent, decoder_entry, preferred_element_type=jnp.float32)
        + decoder_biases[0]
    ).astype(jnp.bfloat16)
    start = (
        jnp.einsum("kjw,kwi->kji", spread, entry, preferred_element_type=jnp.float32)
        + fill_weight[..., None] * mask_token
        + encoding
    )
    decoded, attention, feed, kept_decoder = block_forward(
        start,
        slot_chip,
        decoder_gains,
        decoder_shifts,
        decoder_biases[1:],
        decoder_attend,
        decoder_merge,
        decoder_widen_weight,
        decoder_inner,
        decoder_shrink,
        HDEC,
    )
    decoder_squares = square_sums(slot_valid, (start, attention, feed, decoded))
    start_grad, decoder_grads = block_backward(
        target * slot_valid[..., None],
        kept_decoder,
        decoder_gains,
        decoder_shifts,
        decoder_attend,
        decoder_merge,
        decoder_widen_weight,
        decoder_shrink,
        HDEC,
    )
    mask_grad = jnp.sum(fill_weight[..., None] * start_grad, axis=(0, 1))
    entry_grad = jnp.einsum(
        "ujc,ujr->ucr",
        spread,
        start_grad.astype(jnp.bfloat16),
        preferred_element_type=jnp.float32,
    )
    entry_low = entry_grad.astype(jnp.bfloat16)
    entry_bias = jnp.sum(entry_grad, axis=(0, 1))
    entry_weight = jnp.einsum("bex,bed->xd", sent, entry_low, preferred_element_type=jnp.float32)
    encoded_grad = jnp.einsum(
        "bed,xd->bex", entry_low, decoder_entry, preferred_element_type=jnp.float32
    ).astype(jnp.bfloat16)
    tokens_grad, encoder_grads = block_backward(
        encoded_grad.astype(jnp.float32),
        kept_encoder,
        encoder_gains,
        encoder_shifts,
        encoder_attend,
        encoder_merge,
        encoder_expand,
        encoder_shrink,
        HE,
    )
    sums = jnp.concatenate(
        [encoder_squares, decoder_squares, jnp.sum(token_valid)[None], jnp.sum(slot_valid)[None]]
    )
    e_gains, e_shifts, e_biases, e_attend, e_merge, e_expand, e_inner, e_shrink = encoder_grads
    d_gains, d_shifts, d_biases, d_attend, d_merge, d_expand, d_inner, d_shrink = decoder_grads
    d_biases = jnp.concatenate([entry_bias[None], d_biases], axis=0)
    payload = jnp.where(section == 0, encoded_grad, tokens_grad.astype(jnp.bfloat16))
    wide = (entry_weight, d_attend, d_merge.T, d_expand, d_shrink, e_expand, e_shrink, e_merge.T, e_attend)
    vectors = (
        e_gains, e_shifts, e_biases, e_inner,
        d_biases, mask_grad, d_gains, d_shifts, d_inner,
    )
    if (section_count, lax.axis_size("dp")) == (2, 16):
        wide, vectors, sums, arrived = reduce_all(wide, vectors, sums, payload)
    else:
        wide = [scatter_sum(member, 0) for member in wide]
        vectors = [scatter_sum(member, member.ndim - 1) for member in vectors]
        sums = lax.psum(sums, ("section", "dp"))
        arrived = lax.ppermute(payload, "section", [(0, 1), (1, 0)])
    arrived = arrived.astype(jnp.float32)
    boundary = jnp.where(
        section == 0,
        jnp.concatenate([tokens_grad, arrived], axis=0),
        jnp.concatenate([arrived, encoded_grad.astype(jnp.float32)], axis=0),
    )
    denominators = jnp.concatenate(
        [jnp.full((4,), sums[8] * DE), jnp.full((4,), sums[9] * DD)]
    )
    statistics = jnp.sqrt(sums[:8] / denominators)
    entry_weight, d_attend, d_merge, d_expand, d_shrink, e_expand, e_shrink, e_merge, e_attend = wide
    e_gains, e_shifts, e_biases, e_inner, d_biases, mask_grad, d_gains, d_shifts, d_inner = vectors
    return (
        boundary[None], statistics,
        e_gains, e_shifts, e_biases, e_attend, e_merge.T, e_expand, e_inner, e_shrink,
        entry_weight, d_biases, mask_grad, d_gains, d_shifts, d_attend, d_merge.T, d_expand, d_inner, d_shrink,
    )


def solution(mesh):
    in_specs = (
        P("dp", None, None),
        P("dp", None, None),
        P("dp", None),
        P("dp", None),
        P("dp", None),
        P(),
        P(),
        P(),
        P(),
        P(),
        P(),
        P(),
        P(),
        P(),
        P(),
        P(),
        P(),
        P(),
        P(),
        P(),
        P(),
        P(),
        P(),
    )
    out_specs = (
        P("section", "dp", None, None),
        P(),
        P(None, ("section", "dp")),
        P(None, ("section", "dp")),
        P(None, ("section", "dp")),
        P(("section", "dp"), None),
        P(None, ("section", "dp")),
        P(("section", "dp"), None),
        P(("section", "dp")),
        P(("section", "dp"), None),
        P(("section", "dp"), None),
        P(None, ("section", "dp")),
        P(("section", "dp")),
        P(None, ("section", "dp")),
        P(None, ("section", "dp")),
        P(("section", "dp"), None),
        P(None, ("section", "dp")),
        P(("section", "dp"), None),
        P(("section", "dp")),
        P(("section", "dp"), None),
    )
    return jax.shard_map(body, mesh=mesh, in_specs=in_specs, out_specs=out_specs, check_vma=False)
```

```python
import jax
import jax.numpy as jnp
from jax import lax
from jax.experimental import pallas as pl
from jax.experimental.pallas import tpu as pltpu
from jax.sharding import PartitionSpec as P

DE = 768
DD = 512
TILE = 256
NEGATIVE = -1e30
MESH_ID = pl.DeviceIdType.MESH
CANON = ("x", "z2", "z1", "y")
ROUTES = (("x", "y", "z1", "z2"), ("y", "x", "z1", "z2"), ("z1", "z2", "x", "y"))
WIDTHS = (4, 5, 3)
CHUNKS = 13
DECODER_CHUNKS = 4
STRIDE = sum(WIDTHS)
COLUMNS = CHUNKS * STRIDE * 128
DECODER_COLUMNS = DECODER_CHUNKS * STRIDE * 128
ENCODER_COLUMNS = COLUMNS - DECODER_COLUMNS
OFFSETS = (0, WIDTHS[0], WIDTHS[0] + WIDTHS[1])


def place(names, bits):
    index = 0
    for name in names:
        index = index * 2 + bits[name]
    return index


def left_after(route, stage):
    return tuple(name for name in CANON if name not in route[:stage])


def choices(names):
    for number in range(2 ** len(names)):
        yield {name: (number >> (len(names) - 1 - i)) & 1 for i, name in enumerate(names)}


def reduce_kernel(
    decoder_part, encoder_part, decoder_small, encoder_small, payload,
    out, decoder_sums, encoder_sums, payload_out, *scratch
):
    own, first = scratch[0], scratch[1]
    sent, got = scratch[2:14], scratch[14:26]
    (
        decoder_total, encoder_total, decoder_got, encoder_got,
        own_sem, first_send, first_recv, send_sem, recv_sem, fetch_sem, small_send, small_recv, pay_send, pay_recv,
    ) = scratch[26:]
    section = lax.axis_index("section")
    data = lax.axis_index("dp")
    mine = {"x": section, "c": data % 2, "y": data // 2 % 2, "z1": data // 4 % 2, "z2": data // 8 % 2}
    weight = {"c": 1, "y": 2, "z1": 4, "z2": 8}
    partner = {"x": (1 - section, data)}
    for name, step in weight.items():
        partner[name] = (section, data + step * (1 - 2 * mine[name]))

    barrier = pltpu.get_barrier_semaphore()
    for name in ("c",) + CANON:
        pl.semaphore_signal(barrier, inc=1, device_id=partner[name], device_id_type=MESH_ID)
    pl.semaphore_wait(barrier, 5)

    def remote(source, target, send, recv, name):
        return pltpu.make_async_remote_copy(
            src_ref=source,
            dst_ref=target,
            send_sem=send,
            recv_sem=recv,
            device_id=partner[name],
            device_id_type=MESH_ID,
        )

    def wide(chunk):
        return pl.ds(pl.multiple_of(chunk * (STRIDE * 128), 128), STRIDE * 128)

    def own_copy(source, chunk, origin):
        return pltpu.make_async_copy(
            source.at[:, mine["c"], :, wide(origin)], own.at[:, :, wide(chunk)], own_sem.at[chunk]
        )

    def first_copy(source, chunk, origin):
        return remote(
            source.at[:, 1 - mine["c"], :, wide(origin)],
            first.at[:, :, wide(chunk)],
            first_send.at[chunk],
            first_recv.at[chunk],
            "c",
        )

    def begin(chunk):
        @pl.when(chunk < DECODER_CHUNKS)
        def _():
            own_copy(decoder_part, chunk, chunk).start()
            first_copy(decoder_part, chunk, chunk).start()

        @pl.when((chunk >= DECODER_CHUNKS) & (chunk < CHUNKS))
        def _():
            own_copy(encoder_part, chunk, chunk - DECODER_CHUNKS).start()
            first_copy(encoder_part, chunk, chunk - DECODER_CHUNKS).start()

    def columns(route, chunk):
        width = WIDTHS[route] * 128
        return pl.ds(pl.multiple_of(chunk * width, 128), width)

    def whole_columns(route, chunk):
        start = chunk * (STRIDE * 128) + OFFSETS[route] * 128
        return pl.ds(pl.multiple_of(start, 128), WIDTHS[route] * 128)

    def stage_copy(route, stage, chunk):
        cols = columns(route, chunk)
        return remote(
            sent[route * 4 + stage].at[:, :, cols],
            got[route * 4 + stage].at[:, :, cols],
            send_sem.at[route, stage, chunk],
            recv_sem.at[route, stage, chunk],
            ROUTES[route][stage],
        )

    def total(route, stage, chunk, bits):
        cols = whole_columns(route, chunk)
        spot = place(CANON, bits)
        value = own[spot, :, cols].astype(jnp.float32) + first[spot, :, cols].astype(jnp.float32)
        for earlier in range(stage):
            names = left_after(ROUTES[route], earlier + 1)
            piece = got[route * 4 + earlier][place(names, bits), :, columns(route, chunk)]
            value = value + piece.astype(jnp.float32)
        return value

    def advance(route, stage, chunk):
        path = ROUTES[route]
        if stage == 0:
            pass
        else:
            stage_copy(route, stage - 1, chunk).wait_recv()
        if stage == 4:
            out[:, whole_columns(route, chunk)] = total(route, 4, chunk, mine)
            return
        names = left_after(path, stage + 1)
        for free in choices(names):
            bits = dict(mine)
            bits[path[stage]] = 1 - mine[path[stage]]
            bits.update(free)
            sent[route * 4 + stage][place(names, free), :, columns(route, chunk)] = total(
                route, stage, chunk, bits
            ).astype(jnp.bfloat16)
        stage_copy(route, stage, chunk).start()

    small_route = ("c",) + ROUTES[0]
    totals = ((decoder_total, decoder_got), (encoder_total, encoder_got))

    def small_copy(stage, kind):
        source, target = totals[kind]
        return remote(
            source.at[stage],
            target.at[stage],
            small_send.at[stage, kind],
            small_recv.at[stage, kind],
            small_route[stage],
        )

    def small_advance(stage):
        for kind in range(2):
            source, target = totals[kind]
            if stage > 0:
                small_copy(stage - 1, kind).wait_recv()
                source[stage] = source[stage - 1] + target[stage - 1]
            if stage < 5:
                small_copy(stage, kind).start()

    ahead = 2
    for chunk in range(ahead):
        begin(jnp.int32(chunk))
    fetches = (
        pltpu.make_async_copy(decoder_small, decoder_total.at[0], fetch_sem.at[0]),
        pltpu.make_async_copy(encoder_small, encoder_total.at[0], fetch_sem.at[1]),
    )
    for fetch in fetches:
        fetch.start()
    exchange = remote(payload, payload_out, pay_send, pay_recv, "x")
    exchange.start()
    for fetch in fetches:
        fetch.wait()

    @pl.loop(0, CHUNKS + 4)
    def _(turn):
        begin(turn + ahead)

        for stage in range(4, -1, -1):
            chunk = turn - stage

            @pl.when((chunk >= 0) & (chunk < CHUNKS))
            def _(stage=stage, chunk=chunk):
                if stage == 0:
                    own_copy(encoder_part, chunk, 0).wait()
                    first_copy(encoder_part, chunk, 0).wait_recv()
                for route in range(3):
                    advance(route, stage, chunk)

        for stage in range(6):

            @pl.when(turn == stage)
            def _(stage=stage):
                small_advance(stage)

    @pl.loop(0, CHUNKS)
    def _(chunk):
        first_copy(encoder_part, chunk, 0).wait_send()
        for route in range(3):
            for stage in range(4):
                stage_copy(route, stage, chunk).wait_send()

    for stage in range(5):
        for kind in range(2):
            small_copy(stage, kind).wait_send()
    exchange.wait()
    decoder_sums[...] = decoder_total[5]
    encoder_sums[...] = encoder_total[5]


def reduce_call(decoder_part, encoder_part, decoder_small, encoder_small, payload):
    blocks = [8, 4, 2, 1]
    buffers = [
        pltpu.VMEM((block, 16, CHUNKS * width * 128), jnp.bfloat16)
        for width in WIDTHS
        for block in blocks
    ]
    return pl.pallas_call(
        reduce_kernel,
        out_shape=(
            jax.ShapeDtypeStruct((16, COLUMNS), jnp.float32),
            jax.ShapeDtypeStruct(decoder_small.shape, jnp.float32),
            jax.ShapeDtypeStruct(encoder_small.shape, jnp.float32),
            jax.ShapeDtypeStruct(payload.shape, payload.dtype),
        ),
        in_specs=[pl.BlockSpec(memory_space=pl.ANY)] * 5,
        out_specs=(
            pl.BlockSpec(memory_space=pltpu.VMEM),
            pl.BlockSpec(memory_space=pltpu.VMEM),
            pl.BlockSpec(memory_space=pltpu.VMEM),
            pl.BlockSpec(memory_space=pl.ANY),
        ),
        scratch_shapes=[pltpu.VMEM((16, 16, COLUMNS), jnp.bfloat16)] * 2
        + buffers
        + buffers
        + [
            pltpu.VMEM((6,) + decoder_small.shape, jnp.float32),
            pltpu.VMEM((6,) + encoder_small.shape, jnp.float32),
            pltpu.VMEM((5,) + decoder_small.shape, jnp.float32),
            pltpu.VMEM((5,) + encoder_small.shape, jnp.float32),
            pltpu.SemaphoreType.DMA((CHUNKS,)),
            pltpu.SemaphoreType.DMA((CHUNKS,)),
            pltpu.SemaphoreType.DMA((CHUNKS,)),
            pltpu.SemaphoreType.DMA((3, 4, CHUNKS)),
            pltpu.SemaphoreType.DMA((3, 4, CHUNKS)),
            pltpu.SemaphoreType.DMA((2,)),
            pltpu.SemaphoreType.DMA((5, 2)),
            pltpu.SemaphoreType.DMA((5, 2)),
            pltpu.SemaphoreType.DMA,
            pltpu.SemaphoreType.DMA,
        ],
        compiler_params=pltpu.CompilerParams(
            collective_id=0, has_side_effects=True, vmem_limit_bytes=58 * 2**20
        ),
        cost_estimate=pl.CostEstimate(
            flops=3 * 16 * COLUMNS * 32, bytes_accessed=4 * 16 * COLUMNS * 32, transcendentals=0
        ),
        name="reduce_gradients",
    )(
        decoder_part.reshape(16, 2, 16, DECODER_COLUMNS),
        encoder_part.reshape(16, 2, 16, ENCODER_COLUMNS),
        decoder_small,
        encoder_small,
        payload,
    )


def dot(a, b):
    return jnp.dot(a, b, preferred_element_type=jnp.float32)


def dot_nt(a, b):
    return lax.dot_general(a, b, (((1,), (1,)), ((), ())), preferred_element_type=jnp.float32)


def dot_tn(a, b):
    return lax.dot_general(a, b, (((0,), (0,)), ((), ())), preferred_element_type=jnp.float32)


def low(value):
    return value.astype(jnp.bfloat16)


def standardize(values):
    centered = values - jnp.mean(values, axis=-1, keepdims=True)
    inverse = lax.rsqrt(jnp.mean(centered * centered, axis=-1, keepdims=True) + 1e-05)
    return centered * inverse, inverse


def norm_back(unit, inverse, gain, grad):
    inner = grad * gain
    return inverse * (
        inner
        - jnp.mean(inner, axis=-1, keepdims=True)
        - unit * jnp.mean(inner * unit, axis=-1, keepdims=True)
    )


def row_sum(values):
    return jnp.sum(values, axis=0, keepdims=True)


def gelu_pair(before):
    half = 0.5 * (1.0 + lax.erf(before * 0.7071067811865476))
    density = jnp.exp(-0.5 * before * before) * 0.3989422804014327
    return before * half, half + before * density


def chip_of(places, sizes, pack):
    end = sizes[pack, 0]
    chip = (places >= end).astype(jnp.int32)
    for slot in range(1, 4):
        end = end + sizes[pack, slot]
        chip = chip + (places >= end).astype(jnp.int32)
    return chip


def iota(shape, dimension):
    return lax.broadcasted_iota(jnp.int32, shape, dimension)


def head_lanes(head):
    return (iota((1, 128), 1) // 64) == head % 2


def pair_lanes(head, base=0):
    return pl.ds(pl.multiple_of(base + head // 2 * 128, 128), 128)


def head_rows(head):
    return pl.ds(pl.multiple_of(head * 64, 64), 64)


def rows_of(tile):
    return pl.ds(pl.multiple_of(tile * TILE, TILE), TILE)


def only(values, lanes):
    return jnp.where(lanes, values, jnp.zeros_like(values))


def store_shards(packed, rows, offset, value):
    shards, count, width = value.shape
    for piece in range(count // 16):
        packed[rows, :, offset + piece * width : offset + (piece + 1) * width] = low(
            value[:, piece * 16 : piece * 16 + 16]
        )
    if count % 16:
        half = width // 2
        start = offset + count // 16 * width
        rest = value[:, count - 8 :]
        packed[rows, :, start : start + half] = low(
            jnp.concatenate([rest[:, :, :half], rest[:, :, half:]], axis=1)
        )


def decoder_kernel(
    sizes, distance, slots_row, slots_column, frequency, sent, cotangent, entry_weight, biases, mask_token,
    gains, shifts, attend, merging, expand, inner, shrink,
    packed, vectors, encoded_grad,
    table, start, normed, mixed, turned, probs, context_turned, context, middle, normed_two, active,
    before_grad, go_low, attention_low, middle_grad, context_grad, key_grad, query_turned, mixed_grad, target, target_sem,
):
    pack = lax.axis_index("section")
    fetch = pltpu.make_async_copy(cotangent.at[pack], target, target_sem)
    fetch.start()
    tiles = start.shape[0] // TILE
    vectors[...] = jnp.zeros_like(vectors)
    packed[:, :, 5888:] = jnp.zeros((32, 16, DECODER_COLUMNS - 5888), jnp.bfloat16)
    large = sizes[pack, 0] == 1024

    def add_row(row, value):
        vectors[row : row + 1, :] += value

    positions = iota((32, 128), 0).astype(jnp.float32)
    for chip in range(4):
        spacing = distance[pack, chip].astype(jnp.float32) / 16.0
        angle = positions * (spacing * frequency[...])
        table[0, chip] = jnp.sin(angle)
        table[1, chip] = jnp.cos(angle)
    entry = low(dot(sent[...], entry_weight[...]) + biases[0:1])

    def validity(tile):
        places = iota((TILE, 1), 0) + tile * TILE
        return (chip_of(places, sizes, pack) < 4).astype(jnp.float32)

    def spread_of(tile):
        return (slots_row[pl.ds(pack, 1)] == iota((TILE, TILE), 0) + tile * TILE).astype(jnp.float32)

    @pl.loop(0, tiles)
    def _(tile):
        rows = rows_of(tile)
        valid = validity(tile)
        spread = spread_of(tile)
        fill = valid * (1.0 - jnp.sum(spread, axis=1, keepdims=True))
        pieces = []
        for kind in range(2):
            wave = table[kind, 0, pl.ds(pl.multiple_of(tile * 8, 8), 8)]
            big = jnp.broadcast_to(wave[:, None], (8, 32, 128)).reshape(TILE, 128)
            wave = table[kind, tile, 0:16]
            own = jnp.broadcast_to(wave[:, None], (16, 16, 128)).reshape(TILE, 128)
            pieces.append(jnp.where(large, big, own))
        for kind in range(2):
            wave = table[kind, 0]
            big = jnp.broadcast_to(wave[None], (8, 32, 128)).reshape(TILE, 128)
            wave = table[kind, tile, 0:16]
            own = jnp.broadcast_to(wave[None], (16, 16, 128)).reshape(TILE, 128)
            pieces.append(jnp.where(large, big, own))
        encoding = jnp.concatenate(pieces, axis=1) * valid
        hidden = dot(low(spread), entry) + fill * mask_token[...] + encoding
        start[rows] = hidden
        add_row(12, row_sum(valid * hidden * hidden))
        add_row(16, row_sum(valid))
        unit, _ = standardize(hidden)
        norm = low(unit * gains[0:1] + shifts[0:1])
        normed[rows] = norm
        mix = dot(norm, attend[...])
        mixed[rows] = low(mix)
        turned[:, rows] = low(mix[:, 256:].T)

    @pl.loop(0, 4 * tiles)
    def _(step):
        head, tile = step // tiles, step % tiles
        rows, lanes = rows_of(tile), head_lanes(head)
        query = only(mixed[rows, pair_lanes(head)], lanes) * jnp.bfloat16(0.125)
        scores = dot_nt(mixed[:, pair_lanes(head, 256)], query)
        own_chip = chip_of(iota((1, TILE), 1) + tile * TILE, sizes, pack)
        key_chip = chip_of(iota((start.shape[0], 1), 0), sizes, pack)
        scores = jnp.where(key_chip == own_chip, scores, NEGATIVE)
        expos = jnp.exp(scores - jnp.max(scores, axis=0, keepdims=True))
        prob = low(expos * (1.0 / jnp.sum(expos, axis=0, keepdims=True)))
        probs[head, :, rows] = prob
        values = turned[pl.ds(pl.multiple_of(256 + head * 64, 64), 64)]
        context_turned[head_rows(head), rows] = dot(values, prob)

    fetch.wait()

    @pl.loop(0, tiles)
    def _(tile):
        rows = rows_of(tile)
        valid = validity(tile)
        mingled = low(context_turned[:, rows].T)
        context[rows] = mingled
        attention = dot(mingled, merging[...]) + biases[1:2]
        add_row(13, row_sum(valid * attention * attention))
        center = start[rows] + attention
        middle[rows] = center
        unit, inverse = standardize(center)
        norm = low(unit * gains[1:2] + shifts[1:2])
        normed_two[rows] = norm
        go = target[rows] * valid
        go_below = low(go)
        go_low[rows] = go_below
        add_row(2, row_sum(go))
        feed = jnp.zeros_like(go)
        norm_grad = jnp.zeros_like(go)
        for part in range(4):
            cols = slice(part * 512, part * 512 + 512)
            before = dot(norm, expand[:, cols]) + inner[part : part + 1]
            value, slope = gelu_pair(before)
            value = low(value)
            active[rows, cols] = value
            feed = feed + dot(value, shrink[cols])
            grad = slope * dot_nt(go_below, shrink[cols])
            grad = low(grad)
            before_grad[rows, cols] = grad
            add_row(8 + part, row_sum(grad.astype(jnp.float32)))
            norm_grad = norm_grad + dot_nt(grad, expand[:, cols])
        feed = feed + biases[2:3]
        add_row(14, row_sum(valid * feed * feed))
        output = center + feed
        add_row(15, row_sum(valid * output * output))
        add_row(5, row_sum(norm_grad * unit))
        add_row(7, row_sum(norm_grad))
        grad = go + norm_back(unit, inverse, gains[1:2], norm_grad)
        middle_grad[rows] = grad
        add_row(1, row_sum(grad))
        below = low(grad)
        attention_low[rows] = below
        context_grad[rows] = low(dot_nt(below, merging[...]))

    key_grad[...] = jnp.zeros_like(key_grad)

    @pl.loop(0, 4 * tiles)
    def _(step):
        head, tile = step // tiles, step % tiles
        rows, lanes = rows_of(tile), head_lanes(head)
        pair = pair_lanes(head)
        prob = probs[head, :, rows]
        outer = only(context_grad[rows, pair], lanes)
        wide = prob.astype(jnp.float32)
        grad = dot_nt(mixed[:, pair_lanes(head, 512)], outer)
        raw = low(wide * (grad - jnp.sum(wide * grad, axis=0, keepdims=True)))
        query = only(mixed[rows, pair], lanes)
        key_grad[0, :, pair] += dot(raw, query)
        key_grad[1, :, pair] += dot(prob, outer)
        query_turned[head_rows(head), rows] = dot(turned[head_rows(head)], raw)

    @pl.loop(0, tiles)
    def _(tile):
        rows = rows_of(tile)
        mix = jnp.concatenate(
            [
                low(query_turned[:, rows].T * 0.125),
                low(key_grad[0, rows] * 0.125),
                low(key_grad[1, rows]),
            ],
            axis=1,
        )
        mixed_grad[rows] = mix
        norm_grad = dot_nt(mix, attend[...])
        unit, inverse = standardize(start[rows])
        add_row(4, row_sum(norm_grad * unit))
        add_row(6, row_sum(norm_grad))
        grad = middle_grad[rows] + norm_back(unit, inverse, gains[0:1], norm_grad)
        valid = validity(tile)
        fill = valid * (1.0 - jnp.sum(spread_of(tile), axis=1, keepdims=True))
        add_row(3, row_sum(fill * grad))
        middle_grad[rows] = grad

    gather = (slots_column[pack] == iota((TILE, start.shape[0]), 1)).astype(jnp.bfloat16)
    entry_grad = dot(gather, low(middle_grad[...]))
    add_row(0, row_sum(entry_grad))
    entry_low = low(entry_grad)
    encoded_grad[...] = low(dot_nt(entry_low, entry_weight[...]))

    store_shards(packed, slice(0, 32), 0, dot_tn(sent[...], entry_low).reshape(32, 24, 512))

    for part in range(2):
        cols = slice(part * 256, part * 256 + 256)
        shards = slice(part * 16, part * 16 + 16)
        store_shards(packed, shards, 768, dot_tn(normed[:, cols], mixed_grad[...]).reshape(16, 16, 768))
        store_shards(
            packed, shards, 1536, dot_tn(attention_low[:, cols], context[...]).reshape(16, 16, 256)
        )
        for quarter in range(4):
            wide = slice(quarter * 512, quarter * 512 + 512)
            store_shards(
                packed,
                shards,
                1792 + quarter * 512,
                dot_tn(normed_two[:, cols], before_grad[:, wide]).reshape(16, 16, 512),
            )

    @pl.loop(0, 8)
    def _(part):
        cols = pl.ds(pl.multiple_of(part * 256, 256), 256)
        store_shards(
            packed,
            pl.ds(part * 4, 4),
            3840,
            dot_tn(active[:, cols], go_low[...]).reshape(4, 64, 512),
        )


def vmem_spec():
    return pl.BlockSpec(memory_space=pltpu.VMEM)


def decoder_call(
    sizes, distance, slots, sent, cotangent, entry_weight, biases, mask_token,
    gains, shifts, attend, merging, expand, inner, shrink,
):
    length = cotangent.shape[1]
    width = 512
    f32, bf16 = jnp.float32, jnp.bfloat16
    quarter = width // 4
    frequency = jnp.exp(-jnp.log(10000.0) * jnp.arange(quarter, dtype=f32) / quarter)[None]
    smem = pl.BlockSpec(memory_space=pltpu.SMEM)
    return pl.pallas_call(
        decoder_kernel,
        out_shape=(
            jax.ShapeDtypeStruct((32, 16, DECODER_COLUMNS), bf16),
            jax.ShapeDtypeStruct((24, width), f32),
            jax.ShapeDtypeStruct((256, 768), bf16),
        ),
        in_specs=[smem, smem] + [vmem_spec()] * 4 + [pl.BlockSpec(memory_space=pl.ANY)] + [vmem_spec()] * 10,
        out_specs=(vmem_spec(), vmem_spec(), vmem_spec()),
        scratch_shapes=[
            pltpu.VMEM((2, 4, 32, 128), f32),
            pltpu.VMEM((length, width), f32),
            pltpu.VMEM((length, width), bf16),
            pltpu.VMEM((length, 768), bf16),
            pltpu.VMEM((512, length), bf16),
            pltpu.VMEM((4, length, length), bf16),
            pltpu.VMEM((256, length), f32),
            pltpu.VMEM((length, 256), bf16),
            pltpu.VMEM((length, width), f32),
            pltpu.VMEM((length, width), bf16),
            pltpu.VMEM((length, 2048), bf16),
            pltpu.VMEM((length, 2048), bf16),
            pltpu.VMEM((length, width), bf16),
            pltpu.VMEM((length, width), bf16),
            pltpu.VMEM((length, width), f32),
            pltpu.VMEM((length, 256), bf16),
            pltpu.VMEM((2, length, 256), f32),
            pltpu.VMEM((256, length), f32),
            pltpu.VMEM((length, 768), bf16),
            pltpu.VMEM((length, width), f32),
            pltpu.SemaphoreType.DMA,
        ],
        compiler_params=pltpu.CompilerParams(vmem_limit_bytes=60 * 2**20),
        name="decoder_block",
    )(
        sizes, distance, slots, slots[..., None], frequency, sent, cotangent, entry_weight, biases,
        mask_token[None], gains, shifts, attend, merging, expand, inner.reshape(4, 512), shrink,
    )


def encoder_forward_kernel(
    sizes, tokens, gains, shifts, biases, attend, merging, expand, inner, shrink,
    sent, vectors, normed, mixed, turned, probs, context, middle, normed_two, active, slope,
    hidden, context_turned, fetch_sem,
):
    pack = lax.axis_index("section")
    fetch = pltpu.make_async_copy(tokens.at[pack], hidden, fetch_sem)
    fetch.start()
    vectors[...] = jnp.zeros_like(vectors)
    places = 4 * iota((TILE, 1), 0)
    key_chip = chip_of(places, sizes, pack)
    own_chip = chip_of(4 * iota((1, TILE), 1), sizes, pack)
    valid = (key_chip < 4).astype(jnp.float32)
    fetch.wait()
    values = hidden[...]
    vectors[10:11] = row_sum(valid * values * values)
    unit, _ = standardize(values)
    norm = low(unit * gains[0:1] + shifts[0:1])
    normed[...] = norm
    for part in range(3):
        cols = slice(part * 768, part * 768 + 768)
        mix = dot(norm, attend[:, cols])
        mixed[:, cols] = low(mix)
        if part:
            turned[(part - 1) * 768 : part * 768] = low(mix.T)

    @pl.loop(0, 6)
    def _(pair):
        lanes = pl.ds(pl.multiple_of(pair * 128, 128), 128)
        keys = mixed[:, pl.ds(pl.multiple_of(768 + pair * 128, 128), 128)]
        for half in range(2):
            query = only(mixed[:, lanes], head_lanes(half)) * jnp.bfloat16(0.125)
            scores = jnp.where(key_chip == own_chip, dot_nt(keys, query), NEGATIVE)
            expos = jnp.exp(scores - jnp.max(scores, axis=0, keepdims=True))
            prob = low(expos * (1.0 / jnp.sum(expos, axis=0, keepdims=True)))
            probs[pair * 2 + half] = prob
            rows = pl.ds(pl.multiple_of(pair * 128 + half * 64, 64), 64)
            context_turned[rows] = dot(
                turned[pl.ds(pl.multiple_of(768 + pair * 128 + half * 64, 64), 64)], prob
            )

    mingled = low(context_turned[...].T)
    context[...] = mingled
    attention = dot(mingled, merging[...]) + biases[0:1]
    vectors[11:12] = row_sum(valid * attention * attention)
    center = hidden[...] + attention
    middle[...] = center
    unit, _ = standardize(center)
    norm = low(unit * gains[1:2] + shifts[1:2])
    normed_two[...] = norm
    feed = jnp.zeros_like(center)
    for part in range(4):
        cols = slice(part * 768, part * 768 + 768)
        value, slant = gelu_pair(dot(norm, expand[:, cols]) + inner[part : part + 1])
        value = low(value)
        active[:, cols] = value
        slope[:, cols] = slant
        feed = feed + dot(value, shrink[cols])
    feed = feed + biases[1:2]
    vectors[12:13] = row_sum(valid * feed * feed)
    output = center + feed
    vectors[13:14] = row_sum(valid * output * output)
    vectors[14:15] = jnp.broadcast_to(row_sum(valid), (1, 768))
    sent[...] = low(output)


def encoder_forward_call(sizes, tokens, gains, shifts, biases, attend, merging, expand, inner, shrink):
    f32, bf16 = jnp.float32, jnp.bfloat16
    smem = pl.BlockSpec(memory_space=pltpu.SMEM)
    shapes = (
        ((256, 768), bf16),
        ((16, 768), f32),
        ((256, 768), bf16),
        ((256, 2304), bf16),
        ((1536, 256), bf16),
        ((12, 256, 256), bf16),
        ((256, 768), bf16),
        ((256, 768), f32),
        ((256, 768), bf16),
        ((256, 3072), bf16),
        ((256, 3072), f32),
    )
    return pl.pallas_call(
        encoder_forward_kernel,
        out_shape=tuple(jax.ShapeDtypeStruct(*shape) for shape in shapes),
        in_specs=[smem, pl.BlockSpec(memory_space=pl.ANY)] + [vmem_spec()] * 8,
        out_specs=(vmem_spec(),) * len(shapes),
        scratch_shapes=[
            pltpu.VMEM((256, 768), f32),
            pltpu.VMEM((768, 256), f32),
            pltpu.SemaphoreType.DMA,
        ],
        compiler_params=pltpu.CompilerParams(vmem_limit_bytes=60 * 2**20),
        name="encoder_forward",
    )(sizes, tokens, gains, shifts, biases, attend, merging, expand, inner.reshape(4, 768), shrink)


def encoder_backward_kernel(
    tokens, encoded_grad, sums, normed, mixed, turned, probs, context, middle, normed_two, active, slope,
    gains, attend, merging, expand, shrink,
    packed, vectors, tokens_grad, payload,
    hidden, before_grad, context_grad, key_grad, query_turned, mixed_grad, fetch_sem,
):
    pack = lax.axis_index("section")
    fetch = pltpu.make_async_copy(tokens.at[pack], hidden, fetch_sem)
    fetch.start()
    vectors[...] = sums[...]
    go_low = encoded_grad[...]
    go = go_low.astype(jnp.float32)
    vectors[1:2] = row_sum(go)
    norm_grad = jnp.zeros_like(go)
    for part in range(4):
        cols = slice(part * 768, part * 768 + 768)
        grad = low(slope[:, cols] * dot_nt(go_low, shrink[cols]))
        before_grad[:, cols] = grad
        vectors[6 + part : 7 + part] = row_sum(grad.astype(jnp.float32))
        norm_grad = norm_grad + dot_nt(grad, expand[:, cols])
    unit, inverse = standardize(middle[...])
    vectors[3:4] = row_sum(norm_grad * unit)
    vectors[5:6] = row_sum(norm_grad)
    grad = go + norm_back(unit, inverse, gains[1:2], norm_grad)
    vectors[0:1] = row_sum(grad)
    tokens_grad[...] = grad
    attention_low = low(grad)
    context_grad[...] = low(dot_nt(attention_low, merging[...]))

    @pl.loop(0, 6)
    def _(pair):
        lanes = pl.ds(pl.multiple_of(pair * 128, 128), 128)
        values = mixed[:, pl.ds(pl.multiple_of(1536 + pair * 128, 128), 128)]
        keys_total = jnp.zeros((TILE, 128), jnp.float32)
        values_total = jnp.zeros((TILE, 128), jnp.float32)
        for half in range(2):
            prob = probs[pair * 2 + half]
            outer = only(context_grad[:, lanes], head_lanes(half))
            query = only(mixed[:, lanes], head_lanes(half))
            wide = prob.astype(jnp.float32)
            grad = dot_nt(values, outer)
            raw = low(wide * (grad - jnp.sum(wide * grad, axis=0, keepdims=True)))
            keys_total = keys_total + dot(raw, query)
            values_total = values_total + dot(prob, outer)
            rows = pl.ds(pl.multiple_of(pair * 128 + half * 64, 64), 64)
            query_turned[rows] = dot(turned[rows], raw)
        key_grad[0, :, lanes] = keys_total
        key_grad[1, :, lanes] = values_total

    mixed_grad[:, 0:768] = low(query_turned[...].T * 0.125)
    mixed_grad[:, 768:1536] = low(key_grad[0] * 0.125)
    mixed_grad[:, 1536:2304] = low(key_grad[1])
    norm_grad = dot_nt(mixed_grad[...], attend[...])
    fetch.wait()
    unit, inverse = standardize(hidden[...])
    vectors[2:3] = row_sum(norm_grad * unit)
    vectors[4:5] = row_sum(norm_grad)
    grad = tokens_grad[...] + norm_back(unit, inverse, gains[0:1], norm_grad)
    tokens_grad[...] = grad
    payload[...] = jnp.where(pack == 0, go, grad).astype(jnp.bfloat16)

    shards = slice(0, 32)
    for part in range(4):
        cols = slice(part * 768, part * 768 + 768)
        store_shards(
            packed, shards, part * 1152, dot_tn(normed_two[...], before_grad[:, cols]).reshape(32, 24, 768)
        )
        store_shards(
            packed,
            slice(part * 8, part * 8 + 8),
            4608,
            dot_tn(active[:, cols], go_low).reshape(8, 96, 768),
        )
    store_shards(packed, shards, 9216, dot_tn(attention_low, context[...]).reshape(32, 24, 768))
    for part in range(3):
        cols = slice(part * 768, part * 768 + 768)
        store_shards(
            packed,
            shards,
            10368 + part * 1152,
            dot_tn(normed[...], mixed_grad[:, cols]).reshape(32, 24, 768),
        )


def encoder_backward_call(tokens, encoded_grad, kept, gains, attend, merging, expand, shrink):
    f32, bf16 = jnp.float32, jnp.bfloat16
    return pl.pallas_call(
        encoder_backward_kernel,
        out_shape=(
            jax.ShapeDtypeStruct((32, 16, ENCODER_COLUMNS), bf16),
            jax.ShapeDtypeStruct((16, 768), f32),
            jax.ShapeDtypeStruct((256, 768), f32),
            jax.ShapeDtypeStruct((256, 768), bf16),
        ),
        in_specs=[pl.BlockSpec(memory_space=pl.ANY)] + [vmem_spec()] * 16,
        out_specs=(vmem_spec(),) * 4,
        scratch_shapes=[
            pltpu.VMEM((256, 768), f32),
            pltpu.VMEM((256, 3072), bf16),
            pltpu.VMEM((256, 768), bf16),
            pltpu.VMEM((2, 256, 768), f32),
            pltpu.VMEM((768, 256), f32),
            pltpu.VMEM((256, 2304), bf16),
            pltpu.SemaphoreType.DMA,
        ],
        compiler_params=pltpu.CompilerParams(vmem_limit_bytes=60 * 2**20),
        name="encoder_backward",
    )(tokens, encoded_grad, *kept, gains, attend, merging, expand, shrink)


ENTRY, ATTEND, MERGE, EXPAND, SHRINK = (0, 24, 512), (768, 16, 768), (1536, 16, 256), (1792, 16, 2048), (3840, 64, 512)
ENCODER_EXPAND = tuple((part * 1152, 24, 768) for part in range(4))
ENCODER_SHRINK, ENCODER_MERGE = (4608, 96, 768), (9216, 24, 768)
ENCODER_ATTEND = tuple((10368 + part * 1152, 24, 768) for part in range(3))


def unpack(packed, place, base=0):
    offset, count, width = place
    offset = offset + base
    pieces = [
        packed[..., offset + i * width : offset + (i + 1) * width] for i in range(count // 16)
    ]
    if count % 16:
        offset = offset + count // 16 * width
        half = width // 2
        rest = packed[..., offset : offset + half]
        pieces.append(jnp.concatenate([rest[..., :8, :], rest[..., 8:, :]], axis=-1))
    return pieces[0] if len(pieces) == 1 else jnp.concatenate(pieces, axis=-2)


def finish_kernel(
    summed, decoder_sums, encoder_sums, arrived, tokens_grad, encoded_grad,
    boundary, statistics, e_gains, e_shifts, e_biases, e_attend, e_merge, e_expand, e_inner, e_shrink,
    d_entry, d_biases, mask_grad, d_gains, d_shifts, d_attend, d_merge, d_expand, d_inner, d_shrink,
):
    section = lax.axis_index("section")
    number = section * lax.axis_size("dp") + lax.axis_index("dp")

    @pl.when(section == 0)
    def _():
        boundary[0, 0] = tokens_grad[...]
        boundary[0, 1] = arrived[...].astype(jnp.float32)

    @pl.when(section == 1)
    def _():
        boundary[0, 0] = arrived[...].astype(jnp.float32)
        boundary[0, 1] = encoded_grad[...].astype(jnp.float32)

    def own(rows, count):
        width = rows.shape[1]
        return pltpu.roll(rows, width - number * count, axis=1)[:, :count]

    def own_line(rows, count):
        each = rows.shape[1] // count
        turned = pltpu.roll(rows, rows.shape[1] - number % each * count, axis=1)
        turned = jnp.sum(
            jnp.where(iota((rows.shape[0], 1), 0) == number // each, turned, 0.0),
            axis=0,
            keepdims=True,
        )
        return turned[:, :count]

    lane = iota((1, 128), 1)
    values = jnp.zeros((1, 128), jnp.float32)
    for sums, first, count_row, base in ((encoder_sums, 10, 14, 0), (decoder_sums, 12, 16, 4)):
        scale = 1.0 / (sums[count_row : count_row + 1, 0:1] * sums.shape[1])
        for i in range(4):
            value = jnp.sum(sums[first + i : first + i + 1, :], axis=1, keepdims=True) * scale
            values = jnp.where(lane == base + i, value, values)
    statistics[...] = jnp.sqrt(values)[:, :8]
    rows = encoder_sums[0:8]
    rows = own(rows, 24)
    e_biases[...] = rows[0:2]
    e_gains[...] = rows[2:4]
    e_shifts[...] = rows[4:6]
    e_inner[...] = own_line(encoder_sums[6:10], 96)
    rows = own(decoder_sums[0:8], 16)
    d_biases[...] = rows[0:3]
    mask_grad[...] = rows[3:4]
    d_gains[...] = rows[4:6]
    d_shifts[...] = rows[6:8]
    d_inner[...] = own_line(decoder_sums[8:12], 64)

    def upright(value):
        padding = jnp.zeros((128 - value.shape[0], value.shape[1]), jnp.float32)
        return jnp.concatenate([value, padding], axis=0).T[:, : value.shape[0]]

    d_entry[...] = unpack(summed, ENTRY)
    d_attend[...] = unpack(summed, ATTEND)
    d_merge[...] = upright(unpack(summed, MERGE))
    d_expand[...] = unpack(summed, EXPAND)
    d_shrink[...] = unpack(summed, SHRINK)
    for target, places in ((e_expand, ENCODER_EXPAND), (e_attend, ENCODER_ATTEND)):
        for part, place in enumerate(places):
            target[:, part * 768 : part * 768 + 768] = unpack(summed, place, DECODER_COLUMNS)
    e_shrink[...] = unpack(summed, ENCODER_SHRINK, DECODER_COLUMNS)
    e_merge[...] = upright(unpack(summed, ENCODER_MERGE, DECODER_COLUMNS))


def finish_call(summed, decoder_sums, encoder_sums, arrived, tokens_grad, encoded_grad):
    shapes = (
        (1, 2, 256, 768), (1, 8), (2, 24), (2, 24), (2, 24), (24, 2304), (768, 24), (24, 3072), (1, 96), (96, 768),
        (24, 512), (3, 16), (1, 16), (2, 16), (2, 16), (16, 768), (256, 16), (16, 2048), (1, 64), (64, 512),
    )
    outs = list(
        pl.pallas_call(
            finish_kernel,
            out_shape=tuple(jax.ShapeDtypeStruct(shape, jnp.float32) for shape in shapes),
            in_specs=[vmem_spec()] * 6,
            out_specs=(vmem_spec(),) * len(shapes),
            compiler_params=pltpu.CompilerParams(vmem_limit_bytes=40 * 2**20),
            name="finish",
        )(summed, decoder_sums, encoder_sums, arrived, tokens_grad, encoded_grad)
    )
    for line in (1, 8, 12, 18):
        outs[line] = outs[line].reshape(-1)
    return tuple(outs)


def scatter_sum(member, share_dim):
    return lax.psum_scatter(
        member, ("section", "dp"), scatter_dimension=share_dim, tiled=True
    )


def finish_generic(decoder_part, encoder_part, decoder_sums, encoder_sums, payload, tokens_grad, encoded_grad):
    section = lax.axis_index("section")

    def whole(packed, *places):
        blocks = [unpack(packed, place).reshape(32 * place[1], place[2]) for place in places]
        return scatter_sum(jnp.concatenate(blocks, axis=1).astype(jnp.float32), 0)

    def line(value):
        return scatter_sum(value, value.ndim - 1)

    arrived = lax.ppermute(payload, "section", [(0, 1), (1, 0)]).astype(jnp.float32)
    boundary = jnp.where(
        section == 0,
        jnp.stack([tokens_grad, arrived]),
        jnp.stack([arrived, encoded_grad.astype(jnp.float32)]),
    )
    sums = jnp.concatenate(
        [jnp.sum(encoder_sums[10:14], axis=1), jnp.sum(decoder_sums[12:16], axis=1)]
    )
    sums, counts = lax.psum((sums, (encoder_sums[14, 0], decoder_sums[16, 0])), ("section", "dp"))
    scales = jnp.concatenate([jnp.full((4,), counts[0] * DE), jnp.full((4,), counts[1] * DD)])
    return (
        boundary[None],
        jnp.sqrt(sums / scales),
        line(encoder_sums[2:4]),
        line(encoder_sums[4:6]),
        line(encoder_sums[0:2]),
        whole(encoder_part, *ENCODER_ATTEND),
        whole(encoder_part, ENCODER_MERGE).T,
        whole(encoder_part, *ENCODER_EXPAND),
        line(encoder_sums[6:10].reshape(-1)),
        whole(encoder_part, ENCODER_SHRINK),
        whole(decoder_part, ENTRY),
        line(decoder_sums[0:3]),
        line(decoder_sums[3]),
        line(decoder_sums[4:6]),
        line(decoder_sums[6:8]),
        whole(decoder_part, ATTEND),
        whole(decoder_part, MERGE).T,
        whole(decoder_part, EXPAND),
        line(decoder_sums[8:12].reshape(-1)),
        whole(decoder_part, SHRINK),
    )


def body(
    visible_tokens,
    cotangent,
    chip_sizes,
    ground_distance,
    visible_slots,
    encoder_gains,
    encoder_shifts,
    encoder_biases,
    encoder_attend,
    encoder_merge,
    encoder_expand,
    encoder_inner,
    encoder_shrink,
    decoder_entry,
    decoder_biases,
    mask_token,
    decoder_gains,
    decoder_shifts,
    decoder_attend,
    decoder_merge,
    decoder_widen_weight,
    decoder_inner,
    decoder_shrink,
):
    sent, sums, *kept = encoder_forward_call(
        chip_sizes, visible_tokens, encoder_gains, encoder_shifts, encoder_biases,
        encoder_attend, encoder_merge, encoder_expand, encoder_inner, encoder_shrink,
    )
    decoder_part, decoder_sums, encoded_grad = decoder_call(
        chip_sizes, ground_distance, visible_slots, sent, cotangent, decoder_entry, decoder_biases, mask_token,
        decoder_gains, decoder_shifts, decoder_attend, decoder_merge, decoder_widen_weight, decoder_inner,
        decoder_shrink,
    )
    encoder_part, encoder_sums, tokens_grad, payload = encoder_backward_call(
        visible_tokens, encoded_grad, (sums, *kept),
        encoder_gains, encoder_attend, encoder_merge, encoder_expand, encoder_shrink,
    )
    if (lax.axis_size("section"), lax.axis_size("dp")) == (2, 16):
        summed, decoder_sums, encoder_sums, arrived = reduce_call(
            decoder_part, encoder_part, decoder_sums, encoder_sums, payload
        )
        return finish_call(summed, decoder_sums, encoder_sums, arrived, tokens_grad, encoded_grad)
    return finish_generic(
        decoder_part, encoder_part, decoder_sums, encoder_sums, payload, tokens_grad, encoded_grad
    )


def solution(mesh):
    in_specs = (
        P("dp", None, None),
        P("dp", None, None),
        P("dp", None),
        P("dp", None),
        P("dp", None),
        P(),
        P(),
        P(),
        P(),
        P(),
        P(),
        P(),
        P(),
        P(),
        P(),
        P(),
        P(),
        P(),
        P(),
        P(),
        P(),
        P(),
        P(),
    )
    out_specs = (
        P("section", "dp", None, None),
        P(),
        P(None, ("section", "dp")),
        P(None, ("section", "dp")),
        P(None, ("section", "dp")),
        P(("section", "dp"), None),
        P(None, ("section", "dp")),
        P(("section", "dp"), None),
        P(("section", "dp")),
        P(("section", "dp"), None),
        P(("section", "dp"), None),
        P(None, ("section", "dp")),
        P(("section", "dp")),
        P(None, ("section", "dp")),
        P(None, ("section", "dp")),
        P(("section", "dp"), None),
        P(None, ("section", "dp")),
        P(("section", "dp"), None),
        P(("section", "dp")),
        P(("section", "dp"), None),
    )
    return jax.shard_map(body, mesh=mesh, in_specs=in_specs, out_specs=out_specs, check_vma=False)
```

```python
import functools
import types

import jax
import jax.numpy as jnp
import numpy as np
from jax import lax
from jax.experimental import pallas as pl
from jax.experimental.pallas import tpu as pltpu
from jax.sharding import PartitionSpec as P

DE = 768
DD = 512
TILE = 256
NEGATIVE = -1e30
F32, BF16 = jnp.float32, jnp.bfloat16
MESH_ID = pl.DeviceIdType.MESH

CANON = ("x", "z2", "z1", "y")
ROUTES = (("x", "y", "z1", "z2"), ("y", "x", "z1", "z2"), ("z1", "z2", "x", "y"))
WIDTHS = (4, 5, 3)
OFFSETS = (0, 4, 9)
SPAN = 128 * sum(WIDTHS)
DECODER_CHUNKS = 3
CHUNKS = 10
RING = 3

DECODER_EXPAND, DECODER_SHRINK, DECODER_MERGE = (0, 16, 2048), (2048, 64, 512), (4096, 16, 256)
ENTRY, DECODER_ATTEND = (0, 24, 512), (768, 16, 768)
ENCODER_SHRINK = tuple((SPAN * (1 + part), 96, 256) for part in range(3))
ENCODER_EXPAND = tuple((SPAN * (4 + part), 24, 1024) for part in range(3))
ENCODER_ATTEND = ((SPAN * 7, 24, 1024), (SPAN * 8, 24, 1024), (SPAN * 9, 24, 256))
ENCODER_MERGE = (SPAN * 9 + 384, 24, 768)


def dot(a, b):
    return jnp.dot(a, b, preferred_element_type=F32)


def dot_nt(a, b):
    return lax.dot_general(a, b, (((1,), (1,)), ((), ())), preferred_element_type=F32)


def dot_tn(a, b):
    return lax.dot_general(a, b, (((0,), (0,)), ((), ())), preferred_element_type=F32)


def low(value):
    return value.astype(BF16)


def standardize(values):
    centered = values - jnp.mean(values, axis=-1, keepdims=True)
    inverse = lax.rsqrt(jnp.mean(centered * centered, axis=-1, keepdims=True) + 1e-05)
    return centered * inverse, inverse


def norm_back(unit, inverse, gain, grad):
    inner = grad * gain
    return inverse * (
        inner
        - jnp.mean(inner, axis=-1, keepdims=True)
        - unit * jnp.mean(inner * unit, axis=-1, keepdims=True)
    )


def row_sum(values):
    return jnp.sum(values, axis=0, keepdims=True)


def gelu_pair(before):
    half = 0.5 * (1.0 + lax.erf(before * 0.7071067811865476))
    density = jnp.exp(-0.5 * before * before) * 0.3989422804014327
    return before * half, half + before * density


def chip_of(places, sizes, pack):
    end = sizes[pack, 0]
    chip = (places >= end).astype(jnp.int32)
    for slot in range(1, 4):
        end = end + sizes[pack, slot]
        chip = chip + (places >= end).astype(jnp.int32)
    return chip


def iota(shape, dimension):
    return lax.broadcasted_iota(jnp.int32, shape, dimension)


def aligned(start, size, unit):
    return pl.ds(pl.multiple_of(start, unit), size)


def pair_lanes(pair, base=0):
    return aligned(base + pair * 128, 128, 128)


def head_rows(pair, half, base=0):
    return aligned(base + pair * 128 + half * 64, 64, 64)


def rows_of(tile):
    return aligned(tile * TILE, TILE, TILE)


def only(values, half):
    return jnp.where(iota((1, 128), 1) // 64 == half, values, jnp.zeros_like(values))


def fetch(pairs, sems):
    copies = [
        pltpu.make_async_copy(source, target, sems.at[i]) for i, (source, target) in enumerate(pairs)
    ]
    for copy in copies:
        copy.start()
    return copies


def store_packed(put, first, place, value):
    offset, count, width = place
    value = value.reshape(-1, count, width)
    shards = slice(first, first + value.shape[0]) if isinstance(first, int) else pl.ds(first, value.shape[0])
    for piece in range(count // 16):
        put(shards, offset + piece * width, value[:, piece * 16 : piece * 16 + 16])
    if count % 16:
        half = width // 2
        rest = value[:, count - 8 :]
        rest = jnp.concatenate([rest[:, :, :half], rest[:, :, half:]], axis=1)
        put(shards, offset + count // 16 * width, rest)


def halves(shards, value):
    pairs = value.reshape(value.shape[0] // 2, 2, *value.shape[1:])
    if isinstance(shards, slice):
        return slice(shards.start // 2, shards.stop // 2), pairs[:, 0], pairs[:, 1]
    return pl.ds(shards.start // 2, shards.size // 2), pairs[:, 0], pairs[:, 1]


def place_of(names, bits):
    index = 0
    for name in names:
        index = index * 2 + bits[name]
    return index


def left_after(route, stage):
    return tuple(name for name in CANON if name not in route[:stage])


def choices(names):
    for number in range(2 ** len(names)):
        yield {name: (number >> (len(names) - 1 - i)) & 1 for i, name in enumerate(names)}


def neighbours():
    section = lax.axis_index("section")
    data = lax.axis_index("dp")
    mine = {"x": section, "c": data % 2, "y": data // 2 % 2, "z1": data // 4 % 2, "z2": data // 8 % 2}
    partner = {"x": (1 - section, data)}
    for name, step in {"c": 1, "y": 2, "z1": 4, "z2": 8}.items():
        partner[name] = (section, data + step * (1 - 2 * mine[name]))
    return mine, partner


def greet(partner):
    barrier = pltpu.get_barrier_semaphore()
    for name in ("c",) + CANON:
        pl.semaphore_signal(barrier, inc=1, device_id=partner[name], device_id_type=MESH_ID)


def await_greetings():
    pl.semaphore_wait(pltpu.get_barrier_semaphore(), 5)


def remote(source, target, send, recv, device):
    return pltpu.make_async_remote_copy(
        src_ref=source,
        dst_ref=target,
        send_sem=send,
        recv_sem=recv,
        device_id=device,
        device_id_type=MESH_ID,
    )


def reducer(chunks, slots, mine, partner, out, refs):
    own, staging, first = refs[:3]
    sent, got = refs[3:15], refs[15:27]
    first_send, first_recv, send_sem, recv_sem = refs[27:31]

    def span(chunk):
        return aligned(chunk * SPAN, SPAN, 128)

    def first_copy(chunk, source=None):
        if source is None:
            source = staging.at[:, :, span(chunk % slots)]
        return remote(
            source, first.at[:, :, span(chunk)], first_send.at[chunk], first_recv.at[chunk], partner["c"]
        )

    def columns(route, slot):
        return aligned(slot * (WIDTHS[route] * 128), WIDTHS[route] * 128, 128)

    def whole(route, chunk):
        return aligned(chunk * SPAN + OFFSETS[route] * 128, WIDTHS[route] * 128, 128)

    def stage_copy(route, stage, chunk):
        return remote(
            sent[route * 4 + stage].at[:, :, columns(route, chunk % RING)],
            got[route * 4 + stage].at[:, :, columns(route, chunk)],
            send_sem.at[route, stage, chunk],
            recv_sem.at[route, stage, chunk],
            partner[ROUTES[route][stage]],
        )

    def total(route, stage, chunk, bits):
        spot = place_of(CANON, bits)
        cols = whole(route, chunk)
        value = own[spot, :, cols].astype(F32) + first[spot, :, cols].astype(F32)
        for earlier in range(stage):
            names = left_after(ROUTES[route], earlier + 1)
            piece = got[route * 4 + earlier][place_of(names, bits), :, columns(route, chunk)]
            value = value + piece.astype(F32)
        return value

    def advance(route, stage, chunk):
        path = ROUTES[route]
        if stage:
            stage_copy(route, stage - 1, chunk).wait_recv()
        if stage == 4:
            out[:, whole(route, chunk)] = total(route, 4, chunk, mine)
            return

        @pl.when(chunk >= RING)
        def _():
            stage_copy(route, stage, chunk - RING).wait_send()

        names = left_after(path, stage + 1)
        for free in choices(names):
            bits = dict(mine)
            bits[path[stage]] = 1 - mine[path[stage]]
            bits.update(free)
            value = total(route, stage, chunk, bits)
            sent[route * 4 + stage][place_of(names, free), :, columns(route, chunk % RING)] = low(value)
        stage_copy(route, stage, chunk).start()

    def turn(number):
        for stage in range(4, -1, -1):
            chunk = number - stage

            @pl.when((chunk >= 0) & (chunk < chunks))
            def _(stage=stage, chunk=chunk):
                if stage == 0:
                    first_copy(chunk).wait_recv()
                for route in range(3):
                    advance(route, stage, chunk)

    def put(shards, column, value):
        shards, even, odd = halves(shards, value)
        width = value.shape[2]
        chunk = column // SPAN
        for start in range(column, column + width, SPAN):
            assert start // SPAN == chunk or slots == chunks
        kept = jnp.where(mine["c"] == 0, even, odd)
        given = jnp.where(mine["c"] == 0, odd, even)
        own[shards, :, column : column + width] = low(kept)
        start = column if slots == chunks else chunk % slots * SPAN + column % SPAN
        staging[shards, :, start : start + width] = low(given)

    def release(chunk):
        if chunk >= slots:
            first_copy(chunk - slots).wait_send()

    def close(released):
        for chunk in range(released, chunks):
            first_copy(chunk).wait_send()
        for chunk in range(chunks - RING, chunks):
            for route in range(3):
                for stage in range(4):
                    stage_copy(route, stage, chunk).wait_send()

    return types.SimpleNamespace(
        own=own, span=span, first_copy=first_copy, turn=turn, put=put, release=release, close=close
    )


def reducer_scratch(chunks, slots):
    stages = [(width, block) for width in WIDTHS for block in (8, 4, 2, 1)]
    return (
        [
            pltpu.VMEM((16, 16, chunks * SPAN), BF16),
            pltpu.VMEM((16, 16, slots * SPAN), BF16),
            pltpu.VMEM((16, 16, chunks * SPAN), BF16),
        ]
        + [pltpu.VMEM((block, 16, RING * width * 128), BF16) for width, block in stages]
        + [pltpu.VMEM((block, 16, chunks * width * 128), BF16) for width, block in stages]
        + [
            pltpu.SemaphoreType.DMA((chunks,)),
            pltpu.SemaphoreType.DMA((chunks,)),
            pltpu.SemaphoreType.DMA((3, 4, chunks)),
            pltpu.SemaphoreType.DMA((3, 4, chunks)),
        ]
    )


REDUCER_REFS = 31


def put_into(parts):
    def put(shards, column, value):
        shards, even, odd = halves(shards, value)
        parts[0, shards, :, column : column + value.shape[2]] = low(even)
        parts[1, shards, :, column : column + value.shape[2]] = low(odd)

    return put


def vmem_spec():
    return pl.BlockSpec(memory_space=pltpu.VMEM)


def any_spec():
    return pl.BlockSpec(memory_space=pl.ANY)


def smem_spec():
    return pl.BlockSpec(memory_space=pltpu.SMEM)


def encoder_forward_kernel(
    sizes, gains, shifts, biases, inner, tokens, attend_far, merging_far, expand_far, shrink_far,
    sent, vectors, *refs,
):
    far = refs[:9]
    normed, mixed, turned, probs, context, middle, normed_two, active, slope = refs[9:18]
    hidden, attend, merging, expand, shrink, context_turned, load_sem, save_sem = refs[18:]
    pack = lax.axis_index("section")
    loads = fetch(
        [
            (tokens.at[pack], hidden),
            *[(attend_far.at[:, i * 768 : i * 768 + 768], attend.at[:, i * 768 : i * 768 + 768]) for i in range(3)],
            (merging_far, merging),
            *[(expand_far.at[:, i * 1024 : i * 1024 + 1024], expand.at[:, i * 1024 : i * 1024 + 1024]) for i in range(3)],
            *[(shrink_far.at[i * 1024 : i * 1024 + 1024], shrink.at[i * 1024 : i * 1024 + 1024]) for i in range(3)],
        ],
        load_sem,
    )
    saves = []

    def save(*numbers):
        for number in numbers:
            copy = pltpu.make_async_copy(refs[9 + number], far[number], save_sem.at[number])
            copy.start()
            saves.append(copy)

    vectors[...] = jnp.zeros_like(vectors)
    key_chip = chip_of(4 * iota((TILE, 1), 0), sizes, pack)
    own_chip = chip_of(4 * iota((1, TILE), 1), sizes, pack)
    valid = (key_chip < 4).astype(F32)
    loads[0].wait()
    values = hidden[...]
    vectors[10:11, :768] = row_sum(valid * values * values)
    unit, _ = standardize(values)
    norm = low(unit * gains[0:1] + shifts[0:1])
    normed[...] = norm
    for part in range(3):
        cols = slice(part * 768, part * 768 + 768)
        loads[1 + part].wait()
        mix = dot(norm, attend[:, cols])
        mixed[:, cols] = low(mix)
        if part:
            turned[(part - 1) * 768 : part * 768] = low(mix.T)
    save(0, 1, 2)

    @pl.loop(0, 6)
    def _(pair):
        keys = mixed[:, pair_lanes(pair, 768)]
        for half in range(2):
            query = only(mixed[:, pair_lanes(pair)], half) * BF16(0.125)
            scores = jnp.where(key_chip == own_chip, dot_nt(keys, query), NEGATIVE)
            expos = jnp.exp(scores - jnp.max(scores, axis=0, keepdims=True))
            prob = low(expos * (1.0 / jnp.sum(expos, axis=0, keepdims=True)))
            probs[pair * 2 + half] = prob
            context_turned[head_rows(pair, half)] = dot(turned[head_rows(pair, half, 768)], prob)

    mingled = low(context_turned[...].T)
    context[...] = mingled
    save(3, 4)
    loads[4].wait()
    attention = dot(mingled, merging[...]) + biases[0:1]
    vectors[11:12, :768] = row_sum(valid * attention * attention)
    center = hidden[...] + attention
    middle[...] = center
    unit, _ = standardize(center)
    norm = low(unit * gains[1:2] + shifts[1:2])
    normed_two[...] = norm
    save(5, 6)
    feed = jnp.zeros_like(center)
    for part in range(3):
        cols = slice(part * 1024, part * 1024 + 1024)
        loads[5 + part].wait()
        value, slant = gelu_pair(dot(norm, expand[:, cols]) + inner[:, cols])
        value = low(value)
        active[:, cols] = value
        slope[part] = slant
        loads[8 + part].wait()
        feed = feed + dot(value, shrink[cols])
    save(7, 8)
    feed = feed + biases[1:2]
    vectors[12:13, :768] = row_sum(valid * feed * feed)
    output = center + feed
    vectors[13:14, :768] = row_sum(valid * output * output)
    vectors[14:15, :768] = jnp.broadcast_to(row_sum(valid), (1, 768))
    sent[...] = low(output)
    for copy in saves:
        copy.wait()


def encoder_forward_call(sizes, tokens, gains, shifts, biases, attend, merging, expand, inner, shrink):
    shapes = (
        ((256, 768), BF16),
        ((256, 2304), BF16),
        ((1536, 256), BF16),
        ((12, 256, 256), BF16),
        ((256, 768), BF16),
        ((256, 768), F32),
        ((256, 768), BF16),
        ((256, 3072), BF16),
        ((3, 256, 1024), F32),
    )
    return pl.pallas_call(
        encoder_forward_kernel,
        out_shape=(jax.ShapeDtypeStruct((256, 768), BF16), jax.ShapeDtypeStruct((16, 1024), F32))
        + tuple(jax.ShapeDtypeStruct(*shape) for shape in shapes),
        in_specs=[smem_spec()] + [vmem_spec()] * 4 + [any_spec()] * 5,
        out_specs=(vmem_spec(),) * 2 + (any_spec(),) * len(shapes),
        scratch_shapes=[pltpu.VMEM(*shape) for shape in shapes]
        + [
            pltpu.VMEM((256, 768), F32),
            pltpu.VMEM(attend.shape, BF16),
            pltpu.VMEM(merging.shape, BF16),
            pltpu.VMEM(expand.shape, BF16),
            pltpu.VMEM(shrink.shape, BF16),
            pltpu.VMEM((768, 256), F32),
            pltpu.SemaphoreType.DMA((11,)),
            pltpu.SemaphoreType.DMA((len(shapes),)),
        ],
        compiler_params=pltpu.CompilerParams(vmem_limit_bytes=60 * 2**20),
        name="encoder_forward",
    )(sizes, gains, shifts, biases, inner[None], tokens, attend, merging, expand, shrink)


def decoder_kernel(
    reduce, sizes, distance, slots, frequency, sent, biases, mask_token, gains, shifts, inner,
    cotangent, entry_far, attend_far, merging_far, expand_far, shrink_far,
    summed, rest, vectors, encoded_grad, *refs,
):
    (
        table, start, normed, mixed, turned, probs, flipped, context, normed_two, active,
        before_grad, go_low, attention_low, context_grad, key_grad, mixed_grad, target,
        entry_weight, attend, merging, expand, shrink, load_sem,
    ) = refs[:23]
    pack = lax.axis_index("section")
    if reduce:
        mine, partner = neighbours()
        greet(partner)
        engine = reducer(DECODER_CHUNKS, DECODER_CHUNKS, mine, partner, summed, refs[23:])
        put = engine.put
    else:
        put = put_into(summed)
    put_rest = put_into(rest)
    loads = fetch(
        [
            (entry_far, entry_weight),
            (attend_far, attend),
            (cotangent.at[pack], target),
            (merging_far, merging),
            (expand_far, expand),
            (shrink_far, shrink),
        ],
        load_sem,
    )
    tiles = start.shape[0] // TILE
    vectors[...] = jnp.zeros_like(vectors)
    large = sizes[pack, 0] == 1024

    def add_row(row, value):
        vectors[row : row + 1, :] += value

    positions = iota((32, 128), 0).astype(F32)
    for chip in range(4):
        spacing = distance[pack, chip].astype(F32) / 16.0
        angle = positions * (spacing * frequency[...])
        table[0, chip] = jnp.sin(angle)
        table[1, chip] = jnp.cos(angle)
    loads[0].wait()
    entry = low(dot(sent[...], entry_weight[...]) + biases[0:1])
    loads[1].wait()

    def validity(tile):
        places = iota((TILE, 1), 0) + tile * TILE
        return (chip_of(places, sizes, pack) < 4).astype(F32)

    def spread_of(tile):
        return (slots[pl.ds(pack, 1)] == iota((TILE, TILE), 0) + tile * TILE).astype(F32)

    @pl.loop(0, tiles)
    def _(tile):
        rows = rows_of(tile)
        valid = validity(tile)
        spread = spread_of(tile)
        fill = valid * (1.0 - jnp.sum(spread, axis=1, keepdims=True))
        pieces = []
        for kind in range(2):
            wave = table[kind, 0, aligned(tile * 8, 8, 8)]
            big = jnp.broadcast_to(wave[:, None], (8, 32, 128)).reshape(TILE, 128)
            wave = table[kind, tile, 0:16]
            own = jnp.broadcast_to(wave[:, None], (16, 16, 128)).reshape(TILE, 128)
            pieces.append(jnp.where(large, big, own))
        for kind in range(2):
            wave = table[kind, 0]
            big = jnp.broadcast_to(wave[None], (8, 32, 128)).reshape(TILE, 128)
            wave = table[kind, tile, 0:16]
            own = jnp.broadcast_to(wave[None], (16, 16, 128)).reshape(TILE, 128)
            pieces.append(jnp.where(large, big, own))
        encoding = jnp.concatenate(pieces, axis=1) * valid
        hidden = dot(low(spread), entry) + fill * mask_token[...] + encoding
        start[rows] = hidden
        add_row(12, row_sum(valid * hidden * hidden))
        add_row(16, row_sum(valid))
        unit, _ = standardize(hidden)
        norm = low(unit * gains[0:1] + shifts[0:1])
        normed[rows] = norm
        mix = dot(norm, attend[...])
        mixed[rows] = low(mix)
        turned[:, rows] = low(mix[:, 256:].T)

    @pl.loop(0, 2 * tiles)
    def _(step):
        pair, tile = step // tiles, step % tiles
        rows = rows_of(tile)
        own_chip = chip_of(iota((1, TILE), 1) + tile * TILE, sizes, pack)
        key_chip = chip_of(iota((start.shape[0], 1), 0), sizes, pack)
        for half in range(2):
            query = only(mixed[rows, pair_lanes(pair)], half) * BF16(0.125)
            scores = dot_nt(mixed[:, pair_lanes(pair, 256)], query)
            scores = jnp.where(key_chip == own_chip, scores, NEGATIVE)
            expos = jnp.exp(scores - jnp.max(scores, axis=0, keepdims=True))
            prob = low(expos * (1.0 / jnp.sum(expos, axis=0, keepdims=True)))
            probs[pair * 2 + half, :, rows] = prob
            flipped[head_rows(pair, half), rows] = dot(turned[head_rows(pair, half, 256)], prob)

    for copy in loads[2:]:
        copy.wait()

    @pl.loop(0, tiles)
    def _(tile):
        rows = rows_of(tile)
        valid = validity(tile)
        mingled = low(flipped[:, rows].T)
        context[rows] = mingled
        attention = dot(mingled, merging[...]) + biases[1:2]
        add_row(13, row_sum(valid * attention * attention))
        center = start[rows] + attention
        unit, inverse = standardize(center)
        norm = low(unit * gains[1:2] + shifts[1:2])
        normed_two[rows] = norm
        go = target[rows] * valid
        go_below = low(go)
        go_low[rows] = go_below
        add_row(2, row_sum(go))
        feed = jnp.zeros_like(go)
        norm_grad = jnp.zeros_like(go)
        for part in range(4):
            cols = slice(part * 512, part * 512 + 512)
            before = dot(norm, expand[:, cols]) + inner[:, cols]
            value, slope = gelu_pair(before)
            value = low(value)
            active[rows, cols] = value
            feed = feed + dot(value, shrink[cols])
            grad = low(slope * dot_nt(go_below, shrink[cols]))
            before_grad[rows, cols] = grad
            add_row(8 + part, row_sum(grad.astype(F32)))
            norm_grad = norm_grad + dot_nt(grad, expand[:, cols])
        feed = feed + biases[2:3]
        add_row(14, row_sum(valid * feed * feed))
        output = center + feed
        add_row(15, row_sum(valid * output * output))
        add_row(5, row_sum(norm_grad * unit))
        add_row(7, row_sum(norm_grad))
        grad = go + norm_back(unit, inverse, gains[1:2], norm_grad)
        target[rows] = grad
        add_row(1, row_sum(grad))
        below = low(grad)
        attention_low[rows] = below
        context_grad[rows] = low(dot_nt(below, merging[...]))

    for part in range(2):
        cols = slice(part * 256, part * 256 + 256)
        for quarter in range(4):
            wide = slice(quarter * 512, quarter * 512 + 512)
            value = dot_tn(normed_two[:, cols], before_grad[:, wide])
            store_packed(put, part * 16, (DECODER_EXPAND[0] + quarter * 512, 16, 512), value)
        value = dot_tn(attention_low[:, cols], context[...])
        store_packed(put, part * 16, DECODER_MERGE, value)
    for block in range(2):
        put(slice(block * 16, block * 16 + 16), 4352, jnp.zeros((16, 16, 256), F32))
    if reduce:
        await_greetings()
        engine.first_copy(0).start()

    @pl.loop(0, 8)
    def _(part):
        cols = aligned(part * 256, 256, 256)
        store_packed(put, part * 4, DECODER_SHRINK, dot_tn(active[:, cols], go_low[...]))

    if reduce:
        engine.first_copy(1).start()
        engine.first_copy(2).start()

    key_grad[...] = jnp.zeros_like(key_grad)

    @pl.loop(0, 2 * tiles)
    def _(step):
        pair, tile = step // tiles, step % tiles
        rows = rows_of(tile)
        lanes = pair_lanes(pair)
        values = mixed[:, pair_lanes(pair, 512)]
        for half in range(2):
            prob = probs[pair * 2 + half, :, rows]
            outer = only(context_grad[rows, lanes], half)
            wide = prob.astype(F32)
            grad = dot_nt(values, outer)
            raw = low(wide * (grad - jnp.sum(wide * grad, axis=0, keepdims=True)))
            query = only(mixed[rows, lanes], half)
            key_grad[0, :, lanes] += dot(raw, query)
            key_grad[1, :, lanes] += dot(prob, outer)
            flipped[head_rows(pair, half), rows] = dot(turned[head_rows(pair, half)], raw)
        if reduce:
            engine.turn(step)

    def last(tile, entry_grad):
        rows = rows_of(tile)
        mix = jnp.concatenate(
            [low(flipped[:, rows].T * 0.125), low(key_grad[0, rows] * 0.125), low(key_grad[1, rows])],
            axis=1,
        )
        mixed_grad[rows] = mix
        norm_grad = dot_nt(mix, attend[...])
        unit, inverse = standardize(start[rows])
        add_row(4, row_sum(norm_grad * unit))
        add_row(6, row_sum(norm_grad))
        grad = target[rows] + norm_back(unit, inverse, gains[0:1], norm_grad)
        spread = spread_of(tile)
        fill = validity(tile) * (1.0 - jnp.sum(spread, axis=1, keepdims=True))
        add_row(3, row_sum(fill * grad))
        return entry_grad + dot_tn(low(spread), low(grad))

    entry_grad = lax.fori_loop(0, tiles, last, jnp.zeros((TILE, 512), F32))
    add_row(0, row_sum(entry_grad))
    entry_low = low(entry_grad)
    encoded_grad[...] = low(dot_nt(entry_low, entry_weight[...]))
    store_packed(put_rest, 0, ENTRY, dot_tn(sent[...], entry_low))
    for part in range(2):
        cols = slice(part * 256, part * 256 + 256)
        value = dot_tn(normed[:, cols], mixed_grad[...])
        store_packed(put_rest, part * 16, DECODER_ATTEND, value)
    if reduce:
        engine.close(0)


def decoder_call(
    reduce, sizes, distance, slots, sent, cotangent, entry_weight, biases, mask_token,
    gains, shifts, attend, merging, expand, inner, shrink,
):
    length = cotangent.shape[1]
    width = 512
    frequency = np.exp(-np.log(10000.0) * np.arange(width // 4) / (width // 4)).astype(np.float32)
    columns = DECODER_CHUNKS * SPAN
    if reduce:
        summed = jax.ShapeDtypeStruct((16, columns), F32)
        extra = reducer_scratch(DECODER_CHUNKS, DECODER_CHUNKS)
        params = dict(collective_id=1, has_side_effects=True)
    else:
        summed = jax.ShapeDtypeStruct((2, 16, 16, columns), BF16)
        extra = []
        params = dict()
    return pl.pallas_call(
        functools.partial(decoder_kernel, reduce),
        out_shape=(
            summed,
            jax.ShapeDtypeStruct((2, 16, 16, SPAN), BF16),
            jax.ShapeDtypeStruct((24, width), F32),
            jax.ShapeDtypeStruct((256, 768), BF16),
        ),
        in_specs=[smem_spec()] * 2 + [vmem_spec()] * 8 + [any_spec()] * 6,
        out_specs=(vmem_spec(),) * 4,
        scratch_shapes=[
            pltpu.VMEM((2, 4, 32, 128), F32),
            pltpu.VMEM((length, width), F32),
            pltpu.VMEM((length, width), BF16),
            pltpu.VMEM((length, 768), BF16),
            pltpu.VMEM((512, length), BF16),
            pltpu.VMEM((4, length, length), BF16),
            pltpu.VMEM((256, length), F32),
            pltpu.VMEM((length, 256), BF16),
            pltpu.VMEM((length, width), BF16),
            pltpu.VMEM((length, 2048), BF16),
            pltpu.VMEM((length, 2048), BF16),
            pltpu.VMEM((length, width), BF16),
            pltpu.VMEM((length, width), BF16),
            pltpu.VMEM((length, 256), BF16),
            pltpu.VMEM((2, length, 256), F32),
            pltpu.VMEM((length, 768), BF16),
            pltpu.VMEM((length, width), F32),
            pltpu.VMEM(entry_weight.shape, BF16),
            pltpu.VMEM(attend.shape, BF16),
            pltpu.VMEM(merging.shape, BF16),
            pltpu.VMEM(expand.shape, BF16),
            pltpu.VMEM(shrink.shape, BF16),
            pltpu.SemaphoreType.DMA((6,)),
        ]
        + extra,
        compiler_params=pltpu.CompilerParams(vmem_limit_bytes=60 * 2**20, **params),
        name="decoder_block",
    )(
        sizes, distance, slots, jnp.asarray(frequency)[None], sent, biases, mask_token[None], gains, shifts,
        inner[None], cotangent, entry_weight, attend, merging, expand, shrink,
    )


def encoder_backward_kernel(
    reduce, encoded_grad, sums, decoder_vectors, gains, tokens, rest, attend_far, merging_far, expand_far,
    shrink_far, normed_far, mixed_far, turned_far, probs_far, context_far, middle_far, normed_two_far, active_far,
    slope_far, summed, vectors, tokens_grad, *refs,
):
    if reduce:
        decoder_sums, arrived = refs[:2]
        refs = refs[2:]
    (
        hidden, attend, merging, expand, shrink, normed, mixed, turned, probs, context, middle, normed_two, active,
        slope, before_grad, norm_sum, attention_low, context_grad, key_grad, query_turned, mixed_grad, load_sem,
        part_sem,
    ) = refs[:23]
    pack = lax.axis_index("section")

    def part_loads(part):
        cols = slice(part * 1024, part * 1024 + 1024)
        slot = part % 2
        return [
            pltpu.make_async_copy(expand_far.at[:, cols], expand.at[slot], part_sem.at[slot, 0]),
            pltpu.make_async_copy(shrink_far.at[cols], shrink.at[slot], part_sem.at[slot, 1]),
            pltpu.make_async_copy(slope_far.at[part], slope.at[slot], part_sem.at[slot, 2]),
        ]

    if reduce:
        (
            decoder_total, encoder_total, decoder_got, encoder_got, payload,
            own_sem, small_send, small_recv, pay_send, pay_recv, small_load,
        ) = refs[23:34]
        mine, partner = neighbours()
        greet(partner)
        engine = reducer(CHUNKS, RING, mine, partner, summed, refs[34:])
        put = engine.put
        first_own = pltpu.make_async_copy(rest.at[mine["c"]], engine.own.at[:, :, 0:SPAN], own_sem)
        first_own.start()
        decoder_load = pltpu.make_async_copy(decoder_vectors, decoder_total.at[0], small_load)
        decoder_load.start()
    else:
        put = put_into(summed)
    loads = fetch(
        [
            (active_far, active),
            (normed_two_far, normed_two),
            (middle_far, middle),
            (merging_far, merging),
            (context_far, context),
            (mixed_far, mixed),
            (probs_far, probs),
            (turned_far.at[0:768], turned),
            (normed_far, normed),
            (attend_far, attend),
            (tokens.at[pack], hidden),
        ],
        load_sem,
    )
    for part in range(2):
        for copy in part_loads(part):
            copy.start()
    vectors[...] = sums[...]
    go_low = encoded_grad[...]
    go = go_low.astype(F32)
    vectors[1:2, :768] = row_sum(go)
    norm_sum[...] = jnp.zeros_like(norm_sum)

    def send(chunk):
        if reduce:
            engine.first_copy(chunk).start()

    def release(chunk):
        if reduce:
            engine.release(chunk)

    def shrink_grad(part):
        release(1 + part)
        cols = slice(part * 256, part * 256 + 256)
        for piece in range(4):
            rows = slice(piece * 768, piece * 768 + 768)
            store_packed(put, piece * 8, ENCODER_SHRINK[part], dot_tn(active[:, rows], encoded_grad[:, cols]))
        send(1 + part)

    def hidden_layer(part):
        release(4 + part)
        for copy in part_loads(part):
            copy.wait()
        slot = part % 2
        grad = low(slope[slot] * dot_nt(encoded_grad[...], shrink[slot]))
        before_grad[...] = grad
        vectors[6 + part : 7 + part] = row_sum(grad.astype(F32))
        norm_sum[...] += dot_nt(grad, expand[slot])
        if part == 0:
            for copy in part_loads(2):
                copy.start()
        if part == 0:
            loads[1].wait()
        store_packed(put, 0, ENCODER_EXPAND[part], dot_tn(normed_two[...], before_grad[...]))
        send(4 + part)

    def middle_layer():
        loads[2].wait()
        loads[3].wait()
        unit, inverse = standardize(middle[...])
        norm_grad = norm_sum[...]
        vectors[3:4, :768] = row_sum(norm_grad * unit)
        vectors[5:6, :768] = row_sum(norm_grad)
        grad = encoded_grad[...].astype(F32) + norm_back(unit, inverse, gains[1:2], norm_grad)
        vectors[0:1, :768] = row_sum(grad)
        tokens_grad[...] = grad
        below = low(grad)
        attention_low[...] = below
        context_grad[...] = low(dot_nt(below, merging[...]))
        for copy in loads[4:8]:
            copy.wait()

    def attention(first):
        @pl.loop(first, first + 3)
        def _(pair):
            lanes = pair_lanes(pair)
            values = mixed[:, pair_lanes(pair, 1536)]
            keys_total = jnp.zeros((TILE, 128), F32)
            values_total = jnp.zeros((TILE, 128), F32)
            for half in range(2):
                prob = probs[pair * 2 + half]
                outer = only(context_grad[:, lanes], half)
                query = only(mixed[:, lanes], half)
                wide = prob.astype(F32)
                grad = dot_nt(values, outer)
                raw = low(wide * (grad - jnp.sum(wide * grad, axis=0, keepdims=True)))
                keys_total = keys_total + dot(raw, query)
                values_total = values_total + dot(prob, outer)
                rows = head_rows(pair, half)
                query_turned[rows] = dot(turned[rows], raw)
            key_grad[0, :, lanes] = keys_total
            key_grad[1, :, lanes] = values_total

    def mixing():
        mixed_grad[:, 0:768] = low(query_turned[...].T * 0.125)
        mixed_grad[:, 768:1536] = low(key_grad[0] * 0.125)
        mixed_grad[:, 1536:2304] = low(key_grad[1])

    def attend_grad(part):
        if part == 0:
            loads[8].wait()
        release(7 + part)
        wide = slice(part * 1024, min(part * 1024 + 1024, 2304))
        store_packed(put, 0, ENCODER_ATTEND[part], dot_tn(normed[...], mixed_grad[:, wide]))
        if part == 2:
            store_packed(put, 0, ENCODER_MERGE, dot_tn(attention_low[...], context[...]))
        send(7 + part)

    def input_layer():
        loads[9].wait()
        loads[10].wait()
        norm_grad = dot_nt(mixed_grad[...], attend[...])
        unit, inverse = standardize(hidden[...])
        vectors[2:3, :768] = row_sum(norm_grad * unit)
        vectors[4:5, :768] = row_sum(norm_grad)
        grad = tokens_grad[...] + norm_back(unit, inverse, gains[0:1], norm_grad)
        tokens_grad[...] = grad
        if reduce:
            payload[...] = low(grad)

    if not reduce:
        loads[0].wait()
        for part in range(3):
            shrink_grad(part)
        for part in range(3):
            hidden_layer(part)
        middle_layer()
        attention(0)
        attention(3)
        mixing()
        for part in range(3):
            attend_grad(part)
        input_layer()
        return

    def exchange(source):
        return remote(source, arrived, pay_send, pay_recv, partner["x"])

    small_route = ("c",) + ROUTES[0]
    totals = ((decoder_total, decoder_got), (encoder_total, encoder_got))

    def small_copy(stage, kind):
        source, target = totals[kind]
        return remote(
            source.at[stage],
            target.at[stage],
            small_send.at[stage, kind],
            small_recv.at[stage, kind],
            partner[small_route[stage]],
        )

    def small_advance(stage):
        if stage == 0:
            encoder_total[0] = vectors[...]
        for kind in range(2):
            source, target = totals[kind]
            if stage > 0:
                small_copy(stage - 1, kind).wait_recv()
                source[stage] = source[stage - 1] + target[stage - 1]
            if stage < 5:
                small_copy(stage, kind).start()

    await_greetings()
    opening = engine.first_copy(0, rest.at[1 - mine["c"]])
    opening.start()

    @pl.when(pack == 0)
    def _():
        exchange(encoded_grad).start()

    loads[0].wait()
    shrink_grad(0)
    shrink_grad(1)
    first_own.wait()
    decoder_load.wait()

    def work_0():
        shrink_grad(2)
        hidden_layer(0)

    def work_1():
        hidden_layer(1)

    def work_2():
        hidden_layer(2)
        middle_layer()

    def work_3():
        attention(0)

    def work_4():
        attention(3)
        mixing()
        attend_grad(0)

    def work_5():
        attend_grad(1)
        attend_grad(2)

    def work_6():
        input_layer()

        @pl.when(pack == 1)
        def _():
            exchange(payload).start()

    works = [work_0, work_1, work_2, work_3, work_4, work_5, work_6]
    works += [functools.partial(small_advance, stage) for stage in range(6)]

    @pl.loop(0, CHUNKS + 4)
    def _(number):
        engine.turn(number)
        for position, work in enumerate(works):
            pl.when(number == position)(work)

    for stage in range(5):
        for kind in range(2):
            small_copy(stage, kind).wait_send()
    exchange(payload).wait()
    engine.close(CHUNKS - RING)
    vectors[...] = encoder_total[5]
    decoder_sums[...] = decoder_total[5]


def encoder_backward_call(reduce, tokens, encoded_grad, sums, decoder_vectors, rest, kept, gains, attend, merging, expand, shrink):
    columns = CHUNKS * SPAN
    if reduce:
        summed = jax.ShapeDtypeStruct((16, columns), F32)
        more = (
            jax.ShapeDtypeStruct(decoder_vectors.shape, F32),
            jax.ShapeDtypeStruct((256, 768), BF16),
        )
        more_specs = (vmem_spec(), any_spec())
        extra = [
            pltpu.VMEM((6,) + decoder_vectors.shape, F32),
            pltpu.VMEM((6,) + sums.shape, F32),
            pltpu.VMEM((5,) + decoder_vectors.shape, F32),
            pltpu.VMEM((5,) + sums.shape, F32),
            pltpu.VMEM((256, 768), BF16),
            pltpu.SemaphoreType.DMA,
            pltpu.SemaphoreType.DMA((5, 2)),
            pltpu.SemaphoreType.DMA((5, 2)),
            pltpu.SemaphoreType.DMA,
            pltpu.SemaphoreType.DMA,
            pltpu.SemaphoreType.DMA,
        ] + reducer_scratch(CHUNKS, RING)
        params = dict(collective_id=2, has_side_effects=True)
    else:
        summed = jax.ShapeDtypeStruct((2, 16, 16, columns), BF16)
        more, more_specs, extra, params = (), (), [], dict()
    return pl.pallas_call(
        functools.partial(encoder_backward_kernel, reduce),
        out_shape=(
            summed,
            jax.ShapeDtypeStruct(sums.shape, F32),
            jax.ShapeDtypeStruct((256, 768), F32),
        )
        + more,
        in_specs=[vmem_spec()] * 2 + [any_spec(), vmem_spec()] + [any_spec()] * 15,
        out_specs=(vmem_spec(),) * 3 + more_specs,
        scratch_shapes=[
            pltpu.VMEM((256, 768), F32),
            pltpu.VMEM(attend.shape, BF16),
            pltpu.VMEM(merging.shape, BF16),
            pltpu.VMEM((2, 768, 1024), BF16),
            pltpu.VMEM((2, 1024, 768), BF16),
            pltpu.VMEM((256, 768), BF16),
            pltpu.VMEM((256, 2304), BF16),
            pltpu.VMEM((768, 256), BF16),
            pltpu.VMEM((12, 256, 256), BF16),
            pltpu.VMEM((256, 768), BF16),
            pltpu.VMEM((256, 768), F32),
            pltpu.VMEM((256, 768), BF16),
            pltpu.VMEM((256, 3072), BF16),
            pltpu.VMEM((2, 256, 1024), F32),
            pltpu.VMEM((256, 1024), BF16),
            pltpu.VMEM((256, 768), F32),
            pltpu.VMEM((256, 768), BF16),
            pltpu.VMEM((256, 768), BF16),
            pltpu.VMEM((2, 256, 768), F32),
            pltpu.VMEM((768, 256), F32),
            pltpu.VMEM((256, 2304), BF16),
            pltpu.SemaphoreType.DMA((11,)),
            pltpu.SemaphoreType.DMA((2, 3)),
        ]
        + extra,
        compiler_params=pltpu.CompilerParams(vmem_limit_bytes=60 * 2**20, **params),
        name="encoder_backward",
    )(encoded_grad, sums, decoder_vectors, gains, tokens, rest, attend, merging, expand, shrink, *kept)


def unpack(packed, place):
    offset, count, width = place
    pieces = [
        packed[..., offset + i * width : offset + (i + 1) * width] for i in range(count // 16)
    ]
    if count % 16:
        offset = offset + count // 16 * width
        rest = packed[..., offset : offset + width // 2]
        pieces.append(jnp.concatenate([rest[..., :8, :], rest[..., 8:, :]], axis=-1))
    return pieces[0] if len(pieces) == 1 else jnp.concatenate(pieces, axis=-2)


def finish_kernel(
    decoder_summed, summed, decoder_sums, encoder_sums, arrived, tokens_grad, encoded_grad,
    boundary, statistics, e_gains, e_shifts, e_biases, e_attend, e_merge, e_expand, e_inner, e_shrink,
    d_entry, d_biases, mask_grad, d_gains, d_shifts, d_attend, d_merge, d_expand, d_inner, d_shrink,
):
    section = lax.axis_index("section")
    number = section * lax.axis_size("dp") + lax.axis_index("dp")

    @pl.when(section == 0)
    def _():
        boundary[0, 0] = tokens_grad[...]
        boundary[0, 1] = arrived[...].astype(F32)

    @pl.when(section == 1)
    def _():
        boundary[0, 0] = arrived[...].astype(F32)
        boundary[0, 1] = encoded_grad[...].astype(F32)

    def own(rows, count):
        width = rows.shape[1]
        return pltpu.roll(rows, (width - number * count) % width, axis=1)[:, :count]

    def own_line(rows, count):
        return own(jnp.concatenate([rows[i : i + 1] for i in range(rows.shape[0])], axis=1), count)

    lane = iota((1, 128), 1)
    values = jnp.zeros((1, 128), F32)
    for sums, width, first, count_row, base in ((encoder_sums, DE, 10, 14, 0), (decoder_sums, DD, 12, 16, 4)):
        scale = 1.0 / (sums[count_row : count_row + 1, 0:1] * width)
        for i in range(4):
            value = jnp.sum(sums[first + i : first + i + 1, :], axis=1, keepdims=True) * scale
            values = jnp.where(lane == base + i, value, values)
    statistics[...] = jnp.sqrt(values)[:, :8]
    rows = own(encoder_sums[0:8, :DE], 24)
    e_biases[...] = rows[0:2]
    e_gains[...] = rows[2:4]
    e_shifts[...] = rows[4:6]
    e_inner[...] = own_line(encoder_sums[6:9], 96)
    rows = own(decoder_sums[0:8], 16)
    d_biases[...] = rows[0:3]
    mask_grad[...] = rows[3:4]
    d_gains[...] = rows[4:6]
    d_shifts[...] = rows[6:8]
    d_inner[...] = own_line(decoder_sums[8:12], 64)

    def upright(value):
        padding = jnp.zeros((128 - value.shape[0], value.shape[1]), F32)
        return jnp.concatenate([value, padding], axis=0).T[:, : value.shape[0]]

    d_entry[...] = unpack(summed, ENTRY)
    d_attend[...] = unpack(summed, DECODER_ATTEND)
    d_merge[...] = upright(unpack(decoder_summed, DECODER_MERGE))
    d_expand[...] = unpack(decoder_summed, DECODER_EXPAND)
    d_shrink[...] = unpack(decoder_summed, DECODER_SHRINK)
    for target, places in ((e_expand, ENCODER_EXPAND), (e_attend, ENCODER_ATTEND), (e_shrink, ENCODER_SHRINK)):
        start = 0
        for place in places:
            target[:, start : start + place[2]] = unpack(summed, place)
            start += place[2]
    e_merge[...] = upright(unpack(summed, ENCODER_MERGE))


def finish_call(*operands):
    shapes = (
        (1, 2, 256, 768), (1, 8), (2, 24), (2, 24), (2, 24), (24, 2304), (768, 24), (24, 3072), (1, 96), (96, 768),
        (24, 512), (3, 16), (1, 16), (2, 16), (2, 16), (16, 768), (256, 16), (16, 2048), (1, 64), (64, 512),
    )
    outs = list(
        pl.pallas_call(
            finish_kernel,
            out_shape=tuple(jax.ShapeDtypeStruct(shape, F32) for shape in shapes),
            in_specs=[vmem_spec()] * len(operands),
            out_specs=(vmem_spec(),) * len(shapes),
            compiler_params=pltpu.CompilerParams(vmem_limit_bytes=40 * 2**20),
            name="finish",
        )(*operands)
    )
    for line in (1, 8, 12, 18):
        outs[line] = outs[line].reshape(-1)
    return tuple(outs)


def scatter_sum(member, share_dim):
    return lax.psum_scatter(
        member, ("section", "dp"), scatter_dimension=share_dim, tiled=True
    )


def finish_generic(decoder_part, part, decoder_sums, encoder_sums, tokens_grad, encoded_grad):
    section = lax.axis_index("section")
    payload = jnp.where(section == 0, encoded_grad, low(tokens_grad))

    def whole(packed, *places):
        packed = jnp.swapaxes(packed, 0, 1).reshape(32, 16, -1)
        blocks = [unpack(packed, place).reshape(32 * place[1], place[2]) for place in places]
        return scatter_sum(jnp.concatenate(blocks, axis=1).astype(F32), 0)

    def line(value):
        return scatter_sum(value, value.ndim - 1)

    arrived = lax.ppermute(payload, "section", [(0, 1), (1, 0)]).astype(F32)
    boundary = jnp.where(
        section == 0,
        jnp.stack([tokens_grad, arrived]),
        jnp.stack([arrived, encoded_grad.astype(F32)]),
    )
    sums = jnp.concatenate(
        [jnp.sum(encoder_sums[10:14], axis=1), jnp.sum(decoder_sums[12:16], axis=1)]
    )
    sums, counts = lax.psum((sums, (encoder_sums[14, 0], decoder_sums[16, 0])), ("section", "dp"))
    scales = jnp.concatenate([jnp.full((4,), counts[0] * DE), jnp.full((4,), counts[1] * DD)])
    return (
        boundary[None],
        jnp.sqrt(sums / scales),
        line(encoder_sums[2:4, :DE]),
        line(encoder_sums[4:6, :DE]),
        line(encoder_sums[0:2, :DE]),
        whole(part, *ENCODER_ATTEND),
        whole(part, ENCODER_MERGE).T,
        whole(part, *ENCODER_EXPAND),
        line(encoder_sums[6:9].reshape(-1)),
        whole(part, *ENCODER_SHRINK),
        whole(decoder_part[1], ENTRY),
        line(decoder_sums[0:3]),
        line(decoder_sums[3]),
        line(decoder_sums[4:6]),
        line(decoder_sums[6:8]),
        whole(decoder_part[1], DECODER_ATTEND),
        whole(decoder_part[0], DECODER_MERGE).T,
        whole(decoder_part[0], DECODER_EXPAND),
        line(decoder_sums[8:12].reshape(-1)),
        whole(decoder_part[0], DECODER_SHRINK),
    )


def body(
    visible_tokens,
    cotangent,
    chip_sizes,
    ground_distance,
    visible_slots,
    encoder_gains,
    encoder_shifts,
    encoder_biases,
    encoder_attend,
    encoder_merge,
    encoder_expand,
    encoder_inner,
    encoder_shrink,
    decoder_entry,
    decoder_biases,
    mask_token,
    decoder_gains,
    decoder_shifts,
    decoder_attend,
    decoder_merge,
    decoder_widen_weight,
    decoder_inner,
    decoder_shrink,
):
    reduce = (lax.axis_size("section"), lax.axis_size("dp")) == (2, 16)
    sent, sums, *kept = encoder_forward_call(
        chip_sizes, visible_tokens, encoder_gains, encoder_shifts, encoder_biases,
        encoder_attend, encoder_merge, encoder_expand, encoder_inner, encoder_shrink,
    )
    decoder_summed, rest, decoder_vectors, encoded_grad = decoder_call(
        reduce, chip_sizes, ground_distance, visible_slots, sent, cotangent, decoder_entry, decoder_biases, mask_token,
        decoder_gains, decoder_shifts, decoder_attend, decoder_merge, decoder_widen_weight, decoder_inner,
        decoder_shrink,
    )
    summed, encoder_sums, tokens_grad, *more = encoder_backward_call(
        reduce, visible_tokens, encoded_grad, sums, decoder_vectors, rest, kept,
        encoder_gains, encoder_attend, encoder_merge, encoder_expand, encoder_shrink,
    )
    if reduce:
        decoder_sums, arrived = more
        return finish_call(
            decoder_summed, summed, decoder_sums, encoder_sums, arrived, tokens_grad, encoded_grad
        )
    return finish_generic(
        (decoder_summed, rest), summed, decoder_vectors, encoder_sums, tokens_grad, encoded_grad
    )


def solution(mesh):
    in_specs = (
        P("dp", None, None),
        P("dp", None, None),
        P("dp", None),
        P("dp", None),
        P("dp", None),
        P(),
        P(),
        P(),
        P(),
        P(),
        P(),
        P(),
        P(),
        P(),
        P(),
        P(),
        P(),
        P(),
        P(),
        P(),
        P(),
        P(),
        P(),
    )
    out_specs = (
        P("section", "dp", None, None),
        P(),
        P(None, ("section", "dp")),
        P(None, ("section", "dp")),
        P(None, ("section", "dp")),
        P(("section", "dp"), None),
        P(None, ("section", "dp")),
        P(("section", "dp"), None),
        P(("section", "dp")),
        P(("section", "dp"), None),
        P(("section", "dp"), None),
        P(None, ("section", "dp")),
        P(("section", "dp")),
        P(None, ("section", "dp")),
        P(None, ("section", "dp")),
        P(("section", "dp"), None),
        P(None, ("section", "dp")),
        P(("section", "dp"), None),
        P(("section", "dp")),
        P(("section", "dp"), None),
    )
    return jax.shard_map(body, mesh=mesh, in_specs=in_specs, out_specs=out_specs, check_vma=False)
```

```python
import functools
import types

import jax
import jax.numpy as jnp
import numpy as np
from jax import lax
from jax.experimental import pallas as pl
from jax.experimental.pallas import tpu as pltpu
from jax.sharding import PartitionSpec as P

DE = 768
DD = 512
TILE = 256
NEGATIVE = -1e30
F32, BF16 = jnp.float32, jnp.bfloat16
MESH_ID = pl.DeviceIdType.MESH

CANON = ("x", "z2", "z1", "y")
ROUTES = (("x", "y", "z1", "z2"), ("y", "x", "z1", "z2"), ("z1", "z2", "x", "y"))
WIDTHS = (2, 3, 1)
OFFSETS = (0, 2, 5)
SPAN = 128 * sum(WIDTHS)
UNIT = 2 * SPAN
DECODER_CHUNKS = 6
CHUNKS = 20
RING = 4
STAGING = 6
LAG = 2

DECODER_EXPAND, DECODER_SHRINK, DECODER_MERGE = (0, 16, 2048), (2048, 64, 512), (4096, 16, 256)
ENTRY, DECODER_ATTEND = (0, 24, 512), (768, 16, 768)
ENCODER_SHRINK = tuple((UNIT * (1 + part), 96, 256) for part in range(3))
ENCODER_EXPAND = tuple((UNIT * (4 + part), 24, 1024) for part in range(3))
ENCODER_ATTEND = ((UNIT * 7, 24, 1024), (UNIT * 8, 24, 1024), (UNIT * 9, 24, 256))
ENCODER_MERGE = (UNIT * 9 + 384, 24, 768)


def dot(a, b):
    return jnp.dot(a, b, preferred_element_type=F32)


def dot_nt(a, b):
    return lax.dot_general(a, b, (((1,), (1,)), ((), ())), preferred_element_type=F32)


def dot_tn(a, b):
    return lax.dot_general(a, b, (((0,), (0,)), ((), ())), preferred_element_type=F32)


def low(value):
    return value.astype(BF16)


def standardize(values):
    centered = values - jnp.mean(values, axis=-1, keepdims=True)
    inverse = lax.rsqrt(jnp.mean(centered * centered, axis=-1, keepdims=True) + 1e-05)
    return centered * inverse, inverse


def norm_back(unit, inverse, gain, grad):
    inner = grad * gain
    return inverse * (
        inner
        - jnp.mean(inner, axis=-1, keepdims=True)
        - unit * jnp.mean(inner * unit, axis=-1, keepdims=True)
    )


def row_sum(values):
    return jnp.sum(values, axis=0, keepdims=True)


def gelu_pair(before):
    half = 0.5 * (1.0 + lax.erf(before * 0.7071067811865476))
    density = jnp.exp(-0.5 * before * before) * 0.3989422804014327
    return before * half, half + before * density


def chip_of(places, sizes, pack):
    end = sizes[pack, 0]
    chip = (places >= end).astype(jnp.int32)
    for slot in range(1, 4):
        end = end + sizes[pack, slot]
        chip = chip + (places >= end).astype(jnp.int32)
    return chip


def iota(shape, dimension):
    return lax.broadcasted_iota(jnp.int32, shape, dimension)


def aligned(start, size, unit):
    return pl.ds(pl.multiple_of(start, unit), size)


def pair_lanes(pair, base=0):
    return aligned(base + pair * 128, 128, 128)


def head_rows(pair, half, base=0):
    return aligned(base + pair * 128 + half * 64, 64, 64)


def rows_of(tile):
    return aligned(tile * TILE, TILE, TILE)


def only(values, half):
    return jnp.where(iota((1, 128), 1) // 64 == half, values, jnp.zeros_like(values))


def fetch(pairs, sems):
    copies = [
        pltpu.make_async_copy(source, target, sems.at[i]) for i, (source, target) in enumerate(pairs)
    ]
    for copy in copies:
        copy.start()
    return copies


def store_packed(put, first, place, value):
    offset, count, width = place
    value = value.reshape(-1, count, width)
    shards = slice(first, first + value.shape[0]) if isinstance(first, int) else pl.ds(first, value.shape[0])
    for piece in range(count // 16):
        put(shards, offset + piece * width, value[:, piece * 16 : piece * 16 + 16])
    if count % 16:
        half = width // 2
        rest = value[:, count - 8 :]
        rest = jnp.concatenate([rest[:, :, :half], rest[:, :, half:]], axis=1)
        put(shards, offset + count // 16 * width, rest)


def halves(shards, value):
    pairs = value.reshape(value.shape[0] // 2, 2, *value.shape[1:])
    if isinstance(shards, slice):
        return slice(shards.start // 2, shards.stop // 2), pairs[:, 0], pairs[:, 1]
    return pl.ds(shards.start // 2, shards.size // 2), pairs[:, 0], pairs[:, 1]


def place_of(names, bits):
    index = 0
    for name in names:
        index = index * 2 + bits[name]
    return index


def left_after(route, stage):
    return tuple(name for name in CANON if name not in route[:stage])


def choices(names):
    for number in range(2 ** len(names)):
        yield {name: (number >> (len(names) - 1 - i)) & 1 for i, name in enumerate(names)}


def neighbours():
    section = lax.axis_index("section")
    data = lax.axis_index("dp")
    mine = {"x": section, "c": data % 2, "y": data // 2 % 2, "z1": data // 4 % 2, "z2": data // 8 % 2}
    partner = {"x": (1 - section, data)}
    for name, step in {"c": 1, "y": 2, "z1": 4, "z2": 8}.items():
        partner[name] = (section, data + step * (1 - 2 * mine[name]))
    return mine, partner


def greet(partner):
    barrier = pltpu.get_barrier_semaphore()
    for name in ("c",) + CANON:
        pl.semaphore_signal(barrier, inc=1, device_id=partner[name], device_id_type=MESH_ID)


def await_greetings():
    pl.semaphore_wait(pltpu.get_barrier_semaphore(), 5)


def remote(source, target, send, recv, device):
    return pltpu.make_async_remote_copy(
        src_ref=source,
        dst_ref=target,
        send_sem=send,
        recv_sem=recv,
        device_id=device,
        device_id_type=MESH_ID,
    )


def reducer(chunks, slots, mine, partner, out, refs):
    own, staging, first = refs[:3]
    sent, got = refs[3:15], refs[15:27]
    first_send, first_recv, send_sem, recv_sem = refs[27:31]

    def span(chunk):
        return aligned(chunk * SPAN, SPAN, 128)

    def first_copy(chunk, source=None):
        if source is None:
            source = staging.at[:, :, span(chunk % slots)]
        return remote(
            source, first.at[:, :, span(chunk)], first_send.at[chunk], first_recv.at[chunk], partner["c"]
        )

    def columns(route, slot):
        return aligned(slot * (WIDTHS[route] * 128), WIDTHS[route] * 128, 128)

    def whole(route, chunk):
        return aligned(chunk * SPAN + OFFSETS[route] * 128, WIDTHS[route] * 128, 128)

    def stage_copy(route, stage, chunk):
        return remote(
            sent[route * 4 + stage].at[:, :, columns(route, chunk % RING)],
            got[route * 4 + stage].at[:, :, columns(route, chunk)],
            send_sem.at[route, stage, chunk],
            recv_sem.at[route, stage, chunk],
            partner[ROUTES[route][stage]],
        )

    def total(route, stage, chunk, bits):
        spot = place_of(CANON, bits)
        cols = whole(route, chunk)
        value = own[spot, :, cols].astype(F32) + first[spot, :, cols].astype(F32)
        for earlier in range(stage):
            names = left_after(ROUTES[route], earlier + 1)
            piece = got[route * 4 + earlier][place_of(names, bits), :, columns(route, chunk)]
            value = value + piece.astype(F32)
        return value

    def advance(route, stage, chunk):
        path = ROUTES[route]
        if stage:
            stage_copy(route, stage - 1, chunk).wait_recv()
        if stage == 4:
            out[:, whole(route, chunk)] = total(route, 4, chunk, mine)
            return

        @pl.when(chunk >= RING)
        def _():
            stage_copy(route, stage, chunk - RING).wait_send()

        names = left_after(path, stage + 1)
        for free in choices(names):
            bits = dict(mine)
            bits[path[stage]] = 1 - mine[path[stage]]
            bits.update(free)
            value = total(route, stage, chunk, bits)
            sent[route * 4 + stage][place_of(names, free), :, columns(route, chunk % RING)] = low(value)
        stage_copy(route, stage, chunk).start()

    def turn(number):
        for stage in range(4, -1, -1):
            chunk = number - LAG * stage

            @pl.when((chunk >= 0) & (chunk < chunks))
            def _(stage=stage, chunk=chunk):
                if stage == 0:
                    first_copy(chunk).wait_recv()
                for route in range(3):
                    advance(route, stage, chunk)

    def put(shards, column, value):
        shards, even, odd = halves(shards, value)
        width = value.shape[2]
        assert slots == chunks or column // UNIT == (column + width - 1) // UNIT
        kept = jnp.where(mine["c"] == 0, even, odd)
        given = jnp.where(mine["c"] == 0, odd, even)
        own[shards, :, column : column + width] = low(kept)
        start = column % (slots * SPAN)
        staging[shards, :, start : start + width] = low(given)

    def release(unit):
        for chunk in (2 * unit, 2 * unit + 1):
            if chunk >= slots:
                first_copy(chunk - slots).wait_send()

    def send(unit):
        for chunk in (2 * unit, 2 * unit + 1):
            first_copy(chunk).start()

    def close(released):
        for chunk in range(released, chunks):
            first_copy(chunk).wait_send()
        for chunk in range(chunks - RING, chunks):
            for route in range(3):
                for stage in range(4):
                    stage_copy(route, stage, chunk).wait_send()

    return types.SimpleNamespace(
        own=own, span=span, first_copy=first_copy, turn=turn, put=put, release=release, send=send, close=close
    )


def reducer_scratch(chunks, slots):
    stages = [(width, block) for width in WIDTHS for block in (8, 4, 2, 1)]
    return (
        [
            pltpu.VMEM((16, 16, chunks * SPAN), BF16),
            pltpu.VMEM((16, 16, slots * SPAN), BF16),
            pltpu.VMEM((16, 16, chunks * SPAN), BF16),
        ]
        + [pltpu.VMEM((block, 16, RING * width * 128), BF16) for width, block in stages]
        + [pltpu.VMEM((block, 16, chunks * width * 128), BF16) for width, block in stages]
        + [
            pltpu.SemaphoreType.DMA((chunks,)),
            pltpu.SemaphoreType.DMA((chunks,)),
            pltpu.SemaphoreType.DMA((3, 4, chunks)),
            pltpu.SemaphoreType.DMA((3, 4, chunks)),
        ]
    )


REDUCER_REFS = 31


def put_into(parts):
    def put(shards, column, value):
        shards, even, odd = halves(shards, value)
        parts[0, shards, :, column : column + value.shape[2]] = low(even)
        parts[1, shards, :, column : column + value.shape[2]] = low(odd)

    return put


def vmem_spec():
    return pl.BlockSpec(memory_space=pltpu.VMEM)


def any_spec():
    return pl.BlockSpec(memory_space=pl.ANY)


def smem_spec():
    return pl.BlockSpec(memory_space=pltpu.SMEM)


def encoder_forward_kernel(
    sizes, gains, shifts, biases, inner, tokens, attend_far, merging_far, expand_far, shrink_far,
    sent, vectors, *refs,
):
    far = refs[:9]
    normed, mixed, turned, probs, context, middle, normed_two, active, slope = refs[9:18]
    hidden, attend, merging, expand, shrink, context_turned, load_sem, save_sem = refs[18:]
    pack = lax.axis_index("section")
    loads = fetch(
        [
            (tokens.at[pack], hidden),
            *[(attend_far.at[:, i * 768 : i * 768 + 768], attend.at[:, i * 768 : i * 768 + 768]) for i in range(3)],
            (merging_far, merging),
            *[(expand_far.at[:, i * 1024 : i * 1024 + 1024], expand.at[:, i * 1024 : i * 1024 + 1024]) for i in range(3)],
            *[(shrink_far.at[i * 1024 : i * 1024 + 1024], shrink.at[i * 1024 : i * 1024 + 1024]) for i in range(3)],
        ],
        load_sem,
    )
    saves = []

    def save(*numbers):
        for number in numbers:
            copy = pltpu.make_async_copy(refs[9 + number], far[number], save_sem.at[number])
            copy.start()
            saves.append(copy)

    vectors[...] = jnp.zeros_like(vectors)
    key_chip = chip_of(4 * iota((TILE, 1), 0), sizes, pack)
    own_chip = chip_of(4 * iota((1, TILE), 1), sizes, pack)
    valid = (key_chip < 4).astype(F32)
    loads[0].wait()
    values = hidden[...]
    vectors[10:11, :768] = row_sum(valid * values * values)
    unit, _ = standardize(values)
    norm = low(unit * gains[0:1] + shifts[0:1])
    normed[...] = norm
    for part in range(3):
        cols = slice(part * 768, part * 768 + 768)
        loads[1 + part].wait()
        mix = dot(norm, attend[:, cols])
        mixed[:, cols] = low(mix)
        if part:
            turned[(part - 1) * 768 : part * 768] = low(mix.T)
    save(0, 1, 2)

    @pl.loop(0, 6)
    def _(pair):
        keys = mixed[:, pair_lanes(pair, 768)]
        for half in range(2):
            query = only(mixed[:, pair_lanes(pair)], half) * BF16(0.125)
            scores = jnp.where(key_chip == own_chip, dot_nt(keys, query), NEGATIVE)
            expos = jnp.exp(scores - jnp.max(scores, axis=0, keepdims=True))
            prob = low(expos * (1.0 / jnp.sum(expos, axis=0, keepdims=True)))
            probs[pair * 2 + half] = prob
            context_turned[head_rows(pair, half)] = dot(turned[head_rows(pair, half, 768)], prob)

    mingled = low(context_turned[...].T)
    context[...] = mingled
    save(3, 4)
    loads[4].wait()
    attention = dot(mingled, merging[...]) + biases[0:1]
    vectors[11:12, :768] = row_sum(valid * attention * attention)
    center = hidden[...] + attention
    middle[...] = center
    unit, _ = standardize(center)
    norm = low(unit * gains[1:2] + shifts[1:2])
    normed_two[...] = norm
    save(5, 6)
    feed = jnp.zeros_like(center)
    for part in range(3):
        cols = slice(part * 1024, part * 1024 + 1024)
        loads[5 + part].wait()
        value, slant = gelu_pair(dot(norm, expand[:, cols]) + inner[:, cols])
        value = low(value)
        active[:, cols] = value
        slope[part] = slant
        loads[8 + part].wait()
        feed = feed + dot(value, shrink[cols])
    save(7, 8)
    feed = feed + biases[1:2]
    vectors[12:13, :768] = row_sum(valid * feed * feed)
    output = center + feed
    vectors[13:14, :768] = row_sum(valid * output * output)
    vectors[14:15, :768] = jnp.broadcast_to(row_sum(valid), (1, 768))
    sent[...] = low(output)
    for copy in saves:
        copy.wait()


def encoder_forward_call(sizes, tokens, gains, shifts, biases, attend, merging, expand, inner, shrink):
    shapes = (
        ((256, 768), BF16),
        ((256, 2304), BF16),
        ((1536, 256), BF16),
        ((12, 256, 256), BF16),
        ((256, 768), BF16),
        ((256, 768), F32),
        ((256, 768), BF16),
        ((256, 3072), BF16),
        ((3, 256, 1024), F32),
    )
    return pl.pallas_call(
        encoder_forward_kernel,
        out_shape=(jax.ShapeDtypeStruct((256, 768), BF16), jax.ShapeDtypeStruct((16, 1024), F32))
        + tuple(jax.ShapeDtypeStruct(*shape) for shape in shapes),
        in_specs=[smem_spec()] + [vmem_spec()] * 4 + [any_spec()] * 5,
        out_specs=(vmem_spec(),) * 2 + (any_spec(),) * len(shapes),
        scratch_shapes=[pltpu.VMEM(*shape) for shape in shapes]
        + [
            pltpu.VMEM((256, 768), F32),
            pltpu.VMEM(attend.shape, BF16),
            pltpu.VMEM(merging.shape, BF16),
            pltpu.VMEM(expand.shape, BF16),
            pltpu.VMEM(shrink.shape, BF16),
            pltpu.VMEM((768, 256), F32),
            pltpu.SemaphoreType.DMA((11,)),
            pltpu.SemaphoreType.DMA((len(shapes),)),
        ],
        compiler_params=pltpu.CompilerParams(vmem_limit_bytes=60 * 2**20),
        name="encoder_forward",
    )(sizes, gains, shifts, biases, inner[None], tokens, attend, merging, expand, shrink)


def decoder_kernel(
    reduce, sizes, distance, slots, frequency, sent, biases, mask_token, gains, shifts, inner,
    cotangent, entry_far, attend_far, merging_far, expand_far, shrink_far,
    summed, rest, vectors, encoded_grad, *refs,
):
    (
        table, start, normed, mixed, turned, probs, flipped, context, normed_two, active,
        before_grad, go_low, attention_low, context_grad, key_grad, mixed_grad, target,
        entry_weight, attend, merging, expand, shrink, load_sem,
    ) = refs[:23]
    pack = lax.axis_index("section")
    if reduce:
        mine, partner = neighbours()
        greet(partner)
        engine = reducer(DECODER_CHUNKS, DECODER_CHUNKS, mine, partner, summed, refs[23:])
        put = engine.put
    else:
        put = put_into(summed)
    put_rest = put_into(rest)
    loads = fetch(
        [
            (entry_far, entry_weight),
            (attend_far, attend),
            (cotangent.at[pack], target),
            (merging_far, merging),
            (expand_far, expand),
            (shrink_far, shrink),
        ],
        load_sem,
    )
    tiles = start.shape[0] // TILE
    vectors[...] = jnp.zeros_like(vectors)
    large = sizes[pack, 0] == 1024

    def add_row(row, value):
        vectors[row : row + 1, :] += value

    positions = iota((32, 128), 0).astype(F32)
    for chip in range(4):
        spacing = distance[pack, chip].astype(F32) / 16.0
        angle = positions * (spacing * frequency[...])
        table[0, chip] = jnp.sin(angle)
        table[1, chip] = jnp.cos(angle)
    loads[0].wait()
    entry = low(dot(sent[...], entry_weight[...]) + biases[0:1])
    loads[1].wait()

    def validity(tile):
        places = iota((TILE, 1), 0) + tile * TILE
        return (chip_of(places, sizes, pack) < 4).astype(F32)

    def spread_of(tile):
        return (slots[pl.ds(pack, 1)] == iota((TILE, TILE), 0) + tile * TILE).astype(F32)

    @pl.loop(0, tiles)
    def _(tile):
        rows = rows_of(tile)
        valid = validity(tile)
        spread = spread_of(tile)
        fill = valid * (1.0 - jnp.sum(spread, axis=1, keepdims=True))
        pieces = []
        for kind in range(2):
            wave = table[kind, 0, aligned(tile * 8, 8, 8)]
            big = jnp.broadcast_to(wave[:, None], (8, 32, 128)).reshape(TILE, 128)
            wave = table[kind, tile, 0:16]
            own = jnp.broadcast_to(wave[:, None], (16, 16, 128)).reshape(TILE, 128)
            pieces.append(jnp.where(large, big, own))
        for kind in range(2):
            wave = table[kind, 0]
            big = jnp.broadcast_to(wave[None], (8, 32, 128)).reshape(TILE, 128)
            wave = table[kind, tile, 0:16]
            own = jnp.broadcast_to(wave[None], (16, 16, 128)).reshape(TILE, 128)
            pieces.append(jnp.where(large, big, own))
        encoding = jnp.concatenate(pieces, axis=1) * valid
        hidden = dot(low(spread), entry) + fill * mask_token[...] + encoding
        start[rows] = hidden
        add_row(12, row_sum(valid * hidden * hidden))
        add_row(16, row_sum(valid))
        unit, _ = standardize(hidden)
        norm = low(unit * gains[0:1] + shifts[0:1])
        normed[rows] = norm
        mix = dot(norm, attend[...])
        mixed[rows] = low(mix)
        turned[:, rows] = low(mix[:, 256:].T)

    @pl.loop(0, 2 * tiles)
    def _(step):
        pair, tile = step // tiles, step % tiles
        rows = rows_of(tile)
        own_chip = chip_of(iota((1, TILE), 1) + tile * TILE, sizes, pack)
        key_chip = chip_of(iota((start.shape[0], 1), 0), sizes, pack)
        for half in range(2):
            query = only(mixed[rows, pair_lanes(pair)], half) * BF16(0.125)
            scores = dot_nt(mixed[:, pair_lanes(pair, 256)], query)
            scores = jnp.where(key_chip == own_chip, scores, NEGATIVE)
            expos = jnp.exp(scores - jnp.max(scores, axis=0, keepdims=True))
            prob = low(expos * (1.0 / jnp.sum(expos, axis=0, keepdims=True)))
            probs[pair * 2 + half, :, rows] = prob
            flipped[head_rows(pair, half), rows] = dot(turned[head_rows(pair, half, 256)], prob)

    for copy in loads[2:]:
        copy.wait()

    @pl.loop(0, tiles)
    def _(tile):
        rows = rows_of(tile)
        valid = validity(tile)
        mingled = low(flipped[:, rows].T)
        context[rows] = mingled
        attention = dot(mingled, merging[...]) + biases[1:2]
        add_row(13, row_sum(valid * attention * attention))
        center = start[rows] + attention
        unit, inverse = standardize(center)
        norm = low(unit * gains[1:2] + shifts[1:2])
        normed_two[rows] = norm
        go = target[rows] * valid
        go_below = low(go)
        go_low[rows] = go_below
        add_row(2, row_sum(go))
        feed = jnp.zeros_like(go)
        norm_grad = jnp.zeros_like(go)
        for part in range(4):
            cols = slice(part * 512, part * 512 + 512)
            before = dot(norm, expand[:, cols]) + inner[:, cols]
            value, slope = gelu_pair(before)
            value = low(value)
            active[rows, cols] = value
            feed = feed + dot(value, shrink[cols])
            grad = low(slope * dot_nt(go_below, shrink[cols]))
            before_grad[rows, cols] = grad
            add_row(8 + part, row_sum(grad.astype(F32)))
            norm_grad = norm_grad + dot_nt(grad, expand[:, cols])
        feed = feed + biases[2:3]
        add_row(14, row_sum(valid * feed * feed))
        output = center + feed
        add_row(15, row_sum(valid * output * output))
        add_row(5, row_sum(norm_grad * unit))
        add_row(7, row_sum(norm_grad))
        grad = go + norm_back(unit, inverse, gains[1:2], norm_grad)
        target[rows] = grad
        add_row(1, row_sum(grad))
        below = low(grad)
        attention_low[rows] = below
        context_grad[rows] = low(dot_nt(below, merging[...]))

    for part in range(2):
        cols = slice(part * 256, part * 256 + 256)
        for quarter in range(4):
            wide = slice(quarter * 512, quarter * 512 + 512)
            value = dot_tn(normed_two[:, cols], before_grad[:, wide])
            store_packed(put, part * 16, (DECODER_EXPAND[0] + quarter * 512, 16, 512), value)
        value = dot_tn(attention_low[:, cols], context[...])
        store_packed(put, part * 16, DECODER_MERGE, value)
    for block in range(2):
        put(slice(block * 16, block * 16 + 16), 4352, jnp.zeros((16, 16, 256), F32))
    if reduce:
        await_greetings()
        engine.send(0)

    @pl.loop(0, 8)
    def _(part):
        cols = aligned(part * 256, 256, 256)
        store_packed(put, part * 4, DECODER_SHRINK, dot_tn(active[:, cols], go_low[...]))

    if reduce:
        engine.send(1)
        engine.send(2)

    key_grad[...] = jnp.zeros_like(key_grad)

    @pl.loop(0, 2 * tiles)
    def _(step):
        pair, tile = step // tiles, step % tiles
        rows = rows_of(tile)
        lanes = pair_lanes(pair)
        values = mixed[:, pair_lanes(pair, 512)]
        for half in range(2):
            prob = probs[pair * 2 + half, :, rows]
            outer = only(context_grad[rows, lanes], half)
            wide = prob.astype(F32)
            grad = dot_nt(values, outer)
            raw = low(wide * (grad - jnp.sum(wide * grad, axis=0, keepdims=True)))
            query = only(mixed[rows, lanes], half)
            key_grad[0, :, lanes] += dot(raw, query)
            key_grad[1, :, lanes] += dot(prob, outer)
            flipped[head_rows(pair, half), rows] = dot(turned[head_rows(pair, half)], raw)
        if reduce:
            engine.turn(step)

    def last(tile, entry_grad):
        rows = rows_of(tile)
        mix = jnp.concatenate(
            [low(flipped[:, rows].T * 0.125), low(key_grad[0, rows] * 0.125), low(key_grad[1, rows])],
            axis=1,
        )
        mixed_grad[rows] = mix
        norm_grad = dot_nt(mix, attend[...])
        unit, inverse = standardize(start[rows])
        add_row(4, row_sum(norm_grad * unit))
        add_row(6, row_sum(norm_grad))
        grad = target[rows] + norm_back(unit, inverse, gains[0:1], norm_grad)
        spread = spread_of(tile)
        fill = validity(tile) * (1.0 - jnp.sum(spread, axis=1, keepdims=True))
        add_row(3, row_sum(fill * grad))
        if reduce:
            engine.turn(2 * tiles + tile)
        return entry_grad + dot_tn(low(spread), low(grad))

    entry_grad = lax.fori_loop(0, tiles, last, jnp.zeros((TILE, 512), F32))
    add_row(0, row_sum(entry_grad))
    entry_low = low(entry_grad)
    encoded_grad[...] = low(dot_nt(entry_low, entry_weight[...]))
    store_packed(put_rest, 0, ENTRY, dot_tn(sent[...], entry_low))
    for part in range(2):
        if reduce:
            engine.turn(3 * tiles + part)
        cols = slice(part * 256, part * 256 + 256)
        value = dot_tn(normed[:, cols], mixed_grad[...])
        store_packed(put_rest, part * 16, DECODER_ATTEND, value)
    if reduce:
        engine.close(0)


def decoder_call(
    reduce, sizes, distance, slots, sent, cotangent, entry_weight, biases, mask_token,
    gains, shifts, attend, merging, expand, inner, shrink,
):
    length = cotangent.shape[1]
    width = 512
    frequency = np.exp(-np.log(10000.0) * np.arange(width // 4) / (width // 4)).astype(np.float32)
    columns = DECODER_CHUNKS * SPAN
    if reduce:
        summed = jax.ShapeDtypeStruct((16, columns), F32)
        extra = reducer_scratch(DECODER_CHUNKS, DECODER_CHUNKS)
        params = dict(collective_id=1, has_side_effects=True)
    else:
        summed = jax.ShapeDtypeStruct((2, 16, 16, columns), BF16)
        extra = []
        params = dict()
    return pl.pallas_call(
        functools.partial(decoder_kernel, reduce),
        out_shape=(
            summed,
            jax.ShapeDtypeStruct((2, 16, 16, UNIT), BF16),
            jax.ShapeDtypeStruct((24, width), F32),
            jax.ShapeDtypeStruct((256, 768), BF16),
        ),
        in_specs=[smem_spec()] * 2 + [vmem_spec()] * 8 + [any_spec()] * 6,
        out_specs=(vmem_spec(),) * 4,
        scratch_shapes=[
            pltpu.VMEM((2, 4, 32, 128), F32),
            pltpu.VMEM((length, width), F32),
            pltpu.VMEM((length, width), BF16),
            pltpu.VMEM((length, 768), BF16),
            pltpu.VMEM((512, length), BF16),
            pltpu.VMEM((4, length, length), BF16),
            pltpu.VMEM((256, length), F32),
            pltpu.VMEM((length, 256), BF16),
            pltpu.VMEM((length, width), BF16),
            pltpu.VMEM((length, 2048), BF16),
            pltpu.VMEM((length, 2048), BF16),
            pltpu.VMEM((length, width), BF16),
            pltpu.VMEM((length, width), BF16),
            pltpu.VMEM((length, 256), BF16),
            pltpu.VMEM((2, length, 256), F32),
            pltpu.VMEM((length, 768), BF16),
            pltpu.VMEM((length, width), F32),
            pltpu.VMEM(entry_weight.shape, BF16),
            pltpu.VMEM(attend.shape, BF16),
            pltpu.VMEM(merging.shape, BF16),
            pltpu.VMEM(expand.shape, BF16),
            pltpu.VMEM(shrink.shape, BF16),
            pltpu.SemaphoreType.DMA((6,)),
        ]
        + extra,
        compiler_params=pltpu.CompilerParams(vmem_limit_bytes=60 * 2**20, **params),
        name="decoder_block",
    )(
        sizes, distance, slots, jnp.asarray(frequency)[None], sent, biases, mask_token[None], gains, shifts,
        inner[None], cotangent, entry_weight, attend, merging, expand, shrink,
    )


def encoder_backward_kernel(
    reduce, encoded_grad, sums, decoder_vectors, gains, tokens, rest, attend_far, merging_far, expand_far,
    shrink_far, normed_far, mixed_far, turned_far, probs_far, context_far, middle_far, normed_two_far, active_far,
    slope_far, summed, vectors, tokens_grad, *refs,
):
    if reduce:
        decoder_sums, arrived = refs[:2]
        refs = refs[2:]
    (
        hidden, attend, merging, expand, shrink, normed, mixed, turned, probs, context, middle, normed_two, active,
        slope, before_grad, norm_sum, attention_low, context_grad, key_grad, query_turned, mixed_grad, load_sem,
        part_sem,
    ) = refs[:23]
    pack = lax.axis_index("section")

    def part_loads(part):
        cols = slice(part * 1024, part * 1024 + 1024)
        slot = part % 2
        return [
            pltpu.make_async_copy(expand_far.at[:, cols], expand.at[slot], part_sem.at[slot, 0]),
            pltpu.make_async_copy(shrink_far.at[cols], shrink.at[slot], part_sem.at[slot, 1]),
            pltpu.make_async_copy(slope_far.at[part], slope.at[slot], part_sem.at[slot, 2]),
        ]

    if reduce:
        (
            decoder_total, encoder_total, decoder_got, encoder_got, payload,
            own_sem, small_send, small_recv, pay_send, pay_recv, small_load,
        ) = refs[23:34]
        mine, partner = neighbours()
        greet(partner)
        engine = reducer(CHUNKS, STAGING, mine, partner, summed, refs[34:])
        put = engine.put
        first_own = pltpu.make_async_copy(rest.at[mine["c"]], engine.own.at[:, :, 0:UNIT], own_sem)
        first_own.start()
        decoder_load = pltpu.make_async_copy(decoder_vectors, decoder_total.at[0], small_load)
        decoder_load.start()
    else:
        put = put_into(summed)
    loads = fetch(
        [
            (active_far, active),
            (normed_two_far, normed_two),
            (middle_far, middle),
            (merging_far, merging),
            (context_far, context),
            (mixed_far, mixed),
            (probs_far, probs),
            (turned_far.at[0:768], turned),
            (normed_far, normed),
            (attend_far, attend),
            (tokens.at[pack], hidden),
        ],
        load_sem,
    )
    for part in range(2):
        for copy in part_loads(part):
            copy.start()
    vectors[...] = sums[...]
    go_low = encoded_grad[...]
    go = go_low.astype(F32)
    vectors[1:2, :768] = row_sum(go)
    norm_sum[...] = jnp.zeros_like(norm_sum)

    def send(unit):
        if reduce:
            engine.send(unit)

    def release(unit):
        if reduce:
            engine.release(unit)

    def shrink_grad(part):
        release(1 + part)
        cols = slice(part * 256, part * 256 + 256)
        for piece in range(4):
            rows = slice(piece * 768, piece * 768 + 768)
            store_packed(put, piece * 8, ENCODER_SHRINK[part], dot_tn(active[:, rows], encoded_grad[:, cols]))
        send(1 + part)

    def hidden_layer(part):
        for copy in part_loads(part):
            copy.wait()
        slot = part % 2
        grad = low(slope[slot] * dot_nt(encoded_grad[...], shrink[slot]))
        before_grad[...] = grad
        vectors[6 + part : 7 + part] = row_sum(grad.astype(F32))
        norm_sum[...] += dot_nt(grad, expand[slot])
        if part == 0:
            for copy in part_loads(2):
                copy.start()

    def expand_grad(part):
        release(4 + part)
        if part == 0:
            loads[1].wait()
        store_packed(put, 0, ENCODER_EXPAND[part], dot_tn(normed_two[...], before_grad[...]))
        send(4 + part)

    def middle_layer():
        loads[2].wait()
        loads[3].wait()
        unit, inverse = standardize(middle[...])
        norm_grad = norm_sum[...]
        vectors[3:4, :768] = row_sum(norm_grad * unit)
        vectors[5:6, :768] = row_sum(norm_grad)
        grad = encoded_grad[...].astype(F32) + norm_back(unit, inverse, gains[1:2], norm_grad)
        vectors[0:1, :768] = row_sum(grad)
        tokens_grad[...] = grad
        below = low(grad)
        attention_low[...] = below
        context_grad[...] = low(dot_nt(below, merging[...]))
        for copy in loads[4:8]:
            copy.wait()

    def attention(first):
        @pl.loop(first, first + 2)
        def _(pair):
            lanes = pair_lanes(pair)
            values = mixed[:, pair_lanes(pair, 1536)]
            keys_total = jnp.zeros((TILE, 128), F32)
            values_total = jnp.zeros((TILE, 128), F32)
            for half in range(2):
                prob = probs[pair * 2 + half]
                outer = only(context_grad[:, lanes], half)
                query = only(mixed[:, lanes], half)
                wide = prob.astype(F32)
                grad = dot_nt(values, outer)
                raw = low(wide * (grad - jnp.sum(wide * grad, axis=0, keepdims=True)))
                keys_total = keys_total + dot(raw, query)
                values_total = values_total + dot(prob, outer)
                rows = head_rows(pair, half)
                query_turned[rows] = dot(turned[rows], raw)
            key_grad[0, :, lanes] = keys_total
            key_grad[1, :, lanes] = values_total

    def mixing():
        mixed_grad[:, 0:768] = low(query_turned[...].T * 0.125)
        mixed_grad[:, 768:1536] = low(key_grad[0] * 0.125)
        mixed_grad[:, 1536:2304] = low(key_grad[1])

    def attend_grad(part):
        if part == 0:
            loads[8].wait()
        release(7 + part)
        wide = slice(part * 1024, min(part * 1024 + 1024, 2304))
        store_packed(put, 0, ENCODER_ATTEND[part], dot_tn(normed[...], mixed_grad[:, wide]))
        if part == 2:
            store_packed(put, 0, ENCODER_MERGE, dot_tn(attention_low[...], context[...]))
        send(7 + part)

    def input_layer():
        loads[9].wait()
        loads[10].wait()
        norm_grad = dot_nt(mixed_grad[...], attend[...])
        unit, inverse = standardize(hidden[...])
        vectors[2:3, :768] = row_sum(norm_grad * unit)
        vectors[4:5, :768] = row_sum(norm_grad)
        grad = tokens_grad[...] + norm_back(unit, inverse, gains[0:1], norm_grad)
        tokens_grad[...] = grad
        if reduce:
            payload[...] = low(grad)

    if not reduce:
        loads[0].wait()
        for part in range(3):
            shrink_grad(part)
        for part in range(3):
            hidden_layer(part)
            expand_grad(part)
        middle_layer()
        for first in (0, 2, 4):
            attention(first)
        mixing()
        for part in range(3):
            attend_grad(part)
        input_layer()
        return

    def exchange(source):
        return remote(source, arrived, pay_send, pay_recv, partner["x"])

    small_route = ("c",) + ROUTES[0]
    totals = ((decoder_total, decoder_got), (encoder_total, encoder_got))

    def small_copy(stage, kind):
        source, target = totals[kind]
        return remote(
            source.at[stage],
            target.at[stage],
            small_send.at[stage, kind],
            small_recv.at[stage, kind],
            partner[small_route[stage]],
        )

    def small_advance(stage):
        if stage == 0:
            encoder_total[0] = vectors[...]
        for kind in range(2):
            source, target = totals[kind]
            if stage > 0:
                small_copy(stage - 1, kind).wait_recv()
                source[stage] = source[stage - 1] + target[stage - 1]
            if stage < 5:
                small_copy(stage, kind).start()

    await_greetings()
    for chunk in range(2):
        source = rest.at[1 - mine["c"], :, :, chunk * SPAN : chunk * SPAN + SPAN]
        engine.first_copy(chunk, source).start()

    @pl.when(pack == 0)
    def _():
        exchange(encoded_grad).start()

    loads[0].wait()
    shrink_grad(0)
    first_own.wait()
    decoder_load.wait()

    def attention_end():
        attention(4)
        mixing()

    def input_end():
        input_layer()

        @pl.when(pack == 1)
        def _():
            exchange(payload).start()

    part = functools.partial
    works = [part(shrink_grad, 1), part(shrink_grad, 2)]
    for number in range(3):
        works += [part(hidden_layer, number), part(expand_grad, number)]
    works += [middle_layer, part(attention, 0), part(attention, 2), attention_end]
    works += [part(attend_grad, number) for number in range(3)] + [input_end]
    works = dict(enumerate(works))
    turns = CHUNKS + 4 * LAG
    works.update({turns - 11 + 2 * stage: part(small_advance, stage) for stage in range(6)})

    @pl.loop(0, turns)
    def _(number):
        engine.turn(number)
        for position, work in works.items():
            pl.when(number == position)(work)

    for stage in range(5):
        for kind in range(2):
            small_copy(stage, kind).wait_send()
    exchange(payload).wait()
    engine.close(CHUNKS - STAGING)
    vectors[...] = encoder_total[5]
    decoder_sums[...] = decoder_total[5]


def encoder_backward_call(reduce, tokens, encoded_grad, sums, decoder_vectors, rest, kept, gains, attend, merging, expand, shrink):
    columns = CHUNKS * SPAN
    if reduce:
        summed = jax.ShapeDtypeStruct((16, columns), F32)
        more = (
            jax.ShapeDtypeStruct(decoder_vectors.shape, F32),
            jax.ShapeDtypeStruct((256, 768), BF16),
        )
        more_specs = (vmem_spec(), any_spec())
        extra = [
            pltpu.VMEM((6,) + decoder_vectors.shape, F32),
            pltpu.VMEM((6,) + sums.shape, F32),
            pltpu.VMEM((5,) + decoder_vectors.shape, F32),
            pltpu.VMEM((5,) + sums.shape, F32),
            pltpu.VMEM((256, 768), BF16),
            pltpu.SemaphoreType.DMA,
            pltpu.SemaphoreType.DMA((5, 2)),
            pltpu.SemaphoreType.DMA((5, 2)),
            pltpu.SemaphoreType.DMA,
            pltpu.SemaphoreType.DMA,
            pltpu.SemaphoreType.DMA,
        ] + reducer_scratch(CHUNKS, STAGING)
        params = dict(collective_id=2, has_side_effects=True)
    else:
        summed = jax.ShapeDtypeStruct((2, 16, 16, columns), BF16)
        more, more_specs, extra, params = (), (), [], dict()
    return pl.pallas_call(
        functools.partial(encoder_backward_kernel, reduce),
        out_shape=(
            summed,
            jax.ShapeDtypeStruct(sums.shape, F32),
            jax.ShapeDtypeStruct((256, 768), F32),
        )
        + more,
        in_specs=[vmem_spec()] * 2 + [any_spec(), vmem_spec()] + [any_spec()] * 15,
        out_specs=(vmem_spec(),) * 3 + more_specs,
        scratch_shapes=[
            pltpu.VMEM((256, 768), F32),
            pltpu.VMEM(attend.shape, BF16),
            pltpu.VMEM(merging.shape, BF16),
            pltpu.VMEM((2, 768, 1024), BF16),
            pltpu.VMEM((2, 1024, 768), BF16),
            pltpu.VMEM((256, 768), BF16),
            pltpu.VMEM((256, 2304), BF16),
            pltpu.VMEM((768, 256), BF16),
            pltpu.VMEM((12, 256, 256), BF16),
            pltpu.VMEM((256, 768), BF16),
            pltpu.VMEM((256, 768), F32),
            pltpu.VMEM((256, 768), BF16),
            pltpu.VMEM((256, 3072), BF16),
            pltpu.VMEM((2, 256, 1024), F32),
            pltpu.VMEM((256, 1024), BF16),
            pltpu.VMEM((256, 768), F32),
            pltpu.VMEM((256, 768), BF16),
            pltpu.VMEM((256, 768), BF16),
            pltpu.VMEM((2, 256, 768), F32),
            pltpu.VMEM((768, 256), F32),
            pltpu.VMEM((256, 2304), BF16),
            pltpu.SemaphoreType.DMA((11,)),
            pltpu.SemaphoreType.DMA((2, 3)),
        ]
        + extra,
        compiler_params=pltpu.CompilerParams(vmem_limit_bytes=60 * 2**20, **params),
        name="encoder_backward",
    )(encoded_grad, sums, decoder_vectors, gains, tokens, rest, attend, merging, expand, shrink, *kept)


def unpack(packed, place):
    offset, count, width = place
    pieces = [
        packed[..., offset + i * width : offset + (i + 1) * width] for i in range(count // 16)
    ]
    if count % 16:
        offset = offset + count // 16 * width
        rest = packed[..., offset : offset + width // 2]
        pieces.append(jnp.concatenate([rest[..., :8, :], rest[..., 8:, :]], axis=-1))
    return pieces[0] if len(pieces) == 1 else jnp.concatenate(pieces, axis=-2)


def finish_kernel(
    decoder_summed_far, decoder_sums_far, encoder_sums_far, summed_far, arrived_far, tokens_grad_far, encoded_grad_far,
    boundary, statistics, e_gains, e_shifts, e_biases, e_attend, e_merge, e_expand, e_inner, e_shrink,
    d_entry, d_biases, mask_grad, d_gains, d_shifts, d_attend, d_merge, d_expand, d_inner, d_shrink,
    decoder_summed, decoder_sums, encoder_sums, summed, arrived, tokens_grad, encoded_grad, load_sem,
):
    section = lax.axis_index("section")
    loads = fetch(
        [
            (decoder_summed_far, decoder_summed),
            (decoder_sums_far, decoder_sums),
            (encoder_sums_far, encoder_sums),
            (summed_far, summed),
            (arrived_far, arrived),
            (tokens_grad_far, tokens_grad),
            (encoded_grad_far, encoded_grad),
        ],
        load_sem,
    )
    number = section * lax.axis_size("dp") + lax.axis_index("dp")

    def own(rows, count):
        width = rows.shape[1]
        return pltpu.roll(rows, (width - number * count) % width, axis=1)[:, :count]

    def own_line(rows, count):
        return own(jnp.concatenate([rows[i : i + 1] for i in range(rows.shape[0])], axis=1), count)

    for copy in loads[:3]:
        copy.wait()
    lane = iota((1, 128), 1)
    values = jnp.zeros((1, 128), F32)
    for sums, width, first, count_row, base in ((encoder_sums, DE, 10, 14, 0), (decoder_sums, DD, 12, 16, 4)):
        scale = 1.0 / (sums[count_row : count_row + 1, 0:1] * width)
        for i in range(4):
            value = jnp.sum(sums[first + i : first + i + 1, :], axis=1, keepdims=True) * scale
            values = jnp.where(lane == base + i, value, values)
    statistics[...] = jnp.sqrt(values)[:, :8]
    rows = own(encoder_sums[0:8, :DE], 24)
    e_biases[...] = rows[0:2]
    e_gains[...] = rows[2:4]
    e_shifts[...] = rows[4:6]
    e_inner[...] = own_line(encoder_sums[6:9], 96)
    rows = own(decoder_sums[0:8], 16)
    d_biases[...] = rows[0:3]
    mask_grad[...] = rows[3:4]
    d_gains[...] = rows[4:6]
    d_shifts[...] = rows[6:8]
    d_inner[...] = own_line(decoder_sums[8:12], 64)

    d_merge[...] = unpack(decoder_summed, DECODER_MERGE)
    d_expand[...] = unpack(decoder_summed, DECODER_EXPAND)
    d_shrink[...] = unpack(decoder_summed, DECODER_SHRINK)
    loads[3].wait()
    d_entry[...] = unpack(summed, ENTRY)
    d_attend[...] = unpack(summed, DECODER_ATTEND)
    for target, places in ((e_expand, ENCODER_EXPAND), (e_attend, ENCODER_ATTEND), (e_shrink, ENCODER_SHRINK)):
        start = 0
        for place in places:
            target[:, start : start + place[2]] = unpack(summed, place)
            start += place[2]
    e_merge[...] = unpack(summed, ENCODER_MERGE)
    for copy in loads[4:]:
        copy.wait()

    @pl.when(section == 0)
    def _():
        boundary[0, 0] = tokens_grad[...]
        boundary[0, 1] = arrived[...].astype(F32)

    @pl.when(section == 1)
    def _():
        boundary[0, 0] = arrived[...].astype(F32)
        boundary[0, 1] = encoded_grad[...].astype(F32)


def finish_call(*operands):
    shapes = (
        (1, 2, 256, 768), (1, 8), (2, 24), (2, 24), (2, 24), (24, 2304), (24, 768), (24, 3072), (1, 96), (96, 768),
        (24, 512), (3, 16), (1, 16), (2, 16), (2, 16), (16, 768), (16, 256), (16, 2048), (1, 64), (64, 512),
    )
    outs = list(
        pl.pallas_call(
            finish_kernel,
            out_shape=tuple(jax.ShapeDtypeStruct(shape, F32) for shape in shapes),
            in_specs=[any_spec()] * len(operands),
            out_specs=(vmem_spec(),) * len(shapes),
            scratch_shapes=[pltpu.VMEM(operand.shape, operand.dtype) for operand in operands]
            + [pltpu.SemaphoreType.DMA((len(operands),))],
            compiler_params=pltpu.CompilerParams(vmem_limit_bytes=40 * 2**20),
            name="finish",
        )(*operands)
    )
    for line in (1, 8, 12, 18):
        outs[line] = outs[line].reshape(-1)
    for turned in (6, 16):
        outs[turned] = outs[turned].T
    return tuple(outs)


def scatter_sum(member, share_dim):
    return lax.psum_scatter(
        member, ("section", "dp"), scatter_dimension=share_dim, tiled=True
    )


def finish_generic(decoder_part, part, decoder_sums, encoder_sums, tokens_grad, encoded_grad):
    section = lax.axis_index("section")
    payload = jnp.where(section == 0, encoded_grad, low(tokens_grad))

    def whole(packed, *places):
        packed = jnp.swapaxes(packed, 0, 1).reshape(32, 16, -1)
        blocks = [unpack(packed, place).reshape(32 * place[1], place[2]) for place in places]
        return scatter_sum(jnp.concatenate(blocks, axis=1).astype(F32), 0)

    def line(value):
        return scatter_sum(value, value.ndim - 1)

    arrived = lax.ppermute(payload, "section", [(0, 1), (1, 0)]).astype(F32)
    boundary = jnp.where(
        section == 0,
        jnp.stack([tokens_grad, arrived]),
        jnp.stack([arrived, encoded_grad.astype(F32)]),
    )
    sums = jnp.concatenate(
        [jnp.sum(encoder_sums[10:14], axis=1), jnp.sum(decoder_sums[12:16], axis=1)]
    )
    sums, counts = lax.psum((sums, (encoder_sums[14, 0], decoder_sums[16, 0])), ("section", "dp"))
    scales = jnp.concatenate([jnp.full((4,), counts[0] * DE), jnp.full((4,), counts[1] * DD)])
    return (
        boundary[None],
        jnp.sqrt(sums / scales),
        line(encoder_sums[2:4, :DE]),
        line(encoder_sums[4:6, :DE]),
        line(encoder_sums[0:2, :DE]),
        whole(part, *ENCODER_ATTEND),
        whole(part, ENCODER_MERGE).T,
        whole(part, *ENCODER_EXPAND),
        line(encoder_sums[6:9].reshape(-1)),
        whole(part, *ENCODER_SHRINK),
        whole(decoder_part[1], ENTRY),
        line(decoder_sums[0:3]),
        line(decoder_sums[3]),
        line(decoder_sums[4:6]),
        line(decoder_sums[6:8]),
        whole(decoder_part[1], DECODER_ATTEND),
        whole(decoder_part[0], DECODER_MERGE).T,
        whole(decoder_part[0], DECODER_EXPAND),
        line(decoder_sums[8:12].reshape(-1)),
        whole(decoder_part[0], DECODER_SHRINK),
    )


def body(
    visible_tokens,
    cotangent,
    chip_sizes,
    ground_distance,
    visible_slots,
    encoder_gains,
    encoder_shifts,
    encoder_biases,
    encoder_attend,
    encoder_merge,
    encoder_expand,
    encoder_inner,
    encoder_shrink,
    decoder_entry,
    decoder_biases,
    mask_token,
    decoder_gains,
    decoder_shifts,
    decoder_attend,
    decoder_merge,
    decoder_widen_weight,
    decoder_inner,
    decoder_shrink,
):
    reduce = (lax.axis_size("section"), lax.axis_size("dp")) == (2, 16)
    sent, sums, *kept = encoder_forward_call(
        chip_sizes, visible_tokens, encoder_gains, encoder_shifts, encoder_biases,
        encoder_attend, encoder_merge, encoder_expand, encoder_inner, encoder_shrink,
    )
    decoder_summed, rest, decoder_vectors, encoded_grad = decoder_call(
        reduce, chip_sizes, ground_distance, visible_slots, sent, cotangent, decoder_entry, decoder_biases, mask_token,
        decoder_gains, decoder_shifts, decoder_attend, decoder_merge, decoder_widen_weight, decoder_inner,
        decoder_shrink,
    )
    summed, encoder_sums, tokens_grad, *more = encoder_backward_call(
        reduce, visible_tokens, encoded_grad, sums, decoder_vectors, rest, kept,
        encoder_gains, encoder_attend, encoder_merge, encoder_expand, encoder_shrink,
    )
    if reduce:
        decoder_sums, arrived = more
        return finish_call(
            decoder_summed, decoder_sums, encoder_sums, summed, arrived, tokens_grad, encoded_grad
        )
    return finish_generic(
        (decoder_summed, rest), summed, decoder_vectors, encoder_sums, tokens_grad, encoded_grad
    )


def solution(mesh):
    in_specs = (
        P("dp", None, None),
        P("dp", None, None),
        P("dp", None),
        P("dp", None),
        P("dp", None),
        P(),
        P(),
        P(),
        P(),
        P(),
        P(),
        P(),
        P(),
        P(),
        P(),
        P(),
        P(),
        P(),
        P(),
        P(),
        P(),
        P(),
        P(),
    )
    out_specs = (
        P("section", "dp", None, None),
        P(),
        P(None, ("section", "dp")),
        P(None, ("section", "dp")),
        P(None, ("section", "dp")),
        P(("section", "dp"), None),
        P(None, ("section", "dp")),
        P(("section", "dp"), None),
        P(("section", "dp")),
        P(("section", "dp"), None),
        P(("section", "dp"), None),
        P(None, ("section", "dp")),
        P(("section", "dp")),
        P(None, ("section", "dp")),
        P(None, ("section", "dp")),
        P(("section", "dp"), None),
        P(None, ("section", "dp")),
        P(("section", "dp"), None),
        P(("section", "dp")),
        P(("section", "dp"), None),
    )
    return jax.shard_map(body, mesh=mesh, in_specs=in_specs, out_specs=out_specs, check_vma=False)
```

```python
import functools
import types

import jax
import jax.numpy as jnp
import numpy as np
from jax import lax
from jax.experimental import pallas as pl
from jax.experimental.pallas import tpu as pltpu
from jax.sharding import PartitionSpec as P

DE = 768
DD = 512
TILE = 256
NEGATIVE = -1e30
F32, BF16 = jnp.float32, jnp.bfloat16
MESH_ID = pl.DeviceIdType.MESH

CANON = ("x", "z2", "z1", "y")
ROUTES = (("x", "y", "z1", "z2"), ("y", "x", "z1", "z2"), ("z1", "z2", "x", "y"))
WIDTHS = (2, 3, 1)
OFFSETS = (0, 2, 5)
SPAN = 128 * sum(WIDTHS)
UNIT = 2 * SPAN
DECODER_CHUNKS = 6
CHUNKS = 20
RING = 4
STAGING = 6
LAG = 2

DECODER_EXPAND, DECODER_SHRINK, DECODER_MERGE = (0, 16, 2048), (2048, 64, 512), (4096, 16, 256)
ENTRY, DECODER_ATTEND = (0, 24, 512), (768, 16, 768)
ENCODER_SHRINK = tuple((UNIT * (1 + part), 96, 256) for part in range(3))
ENCODER_EXPAND = tuple((UNIT * (4 + part), 24, 1024) for part in range(3))
ENCODER_ATTEND = ((UNIT * 7, 24, 1024), (UNIT * 8, 24, 1024), (UNIT * 9, 24, 256))
ENCODER_MERGE = (UNIT * 9 + 384, 24, 768)


def dot(a, b):
    return jnp.dot(a, b, preferred_element_type=F32)


def dot_nt(a, b):
    return lax.dot_general(a, b, (((1,), (1,)), ((), ())), preferred_element_type=F32)


def dot_tn(a, b):
    return lax.dot_general(a, b, (((0,), (0,)), ((), ())), preferred_element_type=F32)


def low(value):
    return value.astype(BF16)


def standardize(values):
    centered = values - jnp.mean(values, axis=-1, keepdims=True)
    inverse = lax.rsqrt(jnp.mean(centered * centered, axis=-1, keepdims=True) + 1e-05)
    return centered * inverse, inverse


def norm_back(unit, inverse, gain, grad):
    inner = grad * gain
    return inverse * (
        inner
        - jnp.mean(inner, axis=-1, keepdims=True)
        - unit * jnp.mean(inner * unit, axis=-1, keepdims=True)
    )


def row_sum(values):
    return jnp.sum(values, axis=0, keepdims=True)


def gelu_pair(before):
    half = 0.5 * (1.0 + lax.erf(before * 0.7071067811865476))
    density = jnp.exp(-0.5 * before * before) * 0.3989422804014327
    return before * half, half + before * density


def chip_of(places, sizes, pack):
    end = sizes[pack, 0]
    chip = (places >= end).astype(jnp.int32)
    for slot in range(1, 4):
        end = end + sizes[pack, slot]
        chip = chip + (places >= end).astype(jnp.int32)
    return chip


def iota(shape, dimension):
    return lax.broadcasted_iota(jnp.int32, shape, dimension)


def aligned(start, size, unit):
    return pl.ds(pl.multiple_of(start, unit), size)


def pair_lanes(pair, base=0):
    return aligned(base + pair * 128, 128, 128)


def head_rows(pair, half, base=0):
    return aligned(base + pair * 128 + half * 64, 64, 64)


def rows_of(tile):
    return aligned(tile * TILE, TILE, TILE)


def only(values, half):
    return jnp.where(iota((1, 128), 1) // 64 == half, values, jnp.zeros_like(values))


def fetch(pairs, sems):
    copies = [
        pltpu.make_async_copy(source, target, sems.at[i]) for i, (source, target) in enumerate(pairs)
    ]
    for copy in copies:
        copy.start()
    return copies


def store_packed(put, first, place, value):
    offset, count, width = place
    value = value.reshape(-1, count, width)
    shards = slice(first, first + value.shape[0]) if isinstance(first, int) else pl.ds(first, value.shape[0])
    for piece in range(count // 16):
        put(shards, offset + piece * width, value[:, piece * 16 : piece * 16 + 16])
    if count % 16:
        half = width // 2
        rest = value[:, count - 8 :]
        rest = jnp.concatenate([rest[:, :, :half], rest[:, :, half:]], axis=1)
        put(shards, offset + count // 16 * width, rest)


def halves(shards, value):
    pairs = value.reshape(value.shape[0] // 2, 2, *value.shape[1:])
    if isinstance(shards, slice):
        return slice(shards.start // 2, shards.stop // 2), pairs[:, 0], pairs[:, 1]
    return pl.ds(shards.start // 2, shards.size // 2), pairs[:, 0], pairs[:, 1]


def place_of(names, bits):
    index = 0
    for name in names:
        index = index * 2 + bits[name]
    return index


def left_after(route, stage):
    return tuple(name for name in CANON if name not in route[:stage])


def choices(names):
    for number in range(2 ** len(names)):
        yield {name: (number >> (len(names) - 1 - i)) & 1 for i, name in enumerate(names)}


def neighbours():
    section = lax.axis_index("section")
    data = lax.axis_index("dp")
    mine = {"x": section, "c": data % 2, "y": data // 2 % 2, "z1": data // 4 % 2, "z2": data // 8 % 2}
    partner = {"x": (1 - section, data)}
    for name, step in {"c": 1, "y": 2, "z1": 4, "z2": 8}.items():
        partner[name] = (section, data + step * (1 - 2 * mine[name]))
    return mine, partner


def greet(partner):
    barrier = pltpu.get_barrier_semaphore()
    for name in ("c",) + CANON:
        pl.semaphore_signal(barrier, inc=1, device_id=partner[name], device_id_type=MESH_ID)


def await_greetings():
    pl.semaphore_wait(pltpu.get_barrier_semaphore(), 5)


def remote(source, target, send, recv, device):
    return pltpu.make_async_remote_copy(
        src_ref=source,
        dst_ref=target,
        send_sem=send,
        recv_sem=recv,
        device_id=device,
        device_id_type=MESH_ID,
    )


def reducer(chunks, slots, mine, partner, out, refs):
    own, staging, first = refs[:3]
    sent, got = refs[3:15], refs[15:27]
    first_send, first_recv, send_sem, recv_sem = refs[27:31]

    def first_copy(chunk, source=None):
        if source is None:
            source = staging.at[chunk % slots]
        return remote(source, first.at[chunk], first_send.at[chunk], first_recv.at[chunk], partner["c"])

    def stage_copy(route, stage, chunk):
        return remote(
            sent[route * 4 + stage].at[chunk % RING],
            got[route * 4 + stage].at[chunk],
            send_sem.at[route, stage, chunk],
            recv_sem.at[route, stage, chunk],
            partner[ROUTES[route][stage]],
        )

    def total(route, stage, chunk, bits):
        spot = place_of(CANON, bits)
        cols = slice(OFFSETS[route] * 128, (OFFSETS[route] + WIDTHS[route]) * 128)
        value = own[chunk, spot, :, cols].astype(F32) + first[chunk, spot, :, cols].astype(F32)
        for earlier in range(stage):
            names = left_after(ROUTES[route], earlier + 1)
            value = value + got[route * 4 + earlier][chunk, place_of(names, bits)].astype(F32)
        return value

    def advance(stage, chunk):
        for route in range(3):
            if stage:
                stage_copy(route, stage - 1, chunk).wait_recv()
            else:
                first_copy(chunk).wait_recv() if route == 0 else None
            if stage < 4:

                @pl.when(chunk >= RING)
                def _(route=route):
                    stage_copy(route, stage, chunk - RING).wait_send()

        values = []
        for route in range(3):
            path = ROUTES[route]
            if stage == 4:
                values.append(total(route, 4, chunk, mine))
                continue
            names = left_after(path, stage + 1)
            for free in choices(names):
                bits = dict(mine)
                bits[path[stage]] = 1 - mine[path[stage]]
                bits.update(free)
                values.append((route, place_of(names, free), low(total(route, stage, chunk, bits))))
        if stage == 4:
            out[chunk] = jnp.concatenate(values, axis=1)
            return
        for route, spot, value in values:
            sent[route * 4 + stage][chunk % RING, spot] = value
        for route in range(3):
            stage_copy(route, stage, chunk).start()

    def turn(number):
        for stage in range(4, -1, -1):
            chunk = number - LAG * stage
            pl.when((chunk >= 0) & (chunk < chunks))(functools.partial(advance, stage, chunk))

    def put(shards, column, value):
        shards, even, odd = halves(shards, value)
        kept = low(jnp.where(mine["c"] == 0, even, odd))
        given = low(jnp.where(mine["c"] == 0, odd, even))
        width = value.shape[2]
        done = 0
        while done < width:
            chunk, start = divmod(column + done, SPAN)
            size = min(width - done, SPAN - start)
            own[chunk, shards, :, start : start + size] = kept[:, :, done : done + size]
            staging[chunk % slots, shards, :, start : start + size] = given[:, :, done : done + size]
            done += size

    def release(unit):
        for chunk in (2 * unit, 2 * unit + 1):
            if chunk >= slots:
                first_copy(chunk - slots).wait_send()

    def send(unit):
        for chunk in (2 * unit, 2 * unit + 1):
            first_copy(chunk).start()

    def close(released):
        for chunk in range(released, chunks):
            first_copy(chunk).wait_send()
        for chunk in range(chunks - RING, chunks):
            for route in range(3):
                for stage in range(4):
                    stage_copy(route, stage, chunk).wait_send()

    return types.SimpleNamespace(
        own=own, first_copy=first_copy, turn=turn, put=put, release=release, send=send, close=close
    )


def reducer_scratch(chunks, slots):
    stages = [(width, block) for width in WIDTHS for block in (8, 4, 2, 1)]
    return (
        [
            pltpu.VMEM((chunks, 16, 16, SPAN), BF16),
            pltpu.VMEM((slots, 16, 16, SPAN), BF16),
            pltpu.VMEM((chunks, 16, 16, SPAN), BF16),
        ]
        + [pltpu.VMEM((RING, block, 16, width * 128), BF16) for width, block in stages]
        + [pltpu.VMEM((chunks, block, 16, width * 128), BF16) for width, block in stages]
        + [
            pltpu.SemaphoreType.DMA((chunks,)),
            pltpu.SemaphoreType.DMA((chunks,)),
            pltpu.SemaphoreType.DMA((3, 4, chunks)),
            pltpu.SemaphoreType.DMA((3, 4, chunks)),
        ]
    )


def put_into(parts):
    def put(shards, column, value):
        shards, *pair = halves(shards, value)
        width = value.shape[2]
        done = 0
        while done < width:
            chunk, start = divmod(column + done, SPAN)
            size = min(width - done, SPAN - start)
            for core in range(2):
                parts[chunk, core, shards, :, start : start + size] = low(pair[core][:, :, done : done + size])
            done += size

    return put


def vmem_spec():
    return pl.BlockSpec(memory_space=pltpu.VMEM)


def any_spec():
    return pl.BlockSpec(memory_space=pl.ANY)


def smem_spec():
    return pl.BlockSpec(memory_space=pltpu.SMEM)


def encoder_forward_kernel(
    sizes, gains, shifts, biases, inner, tokens, attend_far, merging_far, expand_far, shrink_far,
    sent, vectors, *refs,
):
    far = refs[:9]
    normed, mixed, turned, probs, context, middle, normed_two, active, slope = refs[9:18]
    hidden, attend, merging, expand, shrink, context_turned, load_sem, save_sem = refs[18:]
    pack = lax.axis_index("section")
    loads = fetch(
        [
            (tokens.at[pack], hidden),
            *[(attend_far.at[:, i * 768 : i * 768 + 768], attend.at[:, i * 768 : i * 768 + 768]) for i in range(3)],
            (merging_far, merging),
            *[(expand_far.at[:, i * 1024 : i * 1024 + 1024], expand.at[:, i * 1024 : i * 1024 + 1024]) for i in range(3)],
            *[(shrink_far.at[i * 1024 : i * 1024 + 1024], shrink.at[i * 1024 : i * 1024 + 1024]) for i in range(3)],
        ],
        load_sem,
    )
    saves = []

    def save(*numbers):
        for number in numbers:
            copy = pltpu.make_async_copy(refs[9 + number], far[number], save_sem.at[number])
            copy.start()
            saves.append(copy)

    vectors[...] = jnp.zeros_like(vectors)
    key_chip = chip_of(4 * iota((TILE, 1), 0), sizes, pack)
    own_chip = chip_of(4 * iota((1, TILE), 1), sizes, pack)
    valid = (key_chip < 4).astype(F32)
    loads[0].wait()
    values = hidden[...]
    vectors[10:11, :768] = row_sum(valid * values * values)
    unit, _ = standardize(values)
    norm = low(unit * gains[0:1] + shifts[0:1])
    normed[...] = norm
    for part in range(3):
        cols = slice(part * 768, part * 768 + 768)
        loads[1 + part].wait()
        mix = dot(norm, attend[:, cols])
        mixed[:, cols] = low(mix)
        if part:
            turned[(part - 1) * 768 : part * 768] = low(mix.T)
    save(0, 1, 2)

    @pl.loop(0, 6)
    def _(pair):
        keys = mixed[:, pair_lanes(pair, 768)]
        for half in range(2):
            query = only(mixed[:, pair_lanes(pair)], half) * BF16(0.125)
            scores = jnp.where(key_chip == own_chip, dot_nt(keys, query), NEGATIVE)
            expos = jnp.exp(scores - jnp.max(scores, axis=0, keepdims=True))
            prob = low(expos * (1.0 / jnp.sum(expos, axis=0, keepdims=True)))
            probs[pair * 2 + half] = prob
            context_turned[head_rows(pair, half)] = dot(turned[head_rows(pair, half, 768)], prob)

    mingled = low(context_turned[...].T)
    context[...] = mingled
    save(3, 4)
    loads[4].wait()
    attention = dot(mingled, merging[...]) + biases[0:1]
    vectors[11:12, :768] = row_sum(valid * attention * attention)
    center = hidden[...] + attention
    middle[...] = center
    unit, _ = standardize(center)
    norm = low(unit * gains[1:2] + shifts[1:2])
    normed_two[...] = norm
    save(5, 6)
    feed = jnp.zeros_like(center)
    for part in range(3):
        cols = slice(part * 1024, part * 1024 + 1024)
        loads[5 + part].wait()
        value, slant = gelu_pair(dot(norm, expand[:, cols]) + inner[:, cols])
        value = low(value)
        active[:, cols] = value
        slope[part] = slant
        loads[8 + part].wait()
        feed = feed + dot(value, shrink[cols])
    save(7, 8)
    feed = feed + biases[1:2]
    vectors[12:13, :768] = row_sum(valid * feed * feed)
    output = center + feed
    vectors[13:14, :768] = row_sum(valid * output * output)
    vectors[14:15, :768] = jnp.broadcast_to(row_sum(valid), (1, 768))
    sent[...] = low(output)
    for copy in saves:
        copy.wait()


def encoder_forward_call(sizes, tokens, gains, shifts, biases, attend, merging, expand, inner, shrink):
    shapes = (
        ((256, 768), BF16),
        ((256, 2304), BF16),
        ((1536, 256), BF16),
        ((12, 256, 256), BF16),
        ((256, 768), BF16),
        ((256, 768), F32),
        ((256, 768), BF16),
        ((256, 3072), BF16),
        ((3, 256, 1024), F32),
    )
    return pl.pallas_call(
        encoder_forward_kernel,
        out_shape=(jax.ShapeDtypeStruct((256, 768), BF16), jax.ShapeDtypeStruct((16, 1024), F32))
        + tuple(jax.ShapeDtypeStruct(*shape) for shape in shapes),
        in_specs=[smem_spec()] + [vmem_spec()] * 4 + [any_spec()] * 5,
        out_specs=(vmem_spec(),) * 2 + (any_spec(),) * len(shapes),
        scratch_shapes=[pltpu.VMEM(*shape) for shape in shapes]
        + [
            pltpu.VMEM((256, 768), F32),
            pltpu.VMEM(attend.shape, BF16),
            pltpu.VMEM(merging.shape, BF16),
            pltpu.VMEM(expand.shape, BF16),
            pltpu.VMEM(shrink.shape, BF16),
            pltpu.VMEM((768, 256), F32),
            pltpu.SemaphoreType.DMA((11,)),
            pltpu.SemaphoreType.DMA((len(shapes),)),
        ],
        compiler_params=pltpu.CompilerParams(vmem_limit_bytes=60 * 2**20),
        name="encoder_forward",
    )(sizes, gains, shifts, biases, inner[None], tokens, attend, merging, expand, shrink)


def decoder_kernel(
    reduce, sizes, distance, slots, frequency, sent, biases, mask_token, gains, shifts, inner,
    cotangent, entry_far, attend_far, merging_far, expand_far, shrink_far,
    summed, rest, vectors, encoded_grad, *refs,
):
    (
        table, start, normed, mixed, turned, probs, flipped, context, normed_two, active,
        before_grad, go_low, attention_low, context_grad, key_grad, mixed_grad, target,
        entry_weight, attend, merging, expand, shrink, load_sem,
    ) = refs[:23]
    pack = lax.axis_index("section")
    if reduce:
        mine, partner = neighbours()
        greet(partner)
        engine = reducer(DECODER_CHUNKS, DECODER_CHUNKS, mine, partner, summed, refs[23:])
        put = engine.put
    else:
        put = put_into(summed)
    put_rest = put_into(rest)
    loads = fetch(
        [
            (entry_far, entry_weight),
            (attend_far, attend),
            (cotangent.at[pack], target),
            (merging_far, merging),
            (expand_far, expand),
            (shrink_far, shrink),
        ],
        load_sem,
    )
    tiles = start.shape[0] // TILE
    vectors[...] = jnp.zeros_like(vectors)
    large = sizes[pack, 0] == 1024

    def add_row(row, value):
        vectors[row : row + 1, :] += value

    positions = iota((32, 128), 0).astype(F32)
    for chip in range(4):
        spacing = distance[pack, chip].astype(F32) / 16.0
        angle = positions * (spacing * frequency[...])
        table[0, chip] = jnp.sin(angle)
        table[1, chip] = jnp.cos(angle)
    loads[0].wait()
    entry = low(dot(sent[...], entry_weight[...]) + biases[0:1])
    loads[1].wait()

    def validity(tile):
        places = iota((TILE, 1), 0) + tile * TILE
        return (chip_of(places, sizes, pack) < 4).astype(F32)

    def spread_of(tile):
        return (slots[pl.ds(pack, 1)] == iota((TILE, TILE), 0) + tile * TILE).astype(F32)

    @pl.loop(0, tiles)
    def _(tile):
        rows = rows_of(tile)
        valid = validity(tile)
        spread = spread_of(tile)
        fill = valid * (1.0 - jnp.sum(spread, axis=1, keepdims=True))
        pieces = []
        for kind in range(2):
            wave = table[kind, 0, aligned(tile * 8, 8, 8)]
            big = jnp.broadcast_to(wave[:, None], (8, 32, 128)).reshape(TILE, 128)
            wave = table[kind, tile, 0:16]
            own = jnp.broadcast_to(wave[:, None], (16, 16, 128)).reshape(TILE, 128)
            pieces.append(jnp.where(large, big, own))
        for kind in range(2):
            wave = table[kind, 0]
            big = jnp.broadcast_to(wave[None], (8, 32, 128)).reshape(TILE, 128)
            wave = table[kind, tile, 0:16]
            own = jnp.broadcast_to(wave[None], (16, 16, 128)).reshape(TILE, 128)
            pieces.append(jnp.where(large, big, own))
        encoding = jnp.concatenate(pieces, axis=1) * valid
        hidden = dot(low(spread), entry) + fill * mask_token[...] + encoding
        start[rows] = hidden
        add_row(12, row_sum(valid * hidden * hidden))
        add_row(16, row_sum(valid))
        unit, _ = standardize(hidden)
        norm = low(unit * gains[0:1] + shifts[0:1])
        normed[rows] = norm
        mix = dot(norm, attend[...])
        mixed[rows] = low(mix)
        turned[:, rows] = low(mix[:, 256:].T)

    @pl.loop(0, 2 * tiles)
    def _(step):
        pair, tile = step // tiles, step % tiles
        rows = rows_of(tile)
        own_chip = chip_of(iota((1, TILE), 1) + tile * TILE, sizes, pack)
        key_chip = chip_of(iota((start.shape[0], 1), 0), sizes, pack)
        for half in range(2):
            query = only(mixed[rows, pair_lanes(pair)], half) * BF16(0.125)
            scores = dot_nt(mixed[:, pair_lanes(pair, 256)], query)
            scores = jnp.where(key_chip == own_chip, scores, NEGATIVE)
            expos = jnp.exp(scores - jnp.max(scores, axis=0, keepdims=True))
            prob = low(expos * (1.0 / jnp.sum(expos, axis=0, keepdims=True)))
            probs[pair * 2 + half, :, rows] = prob
            flipped[head_rows(pair, half), rows] = dot(turned[head_rows(pair, half, 256)], prob)

    for copy in loads[2:]:
        copy.wait()

    @pl.loop(0, tiles)
    def _(tile):
        rows = rows_of(tile)
        valid = validity(tile)
        mingled = low(flipped[:, rows].T)
        context[rows] = mingled
        attention = dot(mingled, merging[...]) + biases[1:2]
        add_row(13, row_sum(valid * attention * attention))
        center = start[rows] + attention
        unit, inverse = standardize(center)
        norm = low(unit * gains[1:2] + shifts[1:2])
        normed_two[rows] = norm
        go = target[rows] * valid
        go_below = low(go)
        go_low[rows] = go_below
        add_row(2, row_sum(go))
        feed = jnp.zeros_like(go)
        norm_grad = jnp.zeros_like(go)
        for part in range(4):
            cols = slice(part * 512, part * 512 + 512)
            before = dot(norm, expand[:, cols]) + inner[:, cols]
            value, slope = gelu_pair(before)
            value = low(value)
            active[rows, cols] = value
            feed = feed + dot(value, shrink[cols])
            grad = low(slope * dot_nt(go_below, shrink[cols]))
            before_grad[rows, cols] = grad
            add_row(8 + part, row_sum(grad.astype(F32)))
            norm_grad = norm_grad + dot_nt(grad, expand[:, cols])
        feed = feed + biases[2:3]
        add_row(14, row_sum(valid * feed * feed))
        output = center + feed
        add_row(15, row_sum(valid * output * output))
        add_row(5, row_sum(norm_grad * unit))
        add_row(7, row_sum(norm_grad))
        grad = go + norm_back(unit, inverse, gains[1:2], norm_grad)
        target[rows] = grad
        add_row(1, row_sum(grad))
        below = low(grad)
        attention_low[rows] = below
        context_grad[rows] = low(dot_nt(below, merging[...]))

    for part in range(2):
        cols = slice(part * 256, part * 256 + 256)
        for quarter in range(4):
            wide = slice(quarter * 512, quarter * 512 + 512)
            value = dot_tn(normed_two[:, cols], before_grad[:, wide])
            store_packed(put, part * 16, (DECODER_EXPAND[0] + quarter * 512, 16, 512), value)
        value = dot_tn(attention_low[:, cols], context[...])
        store_packed(put, part * 16, DECODER_MERGE, value)
    for block in range(2):
        put(slice(block * 16, block * 16 + 16), 4352, jnp.zeros((16, 16, 256), F32))
    if reduce:
        await_greetings()
        engine.send(0)

    @pl.loop(0, 8)
    def _(part):
        cols = aligned(part * 256, 256, 256)
        store_packed(put, part * 4, DECODER_SHRINK, dot_tn(active[:, cols], go_low[...]))

    if reduce:
        engine.send(1)
        engine.send(2)

    key_grad[...] = jnp.zeros_like(key_grad)

    @pl.loop(0, 2 * tiles)
    def _(step):
        pair, tile = step // tiles, step % tiles
        rows = rows_of(tile)
        lanes = pair_lanes(pair)
        values = mixed[:, pair_lanes(pair, 512)]
        for half in range(2):
            prob = probs[pair * 2 + half, :, rows]
            outer = only(context_grad[rows, lanes], half)
            wide = prob.astype(F32)
            grad = dot_nt(values, outer)
            raw = low(wide * (grad - jnp.sum(wide * grad, axis=0, keepdims=True)))
            query = only(mixed[rows, lanes], half)
            key_grad[0, :, lanes] += dot(raw, query)
            key_grad[1, :, lanes] += dot(prob, outer)
            flipped[head_rows(pair, half), rows] = dot(turned[head_rows(pair, half)], raw)
        if reduce:
            engine.turn(step)

    def last(tile, entry_grad):
        rows = rows_of(tile)
        mix = jnp.concatenate(
            [low(flipped[:, rows].T * 0.125), low(key_grad[0, rows] * 0.125), low(key_grad[1, rows])],
            axis=1,
        )
        mixed_grad[rows] = mix
        norm_grad = dot_nt(mix, attend[...])
        unit, inverse = standardize(start[rows])
        add_row(4, row_sum(norm_grad * unit))
        add_row(6, row_sum(norm_grad))
        grad = target[rows] + norm_back(unit, inverse, gains[0:1], norm_grad)
        spread = spread_of(tile)
        fill = validity(tile) * (1.0 - jnp.sum(spread, axis=1, keepdims=True))
        add_row(3, row_sum(fill * grad))
        if reduce:
            engine.turn(2 * tiles + tile)
        return entry_grad + dot_tn(low(spread), low(grad))

    entry_grad = lax.fori_loop(0, tiles, last, jnp.zeros((TILE, 512), F32))
    add_row(0, row_sum(entry_grad))
    entry_low = low(entry_grad)
    encoded_grad[...] = low(dot_nt(entry_low, entry_weight[...]))
    store_packed(put_rest, 0, ENTRY, dot_tn(sent[...], entry_low))
    for part in range(2):
        if reduce:
            engine.turn(3 * tiles + part)
        cols = slice(part * 256, part * 256 + 256)
        value = dot_tn(normed[:, cols], mixed_grad[...])
        store_packed(put_rest, part * 16, DECODER_ATTEND, value)
    if reduce:
        engine.close(0)


def decoder_call(
    reduce, sizes, distance, slots, sent, cotangent, entry_weight, biases, mask_token,
    gains, shifts, attend, merging, expand, inner, shrink,
):
    length = cotangent.shape[1]
    width = 512
    frequency = np.exp(-np.log(10000.0) * np.arange(width // 4) / (width // 4)).astype(np.float32)
    if reduce:
        summed = jax.ShapeDtypeStruct((DECODER_CHUNKS, 16, SPAN), F32)
        extra = reducer_scratch(DECODER_CHUNKS, DECODER_CHUNKS)
        params = dict(collective_id=1, has_side_effects=True)
    else:
        summed = jax.ShapeDtypeStruct((DECODER_CHUNKS, 2, 16, 16, SPAN), BF16)
        extra = []
        params = dict()
    return pl.pallas_call(
        functools.partial(decoder_kernel, reduce),
        out_shape=(
            summed,
            jax.ShapeDtypeStruct((2, 2, 16, 16, SPAN), BF16),
            jax.ShapeDtypeStruct((24, width), F32),
            jax.ShapeDtypeStruct((256, 768), BF16),
        ),
        in_specs=[smem_spec()] * 2 + [vmem_spec()] * 8 + [any_spec()] * 6,
        out_specs=(vmem_spec(),) * 4,
        scratch_shapes=[
            pltpu.VMEM((2, 4, 32, 128), F32),
            pltpu.VMEM((length, width), F32),
            pltpu.VMEM((length, width), BF16),
            pltpu.VMEM((length, 768), BF16),
            pltpu.VMEM((512, length), BF16),
            pltpu.VMEM((4, length, length), BF16),
            pltpu.VMEM((256, length), F32),
            pltpu.VMEM((length, 256), BF16),
            pltpu.VMEM((length, width), BF16),
            pltpu.VMEM((length, 2048), BF16),
            pltpu.VMEM((length, 2048), BF16),
            pltpu.VMEM((length, width), BF16),
            pltpu.VMEM((length, width), BF16),
            pltpu.VMEM((length, 256), BF16),
            pltpu.VMEM((2, length, 256), F32),
            pltpu.VMEM((length, 768), BF16),
            pltpu.VMEM((length, width), F32),
            pltpu.VMEM(entry_weight.shape, BF16),
            pltpu.VMEM(attend.shape, BF16),
            pltpu.VMEM(merging.shape, BF16),
            pltpu.VMEM(expand.shape, BF16),
            pltpu.VMEM(shrink.shape, BF16),
            pltpu.SemaphoreType.DMA((6,)),
        ]
        + extra,
        compiler_params=pltpu.CompilerParams(vmem_limit_bytes=60 * 2**20, **params),
        name="decoder_block",
    )(
        sizes, distance, slots, jnp.asarray(frequency)[None], sent, biases, mask_token[None], gains, shifts,
        inner[None], cotangent, entry_weight, attend, merging, expand, shrink,
    )


def encoder_backward_kernel(
    reduce, encoded_grad, sums, decoder_vectors, gains, tokens, rest, attend_far, merging_far, expand_far,
    shrink_far, normed_far, mixed_far, turned_far, probs_far, context_far, middle_far, normed_two_far, active_far,
    slope_far, summed, vectors, tokens_grad, *refs,
):
    if reduce:
        decoder_sums, arrived = refs[:2]
        refs = refs[2:]
    (
        hidden, attend, merging, expand, shrink, normed, mixed, turned, probs, context, middle, normed_two, active,
        slope, before_grad, norm_sum, attention_low, context_grad, key_grad, query_turned, mixed_grad, load_sem,
        part_sem,
    ) = refs[:23]
    pack = lax.axis_index("section")

    def part_loads(part):
        cols = slice(part * 1024, part * 1024 + 1024)
        slot = part % 2
        return [
            pltpu.make_async_copy(expand_far.at[:, cols], expand.at[slot], part_sem.at[slot, 0]),
            pltpu.make_async_copy(shrink_far.at[cols], shrink.at[slot], part_sem.at[slot, 1]),
            pltpu.make_async_copy(slope_far.at[part], slope.at[slot], part_sem.at[slot, 2]),
        ]

    if reduce:
        (
            decoder_total, encoder_total, decoder_got, encoder_got, payload,
            own_sem, small_send, small_recv, pay_send, pay_recv, small_load,
        ) = refs[23:34]
        mine, partner = neighbours()
        greet(partner)
        engine = reducer(CHUNKS, STAGING, mine, partner, summed, refs[34:])
        put = engine.put
        first_own = [
            pltpu.make_async_copy(rest.at[chunk, mine["c"]], engine.own.at[chunk], own_sem.at[chunk])
            for chunk in range(2)
        ]
        for copy in first_own:
            copy.start()
        decoder_load = pltpu.make_async_copy(decoder_vectors, decoder_total.at[0], small_load)
        decoder_load.start()
    else:
        put = put_into(summed)
    loads = fetch(
        [
            (active_far, active),
            (normed_two_far, normed_two),
            (middle_far, middle),
            (merging_far, merging),
            (context_far, context),
            (mixed_far, mixed),
            (probs_far, probs),
            (turned_far.at[0:768], turned),
            (normed_far, normed),
            (attend_far, attend),
            (tokens.at[pack], hidden),
        ],
        load_sem,
    )
    for part in range(2):
        for copy in part_loads(part):
            copy.start()
    vectors[...] = sums[...]
    go_low = encoded_grad[...]
    go = go_low.astype(F32)
    vectors[1:2, :768] = row_sum(go)
    norm_sum[...] = jnp.zeros_like(norm_sum)

    def send(unit):
        if reduce:
            engine.send(unit)

    def release(unit):
        if reduce:
            engine.release(unit)

    def shrink_grad(part):
        release(1 + part)
        cols = slice(part * 256, part * 256 + 256)
        for piece in range(4):
            rows = slice(piece * 768, piece * 768 + 768)
            store_packed(put, piece * 8, ENCODER_SHRINK[part], dot_tn(active[:, rows], encoded_grad[:, cols]))
        send(1 + part)

    def hidden_layer(part):
        for copy in part_loads(part):
            copy.wait()
        slot = part % 2
        grad = low(slope[slot] * dot_nt(encoded_grad[...], shrink[slot]))
        before_grad[...] = grad
        vectors[6 + part : 7 + part] = row_sum(grad.astype(F32))
        norm_sum[...] += dot_nt(grad, expand[slot])
        if part == 0:
            for copy in part_loads(2):
                copy.start()

    def expand_grad(part):
        release(4 + part)
        if part == 0:
            loads[1].wait()
        store_packed(put, 0, ENCODER_EXPAND[part], dot_tn(normed_two[...], before_grad[...]))
        send(4 + part)

    def middle_layer():
        loads[2].wait()
        loads[3].wait()
        unit, inverse = standardize(middle[...])
        norm_grad = norm_sum[...]
        vectors[3:4, :768] = row_sum(norm_grad * unit)
        vectors[5:6, :768] = row_sum(norm_grad)
        grad = encoded_grad[...].astype(F32) + norm_back(unit, inverse, gains[1:2], norm_grad)
        vectors[0:1, :768] = row_sum(grad)
        tokens_grad[...] = grad
        below = low(grad)
        attention_low[...] = below
        context_grad[...] = low(dot_nt(below, merging[...]))
        for copy in loads[4:8]:
            copy.wait()

    def attention(first):
        @pl.loop(first, first + 2)
        def _(pair):
            lanes = pair_lanes(pair)
            values = mixed[:, pair_lanes(pair, 1536)]
            keys_total = jnp.zeros((TILE, 128), F32)
            values_total = jnp.zeros((TILE, 128), F32)
            for half in range(2):
                prob = probs[pair * 2 + half]
                outer = only(context_grad[:, lanes], half)
                query = only(mixed[:, lanes], half)
                wide = prob.astype(F32)
                grad = dot_nt(values, outer)
                raw = low(wide * (grad - jnp.sum(wide * grad, axis=0, keepdims=True)))
                keys_total = keys_total + dot(raw, query)
                values_total = values_total + dot(prob, outer)
                rows = head_rows(pair, half)
                query_turned[rows] = dot(turned[rows], raw)
            key_grad[0, :, lanes] = keys_total
            key_grad[1, :, lanes] = values_total

    def mixing():
        mixed_grad[:, 0:768] = low(query_turned[...].T * 0.125)
        mixed_grad[:, 768:1536] = low(key_grad[0] * 0.125)
        mixed_grad[:, 1536:2304] = low(key_grad[1])

    def attend_grad(part):
        if part == 0:
            loads[8].wait()
        release(7 + part)
        wide = slice(part * 1024, min(part * 1024 + 1024, 2304))
        store_packed(put, 0, ENCODER_ATTEND[part], dot_tn(normed[...], mixed_grad[:, wide]))
        if part == 2:
            store_packed(put, 0, ENCODER_MERGE, dot_tn(attention_low[...], context[...]))
        send(7 + part)

    def input_layer():
        loads[9].wait()
        loads[10].wait()
        norm_grad = dot_nt(mixed_grad[...], attend[...])
        unit, inverse = standardize(hidden[...])
        vectors[2:3, :768] = row_sum(norm_grad * unit)
        vectors[4:5, :768] = row_sum(norm_grad)
        grad = tokens_grad[...] + norm_back(unit, inverse, gains[0:1], norm_grad)
        tokens_grad[...] = grad
        if reduce:
            payload[...] = low(grad)

    if not reduce:
        loads[0].wait()
        for part in range(3):
            shrink_grad(part)
        for part in range(3):
            hidden_layer(part)
            expand_grad(part)
        middle_layer()
        for first in (0, 2, 4):
            attention(first)
        mixing()
        for part in range(3):
            attend_grad(part)
        input_layer()
        return

    def exchange(source):
        return remote(source, arrived, pay_send, pay_recv, partner["x"])

    small_route = ("c",) + ROUTES[0]
    totals = ((decoder_total, decoder_got), (encoder_total, encoder_got))

    def small_copy(stage, kind):
        source, target = totals[kind]
        return remote(
            source.at[stage],
            target.at[stage],
            small_send.at[stage, kind],
            small_recv.at[stage, kind],
            partner[small_route[stage]],
        )

    def small_advance(stage):
        if stage == 0:
            encoder_total[0] = vectors[...]
        for kind in range(2):
            source, target = totals[kind]
            if stage > 0:
                small_copy(stage - 1, kind).wait_recv()
                source[stage] = source[stage - 1] + target[stage - 1]
            if stage < 5:
                small_copy(stage, kind).start()

    await_greetings()
    for chunk in range(2):
        engine.first_copy(chunk, rest.at[chunk, 1 - mine["c"]]).start()

    @pl.when(pack == 0)
    def _():
        exchange(encoded_grad).start()

    loads[0].wait()
    shrink_grad(0)
    for copy in first_own:
        copy.wait()
    decoder_load.wait()

    def attention_end():
        attention(4)
        mixing()

    def input_end():
        input_layer()

        @pl.when(pack == 1)
        def _():
            exchange(payload).start()

    part = functools.partial
    works = [part(shrink_grad, 1), part(shrink_grad, 2)]
    for number in range(3):
        works += [part(hidden_layer, number), part(expand_grad, number)]
    works += [middle_layer, part(attention, 0), part(attention, 2), attention_end]
    works += [part(attend_grad, number) for number in range(3)] + [input_end]
    works = dict(enumerate(works))
    turns = CHUNKS + 4 * LAG
    works.update({turns - 11 + 2 * stage: part(small_advance, stage) for stage in range(6)})

    @pl.loop(0, turns)
    def _(number):
        engine.turn(number)
        for position, work in works.items():
            pl.when(number == position)(work)

    for stage in range(5):
        for kind in range(2):
            small_copy(stage, kind).wait_send()
    exchange(payload).wait()
    engine.close(CHUNKS - STAGING)
    vectors[...] = encoder_total[5]
    decoder_sums[...] = decoder_total[5]


def encoder_backward_call(reduce, tokens, encoded_grad, sums, decoder_vectors, rest, kept, gains, attend, merging, expand, shrink):
    if reduce:
        summed = jax.ShapeDtypeStruct((CHUNKS, 16, SPAN), F32)
        more = (
            jax.ShapeDtypeStruct(decoder_vectors.shape, F32),
            jax.ShapeDtypeStruct((256, 768), BF16),
        )
        more_specs = (vmem_spec(), any_spec())
        extra = [
            pltpu.VMEM((6,) + decoder_vectors.shape, F32),
            pltpu.VMEM((6,) + sums.shape, F32),
            pltpu.VMEM((5,) + decoder_vectors.shape, F32),
            pltpu.VMEM((5,) + sums.shape, F32),
            pltpu.VMEM((256, 768), BF16),
            pltpu.SemaphoreType.DMA((2,)),
            pltpu.SemaphoreType.DMA((5, 2)),
            pltpu.SemaphoreType.DMA((5, 2)),
            pltpu.SemaphoreType.DMA,
            pltpu.SemaphoreType.DMA,
            pltpu.SemaphoreType.DMA,
        ] + reducer_scratch(CHUNKS, STAGING)
        params = dict(collective_id=2, has_side_effects=True)
    else:
        summed = jax.ShapeDtypeStruct((CHUNKS, 2, 16, 16, SPAN), BF16)
        more, more_specs, extra, params = (), (), [], dict()
    return pl.pallas_call(
        functools.partial(encoder_backward_kernel, reduce),
        out_shape=(
            summed,
            jax.ShapeDtypeStruct(sums.shape, F32),
            jax.ShapeDtypeStruct((256, 768), F32),
        )
        + more,
        in_specs=[vmem_spec()] * 2 + [any_spec(), vmem_spec()] + [any_spec()] * 15,
        out_specs=(vmem_spec(),) * 3 + more_specs,
        scratch_shapes=[
            pltpu.VMEM((256, 768), F32),
            pltpu.VMEM(attend.shape, BF16),
            pltpu.VMEM(merging.shape, BF16),
            pltpu.VMEM((2, 768, 1024), BF16),
            pltpu.VMEM((2, 1024, 768), BF16),
            pltpu.VMEM((256, 768), BF16),
            pltpu.VMEM((256, 2304), BF16),
            pltpu.VMEM((768, 256), BF16),
            pltpu.VMEM((12, 256, 256), BF16),
            pltpu.VMEM((256, 768), BF16),
            pltpu.VMEM((256, 768), F32),
            pltpu.VMEM((256, 768), BF16),
            pltpu.VMEM((256, 3072), BF16),
            pltpu.VMEM((2, 256, 1024), F32),
            pltpu.VMEM((256, 1024), BF16),
            pltpu.VMEM((256, 768), F32),
            pltpu.VMEM((256, 768), BF16),
            pltpu.VMEM((256, 768), BF16),
            pltpu.VMEM((2, 256, 768), F32),
            pltpu.VMEM((768, 256), F32),
            pltpu.VMEM((256, 2304), BF16),
            pltpu.SemaphoreType.DMA((11,)),
            pltpu.SemaphoreType.DMA((2, 3)),
        ]
        + extra,
        compiler_params=pltpu.CompilerParams(vmem_limit_bytes=60 * 2**20, **params),
        name="encoder_backward",
    )(encoded_grad, sums, decoder_vectors, gains, tokens, rest, attend, merging, expand, shrink, *kept)


def unpack(packed, place):
    def take(start, size):
        pieces = []
        while size:
            chunk, first = divmod(start, SPAN)
            length = min(size, SPAN - first)
            pieces.append(packed[chunk, ..., first : first + length])
            start, size = start + length, size - length
        return pieces[0] if len(pieces) == 1 else jnp.concatenate(pieces, axis=-1)

    offset, count, width = place
    pieces = [take(offset + i * width, width) for i in range(count // 16)]
    if count % 16:
        rest = take(offset + count // 16 * width, width // 2)
        pieces.append(jnp.concatenate([rest[..., :8, :], rest[..., 8:, :]], axis=-1))
    return pieces[0] if len(pieces) == 1 else jnp.concatenate(pieces, axis=-2)


def finish_kernel(
    decoder_summed_far, decoder_sums_far, encoder_sums_far, summed_far, arrived_far, tokens_grad_far, encoded_grad_far,
    boundary, statistics, e_gains, e_shifts, e_biases, e_attend, e_merge, e_expand, e_inner, e_shrink,
    d_entry, d_biases, mask_grad, d_gains, d_shifts, d_attend, d_merge, d_expand, d_inner, d_shrink,
    decoder_summed, decoder_sums, encoder_sums, summed, arrived, tokens_grad, encoded_grad, load_sem,
):
    section = lax.axis_index("section")
    loads = fetch(
        [
            (decoder_summed_far, decoder_summed),
            (decoder_sums_far, decoder_sums),
            (encoder_sums_far, encoder_sums),
            (summed_far, summed),
            (arrived_far, arrived),
            (tokens_grad_far, tokens_grad),
            (encoded_grad_far, encoded_grad),
        ],
        load_sem,
    )
    number = section * lax.axis_size("dp") + lax.axis_index("dp")

    def own(rows, count):
        width = rows.shape[1]
        return pltpu.roll(rows, (width - number * count) % width, axis=1)[:, :count]

    def own_line(rows, count):
        return own(jnp.concatenate([rows[i : i + 1] for i in range(rows.shape[0])], axis=1), count)

    for copy in loads[:3]:
        copy.wait()
    lane = iota((1, 128), 1)
    values = jnp.zeros((1, 128), F32)
    for sums, width, first, count_row, base in ((encoder_sums, DE, 10, 14, 0), (decoder_sums, DD, 12, 16, 4)):
        scale = 1.0 / (sums[count_row : count_row + 1, 0:1] * width)
        for i in range(4):
            value = jnp.sum(sums[first + i : first + i + 1, :], axis=1, keepdims=True) * scale
            values = jnp.where(lane == base + i, value, values)
    statistics[...] = jnp.sqrt(values)[:, :8]
    rows = own(encoder_sums[0:8, :DE], 24)
    e_biases[...] = rows[0:2]
    e_gains[...] = rows[2:4]
    e_shifts[...] = rows[4:6]
    e_inner[...] = own_line(encoder_sums[6:9], 96)
    rows = own(decoder_sums[0:8], 16)
    d_biases[...] = rows[0:3]
    mask_grad[...] = rows[3:4]
    d_gains[...] = rows[4:6]
    d_shifts[...] = rows[6:8]
    d_inner[...] = own_line(decoder_sums[8:12], 64)

    d_merge[...] = unpack(decoder_summed, DECODER_MERGE)
    d_expand[...] = unpack(decoder_summed, DECODER_EXPAND)
    d_shrink[...] = unpack(decoder_summed, DECODER_SHRINK)
    loads[3].wait()
    d_entry[...] = unpack(summed, ENTRY)
    d_attend[...] = unpack(summed, DECODER_ATTEND)
    for target, places in ((e_expand, ENCODER_EXPAND), (e_attend, ENCODER_ATTEND), (e_shrink, ENCODER_SHRINK)):
        start = 0
        for place in places:
            target[:, start : start + place[2]] = unpack(summed, place)
            start += place[2]
    e_merge[...] = unpack(summed, ENCODER_MERGE)
    for copy in loads[4:]:
        copy.wait()

    @pl.when(section == 0)
    def _():
        boundary[0, 0] = tokens_grad[...]
        boundary[0, 1] = arrived[...].astype(F32)

    @pl.when(section == 1)
    def _():
        boundary[0, 0] = arrived[...].astype(F32)
        boundary[0, 1] = encoded_grad[...].astype(F32)


def finish_call(*operands):
    shapes = (
        (1, 2, 256, 768), (1, 8), (2, 24), (2, 24), (2, 24), (24, 2304), (24, 768), (24, 3072), (1, 96), (96, 768),
        (24, 512), (3, 16), (1, 16), (2, 16), (2, 16), (16, 768), (16, 256), (16, 2048), (1, 64), (64, 512),
    )
    outs = list(
        pl.pallas_call(
            finish_kernel,
            out_shape=tuple(jax.ShapeDtypeStruct(shape, F32) for shape in shapes),
            in_specs=[any_spec()] * len(operands),
            out_specs=(vmem_spec(),) * len(shapes),
            scratch_shapes=[pltpu.VMEM(operand.shape, operand.dtype) for operand in operands]
            + [pltpu.SemaphoreType.DMA((len(operands),))],
            compiler_params=pltpu.CompilerParams(vmem_limit_bytes=40 * 2**20),
            name="finish",
        )(*operands)
    )
    for line in (1, 8, 12, 18):
        outs[line] = outs[line].reshape(-1)
    for turned in (6, 16):
        outs[turned] = outs[turned].T
    return tuple(outs)


def scatter_sum(member, share_dim):
    return lax.psum_scatter(
        member, ("section", "dp"), scatter_dimension=share_dim, tiled=True
    )


def finish_generic(decoder_part, part, decoder_sums, encoder_sums, tokens_grad, encoded_grad):
    section = lax.axis_index("section")
    payload = jnp.where(section == 0, encoded_grad, low(tokens_grad))

    def whole(packed, *places):
        packed = jnp.swapaxes(packed, 1, 2).reshape(-1, 32, 16, SPAN)
        blocks = [unpack(packed, place).reshape(32 * place[1], place[2]) for place in places]
        return scatter_sum(jnp.concatenate(blocks, axis=1).astype(F32), 0)

    def line(value):
        return scatter_sum(value, value.ndim - 1)

    arrived = lax.ppermute(payload, "section", [(0, 1), (1, 0)]).astype(F32)
    boundary = jnp.where(
        section == 0,
        jnp.stack([tokens_grad, arrived]),
        jnp.stack([arrived, encoded_grad.astype(F32)]),
    )
    sums = jnp.concatenate(
        [jnp.sum(encoder_sums[10:14], axis=1), jnp.sum(decoder_sums[12:16], axis=1)]
    )
    sums, counts = lax.psum((sums, (encoder_sums[14, 0], decoder_sums[16, 0])), ("section", "dp"))
    scales = jnp.concatenate([jnp.full((4,), counts[0] * DE), jnp.full((4,), counts[1] * DD)])
    return (
        boundary[None],
        jnp.sqrt(sums / scales),
        line(encoder_sums[2:4, :DE]),
        line(encoder_sums[4:6, :DE]),
        line(encoder_sums[0:2, :DE]),
        whole(part, *ENCODER_ATTEND),
        whole(part, ENCODER_MERGE).T,
        whole(part, *ENCODER_EXPAND),
        line(encoder_sums[6:9].reshape(-1)),
        whole(part, *ENCODER_SHRINK),
        whole(decoder_part[1], ENTRY),
        line(decoder_sums[0:3]),
        line(decoder_sums[3]),
        line(decoder_sums[4:6]),
        line(decoder_sums[6:8]),
        whole(decoder_part[1], DECODER_ATTEND),
        whole(decoder_part[0], DECODER_MERGE).T,
        whole(decoder_part[0], DECODER_EXPAND),
        line(decoder_sums[8:12].reshape(-1)),
        whole(decoder_part[0], DECODER_SHRINK),
    )


def body(
    visible_tokens,
    cotangent,
    chip_sizes,
    ground_distance,
    visible_slots,
    encoder_gains,
    encoder_shifts,
    encoder_biases,
    encoder_attend,
    encoder_merge,
    encoder_expand,
    encoder_inner,
    encoder_shrink,
    decoder_entry,
    decoder_biases,
    mask_token,
    decoder_gains,
    decoder_shifts,
    decoder_attend,
    decoder_merge,
    decoder_widen_weight,
    decoder_inner,
    decoder_shrink,
):
    reduce = (lax.axis_size("section"), lax.axis_size("dp")) == (2, 16)
    sent, sums, *kept = encoder_forward_call(
        chip_sizes, visible_tokens, encoder_gains, encoder_shifts, encoder_biases,
        encoder_attend, encoder_merge, encoder_expand, encoder_inner, encoder_shrink,
    )
    decoder_summed, rest, decoder_vectors, encoded_grad = decoder_call(
        reduce, chip_sizes, ground_distance, visible_slots, sent, cotangent, decoder_entry, decoder_biases, mask_token,
        decoder_gains, decoder_shifts, decoder_attend, decoder_merge, decoder_widen_weight, decoder_inner,
        decoder_shrink,
    )
    summed, encoder_sums, tokens_grad, *more = encoder_backward_call(
        reduce, visible_tokens, encoded_grad, sums, decoder_vectors, rest, kept,
        encoder_gains, encoder_attend, encoder_merge, encoder_expand, encoder_shrink,
    )
    if reduce:
        decoder_sums, arrived = more
        return finish_call(
            decoder_summed, decoder_sums, encoder_sums, summed, arrived, tokens_grad, encoded_grad
        )
    return finish_generic(
        (decoder_summed, rest), summed, decoder_vectors, encoder_sums, tokens_grad, encoded_grad
    )


def solution(mesh):
    in_specs = (
        P("dp", None, None),
        P("dp", None, None),
        P("dp", None),
        P("dp", None),
        P("dp", None),
        P(),
        P(),
        P(),
        P(),
        P(),
        P(),
        P(),
        P(),
        P(),
        P(),
        P(),
        P(),
        P(),
        P(),
        P(),
        P(),
        P(),
        P(),
    )
    out_specs = (
        P("section", "dp", None, None),
        P(),
        P(None, ("section", "dp")),
        P(None, ("section", "dp")),
        P(None, ("section", "dp")),
        P(("section", "dp"), None),
        P(None, ("section", "dp")),
        P(("section", "dp"), None),
        P(("section", "dp")),
        P(("section", "dp"), None),
        P(("section", "dp"), None),
        P(None, ("section", "dp")),
        P(("section", "dp")),
        P(None, ("section", "dp")),
        P(None, ("section", "dp")),
        P(("section", "dp"), None),
        P(None, ("section", "dp")),
        P(("section", "dp"), None),
        P(("section", "dp")),
        P(("section", "dp"), None),
    )
    return jax.shard_map(body, mesh=mesh, in_specs=in_specs, out_specs=out_specs, check_vma=False)
```

```python
import functools
import types

import jax
import jax.numpy as jnp
import numpy as np
from jax import lax
from jax.experimental import pallas as pl
from jax.experimental.pallas import tpu as pltpu
from jax.sharding import PartitionSpec as P

DE = 768
DD = 512
TILE = 256
NEGATIVE = -1e30
F32, BF16 = jnp.float32, jnp.bfloat16
MESH_ID = pl.DeviceIdType.MESH

CANON = ("x", "z2", "z1", "y")
ROUTES = (("x", "y", "z1", "z2"), ("y", "x", "z1", "z2"), ("z1", "z2", "x", "y"))
WIDTHS = (2, 3, 1)
OFFSETS = (0, 2, 5)
SPAN = 128 * sum(WIDTHS)
UNIT = 2 * SPAN
DECODER_CHUNKS = 6
CHUNKS = 20
RING = 4
STAGING = 6
LAG = 2

DECODER_EXPAND, DECODER_SHRINK, DECODER_MERGE = (0, 16, 2048), (2048, 64, 512), (4096, 16, 256)
ENTRY, DECODER_ATTEND = (0, 24, 512), (768, 16, 768)
ENCODER_SHRINK = tuple((UNIT * (1 + part), 96, 256) for part in range(3))
ENCODER_EXPAND = tuple((UNIT * (4 + part), 24, 1024) for part in range(3))
ENCODER_ATTEND = ((UNIT * 7, 24, 1024), (UNIT * 8, 24, 1024), (UNIT * 9, 24, 256))
ENCODER_MERGE = (UNIT * 9 + 384, 24, 768)


def dot(a, b):
    return jnp.dot(a, b, preferred_element_type=F32)


def dot_nt(a, b):
    return lax.dot_general(a, b, (((1,), (1,)), ((), ())), preferred_element_type=F32)


def dot_tn(a, b):
    return lax.dot_general(a, b, (((0,), (0,)), ((), ())), preferred_element_type=F32)


def low(value):
    return value.astype(BF16)


def standardize(values):
    centered = values - jnp.mean(values, axis=-1, keepdims=True)
    inverse = lax.rsqrt(jnp.mean(centered * centered, axis=-1, keepdims=True) + 1e-05)
    return centered * inverse, inverse


def norm_back(unit, inverse, gain, grad):
    inner = grad * gain
    return inverse * (
        inner
        - jnp.mean(inner, axis=-1, keepdims=True)
        - unit * jnp.mean(inner * unit, axis=-1, keepdims=True)
    )


def row_sum(values):
    return jnp.sum(values, axis=0, keepdims=True)


def gelu_pair(before):
    half = 0.5 * (1.0 + lax.erf(before * 0.7071067811865476))
    density = jnp.exp(-0.5 * before * before) * 0.3989422804014327
    return before * half, half + before * density


def chip_of(places, sizes, pack):
    end = sizes[pack, 0]
    chip = (places >= end).astype(jnp.int32)
    for slot in range(1, 4):
        end = end + sizes[pack, slot]
        chip = chip + (places >= end).astype(jnp.int32)
    return chip


def iota(shape, dimension):
    return lax.broadcasted_iota(jnp.int32, shape, dimension)


def aligned(start, size, unit):
    return pl.ds(pl.multiple_of(start, unit), size)


def pair_lanes(pair, base=0):
    return aligned(base + pair * 128, 128, 128)


def head_rows(pair, half, base=0):
    return aligned(base + pair * 128 + half * 64, 64, 64)


def rows_of(tile):
    return aligned(tile * TILE, TILE, TILE)


def only(values, half):
    return jnp.where(iota((1, 128), 1) // 64 == half, values, jnp.zeros_like(values))


def fetch(pairs, sems):
    copies = [
        pltpu.make_async_copy(source, target, sems.at[i]) for i, (source, target) in enumerate(pairs)
    ]
    for copy in copies:
        copy.start()
    return copies


def store_packed(put, first, place, value):
    offset, count, width = place
    value = value.reshape(-1, count, width)
    shards = slice(first, first + value.shape[0]) if isinstance(first, int) else pl.ds(first, value.shape[0])
    for piece in range(count // 16):
        put(shards, offset + piece * width, value[:, piece * 16 : piece * 16 + 16])
    if count % 16:
        half = width // 2
        rest = value[:, count - 8 :]
        rest = jnp.concatenate([rest[:, :, :half], rest[:, :, half:]], axis=1)
        put(shards, offset + count // 16 * width, rest)


def halves(shards, value):
    pairs = value.reshape(value.shape[0] // 2, 2, *value.shape[1:])
    if isinstance(shards, slice):
        return slice(shards.start // 2, shards.stop // 2), pairs[:, 0], pairs[:, 1]
    return pl.ds(shards.start // 2, shards.size // 2), pairs[:, 0], pairs[:, 1]


def place_of(names, bits):
    index = 0
    for name in names:
        index = index * 2 + bits[name]
    return index


def left_after(route, stage):
    return tuple(name for name in CANON if name not in route[:stage])


def choices(names):
    for number in range(2 ** len(names)):
        yield {name: (number >> (len(names) - 1 - i)) & 1 for i, name in enumerate(names)}


def neighbours():
    section = lax.axis_index("section")
    data = lax.axis_index("dp")
    mine = {"x": section, "c": data % 2, "y": data // 2 % 2, "z1": data // 4 % 2, "z2": data // 8 % 2}
    partner = {"x": (1 - section, data)}
    for name, step in {"c": 1, "y": 2, "z1": 4, "z2": 8}.items():
        partner[name] = (section, data + step * (1 - 2 * mine[name]))
    return mine, partner


def greet(partner):
    barrier = pltpu.get_barrier_semaphore()
    for name in ("c",) + CANON:
        pl.semaphore_signal(barrier, inc=1, device_id=partner[name], device_id_type=MESH_ID)


def await_greetings():
    pl.semaphore_wait(pltpu.get_barrier_semaphore(), 5)


def remote(source, target, send, recv, device):
    return pltpu.make_async_remote_copy(
        src_ref=source,
        dst_ref=target,
        send_sem=send,
        recv_sem=recv,
        device_id=device,
        device_id_type=MESH_ID,
    )


def reducer(chunks, slots, mine, partner, out, refs):
    own, staging, first = refs[:3]
    sent, got = refs[3:15], refs[15:27]
    first_send, first_recv, send_sem, recv_sem = refs[27:31]

    def first_copy(chunk, source=None):
        if source is None:
            source = staging.at[chunk % slots]
        return remote(source, first.at[chunk], first_send.at[chunk], first_recv.at[chunk], partner["c"])

    def stage_copy(route, stage, chunk):
        return remote(
            sent[route * 4 + stage].at[chunk % RING],
            got[route * 4 + stage].at[chunk],
            send_sem.at[route, stage, chunk],
            recv_sem.at[route, stage, chunk],
            partner[ROUTES[route][stage]],
        )

    def total(route, stage, chunk, bits):
        spot = place_of(CANON, bits)
        cols = slice(OFFSETS[route] * 128, (OFFSETS[route] + WIDTHS[route]) * 128)
        value = own[chunk, spot, :, cols].astype(F32) + first[chunk, spot, :, cols].astype(F32)
        for earlier in range(stage):
            names = left_after(ROUTES[route], earlier + 1)
            value = value + got[route * 4 + earlier][chunk, place_of(names, bits)].astype(F32)
        return value

    def advance(stage, chunk):
        for route in range(3):
            if stage:
                stage_copy(route, stage - 1, chunk).wait_recv()
            else:
                first_copy(chunk).wait_recv() if route == 0 else None
            if stage < 4:

                @pl.when(chunk >= RING)
                def _(route=route):
                    stage_copy(route, stage, chunk - RING).wait_send()

        values = []
        for route in range(3):
            path = ROUTES[route]
            if stage == 4:
                values.append(total(route, 4, chunk, mine))
                continue
            names = left_after(path, stage + 1)
            for free in choices(names):
                bits = dict(mine)
                bits[path[stage]] = 1 - mine[path[stage]]
                bits.update(free)
                values.append((route, place_of(names, free), low(total(route, stage, chunk, bits))))
        if stage == 4:
            out[chunk] = jnp.concatenate(values, axis=1)
            return
        for route, spot, value in values:
            sent[route * 4 + stage][chunk % RING, spot] = value
        for route in range(3):
            stage_copy(route, stage, chunk).start()

    def turn(number):
        for stage in range(4, -1, -1):
            chunk = number - LAG * stage
            pl.when((chunk >= 0) & (chunk < chunks))(functools.partial(advance, stage, chunk))

    def put(shards, column, value):
        shards, even, odd = halves(shards, value)
        kept = low(jnp.where(mine["c"] == 0, even, odd))
        given = low(jnp.where(mine["c"] == 0, odd, even))
        width = value.shape[2]
        done = 0
        while done < width:
            chunk, start = divmod(column + done, SPAN)
            size = min(width - done, SPAN - start)
            own[chunk, shards, :, start : start + size] = kept[:, :, done : done + size]
            staging[chunk % slots, shards, :, start : start + size] = given[:, :, done : done + size]
            done += size

    def release(unit):
        for chunk in (2 * unit, 2 * unit + 1):
            if chunk >= slots:
                first_copy(chunk - slots).wait_send()

    def send(unit):
        for chunk in (2 * unit, 2 * unit + 1):
            first_copy(chunk).start()

    def close(released):
        for chunk in range(released, chunks):
            first_copy(chunk).wait_send()
        for chunk in range(chunks - RING, chunks):
            for route in range(3):
                for stage in range(4):
                    stage_copy(route, stage, chunk).wait_send()

    return types.SimpleNamespace(
        own=own, first_copy=first_copy, turn=turn, put=put, release=release, send=send, close=close
    )


def reducer_scratch(chunks, slots):
    stages = [(width, block) for width in WIDTHS for block in (8, 4, 2, 1)]
    return (
        [
            pltpu.VMEM((chunks, 16, 16, SPAN), BF16),
            pltpu.VMEM((slots, 16, 16, SPAN), BF16),
            pltpu.VMEM((chunks, 16, 16, SPAN), BF16),
        ]
        + [pltpu.VMEM((RING, block, 16, width * 128), BF16) for width, block in stages]
        + [pltpu.VMEM((chunks, block, 16, width * 128), BF16) for width, block in stages]
        + [
            pltpu.SemaphoreType.DMA((chunks,)),
            pltpu.SemaphoreType.DMA((chunks,)),
            pltpu.SemaphoreType.DMA((3, 4, chunks)),
            pltpu.SemaphoreType.DMA((3, 4, chunks)),
        ]
    )


def put_into(parts):
    def put(shards, column, value):
        shards, *pair = halves(shards, value)
        width = value.shape[2]
        done = 0
        while done < width:
            chunk, start = divmod(column + done, SPAN)
            size = min(width - done, SPAN - start)
            for core in range(2):
                parts[chunk, core, shards, :, start : start + size] = low(pair[core][:, :, done : done + size])
            done += size

    return put


def vmem_spec():
    return pl.BlockSpec(memory_space=pltpu.VMEM)


def any_spec():
    return pl.BlockSpec(memory_space=pl.ANY)


def smem_spec():
    return pl.BlockSpec(memory_space=pltpu.SMEM)


def encoder_forward_kernel(
    sizes, gains, shifts, biases, inner, tokens, attend_far, merging_far, expand_far, shrink_far,
    sent, vectors, *refs,
):
    far = refs[:9]
    normed, mixed, turned, probs, context, middle, normed_two, active, slope = refs[9:18]
    hidden, attend, merging, expand, shrink, context_turned, load_sem, save_sem = refs[18:]
    pack = lax.axis_index("section")
    loads = fetch(
        [
            (tokens.at[pack], hidden),
            *[(attend_far.at[:, i * 768 : i * 768 + 768], attend.at[:, i * 768 : i * 768 + 768]) for i in range(3)],
            (merging_far, merging),
            *[(expand_far.at[:, i * 1024 : i * 1024 + 1024], expand.at[:, i * 1024 : i * 1024 + 1024]) for i in range(3)],
            *[(shrink_far.at[i * 1024 : i * 1024 + 1024], shrink.at[i * 1024 : i * 1024 + 1024]) for i in range(3)],
        ],
        load_sem,
    )
    saves = []

    def save(*numbers):
        for number in numbers:
            copy = pltpu.make_async_copy(refs[9 + number], far[number], save_sem.at[number])
            copy.start()
            saves.append(copy)

    vectors[...] = jnp.zeros_like(vectors)
    key_chip = chip_of(4 * iota((TILE, 1), 0), sizes, pack)
    own_chip = chip_of(4 * iota((1, TILE), 1), sizes, pack)
    valid = (key_chip < 4).astype(F32)
    loads[0].wait()
    values = hidden[...]
    vectors[10:11, :768] = row_sum(valid * values * values)
    unit, _ = standardize(values)
    norm = low(unit * gains[0:1] + shifts[0:1])
    normed[...] = norm
    for part in range(3):
        cols = slice(part * 768, part * 768 + 768)
        loads[1 + part].wait()
        mix = dot(norm, attend[:, cols])
        mixed[:, cols] = low(mix)
        if part:
            turned[(part - 1) * 768 : part * 768] = low(mix.T)
    save(0, 1, 2)

    @pl.loop(0, 3)
    def _(step):
        for pair, half in ((2 * step, 0), (2 * step, 1), (2 * step + 1, 0), (2 * step + 1, 1)):
            keys = mixed[:, pair_lanes(pair, 768)]
            query = only(mixed[:, pair_lanes(pair)], half) * BF16(0.125)
            scores = jnp.where(key_chip == own_chip, dot_nt(keys, query), NEGATIVE)
            expos = jnp.exp(scores - jnp.max(scores, axis=0, keepdims=True))
            prob = low(expos * (1.0 / jnp.sum(expos, axis=0, keepdims=True)))
            probs[pair * 2 + half] = prob
            context_turned[head_rows(pair, half)] = dot(turned[head_rows(pair, half, 768)], prob)

    mingled = low(context_turned[...].T)
    context[...] = mingled
    save(3, 4)
    loads[4].wait()
    attention = dot(mingled, merging[...]) + biases[0:1]
    vectors[11:12, :768] = row_sum(valid * attention * attention)
    center = hidden[...] + attention
    middle[...] = center
    unit, _ = standardize(center)
    norm = low(unit * gains[1:2] + shifts[1:2])
    normed_two[...] = norm
    save(5, 6)
    feed = jnp.zeros_like(center)
    for part in range(3):
        cols = slice(part * 1024, part * 1024 + 1024)
        loads[5 + part].wait()
        value, slant = gelu_pair(dot(norm, expand[:, cols]) + inner[:, cols])
        value = low(value)
        active[:, cols] = value
        slope[part] = slant
        loads[8 + part].wait()
        feed = feed + dot(value, shrink[cols])
    save(7, 8)
    feed = feed + biases[1:2]
    vectors[12:13, :768] = row_sum(valid * feed * feed)
    output = center + feed
    vectors[13:14, :768] = row_sum(valid * output * output)
    vectors[14:15, :768] = jnp.broadcast_to(row_sum(valid), (1, 768))
    sent[...] = low(output)
    for copy in saves:
        copy.wait()


def encoder_forward_call(sizes, tokens, gains, shifts, biases, attend, merging, expand, inner, shrink):
    shapes = (
        ((256, 768), BF16),
        ((256, 2304), BF16),
        ((1536, 256), BF16),
        ((12, 256, 256), BF16),
        ((256, 768), BF16),
        ((256, 768), F32),
        ((256, 768), BF16),
        ((256, 3072), BF16),
        ((3, 256, 1024), F32),
    )
    return pl.pallas_call(
        encoder_forward_kernel,
        out_shape=(jax.ShapeDtypeStruct((256, 768), BF16), jax.ShapeDtypeStruct((16, 1024), F32))
        + tuple(jax.ShapeDtypeStruct(*shape) for shape in shapes),
        in_specs=[smem_spec()] + [vmem_spec()] * 4 + [any_spec()] * 5,
        out_specs=(vmem_spec(),) * 2 + (any_spec(),) * len(shapes),
        scratch_shapes=[pltpu.VMEM(*shape) for shape in shapes]
        + [
            pltpu.VMEM((256, 768), F32),
            pltpu.VMEM(attend.shape, BF16),
            pltpu.VMEM(merging.shape, BF16),
            pltpu.VMEM(expand.shape, BF16),
            pltpu.VMEM(shrink.shape, BF16),
            pltpu.VMEM((768, 256), F32),
            pltpu.SemaphoreType.DMA((11,)),
            pltpu.SemaphoreType.DMA((len(shapes),)),
        ],
        compiler_params=pltpu.CompilerParams(vmem_limit_bytes=60 * 2**20),
        name="encoder_forward",
    )(sizes, gains, shifts, biases, inner[None], tokens, attend, merging, expand, shrink)


def decoder_kernel(
    reduce, sizes, distance, slots, frequency, sent, biases, mask_token, gains, shifts, inner,
    cotangent, entry_far, attend_far, merging_far, expand_far, shrink_far,
    summed, rest, vectors, encoded_grad, *refs,
):
    (
        table, start, normed, mixed, turned, probs, flipped, context, normed_two, active,
        before_grad, go_low, attention_low, context_grad, delta, mixed_grad, target, masked_keys,
        entry_weight, attend, merging, expand, shrink, load_sem,
    ) = refs[:24]
    pack = lax.axis_index("section")
    if reduce:
        mine, partner = neighbours()
        greet(partner)
        engine = reducer(DECODER_CHUNKS, DECODER_CHUNKS, mine, partner, summed, refs[24:])
        put = engine.put
    else:
        put = put_into(summed)
    put_rest = put_into(rest)
    loads = fetch(
        [
            (entry_far, entry_weight),
            (attend_far, attend),
            (cotangent.at[pack], target),
            (merging_far, merging),
            (expand_far, expand),
            (shrink_far, shrink),
        ],
        load_sem,
    )
    tiles = start.shape[0] // TILE
    vectors[...] = jnp.zeros_like(vectors)
    large = sizes[pack, 0] == 1024

    def add_row(row, value):
        vectors[row : row + 1, :] += value

    positions = iota((32, 128), 0).astype(F32)
    for chip in range(4):
        spacing = distance[pack, chip].astype(F32) / 16.0
        angle = positions * (spacing * frequency[...])
        table[0, chip] = jnp.sin(angle)
        table[1, chip] = jnp.cos(angle)
    loads[0].wait()
    entry = low(dot(sent[...], entry_weight[...]) + biases[0:1])
    loads[1].wait()

    def slot_chip(tile):
        return chip_of(iota((TILE, 1), 0) + tile * TILE, sizes, pack)

    def validity(tile):
        return (slot_chip(tile) < 4).astype(F32)

    def spread_of(tile):
        return (slots[pl.ds(pack, 1)] == iota((TILE, TILE), 0) + tile * TILE).astype(F32)

    @pl.loop(0, tiles)
    def _(tile):
        rows = rows_of(tile)
        valid = validity(tile)
        spread = spread_of(tile)
        fill = valid * (1.0 - jnp.sum(spread, axis=1, keepdims=True))
        pieces = []
        for kind in range(2):
            wave = table[kind, 0, aligned(tile * 8, 8, 8)]
            big = jnp.broadcast_to(wave[:, None], (8, 32, 128)).reshape(TILE, 128)
            wave = table[kind, tile, 0:16]
            own = jnp.broadcast_to(wave[:, None], (16, 16, 128)).reshape(TILE, 128)
            pieces.append(jnp.where(large, big, own))
        for kind in range(2):
            wave = table[kind, 0]
            big = jnp.broadcast_to(wave[None], (8, 32, 128)).reshape(TILE, 128)
            wave = table[kind, tile, 0:16]
            own = jnp.broadcast_to(wave[None], (16, 16, 128)).reshape(TILE, 128)
            pieces.append(jnp.where(large, big, own))
        encoding = jnp.concatenate(pieces, axis=1) * valid
        hidden = dot(low(spread), entry) + fill * mask_token[...] + encoding
        start[rows] = hidden
        add_row(12, row_sum(valid * hidden * hidden))
        add_row(16, row_sum(valid))
        unit, _ = standardize(hidden)
        norm = low(unit * gains[0:1] + shifts[0:1])
        normed[rows] = norm
        mix = dot(norm, attend[...])
        mix_low = low(mix)
        mixed[rows] = mix_low
        turned[:, rows] = low(mix[:, 256:].T)
        lane = iota((TILE, 128), 1)
        other = (lane % 64 < 5) & (lane % 64 != slot_chip(tile))
        other = jnp.where(other, NEGATIVE, 0.0).astype(BF16)
        for head in range(4):
            lanes = slice(256 + head // 2 * 128, 384 + head // 2 * 128)
            masked_keys[head, rows] = jnp.where(lane // 64 == head % 2, mix_low[:, lanes], other)

    @pl.loop(0, 2 * tiles)
    def _(step):
        pair, tile = step // tiles, step % tiles
        rows = rows_of(tile)
        lane = iota((TILE, 128), 1)
        chosen = (lane % 64 == slot_chip(tile)).astype(F32).astype(BF16)
        for half in range(2):
            query = jnp.where(lane // 64 == half, mixed[rows, pair_lanes(pair)] * BF16(0.125), chosen)
            scores = dot_nt(masked_keys[pair * 2 + half], query)
            expos = jnp.exp(scores - jnp.max(scores, axis=0, keepdims=True))
            prob = low(expos * (1.0 / jnp.sum(expos, axis=0, keepdims=True)))
            probs[pair * 2 + half, :, rows] = prob
            flipped[head_rows(pair, half), rows] = dot(turned[head_rows(pair, half, 256)], prob)

    for copy in loads[2:]:
        copy.wait()

    @pl.loop(0, tiles)
    def _(tile):
        rows = rows_of(tile)
        valid = validity(tile)
        mingled_wide = flipped[:, rows].T
        mingled = low(mingled_wide)
        context[rows] = mingled
        attention = dot(mingled, merging[...]) + biases[1:2]
        add_row(13, row_sum(valid * attention * attention))
        center = start[rows] + attention
        unit, inverse = standardize(center)
        norm = low(unit * gains[1:2] + shifts[1:2])
        normed_two[rows] = norm
        go = target[rows] * valid
        go_below = low(go)
        go_low[rows] = go_below
        add_row(2, row_sum(go))
        feed = jnp.zeros_like(go)
        norm_grad = jnp.zeros_like(go)
        for part in range(4):
            cols = slice(part * 512, part * 512 + 512)
            before = dot(norm, expand[:, cols]) + inner[:, cols]
            value, slope = gelu_pair(before)
            value = low(value)
            active[rows, cols] = value
            feed = feed + dot(value, shrink[cols])
            grad = low(slope * dot_nt(go_below, shrink[cols]))
            before_grad[rows, cols] = grad
            add_row(8 + part, row_sum(grad.astype(F32)))
            norm_grad = norm_grad + dot_nt(grad, expand[:, cols])
        feed = feed + biases[2:3]
        add_row(14, row_sum(valid * feed * feed))
        output = center + feed
        add_row(15, row_sum(valid * output * output))
        add_row(5, row_sum(norm_grad * unit))
        add_row(7, row_sum(norm_grad))
        grad = go + norm_back(unit, inverse, gains[1:2], norm_grad)
        target[rows] = grad
        add_row(1, row_sum(grad))
        below = low(grad)
        attention_low[rows] = below
        outer = low(dot_nt(below, merging[...]))
        context_grad[rows] = outer
        product = (outer.astype(F32) * mingled_wide).T
        for head in range(4):
            delta[head, :, rows] = row_sum(product[head * 64 : head * 64 + 64])

    for part in range(2):
        cols = slice(part * 256, part * 256 + 256)
        store_packed(put, part * 16, DECODER_EXPAND, dot_tn(normed_two[:, cols], before_grad[...]))
        value = dot_tn(attention_low[:, cols], context[...])
        store_packed(put, part * 16, DECODER_MERGE, value)
    for block in range(2):
        put(slice(block * 16, block * 16 + 16), 4352, jnp.zeros((16, 16, 256), F32))
    if reduce:
        await_greetings()
        engine.send(0)

    @pl.loop(0, 8)
    def _(part):
        cols = aligned(part * 256, 256, 256)
        store_packed(put, part * 4, DECODER_SHRINK, dot_tn(active[:, cols], go_low[...]))

    if reduce:
        engine.send(1)
        engine.send(2)

    flipped[...] = jnp.zeros_like(flipped)

    @pl.loop(0, 2 * tiles)
    def _(step):
        pair, tile = step // tiles, step % tiles
        rows = rows_of(tile)
        lanes = pair_lanes(pair)
        values = mixed[rows, pair_lanes(pair, 512)]
        raws, probabilities, queries, outers = [], [], [], []
        for half in range(2):
            prob = probs[pair * 2 + half, rows]
            outer = only(context_grad[:, lanes], half)
            raw = low(prob.astype(F32) * (dot_nt(values, outer) - delta[pair * 2 + half]))
            flipped[head_rows(pair, half)] += dot(turned[head_rows(pair, half), rows], raw)
            raws.append(raw)
            probabilities.append(prob)
            outers.append(outer)
            queries.append(only(mixed[:, lanes], half))
        key_grad = dot(jnp.concatenate(raws, axis=1), jnp.concatenate(queries, axis=0))
        mixed_grad[rows, pair_lanes(pair, 256)] = low(key_grad * 0.125)
        value_grad = dot(jnp.concatenate(probabilities, axis=1), jnp.concatenate(outers, axis=0))
        mixed_grad[rows, pair_lanes(pair, 512)] = low(value_grad)
        if reduce:
            engine.turn(step)

    def last(tile, entry_grad):
        rows = rows_of(tile)
        mixed_grad[rows, 0:256] = low(flipped[:, rows].T * 0.125)
        norm_grad = dot_nt(mixed_grad[rows], attend[...])
        unit, inverse = standardize(start[rows])
        add_row(4, row_sum(norm_grad * unit))
        add_row(6, row_sum(norm_grad))
        grad = target[rows] + norm_back(unit, inverse, gains[0:1], norm_grad)
        spread = spread_of(tile)
        fill = validity(tile) * (1.0 - jnp.sum(spread, axis=1, keepdims=True))
        add_row(3, row_sum(fill * grad))
        if reduce:
            engine.turn(2 * tiles + tile)
        return entry_grad + dot_tn(low(spread), low(grad))

    entry_grad = lax.fori_loop(0, tiles, last, jnp.zeros((TILE, 512), F32))
    add_row(0, row_sum(entry_grad))
    entry_low = low(entry_grad)
    encoded_grad[...] = low(dot_nt(entry_low, entry_weight[...]))
    store_packed(put_rest, 0, ENTRY, dot_tn(sent[...], entry_low))
    for part in range(2):
        if reduce:
            engine.turn(3 * tiles + part)
        cols = slice(part * 256, part * 256 + 256)
        value = dot_tn(normed[:, cols], mixed_grad[...])
        store_packed(put_rest, part * 16, DECODER_ATTEND, value)
    if reduce:
        engine.close(0)


def decoder_call(
    reduce, sizes, distance, slots, sent, cotangent, entry_weight, biases, mask_token,
    gains, shifts, attend, merging, expand, inner, shrink,
):
    length = cotangent.shape[1]
    width = 512
    frequency = np.exp(-np.log(10000.0) * np.arange(width // 4) / (width // 4)).astype(np.float32)
    if reduce:
        summed = jax.ShapeDtypeStruct((DECODER_CHUNKS, 16, SPAN), F32)
        extra = reducer_scratch(DECODER_CHUNKS, DECODER_CHUNKS)
        params = dict(collective_id=1, has_side_effects=True)
    else:
        summed = jax.ShapeDtypeStruct((DECODER_CHUNKS, 2, 16, 16, SPAN), BF16)
        extra = []
        params = dict()
    return pl.pallas_call(
        functools.partial(decoder_kernel, reduce),
        out_shape=(
            summed,
            jax.ShapeDtypeStruct((2, 2, 16, 16, SPAN), BF16),
            jax.ShapeDtypeStruct((24, width), F32),
            jax.ShapeDtypeStruct((256, 768), BF16),
        ),
        in_specs=[smem_spec()] * 2 + [vmem_spec()] * 8 + [any_spec()] * 6,
        out_specs=(vmem_spec(),) * 4,
        scratch_shapes=[
            pltpu.VMEM((2, 4, 32, 128), F32),
            pltpu.VMEM((length, width), F32),
            pltpu.VMEM((length, width), BF16),
            pltpu.VMEM((length, 768), BF16),
            pltpu.VMEM((512, length), BF16),
            pltpu.VMEM((4, length, length), BF16),
            pltpu.VMEM((256, length), F32),
            pltpu.VMEM((length, 256), BF16),
            pltpu.VMEM((length, width), BF16),
            pltpu.VMEM((length, 2048), BF16),
            pltpu.VMEM((length, 2048), BF16),
            pltpu.VMEM((length, width), BF16),
            pltpu.VMEM((length, width), BF16),
            pltpu.VMEM((length, 256), BF16),
            pltpu.VMEM((4, 1, length), F32),
            pltpu.VMEM((length, 768), BF16),
            pltpu.VMEM((length, width), F32),
            pltpu.VMEM((4, length, 128), BF16),
            pltpu.VMEM(entry_weight.shape, BF16),
            pltpu.VMEM(attend.shape, BF16),
            pltpu.VMEM(merging.shape, BF16),
            pltpu.VMEM(expand.shape, BF16),
            pltpu.VMEM(shrink.shape, BF16),
            pltpu.SemaphoreType.DMA((6,)),
        ]
        + extra,
        compiler_params=pltpu.CompilerParams(vmem_limit_bytes=60 * 2**20, **params),
        name="decoder_block",
    )(
        sizes, distance, slots, jnp.asarray(frequency)[None], sent, biases, mask_token[None], gains, shifts,
        inner[None], cotangent, entry_weight, attend, merging, expand, shrink,
    )


def encoder_backward_kernel(
    reduce, encoded_grad, sums, decoder_vectors, gains, tokens, rest, attend_far, merging_far, expand_far,
    shrink_far, normed_far, mixed_far, turned_far, probs_far, context_far, middle_far, normed_two_far, active_far,
    slope_far, summed, vectors, tokens_grad, *refs,
):
    if reduce:
        decoder_sums, arrived = refs[:2]
        refs = refs[2:]
    (
        hidden, attend, merging, expand, shrink, normed, mixed, turned, probs, context, middle, normed_two, active,
        slope, before_grad, norm_sum, attention_low, context_grad, key_grad, query_turned, mixed_grad, active_turned,
        flipped, load_sem, part_sem,
    ) = refs[:25]
    pack = lax.axis_index("section")

    def part_loads(part):
        cols = slice(part * 1024, part * 1024 + 1024)
        slot = part % 2
        return [
            pltpu.make_async_copy(expand_far.at[:, cols], expand.at[slot], part_sem.at[slot, 0]),
            pltpu.make_async_copy(shrink_far.at[cols], shrink.at[slot], part_sem.at[slot, 1]),
            pltpu.make_async_copy(slope_far.at[part], slope.at[slot], part_sem.at[slot, 2]),
        ]

    if reduce:
        (
            decoder_total, encoder_total, decoder_got, encoder_got, payload,
            own_sem, small_send, small_recv, pay_send, pay_recv, small_load,
        ) = refs[25:36]
        mine, partner = neighbours()
        greet(partner)
        engine = reducer(CHUNKS, STAGING, mine, partner, summed, refs[36:])
        put = engine.put
        first_own = [
            pltpu.make_async_copy(rest.at[chunk, mine["c"]], engine.own.at[chunk], own_sem.at[chunk])
            for chunk in range(2)
        ]
        for copy in first_own:
            copy.start()
        decoder_load = pltpu.make_async_copy(decoder_vectors, decoder_total.at[0], small_load)
        decoder_load.start()
    else:
        put = put_into(summed)
    early = pltpu.make_async_copy(active_far, active, load_sem.at[10])
    early.start()
    for copy in part_loads(0):
        copy.start()
    if reduce:
        await_greetings()
        for chunk in range(2):
            engine.first_copy(chunk, rest.at[chunk, 1 - mine["c"]]).start()
    loads = fetch(
        [
            (normed_two_far, normed_two),
            (middle_far, middle),
            (merging_far, merging),
            (context_far, context),
            (mixed_far, mixed),
            (probs_far, probs),
            (turned_far.at[0:768], turned),
            (normed_far, normed),
            (attend_far, attend),
            (tokens.at[pack], hidden),
        ],
        load_sem,
    )
    for copy in part_loads(1):
        copy.start()
    vectors[...] = sums[...]
    go_low = encoded_grad[...]
    go = go_low.astype(F32)
    vectors[1:2, :768] = row_sum(go)
    norm_sum[...] = jnp.zeros_like(norm_sum)

    def send(unit):
        if reduce:
            engine.send(unit)

    def release(unit):
        if reduce:
            engine.release(unit)

    def shrink_start():
        early.wait()
        for piece in range(4):
            rows = slice(piece * 768, piece * 768 + 768)
            active_turned[rows] = active[:, rows].T

    def shrink_grad(part):
        release(1 + part)
        cols = slice(part * 256, part * 256 + 256)
        for piece in range(4):
            rows = slice(piece * 768, piece * 768 + 768)
            store_packed(put, piece * 8, ENCODER_SHRINK[part], dot(active_turned[rows], encoded_grad[:, cols]))
        send(1 + part)

    def hidden_layer(part):
        for copy in part_loads(part):
            copy.wait()
        slot = part % 2
        grad = low(slope[slot] * dot_nt(encoded_grad[...], shrink[slot]))
        before_grad[...] = grad
        vectors[6 + part : 7 + part] = row_sum(grad.astype(F32))
        norm_sum[...] += dot_nt(grad, expand[slot])
        if part == 0:
            for copy in part_loads(2):
                copy.start()

    def expand_grad(part):
        release(4 + part)
        if part == 0:
            loads[0].wait()
            flipped[...] = normed_two[...].T
        store_packed(put, 0, ENCODER_EXPAND[part], dot(flipped[...], before_grad[...]))
        send(4 + part)

    def middle_layer():
        loads[1].wait()
        loads[2].wait()
        unit, inverse = standardize(middle[...])
        norm_grad = norm_sum[...]
        vectors[3:4, :768] = row_sum(norm_grad * unit)
        vectors[5:6, :768] = row_sum(norm_grad)
        grad = encoded_grad[...].astype(F32) + norm_back(unit, inverse, gains[1:2], norm_grad)
        vectors[0:1, :768] = row_sum(grad)
        tokens_grad[...] = grad
        below = low(grad)
        attention_low[...] = below
        context_grad[...] = low(dot_nt(below, merging[...]))
        for copy in loads[3:7]:
            copy.wait()

    def attention(first):
        @pl.loop(first, first + 2)
        def _(pair):
            lanes = pair_lanes(pair)
            values = mixed[:, pair_lanes(pair, 1536)]
            keys_total = jnp.zeros((TILE, 128), F32)
            values_total = jnp.zeros((TILE, 128), F32)
            for half in range(2):
                prob = probs[pair * 2 + half]
                outer = only(context_grad[:, lanes], half)
                query = only(mixed[:, lanes], half)
                wide = prob.astype(F32)
                grad = dot_nt(values, outer)
                raw = low(wide * (grad - jnp.sum(wide * grad, axis=0, keepdims=True)))
                keys_total = keys_total + dot(raw, query)
                values_total = values_total + dot(prob, outer)
                rows = head_rows(pair, half)
                query_turned[rows] = dot(turned[rows], raw)
            key_grad[0, :, lanes] = keys_total
            key_grad[1, :, lanes] = values_total

    def mixing():
        mixed_grad[:, 0:768] = low(query_turned[...].T * 0.125)
        mixed_grad[:, 768:1536] = low(key_grad[0] * 0.125)
        mixed_grad[:, 1536:2304] = low(key_grad[1])

    def attend_grad(part):
        if part == 0:
            loads[7].wait()
            flipped[...] = normed[...].T
        release(7 + part)
        wide = slice(part * 1024, min(part * 1024 + 1024, 2304))
        store_packed(put, 0, ENCODER_ATTEND[part], dot(flipped[...], mixed_grad[:, wide]))
        if part == 2:
            store_packed(put, 0, ENCODER_MERGE, dot_tn(attention_low[...], context[...]))
        send(7 + part)

    def input_layer():
        loads[8].wait()
        loads[9].wait()
        norm_grad = dot_nt(mixed_grad[...], attend[...])
        unit, inverse = standardize(hidden[...])
        vectors[2:3, :768] = row_sum(norm_grad * unit)
        vectors[4:5, :768] = row_sum(norm_grad)
        grad = tokens_grad[...] + norm_back(unit, inverse, gains[0:1], norm_grad)
        tokens_grad[...] = grad
        if reduce:
            payload[...] = low(grad)

    if not reduce:
        shrink_start()
        for part in range(3):
            shrink_grad(part)
        for part in range(3):
            hidden_layer(part)
            expand_grad(part)
        middle_layer()
        for first in (0, 2, 4):
            attention(first)
        mixing()
        for part in range(3):
            attend_grad(part)
        input_layer()
        return

    def exchange(source, piece):
        rows = aligned(piece * 32, 32, 32)
        return remote(source.at[rows], arrived.at[rows], pay_send.at[piece], pay_recv.at[piece], partner["x"])

    small_route = ("c",) + ROUTES[0]
    totals = ((decoder_total, decoder_got), (encoder_total, encoder_got))

    def small_copy(stage, kind):
        source, target = totals[kind]
        return remote(
            source.at[stage],
            target.at[stage],
            small_send.at[stage, kind],
            small_recv.at[stage, kind],
            partner[small_route[stage]],
        )

    def small_advance(stage):
        if stage == 0:
            encoder_total[0] = vectors[...]
        for kind in range(2):
            source, target = totals[kind]
            if stage > 0:
                small_copy(stage - 1, kind).wait_recv()
                source[stage] = source[stage - 1] + target[stage - 1]
            if stage < 5:
                small_copy(stage, kind).start()

    shrink_start()
    shrink_grad(0)
    for copy in first_own:
        copy.wait()
    decoder_load.wait()

    def attention_end():
        attention(4)
        mixing()

    part = functools.partial
    works = [part(shrink_grad, 1), part(shrink_grad, 2)]
    for number in range(3):
        works += [part(hidden_layer, number), part(expand_grad, number)]
    works += [middle_layer, part(attention, 0), part(attention, 2), attention_end]
    works += [input_layer] + [part(attend_grad, number) for number in range(3)]
    works = dict(enumerate(works))
    turns = CHUNKS + 4 * LAG
    works.update({turns - 11 + 2 * stage: part(small_advance, stage) for stage in range(6)})

    @pl.loop(0, turns)
    def _(number):
        engine.turn(number)
        for position, work in works.items():
            pl.when(number == position)(work)

        piece = number // 2

        @pl.when((pack == 0) & (number % 2 == 0) & (piece < 8))
        def _():
            exchange(encoded_grad, piece).start()

        @pl.when((pack == 1) & (number % 2 == 0) & (piece >= 6))
        def _():
            exchange(payload, piece - 6).start()

    for stage in range(5):
        for kind in range(2):
            small_copy(stage, kind).wait_send()
    for piece in range(8):
        exchange(payload, piece).wait()
    engine.close(CHUNKS - STAGING)
    vectors[...] = encoder_total[5]
    decoder_sums[...] = decoder_total[5]


def encoder_backward_call(reduce, tokens, encoded_grad, sums, decoder_vectors, rest, kept, gains, attend, merging, expand, shrink):
    if reduce:
        summed = jax.ShapeDtypeStruct((CHUNKS, 16, SPAN), F32)
        more = (
            jax.ShapeDtypeStruct(decoder_vectors.shape, F32),
            jax.ShapeDtypeStruct((256, 768), BF16),
        )
        more_specs = (vmem_spec(), any_spec())
        extra = [
            pltpu.VMEM((6,) + decoder_vectors.shape, F32),
            pltpu.VMEM((6,) + sums.shape, F32),
            pltpu.VMEM((5,) + decoder_vectors.shape, F32),
            pltpu.VMEM((5,) + sums.shape, F32),
            pltpu.VMEM((256, 768), BF16),
            pltpu.SemaphoreType.DMA((2,)),
            pltpu.SemaphoreType.DMA((5, 2)),
            pltpu.SemaphoreType.DMA((5, 2)),
            pltpu.SemaphoreType.DMA((8,)),
            pltpu.SemaphoreType.DMA((8,)),
            pltpu.SemaphoreType.DMA,
        ] + reducer_scratch(CHUNKS, STAGING)
        params = dict(collective_id=2, has_side_effects=True)
    else:
        summed = jax.ShapeDtypeStruct((CHUNKS, 2, 16, 16, SPAN), BF16)
        more, more_specs, extra, params = (), (), [], dict()
    return pl.pallas_call(
        functools.partial(encoder_backward_kernel, reduce),
        out_shape=(
            summed,
            jax.ShapeDtypeStruct(sums.shape, F32),
            jax.ShapeDtypeStruct((256, 768), F32),
        )
        + more,
        in_specs=[vmem_spec()] * 2 + [any_spec(), vmem_spec()] + [any_spec()] * 15,
        out_specs=(vmem_spec(),) * 3 + more_specs,
        scratch_shapes=[
            pltpu.VMEM((256, 768), F32),
            pltpu.VMEM(attend.shape, BF16),
            pltpu.VMEM(merging.shape, BF16),
            pltpu.VMEM((2, 768, 1024), BF16),
            pltpu.VMEM((2, 1024, 768), BF16),
            pltpu.VMEM((256, 768), BF16),
            pltpu.VMEM((256, 2304), BF16),
            pltpu.VMEM((768, 256), BF16),
            pltpu.VMEM((12, 256, 256), BF16),
            pltpu.VMEM((256, 768), BF16),
            pltpu.VMEM((256, 768), F32),
            pltpu.VMEM((256, 768), BF16),
            pltpu.VMEM((256, 3072), BF16),
            pltpu.VMEM((2, 256, 1024), F32),
            pltpu.VMEM((256, 1024), BF16),
            pltpu.VMEM((256, 768), F32),
            pltpu.VMEM((256, 768), BF16),
            pltpu.VMEM((256, 768), BF16),
            pltpu.VMEM((2, 256, 768), F32),
            pltpu.VMEM((768, 256), F32),
            pltpu.VMEM((256, 2304), BF16),
            pltpu.VMEM((3072, 256), BF16),
            pltpu.VMEM((768, 256), BF16),
            pltpu.SemaphoreType.DMA((11,)),
            pltpu.SemaphoreType.DMA((2, 3)),
        ]
        + extra,
        compiler_params=pltpu.CompilerParams(vmem_limit_bytes=60 * 2**20, **params),
        name="encoder_backward",
    )(encoded_grad, sums, decoder_vectors, gains, tokens, rest, attend, merging, expand, shrink, *kept)


def unpack(packed, place):
    def take(start, size):
        pieces = []
        while size:
            chunk, first = divmod(start, SPAN)
            length = min(size, SPAN - first)
            pieces.append(packed[chunk, ..., first : first + length])
            start, size = start + length, size - length
        return pieces[0] if len(pieces) == 1 else jnp.concatenate(pieces, axis=-1)

    offset, count, width = place
    pieces = [take(offset + i * width, width) for i in range(count // 16)]
    if count % 16:
        rest = take(offset + count // 16 * width, width // 2)
        pieces.append(jnp.concatenate([rest[..., :8, :], rest[..., 8:, :]], axis=-1))
    return pieces[0] if len(pieces) == 1 else jnp.concatenate(pieces, axis=-2)


def finish_kernel(
    decoder_summed_far, decoder_sums_far, encoder_sums_far, summed_far, arrived_far, tokens_grad_far, encoded_grad_far,
    boundary, statistics, e_gains, e_shifts, e_biases, e_attend, e_merge, e_expand, e_inner, e_shrink,
    d_entry, d_biases, mask_grad, d_gains, d_shifts, d_attend, d_merge, d_expand, d_inner, d_shrink,
    decoder_summed, decoder_sums, encoder_sums, summed, arrived, tokens_grad, encoded_grad, load_sem,
):
    section = lax.axis_index("section")
    loads = fetch(
        [
            (decoder_summed_far, decoder_summed),
            (decoder_sums_far, decoder_sums),
            (encoder_sums_far, encoder_sums),
            (summed_far, summed),
            (arrived_far, arrived),
            (tokens_grad_far, tokens_grad),
            (encoded_grad_far, encoded_grad),
        ],
        load_sem,
    )
    number = section * lax.axis_size("dp") + lax.axis_index("dp")

    def own(rows, count):
        width = rows.shape[1]
        return pltpu.roll(rows, (width - number * count) % width, axis=1)[:, :count]

    def own_line(rows, count):
        return own(jnp.concatenate([rows[i : i + 1] for i in range(rows.shape[0])], axis=1), count)

    for copy in loads[:3]:
        copy.wait()
    lane = iota((1, 128), 1)
    values = jnp.zeros((1, 128), F32)
    for sums, width, first, count_row, base in ((encoder_sums, DE, 10, 14, 0), (decoder_sums, DD, 12, 16, 4)):
        scale = 1.0 / (sums[count_row : count_row + 1, 0:1] * width)
        for i in range(4):
            value = jnp.sum(sums[first + i : first + i + 1, :], axis=1, keepdims=True) * scale
            values = jnp.where(lane == base + i, value, values)
    statistics[...] = jnp.sqrt(values)[:, :8]
    rows = own(encoder_sums[0:8, :DE], 24)
    e_biases[...] = rows[0:2]
    e_gains[...] = rows[2:4]
    e_shifts[...] = rows[4:6]
    e_inner[...] = own_line(encoder_sums[6:9], 96)
    rows = own(decoder_sums[0:8], 16)
    d_biases[...] = rows[0:3]
    mask_grad[...] = rows[3:4]
    d_gains[...] = rows[4:6]
    d_shifts[...] = rows[6:8]
    d_inner[...] = own_line(decoder_sums[8:12], 64)

    d_merge[...] = unpack(decoder_summed, DECODER_MERGE)
    d_expand[...] = unpack(decoder_summed, DECODER_EXPAND)
    d_shrink[...] = unpack(decoder_summed, DECODER_SHRINK)
    loads[3].wait()
    d_entry[...] = unpack(summed, ENTRY)
    d_attend[...] = unpack(summed, DECODER_ATTEND)
    for target, places in ((e_expand, ENCODER_EXPAND), (e_attend, ENCODER_ATTEND), (e_shrink, ENCODER_SHRINK)):
        start = 0
        for place in places:
            target[:, start : start + place[2]] = unpack(summed, place)
            start += place[2]
    e_merge[...] = unpack(summed, ENCODER_MERGE)
    for copy in loads[4:]:
        copy.wait()

    @pl.when(section == 0)
    def _():
        boundary[0, 0] = tokens_grad[...]
        boundary[0, 1] = arrived[...].astype(F32)

    @pl.when(section == 1)
    def _():
        boundary[0, 0] = arrived[...].astype(F32)
        boundary[0, 1] = encoded_grad[...].astype(F32)


def finish_call(*operands):
    shapes = (
        (1, 2, 256, 768), (1, 8), (2, 24), (2, 24), (2, 24), (24, 2304), (24, 768), (24, 3072), (1, 96), (96, 768),
        (24, 512), (3, 16), (1, 16), (2, 16), (2, 16), (16, 768), (16, 256), (16, 2048), (1, 64), (64, 512),
    )
    outs = list(
        pl.pallas_call(
            finish_kernel,
            out_shape=tuple(jax.ShapeDtypeStruct(shape, F32) for shape in shapes),
            in_specs=[any_spec()] * len(operands),
            out_specs=(vmem_spec(),) * len(shapes),
            scratch_shapes=[pltpu.VMEM(operand.shape, operand.dtype) for operand in operands]
            + [pltpu.SemaphoreType.DMA((len(operands),))],
            compiler_params=pltpu.CompilerParams(vmem_limit_bytes=60 * 2**20),
            name="finish",
        )(*operands)
    )
    for line in (1, 8, 12, 18):
        outs[line] = outs[line].reshape(-1)
    for turned in (6, 16):
        outs[turned] = outs[turned].T
    return tuple(outs)


def scatter_sum(member, share_dim):
    return lax.psum_scatter(
        member, ("section", "dp"), scatter_dimension=share_dim, tiled=True
    )


def finish_generic(decoder_part, part, decoder_sums, encoder_sums, tokens_grad, encoded_grad):
    section = lax.axis_index("section")
    payload = jnp.where(section == 0, encoded_grad, low(tokens_grad))

    def whole(packed, *places):
        packed = jnp.swapaxes(packed, 1, 2).reshape(-1, 32, 16, SPAN)
        blocks = [unpack(packed, place).reshape(32 * place[1], place[2]) for place in places]
        return scatter_sum(jnp.concatenate(blocks, axis=1).astype(F32), 0)

    def line(value):
        return scatter_sum(value, value.ndim - 1)

    arrived = lax.ppermute(payload, "section", [(0, 1), (1, 0)]).astype(F32)
    boundary = jnp.where(
        section == 0,
        jnp.stack([tokens_grad, arrived]),
        jnp.stack([arrived, encoded_grad.astype(F32)]),
    )
    sums = jnp.concatenate(
        [jnp.sum(encoder_sums[10:14], axis=1), jnp.sum(decoder_sums[12:16], axis=1)]
    )
    sums, counts = lax.psum((sums, (encoder_sums[14, 0], decoder_sums[16, 0])), ("section", "dp"))
    scales = jnp.concatenate([jnp.full((4,), counts[0] * DE), jnp.full((4,), counts[1] * DD)])
    return (
        boundary[None],
        jnp.sqrt(sums / scales),
        line(encoder_sums[2:4, :DE]),
        line(encoder_sums[4:6, :DE]),
        line(encoder_sums[0:2, :DE]),
        whole(part, *ENCODER_ATTEND),
        whole(part, ENCODER_MERGE).T,
        whole(part, *ENCODER_EXPAND),
        line(encoder_sums[6:9].reshape(-1)),
        whole(part, *ENCODER_SHRINK),
        whole(decoder_part[1], ENTRY),
        line(decoder_sums[0:3]),
        line(decoder_sums[3]),
        line(decoder_sums[4:6]),
        line(decoder_sums[6:8]),
        whole(decoder_part[1], DECODER_ATTEND),
        whole(decoder_part[0], DECODER_MERGE).T,
        whole(decoder_part[0], DECODER_EXPAND),
        line(decoder_sums[8:12].reshape(-1)),
        whole(decoder_part[0], DECODER_SHRINK),
    )


def body(
    visible_tokens,
    cotangent,
    chip_sizes,
    ground_distance,
    visible_slots,
    encoder_gains,
    encoder_shifts,
    encoder_biases,
    encoder_attend,
    encoder_merge,
    encoder_expand,
    encoder_inner,
    encoder_shrink,
    decoder_entry,
    decoder_biases,
    mask_token,
    decoder_gains,
    decoder_shifts,
    decoder_attend,
    decoder_merge,
    decoder_widen_weight,
    decoder_inner,
    decoder_shrink,
):
    reduce = (lax.axis_size("section"), lax.axis_size("dp")) == (2, 16)
    sent, sums, *kept = encoder_forward_call(
        chip_sizes, visible_tokens, encoder_gains, encoder_shifts, encoder_biases,
        encoder_attend, encoder_merge, encoder_expand, encoder_inner, encoder_shrink,
    )
    decoder_summed, rest, decoder_vectors, encoded_grad = decoder_call(
        reduce, chip_sizes, ground_distance, visible_slots, sent, cotangent, decoder_entry, decoder_biases, mask_token,
        decoder_gains, decoder_shifts, decoder_attend, decoder_merge, decoder_widen_weight, decoder_inner,
        decoder_shrink,
    )
    summed, encoder_sums, tokens_grad, *more = encoder_backward_call(
        reduce, visible_tokens, encoded_grad, sums, decoder_vectors, rest, kept,
        encoder_gains, encoder_attend, encoder_merge, encoder_expand, encoder_shrink,
    )
    if reduce:
        decoder_sums, arrived = more
        return finish_call(
            decoder_summed, decoder_sums, encoder_sums, summed, arrived, tokens_grad, encoded_grad
        )
    return finish_generic(
        (decoder_summed, rest), summed, decoder_vectors, encoder_sums, tokens_grad, encoded_grad
    )


def solution(mesh):
    in_specs = (
        P("dp", None, None),
        P("dp", None, None),
        P("dp", None),
        P("dp", None),
        P("dp", None),
        P(),
        P(),
        P(),
        P(),
        P(),
        P(),
        P(),
        P(),
        P(),
        P(),
        P(),
        P(),
        P(),
        P(),
        P(),
        P(),
        P(),
        P(),
    )
    out_specs = (
        P("section", "dp", None, None),
        P(),
        P(None, ("section", "dp")),
        P(None, ("section", "dp")),
        P(None, ("section", "dp")),
        P(("section", "dp"), None),
        P(None, ("section", "dp")),
        P(("section", "dp"), None),
        P(("section", "dp")),
        P(("section", "dp"), None),
        P(("section", "dp"), None),
        P(None, ("section", "dp")),
        P(("section", "dp")),
        P(None, ("section", "dp")),
        P(None, ("section", "dp")),
        P(("section", "dp"), None),
        P(None, ("section", "dp")),
        P(("section", "dp"), None),
        P(("section", "dp")),
        P(("section", "dp"), None),
    )
    return jax.shard_map(body, mesh=mesh, in_specs=in_specs, out_specs=out_specs, check_vma=False)
```

```python
import functools
import types

import jax
import jax.numpy as jnp
import numpy as np
from jax import lax
from jax.experimental import pallas as pl
from jax.experimental.pallas import tpu as pltpu
from jax.sharding import PartitionSpec as P

DE = 768
DD = 512
TILE = 256
NEGATIVE = -1e30
F32, BF16 = jnp.float32, jnp.bfloat16
MESH_ID = pl.DeviceIdType.MESH

CANON = ("x", "z2", "z1", "y")
ROUTES = (("x", "y", "z1", "z2"), ("y", "x", "z1", "z2"), ("z1", "z2", "x", "y"))
WIDTHS = (2, 3, 1)
OFFSETS = (0, 2, 5)
SPAN = 128 * sum(WIDTHS)
UNIT = 2 * SPAN
DECODER_CHUNKS = 6
CHUNKS = 20
RING = 4
STAGING = 6
STARTS = (0, 3, 5, 7, 9)

DECODER_EXPAND, DECODER_SHRINK, DECODER_MERGE = (0, 16, 2048), (2048, 64, 512), (4096, 16, 256)
ENTRY, DECODER_ATTEND = (0, 24, 512), (768, 16, 768)
ENCODER_SHRINK = tuple((UNIT * (1 + part), 96, 256) for part in range(3))
ENCODER_EXPAND = tuple((UNIT * (4 + part), 24, 1024) for part in range(3))
ENCODER_ATTEND = ((UNIT * 7, 24, 1024), (UNIT * 8, 24, 1024), (UNIT * 9, 24, 256))
ENCODER_MERGE = (UNIT * 9 + 384, 24, 768)


def dot(a, b):
    return jnp.dot(a, b, preferred_element_type=F32)


def dot_nt(a, b):
    return lax.dot_general(a, b, (((1,), (1,)), ((), ())), preferred_element_type=F32)


def dot_tn(a, b):
    return lax.dot_general(a, b, (((0,), (0,)), ((), ())), preferred_element_type=F32)


def low(value):
    return value.astype(BF16)


def standardize(values):
    centered = values - jnp.mean(values, axis=-1, keepdims=True)
    inverse = lax.rsqrt(jnp.mean(centered * centered, axis=-1, keepdims=True) + 1e-05)
    return centered * inverse, inverse


def norm_back(unit, inverse, gain, grad):
    inner = grad * gain
    return inverse * (
        inner
        - jnp.mean(inner, axis=-1, keepdims=True)
        - unit * jnp.mean(inner * unit, axis=-1, keepdims=True)
    )


def row_sum(values):
    return jnp.sum(values, axis=0, keepdims=True)


TAIL = (
    0.119623262, 0.120845547, 0.0993470139, 0.130416843, -0.0571681498, 0.210119301, -0.159378869, 0.0361949972,
)


def gelu_pair(before):
    spot = pl.reciprocal(1.0 + 0.3 * jnp.abs(before))
    bell = jnp.exp(-0.5 * (before * before))
    series = TAIL[-1]
    for factor in TAIL[-2::-1]:
        series = series * spot + factor
    tail = bell * (series * spot)
    below = jnp.where(before < 0.0, tail, 1.0 - tail)
    return before * below, below + (before * bell) * 0.3989422804014327


def chip_of(places, sizes, pack):
    end = sizes[pack, 0]
    chip = (places >= end).astype(jnp.int32)
    for slot in range(1, 4):
        end = end + sizes[pack, slot]
        chip = chip + (places >= end).astype(jnp.int32)
    return chip


def iota(shape, dimension):
    return lax.broadcasted_iota(jnp.int32, shape, dimension)


def aligned(start, size, unit):
    if isinstance(start, int):
        return slice(start, start + size)
    return pl.ds(pl.multiple_of(start, unit), size)


def pair_lanes(pair, base=0):
    return aligned(base + pair * 128, 128, 128)


def head_rows(pair, half, base=0):
    return aligned(base + pair * 128 + half * 64, 64, 64)


def rows_of(tile):
    return aligned(tile * TILE, TILE, TILE)


def only(values, half):
    return jnp.where(iota((1, 128), 1) // 64 == half, values, jnp.zeros_like(values))


def fetch(pairs, sems):
    copies = [
        pltpu.make_async_copy(source, target, sems.at[i]) for i, (source, target) in enumerate(pairs)
    ]
    for copy in copies:
        copy.start()
    return copies


def store_packed(put, first, place, value):
    offset, count, width = place
    value = value.reshape(-1, count, width)
    shards = slice(first, first + value.shape[0]) if isinstance(first, int) else pl.ds(first, value.shape[0])
    for piece in range(count // 16):
        put(shards, offset + piece * width, value[:, piece * 16 : piece * 16 + 16])
    if count % 16:
        half = width // 2
        rest = value[:, count - 8 :]
        rest = jnp.concatenate([rest[:, :, :half], rest[:, :, half:]], axis=1)
        put(shards, offset + count // 16 * width, rest)


def halves(shards, value):
    pairs = value.reshape(value.shape[0] // 2, 2, *value.shape[1:])
    if isinstance(shards, slice):
        return slice(shards.start // 2, shards.stop // 2), pairs[:, 0], pairs[:, 1]
    return pl.ds(shards.start // 2, shards.size // 2), pairs[:, 0], pairs[:, 1]


def place_of(names, bits):
    index = 0
    for name in names:
        index = index * 2 + bits[name]
    return index


def left_after(route, stage):
    return tuple(name for name in CANON if name not in route[:stage])


def choices(names):
    for number in range(2 ** len(names)):
        yield {name: (number >> (len(names) - 1 - i)) & 1 for i, name in enumerate(names)}


def neighbours():
    section = lax.axis_index("section")
    data = lax.axis_index("dp")
    mine = {"x": section, "c": data % 2, "y": data // 2 % 2, "z1": data // 4 % 2, "z2": data // 8 % 2}
    partner = {"x": (1 - section, data)}
    for name, step in {"c": 1, "y": 2, "z1": 4, "z2": 8}.items():
        partner[name] = (section, data + step * (1 - 2 * mine[name]))
    return mine, partner


def greet(partner):
    barrier = pltpu.get_barrier_semaphore()
    for name in ("c",) + CANON:
        pl.semaphore_signal(barrier, inc=1, device_id=partner[name], device_id_type=MESH_ID)


def await_greetings():
    pl.semaphore_wait(pltpu.get_barrier_semaphore(), 5)


def remote(source, target, send, recv, device):
    return pltpu.make_async_remote_copy(
        src_ref=source,
        dst_ref=target,
        send_sem=send,
        recv_sem=recv,
        device_id=device,
        device_id_type=MESH_ID,
    )


def reducer(chunks, slots, mine, partner, out, refs):
    own, staging, first = refs[:3]
    sent, got = refs[3:15], refs[15:27]
    first_send, first_recv, send_sem, recv_sem = refs[27:31]

    def first_copy(chunk, source=None):
        if source is None:
            source = staging.at[chunk % slots]
        return remote(source, first.at[chunk], first_send.at[chunk], first_recv.at[chunk], partner["c"])

    def stage_copy(route, stage, chunk):
        return remote(
            sent[route * 4 + stage].at[chunk % RING],
            got[route * 4 + stage].at[chunk],
            send_sem.at[route, stage, chunk],
            recv_sem.at[route, stage, chunk],
            partner[ROUTES[route][stage]],
        )

    def total(route, stage, chunk, bits):
        spot = place_of(CANON, bits)
        cols = slice(OFFSETS[route] * 128, (OFFSETS[route] + WIDTHS[route]) * 128)
        value = own[chunk, spot, :, cols].astype(F32) + first[chunk, spot, :, cols].astype(F32)
        for earlier in range(stage):
            names = left_after(ROUTES[route], earlier + 1)
            value = value + got[route * 4 + earlier][chunk, place_of(names, bits)].astype(F32)
        return value

    def advance(stage, chunk):
        for route in range(3):
            if stage:
                stage_copy(route, stage - 1, chunk).wait_recv()
            else:
                first_copy(chunk).wait_recv() if route == 0 else None
            if stage < 4:

                @pl.when(chunk >= RING)
                def _(route=route):
                    stage_copy(route, stage, chunk - RING).wait_send()

        values = []
        for route in range(3):
            path = ROUTES[route]
            if stage == 4:
                values.append(total(route, 4, chunk, mine))
                continue
            names = left_after(path, stage + 1)
            for free in choices(names):
                bits = dict(mine)
                bits[path[stage]] = 1 - mine[path[stage]]
                bits.update(free)
                values.append((route, place_of(names, free), low(total(route, stage, chunk, bits))))
        if stage == 4:
            out[chunk] = jnp.concatenate(values, axis=1)
            return
        for route, spot, value in values:
            sent[route * 4 + stage][chunk % RING, spot] = value
        for route in range(3):
            stage_copy(route, stage, chunk).start()

    def turn(number):
        for stage in range(5):
            chunk = number - STARTS[stage]
            pl.when((chunk >= 0) & (chunk < chunks))(functools.partial(advance, stage, chunk))

    def put(shards, column, value):
        shards, even, odd = halves(shards, value)
        kept = low(jnp.where(mine["c"] == 0, even, odd))
        given = low(jnp.where(mine["c"] == 0, odd, even))
        width = value.shape[2]
        done = 0
        while done < width:
            chunk, start = divmod(column + done, SPAN)
            size = min(width - done, SPAN - start)
            own[chunk, shards, :, start : start + size] = kept[:, :, done : done + size]
            staging[chunk % slots, shards, :, start : start + size] = given[:, :, done : done + size]
            done += size

    def release(unit):
        for chunk in (2 * unit, 2 * unit + 1):
            if chunk >= slots:
                first_copy(chunk - slots).wait_send()

    def send(unit):
        for chunk in (2 * unit, 2 * unit + 1):
            first_copy(chunk).start()

    def close(released):
        for chunk in range(released, chunks):
            first_copy(chunk).wait_send()
        for chunk in range(chunks - RING, chunks):
            for route in range(3):
                for stage in range(4):
                    stage_copy(route, stage, chunk).wait_send()

    return types.SimpleNamespace(
        own=own, first_copy=first_copy, turn=turn, put=put, release=release, send=send, close=close
    )


def reducer_scratch(chunks, slots):
    stages = [(width, block) for width in WIDTHS for block in (8, 4, 2, 1)]
    return (
        [
            pltpu.VMEM((chunks, 16, 16, SPAN), BF16),
            pltpu.VMEM((slots, 16, 16, SPAN), BF16),
            pltpu.VMEM((chunks, 16, 16, SPAN), BF16),
        ]
        + [pltpu.VMEM((RING, block, 16, width * 128), BF16) for width, block in stages]
        + [pltpu.VMEM((chunks, block, 16, width * 128), BF16) for width, block in stages]
        + [
            pltpu.SemaphoreType.DMA((chunks,)),
            pltpu.SemaphoreType.DMA((chunks,)),
            pltpu.SemaphoreType.DMA((3, 4, chunks)),
            pltpu.SemaphoreType.DMA((3, 4, chunks)),
        ]
    )


def put_into(parts):
    def put(shards, column, value):
        shards, *pair = halves(shards, value)
        width = value.shape[2]
        done = 0
        while done < width:
            chunk, start = divmod(column + done, SPAN)
            size = min(width - done, SPAN - start)
            for core in range(2):
                parts[chunk, core, shards, :, start : start + size] = low(pair[core][:, :, done : done + size])
            done += size

    return put


def vmem_spec():
    return pl.BlockSpec(memory_space=pltpu.VMEM)


def any_spec():
    return pl.BlockSpec(memory_space=pl.ANY)


def smem_spec():
    return pl.BlockSpec(memory_space=pltpu.SMEM)


def encoder_forward_kernel(
    sizes, gains, shifts, biases, inner, tokens, attend_far, merging_far, expand_far, shrink_far,
    sent, vectors, *refs,
):
    far = refs[:9]
    normed, mixed, turned, probs, context, middle, normed_two, active, slope = refs[9:18]
    hidden, attend, merging, expand, shrink, context_turned, load_sem, save_sem = refs[18:]
    pack = lax.axis_index("section")
    loads = fetch(
        [
            (tokens.at[pack], hidden),
            *[(attend_far.at[:, i * 768 : i * 768 + 768], attend.at[:, i * 768 : i * 768 + 768]) for i in range(3)],
            (merging_far, merging),
            *[(expand_far.at[:, i * 1024 : i * 1024 + 1024], expand.at[:, i * 1024 : i * 1024 + 1024]) for i in range(3)],
            *[(shrink_far.at[i * 1024 : i * 1024 + 1024], shrink.at[i * 1024 : i * 1024 + 1024]) for i in range(3)],
        ],
        load_sem,
    )
    saves = []

    def save(*numbers):
        for number in numbers:
            copy = pltpu.make_async_copy(refs[9 + number], far[number], save_sem.at[number])
            copy.start()
            saves.append(copy)

    vectors[...] = jnp.zeros_like(vectors)
    key_chip = chip_of(4 * iota((TILE, 1), 0), sizes, pack)
    own_chip = chip_of(4 * iota((1, TILE), 1), sizes, pack)
    valid = (key_chip < 4).astype(F32)
    loads[0].wait()
    values = hidden[...]
    vectors[10:11, :768] = row_sum(valid * values * values)
    unit, _ = standardize(values)
    norm = low(unit * gains[0:1] + shifts[0:1])
    normed[...] = norm
    for part in range(3):
        cols = slice(part * 768, part * 768 + 768)
        loads[1 + part].wait()
        mix = dot(norm, attend[:, cols])
        mixed[:, cols] = low(mix)
        if part:
            turned[(part - 1) * 768 : part * 768] = low(mix.T)
    save(0, 1, 2)

    def score(head):
        pair, half = divmod(head, 2)
        query = only(mixed[:, pair_lanes(pair)], half) * BF16(0.125)
        return dot_nt(mixed[:, pair_lanes(pair, 768)], query)

    ready = [score(0), score(1)]
    for head in range(12):
        if head + 2 < 12:
            ready.append(score(head + 2))
        scores = jnp.where(key_chip == own_chip, ready[head], NEGATIVE)
        expos = jnp.exp(scores - jnp.max(scores, axis=0, keepdims=True))
        prob = low(expos * (1.0 / jnp.sum(expos, axis=0, keepdims=True)))
        probs[head] = prob
        context_turned[head * 64 : head * 64 + 64] = dot(turned[768 + head * 64 : 832 + head * 64], prob)

    mingled = low(context_turned[...].T)
    context[...] = mingled
    save(3, 4)
    loads[4].wait()
    attention = dot(mingled, merging[...]) + biases[0:1]
    vectors[11:12, :768] = row_sum(valid * attention * attention)
    center = hidden[...] + attention
    middle[...] = center
    unit, _ = standardize(center)
    norm = low(unit * gains[1:2] + shifts[1:2])
    normed_two[...] = norm
    save(5, 6)
    feed = jnp.zeros_like(center)
    def widened(part):
        if part % 2 == 0:
            loads[5 + part // 2].wait()
        cols = slice(part * 512, part * 512 + 512)
        return dot(norm, expand[:, cols]) + inner[:, cols]

    ready = [widened(0)]
    for part in range(6):
        if part < 5:
            ready.append(widened(part + 1))
        cols = slice(part * 512, part * 512 + 512)
        value, slant = gelu_pair(ready[part])
        value = low(value)
        active[:, cols] = value
        slope[part // 2, :, part % 2 * 512 : part % 2 * 512 + 512] = slant
        if part % 2 == 0:
            loads[8 + part // 2].wait()
        feed = feed + dot(value, shrink[cols])
    save(7, 8)
    feed = feed + biases[1:2]
    vectors[12:13, :768] = row_sum(valid * feed * feed)
    output = center + feed
    vectors[13:14, :768] = row_sum(valid * output * output)
    vectors[14:15, :768] = jnp.broadcast_to(row_sum(valid), (1, 768))
    sent[...] = low(output)
    for copy in saves:
        copy.wait()


def encoder_forward_call(sizes, tokens, gains, shifts, biases, attend, merging, expand, inner, shrink):
    shapes = (
        ((256, 768), BF16),
        ((256, 2304), BF16),
        ((1536, 256), BF16),
        ((12, 256, 256), BF16),
        ((256, 768), BF16),
        ((256, 768), F32),
        ((256, 768), BF16),
        ((256, 3072), BF16),
        ((3, 256, 1024), F32),
    )
    return pl.pallas_call(
        encoder_forward_kernel,
        out_shape=(jax.ShapeDtypeStruct((256, 768), BF16), jax.ShapeDtypeStruct((16, 1024), F32))
        + tuple(jax.ShapeDtypeStruct(*shape) for shape in shapes),
        in_specs=[smem_spec()] + [vmem_spec()] * 4 + [any_spec()] * 5,
        out_specs=(vmem_spec(),) * 2 + (any_spec(),) * len(shapes),
        scratch_shapes=[pltpu.VMEM(*shape) for shape in shapes]
        + [
            pltpu.VMEM((256, 768), F32),
            pltpu.VMEM(attend.shape, BF16),
            pltpu.VMEM(merging.shape, BF16),
            pltpu.VMEM(expand.shape, BF16),
            pltpu.VMEM(shrink.shape, BF16),
            pltpu.VMEM((768, 256), F32),
            pltpu.SemaphoreType.DMA((11,)),
            pltpu.SemaphoreType.DMA((len(shapes),)),
        ],
        compiler_params=pltpu.CompilerParams(vmem_limit_bytes=60 * 2**20),
        name="encoder_forward",
    )(sizes, gains, shifts, biases, inner[None], tokens, attend, merging, expand, shrink)


def decoder_kernel(
    reduce, sizes, distance, slots, frequency, sent, biases, mask_token, gains, shifts, inner,
    cotangent, entry_far, attend_far, merging_far, expand_far, shrink_far,
    summed, rest, vectors, encoded_grad, *refs,
):
    (
        table, start, normed, mixed, turned, probs, flipped, context, normed_two, active,
        before_grad, go_low, attention_low, context_grad, delta, mixed_grad, target, masked_keys,
        entry_weight, attend, merging, expand, shrink, load_sem,
    ) = refs[:24]
    pack = lax.axis_index("section")
    if reduce:
        mine, partner = neighbours()
        greet(partner)
        engine = reducer(DECODER_CHUNKS, DECODER_CHUNKS, mine, partner, summed, refs[24:])
        put = engine.put
    else:
        put = put_into(summed)
    put_rest = put_into(rest)
    loads = fetch(
        [
            (entry_far, entry_weight),
            (attend_far, attend),
            (cotangent.at[pack], target),
            (merging_far, merging),
            (expand_far, expand),
            (shrink_far, shrink),
        ],
        load_sem,
    )
    tiles = start.shape[0] // TILE
    vectors[...] = jnp.zeros_like(vectors)
    large = sizes[pack, 0] == 1024

    def add_row(row, value):
        vectors[row : row + 1, :] += value

    positions = iota((32, 128), 0).astype(F32)
    for chip in range(4):
        spacing = distance[pack, chip].astype(F32) / 16.0
        angle = positions * (spacing * frequency[...])
        table[0, chip] = jnp.sin(angle)
        table[1, chip] = jnp.cos(angle)
    loads[0].wait()
    entry = low(dot(sent[...], entry_weight[...]) + biases[0:1])
    loads[1].wait()

    def slot_chip(tile):
        return chip_of(iota((TILE, 1), 0) + tile * TILE, sizes, pack)

    def validity(tile):
        return (slot_chip(tile) < 4).astype(F32)

    def spread_of(tile):
        return (slots[pl.ds(pack, 1)] == iota((TILE, TILE), 0) + tile * TILE).astype(F32)

    @pl.loop(0, tiles)
    def _(tile):
        rows = rows_of(tile)
        valid = validity(tile)
        spread = spread_of(tile)
        fill = valid * (1.0 - jnp.sum(spread, axis=1, keepdims=True))
        pieces = []
        for kind in range(2):
            wave = table[kind, 0, aligned(tile * 8, 8, 8)]
            big = jnp.broadcast_to(wave[:, None], (8, 32, 128)).reshape(TILE, 128)
            wave = table[kind, tile, 0:16]
            own = jnp.broadcast_to(wave[:, None], (16, 16, 128)).reshape(TILE, 128)
            pieces.append(jnp.where(large, big, own))
        for kind in range(2):
            wave = table[kind, 0]
            big = jnp.broadcast_to(wave[None], (8, 32, 128)).reshape(TILE, 128)
            wave = table[kind, tile, 0:16]
            own = jnp.broadcast_to(wave[None], (16, 16, 128)).reshape(TILE, 128)
            pieces.append(jnp.where(large, big, own))
        encoding = jnp.concatenate(pieces, axis=1) * valid
        hidden = dot(low(spread), entry) + fill * mask_token[...] + encoding
        start[rows] = hidden
        add_row(12, row_sum(valid * hidden * hidden))
        add_row(16, row_sum(valid))
        unit, _ = standardize(hidden)
        norm = low(unit * gains[0:1] + shifts[0:1])
        normed[rows] = norm
        mix = dot(norm, attend[...])
        mix_low = low(mix)
        mixed[rows] = mix_low
        turned[:, rows] = low(mix[:, 256:].T)
        lane = iota((TILE, 128), 1)
        other = (lane % 64 < 5) & (lane % 64 != slot_chip(tile))
        other = jnp.where(other, NEGATIVE, 0.0).astype(BF16)
        for head in range(4):
            lanes = slice(256 + head // 2 * 128, 384 + head // 2 * 128)
            masked_keys[head, rows] = jnp.where(lane // 64 == head % 2, mix_low[:, lanes], other)

    @pl.loop(0, tiles)
    def _(tile):
        rows = rows_of(tile)
        lane = iota((TILE, 128), 1)
        chosen = (lane % 64 == slot_chip(tile)).astype(F32).astype(BF16)

        def score(head):
            query = mixed[rows, pair_lanes(head // 2)] * BF16(0.125)
            return dot_nt(masked_keys[head], jnp.where(lane // 64 == head % 2, query, chosen))

        ready = [score(0)]
        for head in range(4):
            if head + 1 < 4:
                ready.append(score(head + 1))
            scores = ready[head]
            expos = jnp.exp(scores - jnp.max(scores, axis=0, keepdims=True))
            prob = low(expos * (1.0 / jnp.sum(expos, axis=0, keepdims=True)))
            probs[head, :, rows] = prob
            flipped[head * 64 : head * 64 + 64, rows] = dot(turned[256 + head * 64 : 320 + head * 64], prob)

    for copy in loads[2:]:
        copy.wait()

    @pl.loop(0, tiles)
    def _(tile):
        rows = rows_of(tile)
        valid = validity(tile)
        mingled_wide = flipped[:, rows].T
        mingled = low(mingled_wide)
        context[rows] = mingled
        attention = dot(mingled, merging[...]) + biases[1:2]
        add_row(13, row_sum(valid * attention * attention))
        center = start[rows] + attention
        unit, inverse = standardize(center)
        norm = low(unit * gains[1:2] + shifts[1:2])
        normed_two[rows] = norm
        go = target[rows] * valid
        go_below = low(go)
        go_low[rows] = go_below
        add_row(2, row_sum(go))
        feed = jnp.zeros_like(go)
        norm_grad = jnp.zeros_like(go)

        def widened(part):
            cols = slice(part * 512, part * 512 + 512)
            return dot(norm, expand[:, cols]) + inner[:, cols], dot_nt(go_below, shrink[cols])

        ready = [widened(0)]
        for part in range(4):
            if part < 3:
                ready.append(widened(part + 1))
            cols = slice(part * 512, part * 512 + 512)
            before, back = ready[part]
            value, slope = gelu_pair(before)
            value = low(value)
            active[rows, cols] = value
            feed = feed + dot(value, shrink[cols])
            grad = low(slope * back)
            before_grad[rows, cols] = grad
            add_row(8 + part, row_sum(grad.astype(F32)))
            norm_grad = norm_grad + dot_nt(grad, expand[:, cols])
        feed = feed + biases[2:3]
        add_row(14, row_sum(valid * feed * feed))
        output = center + feed
        add_row(15, row_sum(valid * output * output))
        add_row(5, row_sum(norm_grad * unit))
        add_row(7, row_sum(norm_grad))
        grad = go + norm_back(unit, inverse, gains[1:2], norm_grad)
        target[rows] = grad
        add_row(1, row_sum(grad))
        below = low(grad)
        attention_low[rows] = below
        outer = low(dot_nt(below, merging[...]))
        context_grad[rows] = outer
        product = (outer.astype(F32) * mingled_wide).T
        for head in range(4):
            delta[head, :, rows] = row_sum(product[head * 64 : head * 64 + 64])

    for part in range(2):
        cols = slice(part * 256, part * 256 + 256)
        store_packed(put, part * 16, DECODER_EXPAND, dot_tn(normed_two[:, cols], before_grad[...]))
        value = dot_tn(attention_low[:, cols], context[...])
        store_packed(put, part * 16, DECODER_MERGE, value)
    for block in range(2):
        put(slice(block * 16, block * 16 + 16), 4352, jnp.zeros((16, 16, 256), F32))
    if reduce:
        await_greetings()
        engine.send(0)

    @pl.loop(0, 8)
    def _(part):
        cols = aligned(part * 256, 256, 256)
        store_packed(put, part * 4, DECODER_SHRINK, dot_tn(active[:, cols], go_low[...]))

    if reduce:
        engine.send(1)
        engine.send(2)
        engine.turn(0)
        engine.turn(1)

    flipped[...] = jnp.zeros_like(flipped)

    @pl.loop(0, tiles)
    def _(tile):
        rows = rows_of(tile)

        def inward(head):
            lanes = pair_lanes(head // 2)
            outer = only(context_grad[:, lanes], head % 2)
            return outer, dot_nt(mixed[rows, pair_lanes(head // 2, 512)], outer)

        ready = [inward(0)]
        for pair in range(2):
            lanes = pair_lanes(pair)
            raws, probabilities = [], []
            for head in (2 * pair, 2 * pair + 1):
                if head + 1 < 4:
                    ready.append(inward(head + 1))
                prob = probs[head, rows]
                raw = low(prob.astype(F32) * (ready[head][1] - delta[head]))
                own = slice(head * 64, head * 64 + 64)
                flipped[own] += dot(turned[own, rows], raw)
                raws.append(raw)
                probabilities.append(prob)
            queries = jnp.concatenate([only(mixed[:, lanes], half) for half in range(2)], axis=0)
            key_grad = dot(jnp.concatenate(raws, axis=1), queries)
            mixed_grad[rows, pair_lanes(pair, 256)] = low(key_grad * 0.125)
            outers = jnp.concatenate([ready[2 * pair][0], ready[2 * pair + 1][0]], axis=0)
            value_grad = dot(jnp.concatenate(probabilities, axis=1), outers)
            mixed_grad[rows, pair_lanes(pair, 512)] = low(value_grad)
            if reduce:
                engine.turn(2 + 2 * tile + pair)

    def last(tile, entry_grad):
        rows = rows_of(tile)
        mixed_grad[rows, 0:256] = low(flipped[:, rows].T * 0.125)
        norm_grad = dot_nt(mixed_grad[rows], attend[...])
        unit, inverse = standardize(start[rows])
        add_row(4, row_sum(norm_grad * unit))
        add_row(6, row_sum(norm_grad))
        grad = target[rows] + norm_back(unit, inverse, gains[0:1], norm_grad)
        spread = spread_of(tile)
        fill = validity(tile) * (1.0 - jnp.sum(spread, axis=1, keepdims=True))
        add_row(3, row_sum(fill * grad))
        if reduce:
            engine.turn(2 + 2 * tiles + tile)
        return entry_grad + dot_tn(low(spread), low(grad))

    entry_grad = lax.fori_loop(0, tiles, last, jnp.zeros((TILE, 512), F32))
    add_row(0, row_sum(entry_grad))
    entry_low = low(entry_grad)
    encoded_grad[...] = low(dot_nt(entry_low, entry_weight[...]))
    store_packed(put_rest, 0, ENTRY, dot_tn(sent[...], entry_low))
    for part in range(2):
        if reduce and part == 0:
            engine.turn(2 + 3 * tiles)
        cols = slice(part * 256, part * 256 + 256)
        value = dot_tn(normed[:, cols], mixed_grad[...])
        store_packed(put_rest, part * 16, DECODER_ATTEND, value)
    if reduce:
        engine.close(0)


def decoder_call(
    reduce, sizes, distance, slots, sent, cotangent, entry_weight, biases, mask_token,
    gains, shifts, attend, merging, expand, inner, shrink,
):
    length = cotangent.shape[1]
    width = 512
    frequency = np.exp(-np.log(10000.0) * np.arange(width // 4) / (width // 4)).astype(np.float32)
    if reduce:
        summed = jax.ShapeDtypeStruct((DECODER_CHUNKS, 16, SPAN), F32)
        extra = reducer_scratch(DECODER_CHUNKS, DECODER_CHUNKS)
        params = dict(collective_id=1, has_side_effects=True)
    else:
        summed = jax.ShapeDtypeStruct((DECODER_CHUNKS, 2, 16, 16, SPAN), BF16)
        extra = []
        params = dict()
    return pl.pallas_call(
        functools.partial(decoder_kernel, reduce),
        out_shape=(
            summed,
            jax.ShapeDtypeStruct((2, 2, 16, 16, SPAN), BF16),
            jax.ShapeDtypeStruct((24, width), F32),
            jax.ShapeDtypeStruct((256, 768), BF16),
        ),
        in_specs=[smem_spec()] * 2 + [vmem_spec()] * 8 + [any_spec()] * 6,
        out_specs=(vmem_spec(),) * 4,
        scratch_shapes=[
            pltpu.VMEM((2, 4, 32, 128), F32),
            pltpu.VMEM((length, width), F32),
            pltpu.VMEM((length, width), BF16),
            pltpu.VMEM((length, 768), BF16),
            pltpu.VMEM((512, length), BF16),
            pltpu.VMEM((4, length, length), BF16),
            pltpu.VMEM((256, length), F32),
            pltpu.VMEM((length, 256), BF16),
            pltpu.VMEM((length, width), BF16),
            pltpu.VMEM((length, 2048), BF16),
            pltpu.VMEM((length, 2048), BF16),
            pltpu.VMEM((length, width), BF16),
            pltpu.VMEM((length, width), BF16),
            pltpu.VMEM((length, 256), BF16),
            pltpu.VMEM((4, 1, length), F32),
            pltpu.VMEM((length, 768), BF16),
            pltpu.VMEM((length, width), F32),
            pltpu.VMEM((4, length, 128), BF16),
            pltpu.VMEM(entry_weight.shape, BF16),
            pltpu.VMEM(attend.shape, BF16),
            pltpu.VMEM(merging.shape, BF16),
            pltpu.VMEM(expand.shape, BF16),
            pltpu.VMEM(shrink.shape, BF16),
            pltpu.SemaphoreType.DMA((6,)),
        ]
        + extra,
        compiler_params=pltpu.CompilerParams(vmem_limit_bytes=60 * 2**20, **params),
        name="decoder_block",
    )(
        sizes, distance, slots, jnp.asarray(frequency)[None], sent, biases, mask_token[None], gains, shifts,
        inner[None], cotangent, entry_weight, attend, merging, expand, shrink,
    )


def encoder_backward_kernel(
    reduce, encoded_grad, sums, decoder_vectors, gains, tokens, rest, attend_far, merging_far, expand_far,
    shrink_far, normed_far, mixed_far, turned_far, probs_far, context_far, middle_far, normed_two_far, active_far,
    slope_far, summed, vectors, tokens_grad, *refs,
):
    if reduce:
        decoder_sums, arrived = refs[:2]
        refs = refs[2:]
    (
        hidden, attend, merging, expand, shrink, normed, mixed, turned, probs, context, middle, normed_two, active,
        slope, before_grad, norm_sum, attention_low, context_grad, key_grad, query_turned, mixed_grad, active_turned,
        flipped, load_sem, part_sem,
    ) = refs[:25]
    pack = lax.axis_index("section")

    def part_loads(part):
        cols = slice(part * 1024, part * 1024 + 1024)
        slot = part % 2
        return [
            pltpu.make_async_copy(expand_far.at[:, cols], expand.at[slot], part_sem.at[slot, 0]),
            pltpu.make_async_copy(shrink_far.at[cols], shrink.at[slot], part_sem.at[slot, 1]),
            pltpu.make_async_copy(slope_far.at[part], slope.at[slot], part_sem.at[slot, 2]),
        ]

    if reduce:
        (
            decoder_total, encoder_total, decoder_got, encoder_got, payload,
            own_sem, small_send, small_recv, pay_send, pay_recv, small_load,
        ) = refs[25:36]
        mine, partner = neighbours()
        greet(partner)
        engine = reducer(CHUNKS, STAGING, mine, partner, summed, refs[36:])
        put = engine.put
        first_own = [
            pltpu.make_async_copy(rest.at[chunk, mine["c"]], engine.own.at[chunk], own_sem.at[chunk])
            for chunk in range(2)
        ]
        for copy in first_own:
            copy.start()
        decoder_load = pltpu.make_async_copy(decoder_vectors, decoder_total.at[0], small_load)
        decoder_load.start()
    else:
        put = put_into(summed)
    early = pltpu.make_async_copy(active_far, active, load_sem.at[10])
    early.start()
    for copy in part_loads(0):
        copy.start()
    if reduce:
        await_greetings()
        for chunk in range(2):
            engine.first_copy(chunk, rest.at[chunk, 1 - mine["c"]]).start()
    loads = fetch(
        [
            (normed_two_far, normed_two),
            (middle_far, middle),
            (merging_far, merging),
            (context_far, context),
            (mixed_far, mixed),
            (probs_far, probs),
            (turned_far.at[0:768], turned),
            (normed_far, normed),
            (attend_far, attend),
            (tokens.at[pack], hidden),
        ],
        load_sem,
    )
    vectors[...] = sums[...]
    go_low = encoded_grad[...]
    go = go_low.astype(F32)
    vectors[1:2, :768] = row_sum(go)
    norm_sum[...] = jnp.zeros_like(norm_sum)

    def send(unit):
        if reduce:
            engine.send(unit)

    def release(unit):
        if reduce:
            engine.release(unit)

    def shrink_start():
        early.wait()
        for copy in part_loads(1):
            copy.start()
        for piece in range(4):
            rows = slice(piece * 768, piece * 768 + 768)
            active_turned[rows] = active[:, rows].T

    def shrink_grad(part):
        release(1 + part)
        cols = slice(part * 256, part * 256 + 256)
        for piece in range(4):
            rows = slice(piece * 768, piece * 768 + 768)
            store_packed(put, piece * 8, ENCODER_SHRINK[part], dot(active_turned[rows], encoded_grad[:, cols]))
        send(1 + part)

    def hidden_layer(part):
        for copy in part_loads(part):
            copy.wait()
        slot = part % 2
        grad = low(slope[slot] * dot_nt(encoded_grad[...], shrink[slot]))
        before_grad[...] = grad
        vectors[6 + part : 7 + part] = row_sum(grad.astype(F32))
        norm_sum[...] += dot_nt(grad, expand[slot])
        if part == 0:
            for copy in part_loads(2):
                copy.start()

    def expand_grad(part):
        release(4 + part)
        if part == 0:
            loads[0].wait()
            flipped[...] = normed_two[...].T
        store_packed(put, 0, ENCODER_EXPAND[part], dot(flipped[...], before_grad[...]))
        send(4 + part)

    def middle_layer():
        loads[1].wait()
        loads[2].wait()
        unit, inverse = standardize(middle[...])
        norm_grad = norm_sum[...]
        vectors[3:4, :768] = row_sum(norm_grad * unit)
        vectors[5:6, :768] = row_sum(norm_grad)
        grad = encoded_grad[...].astype(F32) + norm_back(unit, inverse, gains[1:2], norm_grad)
        vectors[0:1, :768] = row_sum(grad)
        tokens_grad[...] = grad
        below = low(grad)
        attention_low[...] = below
        context_grad[...] = low(dot_nt(below, merging[...]))
        for copy in loads[3:7]:
            copy.wait()

    def attention(first):
        @pl.loop(first, first + 2)
        def _(pair):
            lanes = pair_lanes(pair)
            values = mixed[:, pair_lanes(pair, 1536)]
            keys_total = jnp.zeros((TILE, 128), F32)
            values_total = jnp.zeros((TILE, 128), F32)
            for half in range(2):
                prob = probs[pair * 2 + half]
                outer = only(context_grad[:, lanes], half)
                query = only(mixed[:, lanes], half)
                wide = prob.astype(F32)
                grad = dot_nt(values, outer)
                raw = low(wide * (grad - jnp.sum(wide * grad, axis=0, keepdims=True)))
                keys_total = keys_total + dot(raw, query)
                values_total = values_total + dot(prob, outer)
                rows = head_rows(pair, half)
                query_turned[rows] = dot(turned[rows], raw)
            key_grad[0, :, lanes] = keys_total
            key_grad[1, :, lanes] = values_total

    def mixing():
        mixed_grad[:, 0:768] = low(query_turned[...].T * 0.125)
        mixed_grad[:, 768:1536] = low(key_grad[0] * 0.125)
        mixed_grad[:, 1536:2304] = low(key_grad[1])

    def attend_grad(part):
        if part == 0:
            loads[7].wait()
            flipped[...] = normed[...].T
        release(7 + part)
        wide = slice(part * 1024, min(part * 1024 + 1024, 2304))
        store_packed(put, 0, ENCODER_ATTEND[part], dot(flipped[...], mixed_grad[:, wide]))
        if part == 2:
            store_packed(put, 0, ENCODER_MERGE, dot_tn(attention_low[...], context[...]))
        send(7 + part)

    def input_layer():
        loads[8].wait()
        loads[9].wait()
        norm_grad = dot_nt(mixed_grad[...], attend[...])
        unit, inverse = standardize(hidden[...])
        vectors[2:3, :768] = row_sum(norm_grad * unit)
        vectors[4:5, :768] = row_sum(norm_grad)
        grad = tokens_grad[...] + norm_back(unit, inverse, gains[0:1], norm_grad)
        tokens_grad[...] = grad
        if reduce:
            payload[...] = low(grad)

    if not reduce:
        shrink_start()
        for part in range(3):
            shrink_grad(part)
        for part in range(3):
            hidden_layer(part)
            expand_grad(part)
        middle_layer()
        for first in (0, 2, 4):
            attention(first)
        mixing()
        for part in range(3):
            attend_grad(part)
        input_layer()
        return

    def exchange(source, piece):
        rows = aligned(piece * 32, 32, 32)
        return remote(source.at[rows], arrived.at[rows], pay_send.at[piece], pay_recv.at[piece], partner["x"])

    small_route = ("c",) + ROUTES[0]
    totals = ((decoder_total, decoder_got), (encoder_total, encoder_got))

    def small_copy(stage, kind):
        source, target = totals[kind]
        return remote(
            source.at[stage],
            target.at[stage],
            small_send.at[stage, kind],
            small_recv.at[stage, kind],
            partner[small_route[stage]],
        )

    def small_advance(stage):
        if stage == 0:
            encoder_total[0] = vectors[...]
        for kind in range(2):
            source, target = totals[kind]
            if stage > 0:
                small_copy(stage - 1, kind).wait_recv()
                source[stage] = source[stage - 1] + target[stage - 1]
            if stage < 5:
                small_copy(stage, kind).start()

    for copy in first_own:
        copy.wait()
    decoder_load.wait()

    def expand_end():
        expand_grad(2)
        middle_layer()

    def attention_end():
        attention(4)
        mixing()

    part = functools.partial
    works = [shrink_start] + [part(shrink_grad, number) for number in range(3)]
    for number in range(2):
        works += [part(hidden_layer, number), part(expand_grad, number)]
    works += [part(hidden_layer, 2), expand_end, part(attention, 0), part(attention, 2), attention_end]
    works += [part(attend_grad, number) for number in range(3)] + [input_layer]
    works = dict(enumerate(works))
    turns = CHUNKS + STARTS[4]
    works.update({turns - 11 + 2 * stage: part(small_advance, stage) for stage in range(6)})

    @pl.loop(0, turns)
    def _(number):
        engine.turn(number)
        for position, work in works.items():
            pl.when(number == position)(work)

        piece = number // 2

        @pl.when((pack == 0) & (number % 2 == 0) & (piece < 8))
        def _():
            exchange(encoded_grad, piece).start()

        @pl.when((pack == 1) & (number >= 18) & (number < 26))
        def _():
            exchange(payload, number - 18).start()

    for stage in range(5):
        for kind in range(2):
            small_copy(stage, kind).wait_send()
    for piece in range(8):
        exchange(payload, piece).wait()
    engine.close(CHUNKS - STAGING)
    vectors[...] = encoder_total[5]
    decoder_sums[...] = decoder_total[5]


def encoder_backward_call(reduce, tokens, encoded_grad, sums, decoder_vectors, rest, kept, gains, attend, merging, expand, shrink):
    if reduce:
        summed = jax.ShapeDtypeStruct((CHUNKS, 16, SPAN), F32)
        more = (
            jax.ShapeDtypeStruct(decoder_vectors.shape, F32),
            jax.ShapeDtypeStruct((256, 768), BF16),
        )
        more_specs = (vmem_spec(), any_spec())
        extra = [
            pltpu.VMEM((6,) + decoder_vectors.shape, F32),
            pltpu.VMEM((6,) + sums.shape, F32),
            pltpu.VMEM((5,) + decoder_vectors.shape, F32),
            pltpu.VMEM((5,) + sums.shape, F32),
            pltpu.VMEM((256, 768), BF16),
            pltpu.SemaphoreType.DMA((2,)),
            pltpu.SemaphoreType.DMA((5, 2)),
            pltpu.SemaphoreType.DMA((5, 2)),
            pltpu.SemaphoreType.DMA((8,)),
            pltpu.SemaphoreType.DMA((8,)),
            pltpu.SemaphoreType.DMA,
        ] + reducer_scratch(CHUNKS, STAGING)
        params = dict(collective_id=2, has_side_effects=True)
    else:
        summed = jax.ShapeDtypeStruct((CHUNKS, 2, 16, 16, SPAN), BF16)
        more, more_specs, extra, params = (), (), [], dict()
    return pl.pallas_call(
        functools.partial(encoder_backward_kernel, reduce),
        out_shape=(
            summed,
            jax.ShapeDtypeStruct(sums.shape, F32),
            jax.ShapeDtypeStruct((256, 768), F32),
        )
        + more,
        in_specs=[vmem_spec()] * 2 + [any_spec(), vmem_spec()] + [any_spec()] * 15,
        out_specs=(vmem_spec(),) * 3 + more_specs,
        scratch_shapes=[
            pltpu.VMEM((256, 768), F32),
            pltpu.VMEM(attend.shape, BF16),
            pltpu.VMEM(merging.shape, BF16),
            pltpu.VMEM((2, 768, 1024), BF16),
            pltpu.VMEM((2, 1024, 768), BF16),
            pltpu.VMEM((256, 768), BF16),
            pltpu.VMEM((256, 2304), BF16),
            pltpu.VMEM((768, 256), BF16),
            pltpu.VMEM((12, 256, 256), BF16),
            pltpu.VMEM((256, 768), BF16),
            pltpu.VMEM((256, 768), F32),
            pltpu.VMEM((256, 768), BF16),
            pltpu.VMEM((256, 3072), BF16),
            pltpu.VMEM((2, 256, 1024), F32),
            pltpu.VMEM((256, 1024), BF16),
            pltpu.VMEM((256, 768), F32),
            pltpu.VMEM((256, 768), BF16),
            pltpu.VMEM((256, 768), BF16),
            pltpu.VMEM((2, 256, 768), F32),
            pltpu.VMEM((768, 256), F32),
            pltpu.VMEM((256, 2304), BF16),
            pltpu.VMEM((3072, 256), BF16),
            pltpu.VMEM((768, 256), BF16),
            pltpu.SemaphoreType.DMA((11,)),
            pltpu.SemaphoreType.DMA((2, 3)),
        ]
        + extra,
        compiler_params=pltpu.CompilerParams(vmem_limit_bytes=60 * 2**20, **params),
        name="encoder_backward",
    )(encoded_grad, sums, decoder_vectors, gains, tokens, rest, attend, merging, expand, shrink, *kept)


def unpack(packed, place):
    def take(start, size):
        pieces = []
        while size:
            chunk, first = divmod(start, SPAN)
            length = min(size, SPAN - first)
            pieces.append(packed[chunk, ..., first : first + length])
            start, size = start + length, size - length
        return pieces[0] if len(pieces) == 1 else jnp.concatenate(pieces, axis=-1)

    offset, count, width = place
    pieces = [take(offset + i * width, width) for i in range(count // 16)]
    if count % 16:
        rest = take(offset + count // 16 * width, width // 2)
        pieces.append(jnp.concatenate([rest[..., :8, :], rest[..., 8:, :]], axis=-1))
    return pieces[0] if len(pieces) == 1 else jnp.concatenate(pieces, axis=-2)


def finish_kernel(
    decoder_summed_far, decoder_sums_far, encoder_sums_far, summed_far, arrived_far, tokens_grad_far, encoded_grad_far,
    boundary, statistics, e_gains, e_shifts, e_biases, e_attend, e_merge, e_expand, e_inner, e_shrink,
    d_entry, d_biases, mask_grad, d_gains, d_shifts, d_attend, d_merge, d_expand, d_inner, d_shrink,
    decoder_summed, decoder_sums, encoder_sums, summed, arrived, tokens_grad, encoded_grad, load_sem,
):
    section = lax.axis_index("section")
    loads = fetch(
        [
            (decoder_summed_far, decoder_summed),
            (decoder_sums_far, decoder_sums),
            (encoder_sums_far, encoder_sums),
            (summed_far, summed),
            (arrived_far, arrived),
            (tokens_grad_far, tokens_grad),
            (encoded_grad_far, encoded_grad),
        ],
        load_sem,
    )
    number = section * lax.axis_size("dp") + lax.axis_index("dp")

    def own(rows, count):
        width = rows.shape[1]
        return pltpu.roll(rows, (width - number * count) % width, axis=1)[:, :count]

    def own_line(rows, count):
        return own(jnp.concatenate([rows[i : i + 1] for i in range(rows.shape[0])], axis=1), count)

    for copy in loads[:3]:
        copy.wait()
    lane = iota((1, 128), 1)
    values = jnp.zeros((1, 128), F32)
    for sums, width, first, count_row, base in ((encoder_sums, DE, 10, 14, 0), (decoder_sums, DD, 12, 16, 4)):
        scale = 1.0 / (sums[count_row : count_row + 1, 0:1] * width)
        for i in range(4):
            value = jnp.sum(sums[first + i : first + i + 1, :], axis=1, keepdims=True) * scale
            values = jnp.where(lane == base + i, value, values)
    statistics[...] = jnp.sqrt(values)[:, :8]
    rows = own(encoder_sums[0:8, :DE], 24)
    e_biases[...] = rows[0:2]
    e_gains[...] = rows[2:4]
    e_shifts[...] = rows[4:6]
    e_inner[...] = own_line(encoder_sums[6:9], 96)
    rows = own(decoder_sums[0:8], 16)
    d_biases[...] = rows[0:3]
    mask_grad[...] = rows[3:4]
    d_gains[...] = rows[4:6]
    d_shifts[...] = rows[6:8]
    d_inner[...] = own_line(decoder_sums[8:12], 64)

    d_merge[...] = unpack(decoder_summed, DECODER_MERGE)
    d_expand[...] = unpack(decoder_summed, DECODER_EXPAND)
    d_shrink[...] = unpack(decoder_summed, DECODER_SHRINK)
    loads[3].wait()
    d_entry[...] = unpack(summed, ENTRY)
    d_attend[...] = unpack(summed, DECODER_ATTEND)
    for target, places in ((e_expand, ENCODER_EXPAND), (e_attend, ENCODER_ATTEND), (e_shrink, ENCODER_SHRINK)):
        start = 0
        for place in places:
            target[:, start : start + place[2]] = unpack(summed, place)
            start += place[2]
    e_merge[...] = unpack(summed, ENCODER_MERGE)
    for copy in loads[4:]:
        copy.wait()

    @pl.when(section == 0)
    def _():
        boundary[0, 0] = tokens_grad[...]
        boundary[0, 1] = arrived[...].astype(F32)

    @pl.when(section == 1)
    def _():
        boundary[0, 0] = arrived[...].astype(F32)
        boundary[0, 1] = encoded_grad[...].astype(F32)


def finish_call(*operands):
    shapes = (
        (1, 2, 256, 768), (1, 8), (2, 24), (2, 24), (2, 24), (24, 2304), (24, 768), (24, 3072), (1, 96), (96, 768),
        (24, 512), (3, 16), (1, 16), (2, 16), (2, 16), (16, 768), (16, 256), (16, 2048), (1, 64), (64, 512),
    )
    outs = list(
        pl.pallas_call(
            finish_kernel,
            out_shape=tuple(jax.ShapeDtypeStruct(shape, F32) for shape in shapes),
            in_specs=[any_spec()] * len(operands),
            out_specs=(vmem_spec(),) * len(shapes),
            scratch_shapes=[pltpu.VMEM(operand.shape, operand.dtype) for operand in operands]
            + [pltpu.SemaphoreType.DMA((len(operands),))],
            compiler_params=pltpu.CompilerParams(vmem_limit_bytes=60 * 2**20),
            name="finish",
        )(*operands)
    )
    for line in (1, 8, 12, 18):
        outs[line] = outs[line].reshape(-1)
    for turned in (6, 16):
        outs[turned] = outs[turned].T
    return tuple(outs)


def scatter_sum(member, share_dim):
    return lax.psum_scatter(
        member, ("section", "dp"), scatter_dimension=share_dim, tiled=True
    )


def finish_generic(decoder_part, part, decoder_sums, encoder_sums, tokens_grad, encoded_grad):
    section = lax.axis_index("section")
    payload = jnp.where(section == 0, encoded_grad, low(tokens_grad))

    def whole(packed, *places):
        packed = jnp.swapaxes(packed, 1, 2).reshape(-1, 32, 16, SPAN)
        blocks = [unpack(packed, place).reshape(32 * place[1], place[2]) for place in places]
        return scatter_sum(jnp.concatenate(blocks, axis=1).astype(F32), 0)

    def line(value):
        return scatter_sum(value, value.ndim - 1)

    arrived = lax.ppermute(payload, "section", [(0, 1), (1, 0)]).astype(F32)
    boundary = jnp.where(
        section == 0,
        jnp.stack([tokens_grad, arrived]),
        jnp.stack([arrived, encoded_grad.astype(F32)]),
    )
    sums = jnp.concatenate(
        [jnp.sum(encoder_sums[10:14], axis=1), jnp.sum(decoder_sums[12:16], axis=1)]
    )
    sums, counts = lax.psum((sums, (encoder_sums[14, 0], decoder_sums[16, 0])), ("section", "dp"))
    scales = jnp.concatenate([jnp.full((4,), counts[0] * DE), jnp.full((4,), counts[1] * DD)])
    return (
        boundary[None],
        jnp.sqrt(sums / scales),
        line(encoder_sums[2:4, :DE]),
        line(encoder_sums[4:6, :DE]),
        line(encoder_sums[0:2, :DE]),
        whole(part, *ENCODER_ATTEND),
        whole(part, ENCODER_MERGE).T,
        whole(part, *ENCODER_EXPAND),
        line(encoder_sums[6:9].reshape(-1)),
        whole(part, *ENCODER_SHRINK),
        whole(decoder_part[1], ENTRY),
        line(decoder_sums[0:3]),
        line(decoder_sums[3]),
        line(decoder_sums[4:6]),
        line(decoder_sums[6:8]),
        whole(decoder_part[1], DECODER_ATTEND),
        whole(decoder_part[0], DECODER_MERGE).T,
        whole(decoder_part[0], DECODER_EXPAND),
        line(decoder_sums[8:12].reshape(-1)),
        whole(decoder_part[0], DECODER_SHRINK),
    )


def body(
    visible_tokens,
    cotangent,
    chip_sizes,
    ground_distance,
    visible_slots,
    encoder_gains,
    encoder_shifts,
    encoder_biases,
    encoder_attend,
    encoder_merge,
    encoder_expand,
    encoder_inner,
    encoder_shrink,
    decoder_entry,
    decoder_biases,
    mask_token,
    decoder_gains,
    decoder_shifts,
    decoder_attend,
    decoder_merge,
    decoder_widen_weight,
    decoder_inner,
    decoder_shrink,
):
    reduce = (lax.axis_size("section"), lax.axis_size("dp")) == (2, 16)
    sent, sums, *kept = encoder_forward_call(
        chip_sizes, visible_tokens, encoder_gains, encoder_shifts, encoder_biases,
        encoder_attend, encoder_merge, encoder_expand, encoder_inner, encoder_shrink,
    )
    decoder_summed, rest, decoder_vectors, encoded_grad = decoder_call(
        reduce, chip_sizes, ground_distance, visible_slots, sent, cotangent, decoder_entry, decoder_biases, mask_token,
        decoder_gains, decoder_shifts, decoder_attend, decoder_merge, decoder_widen_weight, decoder_inner,
        decoder_shrink,
    )
    summed, encoder_sums, tokens_grad, *more = encoder_backward_call(
        reduce, visible_tokens, encoded_grad, sums, decoder_vectors, rest, kept,
        encoder_gains, encoder_attend, encoder_merge, encoder_expand, encoder_shrink,
    )
    if reduce:
        decoder_sums, arrived = more
        return finish_call(
            decoder_summed, decoder_sums, encoder_sums, summed, arrived, tokens_grad, encoded_grad
        )
    return finish_generic(
        (decoder_summed, rest), summed, decoder_vectors, encoder_sums, tokens_grad, encoded_grad
    )


def solution(mesh):
    in_specs = (
        P("dp", None, None),
        P("dp", None, None),
        P("dp", None),
        P("dp", None),
        P("dp", None),
        P(),
        P(),
        P(),
        P(),
        P(),
        P(),
        P(),
        P(),
        P(),
        P(),
        P(),
        P(),
        P(),
        P(),
        P(),
        P(),
        P(),
        P(),
    )
    out_specs = (
        P("section", "dp", None, None),
        P(),
        P(None, ("section", "dp")),
        P(None, ("section", "dp")),
        P(None, ("section", "dp")),
        P(("section", "dp"), None),
        P(None, ("section", "dp")),
        P(("section", "dp"), None),
        P(("section", "dp")),
        P(("section", "dp"), None),
        P(("section", "dp"), None),
        P(None, ("section", "dp")),
        P(("section", "dp")),
        P(None, ("section", "dp")),
        P(None, ("section", "dp")),
        P(("section", "dp"), None),
        P(None, ("section", "dp")),
        P(("section", "dp"), None),
        P(("section", "dp")),
        P(("section", "dp"), None),
    )
    return jax.shard_map(body, mesh=mesh, in_specs=in_specs, out_specs=out_specs, check_vma=False)
```

```python
import functools
import types

import jax
import jax.numpy as jnp
import numpy as np
from jax import lax
from jax.experimental import pallas as pl
from jax.experimental.pallas import tpu as pltpu
from jax.sharding import PartitionSpec as P

DE = 768
DD = 512
TILE = 256
NEGATIVE = -1e30
F32, BF16 = jnp.float32, jnp.bfloat16
MESH_ID = pl.DeviceIdType.MESH

CANON = ("x", "z2", "z1", "y")
ROUTES = (("x", "y", "z1", "z2"), ("y", "x", "z1", "z2"), ("z1", "z2", "x", "y"))
WIDTHS = (2, 3, 1)
OFFSETS = (0, 2, 5)
SPAN = 128 * sum(WIDTHS)
UNIT = 2 * SPAN
DECODER_CHUNKS = 6
CHUNKS = 20
RING = 4
STARTS = (0, 2, 4, 6, 8)

DECODER_EXPAND, DECODER_SHRINK, DECODER_MERGE = (0, 16, 2048), (2048, 64, 512), (4096, 16, 256)
ENCODER_SHRINK = tuple((UNIT * part, 96, 256) for part in range(3))
ENCODER_EXPAND = tuple((UNIT * (3 + part), 24, 1024) for part in range(3))
REST = 6
ENTRY, DECODER_ATTEND = (UNIT * REST, 24, 512), (UNIT * REST + 768, 16, 768)
ENCODER_ATTEND = ((UNIT * 7, 24, 1024), (UNIT * 8, 24, 1024), (UNIT * 9, 24, 256))
ENCODER_MERGE = (UNIT * 9 + 384, 24, 768)


def dot(a, b):
    return jnp.dot(a, b, preferred_element_type=F32)


def dot_nt(a, b):
    return lax.dot_general(a, b, (((1,), (1,)), ((), ())), preferred_element_type=F32)


def dot_tn(a, b):
    return lax.dot_general(a, b, (((0,), (0,)), ((), ())), preferred_element_type=F32)


def low(value):
    return value.astype(BF16)


def standardize(values):
    centered = values - jnp.mean(values, axis=-1, keepdims=True)
    inverse = lax.rsqrt(jnp.mean(centered * centered, axis=-1, keepdims=True) + 1e-05)
    return centered * inverse, inverse


def norm_back(unit, inverse, gain, grad):
    inner = grad * gain
    return inverse * (
        inner
        - jnp.mean(inner, axis=-1, keepdims=True)
        - unit * jnp.mean(inner * unit, axis=-1, keepdims=True)
    )


def row_sum(values):
    return jnp.sum(values, axis=0, keepdims=True)


TAIL = (
    0.119623262, 0.120845547, 0.0993470139, 0.130416843, -0.0571681498, 0.210119301, -0.159378869, 0.0361949972,
)


def gelu_pair(before):
    spot = pl.reciprocal(1.0 + 0.3 * jnp.abs(before))
    bell = jnp.exp(-0.5 * (before * before))
    series = TAIL[-1]
    for factor in TAIL[-2::-1]:
        series = series * spot + factor
    tail = bell * (series * spot)
    below = jnp.where(before < 0.0, tail, 1.0 - tail)
    return before * below, below + (before * bell) * 0.3989422804014327


def chip_of(places, sizes, pack):
    end = sizes[pack, 0]
    chip = (places >= end).astype(jnp.int32)
    for slot in range(1, 4):
        end = end + sizes[pack, slot]
        chip = chip + (places >= end).astype(jnp.int32)
    return chip


def iota(shape, dimension):
    return lax.broadcasted_iota(jnp.int32, shape, dimension)


def aligned(start, size, unit):
    if isinstance(start, int):
        return slice(start, start + size)
    return pl.ds(pl.multiple_of(start, unit), size)


def pair_lanes(pair, base=0):
    return aligned(base + pair * 128, 128, 128)


def head_rows(pair, half, base=0):
    return aligned(base + pair * 128 + half * 64, 64, 64)


def rows_of(tile):
    return aligned(tile * TILE, TILE, TILE)


def only(values, half):
    return jnp.where(iota((1, 128), 1) // 64 == half, values, jnp.zeros_like(values))


def fetch(pairs, sems):
    copies = [
        pltpu.make_async_copy(source, target, sems.at[i]) for i, (source, target) in enumerate(pairs)
    ]
    for copy in copies:
        copy.start()
    return copies


def store_packed(put, first, place, value):
    offset, count, width = place
    value = value.reshape(-1, count, width)
    shards = slice(first, first + value.shape[0]) if isinstance(first, int) else pl.ds(first, value.shape[0])
    for piece in range(count // 16):
        put(shards, offset + piece * width, value[:, piece * 16 : piece * 16 + 16])
    if count % 16:
        half = width // 2
        rest = value[:, count - 8 :]
        rest = jnp.concatenate([rest[:, :, :half], rest[:, :, half:]], axis=1)
        put(shards, offset + count // 16 * width, rest)


def halves(shards, value):
    pairs = value.reshape(value.shape[0] // 2, 2, *value.shape[1:])
    if isinstance(shards, slice):
        return slice(shards.start // 2, shards.stop // 2), pairs[:, 0], pairs[:, 1]
    return pl.ds(shards.start // 2, shards.size // 2), pairs[:, 0], pairs[:, 1]


def place_of(names, bits):
    index = 0
    for name in names:
        index = index * 2 + bits[name]
    return index


def left_after(route, stage):
    return tuple(name for name in CANON if name not in route[:stage])


def choices(names):
    for number in range(2 ** len(names)):
        yield {name: (number >> (len(names) - 1 - i)) & 1 for i, name in enumerate(names)}


def neighbours():
    section = lax.axis_index("section")
    data = lax.axis_index("dp")
    mine = {"x": section, "c": data % 2, "y": data // 2 % 2, "z1": data // 4 % 2, "z2": data // 8 % 2}
    partner = {"x": (1 - section, data)}
    for name, step in {"c": 1, "y": 2, "z1": 4, "z2": 8}.items():
        partner[name] = (section, data + step * (1 - 2 * mine[name]))
    return mine, partner


def greet(partner):
    barrier = pltpu.get_barrier_semaphore()
    for name in ("c",) + CANON:
        pl.semaphore_signal(barrier, inc=1, device_id=partner[name], device_id_type=MESH_ID)


def await_greetings():
    pl.semaphore_wait(pltpu.get_barrier_semaphore(), 5)


def remote(source, target, send, recv, device):
    return pltpu.make_async_remote_copy(
        src_ref=source,
        dst_ref=target,
        send_sem=send,
        recv_sem=recv,
        device_id=device,
        device_id_type=MESH_ID,
    )


def reducer(chunks, mine, partner, out, refs, paired):
    own, sent, got = refs[0], refs[1:13], refs[13:25]
    send_sem, recv_sem = refs[25:27]
    if not paired:
        staging, first, first_send, first_recv = refs[27:31]

    def first_copy(chunk):
        return remote(
            staging.at[chunk], first.at[chunk], first_send.at[chunk], first_recv.at[chunk], partner["c"]
        )

    def stage_copy(route, stage, chunk):
        return remote(
            sent[route * 4 + stage].at[chunk % RING],
            got[route * 4 + stage].at[chunk],
            send_sem.at[route, stage, chunk],
            recv_sem.at[route, stage, chunk],
            partner[ROUTES[route][stage]],
        )

    def total(route, stage, chunk, bits):
        spot = place_of(CANON, bits)
        cols = slice(OFFSETS[route] * 128, (OFFSETS[route] + WIDTHS[route]) * 128)
        value = own[chunk, spot, :, cols].astype(F32)
        if not paired:
            value = value + first[chunk, spot, :, cols].astype(F32)
        for earlier in range(stage):
            names = left_after(ROUTES[route], earlier + 1)
            value = value + got[route * 4 + earlier][chunk, place_of(names, bits)].astype(F32)
        return value

    def advance(stage, chunk):
        for route in range(3):
            if stage:
                stage_copy(route, stage - 1, chunk).wait_recv()
            elif route == 0 and not paired:
                first_copy(chunk).wait_recv()
            if stage < 4:

                @pl.when(chunk >= RING)
                def _(route=route):
                    stage_copy(route, stage, chunk - RING).wait_send()

        values = []
        for route in range(3):
            path = ROUTES[route]
            if stage == 4:
                values.append(total(route, 4, chunk, mine))
                continue
            names = left_after(path, stage + 1)
            for free in choices(names):
                bits = dict(mine)
                bits[path[stage]] = 1 - mine[path[stage]]
                bits.update(free)
                values.append((route, place_of(names, free), low(total(route, stage, chunk, bits))))
        if stage == 4:
            out[chunk] = jnp.concatenate(values, axis=1)
            return
        for route, spot, value in values:
            sent[route * 4 + stage][chunk % RING, spot] = value
        for route in range(3):
            stage_copy(route, stage, chunk).start()

    def turn(number):
        for stage in range(5):
            chunk = number - STARTS[stage]
            pl.when((chunk >= 0) & (chunk < chunks))(functools.partial(advance, stage, chunk))

    def put(shards, column, value):
        if paired:
            store_chunks(own, (shards,), column, value)
            return
        shards, even, odd = halves(shards, value)
        store_chunks(own, (shards,), column, jnp.where(mine["c"] == 0, even, odd))
        store_chunks(staging, (shards,), column, jnp.where(mine["c"] == 0, odd, even))

    def send(unit):
        for chunk in (2 * unit, 2 * unit + 1):
            first_copy(chunk).start()

    def close():
        for chunk in range(0 if not paired else chunks, chunks):
            first_copy(chunk).wait_send()
        for chunk in range(chunks - RING, chunks):
            for route in range(3):
                for stage in range(4):
                    stage_copy(route, stage, chunk).wait_send()

    return types.SimpleNamespace(own=own, turn=turn, put=put, send=send, close=close)


def reducer_scratch(chunks, paired):
    stages = [(width, block) for width in WIDTHS for block in (8, 4, 2, 1)]
    half = pltpu.VMEM((chunks, 16, 16, SPAN), BF16)
    scratch = (
        [half]
        + [pltpu.VMEM((RING, block, 16, width * 128), BF16) for width, block in stages]
        + [pltpu.VMEM((chunks, block, 16, width * 128), BF16) for width, block in stages]
        + [pltpu.SemaphoreType.DMA((3, 4, chunks))] * 2
    )
    if not paired:
        scratch += [half, half] + [pltpu.SemaphoreType.DMA((chunks,))] * 2
    return scratch


def store_chunks(target, where, column, value):
    width = value.shape[-1]
    done = 0
    while done < width:
        chunk, start = divmod(column + done, SPAN)
        size = min(width - done, SPAN - start)
        target[(chunk, *where, slice(None), slice(start, start + size))] = low(value[..., done : done + size])
        done += size


def put_into(parts, base=0):
    def put(shards, column, value):
        shards, *pair = halves(shards, value)
        for core in range(2):
            store_chunks(parts, (core, shards), column - base, pair[core])

    return put


def vmem_spec():
    return pl.BlockSpec(memory_space=pltpu.VMEM)


def any_spec():
    return pl.BlockSpec(memory_space=pl.ANY)


def smem_spec():
    return pl.BlockSpec(memory_space=pltpu.SMEM)


def flipped_halves(value, count, core):
    rows = value.T.reshape(value.shape[1] // (2 * count), 2, count, value.shape[0])
    own = jnp.where(core == 0, rows[:, 0], rows[:, 1]).reshape(value.shape[1] // 2, value.shape[0])
    other = jnp.where(core == 0, rows[:, 1], rows[:, 0]).reshape(value.shape[1] // 2, value.shape[0])
    return low(own), low(other)


def encoder_forward_kernel(
    reduce, sizes, gains, shifts, biases, inner, tokens, attend_far, merging_far, expand_far, shrink_far,
    sent, vectors, *refs,
):
    far = refs[:9]
    normed, mixed, turned_keys, probs, context, middle, normed_two, active, slope = refs[9:18]
    hidden, attend, merging, expand, shrink, context_turned, turned_values, load_sem, save_sem = refs[18:]
    pack = lax.axis_index("section")
    core = lax.axis_index("dp") % 2 if reduce else 0
    loads = fetch(
        [
            (tokens.at[pack], hidden),
            *[(attend_far.at[:, i * 768 : i * 768 + 768], attend.at[:, i * 768 : i * 768 + 768]) for i in range(3)],
            (merging_far, merging),
            *[(expand_far.at[:, i * 768 : i * 768 + 768], expand.at[:, i * 768 : i * 768 + 768]) for i in range(4)],
            *[(shrink_far.at[i * 768 : i * 768 + 768], shrink.at[i * 768 : i * 768 + 768]) for i in range(4)],
        ],
        load_sem,
    )
    saves = []

    def save(*numbers):
        for number in numbers:
            copy = pltpu.make_async_copy(refs[9 + number], far[number], save_sem.at[number])
            copy.start()
            saves.append(copy)

    vectors[...] = jnp.zeros_like(vectors)
    key_chip = chip_of(4 * iota((TILE, 1), 0), sizes, pack)
    own_chip = chip_of(4 * iota((1, TILE), 1), sizes, pack)
    valid = (key_chip < 4).astype(F32)
    loads[0].wait()
    values = hidden[...]
    vectors[10:11, :768] = row_sum(valid * values * values)
    unit, _ = standardize(values)
    norm_wide = unit * gains[0:1] + shifts[0:1]
    norm = low(norm_wide)
    for part in range(3):
        cols = slice(part * 768, part * 768 + 768)
        loads[1 + part].wait()
        mix = dot(norm, attend[:, cols])
        mixed[:, cols] = low(mix)
        if part:
            (turned_keys, turned_values)[part - 1][...] = low(mix.T)
    normed[0], normed[1] = flipped_halves(norm_wide, 24, core)
    save(0, 1, 2)

    for head in range(12):
        pair, half = divmod(head, 2)
        query = only(mixed[:, pair_lanes(pair)], half) * BF16(0.125)
        scores = dot_nt(mixed[:, pair_lanes(pair, 768)], query)
        scores = jnp.where(key_chip == own_chip, scores, NEGATIVE)
        expos = jnp.exp(scores - jnp.max(scores, axis=0, keepdims=True))
        prob = low(expos * (1.0 / jnp.sum(expos, axis=0, keepdims=True)))
        probs[head] = prob
        rows = slice(head * 64, head * 64 + 64)
        context_turned[rows] = dot(turned_values[rows], prob)

    mingled = low(context_turned[...].T)
    context[...] = mingled
    save(3, 4)
    loads[4].wait()
    attention = dot(mingled, merging[...]) + biases[0:1]
    vectors[11:12, :768] = row_sum(valid * attention * attention)
    center = hidden[...] + attention
    middle[...] = center
    unit, _ = standardize(center)
    norm_wide = unit * gains[1:2] + shifts[1:2]
    norm = low(norm_wide)
    normed_two[0], normed_two[1] = flipped_halves(norm_wide, 24, core)
    save(5, 6)
    feed = jnp.zeros_like(center)
    for part in range(4):
        cols = slice(part * 768, part * 768 + 768)
        loads[5 + part].wait()
        value, slant = gelu_pair(dot(norm, expand[:, cols]) + inner[:, cols])
        value = low(value)
        rows = slice(part * 384, part * 384 + 384)
        active[0, rows], active[1, rows] = flipped_halves(value, 96, core)
        slope[:, cols] = slant
        loads[9 + part].wait()
        feed = feed + dot(value, shrink[cols])
    save(7, 8)
    feed = feed + biases[1:2]
    vectors[12:13, :768] = row_sum(valid * feed * feed)
    output = center + feed
    vectors[13:14, :768] = row_sum(valid * output * output)
    vectors[14:15, :768] = jnp.broadcast_to(row_sum(valid), (1, 768))
    sent[...] = low(output)
    for copy in saves:
        copy.wait()


def encoder_forward_call(
    reduce, sizes, tokens, gains, shifts, biases, attend, merging, expand, inner, shrink
):
    shapes = (
        ((2, 384, 256), BF16),
        ((256, 2304), BF16),
        ((768, 256), BF16),
        ((12, 256, 256), BF16),
        ((256, 768), BF16),
        ((256, 768), F32),
        ((2, 384, 256), BF16),
        ((2, 1536, 256), BF16),
        ((256, 3072), F32),
    )
    return pl.pallas_call(
        functools.partial(encoder_forward_kernel, reduce),
        out_shape=(jax.ShapeDtypeStruct((256, 768), BF16), jax.ShapeDtypeStruct((16, 1024), F32))
        + tuple(jax.ShapeDtypeStruct(*shape) for shape in shapes),
        in_specs=[smem_spec()] + [vmem_spec()] * 4 + [any_spec()] * 5,
        out_specs=(vmem_spec(),) * 2 + (any_spec(),) * len(shapes),
        scratch_shapes=[pltpu.VMEM(*shape) for shape in shapes]
        + [
            pltpu.VMEM((256, 768), F32),
            pltpu.VMEM(attend.shape, BF16),
            pltpu.VMEM(merging.shape, BF16),
            pltpu.VMEM(expand.shape, BF16),
            pltpu.VMEM(shrink.shape, BF16),
            pltpu.VMEM((768, 256), F32),
            pltpu.VMEM((768, 256), BF16),
            pltpu.SemaphoreType.DMA((13,)),
            pltpu.SemaphoreType.DMA((len(shapes),)),
        ],
        compiler_params=pltpu.CompilerParams(vmem_limit_bytes=60 * 2**20),
        name="encoder_forward",
    )(sizes, gains, shifts, biases, inner[None], tokens, attend, merging, expand, shrink)


def decoder_kernel(
    reduce, sizes, distance, slots, frequency, sent, biases, mask_token, gains, shifts, inner,
    cotangent, entry_far, attend_far, merging_far, expand_far, shrink_far, *refs,
):
    if reduce:
        given, refs = refs[:4], refs[4:]
    summed, rest, vectors, encoded_grad, *refs = refs
    if reduce:
        taken, refs = refs[:4], refs[4:]
    (
        table, start, normed, mixed, turned, probs, flipped, context, normed_two, active,
        before_grad, go_low, attention_low, context_grad, delta, mixed_grad, target, masked_keys,
        entry_weight, attend, merging, expand, shrink, load_sem,
    ) = refs[:24]
    pack = lax.axis_index("section")
    if reduce:
        mine, partner = neighbours()
        greet(partner)
        pair_send, pair_recv = refs[24:26]
        engine = reducer(DECODER_CHUNKS, mine, partner, summed, refs[26:], False)
        put = engine.put
    else:
        put = put_into(summed)
    put_rest = put_into(rest, REST * UNIT)
    loads = fetch(
        [
            (entry_far, entry_weight),
            (attend_far, attend),
            (cotangent.at[pack], target),
            (merging_far, merging),
            (expand_far, expand),
            (shrink_far, shrink),
        ],
        load_sem,
    )
    pairs = []
    if reduce:
        await_greetings()
        for i in range(4):
            source = given[i] if i == 3 else given[i].at[1]
            pairs.append(remote(source, taken[i], pair_send.at[i], pair_recv.at[i], partner["c"]))
            pairs[i].start()
    tiles = start.shape[0] // TILE
    vectors[...] = jnp.zeros_like(vectors)
    large = sizes[pack, 0] == 1024

    def add_row(row, value):
        vectors[row : row + 1, :] += value

    positions = iota((32, 128), 0).astype(F32)
    for chip in range(4):
        spacing = distance[pack, chip].astype(F32) / 16.0
        angle = positions * (spacing * frequency[...])
        table[0, chip] = jnp.sin(angle)
        table[1, chip] = jnp.cos(angle)
    loads[0].wait()
    entry = low(dot(sent[...], entry_weight[...]) + biases[0:1])
    loads[1].wait()

    def slot_chip(tile):
        return chip_of(iota((TILE, 1), 0) + tile * TILE, sizes, pack)

    def validity(tile):
        return (slot_chip(tile) < 4).astype(F32)

    def spread_of(tile):
        return (slots[pl.ds(pack, 1)] == iota((TILE, TILE), 0) + tile * TILE).astype(F32)

    @pl.loop(0, tiles)
    def _(tile):
        rows = rows_of(tile)
        valid = validity(tile)
        spread = spread_of(tile)
        fill = valid * (1.0 - jnp.sum(spread, axis=1, keepdims=True))
        pieces = []
        for kind in range(2):
            wave = table[kind, 0, aligned(tile * 8, 8, 8)]
            big = jnp.broadcast_to(wave[:, None], (8, 32, 128)).reshape(TILE, 128)
            wave = table[kind, tile, 0:16]
            own = jnp.broadcast_to(wave[:, None], (16, 16, 128)).reshape(TILE, 128)
            pieces.append(jnp.where(large, big, own))
        for kind in range(2):
            wave = table[kind, 0]
            big = jnp.broadcast_to(wave[None], (8, 32, 128)).reshape(TILE, 128)
            wave = table[kind, tile, 0:16]
            own = jnp.broadcast_to(wave[None], (16, 16, 128)).reshape(TILE, 128)
            pieces.append(jnp.where(large, big, own))
        encoding = jnp.concatenate(pieces, axis=1) * valid
        hidden = dot(low(spread), entry) + fill * mask_token[...] + encoding
        start[rows] = hidden
        add_row(12, row_sum(valid * hidden * hidden))
        add_row(16, row_sum(valid))
        unit, _ = standardize(hidden)
        norm = low(unit * gains[0:1] + shifts[0:1])
        normed[rows] = norm
        mix = dot(norm, attend[...])
        mix_low = low(mix)
        mixed[rows] = mix_low
        turned[:, rows] = low(mix[:, 256:].T)
        lane = iota((TILE, 128), 1)
        other = (lane % 64 < 5) & (lane % 64 != slot_chip(tile))
        other = jnp.where(other, NEGATIVE, 0.0).astype(BF16)
        for head in range(4):
            lanes = slice(256 + head // 2 * 128, 384 + head // 2 * 128)
            masked_keys[head, rows] = jnp.where(lane // 64 == head % 2, mix_low[:, lanes], other)

    @pl.loop(0, 2 * tiles)
    def _(step):
        pair, tile = step // tiles, step % tiles
        rows = rows_of(tile)
        lane = iota((TILE, 128), 1)
        chosen = (lane % 64 == slot_chip(tile)).astype(F32).astype(BF16)
        for half in range(2):
            query = jnp.where(lane // 64 == half, mixed[rows, pair_lanes(pair)] * BF16(0.125), chosen)
            scores = dot_nt(masked_keys[pair * 2 + half], query)
            expos = jnp.exp(scores - jnp.max(scores, axis=0, keepdims=True))
            prob = low(expos * (1.0 / jnp.sum(expos, axis=0, keepdims=True)))
            probs[pair * 2 + half, :, rows] = prob
            flipped[head_rows(pair, half), rows] = dot(turned[head_rows(pair, half, 256)], prob)

    for copy in loads[2:]:
        copy.wait()

    @pl.loop(0, tiles)
    def _(tile):
        rows = rows_of(tile)
        valid = validity(tile)
        mingled_wide = flipped[:, rows].T
        mingled = low(mingled_wide)
        context[rows] = mingled
        attention = dot(mingled, merging[...]) + biases[1:2]
        add_row(13, row_sum(valid * attention * attention))
        center = start[rows] + attention
        unit, inverse = standardize(center)
        norm = low(unit * gains[1:2] + shifts[1:2])
        normed_two[rows] = norm
        go = target[rows] * valid
        go_below = low(go)
        go_low[rows] = go_below
        add_row(2, row_sum(go))
        feed = jnp.zeros_like(go)
        norm_grad = jnp.zeros_like(go)
        for part in range(4):
            cols = slice(part * 512, part * 512 + 512)
            before = dot(norm, expand[:, cols]) + inner[:, cols]
            value, slope = gelu_pair(before)
            value = low(value)
            active[rows, cols] = value
            feed = feed + dot(value, shrink[cols])
            grad = low(slope * dot_nt(go_below, shrink[cols]))
            before_grad[rows, cols] = grad
            add_row(8 + part, row_sum(grad.astype(F32)))
            norm_grad = norm_grad + dot_nt(grad, expand[:, cols])
        feed = feed + biases[2:3]
        add_row(14, row_sum(valid * feed * feed))
        output = center + feed
        add_row(15, row_sum(valid * output * output))
        add_row(5, row_sum(norm_grad * unit))
        add_row(7, row_sum(norm_grad))
        grad = go + norm_back(unit, inverse, gains[1:2], norm_grad)
        target[rows] = grad
        add_row(1, row_sum(grad))
        below = low(grad)
        attention_low[rows] = below
        outer = low(dot_nt(below, merging[...]))
        context_grad[rows] = outer
        product = (outer.astype(F32) * mingled_wide).T
        for head in range(4):
            delta[head, :, rows] = row_sum(product[head * 64 : head * 64 + 64])

    for part in range(2):
        cols = slice(part * 256, part * 256 + 256)
        store_packed(put, part * 16, DECODER_EXPAND, dot_tn(normed_two[:, cols], before_grad[...]))
        value = dot_tn(attention_low[:, cols], context[...])
        store_packed(put, part * 16, DECODER_MERGE, value)
    for block in range(2):
        put(slice(block * 16, block * 16 + 16), 4352, jnp.zeros((16, 16, 256), F32))
    if reduce:
        engine.send(0)

    @pl.loop(0, 8)
    def _(part):
        cols = aligned(part * 256, 256, 256)
        store_packed(put, part * 4, DECODER_SHRINK, dot_tn(active[:, cols], go_low[...]))

    if reduce:
        engine.send(1)
        engine.send(2)

    flipped[...] = jnp.zeros_like(flipped)

    @pl.loop(0, 2 * tiles)
    def _(step):
        pair, tile = step // tiles, step % tiles
        rows = rows_of(tile)
        lanes = pair_lanes(pair)
        values = mixed[rows, pair_lanes(pair, 512)]
        raws, probabilities, queries, outers = [], [], [], []
        for half in range(2):
            prob = probs[pair * 2 + half, rows]
            outer = only(context_grad[:, lanes], half)
            raw = low(prob.astype(F32) * (dot_nt(values, outer) - delta[pair * 2 + half]))
            flipped[head_rows(pair, half)] += dot(turned[head_rows(pair, half), rows], raw)
            raws.append(raw)
            probabilities.append(prob)
            outers.append(outer)
            queries.append(only(mixed[:, lanes], half))
        key_grad = dot(jnp.concatenate(raws, axis=1), jnp.concatenate(queries, axis=0))
        mixed_grad[rows, pair_lanes(pair, 256)] = low(key_grad * 0.125)
        value_grad = dot(jnp.concatenate(probabilities, axis=1), jnp.concatenate(outers, axis=0))
        mixed_grad[rows, pair_lanes(pair, 512)] = low(value_grad)
        if reduce:
            engine.turn(step)

    def last(tile, entry_grad):
        rows = rows_of(tile)
        mixed_grad[rows, 0:256] = low(flipped[:, rows].T * 0.125)
        norm_grad = dot_nt(mixed_grad[rows], attend[...])
        unit, inverse = standardize(start[rows])
        add_row(4, row_sum(norm_grad * unit))
        add_row(6, row_sum(norm_grad))
        grad = target[rows] + norm_back(unit, inverse, gains[0:1], norm_grad)
        spread = spread_of(tile)
        fill = validity(tile) * (1.0 - jnp.sum(spread, axis=1, keepdims=True))
        add_row(3, row_sum(fill * grad))
        if reduce:
            engine.turn(2 * tiles + tile)
        return entry_grad + dot_tn(low(spread), low(grad))

    entry_grad = lax.fori_loop(0, tiles, last, jnp.zeros((TILE, 512), F32))
    add_row(0, row_sum(entry_grad))
    entry_low = low(entry_grad)
    encoded_grad[...] = low(dot_nt(entry_low, entry_weight[...]))
    store_packed(put_rest, 0, ENTRY, dot_tn(sent[...], entry_low))
    for part in range(2):
        if reduce:
            engine.turn(3 * tiles + part)
        cols = slice(part * 256, part * 256 + 256)
        value = dot_tn(normed[:, cols], mixed_grad[...])
        store_packed(put_rest, part * 16, DECODER_ATTEND, value)
    if reduce:
        for copy in pairs:
            copy.wait()
        engine.close()


def decoder_call(
    reduce, sizes, distance, slots, sent, cotangent, entry_weight, biases, mask_token,
    gains, shifts, attend, merging, expand, inner, shrink, given,
):
    length = cotangent.shape[1]
    width = 512
    frequency = np.exp(-np.log(10000.0) * np.arange(width // 4) / (width // 4)).astype(np.float32)
    if reduce:
        summed = jax.ShapeDtypeStruct((DECODER_CHUNKS, 16, SPAN), F32)
        extra = [pltpu.SemaphoreType.DMA((4,))] * 2 + reducer_scratch(DECODER_CHUNKS, False)
        taken = tuple(
            jax.ShapeDtypeStruct(member.shape[-2:], member.dtype) for member in given
        )
        params = dict(collective_id=1, has_side_effects=True)
    else:
        summed = jax.ShapeDtypeStruct((DECODER_CHUNKS, 2, 16, 16, SPAN), BF16)
        extra, given, taken = [], (), ()
        params = dict()
    return pl.pallas_call(
        functools.partial(decoder_kernel, reduce),
        out_shape=(
            summed,
            jax.ShapeDtypeStruct((2, 2, 16, 16, SPAN), BF16),
            jax.ShapeDtypeStruct((24, width), F32),
            jax.ShapeDtypeStruct((256, 768), BF16),
        )
        + taken,
        in_specs=[smem_spec()] * 2 + [vmem_spec()] * 8 + [any_spec()] * (6 + len(given)),
        out_specs=(vmem_spec(),) * 4 + (any_spec(),) * len(taken),
        scratch_shapes=[
            pltpu.VMEM((2, 4, 32, 128), F32),
            pltpu.VMEM((length, width), F32),
            pltpu.VMEM((length, width), BF16),
            pltpu.VMEM((length, 768), BF16),
            pltpu.VMEM((512, length), BF16),
            pltpu.VMEM((4, length, length), BF16),
            pltpu.VMEM((256, length), F32),
            pltpu.VMEM((length, 256), BF16),
            pltpu.VMEM((length, width), BF16),
            pltpu.VMEM((length, 2048), BF16),
            pltpu.VMEM((length, 2048), BF16),
            pltpu.VMEM((length, width), BF16),
            pltpu.VMEM((length, width), BF16),
            pltpu.VMEM((length, 256), BF16),
            pltpu.VMEM((4, 1, length), F32),
            pltpu.VMEM((length, 768), BF16),
            pltpu.VMEM((length, width), F32),
            pltpu.VMEM((4, length, 128), BF16),
            pltpu.VMEM(entry_weight.shape, BF16),
            pltpu.VMEM(attend.shape, BF16),
            pltpu.VMEM(merging.shape, BF16),
            pltpu.VMEM(expand.shape, BF16),
            pltpu.VMEM(shrink.shape, BF16),
            pltpu.SemaphoreType.DMA((6,)),
        ]
        + extra,
        compiler_params=pltpu.CompilerParams(vmem_limit_bytes=60 * 2**20, **params),
        name="decoder_block",
    )(
        sizes, distance, slots, jnp.asarray(frequency)[None], sent, biases, mask_token[None], gains, shifts,
        inner[None], cotangent, entry_weight, attend, merging, expand, shrink, *given,
    )


def encoder_backward_kernel(
    reduce, encoded_grad, sums, decoder_vectors, gains, tokens, rest, attend_far, merging_far, expand_far,
    shrink_far, normed_far, mixed_far, turned_far, probs_far, context_far, middle_far, normed_two_far, active_far,
    slope_far, *refs,
):
    if reduce:
        (active_taken, normed_taken, normed_two_taken, context_taken), refs = refs[:4], refs[4:]
        (summed, vectors, tokens_grad, decoder_sums, arrived), refs = refs[:5], refs[5:]
    else:
        active_taken, normed_taken, normed_two_taken = active_far.at[1], normed_far.at[1], normed_two_far.at[1]
        (summed, vectors, tokens_grad), refs = refs[:3], refs[3:]
    (
        hidden, attend, merging, expand, shrink, mixed, turned, probs, middle, slope,
        normed, normed_two, active, context, go, before_grad, attention_rows, mixed_grad,
        norm_sum, context_grad, key_grad, query_turned, load_sem, part_sem,
    ) = refs[:24]
    pack = lax.axis_index("section")

    def part_loads(part):
        cols = slice(part * 1024, part * 1024 + 1024)
        slot = part % 2
        return [
            pltpu.make_async_copy(expand_far.at[:, cols], expand.at[slot], part_sem.at[slot, 0]),
            pltpu.make_async_copy(shrink_far.at[cols], shrink.at[slot], part_sem.at[slot, 1]),
            pltpu.make_async_copy(slope_far.at[:, cols], slope.at[slot], part_sem.at[slot, 2]),
        ]

    for copy in part_loads(0):
        copy.start()
    if reduce:
        (
            decoder_total, encoder_total, decoder_got, encoder_got, payload, rest_own, rest_got, attention_given,
            small_send, small_recv, pay_send, pay_recv, small_load, rest_load, rest_send, rest_recv,
            pair_send, pair_recv,
        ) = refs[24:42]
        mine, partner = neighbours()
        greet(partner)
        engine = reducer(CHUNKS, mine, partner, summed, refs[42:], True)
        rest_loads = fetch([(rest.at[chunk, mine["c"]], rest_own.at[chunk]) for chunk in range(2)], rest_load)
        decoder_load = pltpu.make_async_copy(decoder_vectors, decoder_total.at[0], small_load)
        decoder_load.start()

        def pair_copy(number):
            own, other = slice(0, 256), slice(256, 512)
            wide = slice((number - 5) * 1024, min((number - 5) * 1024 + 1024, 2304))
            if number == 0:
                source, target = encoded_grad, go.at[other]
            elif number < 4:
                source, target = before_grad.at[number - 1, own], before_grad.at[number - 1, other]
            elif number == 4:
                source, target = attention_given, attention_rows.at[:, other]
            else:
                source, target = mixed_grad.at[own, wide], mixed_grad.at[other, wide]
            return remote(source, target, pair_send.at[number], pair_recv.at[number], partner["c"])

        def rest_copy(chunk):
            return remote(
                rest.at[chunk, 1 - mine["c"]], rest_got.at[chunk], rest_send.at[chunk], rest_recv.at[chunk],
                partner["c"],
            )

    loads = [
        (active_far.at[0], active.at[:, 0:256]),
        (active_taken, active.at[:, 256:512]),
        (middle_far, middle),
        (merging_far, merging),
        (normed_two_far.at[0], normed_two.at[:, 0:256]),
        (normed_two_taken, normed_two.at[:, 256:512]),
        (mixed_far, mixed),
        (probs_far, probs),
        (turned_far, turned),
        (context_far, context.at[0:256]),
        (normed_far.at[0], normed.at[:, 0:256]),
        (normed_taken, normed.at[:, 256:512]),
        (attend_far, attend),
        (tokens.at[pack], hidden),
    ]
    if reduce:
        loads.append((context_taken, context.at[256:512]))
        await_greetings()
        pair_copy(0).start()
    loads = fetch(loads, load_sem)
    for copy in part_loads(1):
        copy.start()
    vectors[...] = sums[...]
    go[0:256] = encoded_grad[...]
    vectors[1:2, :768] = row_sum(encoded_grad[...].astype(F32))
    norm_sum[...] = jnp.zeros_like(norm_sum)

    def send(number):
        if reduce:
            pair_copy(number).start()

    def receive(number):
        if reduce:
            pair_copy(number).wait_recv()

    def weight_grad(place, left, right):
        if reduce:
            store_packed(engine.put, 0, place, dot(left, right))
            return
        for core in range(2):

            def put(shards, column, value, core=core):
                store_chunks(summed, (core, shards), column, value)

            store_packed(put, 0, place, dot(left[:, core * 256 : core * 256 + 256], right[0:256]))

    def shrink_grad(part):
        if part == 0:
            for copy in loads[0:2]:
                copy.wait()
            receive(0)
        weight_grad(ENCODER_SHRINK[part], active[...], go[:, part * 256 : part * 256 + 256])

    def hidden_layer(part):
        for copy in part_loads(part):
            copy.wait()
        slot = part % 2
        grad = low(slope[slot] * dot_nt(encoded_grad[...], shrink[slot]))
        before_grad[part, 0:256] = grad
        send(1 + part)
        vectors[6 + part : 7 + part] = row_sum(grad.astype(F32))
        norm_sum[...] += dot_nt(grad, expand[slot])
        if part == 0:
            for copy in part_loads(2):
                copy.start()

    def expand_grad(part):
        if part == 0:
            for copy in loads[4:6]:
                copy.wait()
        receive(1 + part)
        weight_grad(ENCODER_EXPAND[part], normed_two[...], before_grad[part])

    def middle_layer():
        for copy in loads[2:4]:
            copy.wait()
        unit, inverse = standardize(middle[...])
        norm_grad = norm_sum[...]
        vectors[3:4, :768] = row_sum(norm_grad * unit)
        vectors[5:6, :768] = row_sum(norm_grad)
        grad = encoded_grad[...].astype(F32) + norm_back(unit, inverse, gains[1:2], norm_grad)
        vectors[0:1, :768] = row_sum(grad)
        tokens_grad[...] = grad
        own, other = flipped_halves(grad, 24, mine["c"] if reduce else 0)
        attention_rows[:, 0:256] = own
        if reduce:
            attention_given[...] = other
        else:
            attention_rows[:, 256:512] = other
        send(4)
        context_grad[...] = low(dot_nt(low(grad), merging[...]))
        for copy in loads[6:9]:
            copy.wait()

    def attention(first):
        @pl.loop(first, first + 2)
        def _(pair):
            lanes = pair_lanes(pair)
            values = mixed[:, pair_lanes(pair, 1536)]
            keys_total = jnp.zeros((TILE, 128), F32)
            values_total = jnp.zeros((TILE, 128), F32)
            for half in range(2):
                prob = probs[pair * 2 + half]
                outer = only(context_grad[:, lanes], half)
                query = only(mixed[:, lanes], half)
                wide = prob.astype(F32)
                grad = dot_nt(values, outer)
                raw = low(wide * (grad - jnp.sum(wide * grad, axis=0, keepdims=True)))
                keys_total = keys_total + dot(raw, query)
                values_total = values_total + dot(prob, outer)
                rows = head_rows(pair, half)
                query_turned[rows] = dot(turned[rows], raw)
            key_grad[0, :, lanes] = keys_total
            key_grad[1, :, lanes] = values_total

    def mixing():
        mixed_grad[0:256, 0:768] = low(query_turned[...].T * 0.125)
        mixed_grad[0:256, 768:1536] = low(key_grad[0] * 0.125)
        mixed_grad[0:256, 1536:2304] = low(key_grad[1])
        for part in range(3):
            send(5 + part)

    def attend_grad(part):
        if part == 0:
            for copy in loads[10:12]:
                copy.wait()
        receive(5 + part)
        wide = slice(part * 1024, min(part * 1024 + 1024, 2304))
        weight_grad(ENCODER_ATTEND[part], normed[...], mixed_grad[:, wide])

    def merge_grad():
        receive(4)
        for copy in loads[9:10] + loads[14:]:
            copy.wait()
        weight_grad(ENCODER_MERGE, attention_rows[...], context[...])

    def input_layer():
        for copy in loads[12:14]:
            copy.wait()
        norm_grad = dot_nt(mixed_grad[0:256], attend[...])
        unit, inverse = standardize(hidden[...])
        vectors[2:3, :768] = row_sum(norm_grad * unit)
        vectors[4:5, :768] = row_sum(norm_grad)
        grad = tokens_grad[...] + norm_back(unit, inverse, gains[0:1], norm_grad)
        tokens_grad[...] = grad
        if reduce:
            payload[...] = low(grad)

    if not reduce:
        for part in range(3):
            shrink_grad(part)
        for part in range(3):
            hidden_layer(part)
            expand_grad(part)
        middle_layer()
        for first in (0, 2, 4):
            attention(first)
        mixing()
        for part in range(3):
            attend_grad(part)
        merge_grad()
        input_layer()
        store_chunks(summed, (slice(None), slice(None)), REST * UNIT, jnp.zeros((2, 16, 16, UNIT), F32))
        return

    def exchange(source, piece):
        rows = aligned(piece * 32, 32, 32)
        return remote(source.at[rows], arrived.at[rows], pay_send.at[piece], pay_recv.at[piece], partner["x"])

    small_route = ("c",) + ROUTES[0]
    totals = ((decoder_total, decoder_got), (encoder_total, encoder_got))

    def small_copy(stage, kind):
        source, target = totals[kind]
        return remote(
            source.at[stage],
            target.at[stage],
            small_send.at[stage, kind],
            small_recv.at[stage, kind],
            partner[small_route[stage]],
        )

    def small_advance(stage):
        if stage == 0:
            decoder_load.wait()
            encoder_total[0] = vectors[...]
        for kind in range(2):
            source, target = totals[kind]
            if stage > 0:
                small_copy(stage - 1, kind).wait_recv()
                source[stage] = source[stage - 1] + target[stage - 1]
            if stage < 5:
                small_copy(stage, kind).start()

    def hidden_and_rest():
        hidden_layer(1)
        for chunk in range(2):
            rest_copy(chunk).start()

    def rest_sum():
        for chunk in range(2):
            rest_loads[chunk].wait()
            rest_copy(chunk).wait_recv()
            value = rest_own[chunk].astype(F32) + rest_got[chunk].astype(F32)
            engine.own[REST * 2 + chunk] = low(value)

    def attention_end():
        attention(4)
        mixing()

    def attend_end():
        attend_grad(2)
        merge_grad()

    hidden_layer(0)
    shrink_grad(0)
    part = functools.partial
    works = [
        part(shrink_grad, 1), hidden_and_rest, part(shrink_grad, 2), part(hidden_layer, 2), part(expand_grad, 0),
        middle_layer, part(expand_grad, 1), part(attention, 0), part(expand_grad, 2), part(attention, 2),
        attention_end, rest_sum, input_layer, part(attend_grad, 0), part(attend_grad, 1), attend_end,
    ]
    works = dict(enumerate(works))
    turns = CHUNKS + STARTS[4]
    works.update({turns - 11 + 2 * stage: part(small_advance, stage) for stage in range(6)})

    @pl.loop(0, turns)
    def _(number):
        engine.turn(number)
        for position, work in works.items():
            pl.when(number == position)(work)

        piece = number // 2

        @pl.when((pack == 0) & (number % 2 == 0) & (piece < 8))
        def _():
            exchange(encoded_grad, piece).start()

        @pl.when((pack == 1) & (number % 2 == 0) & (piece >= 6))
        def _():
            exchange(payload, piece - 6).start()

    for stage in range(5):
        for kind in range(2):
            small_copy(stage, kind).wait_send()
    for piece in range(8):
        exchange(payload, piece).wait()
    for chunk in range(2):
        rest_copy(chunk).wait_send()
    for number in range(8):
        pair_copy(number).wait_send()
    engine.close()
    vectors[...] = encoder_total[5]
    decoder_sums[...] = decoder_total[5]


def encoder_backward_call(
    reduce, tokens, encoded_grad, sums, decoder_vectors, rest, kept, taken, gains, attend, merging, expand, shrink
):
    if reduce:
        summed = jax.ShapeDtypeStruct((CHUNKS, 16, SPAN), F32)
        more = (
            jax.ShapeDtypeStruct(decoder_vectors.shape, F32),
            jax.ShapeDtypeStruct((256, 768), BF16),
        )
        more_specs = (vmem_spec(), any_spec())
        extra = [
            pltpu.VMEM((6,) + decoder_vectors.shape, F32),
            pltpu.VMEM((6,) + sums.shape, F32),
            pltpu.VMEM((5,) + decoder_vectors.shape, F32),
            pltpu.VMEM((5,) + sums.shape, F32),
            pltpu.VMEM((256, 768), BF16),
            pltpu.VMEM((2, 16, 16, SPAN), BF16),
            pltpu.VMEM((2, 16, 16, SPAN), BF16),
            pltpu.VMEM((384, 256), BF16),
            pltpu.SemaphoreType.DMA((5, 2)),
            pltpu.SemaphoreType.DMA((5, 2)),
            pltpu.SemaphoreType.DMA((8,)),
            pltpu.SemaphoreType.DMA((8,)),
            pltpu.SemaphoreType.DMA,
            pltpu.SemaphoreType.DMA((2,)),
            pltpu.SemaphoreType.DMA((2,)),
            pltpu.SemaphoreType.DMA((2,)),
            pltpu.SemaphoreType.DMA((8,)),
            pltpu.SemaphoreType.DMA((8,)),
        ] + reducer_scratch(CHUNKS, True)
        params = dict(collective_id=2, has_side_effects=True)
    else:
        summed = jax.ShapeDtypeStruct((CHUNKS, 2, 16, 16, SPAN), BF16)
        more, more_specs, extra, params = (), (), [], dict()
    return pl.pallas_call(
        functools.partial(encoder_backward_kernel, reduce),
        out_shape=(
            summed,
            jax.ShapeDtypeStruct(sums.shape, F32),
            jax.ShapeDtypeStruct((256, 768), F32),
        )
        + more,
        in_specs=[vmem_spec()] * 2 + [any_spec(), vmem_spec()] + [any_spec()] * (15 + len(taken)),
        out_specs=(vmem_spec(),) * 3 + more_specs,
        scratch_shapes=[
            pltpu.VMEM((256, 768), F32),
            pltpu.VMEM(attend.shape, BF16),
            pltpu.VMEM(merging.shape, BF16),
            pltpu.VMEM((2, 768, 1024), BF16),
            pltpu.VMEM((2, 1024, 768), BF16),
            pltpu.VMEM((256, 2304), BF16),
            pltpu.VMEM((768, 256), BF16),
            pltpu.VMEM((12, 256, 256), BF16),
            pltpu.VMEM((256, 768), F32),
            pltpu.VMEM((2, 256, 1024), F32),
            pltpu.VMEM((384, 512), BF16),
            pltpu.VMEM((384, 512), BF16),
            pltpu.VMEM((1536, 512), BF16),
            pltpu.VMEM((512, 768), BF16),
            pltpu.VMEM((512, 768), BF16),
            pltpu.VMEM((3, 512, 1024), BF16),
            pltpu.VMEM((384, 512), BF16),
            pltpu.VMEM((512, 2304), BF16),
            pltpu.VMEM((256, 768), F32),
            pltpu.VMEM((256, 768), BF16),
            pltpu.VMEM((2, 256, 768), F32),
            pltpu.VMEM((768, 256), F32),
            pltpu.SemaphoreType.DMA((15,)),
            pltpu.SemaphoreType.DMA((2, 3)),
        ]
        + extra,
        compiler_params=pltpu.CompilerParams(vmem_limit_bytes=60 * 2**20, **params),
        name="encoder_backward",
    )(
        encoded_grad, sums, decoder_vectors, gains, tokens, rest, attend, merging, expand, shrink, *kept, *taken
    )


def unpack(packed, place):
    def take(start, size):
        pieces = []
        while size:
            chunk, first = divmod(start, SPAN)
            length = min(size, SPAN - first)
            pieces.append(packed[chunk, ..., first : first + length])
            start, size = start + length, size - length
        return pieces[0] if len(pieces) == 1 else jnp.concatenate(pieces, axis=-1)

    offset, count, width = place
    pieces = [take(offset + i * width, width) for i in range(count // 16)]
    if count % 16:
        rest = take(offset + count // 16 * width, width // 2)
        pieces.append(jnp.concatenate([rest[..., :8, :], rest[..., 8:, :]], axis=-1))
    return pieces[0] if len(pieces) == 1 else jnp.concatenate(pieces, axis=-2)


def finish_kernel(
    decoder_summed_far, decoder_sums_far, encoder_sums_far, summed_far, arrived_far, tokens_grad_far, encoded_grad_far,
    boundary, statistics, e_gains, e_shifts, e_biases, e_attend, e_merge, e_expand, e_inner, e_shrink,
    d_entry, d_biases, mask_grad, d_gains, d_shifts, d_attend, d_merge, d_expand, d_inner, d_shrink,
    decoder_summed, decoder_sums, encoder_sums, summed, arrived, tokens_grad, encoded_grad, load_sem,
):
    section = lax.axis_index("section")
    loads = fetch(
        [
            (decoder_summed_far, decoder_summed),
            (decoder_sums_far, decoder_sums),
            (encoder_sums_far, encoder_sums),
            (summed_far, summed),
            (arrived_far, arrived),
            (tokens_grad_far, tokens_grad),
            (encoded_grad_far, encoded_grad),
        ],
        load_sem,
    )
    number = section * lax.axis_size("dp") + lax.axis_index("dp")

    def own(rows, count):
        width = rows.shape[1]
        return pltpu.roll(rows, (width - number * count) % width, axis=1)[:, :count]

    def own_line(rows, count):
        return own(jnp.concatenate([rows[i : i + 1] for i in range(rows.shape[0])], axis=1), count)

    for copy in loads[:3]:
        copy.wait()
    lane = iota((1, 128), 1)
    values = jnp.zeros((1, 128), F32)
    for sums, width, first, count_row, base in ((encoder_sums, DE, 10, 14, 0), (decoder_sums, DD, 12, 16, 4)):
        scale = 1.0 / (sums[count_row : count_row + 1, 0:1] * width)
        for i in range(4):
            value = jnp.sum(sums[first + i : first + i + 1, :], axis=1, keepdims=True) * scale
            values = jnp.where(lane == base + i, value, values)
    statistics[...] = jnp.sqrt(values)[:, :8]
    rows = own(encoder_sums[0:8, :DE], 24)
    e_biases[...] = rows[0:2]
    e_gains[...] = rows[2:4]
    e_shifts[...] = rows[4:6]
    e_inner[...] = own_line(encoder_sums[6:9], 96)
    rows = own(decoder_sums[0:8], 16)
    d_biases[...] = rows[0:3]
    mask_grad[...] = rows[3:4]
    d_gains[...] = rows[4:6]
    d_shifts[...] = rows[6:8]
    d_inner[...] = own_line(decoder_sums[8:12], 64)

    d_merge[...] = unpack(decoder_summed, DECODER_MERGE)
    d_expand[...] = unpack(decoder_summed, DECODER_EXPAND)
    d_shrink[...] = unpack(decoder_summed, DECODER_SHRINK)
    loads[3].wait()
    d_entry[...] = unpack(summed, ENTRY)
    d_attend[...] = unpack(summed, DECODER_ATTEND)
    for target, places in ((e_expand, ENCODER_EXPAND), (e_attend, ENCODER_ATTEND), (e_shrink, ENCODER_SHRINK)):
        start = 0
        for place in places:
            target[:, start : start + place[2]] = unpack(summed, place)
            start += place[2]
    e_merge[...] = unpack(summed, ENCODER_MERGE)
    for copy in loads[4:]:
        copy.wait()

    @pl.when(section == 0)
    def _():
        boundary[0, 0] = tokens_grad[...]
        boundary[0, 1] = arrived[...].astype(F32)

    @pl.when(section == 1)
    def _():
        boundary[0, 0] = arrived[...].astype(F32)
        boundary[0, 1] = encoded_grad[...].astype(F32)


def finish_call(*operands):
    shapes = (
        (1, 2, 256, 768), (1, 8), (2, 24), (2, 24), (2, 24), (24, 2304), (24, 768), (24, 3072), (1, 96), (96, 768),
        (24, 512), (3, 16), (1, 16), (2, 16), (2, 16), (16, 768), (16, 256), (16, 2048), (1, 64), (64, 512),
    )
    outs = list(
        pl.pallas_call(
            finish_kernel,
            out_shape=tuple(jax.ShapeDtypeStruct(shape, F32) for shape in shapes),
            in_specs=[any_spec()] * len(operands),
            out_specs=(vmem_spec(),) * len(shapes),
            scratch_shapes=[pltpu.VMEM(operand.shape, operand.dtype) for operand in operands]
            + [pltpu.SemaphoreType.DMA((len(operands),))],
            compiler_params=pltpu.CompilerParams(vmem_limit_bytes=60 * 2**20),
            name="finish",
        )(*operands)
    )
    for line in (1, 8, 12, 18):
        outs[line] = outs[line].reshape(-1)
    for turned in (6, 16):
        outs[turned] = outs[turned].T
    return tuple(outs)


def scatter_sum(member, share_dim):
    return lax.psum_scatter(
        member, ("section", "dp"), scatter_dimension=share_dim, tiled=True
    )


def finish_generic(decoder_part, part, decoder_sums, encoder_sums, tokens_grad, encoded_grad):
    section = lax.axis_index("section")
    payload = jnp.where(section == 0, encoded_grad, low(tokens_grad))

    def whole(packed, *places):
        packed = jnp.swapaxes(packed, 1, 2).reshape(-1, 32, 16, SPAN)
        blocks = [unpack(packed, place).reshape(32 * place[1], place[2]) for place in places]
        return scatter_sum(jnp.concatenate(blocks, axis=1).astype(F32), 0)

    def line(value):
        return scatter_sum(value, value.ndim - 1)

    arrived = lax.ppermute(payload, "section", [(0, 1), (1, 0)]).astype(F32)
    boundary = jnp.where(
        section == 0,
        jnp.stack([tokens_grad, arrived]),
        jnp.stack([arrived, encoded_grad.astype(F32)]),
    )
    sums = jnp.concatenate(
        [jnp.sum(encoder_sums[10:14], axis=1), jnp.sum(decoder_sums[12:16], axis=1)]
    )
    sums, counts = lax.psum((sums, (encoder_sums[14, 0], decoder_sums[16, 0])), ("section", "dp"))
    scales = jnp.concatenate([jnp.full((4,), counts[0] * DE), jnp.full((4,), counts[1] * DD)])
    return (
        boundary[None],
        jnp.sqrt(sums / scales),
        line(encoder_sums[2:4, :DE]),
        line(encoder_sums[4:6, :DE]),
        line(encoder_sums[0:2, :DE]),
        whole(part, *ENCODER_ATTEND),
        whole(part, ENCODER_MERGE).T,
        whole(part, *ENCODER_EXPAND),
        line(encoder_sums[6:9].reshape(-1)),
        whole(part, *ENCODER_SHRINK),
        whole(decoder_part[1], (0,) + ENTRY[1:]),
        line(decoder_sums[0:3]),
        line(decoder_sums[3]),
        line(decoder_sums[4:6]),
        line(decoder_sums[6:8]),
        whole(decoder_part[1], (768,) + DECODER_ATTEND[1:]),
        whole(decoder_part[0], DECODER_MERGE).T,
        whole(decoder_part[0], DECODER_EXPAND),
        line(decoder_sums[8:12].reshape(-1)),
        whole(decoder_part[0], DECODER_SHRINK),
    )


def body(
    visible_tokens,
    cotangent,
    chip_sizes,
    ground_distance,
    visible_slots,
    encoder_gains,
    encoder_shifts,
    encoder_biases,
    encoder_attend,
    encoder_merge,
    encoder_expand,
    encoder_inner,
    encoder_shrink,
    decoder_entry,
    decoder_biases,
    mask_token,
    decoder_gains,
    decoder_shifts,
    decoder_attend,
    decoder_merge,
    decoder_widen_weight,
    decoder_inner,
    decoder_shrink,
):
    reduce = (lax.axis_size("section"), lax.axis_size("dp")) == (2, 16)
    sent, sums, *kept = encoder_forward_call(
        reduce, chip_sizes, visible_tokens, encoder_gains, encoder_shifts, encoder_biases,
        encoder_attend, encoder_merge, encoder_expand, encoder_inner, encoder_shrink,
    )
    given = (kept[7], kept[0], kept[6], kept[4])
    decoder_summed, rest, decoder_vectors, encoded_grad, *taken = decoder_call(
        reduce, chip_sizes, ground_distance, visible_slots, sent, cotangent, decoder_entry, decoder_biases, mask_token,
        decoder_gains, decoder_shifts, decoder_attend, decoder_merge, decoder_widen_weight, decoder_inner,
        decoder_shrink, given,
    )
    summed, encoder_sums, tokens_grad, *more = encoder_backward_call(
        reduce, visible_tokens, encoded_grad, sums, decoder_vectors, rest, kept, taken,
        encoder_gains, encoder_attend, encoder_merge, encoder_expand, encoder_shrink,
    )
    if reduce:
        decoder_sums, arrived = more
        return finish_call(
            decoder_summed, decoder_sums, encoder_sums, summed, arrived, tokens_grad, encoded_grad
        )
    return finish_generic(
        (decoder_summed, rest), summed, decoder_vectors, encoder_sums, tokens_grad, encoded_grad
    )


def solution(mesh):
    in_specs = (
        P("dp", None, None),
        P("dp", None, None),
        P("dp", None),
        P("dp", None),
        P("dp", None),
        P(),
        P(),
        P(),
        P(),
        P(),
        P(),
        P(),
        P(),
        P(),
        P(),
        P(),
        P(),
        P(),
        P(),
        P(),
        P(),
        P(),
        P(),
    )
    out_specs = (
        P("section", "dp", None, None),
        P(),
        P(None, ("section", "dp")),
        P(None, ("section", "dp")),
        P(None, ("section", "dp")),
        P(("section", "dp"), None),
        P(None, ("section", "dp")),
        P(("section", "dp"), None),
        P(("section", "dp")),
        P(("section", "dp"), None),
        P(("section", "dp"), None),
        P(None, ("section", "dp")),
        P(("section", "dp")),
        P(None, ("section", "dp")),
        P(None, ("section", "dp")),
        P(("section", "dp"), None),
        P(None, ("section", "dp")),
        P(("section", "dp"), None),
        P(("section", "dp")),
        P(("section", "dp"), None),
    )
    return jax.shard_map(body, mesh=mesh, in_specs=in_specs, out_specs=out_specs, check_vma=False)
```

```python
import functools
import types

import jax
import jax.numpy as jnp
import numpy as np
from jax import lax
from jax.experimental import pallas as pl
from jax.experimental.pallas import tpu as pltpu
from jax.sharding import PartitionSpec as P

DE = 768
DD = 512
TILE = 256
BLOCK = 512
NEGATIVE = -1e30
F32, BF16 = jnp.float32, jnp.bfloat16
MESH_ID = pl.DeviceIdType.MESH

CANON = ("x", "z2", "z1", "y")
ROUTES = (("x", "y", "z1", "z2"), ("y", "x", "z1", "z2"), ("z1", "z2", "x", "y"))
WIDTHS = (2, 3, 1)
OFFSETS = (0, 2, 5)
SPAN = 128 * sum(WIDTHS)
UNIT = 2 * SPAN
DECODER_CHUNKS = 6
CHUNKS = 20
RING = 3
STAGING = 6
LAG = 2

DECODER_EXPAND, DECODER_SHRINK, DECODER_MERGE = (0, 16, 2048), (2048, 64, 512), (4096, 16, 256)
ENTRY, DECODER_ATTEND = (0, 24, 512), (768, 16, 768)
ENCODER_SHRINK = tuple((UNIT * (1 + part), 96, 256) for part in range(3))
ENCODER_EXPAND = tuple((UNIT * (4 + part), 24, 1024) for part in range(3))
ENCODER_ATTEND = ((UNIT * 7, 24, 1024), (UNIT * 8, 24, 1024), (UNIT * 9, 24, 256))
ENCODER_MERGE = (UNIT * 9 + 384, 24, 768)


def dot(a, b):
    return jnp.dot(a, b, preferred_element_type=F32)


def dot_nt(a, b):
    return lax.dot_general(a, b, (((1,), (1,)), ((), ())), preferred_element_type=F32)


def dot_tn(a, b):
    return lax.dot_general(a, b, (((0,), (0,)), ((), ())), preferred_element_type=F32)


def low(value):
    return value.astype(BF16)


def standardize(values):
    centered = values - jnp.mean(values, axis=-1, keepdims=True)
    inverse = lax.rsqrt(jnp.mean(centered * centered, axis=-1, keepdims=True) + 1e-05)
    return centered * inverse, inverse


def norm_back(unit, inverse, gain, grad):
    inner = grad * gain
    return inverse * (
        inner
        - jnp.mean(inner, axis=-1, keepdims=True)
        - unit * jnp.mean(inner * unit, axis=-1, keepdims=True)
    )


def row_sum(values):
    return jnp.sum(values, axis=0, keepdims=True)


def gelu_pair(before):
    half = 0.5 * (1.0 + lax.erf(before * 0.7071067811865476))
    density = jnp.exp(-0.5 * before * before) * 0.3989422804014327
    return before * half, half + before * density


def chip_of(places, sizes, pack):
    end = sizes[pack, 0]
    chip = (places >= end).astype(jnp.int32)
    for slot in range(1, 4):
        end = end + sizes[pack, slot]
        chip = chip + (places >= end).astype(jnp.int32)
    return chip


def iota(shape, dimension):
    return lax.broadcasted_iota(jnp.int32, shape, dimension)


def aligned(start, size, unit):
    if isinstance(start, int):
        return slice(start, start + size)
    return pl.ds(pl.multiple_of(start, unit), size)


def pair_lanes(pair, base=0):
    return aligned(base + pair * 128, 128, 128)


def head_rows(pair, half, base=0):
    return aligned(base + pair * 128 + half * 64, 64, 64)


def rows_of(tile, size=TILE):
    return aligned(tile * size, size, size)


def only(values, half):
    return jnp.where(iota((1, 128), 1) // 64 == half, values, jnp.zeros_like(values))


def fetch(pairs, sems):
    copies = [
        pltpu.make_async_copy(source, target, sems.at[i]) for i, (source, target) in enumerate(pairs)
    ]
    for copy in copies:
        copy.start()
    return copies


def store_packed(put, first, place, value):
    offset, count, width = place
    value = value.reshape(-1, count, width)
    shards = slice(first, first + value.shape[0]) if isinstance(first, int) else pl.ds(first, value.shape[0])
    for piece in range(count // 16):
        put(shards, offset + piece * width, value[:, piece * 16 : piece * 16 + 16])
    if count % 16:
        half = width // 2
        rest = value[:, count - 8 :]
        rest = jnp.concatenate([rest[:, :, :half], rest[:, :, half:]], axis=1)
        put(shards, offset + count // 16 * width, rest)


def halves(shards, value):
    pairs = value.reshape(value.shape[0] // 2, 2, *value.shape[1:])
    if isinstance(shards, slice):
        return slice(shards.start // 2, shards.stop // 2), pairs[:, 0], pairs[:, 1]
    return pl.ds(shards.start // 2, shards.size // 2), pairs[:, 0], pairs[:, 1]


def place_of(names, bits):
    index = 0
    for name in names:
        index = index * 2 + bits[name]
    return index


def left_after(route, stage):
    return tuple(name for name in CANON if name not in route[:stage])


def choices(names):
    for number in range(2 ** len(names)):
        yield {name: (number >> (len(names) - 1 - i)) & 1 for i, name in enumerate(names)}


def neighbours():
    section = lax.axis_index("section")
    data = lax.axis_index("dp")
    mine = {"x": section, "c": data % 2, "y": data // 2 % 2, "z1": data // 4 % 2, "z2": data // 8 % 2}
    partner = {"x": (1 - section, data)}
    for name, step in {"c": 1, "y": 2, "z1": 4, "z2": 8}.items():
        partner[name] = (section, data + step * (1 - 2 * mine[name]))
    return mine, partner


def greet(partner):
    barrier = pltpu.get_barrier_semaphore()
    for name in ("c",) + CANON:
        pl.semaphore_signal(barrier, inc=1, device_id=partner[name], device_id_type=MESH_ID)


def await_greetings():
    pl.semaphore_wait(pltpu.get_barrier_semaphore(), 5)


def remote(source, target, send, recv, device):
    return pltpu.make_async_remote_copy(
        src_ref=source,
        dst_ref=target,
        send_sem=send,
        recv_sem=recv,
        device_id=device,
        device_id_type=MESH_ID,
    )


def reducer(chunks, slots, mine, partner, out, refs):
    own, staging, first = refs[:3]
    sent, got = refs[3:15], refs[15:27]
    first_send, first_recv, send_sem, recv_sem = refs[27:31]

    def first_copy(chunk, source=None):
        if source is None:
            source = staging.at[chunk % slots]
        return remote(source, first.at[chunk], first_send.at[chunk], first_recv.at[chunk], partner["c"])

    def stage_copy(route, stage, chunk):
        return remote(
            sent[route * 4 + stage].at[chunk % RING],
            got[route * 4 + stage].at[chunk],
            send_sem.at[route, stage, chunk],
            recv_sem.at[route, stage, chunk],
            partner[ROUTES[route][stage]],
        )

    def total(route, stage, chunk, bits):
        spot = place_of(CANON, bits)
        cols = slice(OFFSETS[route] * 128, (OFFSETS[route] + WIDTHS[route]) * 128)
        value = own[chunk, spot, :, cols].astype(F32) + first[chunk, spot, :, cols].astype(F32)
        for earlier in range(stage):
            names = left_after(ROUTES[route], earlier + 1)
            value = value + got[route * 4 + earlier][chunk, place_of(names, bits)].astype(F32)
        return value

    def advance(stage, chunk):
        for route in range(3):
            if stage:
                stage_copy(route, stage - 1, chunk).wait_recv()
            else:
                first_copy(chunk).wait_recv() if route == 0 else None
            if stage < 4:

                @pl.when(chunk >= RING)
                def _(route=route):
                    stage_copy(route, stage, chunk - RING).wait_send()

        values = []
        for route in range(3):
            path = ROUTES[route]
            if stage == 4:
                values.append(total(route, 4, chunk, mine))
                continue
            names = left_after(path, stage + 1)
            for free in choices(names):
                bits = dict(mine)
                bits[path[stage]] = 1 - mine[path[stage]]
                bits.update(free)
                values.append((route, place_of(names, free), low(total(route, stage, chunk, bits))))
        if stage == 4:
            out[chunk] = jnp.concatenate(values, axis=1)
            return
        for route, spot, value in values:
            sent[route * 4 + stage][chunk % RING, spot] = value
        for route in range(3):
            stage_copy(route, stage, chunk).start()

    def turn(number):
        for stage in range(4, -1, -1):
            chunk = number - LAG * stage
            pl.when((chunk >= 0) & (chunk < chunks))(functools.partial(advance, stage, chunk))

    def put(shards, column, value):
        shards, even, odd = halves(shards, value)
        kept = low(jnp.where(mine["c"] == 0, even, odd))
        given = low(jnp.where(mine["c"] == 0, odd, even))
        width = value.shape[2]
        done = 0
        while done < width:
            chunk, start = divmod(column + done, SPAN)
            size = min(width - done, SPAN - start)
            own[chunk, shards, :, start : start + size] = kept[:, :, done : done + size]
            staging[chunk % slots, shards, :, start : start + size] = given[:, :, done : done + size]
            done += size

    def release(unit):
        for chunk in (2 * unit, 2 * unit + 1):
            if chunk >= slots:
                first_copy(chunk - slots).wait_send()

    def send(unit):
        for chunk in (2 * unit, 2 * unit + 1):
            first_copy(chunk).start()

    def close(released):
        for chunk in range(released, chunks):
            first_copy(chunk).wait_send()
        for chunk in range(chunks - RING, chunks):
            for route in range(3):
                for stage in range(4):
                    stage_copy(route, stage, chunk).wait_send()

    return types.SimpleNamespace(
        own=own, first_copy=first_copy, turn=turn, put=put, release=release, send=send, close=close
    )


def reducer_scratch(chunks, slots):
    stages = [(width, block) for width in WIDTHS for block in (8, 4, 2, 1)]
    return (
        [
            pltpu.VMEM((chunks, 16, 16, SPAN), BF16),
            pltpu.VMEM((slots, 16, 16, SPAN), BF16),
            pltpu.VMEM((chunks, 16, 16, SPAN), BF16),
        ]
        + [pltpu.VMEM((RING, block, 16, width * 128), BF16) for width, block in stages]
        + [pltpu.VMEM((chunks, block, 16, width * 128), BF16) for width, block in stages]
        + [
            pltpu.SemaphoreType.DMA((chunks,)),
            pltpu.SemaphoreType.DMA((chunks,)),
            pltpu.SemaphoreType.DMA((3, 4, chunks)),
            pltpu.SemaphoreType.DMA((3, 4, chunks)),
        ]
    )


def put_into(parts):
    def put(shards, column, value):
        shards, *pair = halves(shards, value)
        width = value.shape[2]
        done = 0
        while done < width:
            chunk, start = divmod(column + done, SPAN)
            size = min(width - done, SPAN - start)
            for core in range(2):
                parts[chunk, core, shards, :, start : start + size] = low(pair[core][:, :, done : done + size])
            done += size

    return put


def vmem_spec():
    return pl.BlockSpec(memory_space=pltpu.VMEM)


def any_spec():
    return pl.BlockSpec(memory_space=pl.ANY)


def smem_spec():
    return pl.BlockSpec(memory_space=pltpu.SMEM)


def encoder_forward_kernel(
    sizes, gains, shifts, biases, inner, tokens, attend_far, merging_far, expand_far, shrink_far,
    sent, vectors, *refs,
):
    far = refs[:9]
    normed, mixed, turned, probs, context, middle, normed_two, active, slope = refs[9:18]
    hidden, attend, merging, expand, shrink, context_turned, load_sem, save_sem = refs[18:]
    pack = lax.axis_index("section")
    loads = fetch(
        [
            (tokens.at[pack], hidden),
            *[(attend_far.at[:, i * 768 : i * 768 + 768], attend.at[:, i * 768 : i * 768 + 768]) for i in range(3)],
            (merging_far, merging),
            *[(expand_far.at[:, i * 1024 : i * 1024 + 1024], expand.at[:, i * 1024 : i * 1024 + 1024]) for i in range(3)],
            *[(shrink_far.at[i * 1024 : i * 1024 + 1024], shrink.at[i * 1024 : i * 1024 + 1024]) for i in range(3)],
        ],
        load_sem,
    )
    saves = []

    def save(*numbers):
        for number in numbers:
            copy = pltpu.make_async_copy(refs[9 + number], far[number], save_sem.at[number])
            copy.start()
            saves.append(copy)

    vectors[...] = jnp.zeros_like(vectors)
    key_chip = chip_of(4 * iota((TILE, 1), 0), sizes, pack)
    own_chip = chip_of(4 * iota((1, TILE), 1), sizes, pack)
    valid = (key_chip < 4).astype(F32)
    loads[0].wait()
    values = hidden[...]
    vectors[10:11, :768] = row_sum(valid * values * values)
    unit, _ = standardize(values)
    norm = low(unit * gains[0:1] + shifts[0:1])
    normed[...] = norm
    for part in range(3):
        cols = slice(part * 768, part * 768 + 768)
        loads[1 + part].wait()
        mix = dot(norm, attend[:, cols])
        mixed[:, cols] = low(mix)
        if part:
            turned[(part - 1) * 768 : part * 768] = low(mix.T)
    save(0, 1, 2)

    def score(head):
        pair, half = divmod(head, 2)
        query = only(mixed[:, pair_lanes(pair)], half) * BF16(0.125)
        return dot_nt(mixed[:, pair_lanes(pair, 768)], query)

    ready = [score(0), score(1)]
    for head in range(12):
        if head + 2 < 12:
            ready.append(score(head + 2))
        scores = jnp.where(key_chip == own_chip, ready[head], NEGATIVE)
        expos = jnp.exp(scores - jnp.max(scores, axis=0, keepdims=True))
        prob = low(expos * (1.0 / jnp.sum(expos, axis=0, keepdims=True)))
        probs[head] = prob
        context_turned[head * 64 : head * 64 + 64] = dot(turned[768 + head * 64 : 832 + head * 64], prob)

    mingled = low(context_turned[...].T)
    context[...] = mingled
    save(3, 4)
    loads[4].wait()
    attention = dot(mingled, merging[...]) + biases[0:1]
    vectors[11:12, :768] = row_sum(valid * attention * attention)
    center = hidden[...] + attention
    middle[...] = center
    unit, _ = standardize(center)
    norm = low(unit * gains[1:2] + shifts[1:2])
    normed_two[...] = norm
    save(5, 6)
    feed = jnp.zeros_like(center)
    def widened(part):
        if part % 2 == 0:
            loads[5 + part // 2].wait()
        cols = slice(part * 512, part * 512 + 512)
        return dot(norm, expand[:, cols]) + inner[:, cols]

    ready = [widened(0)]
    for part in range(6):
        if part < 5:
            ready.append(widened(part + 1))
        cols = slice(part * 512, part * 512 + 512)
        value, slant = gelu_pair(ready[part])
        value = low(value)
        active[:, cols] = value
        slope[part // 2, :, part % 2 * 512 : part % 2 * 512 + 512] = slant
        if part % 2 == 0:
            loads[8 + part // 2].wait()
        feed = feed + dot(value, shrink[cols])
    save(7, 8)
    feed = feed + biases[1:2]
    vectors[12:13, :768] = row_sum(valid * feed * feed)
    output = center + feed
    vectors[13:14, :768] = row_sum(valid * output * output)
    vectors[14:15, :768] = jnp.broadcast_to(row_sum(valid), (1, 768))
    sent[...] = low(output)
    for copy in saves:
        copy.wait()


def encoder_forward_call(sizes, tokens, gains, shifts, biases, attend, merging, expand, inner, shrink):
    shapes = (
        ((256, 768), BF16),
        ((256, 2304), BF16),
        ((1536, 256), BF16),
        ((12, 256, 256), BF16),
        ((256, 768), BF16),
        ((256, 768), F32),
        ((256, 768), BF16),
        ((256, 3072), BF16),
        ((3, 256, 1024), F32),
    )
    return pl.pallas_call(
        encoder_forward_kernel,
        out_shape=(jax.ShapeDtypeStruct((256, 768), BF16), jax.ShapeDtypeStruct((16, 1024), F32))
        + tuple(jax.ShapeDtypeStruct(*shape) for shape in shapes),
        in_specs=[smem_spec()] + [vmem_spec()] * 4 + [any_spec()] * 5,
        out_specs=(vmem_spec(),) * 2 + (any_spec(),) * len(shapes),
        scratch_shapes=[pltpu.VMEM(*shape) for shape in shapes]
        + [
            pltpu.VMEM((256, 768), F32),
            pltpu.VMEM(attend.shape, BF16),
            pltpu.VMEM(merging.shape, BF16),
            pltpu.VMEM(expand.shape, BF16),
            pltpu.VMEM(shrink.shape, BF16),
            pltpu.VMEM((768, 256), F32),
            pltpu.SemaphoreType.DMA((11,)),
            pltpu.SemaphoreType.DMA((len(shapes),)),
        ],
        compiler_params=pltpu.CompilerParams(vmem_limit_bytes=60 * 2**20),
        name="encoder_forward",
    )(sizes, gains, shifts, biases, inner[None], tokens, attend, merging, expand, shrink)


def decoder_kernel(
    reduce, sizes, distance, slots, frequency, sent, biases, mask_token, gains, shifts, inner,
    cotangent, entry_far, attend_far, merging_far, expand_far, shrink_far,
    summed, rest, vectors, encoded_grad, *refs,
):
    (
        table, start, normed, mixed, turned, probs, flipped, context, normed_two, active,
        before_grad, go_low, attention_low, context_grad, delta, mixed_grad, target, masked_keys,
        entry_weight, attend, merging, expand, shrink, load_sem,
    ) = refs[:24]
    pack = lax.axis_index("section")
    if reduce:
        mine, partner = neighbours()
        greet(partner)
        engine = reducer(DECODER_CHUNKS, DECODER_CHUNKS, mine, partner, summed, refs[24:])
        put = engine.put
    else:
        put = put_into(summed)
    put_rest = put_into(rest)
    loads = fetch(
        [
            (entry_far, entry_weight),
            (attend_far, attend),
            (cotangent.at[pack], target),
            (merging_far, merging),
            (expand_far, expand),
            (shrink_far, shrink),
        ],
        load_sem,
    )
    tiles = start.shape[0] // TILE
    vectors[...] = jnp.zeros_like(vectors)
    large = sizes[pack, 0] == 1024

    def add_row(row, value):
        vectors[row : row + 1, :] += value

    positions = iota((32, 128), 0).astype(F32)
    for chip in range(4):
        spacing = distance[pack, chip].astype(F32) / 16.0
        angle = positions * (spacing * frequency[...])
        table[0, chip] = jnp.sin(angle)
        table[1, chip] = jnp.cos(angle)
    loads[0].wait()
    entry = low(dot(sent[...], entry_weight[...]) + biases[0:1])
    loads[1].wait()

    blocks = start.shape[0] // BLOCK

    def slot_chip(tile, size):
        return chip_of(iota((size, 1), 0) + tile * size, sizes, pack)

    def validity(tile, size):
        return (slot_chip(tile, size) < 4).astype(F32)

    def spread_of(tile):
        return (slots[pl.ds(pack, 1)] == iota((TILE, TILE), 0) + tile * TILE).astype(F32)

    def encoding_of(tile):
        pieces = []
        for kind in range(2):
            wave = table[kind, 0, aligned(tile * 8, 8, 8)]
            big = jnp.broadcast_to(wave[:, None], (8, 32, 128)).reshape(TILE, 128)
            wave = table[kind, tile, 0:16]
            own = jnp.broadcast_to(wave[:, None], (16, 16, 128)).reshape(TILE, 128)
            pieces.append(jnp.where(large, big, own))
        for kind in range(2):
            wave = table[kind, 0]
            big = jnp.broadcast_to(wave[None], (8, 32, 128)).reshape(TILE, 128)
            wave = table[kind, tile, 0:16]
            own = jnp.broadcast_to(wave[None], (16, 16, 128)).reshape(TILE, 128)
            pieces.append(jnp.where(large, big, own))
        return jnp.concatenate(pieces, axis=1)

    @pl.loop(0, tiles)
    def _(tile):
        rows = rows_of(tile)
        valid = validity(tile, TILE)
        spread = spread_of(tile)
        fill = valid * (1.0 - jnp.sum(spread, axis=1, keepdims=True))
        hidden = dot(low(spread), entry) + fill * mask_token[...] + encoding_of(tile) * valid
        start[rows] = hidden
        add_row(12, row_sum(valid * hidden * hidden))
        add_row(16, row_sum(valid))
        unit, _ = standardize(hidden)
        norm = low(unit * gains[0:1] + shifts[0:1])
        normed[rows] = norm
        mix = dot(norm, attend[...])
        mix_low = low(mix)
        mixed[rows] = mix_low
        turned[:, rows] = low(mix[:, 256:].T)
        lane = iota((TILE, 128), 1)
        other = (lane % 64 < 5) & (lane % 64 != slot_chip(tile, TILE))
        other = jnp.where(other, NEGATIVE, 0.0).astype(BF16)
        for head in range(4):
            lanes = slice(256 + head // 2 * 128, 384 + head // 2 * 128)
            masked_keys[head, rows] = jnp.where(lane // 64 == head % 2, mix_low[:, lanes], other)

    @pl.loop(0, 2 * tiles)
    def _(step):
        pair, tile = step // tiles, step % tiles
        rows = rows_of(tile)
        lane = iota((TILE, 128), 1)
        chosen = (lane % 64 == slot_chip(tile, TILE)).astype(F32).astype(BF16)
        for half in range(2):
            query = jnp.where(lane // 64 == half, mixed[rows, pair_lanes(pair)] * BF16(0.125), chosen)
            scores = dot_nt(masked_keys[pair * 2 + half], query)
            expos = jnp.exp(scores - jnp.max(scores, axis=0, keepdims=True))
            prob = low(expos * (1.0 / jnp.sum(expos, axis=0, keepdims=True)))
            probs[pair * 2 + half, :, rows] = prob
            flipped[head_rows(pair, half), rows] = dot(turned[head_rows(pair, half, 256)], prob)

    for copy in loads[2:]:
        copy.wait()

    @pl.loop(0, blocks)
    def _(tile):
        rows = rows_of(tile, BLOCK)
        valid = validity(tile, BLOCK)
        mingled_wide = flipped[:, rows].T
        mingled = low(mingled_wide)
        context[rows] = mingled
        attention = dot(mingled, merging[...]) + biases[1:2]
        add_row(13, row_sum(valid * attention * attention))
        center = start[rows] + attention
        unit, inverse = standardize(center)
        norm = low(unit * gains[1:2] + shifts[1:2])
        normed_two[rows] = norm
        go = target[rows] * valid
        go_below = low(go)
        go_low[rows] = go_below
        add_row(2, row_sum(go))
        feed = jnp.zeros_like(go)
        norm_grad = jnp.zeros_like(go)
        for part in range(8):
            cols = slice(part * 256, part * 256 + 256)
            before = dot(norm, expand[:, cols]) + inner[:, cols]
            value, slope = gelu_pair(before)
            value = low(value)
            active[rows, cols] = value
            feed = feed + dot(value, shrink[cols])
            grad = low(slope * dot_nt(go_below, shrink[cols]))
            before_grad[rows, cols] = grad
            lanes = slice(part % 2 * 256, part % 2 * 256 + 256)
            vectors[8 + part // 2 : 9 + part // 2, lanes] += row_sum(grad.astype(F32))
            norm_grad = norm_grad + dot_nt(grad, expand[:, cols])
        feed = feed + biases[2:3]
        add_row(14, row_sum(valid * feed * feed))
        output = center + feed
        add_row(15, row_sum(valid * output * output))
        add_row(5, row_sum(norm_grad * unit))
        add_row(7, row_sum(norm_grad))
        grad = go + norm_back(unit, inverse, gains[1:2], norm_grad)
        target[rows] = grad
        add_row(1, row_sum(grad))
        below = low(grad)
        attention_low[rows] = below
        outer = low(dot_nt(below, merging[...]))
        context_grad[rows] = outer
        product = (outer.astype(F32) * mingled_wide).T
        for head in range(4):
            delta[head, :, rows] = row_sum(product[head * 64 : head * 64 + 64])

    for part in range(2):
        cols = slice(part * 256, part * 256 + 256)
        store_packed(put, part * 16, DECODER_EXPAND, dot_tn(normed_two[:, cols], before_grad[...]))
        value = dot_tn(attention_low[:, cols], context[...])
        store_packed(put, part * 16, DECODER_MERGE, value)
    for block in range(2):
        put(slice(block * 16, block * 16 + 16), 4352, jnp.zeros((16, 16, 256), F32))
    if reduce:
        await_greetings()
        engine.send(0)

    @pl.loop(0, 8)
    def _(part):
        cols = aligned(part * 256, 256, 256)
        store_packed(put, part * 4, DECODER_SHRINK, dot_tn(active[:, cols], go_low[...]))

    if reduce:
        engine.send(1)
        engine.send(2)

    flipped[...] = jnp.zeros_like(flipped)

    @pl.loop(0, 2 * tiles)
    def _(step):
        pair, tile = step // tiles, step % tiles
        rows = rows_of(tile)
        lanes = pair_lanes(pair)
        values = mixed[rows, pair_lanes(pair, 512)]
        raws, probabilities, queries, outers = [], [], [], []
        for half in range(2):
            prob = probs[pair * 2 + half, rows]
            outer = only(context_grad[:, lanes], half)
            raw = low(prob.astype(F32) * (dot_nt(values, outer) - delta[pair * 2 + half]))
            flipped[head_rows(pair, half)] += dot(turned[head_rows(pair, half), rows], raw)
            raws.append(raw)
            probabilities.append(prob)
            outers.append(outer)
            queries.append(only(mixed[:, lanes], half))
        key_grad = dot(jnp.concatenate(raws, axis=1), jnp.concatenate(queries, axis=0))
        mixed_grad[rows, pair_lanes(pair, 256)] = low(key_grad * 0.125)
        value_grad = dot(jnp.concatenate(probabilities, axis=1), jnp.concatenate(outers, axis=0))
        mixed_grad[rows, pair_lanes(pair, 512)] = low(value_grad)
        if reduce:
            engine.turn(step)

    def last(tile, entry_grad):
        rows = rows_of(tile)
        mixed_grad[rows, 0:256] = low(flipped[:, rows].T * 0.125)
        norm_grad = dot_nt(mixed_grad[rows], attend[...])
        unit, inverse = standardize(start[rows])
        add_row(4, row_sum(norm_grad * unit))
        add_row(6, row_sum(norm_grad))
        grad = target[rows] + norm_back(unit, inverse, gains[0:1], norm_grad)
        spread = spread_of(tile)
        fill = validity(tile, TILE) * (1.0 - jnp.sum(spread, axis=1, keepdims=True))
        add_row(3, row_sum(fill * grad))
        if reduce:
            engine.turn(2 * tiles + tile)
        return entry_grad + dot_tn(low(spread), low(grad))

    entry_grad = lax.fori_loop(0, tiles, last, jnp.zeros((TILE, 512), F32))
    add_row(0, row_sum(entry_grad))
    entry_low = low(entry_grad)
    encoded_grad[...] = low(dot_nt(entry_low, entry_weight[...]))
    store_packed(put_rest, 0, ENTRY, dot_tn(sent[...], entry_low))
    for part in range(2):
        if reduce:
            engine.turn(3 * tiles + part)
        cols = slice(part * 256, part * 256 + 256)
        value = dot_tn(normed[:, cols], mixed_grad[...])
        store_packed(put_rest, part * 16, DECODER_ATTEND, value)
    if reduce:
        engine.close(0)


def decoder_call(
    reduce, sizes, distance, slots, sent, cotangent, entry_weight, biases, mask_token,
    gains, shifts, attend, merging, expand, inner, shrink,
):
    length = cotangent.shape[1]
    width = 512
    frequency = np.exp(-np.log(10000.0) * np.arange(width // 4) / (width // 4)).astype(np.float32)
    if reduce:
        summed = jax.ShapeDtypeStruct((DECODER_CHUNKS, 16, SPAN), F32)
        extra = reducer_scratch(DECODER_CHUNKS, DECODER_CHUNKS)
        params = dict(collective_id=1, has_side_effects=True)
    else:
        summed = jax.ShapeDtypeStruct((DECODER_CHUNKS, 2, 16, 16, SPAN), BF16)
        extra = []
        params = dict()
    return pl.pallas_call(
        functools.partial(decoder_kernel, reduce),
        out_shape=(
            summed,
            jax.ShapeDtypeStruct((2, 2, 16, 16, SPAN), BF16),
            jax.ShapeDtypeStruct((24, width), F32),
            jax.ShapeDtypeStruct((256, 768), BF16),
        ),
        in_specs=[smem_spec()] * 2 + [vmem_spec()] * 8 + [any_spec()] * 6,
        out_specs=(vmem_spec(),) * 4,
        scratch_shapes=[
            pltpu.VMEM((2, 4, 32, 128), F32),
            pltpu.VMEM((length, width), F32),
            pltpu.VMEM((length, width), BF16),
            pltpu.VMEM((length, 768), BF16),
            pltpu.VMEM((512, length), BF16),
            pltpu.VMEM((4, length, length), BF16),
            pltpu.VMEM((256, length), F32),
            pltpu.VMEM((length, 256), BF16),
            pltpu.VMEM((length, width), BF16),
            pltpu.VMEM((length, 2048), BF16),
            pltpu.VMEM((length, 2048), BF16),
            pltpu.VMEM((length, width), BF16),
            pltpu.VMEM((length, width), BF16),
            pltpu.VMEM((length, 256), BF16),
            pltpu.VMEM((4, 1, length), F32),
            pltpu.VMEM((length, 768), BF16),
            pltpu.VMEM((length, width), F32),
            pltpu.VMEM((4, length, 128), BF16),
            pltpu.VMEM(entry_weight.shape, BF16),
            pltpu.VMEM(attend.shape, BF16),
            pltpu.VMEM(merging.shape, BF16),
            pltpu.VMEM(expand.shape, BF16),
            pltpu.VMEM(shrink.shape, BF16),
            pltpu.SemaphoreType.DMA((6,)),
        ]
        + extra,
        compiler_params=pltpu.CompilerParams(vmem_limit_bytes=63 * 2**20, **params),
        name="decoder_block",
    )(
        sizes, distance, slots, jnp.asarray(frequency)[None], sent, biases, mask_token[None], gains, shifts,
        inner[None], cotangent, entry_weight, attend, merging, expand, shrink,
    )


def encoder_backward_kernel(
    reduce, encoded_grad, sums, decoder_vectors, gains, tokens, rest, attend_far, merging_far, expand_far,
    shrink_far, normed_far, mixed_far, turned_far, probs_far, context_far, middle_far, normed_two_far, active_far,
    slope_far, summed, vectors, tokens_grad, *refs,
):
    if reduce:
        decoder_sums, arrived = refs[:2]
        refs = refs[2:]
    (
        hidden, attend, merging, expand, shrink, normed, mixed, turned, probs, context, middle, normed_two, active,
        slope, before_grad, norm_sum, attention_low, context_grad, key_grad, query_turned, mixed_grad, active_turned,
        flipped, load_sem, part_sem,
    ) = refs[:25]
    pack = lax.axis_index("section")

    def part_loads(part):
        cols = slice(part * 1024, part * 1024 + 1024)
        slot = part % 2
        return [
            pltpu.make_async_copy(expand_far.at[:, cols], expand.at[slot], part_sem.at[slot, 0]),
            pltpu.make_async_copy(shrink_far.at[cols], shrink.at[slot], part_sem.at[slot, 1]),
            pltpu.make_async_copy(slope_far.at[part], slope.at[slot], part_sem.at[slot, 2]),
        ]

    if reduce:
        (
            decoder_total, encoder_total, decoder_got, encoder_got, payload,
            own_sem, small_send, small_recv, pay_send, pay_recv, small_load,
        ) = refs[25:36]
        mine, partner = neighbours()
        greet(partner)
        engine = reducer(CHUNKS, STAGING, mine, partner, summed, refs[36:])
        put = engine.put
        first_own = [
            pltpu.make_async_copy(rest.at[chunk, mine["c"]], engine.own.at[chunk], own_sem.at[chunk])
            for chunk in range(2)
        ]
        for copy in first_own:
            copy.start()
        decoder_load = pltpu.make_async_copy(decoder_vectors, decoder_total.at[0], small_load)
        decoder_load.start()
    else:
        put = put_into(summed)
    early = pltpu.make_async_copy(active_far, active, load_sem.at[10])
    early.start()
    for copy in part_loads(0):
        copy.start()
    if reduce:
        await_greetings()
        for chunk in range(2):
            engine.first_copy(chunk, rest.at[chunk, 1 - mine["c"]]).start()
    loads = fetch(
        [
            (normed_two_far, normed_two),
            (middle_far, middle),
            (merging_far, merging),
            (context_far, context),
            (mixed_far, mixed),
            (probs_far, probs),
            (turned_far.at[0:768], turned),
            (normed_far, normed),
            (attend_far, attend),
            (tokens.at[pack], hidden),
        ],
        load_sem,
    )
    for copy in part_loads(1):
        copy.start()
    vectors[...] = sums[...]
    go_low = encoded_grad[...]
    go = go_low.astype(F32)
    vectors[1:2, :768] = row_sum(go)
    norm_sum[...] = jnp.zeros_like(norm_sum)

    def send(unit):
        if reduce:
            engine.send(unit)

    def release(unit):
        if reduce:
            engine.release(unit)

    def shrink_start():
        early.wait()
        for piece in range(4):
            rows = slice(piece * 768, piece * 768 + 768)
            active_turned[rows] = active[:, rows].T

    def shrink_grad(part):
        release(1 + part)
        cols = slice(part * 256, part * 256 + 256)
        for piece in range(4):
            rows = slice(piece * 768, piece * 768 + 768)
            store_packed(put, piece * 8, ENCODER_SHRINK[part], dot(active_turned[rows], encoded_grad[:, cols]))
        send(1 + part)

    def hidden_layer(part):
        for copy in part_loads(part):
            copy.wait()
        slot = part % 2
        grad = low(slope[slot] * dot_nt(encoded_grad[...], shrink[slot]))
        before_grad[...] = grad
        vectors[6 + part : 7 + part] = row_sum(grad.astype(F32))
        norm_sum[...] += dot_nt(grad, expand[slot])
        if part == 0:
            for copy in part_loads(2):
                copy.start()

    def expand_grad(part):
        release(4 + part)
        if part == 0:
            loads[0].wait()
            flipped[...] = normed_two[...].T
        store_packed(put, 0, ENCODER_EXPAND[part], dot(flipped[...], before_grad[...]))
        send(4 + part)

    def middle_layer():
        loads[1].wait()
        loads[2].wait()
        unit, inverse = standardize(middle[...])
        norm_grad = norm_sum[...]
        vectors[3:4, :768] = row_sum(norm_grad * unit)
        vectors[5:6, :768] = row_sum(norm_grad)
        grad = encoded_grad[...].astype(F32) + norm_back(unit, inverse, gains[1:2], norm_grad)
        vectors[0:1, :768] = row_sum(grad)
        tokens_grad[...] = grad
        below = low(grad)
        attention_low[...] = below
        context_grad[...] = low(dot_nt(below, merging[...]))
        for copy in loads[3:7]:
            copy.wait()

    def attention(first):
        @pl.loop(first, first + 2)
        def _(pair):
            lanes = pair_lanes(pair)
            values = mixed[:, pair_lanes(pair, 1536)]
            keys_total = jnp.zeros((TILE, 128), F32)
            values_total = jnp.zeros((TILE, 128), F32)
            for half in range(2):
                prob = probs[pair * 2 + half]
                outer = only(context_grad[:, lanes], half)
                query = only(mixed[:, lanes], half)
                wide = prob.astype(F32)
                grad = dot_nt(values, outer)
                raw = low(wide * (grad - jnp.sum(wide * grad, axis=0, keepdims=True)))
                keys_total = keys_total + dot(raw, query)
                values_total = values_total + dot(prob, outer)
                rows = head_rows(pair, half)
                query_turned[rows] = dot(turned[rows], raw)
            key_grad[0, :, lanes] = keys_total
            key_grad[1, :, lanes] = values_total

    def mixing():
        mixed_grad[:, 0:768] = low(query_turned[...].T * 0.125)
        mixed_grad[:, 768:1536] = low(key_grad[0] * 0.125)
        mixed_grad[:, 1536:2304] = low(key_grad[1])

    def attend_grad(part):
        if part == 0:
            loads[7].wait()
            flipped[...] = normed[...].T
        release(7 + part)
        wide = slice(part * 1024, min(part * 1024 + 1024, 2304))
        store_packed(put, 0, ENCODER_ATTEND[part], dot(flipped[...], mixed_grad[:, wide]))
        if part == 2:
            store_packed(put, 0, ENCODER_MERGE, dot_tn(attention_low[...], context[...]))
        send(7 + part)

    def input_layer():
        loads[8].wait()
        loads[9].wait()
        norm_grad = dot_nt(mixed_grad[...], attend[...])
        unit, inverse = standardize(hidden[...])
        vectors[2:3, :768] = row_sum(norm_grad * unit)
        vectors[4:5, :768] = row_sum(norm_grad)
        grad = tokens_grad[...] + norm_back(unit, inverse, gains[0:1], norm_grad)
        tokens_grad[...] = grad
        if reduce:
            payload[...] = low(grad)

    if not reduce:
        shrink_start()
        for part in range(3):
            shrink_grad(part)
        for part in range(3):
            hidden_layer(part)
            expand_grad(part)
        middle_layer()
        for first in (0, 2, 4):
            attention(first)
        mixing()
        for part in range(3):
            attend_grad(part)
        input_layer()
        return

    def exchange(source, piece):
        rows = aligned(piece * 32, 32, 32)
        return remote(source.at[rows], arrived.at[rows], pay_send.at[piece], pay_recv.at[piece], partner["x"])

    small_route = ("c",) + ROUTES[0]
    totals = ((decoder_total, decoder_got), (encoder_total, encoder_got))

    def small_copy(stage, kind):
        source, target = totals[kind]
        return remote(
            source.at[stage],
            target.at[stage],
            small_send.at[stage, kind],
            small_recv.at[stage, kind],
            partner[small_route[stage]],
        )

    def small_advance(stage):
        if stage == 0:
            encoder_total[0] = vectors[...]
        for kind in range(2):
            source, target = totals[kind]
            if stage > 0:
                small_copy(stage - 1, kind).wait_recv()
                source[stage] = source[stage - 1] + target[stage - 1]
            if stage < 5:
                small_copy(stage, kind).start()

    shrink_start()
    shrink_grad(0)
    for copy in first_own:
        copy.wait()
    decoder_load.wait()

    def attention_end():
        attention(4)
        mixing()

    part = functools.partial
    works = [part(shrink_grad, 1), part(shrink_grad, 2)]
    for number in range(3):
        works += [part(hidden_layer, number), part(expand_grad, number)]
    works += [middle_layer, part(attention, 0), part(attention, 2), attention_end]
    works += [input_layer] + [part(attend_grad, number) for number in range(3)]
    works = dict(enumerate(works))
    turns = CHUNKS + 4 * LAG
    works.update({turns - 11 + 2 * stage: part(small_advance, stage) for stage in range(6)})

    @pl.loop(0, turns)
    def _(number):
        engine.turn(number)
        for position, work in works.items():
            pl.when(number == position)(work)

        piece = number // 2

        @pl.when((pack == 0) & (number % 2 == 0) & (piece < 8))
        def _():
            exchange(encoded_grad, piece).start()

        @pl.when((pack == 1) & (number % 2 == 0) & (piece >= 6))
        def _():
            exchange(payload, piece - 6).start()

    for stage in range(5):
        for kind in range(2):
            small_copy(stage, kind).wait_send()
    for piece in range(8):
        exchange(payload, piece).wait()
    engine.close(CHUNKS - STAGING)
    vectors[...] = encoder_total[5]
    decoder_sums[...] = decoder_total[5]


def encoder_backward_call(reduce, tokens, encoded_grad, sums, decoder_vectors, rest, kept, gains, attend, merging, expand, shrink):
    if reduce:
        summed = jax.ShapeDtypeStruct((CHUNKS, 16, SPAN), F32)
        more = (
            jax.ShapeDtypeStruct(decoder_vectors.shape, F32),
            jax.ShapeDtypeStruct((256, 768), BF16),
        )
        more_specs = (vmem_spec(), any_spec())
        extra = [
            pltpu.VMEM((6,) + decoder_vectors.shape, F32),
            pltpu.VMEM((6,) + sums.shape, F32),
            pltpu.VMEM((5,) + decoder_vectors.shape, F32),
            pltpu.VMEM((5,) + sums.shape, F32),
            pltpu.VMEM((256, 768), BF16),
            pltpu.SemaphoreType.DMA((2,)),
            pltpu.SemaphoreType.DMA((5, 2)),
            pltpu.SemaphoreType.DMA((5, 2)),
            pltpu.SemaphoreType.DMA((8,)),
            pltpu.SemaphoreType.DMA((8,)),
            pltpu.SemaphoreType.DMA,
        ] + reducer_scratch(CHUNKS, STAGING)
        params = dict(collective_id=2, has_side_effects=True)
    else:
        summed = jax.ShapeDtypeStruct((CHUNKS, 2, 16, 16, SPAN), BF16)
        more, more_specs, extra, params = (), (), [], dict()
    return pl.pallas_call(
        functools.partial(encoder_backward_kernel, reduce),
        out_shape=(
            summed,
            jax.ShapeDtypeStruct(sums.shape, F32),
            jax.ShapeDtypeStruct((256, 768), F32),
        )
        + more,
        in_specs=[vmem_spec()] * 2 + [any_spec(), vmem_spec()] + [any_spec()] * 15,
        out_specs=(vmem_spec(),) * 3 + more_specs,
        scratch_shapes=[
            pltpu.VMEM((256, 768), F32),
            pltpu.VMEM(attend.shape, BF16),
            pltpu.VMEM(merging.shape, BF16),
            pltpu.VMEM((2, 768, 1024), BF16),
            pltpu.VMEM((2, 1024, 768), BF16),
            pltpu.VMEM((256, 768), BF16),
            pltpu.VMEM((256, 2304), BF16),
            pltpu.VMEM((768, 256), BF16),
            pltpu.VMEM((12, 256, 256), BF16),
            pltpu.VMEM((256, 768), BF16),
            pltpu.VMEM((256, 768), F32),
            pltpu.VMEM((256, 768), BF16),
            pltpu.VMEM((256, 3072), BF16),
            pltpu.VMEM((2, 256, 1024), F32),
            pltpu.VMEM((256, 1024), BF16),
            pltpu.VMEM((256, 768), F32),
            pltpu.VMEM((256, 768), BF16),
            pltpu.VMEM((256, 768), BF16),
            pltpu.VMEM((2, 256, 768), F32),
            pltpu.VMEM((768, 256), F32),
            pltpu.VMEM((256, 2304), BF16),
            pltpu.VMEM((3072, 256), BF16),
            pltpu.VMEM((768, 256), BF16),
            pltpu.SemaphoreType.DMA((11,)),
            pltpu.SemaphoreType.DMA((2, 3)),
        ]
        + extra,
        compiler_params=pltpu.CompilerParams(vmem_limit_bytes=60 * 2**20, **params),
        name="encoder_backward",
    )(encoded_grad, sums, decoder_vectors, gains, tokens, rest, attend, merging, expand, shrink, *kept)


def unpack(packed, place):
    def take(start, size):
        pieces = []
        while size:
            chunk, first = divmod(start, SPAN)
            length = min(size, SPAN - first)
            pieces.append(packed[chunk, ..., first : first + length])
            start, size = start + length, size - length
        return pieces[0] if len(pieces) == 1 else jnp.concatenate(pieces, axis=-1)

    offset, count, width = place
    pieces = [take(offset + i * width, width) for i in range(count // 16)]
    if count % 16:
        rest = take(offset + count // 16 * width, width // 2)
        pieces.append(jnp.concatenate([rest[..., :8, :], rest[..., 8:, :]], axis=-1))
    return pieces[0] if len(pieces) == 1 else jnp.concatenate(pieces, axis=-2)


def finish_kernel(
    decoder_summed_far, decoder_sums_far, encoder_sums_far, summed_far, arrived_far, tokens_grad_far, encoded_grad_far,
    boundary, statistics, e_gains, e_shifts, e_biases, e_attend, e_merge, e_expand, e_inner, e_shrink,
    d_entry, d_biases, mask_grad, d_gains, d_shifts, d_attend, d_merge, d_expand, d_inner, d_shrink,
    decoder_summed, decoder_sums, encoder_sums, summed, arrived, tokens_grad, encoded_grad, load_sem,
):
    section = lax.axis_index("section")
    loads = fetch(
        [
            (decoder_summed_far, decoder_summed),
            (decoder_sums_far, decoder_sums),
            (encoder_sums_far, encoder_sums),
            (summed_far, summed),
            (arrived_far, arrived),
            (tokens_grad_far, tokens_grad),
            (encoded_grad_far, encoded_grad),
        ],
        load_sem,
    )
    number = section * lax.axis_size("dp") + lax.axis_index("dp")

    def own(rows, count):
        width = rows.shape[1]
        return pltpu.roll(rows, (width - number * count) % width, axis=1)[:, :count]

    def own_line(rows, count):
        return own(jnp.concatenate([rows[i : i + 1] for i in range(rows.shape[0])], axis=1), count)

    for copy in loads[:3]:
        copy.wait()
    lane = iota((1, 128), 1)
    values = jnp.zeros((1, 128), F32)
    for sums, width, first, count_row, base in ((encoder_sums, DE, 10, 14, 0), (decoder_sums, DD, 12, 16, 4)):
        scale = 1.0 / (sums[count_row : count_row + 1, 0:1] * width)
        for i in range(4):
            value = jnp.sum(sums[first + i : first + i + 1, :], axis=1, keepdims=True) * scale
            values = jnp.where(lane == base + i, value, values)
    statistics[...] = jnp.sqrt(values)[:, :8]
    rows = own(encoder_sums[0:8, :DE], 24)
    e_biases[...] = rows[0:2]
    e_gains[...] = rows[2:4]
    e_shifts[...] = rows[4:6]
    e_inner[...] = own_line(encoder_sums[6:9], 96)
    rows = own(decoder_sums[0:8], 16)
    d_biases[...] = rows[0:3]
    mask_grad[...] = rows[3:4]
    d_gains[...] = rows[4:6]
    d_shifts[...] = rows[6:8]
    d_inner[...] = own_line(decoder_sums[8:12], 64)

    d_merge[...] = unpack(decoder_summed, DECODER_MERGE)
    d_expand[...] = unpack(decoder_summed, DECODER_EXPAND)
    d_shrink[...] = unpack(decoder_summed, DECODER_SHRINK)
    loads[3].wait()
    d_entry[...] = unpack(summed, ENTRY)
    d_attend[...] = unpack(summed, DECODER_ATTEND)
    for target, places in ((e_expand, ENCODER_EXPAND), (e_attend, ENCODER_ATTEND), (e_shrink, ENCODER_SHRINK)):
        start = 0
        for place in places:
            target[:, start : start + place[2]] = unpack(summed, place)
            start += place[2]
    e_merge[...] = unpack(summed, ENCODER_MERGE)
    for copy in loads[4:]:
        copy.wait()

    @pl.when(section == 0)
    def _():
        boundary[0, 0] = tokens_grad[...]
        boundary[0, 1] = arrived[...].astype(F32)

    @pl.when(section == 1)
    def _():
        boundary[0, 0] = arrived[...].astype(F32)
        boundary[0, 1] = encoded_grad[...].astype(F32)


def finish_call(*operands):
    shapes = (
        (1, 2, 256, 768), (1, 8), (2, 24), (2, 24), (2, 24), (24, 2304), (24, 768), (24, 3072), (1, 96), (96, 768),
        (24, 512), (3, 16), (1, 16), (2, 16), (2, 16), (16, 768), (16, 256), (16, 2048), (1, 64), (64, 512),
    )
    outs = list(
        pl.pallas_call(
            finish_kernel,
            out_shape=tuple(jax.ShapeDtypeStruct(shape, F32) for shape in shapes),
            in_specs=[any_spec()] * len(operands),
            out_specs=(vmem_spec(),) * len(shapes),
            scratch_shapes=[pltpu.VMEM(operand.shape, operand.dtype) for operand in operands]
            + [pltpu.SemaphoreType.DMA((len(operands),))],
            compiler_params=pltpu.CompilerParams(vmem_limit_bytes=60 * 2**20),
            name="finish",
        )(*operands)
    )
    for line in (1, 8, 12, 18):
        outs[line] = outs[line].reshape(-1)
    for turned in (6, 16):
        outs[turned] = outs[turned].T
    return tuple(outs)


def scatter_sum(member, share_dim):
    return lax.psum_scatter(
        member, ("section", "dp"), scatter_dimension=share_dim, tiled=True
    )


def finish_generic(decoder_part, part, decoder_sums, encoder_sums, tokens_grad, encoded_grad):
    section = lax.axis_index("section")
    payload = jnp.where(section == 0, encoded_grad, low(tokens_grad))

    def whole(packed, *places):
        packed = jnp.swapaxes(packed, 1, 2).reshape(-1, 32, 16, SPAN)
        blocks = [unpack(packed, place).reshape(32 * place[1], place[2]) for place in places]
        return scatter_sum(jnp.concatenate(blocks, axis=1).astype(F32), 0)

    def line(value):
        return scatter_sum(value, value.ndim - 1)

    arrived = lax.ppermute(payload, "section", [(0, 1), (1, 0)]).astype(F32)
    boundary = jnp.where(
        section == 0,
        jnp.stack([tokens_grad, arrived]),
        jnp.stack([arrived, encoded_grad.astype(F32)]),
    )
    sums = jnp.concatenate(
        [jnp.sum(encoder_sums[10:14], axis=1), jnp.sum(decoder_sums[12:16], axis=1)]
    )
    sums, counts = lax.psum((sums, (encoder_sums[14, 0], decoder_sums[16, 0])), ("section", "dp"))
    scales = jnp.concatenate([jnp.full((4,), counts[0] * DE), jnp.full((4,), counts[1] * DD)])
    return (
        boundary[None],
        jnp.sqrt(sums / scales),
        line(encoder_sums[2:4, :DE]),
        line(encoder_sums[4:6, :DE]),
        line(encoder_sums[0:2, :DE]),
        whole(part, *ENCODER_ATTEND),
        whole(part, ENCODER_MERGE).T,
        whole(part, *ENCODER_EXPAND),
        line(encoder_sums[6:9].reshape(-1)),
        whole(part, *ENCODER_SHRINK),
        whole(decoder_part[1], ENTRY),
        line(decoder_sums[0:3]),
        line(decoder_sums[3]),
        line(decoder_sums[4:6]),
        line(decoder_sums[6:8]),
        whole(decoder_part[1], DECODER_ATTEND),
        whole(decoder_part[0], DECODER_MERGE).T,
        whole(decoder_part[0], DECODER_EXPAND),
        line(decoder_sums[8:12].reshape(-1)),
        whole(decoder_part[0], DECODER_SHRINK),
    )


def body(
    visible_tokens,
    cotangent,
    chip_sizes,
    ground_distance,
    visible_slots,
    encoder_gains,
    encoder_shifts,
    encoder_biases,
    encoder_attend,
    encoder_merge,
    encoder_expand,
    encoder_inner,
    encoder_shrink,
    decoder_entry,
    decoder_biases,
    mask_token,
    decoder_gains,
    decoder_shifts,
    decoder_attend,
    decoder_merge,
    decoder_widen_weight,
    decoder_inner,
    decoder_shrink,
):
    reduce = (lax.axis_size("section"), lax.axis_size("dp")) == (2, 16)
    sent, sums, *kept = encoder_forward_call(
        chip_sizes, visible_tokens, encoder_gains, encoder_shifts, encoder_biases,
        encoder_attend, encoder_merge, encoder_expand, encoder_inner, encoder_shrink,
    )
    decoder_summed, rest, decoder_vectors, encoded_grad = decoder_call(
        reduce, chip_sizes, ground_distance, visible_slots, sent, cotangent, decoder_entry, decoder_biases, mask_token,
        decoder_gains, decoder_shifts, decoder_attend, decoder_merge, decoder_widen_weight, decoder_inner,
        decoder_shrink,
    )
    summed, encoder_sums, tokens_grad, *more = encoder_backward_call(
        reduce, visible_tokens, encoded_grad, sums, decoder_vectors, rest, kept,
        encoder_gains, encoder_attend, encoder_merge, encoder_expand, encoder_shrink,
    )
    if reduce:
        decoder_sums, arrived = more
        return finish_call(
            decoder_summed, decoder_sums, encoder_sums, summed, arrived, tokens_grad, encoded_grad
        )
    return finish_generic(
        (decoder_summed, rest), summed, decoder_vectors, encoder_sums, tokens_grad, encoded_grad
    )


def solution(mesh):
    in_specs = (
        P("dp", None, None),
        P("dp", None, None),
        P("dp", None),
        P("dp", None),
        P("dp", None),
        P(),
        P(),
        P(),
        P(),
        P(),
        P(),
        P(),
        P(),
        P(),
        P(),
        P(),
        P(),
        P(),
        P(),
        P(),
        P(),
        P(),
        P(),
    )
    out_specs = (
        P("section", "dp", None, None),
        P(),
        P(None, ("section", "dp")),
        P(None, ("section", "dp")),
        P(None, ("section", "dp")),
        P(("section", "dp"), None),
        P(None, ("section", "dp")),
        P(("section", "dp"), None),
        P(("section", "dp")),
        P(("section", "dp"), None),
        P(("section", "dp"), None),
        P(None, ("section", "dp")),
        P(("section", "dp")),
        P(None, ("section", "dp")),
        P(None, ("section", "dp")),
        P(("section", "dp"), None),
        P(None, ("section", "dp")),
        P(("section", "dp"), None),
        P(("section", "dp")),
        P(("section", "dp"), None),
    )
    return jax.shard_map(body, mesh=mesh, in_specs=in_specs, out_specs=out_specs, check_vma=False)
```

```python
import functools
import types

import jax
import jax.numpy as jnp
import numpy as np
from jax import lax
from jax.experimental import pallas as pl
from jax.experimental.pallas import tpu as pltpu
from jax.sharding import PartitionSpec as P

DE = 768
DD = 512
TILE = 256
BLOCK = 512
NEGATIVE = -1e30
F32, BF16 = jnp.float32, jnp.bfloat16
MESH_ID = pl.DeviceIdType.MESH

CANON = ("x", "z2", "z1", "y")
ROUTES = (("x", "y", "z1", "z2"), ("y", "x", "z1", "z2"), ("z1", "z2", "x", "y"))
WIDTHS = (2, 2, 1)
OFFSETS = (0, 2, 4)
SPAN = 128 * sum(WIDTHS)
UNIT = 1536
DECODER_CHUNKS = 7
CHUNKS = 24
RING = 3
STAGING = 8
REST_CHUNKS = 3
LAG = 2

DECODER_EXPAND, DECODER_SHRINK, DECODER_MERGE = (0, 16, 2048), (2048, 64, 512), (4096, 16, 256)
ENTRY, DECODER_ATTEND = (0, 24, 512), (768, 16, 768)
ENCODER_SHRINK = tuple((UNIT * (1 + part), 96, 256) for part in range(3))
ENCODER_EXPAND = tuple((UNIT * (4 + part), 24, 1024) for part in range(3))
ENCODER_ATTEND = ((UNIT * 7, 24, 1024), (UNIT * 8, 24, 1024), (UNIT * 9, 24, 256))
ENCODER_MERGE = (UNIT * 9 + 384, 24, 768)


def dot(a, b):
    return jnp.dot(a, b, preferred_element_type=F32)


def dot_nt(a, b):
    return lax.dot_general(a, b, (((1,), (1,)), ((), ())), preferred_element_type=F32)


def dot_tn(a, b):
    return lax.dot_general(a, b, (((0,), (0,)), ((), ())), preferred_element_type=F32)


def low(value):
    return value.astype(BF16)


def standardize(values):
    centered = values - jnp.mean(values, axis=-1, keepdims=True)
    inverse = lax.rsqrt(jnp.mean(centered * centered, axis=-1, keepdims=True) + 1e-05)
    return centered * inverse, inverse


def norm_back(unit, inverse, gain, grad):
    inner = grad * gain
    return inverse * (
        inner
        - jnp.mean(inner, axis=-1, keepdims=True)
        - unit * jnp.mean(inner * unit, axis=-1, keepdims=True)
    )


def row_sum(values):
    return jnp.sum(values, axis=0, keepdims=True)


def gelu_pair(before):
    half = 0.5 * (1.0 + lax.erf(before * 0.7071067811865476))
    density = jnp.exp(-0.5 * before * before) * 0.3989422804014327
    return before * half, half + before * density


def chip_of(places, sizes, pack):
    end = sizes[pack, 0]
    chip = (places >= end).astype(jnp.int32)
    for slot in range(1, 4):
        end = end + sizes[pack, slot]
        chip = chip + (places >= end).astype(jnp.int32)
    return chip


def iota(shape, dimension):
    return lax.broadcasted_iota(jnp.int32, shape, dimension)


def aligned(start, size, unit):
    if isinstance(start, int):
        return slice(start, start + size)
    return pl.ds(pl.multiple_of(start, unit), size)


def pair_lanes(pair, base=0):
    return aligned(base + pair * 128, 128, 128)


def head_rows(pair, half, base=0):
    return aligned(base + pair * 128 + half * 64, 64, 64)


def rows_of(tile, size=TILE):
    return aligned(tile * size, size, size)


def only(values, half):
    return jnp.where(iota((1, 128), 1) // 64 == half, values, jnp.zeros_like(values))


def fetch(pairs, sems):
    copies = [
        pltpu.make_async_copy(source, target, sems.at[i]) for i, (source, target) in enumerate(pairs)
    ]
    for copy in copies:
        copy.start()
    return copies


def store_packed(put, first, place, value):
    offset, count, width = place
    value = value.reshape(-1, count, width)
    shards = slice(first, first + value.shape[0]) if isinstance(first, int) else pl.ds(first, value.shape[0])
    for piece in range(count // 16):
        put(shards, offset + piece * width, value[:, piece * 16 : piece * 16 + 16])
    if count % 16:
        half = width // 2
        rest = value[:, count - 8 :]
        rest = jnp.concatenate([rest[:, :, :half], rest[:, :, half:]], axis=1)
        put(shards, offset + count // 16 * width, rest)


def halves(shards, value):
    pairs = value.reshape(value.shape[0] // 2, 2, *value.shape[1:])
    if isinstance(shards, slice):
        return slice(shards.start // 2, shards.stop // 2), pairs[:, 0], pairs[:, 1]
    return pl.ds(shards.start // 2, shards.size // 2), pairs[:, 0], pairs[:, 1]


def place_of(names, bits):
    index = 0
    for name in names:
        index = index * 2 + bits[name]
    return index


def left_after(route, stage):
    return tuple(name for name in CANON if name not in route[:stage])


def choices(names):
    for number in range(2 ** len(names)):
        yield {name: (number >> (len(names) - 1 - i)) & 1 for i, name in enumerate(names)}


def neighbours():
    section = lax.axis_index("section")
    data = lax.axis_index("dp")
    mine = {"x": section, "c": data % 2, "y": data // 2 % 2, "z1": data // 4 % 2, "z2": data // 8 % 2}
    partner = {"x": (1 - section, data)}
    for name, step in {"c": 1, "y": 2, "z1": 4, "z2": 8}.items():
        partner[name] = (section, data + step * (1 - 2 * mine[name]))
    return mine, partner


def greet(partner):
    barrier = pltpu.get_barrier_semaphore()
    for name in ("c",) + CANON:
        pl.semaphore_signal(barrier, inc=1, device_id=partner[name], device_id_type=MESH_ID)


def await_greetings():
    pl.semaphore_wait(pltpu.get_barrier_semaphore(), 5)


def remote(source, target, send, recv, device):
    return pltpu.make_async_remote_copy(
        src_ref=source,
        dst_ref=target,
        send_sem=send,
        recv_sem=recv,
        device_id=device,
        device_id_type=MESH_ID,
    )


def reducer(chunks, slots, mine, partner, out, refs):
    progress = types.SimpleNamespace(opened=0, sent=0)
    own, staging, first = refs[:3]
    sent, got = refs[3:15], refs[15:27]
    first_send, first_recv, send_sem, recv_sem = refs[27:31]

    def first_copy(chunk):
        return remote(staging.at[chunk % slots], first.at[chunk], first_send.at[chunk], first_recv.at[chunk], partner["c"])

    def stage_copy(route, stage, chunk):
        return remote(
            sent[route * 4 + stage].at[chunk % RING],
            got[route * 4 + stage].at[chunk],
            send_sem.at[route, stage, chunk],
            recv_sem.at[route, stage, chunk],
            partner[ROUTES[route][stage]],
        )

    def total(route, stage, chunk, bits):
        spot = place_of(CANON, bits)
        cols = slice(OFFSETS[route] * 128, (OFFSETS[route] + WIDTHS[route]) * 128)
        value = own[chunk, spot, :, cols].astype(F32) + first[chunk, spot, :, cols].astype(F32)
        for earlier in range(stage):
            names = left_after(ROUTES[route], earlier + 1)
            value = value + got[route * 4 + earlier][chunk, place_of(names, bits)].astype(F32)
        return value

    def advance(stage, chunk):
        for route in range(3):
            if stage:
                stage_copy(route, stage - 1, chunk).wait_recv()
            else:
                first_copy(chunk).wait_recv() if route == 0 else None
            if stage < 4:

                @pl.when(chunk >= RING)
                def _(route=route):
                    stage_copy(route, stage, chunk - RING).wait_send()

        values = []
        for route in range(3):
            path = ROUTES[route]
            if stage == 4:
                values.append(total(route, 4, chunk, mine))
                continue
            names = left_after(path, stage + 1)
            for free in choices(names):
                bits = dict(mine)
                bits[path[stage]] = 1 - mine[path[stage]]
                bits.update(free)
                values.append((route, place_of(names, free), low(total(route, stage, chunk, bits))))
        if stage == 4:
            out[chunk] = jnp.concatenate(values, axis=1)
            return
        for route, spot, value in values:
            sent[route * 4 + stage][chunk % RING, spot] = value
        for route in range(3):
            stage_copy(route, stage, chunk).start()

    def turn(number):
        for stage in range(4, -1, -1):
            chunk = number - LAG * stage
            pl.when((chunk >= 0) & (chunk < chunks))(functools.partial(advance, stage, chunk))

    def put(shards, column, value):
        shards, even, odd = halves(shards, value)
        kept = low(jnp.where(mine["c"] == 0, even, odd))
        given = low(jnp.where(mine["c"] == 0, odd, even))
        width = value.shape[2]
        done = 0
        while done < width:
            chunk, start = divmod(column + done, SPAN)
            size = min(width - done, SPAN - start)
            own[chunk, shards, :, start : start + size] = kept[:, :, done : done + size]
            staging[chunk % slots, shards, :, start : start + size] = given[:, :, done : done + size]
            done += size

    def release(column):
        while progress.opened * SPAN < column:
            if progress.opened >= slots:
                first_copy(progress.opened - slots).wait_send()
            progress.opened += 1

    def send(column):
        while (progress.sent + 1) * SPAN <= column:
            first_copy(progress.sent).start()
            progress.sent += 1

    def close():
        for chunk in range(max(0, chunks - slots), chunks):
            first_copy(chunk).wait_send()
        for chunk in range(chunks - RING, chunks):
            for route in range(3):
                for stage in range(4):
                    stage_copy(route, stage, chunk).wait_send()

    return types.SimpleNamespace(
        own=own, staging=staging, turn=turn, put=put, release=release, send=send, close=close
    )


def reducer_scratch(chunks, slots):
    stages = [(width, block) for width in WIDTHS for block in (8, 4, 2, 1)]
    return (
        [
            pltpu.VMEM((chunks, 16, 16, SPAN), BF16),
            pltpu.VMEM((slots, 16, 16, SPAN), BF16),
            pltpu.VMEM((chunks, 16, 16, SPAN), BF16),
        ]
        + [pltpu.VMEM((RING, block, 16, width * 128), BF16) for width, block in stages]
        + [pltpu.VMEM((chunks, block, 16, width * 128), BF16) for width, block in stages]
        + [
            pltpu.SemaphoreType.DMA((chunks,)),
            pltpu.SemaphoreType.DMA((chunks,)),
            pltpu.SemaphoreType.DMA((3, 4, chunks)),
            pltpu.SemaphoreType.DMA((3, 4, chunks)),
        ]
    )


def put_into(parts):
    def put(shards, column, value):
        shards, *pair = halves(shards, value)
        width = value.shape[2]
        done = 0
        while done < width:
            chunk, start = divmod(column + done, SPAN)
            size = min(width - done, SPAN - start)
            for core in range(2):
                parts[chunk, core, shards, :, start : start + size] = low(pair[core][:, :, done : done + size])
            done += size

    return put


def vmem_spec():
    return pl.BlockSpec(memory_space=pltpu.VMEM)


def any_spec():
    return pl.BlockSpec(memory_space=pl.ANY)


def smem_spec():
    return pl.BlockSpec(memory_space=pltpu.SMEM)


def encoder_forward_kernel(
    sizes, gains, shifts, biases, inner, tokens, attend_far, merging_far, expand_far, shrink_far,
    sent, vectors, *refs,
):
    far = refs[:9]
    normed, mixed, turned, probs, context, middle, normed_two, active, slope = refs[9:18]
    hidden, attend, merging, expand, shrink, context_turned, load_sem, save_sem = refs[18:]
    pack = lax.axis_index("section")
    loads = fetch(
        [
            (tokens.at[pack], hidden),
            *[(attend_far.at[:, i * 768 : i * 768 + 768], attend.at[:, i * 768 : i * 768 + 768]) for i in range(3)],
            (merging_far, merging),
            *[(expand_far.at[:, i * 1024 : i * 1024 + 1024], expand.at[:, i * 1024 : i * 1024 + 1024]) for i in range(3)],
            *[(shrink_far.at[i * 1024 : i * 1024 + 1024], shrink.at[i * 1024 : i * 1024 + 1024]) for i in range(3)],
        ],
        load_sem,
    )
    saves = []

    def save(*numbers):
        for number in numbers:
            copy = pltpu.make_async_copy(refs[9 + number], far[number], save_sem.at[number])
            copy.start()
            saves.append(copy)

    vectors[...] = jnp.zeros_like(vectors)
    key_chip = chip_of(4 * iota((TILE, 1), 0), sizes, pack)
    own_chip = chip_of(4 * iota((1, TILE), 1), sizes, pack)
    valid = (key_chip < 4).astype(F32)
    loads[0].wait()
    values = hidden[...]
    vectors[10:11, :768] = row_sum(valid * values * values)
    unit, _ = standardize(values)
    norm = low(unit * gains[0:1] + shifts[0:1])
    normed[...] = norm
    for part in range(3):
        cols = slice(part * 768, part * 768 + 768)
        loads[1 + part].wait()
        mix = dot(norm, attend[:, cols])
        mixed[:, cols] = low(mix)
        if part:
            turned[(part - 1) * 768 : part * 768] = low(mix.T)
    save(0, 1, 2)

    @pl.loop(0, 3)
    def _(step):
        def score(number):
            pair, half = 2 * step + number // 2, number % 2
            query = only(mixed[:, pair_lanes(pair)], half) * BF16(0.125)
            return dot_nt(mixed[:, pair_lanes(pair, 768)], query)

        ready = [score(0), score(1)]
        for number in range(4):
            if number + 2 < 4:
                ready.append(score(number + 2))
            pair, half = 2 * step + number // 2, number % 2
            scores = jnp.where(key_chip == own_chip, ready[number], NEGATIVE)
            expos = jnp.exp(scores - jnp.max(scores, axis=0, keepdims=True))
            prob = low(expos * (1.0 / jnp.sum(expos, axis=0, keepdims=True)))
            probs[pair * 2 + half] = prob
            context_turned[head_rows(pair, half)] = dot(turned[head_rows(pair, half, 768)], prob)

    mingled = low(context_turned[...].T)
    context[...] = mingled
    save(3, 4)
    loads[4].wait()
    attention = dot(mingled, merging[...]) + biases[0:1]
    vectors[11:12, :768] = row_sum(valid * attention * attention)
    center = hidden[...] + attention
    middle[...] = center
    unit, _ = standardize(center)
    norm = low(unit * gains[1:2] + shifts[1:2])
    normed_two[...] = norm
    save(5, 6)
    feed = jnp.zeros_like(center)
    def widened(part):
        if part % 2 == 0:
            loads[5 + part // 2].wait()
        cols = slice(part * 512, part * 512 + 512)
        return dot(norm, expand[:, cols]) + inner[:, cols]

    ready = [widened(0)]
    for part in range(6):
        if part < 5:
            ready.append(widened(part + 1))
        cols = slice(part * 512, part * 512 + 512)
        value, slant = gelu_pair(ready[part])
        value = low(value)
        active[:, cols] = value
        slope[part // 2, :, part % 2 * 512 : part % 2 * 512 + 512] = slant
        if part % 2 == 0:
            loads[8 + part // 2].wait()
        feed = feed + dot(value, shrink[cols])
    save(7, 8)
    feed = feed + biases[1:2]
    vectors[12:13, :768] = row_sum(valid * feed * feed)
    output = center + feed
    vectors[13:14, :768] = row_sum(valid * output * output)
    vectors[14:15, :768] = jnp.broadcast_to(row_sum(valid), (1, 768))
    sent[...] = low(output)
    for copy in saves:
        copy.wait()


def encoder_forward_call(sizes, tokens, gains, shifts, biases, attend, merging, expand, inner, shrink):
    shapes = (
        ((256, 768), BF16),
        ((256, 2304), BF16),
        ((1536, 256), BF16),
        ((12, 256, 256), BF16),
        ((256, 768), BF16),
        ((256, 768), F32),
        ((256, 768), BF16),
        ((256, 3072), BF16),
        ((3, 256, 1024), F32),
    )
    return pl.pallas_call(
        encoder_forward_kernel,
        out_shape=(jax.ShapeDtypeStruct((256, 768), BF16), jax.ShapeDtypeStruct((16, 1024), F32))
        + tuple(jax.ShapeDtypeStruct(*shape) for shape in shapes),
        in_specs=[smem_spec()] + [vmem_spec()] * 4 + [any_spec()] * 5,
        out_specs=(vmem_spec(),) * 2 + (any_spec(),) * len(shapes),
        scratch_shapes=[pltpu.VMEM(*shape) for shape in shapes]
        + [
            pltpu.VMEM((256, 768), F32),
            pltpu.VMEM(attend.shape, BF16),
            pltpu.VMEM(merging.shape, BF16),
            pltpu.VMEM(expand.shape, BF16),
            pltpu.VMEM(shrink.shape, BF16),
            pltpu.VMEM((768, 256), F32),
            pltpu.SemaphoreType.DMA((11,)),
            pltpu.SemaphoreType.DMA((len(shapes),)),
        ],
        compiler_params=pltpu.CompilerParams(vmem_limit_bytes=60 * 2**20),
        name="encoder_forward",
    )(sizes, gains, shifts, biases, inner[None], tokens, attend, merging, expand, shrink)


def decoder_kernel(
    reduce, sizes, distance, slots, frequency, sent, biases, mask_token, gains, shifts, inner,
    cotangent, entry_far, attend_far, merging_far, expand_far, shrink_far,
    summed, rest, vectors, encoded_grad, *refs,
):
    (
        table, start, normed, mixed, turned, probs, flipped, context, normed_two, active,
        before_grad, go_low, attention_low, context_grad, delta, mixed_grad, target, masked_keys,
        entry_weight, attend, merging, expand, shrink, load_sem,
    ) = refs[:24]
    pack = lax.axis_index("section")
    if reduce:
        mine, partner = neighbours()
        greet(partner)
        engine = reducer(DECODER_CHUNKS, DECODER_CHUNKS, mine, partner, summed, refs[24:])
        put = engine.put
    else:
        put = put_into(summed)
    put_rest = put_into(rest)
    loads = fetch(
        [
            (entry_far, entry_weight),
            (attend_far, attend),
            (cotangent.at[pack], target),
            (merging_far, merging),
            (expand_far, expand),
            (shrink_far, shrink),
        ],
        load_sem,
    )
    tiles = start.shape[0] // TILE
    vectors[...] = jnp.zeros_like(vectors)
    large = sizes[pack, 0] == 1024

    def add_row(row, value):
        vectors[row : row + 1, :] += value

    positions = iota((32, 128), 0).astype(F32)
    for chip in range(4):
        spacing = distance[pack, chip].astype(F32) / 16.0
        angle = positions * (spacing * frequency[...])
        table[0, chip] = jnp.sin(angle)
        table[1, chip] = jnp.cos(angle)
    loads[0].wait()
    entry = low(dot(sent[...], entry_weight[...]) + biases[0:1])
    loads[1].wait()

    blocks = start.shape[0] // BLOCK

    def slot_chip(tile, size):
        return chip_of(iota((size, 1), 0) + tile * size, sizes, pack)

    def validity(tile, size):
        return (slot_chip(tile, size) < 4).astype(F32)

    def spread_of(tile):
        return (slots[pl.ds(pack, 1)] == iota((TILE, TILE), 0) + tile * TILE).astype(F32)

    def encoding_of(tile):
        pieces = []
        for kind in range(2):
            wave = table[kind, 0, aligned(tile * 8, 8, 8)]
            big = jnp.broadcast_to(wave[:, None], (8, 32, 128)).reshape(TILE, 128)
            wave = table[kind, tile, 0:16]
            own = jnp.broadcast_to(wave[:, None], (16, 16, 128)).reshape(TILE, 128)
            pieces.append(jnp.where(large, big, own))
        for kind in range(2):
            wave = table[kind, 0]
            big = jnp.broadcast_to(wave[None], (8, 32, 128)).reshape(TILE, 128)
            wave = table[kind, tile, 0:16]
            own = jnp.broadcast_to(wave[None], (16, 16, 128)).reshape(TILE, 128)
            pieces.append(jnp.where(large, big, own))
        return jnp.concatenate(pieces, axis=1)

    @pl.loop(0, tiles)
    def _(tile):
        rows = rows_of(tile)
        valid = validity(tile, TILE)
        spread = spread_of(tile)
        fill = valid * (1.0 - jnp.sum(spread, axis=1, keepdims=True))
        hidden = dot(low(spread), entry) + fill * mask_token[...] + encoding_of(tile) * valid
        start[rows] = hidden
        add_row(12, row_sum(valid * hidden * hidden))
        add_row(16, row_sum(valid))
        unit, _ = standardize(hidden)
        norm = low(unit * gains[0:1] + shifts[0:1])
        normed[rows] = norm
        mix = dot(norm, attend[...])
        mix_low = low(mix)
        mixed[rows] = mix_low
        turned[:, rows] = low(mix[:, 256:].T)
        lane = iota((TILE, 128), 1)
        other = (lane % 64 < 5) & (lane % 64 != slot_chip(tile, TILE))
        other = jnp.where(other, NEGATIVE, 0.0).astype(BF16)
        for head in range(4):
            lanes = slice(256 + head // 2 * 128, 384 + head // 2 * 128)
            masked_keys[head, rows] = jnp.where(lane // 64 == head % 2, mix_low[:, lanes], other)

    @pl.loop(0, 2 * tiles)
    def _(step):
        pair, tile = step // tiles, step % tiles
        rows = rows_of(tile)
        lane = iota((TILE, 128), 1)
        chosen = (lane % 64 == slot_chip(tile, TILE)).astype(F32).astype(BF16)
        for half in range(2):
            query = jnp.where(lane // 64 == half, mixed[rows, pair_lanes(pair)] * BF16(0.125), chosen)
            scores = dot_nt(masked_keys[pair * 2 + half], query)
            expos = jnp.exp(scores - jnp.max(scores, axis=0, keepdims=True))
            prob = low(expos * (1.0 / jnp.sum(expos, axis=0, keepdims=True)))
            probs[pair * 2 + half, :, rows] = prob
            flipped[head_rows(pair, half), rows] = dot(turned[head_rows(pair, half, 256)], prob)

    for copy in loads[2:]:
        copy.wait()

    @pl.loop(0, blocks)
    def _(tile):
        rows = rows_of(tile, BLOCK)
        valid = validity(tile, BLOCK)
        mingled_wide = flipped[:, rows].T
        mingled = low(mingled_wide)
        context[rows] = mingled
        attention = dot(mingled, merging[...]) + biases[1:2]
        add_row(13, row_sum(valid * attention * attention))
        center = start[rows] + attention
        unit, inverse = standardize(center)
        norm = low(unit * gains[1:2] + shifts[1:2])
        normed_two[rows] = norm
        go = target[rows] * valid
        go_below = low(go)
        go_low[rows] = go_below
        add_row(2, row_sum(go))
        feed = jnp.zeros_like(go)
        norm_grad = jnp.zeros_like(go)
        for part in range(8):
            cols = slice(part * 256, part * 256 + 256)
            before = dot(norm, expand[:, cols]) + inner[:, cols]
            value, slope = gelu_pair(before)
            value = low(value)
            active[rows, cols] = value
            feed = feed + dot(value, shrink[cols])
            grad = low(slope * dot_nt(go_below, shrink[cols]))
            before_grad[rows, cols] = grad
            lanes = slice(part % 2 * 256, part % 2 * 256 + 256)
            vectors[8 + part // 2 : 9 + part // 2, lanes] += row_sum(grad.astype(F32))
            norm_grad = norm_grad + dot_nt(grad, expand[:, cols])
        feed = feed + biases[2:3]
        add_row(14, row_sum(valid * feed * feed))
        output = center + feed
        add_row(15, row_sum(valid * output * output))
        add_row(5, row_sum(norm_grad * unit))
        add_row(7, row_sum(norm_grad))
        grad = go + norm_back(unit, inverse, gains[1:2], norm_grad)
        target[rows] = grad
        add_row(1, row_sum(grad))
        below = low(grad)
        attention_low[rows] = below
        outer = low(dot_nt(below, merging[...]))
        context_grad[rows] = outer
        product = (outer.astype(F32) * mingled_wide).T
        for head in range(4):
            delta[head, :, rows] = row_sum(product[head * 64 : head * 64 + 64])

    for part in range(2):
        cols = slice(part * 256, part * 256 + 256)
        store_packed(put, part * 16, DECODER_EXPAND, dot_tn(normed_two[:, cols], before_grad[...]))
        value = dot_tn(attention_low[:, cols], context[...])
        store_packed(put, part * 16, DECODER_MERGE, value)
    for block in range(2):
        put(slice(block * 16, block * 16 + 16), 4352, jnp.zeros((16, 16, DECODER_CHUNKS * SPAN - 4352), F32))
    if reduce:
        await_greetings()
        engine.send(2048)

    @pl.loop(0, 8)
    def _(part):
        cols = aligned(part * 256, 256, 256)
        store_packed(put, part * 4, DECODER_SHRINK, dot_tn(active[:, cols], go_low[...]))

    if reduce:
        engine.send(DECODER_CHUNKS * SPAN)

    flipped[...] = jnp.zeros_like(flipped)

    @pl.loop(0, 2 * tiles)
    def _(step):
        pair, tile = step // tiles, step % tiles
        rows = rows_of(tile)
        lanes = pair_lanes(pair)
        values = mixed[rows, pair_lanes(pair, 512)]
        raws, probabilities, queries, outers = [], [], [], []
        for half in range(2):
            prob = probs[pair * 2 + half, rows]
            outer = only(context_grad[:, lanes], half)
            raw = low(prob.astype(F32) * (dot_nt(values, outer) - delta[pair * 2 + half]))
            flipped[head_rows(pair, half)] += dot(turned[head_rows(pair, half), rows], raw)
            raws.append(raw)
            probabilities.append(prob)
            outers.append(outer)
            queries.append(only(mixed[:, lanes], half))
        key_grad = dot(jnp.concatenate(raws, axis=1), jnp.concatenate(queries, axis=0))
        mixed_grad[rows, pair_lanes(pair, 256)] = low(key_grad * 0.125)
        value_grad = dot(jnp.concatenate(probabilities, axis=1), jnp.concatenate(outers, axis=0))
        mixed_grad[rows, pair_lanes(pair, 512)] = low(value_grad)
        if reduce:
            engine.turn(step)

    def last(tile, entry_grad):
        rows = rows_of(tile)
        mixed_grad[rows, 0:256] = low(flipped[:, rows].T * 0.125)
        norm_grad = dot_nt(mixed_grad[rows], attend[...])
        unit, inverse = standardize(start[rows])
        add_row(4, row_sum(norm_grad * unit))
        add_row(6, row_sum(norm_grad))
        grad = target[rows] + norm_back(unit, inverse, gains[0:1], norm_grad)
        spread = spread_of(tile)
        fill = validity(tile, TILE) * (1.0 - jnp.sum(spread, axis=1, keepdims=True))
        add_row(3, row_sum(fill * grad))
        if reduce:
            engine.turn(2 * tiles + tile)
        return entry_grad + dot_tn(low(spread), low(grad))

    entry_grad = lax.fori_loop(0, tiles, last, jnp.zeros((TILE, 512), F32))
    add_row(0, row_sum(entry_grad))
    entry_low = low(entry_grad)
    encoded_grad[...] = low(dot_nt(entry_low, entry_weight[...]))
    store_packed(put_rest, 0, ENTRY, dot_tn(sent[...], entry_low))

    @pl.loop(0, 3)
    def _(part):
        if reduce:
            engine.turn(3 * tiles + part)

        @pl.when(part < 2)
        def _():
            cols = aligned(part * 256, 256, 256)
            store_packed(put_rest, part * 16, DECODER_ATTEND, dot_tn(normed[:, cols], mixed_grad[...]))

    if reduce:
        engine.close()


def decoder_call(
    reduce, sizes, distance, slots, sent, cotangent, entry_weight, biases, mask_token,
    gains, shifts, attend, merging, expand, inner, shrink,
):
    length = cotangent.shape[1]
    width = 512
    frequency = np.exp(-np.log(10000.0) * np.arange(width // 4) / (width // 4)).astype(np.float32)
    if reduce:
        summed = jax.ShapeDtypeStruct((DECODER_CHUNKS, 16, SPAN), F32)
        extra = reducer_scratch(DECODER_CHUNKS, DECODER_CHUNKS)
        params = dict(collective_id=1, has_side_effects=True)
    else:
        summed = jax.ShapeDtypeStruct((DECODER_CHUNKS, 2, 16, 16, SPAN), BF16)
        extra = []
        params = dict()
    return pl.pallas_call(
        functools.partial(decoder_kernel, reduce),
        out_shape=(
            summed,
            jax.ShapeDtypeStruct((REST_CHUNKS, 2, 16, 16, SPAN), BF16),
            jax.ShapeDtypeStruct((24, width), F32),
            jax.ShapeDtypeStruct((256, 768), BF16),
        ),
        in_specs=[smem_spec()] * 2 + [vmem_spec()] * 8 + [any_spec()] * 6,
        out_specs=(vmem_spec(),) * 4,
        scratch_shapes=[
            pltpu.VMEM((2, 4, 32, 128), F32),
            pltpu.VMEM((length, width), F32),
            pltpu.VMEM((length, width), BF16),
            pltpu.VMEM((length, 768), BF16),
            pltpu.VMEM((512, length), BF16),
            pltpu.VMEM((4, length, length), BF16),
            pltpu.VMEM((256, length), F32),
            pltpu.VMEM((length, 256), BF16),
            pltpu.VMEM((length, width), BF16),
            pltpu.VMEM((length, 2048), BF16),
            pltpu.VMEM((length, 2048), BF16),
            pltpu.VMEM((length, width), BF16),
            pltpu.VMEM((length, width), BF16),
            pltpu.VMEM((length, 256), BF16),
            pltpu.VMEM((4, 1, length), F32),
            pltpu.VMEM((length, 768), BF16),
            pltpu.VMEM((length, width), F32),
            pltpu.VMEM((4, length, 128), BF16),
            pltpu.VMEM(entry_weight.shape, BF16),
            pltpu.VMEM(attend.shape, BF16),
            pltpu.VMEM(merging.shape, BF16),
            pltpu.VMEM(expand.shape, BF16),
            pltpu.VMEM(shrink.shape, BF16),
            pltpu.SemaphoreType.DMA((6,)),
        ]
        + extra,
        compiler_params=pltpu.CompilerParams(vmem_limit_bytes=63 * 2**20, **params),
        name="decoder_block",
    )(
        sizes, distance, slots, jnp.asarray(frequency)[None], sent, biases, mask_token[None], gains, shifts,
        inner[None], cotangent, entry_weight, attend, merging, expand, shrink,
    )


def encoder_backward_kernel(
    reduce, encoded_grad, sums, decoder_vectors, gains, tokens, rest, attend_far, merging_far, expand_far,
    shrink_far, normed_far, mixed_far, turned_far, probs_far, context_far, middle_far, normed_two_far, active_far,
    slope_far, summed, vectors, tokens_grad, *refs,
):
    if reduce:
        decoder_sums, arrived = refs[:2]
        refs = refs[2:]
    (
        hidden, attend, merging, expand, shrink, normed, mixed, turned, probs, context, middle, normed_two, active,
        slope, before_grad, norm_sum, attention_low, context_grad, key_grad, query_turned, mixed_grad, active_turned,
        flipped, inner_sum, load_sem, part_sem,
    ) = refs[:26]
    pack = lax.axis_index("section")

    def part_loads(part):
        cols = aligned(part * 1024, 1024, 1024)
        slot = part % 2
        return [
            pltpu.make_async_copy(expand_far.at[:, cols], expand.at[slot], part_sem.at[slot, 0]),
            pltpu.make_async_copy(shrink_far.at[cols], shrink.at[slot], part_sem.at[slot, 1]),
            pltpu.make_async_copy(slope_far.at[part], slope.at[slot], part_sem.at[slot, 2]),
        ]

    if reduce:
        (
            decoder_total, encoder_total, decoder_got, encoder_got, payload,
            own_sem, small_send, small_recv, pay_send, pay_recv, small_load,
        ) = refs[26:37]
        mine, partner = neighbours()
        greet(partner)
        engine = reducer(CHUNKS, STAGING, mine, partner, summed, refs[37:])
        put = engine.put
        engine.release(UNIT)
        first_own = fetch(
            [
                pair
                for chunk in range(REST_CHUNKS)
                for pair in (
                    (rest.at[chunk, 1 - mine["c"]], engine.staging.at[chunk]),
                    (rest.at[chunk, mine["c"]], engine.own.at[chunk]),
                )
            ],
            own_sem,
        )
        decoder_load = pltpu.make_async_copy(decoder_vectors, decoder_total.at[0], small_load)
        decoder_load.start()
    else:
        put = put_into(summed)
    early = pltpu.make_async_copy(active_far, active, load_sem.at[10])
    early.start()
    for copy in part_loads(0):
        copy.start()
    if reduce:
        for copy in first_own:
            copy.wait()
        await_greetings()
        engine.send(UNIT)
    loads = fetch(
        [
            (normed_two_far, normed_two),
            (middle_far, middle),
            (merging_far, merging),
            (context_far, context),
            (mixed_far, mixed),
            (probs_far, probs),
            (turned_far.at[0:768], turned),
            (normed_far, normed),
            (attend_far, attend),
            (tokens.at[pack], hidden),
        ],
        load_sem,
    )
    for copy in part_loads(1):
        copy.start()
    vectors[...] = sums[...]
    go_low = encoded_grad[...]
    go = go_low.astype(F32)
    vectors[1:2, :768] = row_sum(go)
    norm_sum[...] = jnp.zeros_like(norm_sum)

    def send(unit):
        if reduce:
            engine.send((unit + 1) * UNIT)

    def release(unit):
        if reduce:
            engine.release((unit + 1) * UNIT)

    def shrink_start():
        early.wait()
        for piece in range(4):
            rows = slice(piece * 768, piece * 768 + 768)
            active_turned[rows] = active[:, rows].T

    def shrink_grad(part):
        release(1 + part)
        cols = slice(part * 256, part * 256 + 256)
        for piece in range(4):
            rows = slice(piece * 768, piece * 768 + 768)
            store_packed(put, piece * 8, ENCODER_SHRINK[part], dot(active_turned[rows], encoded_grad[:, cols]))
        send(1 + part)

    def hidden_layer(part):
        for copy in part_loads(part):
            copy.wait()
        slot = part % 2
        grad = low(slope[slot] * dot_nt(encoded_grad[...], shrink[slot]))
        before_grad[...] = grad
        inner_sum[part] = row_sum(grad.astype(F32))
        norm_sum[...] += dot_nt(grad, expand[slot])

        @pl.when(part == 0)
        def _():
            for copy in part_loads(2):
                copy.start()

    def expand_grad(part):
        release(4 + part)
        if part == 0:
            loads[0].wait()
            flipped[...] = normed_two[...].T
        store_packed(put, 0, ENCODER_EXPAND[part], dot(flipped[...], before_grad[...]))
        send(4 + part)

    def middle_layer():
        loads[1].wait()
        loads[2].wait()
        for part in range(3):
            vectors[6 + part : 7 + part] = inner_sum[part]
        unit, inverse = standardize(middle[...])
        norm_grad = norm_sum[...]
        vectors[3:4, :768] = row_sum(norm_grad * unit)
        vectors[5:6, :768] = row_sum(norm_grad)
        grad = encoded_grad[...].astype(F32) + norm_back(unit, inverse, gains[1:2], norm_grad)
        vectors[0:1, :768] = row_sum(grad)
        tokens_grad[...] = grad
        below = low(grad)
        attention_low[...] = below
        context_grad[...] = low(dot_nt(below, merging[...]))
        for copy in loads[3:7]:
            copy.wait()

    def attention(first):
        @pl.loop(first, first + 2)
        def _(pair):
            lanes = pair_lanes(pair)
            values = mixed[:, pair_lanes(pair, 1536)]
            keys_total = jnp.zeros((TILE, 128), F32)
            values_total = jnp.zeros((TILE, 128), F32)
            for half in range(2):
                prob = probs[pair * 2 + half]
                outer = only(context_grad[:, lanes], half)
                query = only(mixed[:, lanes], half)
                wide = prob.astype(F32)
                grad = dot_nt(values, outer)
                raw = low(wide * (grad - jnp.sum(wide * grad, axis=0, keepdims=True)))
                keys_total = keys_total + dot(raw, query)
                values_total = values_total + dot(prob, outer)
                rows = head_rows(pair, half)
                query_turned[rows] = dot(turned[rows], raw)
            key_grad[0, :, lanes] = keys_total
            key_grad[1, :, lanes] = values_total

    def mixing():
        mixed_grad[:, 0:768] = low(query_turned[...].T * 0.125)
        mixed_grad[:, 768:1536] = low(key_grad[0] * 0.125)
        mixed_grad[:, 1536:2304] = low(key_grad[1])

    def attend_grad(part):
        if part == 0:
            loads[7].wait()
            flipped[...] = normed[...].T
        release(7 + part)
        wide = slice(part * 1024, min(part * 1024 + 1024, 2304))
        store_packed(put, 0, ENCODER_ATTEND[part], dot(flipped[...], mixed_grad[:, wide]))
        if part == 2:
            store_packed(put, 0, ENCODER_MERGE, dot_tn(attention_low[...], context[...]))
        send(7 + part)

    def input_layer():
        loads[8].wait()
        loads[9].wait()
        norm_grad = dot_nt(mixed_grad[...], attend[...])
        unit, inverse = standardize(hidden[...])
        vectors[2:3, :768] = row_sum(norm_grad * unit)
        vectors[4:5, :768] = row_sum(norm_grad)
        grad = tokens_grad[...] + norm_back(unit, inverse, gains[0:1], norm_grad)
        tokens_grad[...] = grad
        if reduce:
            payload[...] = low(grad)

    if not reduce:
        shrink_start()
        for part in range(3):
            shrink_grad(part)
        for part in range(3):
            hidden_layer(part)
            expand_grad(part)
        middle_layer()
        for first in (0, 2, 4):
            attention(first)
        mixing()
        for part in range(3):
            attend_grad(part)
        input_layer()
        return

    def exchange(source, piece):
        rows = aligned(piece * 32, 32, 32)
        return remote(source.at[rows], arrived.at[rows], pay_send.at[piece], pay_recv.at[piece], partner["x"])

    small_route = ("c",) + ROUTES[0]
    totals = ((decoder_total, decoder_got), (encoder_total, encoder_got))

    def small_copy(stage, kind):
        source, target = totals[kind]
        return remote(
            source.at[stage],
            target.at[stage],
            small_send.at[stage, kind],
            small_recv.at[stage, kind],
            partner[small_route[stage]],
        )

    def small_advance(stage):
        if stage == 0:
            encoder_total[0] = vectors[...]
        for kind in range(2):
            source, target = totals[kind]
            if stage > 0:
                small_copy(stage - 1, kind).wait_recv()
                source[stage] = source[stage - 1] + target[stage - 1]
            if stage < 5:
                small_copy(stage, kind).start()

    shrink_start()
    shrink_grad(0)
    decoder_load.wait()

    part = functools.partial
    works = {0: part(shrink_grad, 1), 1: part(shrink_grad, 2)}
    works.update({3 + 2 * number: part(expand_grad, number) for number in range(3)})
    works.update({8: middle_layer, 12: input_layer})
    works.update({13 + number: part(attend_grad, number) for number in range(3)})
    turns = CHUNKS + 4 * LAG
    works.update({turns - 11 + 2 * stage: part(small_advance, stage) for stage in range(6)})

    @pl.loop(0, turns)
    def _(number):
        engine.turn(number)
        @pl.when((number >= 2) & (number <= 6) & (number % 2 == 0))
        def _():
            hidden_layer(number // 2 - 1)

        @pl.when((number >= 9) & (number <= 11))
        def _():
            attention(2 * (number - 9))

        pl.when(number == 11)(mixing)
        for position, work in works.items():
            pl.when(number == position)(work)

        piece = number // 2

        @pl.when((pack == 0) & (number % 2 == 0) & (piece < 8))
        def _():
            exchange(encoded_grad, piece).start()

        @pl.when((pack == 1) & (number >= 12) & (number % 2 == 0) & (number < 28))
        def _():
            exchange(payload, piece - 6).start()

    for stage in range(5):
        for kind in range(2):
            small_copy(stage, kind).wait_send()
    for piece in range(8):
        exchange(payload, piece).wait()
    engine.close()
    vectors[...] = encoder_total[5]
    decoder_sums[...] = decoder_total[5]


def encoder_backward_call(reduce, tokens, encoded_grad, sums, decoder_vectors, rest, kept, gains, attend, merging, expand, shrink):
    if reduce:
        summed = jax.ShapeDtypeStruct((CHUNKS, 16, SPAN), F32)
        more = (
            jax.ShapeDtypeStruct(decoder_vectors.shape, F32),
            jax.ShapeDtypeStruct((256, 768), BF16),
        )
        more_specs = (vmem_spec(), any_spec())
        extra = [
            pltpu.VMEM((6,) + decoder_vectors.shape, F32),
            pltpu.VMEM((6,) + sums.shape, F32),
            pltpu.VMEM((5,) + decoder_vectors.shape, F32),
            pltpu.VMEM((5,) + sums.shape, F32),
            pltpu.VMEM((256, 768), BF16),
            pltpu.SemaphoreType.DMA((2 * REST_CHUNKS,)),
            pltpu.SemaphoreType.DMA((5, 2)),
            pltpu.SemaphoreType.DMA((5, 2)),
            pltpu.SemaphoreType.DMA((8,)),
            pltpu.SemaphoreType.DMA((8,)),
            pltpu.SemaphoreType.DMA,
        ] + reducer_scratch(CHUNKS, STAGING)
        params = dict(collective_id=2, has_side_effects=True)
    else:
        summed = jax.ShapeDtypeStruct((CHUNKS, 2, 16, 16, SPAN), BF16)
        more, more_specs, extra, params = (), (), [], dict()
    return pl.pallas_call(
        functools.partial(encoder_backward_kernel, reduce),
        out_shape=(
            summed,
            jax.ShapeDtypeStruct(sums.shape, F32),
            jax.ShapeDtypeStruct((256, 768), F32),
        )
        + more,
        in_specs=[vmem_spec()] * 2 + [any_spec(), vmem_spec()] + [any_spec()] * 15,
        out_specs=(vmem_spec(),) * 3 + more_specs,
        scratch_shapes=[
            pltpu.VMEM((256, 768), F32),
            pltpu.VMEM(attend.shape, BF16),
            pltpu.VMEM(merging.shape, BF16),
            pltpu.VMEM((2, 768, 1024), BF16),
            pltpu.VMEM((2, 1024, 768), BF16),
            pltpu.VMEM((256, 768), BF16),
            pltpu.VMEM((256, 2304), BF16),
            pltpu.VMEM((768, 256), BF16),
            pltpu.VMEM((12, 256, 256), BF16),
            pltpu.VMEM((256, 768), BF16),
            pltpu.VMEM((256, 768), F32),
            pltpu.VMEM((256, 768), BF16),
            pltpu.VMEM((256, 3072), BF16),
            pltpu.VMEM((2, 256, 1024), F32),
            pltpu.VMEM((256, 1024), BF16),
            pltpu.VMEM((256, 768), F32),
            pltpu.VMEM((256, 768), BF16),
            pltpu.VMEM((256, 768), BF16),
            pltpu.VMEM((2, 256, 768), F32),
            pltpu.VMEM((768, 256), F32),
            pltpu.VMEM((256, 2304), BF16),
            pltpu.VMEM((3072, 256), BF16),
            pltpu.VMEM((768, 256), BF16),
            pltpu.VMEM((3, 1, 1024), F32),
            pltpu.SemaphoreType.DMA((11,)),
            pltpu.SemaphoreType.DMA((2, 3)),
        ]
        + extra,
        compiler_params=pltpu.CompilerParams(vmem_limit_bytes=60 * 2**20, **params),
        name="encoder_backward",
    )(encoded_grad, sums, decoder_vectors, gains, tokens, rest, attend, merging, expand, shrink, *kept)


def unpack(packed, place):
    def take(start, size):
        pieces = []
        while size:
            chunk, first = divmod(start, SPAN)
            length = min(size, SPAN - first)
            pieces.append(packed[chunk, ..., first : first + length])
            start, size = start + length, size - length
        return pieces[0] if len(pieces) == 1 else jnp.concatenate(pieces, axis=-1)

    offset, count, width = place
    pieces = [take(offset + i * width, width) for i in range(count // 16)]
    if count % 16:
        rest = take(offset + count // 16 * width, width // 2)
        pieces.append(jnp.concatenate([rest[..., :8, :], rest[..., 8:, :]], axis=-1))
    return pieces[0] if len(pieces) == 1 else jnp.concatenate(pieces, axis=-2)


def finish_kernel(
    decoder_summed_far, decoder_sums_far, encoder_sums_far, summed_far, arrived_far, tokens_grad_far, encoded_grad_far,
    boundary, statistics, e_gains, e_shifts, e_biases, e_attend, e_merge, e_expand, e_inner, e_shrink,
    d_entry, d_biases, mask_grad, d_gains, d_shifts, d_attend, d_merge, d_expand, d_inner, d_shrink,
    decoder_summed, decoder_sums, encoder_sums, summed, arrived, tokens_grad, encoded_grad, load_sem,
):
    section = lax.axis_index("section")
    loads = fetch(
        [
            (decoder_summed_far, decoder_summed),
            (decoder_sums_far, decoder_sums),
            (encoder_sums_far, encoder_sums),
            (summed_far, summed),
            (arrived_far, arrived),
            (tokens_grad_far, tokens_grad),
            (encoded_grad_far, encoded_grad),
        ],
        load_sem,
    )
    number = section * lax.axis_size("dp") + lax.axis_index("dp")

    def own(rows, count):
        width = rows.shape[1]
        return pltpu.roll(rows, (width - number * count) % width, axis=1)[:, :count]

    def own_line(rows, count):
        return own(jnp.concatenate([rows[i : i + 1] for i in range(rows.shape[0])], axis=1), count)

    for copy in loads[:3]:
        copy.wait()
    lane = iota((1, 128), 1)
    values = jnp.zeros((1, 128), F32)
    for sums, width, first, count_row, base in ((encoder_sums, DE, 10, 14, 0), (decoder_sums, DD, 12, 16, 4)):
        scale = 1.0 / (sums[count_row : count_row + 1, 0:1] * width)
        for i in range(4):
            value = jnp.sum(sums[first + i : first + i + 1, :], axis=1, keepdims=True) * scale
            values = jnp.where(lane == base + i, value, values)
    statistics[...] = jnp.sqrt(values)[:, :8]
    rows = own(encoder_sums[0:8, :DE], 24)
    e_biases[...] = rows[0:2]
    e_gains[...] = rows[2:4]
    e_shifts[...] = rows[4:6]
    e_inner[...] = own_line(encoder_sums[6:9], 96)
    rows = own(decoder_sums[0:8], 16)
    d_biases[...] = rows[0:3]
    mask_grad[...] = rows[3:4]
    d_gains[...] = rows[4:6]
    d_shifts[...] = rows[6:8]
    d_inner[...] = own_line(decoder_sums[8:12], 64)

    d_merge[...] = unpack(decoder_summed, DECODER_MERGE)
    d_expand[...] = unpack(decoder_summed, DECODER_EXPAND)
    d_shrink[...] = unpack(decoder_summed, DECODER_SHRINK)
    loads[3].wait()
    d_entry[...] = unpack(summed, ENTRY)
    d_attend[...] = unpack(summed, DECODER_ATTEND)
    for target, places in ((e_expand, ENCODER_EXPAND), (e_attend, ENCODER_ATTEND), (e_shrink, ENCODER_SHRINK)):
        start = 0
        for place in places:
            target[:, start : start + place[2]] = unpack(summed, place)
            start += place[2]
    e_merge[...] = unpack(summed, ENCODER_MERGE)
    for copy in loads[4:]:
        copy.wait()

    @pl.when(section == 0)
    def _():
        boundary[0, 0] = tokens_grad[...]
        boundary[0, 1] = arrived[...].astype(F32)

    @pl.when(section == 1)
    def _():
        boundary[0, 0] = arrived[...].astype(F32)
        boundary[0, 1] = encoded_grad[...].astype(F32)


def finish_call(*operands):
    shapes = (
        (1, 2, 256, 768), (1, 8), (2, 24), (2, 24), (2, 24), (24, 2304), (24, 768), (24, 3072), (1, 96), (96, 768),
        (24, 512), (3, 16), (1, 16), (2, 16), (2, 16), (16, 768), (16, 256), (16, 2048), (1, 64), (64, 512),
    )
    outs = list(
        pl.pallas_call(
            finish_kernel,
            out_shape=tuple(jax.ShapeDtypeStruct(shape, F32) for shape in shapes),
            in_specs=[any_spec()] * len(operands),
            out_specs=(vmem_spec(),) * len(shapes),
            scratch_shapes=[pltpu.VMEM(operand.shape, operand.dtype) for operand in operands]
            + [pltpu.SemaphoreType.DMA((len(operands),))],
            compiler_params=pltpu.CompilerParams(vmem_limit_bytes=60 * 2**20),
            name="finish",
        )(*operands)
    )
    for line in (1, 8, 12, 18):
        outs[line] = outs[line].reshape(-1)
    for turned in (6, 16):
        outs[turned] = outs[turned].T
    return tuple(outs)


def scatter_sum(member, share_dim):
    return lax.psum_scatter(
        member, ("section", "dp"), scatter_dimension=share_dim, tiled=True
    )


def finish_generic(decoder_part, part, decoder_sums, encoder_sums, tokens_grad, encoded_grad):
    section = lax.axis_index("section")
    payload = jnp.where(section == 0, encoded_grad, low(tokens_grad))

    def whole(packed, *places):
        packed = jnp.swapaxes(packed, 1, 2).reshape(-1, 32, 16, SPAN)
        blocks = [unpack(packed, place).reshape(32 * place[1], place[2]) for place in places]
        return scatter_sum(jnp.concatenate(blocks, axis=1).astype(F32), 0)

    def line(value):
        return scatter_sum(value, value.ndim - 1)

    arrived = lax.ppermute(payload, "section", [(0, 1), (1, 0)]).astype(F32)
    boundary = jnp.where(
        section == 0,
        jnp.stack([tokens_grad, arrived]),
        jnp.stack([arrived, encoded_grad.astype(F32)]),
    )
    sums = jnp.concatenate(
        [jnp.sum(encoder_sums[10:14], axis=1), jnp.sum(decoder_sums[12:16], axis=1)]
    )
    sums, counts = lax.psum((sums, (encoder_sums[14, 0], decoder_sums[16, 0])), ("section", "dp"))
    scales = jnp.concatenate([jnp.full((4,), counts[0] * DE), jnp.full((4,), counts[1] * DD)])
    return (
        boundary[None],
        jnp.sqrt(sums / scales),
        line(encoder_sums[2:4, :DE]),
        line(encoder_sums[4:6, :DE]),
        line(encoder_sums[0:2, :DE]),
        whole(part, *ENCODER_ATTEND),
        whole(part, ENCODER_MERGE).T,
        whole(part, *ENCODER_EXPAND),
        line(encoder_sums[6:9].reshape(-1)),
        whole(part, *ENCODER_SHRINK),
        whole(decoder_part[1], ENTRY),
        line(decoder_sums[0:3]),
        line(decoder_sums[3]),
        line(decoder_sums[4:6]),
        line(decoder_sums[6:8]),
        whole(decoder_part[1], DECODER_ATTEND),
        whole(decoder_part[0], DECODER_MERGE).T,
        whole(decoder_part[0], DECODER_EXPAND),
        line(decoder_sums[8:12].reshape(-1)),
        whole(decoder_part[0], DECODER_SHRINK),
    )


def body(
    visible_tokens,
    cotangent,
    chip_sizes,
    ground_distance,
    visible_slots,
    encoder_gains,
    encoder_shifts,
    encoder_biases,
    encoder_attend,
    encoder_merge,
    encoder_expand,
    encoder_inner,
    encoder_shrink,
    decoder_entry,
    decoder_biases,
    mask_token,
    decoder_gains,
    decoder_shifts,
    decoder_attend,
    decoder_merge,
    decoder_widen_weight,
    decoder_inner,
    decoder_shrink,
):
    reduce = (lax.axis_size("section"), lax.axis_size("dp")) == (2, 16)
    sent, sums, *kept = encoder_forward_call(
        chip_sizes, visible_tokens, encoder_gains, encoder_shifts, encoder_biases,
        encoder_attend, encoder_merge, encoder_expand, encoder_inner, encoder_shrink,
    )
    decoder_summed, rest, decoder_vectors, encoded_grad = decoder_call(
        reduce, chip_sizes, ground_distance, visible_slots, sent, cotangent, decoder_entry, decoder_biases, mask_token,
        decoder_gains, decoder_shifts, decoder_attend, decoder_merge, decoder_widen_weight, decoder_inner,
        decoder_shrink,
    )
    summed, encoder_sums, tokens_grad, *more = encoder_backward_call(
        reduce, visible_tokens, encoded_grad, sums, decoder_vectors, rest, kept,
        encoder_gains, encoder_attend, encoder_merge, encoder_expand, encoder_shrink,
    )
    if reduce:
        decoder_sums, arrived = more
        return finish_call(
            decoder_summed, decoder_sums, encoder_sums, summed, arrived, tokens_grad, encoded_grad
        )
    return finish_generic(
        (decoder_summed, rest), summed, decoder_vectors, encoder_sums, tokens_grad, encoded_grad
    )


def solution(mesh):
    in_specs = (
        P("dp", None, None),
        P("dp", None, None),
        P("dp", None),
        P("dp", None),
        P("dp", None),
        P(),
        P(),
        P(),
        P(),
        P(),
        P(),
        P(),
        P(),
        P(),
        P(),
        P(),
        P(),
        P(),
        P(),
        P(),
        P(),
        P(),
        P(),
    )
    out_specs = (
        P("section", "dp", None, None),
        P(),
        P(None, ("section", "dp")),
        P(None, ("section", "dp")),
        P(None, ("section", "dp")),
        P(("section", "dp"), None),
        P(None, ("section", "dp")),
        P(("section", "dp"), None),
        P(("section", "dp")),
        P(("section", "dp"), None),
        P(("section", "dp"), None),
        P(None, ("section", "dp")),
        P(("section", "dp")),
        P(None, ("section", "dp")),
        P(None, ("section", "dp")),
        P(("section", "dp"), None),
        P(None, ("section", "dp")),
        P(("section", "dp"), None),
        P(("section", "dp")),
        P(("section", "dp"), None),
    )
    return jax.shard_map(body, mesh=mesh, in_specs=in_specs, out_specs=out_specs, check_vma=False)
```

```python
import functools
import types

import jax
import jax.numpy as jnp
import numpy as np
from jax import lax
from jax.experimental import pallas as pl
from jax.experimental.pallas import tpu as pltpu
from jax.sharding import PartitionSpec as P

DE = 768
DD = 512
TILE = 256
BLOCK = 512
NEGATIVE = -1e30
F32, BF16 = jnp.float32, jnp.bfloat16
MESH_ID = pl.DeviceIdType.MESH

CANON = ("x", "z2", "z1", "y")
ROUTES = (("x", "y", "z1", "z2"), ("y", "x", "z1", "z2"), ("z1", "z2", "x", "y"))
UNIT = 1536
LAG = 2
DECODER_PLAN = types.SimpleNamespace(widths=(2, 2, 1), chunks=7, slots=7, ring=3, span=640)
ENCODER_PLAN = types.SimpleNamespace(widths=(4, 5, 3), chunks=10, slots=4, ring=3, span=1536)

DECODER_EXPAND, DECODER_SHRINK, DECODER_MERGE = (0, 16, 2048), (2048, 64, 512), (4096, 16, 256)
ENTRY, DECODER_ATTEND = (0, 24, 512), (768, 16, 768)
ENCODER_SHRINK = tuple((UNIT * (1 + part), 96, 256) for part in range(3))
ENCODER_EXPAND = tuple((UNIT * (4 + part), 24, 1024) for part in range(3))
ENCODER_ATTEND = ((UNIT * 7, 24, 1024), (UNIT * 8, 24, 1024), (UNIT * 9, 24, 256))
ENCODER_MERGE = (UNIT * 9 + 384, 24, 768)


def dot(a, b):
    return jnp.dot(a, b, preferred_element_type=F32)


def dot_nt(a, b):
    return lax.dot_general(a, b, (((1,), (1,)), ((), ())), preferred_element_type=F32)


def dot_tn(a, b):
    return lax.dot_general(a, b, (((0,), (0,)), ((), ())), preferred_element_type=F32)


def low(value):
    return value.astype(BF16)


def standardize(values):
    centered = values - jnp.mean(values, axis=-1, keepdims=True)
    inverse = lax.rsqrt(jnp.mean(centered * centered, axis=-1, keepdims=True) + 1e-05)
    return centered * inverse, inverse


def norm_back(unit, inverse, gain, grad):
    inner = grad * gain
    return inverse * (
        inner
        - jnp.mean(inner, axis=-1, keepdims=True)
        - unit * jnp.mean(inner * unit, axis=-1, keepdims=True)
    )


def row_sum(values):
    return jnp.sum(values, axis=0, keepdims=True)


def gelu_pair(before):
    half = 0.5 * (1.0 + lax.erf(before * 0.7071067811865476))
    density = jnp.exp(-0.5 * before * before) * 0.3989422804014327
    return before * half, half + before * density


def chip_of(places, sizes, pack):
    end = sizes[pack, 0]
    chip = (places >= end).astype(jnp.int32)
    for slot in range(1, 4):
        end = end + sizes[pack, slot]
        chip = chip + (places >= end).astype(jnp.int32)
    return chip


def iota(shape, dimension):
    return lax.broadcasted_iota(jnp.int32, shape, dimension)


def aligned(start, size, unit):
    if isinstance(start, int):
        return slice(start, start + size)
    return pl.ds(pl.multiple_of(start, unit), size)


def pair_lanes(pair, base=0):
    return aligned(base + pair * 128, 128, 128)


def head_rows(pair, half, base=0):
    return aligned(base + pair * 128 + half * 64, 64, 64)


def rows_of(tile, size=TILE):
    return aligned(tile * size, size, size)


def only(values, half):
    return jnp.where(iota((1, 128), 1) // 64 == half, values, jnp.zeros_like(values))


def fetch(pairs, sems):
    copies = [
        pltpu.make_async_copy(source, target, sems.at[i]) for i, (source, target) in enumerate(pairs)
    ]
    for copy in copies:
        copy.start()
    return copies


def store_packed(put, first, place, value):
    offset, count, width = place
    value = value.reshape(-1, count, width)
    shards = slice(first, first + value.shape[0]) if isinstance(first, int) else pl.ds(first, value.shape[0])
    for piece in range(count // 16):
        put(shards, offset + piece * width, value[:, piece * 16 : piece * 16 + 16])
    if count % 16:
        half = width // 2
        rest = value[:, count - 8 :]
        rest = jnp.concatenate([rest[:, :, :half], rest[:, :, half:]], axis=1)
        put(shards, offset + count // 16 * width, rest)


def halves(shards, value):
    pairs = value.reshape(value.shape[0] // 2, 2, *value.shape[1:])
    if isinstance(shards, slice):
        return slice(shards.start // 2, shards.stop // 2), pairs[:, 0], pairs[:, 1]
    return pl.ds(shards.start // 2, shards.size // 2), pairs[:, 0], pairs[:, 1]


def place_of(names, bits):
    index = 0
    for name in names:
        index = index * 2 + bits[name]
    return index


def left_after(route, stage):
    return tuple(name for name in CANON if name not in route[:stage])


def choices(names):
    for number in range(2 ** len(names)):
        yield {name: (number >> (len(names) - 1 - i)) & 1 for i, name in enumerate(names)}


def neighbours():
    section = lax.axis_index("section")
    data = lax.axis_index("dp")
    mine = {"x": section, "c": data % 2, "y": data // 2 % 2, "z1": data // 4 % 2, "z2": data // 8 % 2}
    partner = {"x": (1 - section, data)}
    for name, step in {"c": 1, "y": 2, "z1": 4, "z2": 8}.items():
        partner[name] = (section, data + step * (1 - 2 * mine[name]))
    return mine, partner


def greet(partner):
    barrier = pltpu.get_barrier_semaphore()
    for name in ("c",) + CANON:
        pl.semaphore_signal(barrier, inc=1, device_id=partner[name], device_id_type=MESH_ID)


def await_greetings():
    pl.semaphore_wait(pltpu.get_barrier_semaphore(), 5)


def remote(source, target, send, recv, device):
    return pltpu.make_async_remote_copy(
        src_ref=source,
        dst_ref=target,
        send_sem=send,
        recv_sem=recv,
        device_id=device,
        device_id_type=MESH_ID,
    )


def reducer(plan, mine, partner, out, refs):
    chunks, slots, span, ring = plan.chunks, plan.slots, plan.span, plan.ring
    progress = types.SimpleNamespace(opened=0, sent=0)
    own, staging, first = refs[:3]
    sent, got = refs[3:15], refs[15:27]
    first_send, first_recv, send_sem, recv_sem = refs[27:31]

    def first_copy(chunk):
        return remote(staging.at[chunk % slots], first.at[chunk], first_send.at[chunk], first_recv.at[chunk], partner["c"])

    def stage_copy(route, stage, chunk):
        return remote(
            sent[route * 4 + stage].at[chunk % ring],
            got[route * 4 + stage].at[chunk],
            send_sem.at[route, stage, chunk],
            recv_sem.at[route, stage, chunk],
            partner[ROUTES[route][stage]],
        )

    def total(route, stage, chunk, bits):
        spot = place_of(CANON, bits)
        cols = slice(sum(plan.widths[:route]) * 128, sum(plan.widths[: route + 1]) * 128)
        value = own[chunk, spot, :, cols].astype(F32) + first[chunk, spot, :, cols].astype(F32)
        for earlier in range(stage):
            names = left_after(ROUTES[route], earlier + 1)
            value = value + got[route * 4 + earlier][chunk, place_of(names, bits)].astype(F32)
        return value

    def advance(stage, chunk):
        for route in range(3):
            if stage:
                stage_copy(route, stage - 1, chunk).wait_recv()
            else:
                first_copy(chunk).wait_recv() if route == 0 else None
            if stage < 4:

                @pl.when(chunk >= ring)
                def _(route=route):
                    stage_copy(route, stage, chunk - ring).wait_send()

        values = []
        for route in range(3):
            path = ROUTES[route]
            if stage == 4:
                values.append(total(route, 4, chunk, mine))
                continue
            names = left_after(path, stage + 1)
            for free in choices(names):
                bits = dict(mine)
                bits[path[stage]] = 1 - mine[path[stage]]
                bits.update(free)
                values.append((route, place_of(names, free), low(total(route, stage, chunk, bits))))
        if stage == 4:
            out[chunk] = jnp.concatenate(values, axis=1)
            return
        for route, spot, value in values:
            sent[route * 4 + stage][chunk % ring, spot] = value
        for route in range(3):
            stage_copy(route, stage, chunk).start()

    def turn(number):
        for stage in range(4, -1, -1):
            chunk = number - LAG * stage
            pl.when((chunk >= 0) & (chunk < chunks))(functools.partial(advance, stage, chunk))

    def put(shards, column, value):
        shards, even, odd = halves(shards, value)
        kept = low(jnp.where(mine["c"] == 0, even, odd))
        given = low(jnp.where(mine["c"] == 0, odd, even))
        width = value.shape[2]
        done = 0
        while done < width:
            chunk, start = divmod(column + done, span)
            size = min(width - done, span - start)
            own[chunk, shards, :, start : start + size] = kept[:, :, done : done + size]
            staging[chunk % slots, shards, :, start : start + size] = given[:, :, done : done + size]
            done += size

    def release(column):
        while progress.opened * span < column:
            if progress.opened >= slots:
                first_copy(progress.opened - slots).wait_send()
            progress.opened += 1

    def send(column):
        while (progress.sent + 1) * span <= column:
            first_copy(progress.sent).start()
            progress.sent += 1

    def close():
        for chunk in range(max(0, chunks - slots), chunks):
            first_copy(chunk).wait_send()
        for chunk in range(chunks - ring, chunks):
            for route in range(3):
                for stage in range(4):
                    stage_copy(route, stage, chunk).wait_send()

    return types.SimpleNamespace(
        own=own, staging=staging, turn=turn, put=put, release=release, send=send, close=close
    )


def reducer_scratch(plan):
    stages = [(width, block) for width in plan.widths for block in (8, 4, 2, 1)]
    return (
        [
            pltpu.VMEM((plan.chunks, 16, 16, plan.span), BF16),
            pltpu.VMEM((plan.slots, 16, 16, plan.span), BF16),
            pltpu.VMEM((plan.chunks, 16, 16, plan.span), BF16),
        ]
        + [pltpu.VMEM((plan.ring, block, 16, width * 128), BF16) for width, block in stages]
        + [pltpu.VMEM((plan.chunks, block, 16, width * 128), BF16) for width, block in stages]
        + [
            pltpu.SemaphoreType.DMA((plan.chunks,)),
            pltpu.SemaphoreType.DMA((plan.chunks,)),
            pltpu.SemaphoreType.DMA((3, 4, plan.chunks)),
            pltpu.SemaphoreType.DMA((3, 4, plan.chunks)),
        ]
    )


def put_into(parts):
    span = parts.shape[-1]

    def put(shards, column, value):
        shards, *pair = halves(shards, value)
        width = value.shape[2]
        done = 0
        while done < width:
            chunk, start = divmod(column + done, span)
            size = min(width - done, span - start)
            for core in range(2):
                parts[chunk, core, shards, :, start : start + size] = low(pair[core][:, :, done : done + size])
            done += size

    return put


def vmem_spec():
    return pl.BlockSpec(memory_space=pltpu.VMEM)


def any_spec():
    return pl.BlockSpec(memory_space=pl.ANY)


def smem_spec():
    return pl.BlockSpec(memory_space=pltpu.SMEM)


def encoder_forward_kernel(
    sizes, gains, shifts, biases, inner, tokens, attend_far, merging_far, expand_far, shrink_far,
    sent, vectors, *refs,
):
    far = refs[:9]
    normed, mixed, turned, probs, context, middle, normed_two, active, slope = refs[9:18]
    hidden, attend, merging, expand, shrink, context_turned, load_sem, save_sem = refs[18:]
    pack = lax.axis_index("section")
    loads = fetch(
        [
            (tokens.at[pack], hidden),
            *[(attend_far.at[:, i * 768 : i * 768 + 768], attend.at[:, i * 768 : i * 768 + 768]) for i in range(3)],
            (merging_far, merging),
            *[(expand_far.at[:, i * 1024 : i * 1024 + 1024], expand.at[:, i * 1024 : i * 1024 + 1024]) for i in range(3)],
            *[(shrink_far.at[i * 1024 : i * 1024 + 1024], shrink.at[i * 1024 : i * 1024 + 1024]) for i in range(3)],
        ],
        load_sem,
    )
    saves = []

    def save(*numbers):
        for number in numbers:
            copy = pltpu.make_async_copy(refs[9 + number], far[number], save_sem.at[number])
            copy.start()
            saves.append(copy)

    vectors[...] = jnp.zeros_like(vectors)
    key_chip = chip_of(4 * iota((TILE, 1), 0), sizes, pack)
    own_chip = chip_of(4 * iota((1, TILE), 1), sizes, pack)
    valid = (key_chip < 4).astype(F32)
    loads[0].wait()
    values = hidden[...]
    vectors[10:11, :768] = row_sum(valid * values * values)
    unit, _ = standardize(values)
    norm = low(unit * gains[0:1] + shifts[0:1])
    normed[...] = norm
    for part in range(3):
        cols = slice(part * 768, part * 768 + 768)
        loads[1 + part].wait()
        mix = dot(norm, attend[:, cols])
        mixed[:, cols] = low(mix)
        if part:
            turned[(part - 1) * 768 : part * 768] = low(mix.T)
    save(0, 1, 2)

    @pl.loop(0, 3)
    def _(step):
        def score(number):
            pair, half = 2 * step + number // 2, number % 2
            query = only(mixed[:, pair_lanes(pair)], half) * BF16(0.125)
            return dot_nt(mixed[:, pair_lanes(pair, 768)], query)

        ready = [score(0), score(1)]
        for number in range(4):
            if number + 2 < 4:
                ready.append(score(number + 2))
            pair, half = 2 * step + number // 2, number % 2
            scores = jnp.where(key_chip == own_chip, ready[number], NEGATIVE)
            expos = jnp.exp(scores - jnp.max(scores, axis=0, keepdims=True))
            prob = low(expos * (1.0 / jnp.sum(expos, axis=0, keepdims=True)))
            probs[pair * 2 + half] = prob
            context_turned[head_rows(pair, half)] = dot(turned[head_rows(pair, half, 768)], prob)

    mingled = low(context_turned[...].T)
    context[...] = mingled
    save(3, 4)
    loads[4].wait()
    attention = dot(mingled, merging[...]) + biases[0:1]
    vectors[11:12, :768] = row_sum(valid * attention * attention)
    center = hidden[...] + attention
    middle[...] = center
    unit, _ = standardize(center)
    norm = low(unit * gains[1:2] + shifts[1:2])
    normed_two[...] = norm
    save(5, 6)
    feed = jnp.zeros_like(center)
    def widened(part):
        if part % 2 == 0:
            loads[5 + part // 2].wait()
        cols = slice(part * 512, part * 512 + 512)
        return dot(norm, expand[:, cols]) + inner[:, cols]

    ready = [widened(0)]
    for part in range(6):
        if part < 5:
            ready.append(widened(part + 1))
        cols = slice(part * 512, part * 512 + 512)
        value, slant = gelu_pair(ready[part])
        value = low(value)
        active[:, cols] = value
        slope[part // 2, :, part % 2 * 512 : part % 2 * 512 + 512] = slant
        if part % 2 == 0:
            loads[8 + part // 2].wait()
        feed = feed + dot(value, shrink[cols])
    save(7, 8)
    feed = feed + biases[1:2]
    vectors[12:13, :768] = row_sum(valid * feed * feed)
    output = center + feed
    vectors[13:14, :768] = row_sum(valid * output * output)
    vectors[14:15, :768] = jnp.broadcast_to(row_sum(valid), (1, 768))
    sent[...] = low(output)
    for copy in saves:
        copy.wait()


def encoder_forward_call(sizes, tokens, gains, shifts, biases, attend, merging, expand, inner, shrink):
    shapes = (
        ((256, 768), BF16),
        ((256, 2304), BF16),
        ((1536, 256), BF16),
        ((12, 256, 256), BF16),
        ((256, 768), BF16),
        ((256, 768), F32),
        ((256, 768), BF16),
        ((256, 3072), BF16),
        ((3, 256, 1024), F32),
    )
    return pl.pallas_call(
        encoder_forward_kernel,
        out_shape=(jax.ShapeDtypeStruct((256, 768), BF16), jax.ShapeDtypeStruct((16, 1024), F32))
        + tuple(jax.ShapeDtypeStruct(*shape) for shape in shapes),
        in_specs=[smem_spec()] + [vmem_spec()] * 4 + [any_spec()] * 5,
        out_specs=(vmem_spec(),) * 2 + (any_spec(),) * len(shapes),
        scratch_shapes=[pltpu.VMEM(*shape) for shape in shapes]
        + [
            pltpu.VMEM((256, 768), F32),
            pltpu.VMEM(attend.shape, BF16),
            pltpu.VMEM(merging.shape, BF16),
            pltpu.VMEM(expand.shape, BF16),
            pltpu.VMEM(shrink.shape, BF16),
            pltpu.VMEM((768, 256), F32),
            pltpu.SemaphoreType.DMA((11,)),
            pltpu.SemaphoreType.DMA((len(shapes),)),
        ],
        compiler_params=pltpu.CompilerParams(vmem_limit_bytes=60 * 2**20),
        name="encoder_forward",
    )(sizes, gains, shifts, biases, inner[None], tokens, attend, merging, expand, shrink)


def decoder_kernel(
    reduce, sizes, distance, slots, frequency, sent, biases, mask_token, gains, shifts, inner,
    cotangent, entry_far, attend_far, merging_far, expand_far, shrink_far,
    summed, rest, vectors, encoded_grad, *refs,
):
    (
        table, start, normed, mixed, turned, probs, flipped, context, normed_two, active,
        before_grad, go_low, attention_low, context_grad, delta, mixed_grad, target, masked_keys,
        entry_weight, attend, merging, expand, shrink, load_sem,
    ) = refs[:24]
    pack = lax.axis_index("section")
    if reduce:
        mine, partner = neighbours()
        greet(partner)
        engine = reducer(DECODER_PLAN, mine, partner, summed, refs[24:])
        put = engine.put
    else:
        put = put_into(summed)
    put_rest = put_into(rest)
    loads = fetch(
        [
            (entry_far, entry_weight),
            (attend_far, attend),
            (cotangent.at[pack], target),
            (merging_far, merging),
            (expand_far, expand),
            (shrink_far, shrink),
        ],
        load_sem,
    )
    tiles = start.shape[0] // TILE
    vectors[...] = jnp.zeros_like(vectors)
    large = sizes[pack, 0] == 1024

    def add_row(row, value):
        vectors[row : row + 1, :] += value

    positions = iota((32, 128), 0).astype(F32)
    for chip in range(4):
        spacing = distance[pack, chip].astype(F32) / 16.0
        angle = positions * (spacing * frequency[...])
        table[0, chip] = jnp.sin(angle)
        table[1, chip] = jnp.cos(angle)
    loads[0].wait()
    entry = low(dot(sent[...], entry_weight[...]) + biases[0:1])
    loads[1].wait()

    blocks = start.shape[0] // BLOCK

    def slot_chip(tile, size):
        return chip_of(iota((size, 1), 0) + tile * size, sizes, pack)

    def validity(tile, size):
        return (slot_chip(tile, size) < 4).astype(F32)

    def spread_of(tile):
        return (slots[pl.ds(pack, 1)] == iota((TILE, TILE), 0) + tile * TILE).astype(F32)

    def encoding_of(tile):
        pieces = []
        for kind in range(2):
            wave = table[kind, 0, aligned(tile * 8, 8, 8)]
            big = jnp.broadcast_to(wave[:, None], (8, 32, 128)).reshape(TILE, 128)
            wave = table[kind, tile, 0:16]
            own = jnp.broadcast_to(wave[:, None], (16, 16, 128)).reshape(TILE, 128)
            pieces.append(jnp.where(large, big, own))
        for kind in range(2):
            wave = table[kind, 0]
            big = jnp.broadcast_to(wave[None], (8, 32, 128)).reshape(TILE, 128)
            wave = table[kind, tile, 0:16]
            own = jnp.broadcast_to(wave[None], (16, 16, 128)).reshape(TILE, 128)
            pieces.append(jnp.where(large, big, own))
        return jnp.concatenate(pieces, axis=1)

    @pl.loop(0, tiles)
    def _(tile):
        rows = rows_of(tile)
        valid = validity(tile, TILE)
        spread = spread_of(tile)
        fill = valid * (1.0 - jnp.sum(spread, axis=1, keepdims=True))
        hidden = dot(low(spread), entry) + fill * mask_token[...] + encoding_of(tile) * valid
        start[rows] = hidden
        add_row(12, row_sum(valid * hidden * hidden))
        add_row(16, row_sum(valid))
        unit, _ = standardize(hidden)
        norm = low(unit * gains[0:1] + shifts[0:1])
        normed[rows] = norm
        mix = dot(norm, attend[...])
        mix_low = low(mix)
        mixed[rows] = mix_low
        turned[:, rows] = low(mix[:, 256:].T)
        lane = iota((TILE, 128), 1)
        other = (lane % 64 < 5) & (lane % 64 != slot_chip(tile, TILE))
        other = jnp.where(other, NEGATIVE, 0.0).astype(BF16)
        for head in range(4):
            lanes = slice(256 + head // 2 * 128, 384 + head // 2 * 128)
            masked_keys[head, rows] = jnp.where(lane // 64 == head % 2, mix_low[:, lanes], other)

    @pl.loop(0, 2 * tiles)
    def _(step):
        pair, tile = step // tiles, step % tiles
        rows = rows_of(tile)
        lane = iota((TILE, 128), 1)
        chosen = (lane % 64 == slot_chip(tile, TILE)).astype(F32).astype(BF16)
        for half in range(2):
            query = jnp.where(lane // 64 == half, mixed[rows, pair_lanes(pair)] * BF16(0.125), chosen)
            scores = dot_nt(masked_keys[pair * 2 + half], query)
            expos = jnp.exp(scores - jnp.max(scores, axis=0, keepdims=True))
            prob = low(expos * (1.0 / jnp.sum(expos, axis=0, keepdims=True)))
            probs[pair * 2 + half, :, rows] = prob
            flipped[head_rows(pair, half), rows] = dot(turned[head_rows(pair, half, 256)], prob)

    for copy in loads[2:]:
        copy.wait()

    @pl.loop(0, blocks)
    def _(tile):
        rows = rows_of(tile, BLOCK)
        valid = validity(tile, BLOCK)
        mingled_wide = flipped[:, rows].T
        mingled = low(mingled_wide)
        context[rows] = mingled
        attention = dot(mingled, merging[...]) + biases[1:2]
        add_row(13, row_sum(valid * attention * attention))
        center = start[rows] + attention
        unit, inverse = standardize(center)
        norm = low(unit * gains[1:2] + shifts[1:2])
        normed_two[rows] = norm
        go = target[rows] * valid
        go_below = low(go)
        go_low[rows] = go_below
        add_row(2, row_sum(go))
        feed = jnp.zeros_like(go)
        norm_grad = jnp.zeros_like(go)
        for part in range(8):
            cols = slice(part * 256, part * 256 + 256)
            before = dot(norm, expand[:, cols]) + inner[:, cols]
            value, slope = gelu_pair(before)
            value = low(value)
            active[rows, cols] = value
            feed = feed + dot(value, shrink[cols])
            grad = low(slope * dot_nt(go_below, shrink[cols]))
            before_grad[rows, cols] = grad
            lanes = slice(part % 2 * 256, part % 2 * 256 + 256)
            vectors[8 + part // 2 : 9 + part // 2, lanes] += row_sum(grad.astype(F32))
            norm_grad = norm_grad + dot_nt(grad, expand[:, cols])
        feed = feed + biases[2:3]
        add_row(14, row_sum(valid * feed * feed))
        output = center + feed
        add_row(15, row_sum(valid * output * output))
        add_row(5, row_sum(norm_grad * unit))
        add_row(7, row_sum(norm_grad))
        grad = go + norm_back(unit, inverse, gains[1:2], norm_grad)
        target[rows] = grad
        add_row(1, row_sum(grad))
        below = low(grad)
        attention_low[rows] = below
        outer = low(dot_nt(below, merging[...]))
        context_grad[rows] = outer
        product = (outer.astype(F32) * mingled_wide).T
        for head in range(4):
            delta[head, :, rows] = row_sum(product[head * 64 : head * 64 + 64])

    for part in range(2):
        cols = slice(part * 256, part * 256 + 256)
        store_packed(put, part * 16, DECODER_EXPAND, dot_tn(normed_two[:, cols], before_grad[...]))
        value = dot_tn(attention_low[:, cols], context[...])
        store_packed(put, part * 16, DECODER_MERGE, value)
    for block in range(2):
        put(slice(block * 16, block * 16 + 16), 4352, jnp.zeros((16, 16, DECODER_PLAN.chunks * DECODER_PLAN.span - 4352), F32))
    if reduce:
        await_greetings()
        engine.send(2048)

    @pl.loop(0, 8)
    def _(part):
        cols = aligned(part * 256, 256, 256)
        store_packed(put, part * 4, DECODER_SHRINK, dot_tn(active[:, cols], go_low[...]))

    if reduce:
        engine.send(DECODER_PLAN.chunks * DECODER_PLAN.span)

    flipped[...] = jnp.zeros_like(flipped)

    @pl.loop(0, 2 * tiles)
    def _(step):
        pair, tile = step // tiles, step % tiles
        rows = rows_of(tile)
        lanes = pair_lanes(pair)
        values = mixed[rows, pair_lanes(pair, 512)]
        raws, probabilities, queries, outers = [], [], [], []
        for half in range(2):
            prob = probs[pair * 2 + half, rows]
            outer = only(context_grad[:, lanes], half)
            raw = low(prob.astype(F32) * (dot_nt(values, outer) - delta[pair * 2 + half]))
            flipped[head_rows(pair, half)] += dot(turned[head_rows(pair, half), rows], raw)
            raws.append(raw)
            probabilities.append(prob)
            outers.append(outer)
            queries.append(only(mixed[:, lanes], half))
        key_grad = dot(jnp.concatenate(raws, axis=1), jnp.concatenate(queries, axis=0))
        mixed_grad[rows, pair_lanes(pair, 256)] = low(key_grad * 0.125)
        value_grad = dot(jnp.concatenate(probabilities, axis=1), jnp.concatenate(outers, axis=0))
        mixed_grad[rows, pair_lanes(pair, 512)] = low(value_grad)
        if reduce:
            engine.turn(step)

    def last(tile, entry_grad):
        rows = rows_of(tile)
        mixed_grad[rows, 0:256] = low(flipped[:, rows].T * 0.125)
        norm_grad = dot_nt(mixed_grad[rows], attend[...])
        unit, inverse = standardize(start[rows])
        add_row(4, row_sum(norm_grad * unit))
        add_row(6, row_sum(norm_grad))
        grad = target[rows] + norm_back(unit, inverse, gains[0:1], norm_grad)
        spread = spread_of(tile)
        fill = validity(tile, TILE) * (1.0 - jnp.sum(spread, axis=1, keepdims=True))
        add_row(3, row_sum(fill * grad))
        if reduce:
            engine.turn(2 * tiles + tile)
        return entry_grad + dot_tn(low(spread), low(grad))

    entry_grad = lax.fori_loop(0, tiles, last, jnp.zeros((TILE, 512), F32))
    add_row(0, row_sum(entry_grad))
    entry_low = low(entry_grad)
    encoded_grad[...] = low(dot_nt(entry_low, entry_weight[...]))
    store_packed(put_rest, 0, ENTRY, dot_tn(sent[...], entry_low))

    @pl.loop(0, 3)
    def _(part):
        if reduce:
            engine.turn(3 * tiles + part)

        @pl.when(part < 2)
        def _():
            cols = aligned(part * 256, 256, 256)
            store_packed(put_rest, part * 16, DECODER_ATTEND, dot_tn(normed[:, cols], mixed_grad[...]))

    if reduce:
        engine.close()


def decoder_call(
    reduce, sizes, distance, slots, sent, cotangent, entry_weight, biases, mask_token,
    gains, shifts, attend, merging, expand, inner, shrink,
):
    length = cotangent.shape[1]
    width = 512
    frequency = np.exp(-np.log(10000.0) * np.arange(width // 4) / (width // 4)).astype(np.float32)
    if reduce:
        summed = jax.ShapeDtypeStruct((DECODER_PLAN.chunks, 16, DECODER_PLAN.span), F32)
        extra = reducer_scratch(DECODER_PLAN)
        params = dict(collective_id=1, has_side_effects=True)
    else:
        summed = jax.ShapeDtypeStruct((DECODER_PLAN.chunks, 2, 16, 16, DECODER_PLAN.span), BF16)
        extra = []
        params = dict()
    return pl.pallas_call(
        functools.partial(decoder_kernel, reduce),
        out_shape=(
            summed,
            jax.ShapeDtypeStruct((1, 2, 16, 16, UNIT), BF16),
            jax.ShapeDtypeStruct((24, width), F32),
            jax.ShapeDtypeStruct((256, 768), BF16),
        ),
        in_specs=[smem_spec()] * 2 + [vmem_spec()] * 8 + [any_spec()] * 6,
        out_specs=(vmem_spec(),) * 4,
        scratch_shapes=[
            pltpu.VMEM((2, 4, 32, 128), F32),
            pltpu.VMEM((length, width), F32),
            pltpu.VMEM((length, width), BF16),
            pltpu.VMEM((length, 768), BF16),
            pltpu.VMEM((512, length), BF16),
            pltpu.VMEM((4, length, length), BF16),
            pltpu.VMEM((256, length), F32),
            pltpu.VMEM((length, 256), BF16),
            pltpu.VMEM((length, width), BF16),
            pltpu.VMEM((length, 2048), BF16),
            pltpu.VMEM((length, 2048), BF16),
            pltpu.VMEM((length, width), BF16),
            pltpu.VMEM((length, width), BF16),
            pltpu.VMEM((length, 256), BF16),
            pltpu.VMEM((4, 1, length), F32),
            pltpu.VMEM((length, 768), BF16),
            pltpu.VMEM((length, width), F32),
            pltpu.VMEM((4, length, 128), BF16),
            pltpu.VMEM(entry_weight.shape, BF16),
            pltpu.VMEM(attend.shape, BF16),
            pltpu.VMEM(merging.shape, BF16),
            pltpu.VMEM(expand.shape, BF16),
            pltpu.VMEM(shrink.shape, BF16),
            pltpu.SemaphoreType.DMA((6,)),
        ]
        + extra,
        compiler_params=pltpu.CompilerParams(vmem_limit_bytes=63 * 2**20, **params),
        name="decoder_block",
    )(
        sizes, distance, slots, jnp.asarray(frequency)[None], sent, biases, mask_token[None], gains, shifts,
        inner[None], cotangent, entry_weight, attend, merging, expand, shrink,
    )


def encoder_backward_kernel(
    reduce, encoded_grad, sums, decoder_vectors, gains, tokens, rest, attend_far, merging_far, expand_far,
    shrink_far, normed_far, mixed_far, turned_far, probs_far, context_far, middle_far, normed_two_far, active_far,
    slope_far, summed, vectors, tokens_grad, *refs,
):
    if reduce:
        decoder_sums, arrived = refs[:2]
        refs = refs[2:]
    (
        hidden, attend, merging, expand, shrink, normed, mixed, turned, probs, context, middle, normed_two, active,
        slope, before_grad, norm_sum, attention_low, context_grad, key_grad, query_turned, mixed_grad, active_turned,
        flipped, inner_sum, load_sem, part_sem,
    ) = refs[:26]
    pack = lax.axis_index("section")

    def part_loads(part):
        cols = aligned(part * 1024, 1024, 1024)
        slot = part % 2
        return [
            pltpu.make_async_copy(expand_far.at[:, cols], expand.at[slot], part_sem.at[slot, 0]),
            pltpu.make_async_copy(shrink_far.at[cols], shrink.at[slot], part_sem.at[slot, 1]),
            pltpu.make_async_copy(slope_far.at[part], slope.at[slot], part_sem.at[slot, 2]),
        ]

    if reduce:
        (
            decoder_total, encoder_total, decoder_got, encoder_got, payload,
            own_sem, small_send, small_recv, pay_send, pay_recv, small_load,
        ) = refs[26:37]
        mine, partner = neighbours()
        greet(partner)
        engine = reducer(ENCODER_PLAN, mine, partner, summed, refs[37:])
        put = engine.put
        engine.release(UNIT)
        first_own = fetch(
            [
                pair
                for pair in (
                    (rest.at[0, 1 - mine["c"]], engine.staging.at[0]),
                    (rest.at[0, mine["c"]], engine.own.at[0]),
                )
            ],
            own_sem,
        )
        decoder_load = pltpu.make_async_copy(decoder_vectors, decoder_total.at[0], small_load)
        decoder_load.start()
    else:
        put = put_into(summed)
    early = pltpu.make_async_copy(active_far, active, load_sem.at[10])
    early.start()
    for copy in part_loads(0):
        copy.start()
    if reduce:
        for copy in first_own:
            copy.wait()
        await_greetings()
        engine.send(UNIT)
    loads = fetch(
        [
            (normed_two_far, normed_two),
            (middle_far, middle),
            (merging_far, merging),
            (context_far, context),
            (mixed_far, mixed),
            (probs_far, probs),
            (turned_far.at[0:768], turned),
            (normed_far, normed),
            (attend_far, attend),
            (tokens.at[pack], hidden),
        ],
        load_sem,
    )
    for copy in part_loads(1):
        copy.start()
    vectors[...] = sums[...]
    go_low = encoded_grad[...]
    go = go_low.astype(F32)
    vectors[1:2, :768] = row_sum(go)
    norm_sum[...] = jnp.zeros_like(norm_sum)

    def send(unit):
        if reduce:
            engine.send((unit + 1) * UNIT)

    def release(unit):
        if reduce:
            engine.release((unit + 1) * UNIT)

    def shrink_start():
        early.wait()
        for piece in range(4):
            rows = slice(piece * 768, piece * 768 + 768)
            active_turned[rows] = active[:, rows].T

    def shrink_grad(part):
        release(1 + part)
        cols = slice(part * 256, part * 256 + 256)
        for piece in range(4):
            rows = slice(piece * 768, piece * 768 + 768)
            store_packed(put, piece * 8, ENCODER_SHRINK[part], dot(active_turned[rows], encoded_grad[:, cols]))
        send(1 + part)

    def hidden_layer(part):
        for copy in part_loads(part):
            copy.wait()
        slot = part % 2
        grad = low(slope[slot] * dot_nt(encoded_grad[...], shrink[slot]))
        before_grad[...] = grad
        inner_sum[part] = row_sum(grad.astype(F32))
        norm_sum[...] += dot_nt(grad, expand[slot])

        @pl.when(part == 0)
        def _():
            for copy in part_loads(2):
                copy.start()

    def expand_grad(part):
        release(4 + part)
        if part == 0:
            loads[0].wait()
            flipped[...] = normed_two[...].T
        store_packed(put, 0, ENCODER_EXPAND[part], dot(flipped[...], before_grad[...]))
        send(4 + part)

    def middle_layer():
        loads[1].wait()
        loads[2].wait()
        for part in range(3):
            vectors[6 + part : 7 + part] = inner_sum[part]
        unit, inverse = standardize(middle[...])
        norm_grad = norm_sum[...]
        vectors[3:4, :768] = row_sum(norm_grad * unit)
        vectors[5:6, :768] = row_sum(norm_grad)
        grad = encoded_grad[...].astype(F32) + norm_back(unit, inverse, gains[1:2], norm_grad)
        vectors[0:1, :768] = row_sum(grad)
        tokens_grad[...] = grad
        below = low(grad)
        attention_low[...] = below
        context_grad[...] = low(dot_nt(below, merging[...]))
        for copy in loads[3:7]:
            copy.wait()

    def attention(first):
        @pl.loop(first, first + 2)
        def _(pair):
            lanes = pair_lanes(pair)
            values = mixed[:, pair_lanes(pair, 1536)]
            keys_total = jnp.zeros((TILE, 128), F32)
            values_total = jnp.zeros((TILE, 128), F32)
            for half in range(2):
                prob = probs[pair * 2 + half]
                outer = only(context_grad[:, lanes], half)
                query = only(mixed[:, lanes], half)
                wide = prob.astype(F32)
                grad = dot_nt(values, outer)
                raw = low(wide * (grad - jnp.sum(wide * grad, axis=0, keepdims=True)))
                keys_total = keys_total + dot(raw, query)
                values_total = values_total + dot(prob, outer)
                rows = head_rows(pair, half)
                query_turned[rows] = dot(turned[rows], raw)
            key_grad[0, :, lanes] = keys_total
            key_grad[1, :, lanes] = values_total

    def mixing():
        mixed_grad[:, 0:768] = low(query_turned[...].T * 0.125)
        mixed_grad[:, 768:1536] = low(key_grad[0] * 0.125)
        mixed_grad[:, 1536:2304] = low(key_grad[1])

    def attend_grad(part):
        if part == 0:
            loads[7].wait()
            flipped[...] = normed[...].T
        release(7 + part)
        wide = slice(part * 1024, min(part * 1024 + 1024, 2304))
        store_packed(put, 0, ENCODER_ATTEND[part], dot(flipped[...], mixed_grad[:, wide]))
        if part == 2:
            store_packed(put, 0, ENCODER_MERGE, dot_tn(attention_low[...], context[...]))
        send(7 + part)

    def input_layer():
        loads[8].wait()
        loads[9].wait()
        norm_grad = dot_nt(mixed_grad[...], attend[...])
        unit, inverse = standardize(hidden[...])
        vectors[2:3, :768] = row_sum(norm_grad * unit)
        vectors[4:5, :768] = row_sum(norm_grad)
        grad = tokens_grad[...] + norm_back(unit, inverse, gains[0:1], norm_grad)
        tokens_grad[...] = grad
        if reduce:
            payload[...] = low(grad)

    if not reduce:
        shrink_start()
        for part in range(3):
            shrink_grad(part)
        for part in range(3):
            hidden_layer(part)
            expand_grad(part)
        middle_layer()
        for first in (0, 2, 4):
            attention(first)
        mixing()
        for part in range(3):
            attend_grad(part)
        input_layer()
        return

    def exchange(source, piece):
        rows = aligned(piece * 32, 32, 32)
        return remote(source.at[rows], arrived.at[rows], pay_send.at[piece], pay_recv.at[piece], partner["x"])

    small_route = ("c",) + ROUTES[0]
    totals = ((decoder_total, decoder_got), (encoder_total, encoder_got))

    def small_copy(stage, kind):
        source, target = totals[kind]
        return remote(
            source.at[stage],
            target.at[stage],
            small_send.at[stage, kind],
            small_recv.at[stage, kind],
            partner[small_route[stage]],
        )

    def small_advance(stage):
        if stage == 0:
            encoder_total[0] = vectors[...]
        for kind in range(2):
            source, target = totals[kind]
            if stage > 0:
                small_copy(stage - 1, kind).wait_recv()
                source[stage] = source[stage - 1] + target[stage - 1]
            if stage < 5:
                small_copy(stage, kind).start()

    shrink_start()
    shrink_grad(0)
    decoder_load.wait()

    def expand_end():
        expand_grad(2)
        middle_layer()

    def attention_all():
        @pl.loop(0, 3)
        def _(step):
            attention(2 * step)

        mixing()

    def attend_start():
        attend_grad(0)
        attend_grad(1)

    def attend_end():
        attend_grad(2)
        input_layer()

    part = functools.partial
    works = {
        0: part(shrink_grad, 1),
        1: part(shrink_grad, 2),
        2: part(expand_grad, 0),
        3: part(expand_grad, 1),
        4: expand_end,
        5: attention_all,
        6: attend_start,
        7: attend_end,
    }
    turns = ENCODER_PLAN.chunks + 4 * LAG
    works.update({turns - 10 + stage + max(0, stage - 1): part(small_advance, stage) for stage in range(6)})

    @pl.loop(0, turns)
    def _(number):
        engine.turn(number)

        for position, work in works.items():
            pl.when(number == position)(work)

        @pl.when((number >= 1) & (number <= 3))
        def _():
            hidden_layer(number - 1)

        @pl.when((pack == 0) & (number < 8))
        def _():
            exchange(encoded_grad, number).start()

        @pl.when((pack == 1) & (number >= 8) & (number < 16))
        def _():
            exchange(payload, number - 8).start()

    for stage in range(5):
        for kind in range(2):
            small_copy(stage, kind).wait_send()
    for piece in range(8):
        exchange(payload, piece).wait()
    engine.close()
    vectors[...] = encoder_total[5]
    decoder_sums[...] = decoder_total[5]


def encoder_backward_call(reduce, tokens, encoded_grad, sums, decoder_vectors, rest, kept, gains, attend, merging, expand, shrink):
    if reduce:
        summed = jax.ShapeDtypeStruct((ENCODER_PLAN.chunks, 16, UNIT), F32)
        more = (
            jax.ShapeDtypeStruct(decoder_vectors.shape, F32),
            jax.ShapeDtypeStruct((256, 768), BF16),
        )
        more_specs = (vmem_spec(), any_spec())
        extra = [
            pltpu.VMEM((6,) + decoder_vectors.shape, F32),
            pltpu.VMEM((6,) + sums.shape, F32),
            pltpu.VMEM((5,) + decoder_vectors.shape, F32),
            pltpu.VMEM((5,) + sums.shape, F32),
            pltpu.VMEM((256, 768), BF16),
            pltpu.SemaphoreType.DMA((2,)),
            pltpu.SemaphoreType.DMA((5, 2)),
            pltpu.SemaphoreType.DMA((5, 2)),
            pltpu.SemaphoreType.DMA((8,)),
            pltpu.SemaphoreType.DMA((8,)),
            pltpu.SemaphoreType.DMA,
        ] + reducer_scratch(ENCODER_PLAN)
        params = dict(collective_id=2, has_side_effects=True)
    else:
        summed = jax.ShapeDtypeStruct((ENCODER_PLAN.chunks, 2, 16, 16, UNIT), BF16)
        more, more_specs, extra, params = (), (), [], dict()
    return pl.pallas_call(
        functools.partial(encoder_backward_kernel, reduce),
        out_shape=(
            summed,
            jax.ShapeDtypeStruct(sums.shape, F32),
            jax.ShapeDtypeStruct((256, 768), F32),
        )
        + more,
        in_specs=[vmem_spec()] * 2 + [any_spec(), vmem_spec()] + [any_spec()] * 15,
        out_specs=(vmem_spec(),) * 3 + more_specs,
        scratch_shapes=[
            pltpu.VMEM((256, 768), F32),
            pltpu.VMEM(attend.shape, BF16),
            pltpu.VMEM(merging.shape, BF16),
            pltpu.VMEM((2, 768, 1024), BF16),
            pltpu.VMEM((2, 1024, 768), BF16),
            pltpu.VMEM((256, 768), BF16),
            pltpu.VMEM((256, 2304), BF16),
            pltpu.VMEM((768, 256), BF16),
            pltpu.VMEM((12, 256, 256), BF16),
            pltpu.VMEM((256, 768), BF16),
            pltpu.VMEM((256, 768), F32),
            pltpu.VMEM((256, 768), BF16),
            pltpu.VMEM((256, 3072), BF16),
            pltpu.VMEM((2, 256, 1024), F32),
            pltpu.VMEM((256, 1024), BF16),
            pltpu.VMEM((256, 768), F32),
            pltpu.VMEM((256, 768), BF16),
            pltpu.VMEM((256, 768), BF16),
            pltpu.VMEM((2, 256, 768), F32),
            pltpu.VMEM((768, 256), F32),
            pltpu.VMEM((256, 2304), BF16),
            pltpu.VMEM((3072, 256), BF16),
            pltpu.VMEM((768, 256), BF16),
            pltpu.VMEM((3, 1, 1024), F32),
            pltpu.SemaphoreType.DMA((11,)),
            pltpu.SemaphoreType.DMA((2, 3)),
        ]
        + extra,
        compiler_params=pltpu.CompilerParams(vmem_limit_bytes=60 * 2**20, **params),
        name="encoder_backward",
    )(encoded_grad, sums, decoder_vectors, gains, tokens, rest, attend, merging, expand, shrink, *kept)


def unpack(packed, place):
    span = packed.shape[-1]

    def take(start, size):
        pieces = []
        while size:
            chunk, first = divmod(start, span)
            length = min(size, span - first)
            pieces.append(packed[chunk, ..., first : first + length])
            start, size = start + length, size - length
        return pieces[0] if len(pieces) == 1 else jnp.concatenate(pieces, axis=-1)

    offset, count, width = place
    pieces = [take(offset + i * width, width) for i in range(count // 16)]
    if count % 16:
        rest = take(offset + count // 16 * width, width // 2)
        pieces.append(jnp.concatenate([rest[..., :8, :], rest[..., 8:, :]], axis=-1))
    return pieces[0] if len(pieces) == 1 else jnp.concatenate(pieces, axis=-2)


def finish_kernel(
    decoder_summed_far, decoder_sums_far, encoder_sums_far, summed_far, arrived_far, tokens_grad_far, encoded_grad_far,
    boundary, statistics, e_gains, e_shifts, e_biases, e_attend, e_merge, e_expand, e_inner, e_shrink,
    d_entry, d_biases, mask_grad, d_gains, d_shifts, d_attend, d_merge, d_expand, d_inner, d_shrink,
    decoder_summed, decoder_sums, encoder_sums, summed, arrived, tokens_grad, encoded_grad, load_sem,
):
    section = lax.axis_index("section")
    loads = fetch(
        [
            (decoder_summed_far, decoder_summed),
            (decoder_sums_far, decoder_sums),
            (encoder_sums_far, encoder_sums),
            (summed_far, summed),
            (arrived_far, arrived),
            (tokens_grad_far, tokens_grad),
            (encoded_grad_far, encoded_grad),
        ],
        load_sem,
    )
    number = section * lax.axis_size("dp") + lax.axis_index("dp")

    def own(rows, count):
        width = rows.shape[1]
        return pltpu.roll(rows, (width - number * count) % width, axis=1)[:, :count]

    def own_line(rows, count):
        return own(jnp.concatenate([rows[i : i + 1] for i in range(rows.shape[0])], axis=1), count)

    for copy in loads[:3]:
        copy.wait()
    lane = iota((1, 128), 1)
    values = jnp.zeros((1, 128), F32)
    for sums, width, first, count_row, base in ((encoder_sums, DE, 10, 14, 0), (decoder_sums, DD, 12, 16, 4)):
        scale = 1.0 / (sums[count_row : count_row + 1, 0:1] * width)
        for i in range(4):
            value = jnp.sum(sums[first + i : first + i + 1, :], axis=1, keepdims=True) * scale
            values = jnp.where(lane == base + i, value, values)
    statistics[...] = jnp.sqrt(values)[:, :8]
    rows = own(encoder_sums[0:8, :DE], 24)
    e_biases[...] = rows[0:2]
    e_gains[...] = rows[2:4]
    e_shifts[...] = rows[4:6]
    e_inner[...] = own_line(encoder_sums[6:9], 96)
    rows = own(decoder_sums[0:8], 16)
    d_biases[...] = rows[0:3]
    mask_grad[...] = rows[3:4]
    d_gains[...] = rows[4:6]
    d_shifts[...] = rows[6:8]
    d_inner[...] = own_line(decoder_sums[8:12], 64)

    d_merge[...] = unpack(decoder_summed, DECODER_MERGE)
    d_expand[...] = unpack(decoder_summed, DECODER_EXPAND)
    d_shrink[...] = unpack(decoder_summed, DECODER_SHRINK)
    loads[3].wait()
    d_entry[...] = unpack(summed, ENTRY)
    d_attend[...] = unpack(summed, DECODER_ATTEND)
    for target, places in ((e_expand, ENCODER_EXPAND), (e_attend, ENCODER_ATTEND), (e_shrink, ENCODER_SHRINK)):
        start = 0
        for place in places:
            target[:, start : start + place[2]] = unpack(summed, place)
            start += place[2]
    e_merge[...] = unpack(summed, ENCODER_MERGE)
    for copy in loads[4:]:
        copy.wait()

    @pl.when(section == 0)
    def _():
        boundary[0, 0] = tokens_grad[...]
        boundary[0, 1] = arrived[...].astype(F32)

    @pl.when(section == 1)
    def _():
        boundary[0, 0] = arrived[...].astype(F32)
        boundary[0, 1] = encoded_grad[...].astype(F32)


def finish_call(*operands):
    shapes = (
        (1, 2, 256, 768), (1, 8), (2, 24), (2, 24), (2, 24), (24, 2304), (24, 768), (24, 3072), (1, 96), (96, 768),
        (24, 512), (3, 16), (1, 16), (2, 16), (2, 16), (16, 768), (16, 256), (16, 2048), (1, 64), (64, 512),
    )
    outs = list(
        pl.pallas_call(
            finish_kernel,
            out_shape=tuple(jax.ShapeDtypeStruct(shape, F32) for shape in shapes),
            in_specs=[any_spec()] * len(operands),
            out_specs=(vmem_spec(),) * len(shapes),
            scratch_shapes=[pltpu.VMEM(operand.shape, operand.dtype) for operand in operands]
            + [pltpu.SemaphoreType.DMA((len(operands),))],
            compiler_params=pltpu.CompilerParams(vmem_limit_bytes=60 * 2**20),
            name="finish",
        )(*operands)
    )
    for line in (1, 8, 12, 18):
        outs[line] = outs[line].reshape(-1)
    for turned in (6, 16):
        outs[turned] = outs[turned].T
    return tuple(outs)


def scatter_sum(member, share_dim):
    return lax.psum_scatter(
        member, ("section", "dp"), scatter_dimension=share_dim, tiled=True
    )


def finish_generic(decoder_part, part, decoder_sums, encoder_sums, tokens_grad, encoded_grad):
    section = lax.axis_index("section")
    payload = jnp.where(section == 0, encoded_grad, low(tokens_grad))

    def whole(packed, *places):
        packed = jnp.swapaxes(packed, 1, 2).reshape(-1, 32, 16, packed.shape[-1])
        blocks = [unpack(packed, place).reshape(32 * place[1], place[2]) for place in places]
        return scatter_sum(jnp.concatenate(blocks, axis=1).astype(F32), 0)

    def line(value):
        return scatter_sum(value, value.ndim - 1)

    arrived = lax.ppermute(payload, "section", [(0, 1), (1, 0)]).astype(F32)
    boundary = jnp.where(
        section == 0,
        jnp.stack([tokens_grad, arrived]),
        jnp.stack([arrived, encoded_grad.astype(F32)]),
    )
    sums = jnp.concatenate(
        [jnp.sum(encoder_sums[10:14], axis=1), jnp.sum(decoder_sums[12:16], axis=1)]
    )
    sums, counts = lax.psum((sums, (encoder_sums[14, 0], decoder_sums[16, 0])), ("section", "dp"))
    scales = jnp.concatenate([jnp.full((4,), counts[0] * DE), jnp.full((4,), counts[1] * DD)])
    return (
        boundary[None],
        jnp.sqrt(sums / scales),
        line(encoder_sums[2:4, :DE]),
        line(encoder_sums[4:6, :DE]),
        line(encoder_sums[0:2, :DE]),
        whole(part, *ENCODER_ATTEND),
        whole(part, ENCODER_MERGE).T,
        whole(part, *ENCODER_EXPAND),
        line(encoder_sums[6:9].reshape(-1)),
        whole(part, *ENCODER_SHRINK),
        whole(decoder_part[1], ENTRY),
        line(decoder_sums[0:3]),
        line(decoder_sums[3]),
        line(decoder_sums[4:6]),
        line(decoder_sums[6:8]),
        whole(decoder_part[1], DECODER_ATTEND),
        whole(decoder_part[0], DECODER_MERGE).T,
        whole(decoder_part[0], DECODER_EXPAND),
        line(decoder_sums[8:12].reshape(-1)),
        whole(decoder_part[0], DECODER_SHRINK),
    )


def body(
    visible_tokens,
    cotangent,
    chip_sizes,
    ground_distance,
    visible_slots,
    encoder_gains,
    encoder_shifts,
    encoder_biases,
    encoder_attend,
    encoder_merge,
    encoder_expand,
    encoder_inner,
    encoder_shrink,
    decoder_entry,
    decoder_biases,
    mask_token,
    decoder_gains,
    decoder_shifts,
    decoder_attend,
    decoder_merge,
    decoder_widen_weight,
    decoder_inner,
    decoder_shrink,
):
    reduce = (lax.axis_size("section"), lax.axis_size("dp")) == (2, 16)
    sent, sums, *kept = encoder_forward_call(
        chip_sizes, visible_tokens, encoder_gains, encoder_shifts, encoder_biases,
        encoder_attend, encoder_merge, encoder_expand, encoder_inner, encoder_shrink,
    )
    decoder_summed, rest, decoder_vectors, encoded_grad = decoder_call(
        reduce, chip_sizes, ground_distance, visible_slots, sent, cotangent, decoder_entry, decoder_biases, mask_token,
        decoder_gains, decoder_shifts, decoder_attend, decoder_merge, decoder_widen_weight, decoder_inner,
        decoder_shrink,
    )
    summed, encoder_sums, tokens_grad, *more = encoder_backward_call(
        reduce, visible_tokens, encoded_grad, sums, decoder_vectors, rest, kept,
        encoder_gains, encoder_attend, encoder_merge, encoder_expand, encoder_shrink,
    )
    if reduce:
        decoder_sums, arrived = more
        return finish_call(
            decoder_summed, decoder_sums, encoder_sums, summed, arrived, tokens_grad, encoded_grad
        )
    return finish_generic(
        (decoder_summed, rest), summed, decoder_vectors, encoder_sums, tokens_grad, encoded_grad
    )


def solution(mesh):
    in_specs = (
        P("dp", None, None),
        P("dp", None, None),
        P("dp", None),
        P("dp", None),
        P("dp", None),
        P(),
        P(),
        P(),
        P(),
        P(),
        P(),
        P(),
        P(),
        P(),
        P(),
        P(),
        P(),
        P(),
        P(),
        P(),
        P(),
        P(),
        P(),
    )
    out_specs = (
        P("section", "dp", None, None),
        P(),
        P(None, ("section", "dp")),
        P(None, ("section", "dp")),
        P(None, ("section", "dp")),
        P(("section", "dp"), None),
        P(None, ("section", "dp")),
        P(("section", "dp"), None),
        P(("section", "dp")),
        P(("section", "dp"), None),
        P(("section", "dp"), None),
        P(None, ("section", "dp")),
        P(("section", "dp")),
        P(None, ("section", "dp")),
        P(None, ("section", "dp")),
        P(("section", "dp"), None),
        P(None, ("section", "dp")),
        P(("section", "dp"), None),
        P(("section", "dp")),
        P(("section", "dp"), None),
    )
    return jax.shard_map(body, mesh=mesh, in_specs=in_specs, out_specs=out_specs, check_vma=False)
```

```python
import functools
import types

import jax
import jax.numpy as jnp
import numpy as np
from jax import lax
from jax.experimental import pallas as pl
from jax.experimental.pallas import tpu as pltpu
from jax.sharding import PartitionSpec as P

DE = 768
DD = 512
TILE = 256
BLOCK = 512
NEGATIVE = -1e30
F32, BF16 = jnp.float32, jnp.bfloat16
MESH_ID = pl.DeviceIdType.MESH

CANON = ("x", "z2", "z1", "y")
ROUTES = (("x", "y", "z1", "z2"), ("y", "x", "z1", "z2"), ("z1", "z2", "x", "y"))
UNIT = 1536
LAG = 2
DECODER_PLAN = types.SimpleNamespace(widths=(2, 2, 1), chunks=7, slots=7, ring=3, span=640)
ENCODER_PLAN = types.SimpleNamespace(widths=(3, 6, 3), chunks=9, slots=3, ring=3, span=1536)
TAIL_PLAN = types.SimpleNamespace(widths=(2, 3, 1), chunks=2, slots=2, ring=2, span=768)

DECODER_EXPAND, DECODER_SHRINK, DECODER_MERGE = (0, 16, 2048), (2048, 64, 512), (4096, 16, 256)
ENTRY, DECODER_ATTEND = (0, 24, 512), (768, 16, 768)
ENCODER_SHRINK = tuple((UNIT * (1 + part), 96, 256) for part in range(3))
ENCODER_EXPAND = tuple((UNIT * (4 + part), 24, 1024) for part in range(3))
ENCODER_ATTEND = ((UNIT * 7, 24, 1024), (UNIT * 8, 24, 1024), (0, 24, 256))
ENCODER_MERGE = (384, 24, 768)


def dot(a, b):
    return jnp.dot(a, b, preferred_element_type=F32)


def dot_nt(a, b):
    return lax.dot_general(a, b, (((1,), (1,)), ((), ())), preferred_element_type=F32)


def dot_tn(a, b):
    return lax.dot_general(a, b, (((0,), (0,)), ((), ())), preferred_element_type=F32)


def low(value):
    return value.astype(BF16)


def standardize(values):
    centered = values - jnp.mean(values, axis=-1, keepdims=True)
    inverse = lax.rsqrt(jnp.mean(centered * centered, axis=-1, keepdims=True) + 1e-05)
    return centered * inverse, inverse


def norm_back(unit, inverse, gain, grad):
    inner = grad * gain
    return inverse * (
        inner
        - jnp.mean(inner, axis=-1, keepdims=True)
        - unit * jnp.mean(inner * unit, axis=-1, keepdims=True)
    )


def row_sum(values):
    return jnp.sum(values, axis=0, keepdims=True)


def gelu_pair(before):
    half = 0.5 * (1.0 + lax.erf(before * 0.7071067811865476))
    density = jnp.exp(-0.5 * before * before) * 0.3989422804014327
    return before * half, half + before * density


def chip_of(places, sizes, pack):
    end = sizes[pack, 0]
    chip = (places >= end).astype(jnp.int32)
    for slot in range(1, 4):
        end = end + sizes[pack, slot]
        chip = chip + (places >= end).astype(jnp.int32)
    return chip


def iota(shape, dimension):
    return lax.broadcasted_iota(jnp.int32, shape, dimension)


def aligned(start, size, unit):
    if isinstance(start, int):
        return slice(start, start + size)
    return pl.ds(pl.multiple_of(start, unit), size)


def pair_lanes(pair, base=0):
    return aligned(base + pair * 128, 128, 128)


def head_rows(pair, half, base=0):
    return aligned(base + pair * 128 + half * 64, 64, 64)


def rows_of(tile, size=TILE):
    return aligned(tile * size, size, size)


def only(values, half):
    return jnp.where(iota((1, 128), 1) // 64 == half, values, jnp.zeros_like(values))


def fetch(pairs, sems):
    copies = [
        pltpu.make_async_copy(source, target, sems.at[i]) for i, (source, target) in enumerate(pairs)
    ]
    for copy in copies:
        copy.start()
    return copies


def store_packed(put, first, place, value):
    offset, count, width = place
    value = value.reshape(-1, count, width)
    shards = slice(first, first + value.shape[0]) if isinstance(first, int) else pl.ds(first, value.shape[0])
    for piece in range(count // 16):
        put(shards, offset + piece * width, value[:, piece * 16 : piece * 16 + 16])
    if count % 16:
        half = width // 2
        rest = value[:, count - 8 :]
        rest = jnp.concatenate([rest[:, :, :half], rest[:, :, half:]], axis=1)
        put(shards, offset + count // 16 * width, rest)


def halves(shards, value):
    pairs = value.reshape(value.shape[0] // 2, 2, *value.shape[1:])
    if isinstance(shards, slice):
        return slice(shards.start // 2, shards.stop // 2), pairs[:, 0], pairs[:, 1]
    return pl.ds(shards.start // 2, shards.size // 2), pairs[:, 0], pairs[:, 1]


def place_of(names, bits):
    index = 0
    for name in names:
        index = index * 2 + bits[name]
    return index


def left_after(route, stage):
    return tuple(name for name in CANON if name not in route[:stage])


def choices(names):
    for number in range(2 ** len(names)):
        yield {name: (number >> (len(names) - 1 - i)) & 1 for i, name in enumerate(names)}


def neighbours():
    section = lax.axis_index("section")
    data = lax.axis_index("dp")
    mine = {"x": section, "c": data % 2, "y": data // 2 % 2, "z1": data // 4 % 2, "z2": data // 8 % 2}
    partner = {"x": (1 - section, data)}
    for name, step in {"c": 1, "y": 2, "z1": 4, "z2": 8}.items():
        partner[name] = (section, data + step * (1 - 2 * mine[name]))
    return mine, partner


def greet(partner):
    barrier = pltpu.get_barrier_semaphore()
    for name in ("c",) + CANON:
        pl.semaphore_signal(barrier, inc=1, device_id=partner[name], device_id_type=MESH_ID)


def await_greetings():
    pl.semaphore_wait(pltpu.get_barrier_semaphore(), 5)


def remote(source, target, send, recv, device):
    return pltpu.make_async_remote_copy(
        src_ref=source,
        dst_ref=target,
        send_sem=send,
        recv_sem=recv,
        device_id=device,
        device_id_type=MESH_ID,
    )


def reducer(plan, mine, partner, out, refs):
    chunks, slots, span, ring = plan.chunks, plan.slots, plan.span, plan.ring
    progress = types.SimpleNamespace(opened=0, sent=0)
    own, staging, first = refs[:3]
    sent, got = refs[3:15], refs[15:27]
    first_send, first_recv, send_sem, recv_sem = refs[27:31]

    def first_copy(chunk):
        return remote(staging.at[chunk % slots], first.at[chunk], first_send.at[chunk], first_recv.at[chunk], partner["c"])

    def stage_copy(route, stage, chunk):
        return remote(
            sent[route * 4 + stage].at[chunk % ring],
            got[route * 4 + stage].at[chunk],
            send_sem.at[route, stage, chunk],
            recv_sem.at[route, stage, chunk],
            partner[ROUTES[route][stage]],
        )

    def total(route, stage, chunk, bits):
        spot = place_of(CANON, bits)
        cols = slice(sum(plan.widths[:route]) * 128, sum(plan.widths[: route + 1]) * 128)
        value = own[chunk, spot, :, cols].astype(F32) + first[chunk, spot, :, cols].astype(F32)
        for earlier in range(stage):
            names = left_after(ROUTES[route], earlier + 1)
            value = value + got[route * 4 + earlier][chunk, place_of(names, bits)].astype(F32)
        return value

    def advance(stage, chunk):
        for route in range(3):
            if stage:
                stage_copy(route, stage - 1, chunk).wait_recv()
            else:
                first_copy(chunk).wait_recv() if route == 0 else None
            if stage < 4:

                @pl.when(chunk >= ring)
                def _(route=route):
                    stage_copy(route, stage, chunk - ring).wait_send()

        values = []
        for route in range(3):
            path = ROUTES[route]
            if stage == 4:
                values.append(total(route, 4, chunk, mine))
                continue
            names = left_after(path, stage + 1)
            for free in choices(names):
                bits = dict(mine)
                bits[path[stage]] = 1 - mine[path[stage]]
                bits.update(free)
                values.append((route, place_of(names, free), low(total(route, stage, chunk, bits))))
        if stage == 4:
            out[chunk] = jnp.concatenate(values, axis=1)
            return
        for route, spot, value in values:
            sent[route * 4 + stage][chunk % ring, spot] = value
        for route in range(3):
            stage_copy(route, stage, chunk).start()

    def turn(number):
        for stage in range(4, -1, -1):
            chunk = number - LAG * stage
            pl.when((chunk >= 0) & (chunk < chunks))(functools.partial(advance, stage, chunk))

    def put(shards, column, value):
        shards, even, odd = halves(shards, value)
        kept = low(jnp.where(mine["c"] == 0, even, odd))
        given = low(jnp.where(mine["c"] == 0, odd, even))
        width = value.shape[2]
        done = 0
        while done < width:
            chunk, start = divmod(column + done, span)
            size = min(width - done, span - start)
            own[chunk, shards, :, start : start + size] = kept[:, :, done : done + size]
            staging[chunk % slots, shards, :, start : start + size] = given[:, :, done : done + size]
            done += size

    def release(column):
        while progress.opened * span < column:
            if progress.opened >= slots:
                first_copy(progress.opened - slots).wait_send()
            progress.opened += 1

    def send(column):
        while (progress.sent + 1) * span <= column:
            first_copy(progress.sent).start()
            progress.sent += 1

    def close():
        for chunk in range(max(0, chunks - slots), chunks):
            first_copy(chunk).wait_send()
        for chunk in range(chunks - ring, chunks):
            for route in range(3):
                for stage in range(4):
                    stage_copy(route, stage, chunk).wait_send()

    return types.SimpleNamespace(
        own=own, staging=staging, turn=turn, put=put, release=release, send=send, close=close
    )


def reducer_scratch(plan):
    stages = [(width, block) for width in plan.widths for block in (8, 4, 2, 1)]
    return (
        [
            pltpu.VMEM((plan.chunks, 16, 16, plan.span), BF16),
            pltpu.VMEM((plan.slots, 16, 16, plan.span), BF16),
            pltpu.VMEM((plan.chunks, 16, 16, plan.span), BF16),
        ]
        + [pltpu.VMEM((plan.ring, block, 16, width * 128), BF16) for width, block in stages]
        + [pltpu.VMEM((plan.chunks, block, 16, width * 128), BF16) for width, block in stages]
        + [
            pltpu.SemaphoreType.DMA((plan.chunks,)),
            pltpu.SemaphoreType.DMA((plan.chunks,)),
            pltpu.SemaphoreType.DMA((3, 4, plan.chunks)),
            pltpu.SemaphoreType.DMA((3, 4, plan.chunks)),
        ]
    )


def put_into(parts):
    span = parts.shape[-1]

    def put(shards, column, value):
        shards, *pair = halves(shards, value)
        width = value.shape[2]
        done = 0
        while done < width:
            chunk, start = divmod(column + done, span)
            size = min(width - done, span - start)
            for core in range(2):
                parts[chunk, core, shards, :, start : start + size] = low(pair[core][:, :, done : done + size])
            done += size

    return put


def vmem_spec():
    return pl.BlockSpec(memory_space=pltpu.VMEM)


def any_spec():
    return pl.BlockSpec(memory_space=pl.ANY)


def smem_spec():
    return pl.BlockSpec(memory_space=pltpu.SMEM)


def encoder_forward_kernel(
    sizes, gains, shifts, biases, inner, tokens, attend_far, merging_far, expand_far, shrink_far,
    sent, vectors, *refs,
):
    far = refs[:9]
    normed, mixed, turned, probs, context, middle, normed_two, active, slope = refs[9:18]
    hidden, attend, merging, expand, shrink, context_turned, load_sem, save_sem = refs[18:]
    pack = lax.axis_index("section")
    loads = fetch(
        [
            (tokens.at[pack], hidden),
            *[(attend_far.at[:, i * 768 : i * 768 + 768], attend.at[:, i * 768 : i * 768 + 768]) for i in range(3)],
            (merging_far, merging),
            *[(expand_far.at[:, i * 1024 : i * 1024 + 1024], expand.at[:, i * 1024 : i * 1024 + 1024]) for i in range(3)],
            *[(shrink_far.at[i * 1024 : i * 1024 + 1024], shrink.at[i * 1024 : i * 1024 + 1024]) for i in range(3)],
        ],
        load_sem,
    )
    saves = []

    def save(*numbers):
        for number in numbers:
            copy = pltpu.make_async_copy(refs[9 + number], far[number], save_sem.at[number])
            copy.start()
            saves.append(copy)

    vectors[...] = jnp.zeros_like(vectors)
    key_chip = chip_of(4 * iota((TILE, 1), 0), sizes, pack)
    own_chip = chip_of(4 * iota((1, TILE), 1), sizes, pack)
    valid = (key_chip < 4).astype(F32)
    loads[0].wait()
    values = hidden[...]
    vectors[10:11, :768] = row_sum(valid * values * values)
    unit, _ = standardize(values)
    norm = low(unit * gains[0:1] + shifts[0:1])
    normed[...] = norm
    for part in range(3):
        cols = slice(part * 768, part * 768 + 768)
        loads[1 + part].wait()
        mix = dot(norm, attend[:, cols])
        mixed[:, cols] = low(mix)
        if part:
            turned[(part - 1) * 768 : part * 768] = low(mix.T)
    save(0, 1, 2)

    @pl.loop(0, 3)
    def _(step):
        def score(number):
            pair, half = 2 * step + number // 2, number % 2
            query = only(mixed[:, pair_lanes(pair)], half) * BF16(0.125)
            return dot_nt(mixed[:, pair_lanes(pair, 768)], query)

        ready = [score(0), score(1)]
        for number in range(4):
            if number + 2 < 4:
                ready.append(score(number + 2))
            pair, half = 2 * step + number // 2, number % 2
            scores = jnp.where(key_chip == own_chip, ready[number], NEGATIVE)
            expos = jnp.exp(scores - jnp.max(scores, axis=0, keepdims=True))
            prob = low(expos * (1.0 / jnp.sum(expos, axis=0, keepdims=True)))
            probs[pair * 2 + half] = prob
            context_turned[head_rows(pair, half)] = dot(turned[head_rows(pair, half, 768)], prob)

    mingled = low(context_turned[...].T)
    context[...] = mingled
    save(3, 4)
    loads[4].wait()
    attention = dot(mingled, merging[...]) + biases[0:1]
    vectors[11:12, :768] = row_sum(valid * attention * attention)
    center = hidden[...] + attention
    middle[...] = center
    unit, _ = standardize(center)
    norm = low(unit * gains[1:2] + shifts[1:2])
    normed_two[...] = norm
    save(5, 6)
    feed = jnp.zeros_like(center)
    def widened(part):
        if part % 2 == 0:
            loads[5 + part // 2].wait()
        cols = slice(part * 512, part * 512 + 512)
        return dot(norm, expand[:, cols]) + inner[:, cols]

    ready = [widened(0)]
    for part in range(6):
        if part < 5:
            ready.append(widened(part + 1))
        cols = slice(part * 512, part * 512 + 512)
        value, slant = gelu_pair(ready[part])
        value = low(value)
        active[:, cols] = value
        slope[part // 2, :, part % 2 * 512 : part % 2 * 512 + 512] = slant
        if part % 2 == 0:
            loads[8 + part // 2].wait()
        feed = feed + dot(value, shrink[cols])
    save(7, 8)
    feed = feed + biases[1:2]
    vectors[12:13, :768] = row_sum(valid * feed * feed)
    output = center + feed
    vectors[13:14, :768] = row_sum(valid * output * output)
    vectors[14:15, :768] = jnp.broadcast_to(row_sum(valid), (1, 768))
    sent[...] = low(output)
    for copy in saves:
        copy.wait()


def encoder_forward_call(sizes, tokens, gains, shifts, biases, attend, merging, expand, inner, shrink):
    shapes = (
        ((256, 768), BF16),
        ((256, 2304), BF16),
        ((1536, 256), BF16),
        ((12, 256, 256), BF16),
        ((256, 768), BF16),
        ((256, 768), F32),
        ((256, 768), BF16),
        ((256, 3072), BF16),
        ((3, 256, 1024), F32),
    )
    return pl.pallas_call(
        encoder_forward_kernel,
        out_shape=(jax.ShapeDtypeStruct((256, 768), BF16), jax.ShapeDtypeStruct((16, 1024), F32))
        + tuple(jax.ShapeDtypeStruct(*shape) for shape in shapes),
        in_specs=[smem_spec()] + [vmem_spec()] * 4 + [any_spec()] * 5,
        out_specs=(vmem_spec(),) * 2 + (any_spec(),) * len(shapes),
        scratch_shapes=[pltpu.VMEM(*shape) for shape in shapes]
        + [
            pltpu.VMEM((256, 768), F32),
            pltpu.VMEM(attend.shape, BF16),
            pltpu.VMEM(merging.shape, BF16),
            pltpu.VMEM(expand.shape, BF16),
            pltpu.VMEM(shrink.shape, BF16),
            pltpu.VMEM((768, 256), F32),
            pltpu.SemaphoreType.DMA((11,)),
            pltpu.SemaphoreType.DMA((len(shapes),)),
        ],
        compiler_params=pltpu.CompilerParams(vmem_limit_bytes=60 * 2**20),
        name="encoder_forward",
    )(sizes, gains, shifts, biases, inner[None], tokens, attend, merging, expand, shrink)


def decoder_kernel(
    reduce, sizes, distance, slots, frequency, sent, biases, mask_token, gains, shifts, inner,
    cotangent, entry_far, attend_far, merging_far, expand_far, shrink_far,
    summed, rest, vectors, encoded_grad, *refs,
):
    (
        table, start, normed, mixed, turned, probs, flipped, context, normed_two, active,
        before_grad, go_low, attention_low, context_grad, delta, mixed_grad, target, masked_keys,
        entry_weight, attend, merging, expand, shrink, load_sem,
    ) = refs[:24]
    pack = lax.axis_index("section")
    if reduce:
        mine, partner = neighbours()
        greet(partner)
        engine = reducer(DECODER_PLAN, mine, partner, summed, refs[24:])
        put = engine.put
    else:
        put = put_into(summed)
    put_rest = put_into(rest)
    loads = fetch(
        [
            (entry_far, entry_weight),
            (attend_far, attend),
            (cotangent.at[pack], target),
            (merging_far, merging),
            (expand_far, expand),
            (shrink_far, shrink),
        ],
        load_sem,
    )
    tiles = start.shape[0] // TILE
    vectors[...] = jnp.zeros_like(vectors)
    large = sizes[pack, 0] == 1024

    def add_row(row, value):
        vectors[row : row + 1, :] += value

    positions = iota((32, 128), 0).astype(F32)
    for chip in range(4):
        spacing = distance[pack, chip].astype(F32) / 16.0
        angle = positions * (spacing * frequency[...])
        table[0, chip] = jnp.sin(angle)
        table[1, chip] = jnp.cos(angle)
    loads[0].wait()
    entry = low(dot(sent[...], entry_weight[...]) + biases[0:1])
    loads[1].wait()

    blocks = start.shape[0] // BLOCK

    def slot_chip(tile, size):
        return chip_of(iota((size, 1), 0) + tile * size, sizes, pack)

    def validity(tile, size):
        return (slot_chip(tile, size) < 4).astype(F32)

    def spread_of(tile):
        return (slots[pl.ds(pack, 1)] == iota((TILE, TILE), 0) + tile * TILE).astype(F32)

    def encoding_of(tile):
        pieces = []
        for kind in range(2):
            wave = table[kind, 0, aligned(tile * 8, 8, 8)]
            big = jnp.broadcast_to(wave[:, None], (8, 32, 128)).reshape(TILE, 128)
            wave = table[kind, tile, 0:16]
            own = jnp.broadcast_to(wave[:, None], (16, 16, 128)).reshape(TILE, 128)
            pieces.append(jnp.where(large, big, own))
        for kind in range(2):
            wave = table[kind, 0]
            big = jnp.broadcast_to(wave[None], (8, 32, 128)).reshape(TILE, 128)
            wave = table[kind, tile, 0:16]
            own = jnp.broadcast_to(wave[None], (16, 16, 128)).reshape(TILE, 128)
            pieces.append(jnp.where(large, big, own))
        return jnp.concatenate(pieces, axis=1)

    @pl.loop(0, tiles)
    def _(tile):
        rows = rows_of(tile)
        valid = validity(tile, TILE)
        spread = spread_of(tile)
        fill = valid * (1.0 - jnp.sum(spread, axis=1, keepdims=True))
        hidden = dot(low(spread), entry) + fill * mask_token[...] + encoding_of(tile) * valid
        start[rows] = hidden
        add_row(12, row_sum(valid * hidden * hidden))
        add_row(16, row_sum(valid))
        unit, _ = standardize(hidden)
        norm = low(unit * gains[0:1] + shifts[0:1])
        normed[rows] = norm
        mix = dot(norm, attend[...])
        mix_low = low(mix)
        mixed[rows] = mix_low
        turned[:, rows] = low(mix[:, 256:].T)
        lane = iota((TILE, 128), 1)
        other = (lane % 64 < 5) & (lane % 64 != slot_chip(tile, TILE))
        other = jnp.where(other, NEGATIVE, 0.0).astype(BF16)
        for head in range(4):
            lanes = slice(256 + head // 2 * 128, 384 + head // 2 * 128)
            masked_keys[head, rows] = jnp.where(lane // 64 == head % 2, mix_low[:, lanes], other)

    @pl.loop(0, 2 * tiles)
    def _(step):
        pair, tile = step // tiles, step % tiles
        rows = rows_of(tile)
        lane = iota((TILE, 128), 1)
        chosen = (lane % 64 == slot_chip(tile, TILE)).astype(F32).astype(BF16)
        for half in range(2):
            query = jnp.where(lane // 64 == half, mixed[rows, pair_lanes(pair)] * BF16(0.125), chosen)
            scores = dot_nt(masked_keys[pair * 2 + half], query)
            expos = jnp.exp(scores - jnp.max(scores, axis=0, keepdims=True))
            prob = low(expos * (1.0 / jnp.sum(expos, axis=0, keepdims=True)))
            probs[pair * 2 + half, :, rows] = prob
            flipped[head_rows(pair, half), rows] = dot(turned[head_rows(pair, half, 256)], prob)

    for copy in loads[2:]:
        copy.wait()

    @pl.loop(0, blocks)
    def _(tile):
        rows = rows_of(tile, BLOCK)
        valid = validity(tile, BLOCK)
        mingled_wide = flipped[:, rows].T
        mingled = low(mingled_wide)
        context[rows] = mingled
        attention = dot(mingled, merging[...]) + biases[1:2]
        add_row(13, row_sum(valid * attention * attention))
        center = start[rows] + attention
        unit, inverse = standardize(center)
        norm = low(unit * gains[1:2] + shifts[1:2])
        normed_two[rows] = norm
        go = target[rows] * valid
        go_below = low(go)
        go_low[rows] = go_below
        add_row(2, row_sum(go))
        feed = jnp.zeros_like(go)
        norm_grad = jnp.zeros_like(go)
        for part in range(8):
            cols = slice(part * 256, part * 256 + 256)
            before = dot(norm, expand[:, cols]) + inner[:, cols]
            value, slope = gelu_pair(before)
            value = low(value)
            active[rows, cols] = value
            feed = feed + dot(value, shrink[cols])
            grad = low(slope * dot_nt(go_below, shrink[cols]))
            before_grad[rows, cols] = grad
            lanes = slice(part % 2 * 256, part % 2 * 256 + 256)
            vectors[8 + part // 2 : 9 + part // 2, lanes] += row_sum(grad.astype(F32))
            norm_grad = norm_grad + dot_nt(grad, expand[:, cols])
        feed = feed + biases[2:3]
        add_row(14, row_sum(valid * feed * feed))
        output = center + feed
        add_row(15, row_sum(valid * output * output))
        add_row(5, row_sum(norm_grad * unit))
        add_row(7, row_sum(norm_grad))
        grad = go + norm_back(unit, inverse, gains[1:2], norm_grad)
        target[rows] = grad
        add_row(1, row_sum(grad))
        below = low(grad)
        attention_low[rows] = below
        outer = low(dot_nt(below, merging[...]))
        context_grad[rows] = outer
        product = (outer.astype(F32) * mingled_wide).T
        for head in range(4):
            delta[head, :, rows] = row_sum(product[head * 64 : head * 64 + 64])

    for part in range(2):
        cols = slice(part * 256, part * 256 + 256)
        store_packed(put, part * 16, DECODER_EXPAND, dot_tn(normed_two[:, cols], before_grad[...]))
        value = dot_tn(attention_low[:, cols], context[...])
        store_packed(put, part * 16, DECODER_MERGE, value)
    for block in range(2):
        put(slice(block * 16, block * 16 + 16), 4352, jnp.zeros((16, 16, DECODER_PLAN.chunks * DECODER_PLAN.span - 4352), F32))
    if reduce:
        await_greetings()
        engine.send(2048)

    @pl.loop(0, 8)
    def _(part):
        cols = aligned(part * 256, 256, 256)
        store_packed(put, part * 4, DECODER_SHRINK, dot_tn(active[:, cols], go_low[...]))

    if reduce:
        engine.send(DECODER_PLAN.chunks * DECODER_PLAN.span)

    flipped[...] = jnp.zeros_like(flipped)

    @pl.loop(0, 2 * tiles)
    def _(step):
        pair, tile = step // tiles, step % tiles
        rows = rows_of(tile)
        lanes = pair_lanes(pair)
        values = mixed[rows, pair_lanes(pair, 512)]
        raws, probabilities, queries, outers = [], [], [], []
        for half in range(2):
            prob = probs[pair * 2 + half, rows]
            outer = only(context_grad[:, lanes], half)
            raw = low(prob.astype(F32) * (dot_nt(values, outer) - delta[pair * 2 + half]))
            flipped[head_rows(pair, half)] += dot(turned[head_rows(pair, half), rows], raw)
            raws.append(raw)
            probabilities.append(prob)
            outers.append(outer)
            queries.append(only(mixed[:, lanes], half))
        key_grad = dot(jnp.concatenate(raws, axis=1), jnp.concatenate(queries, axis=0))
        mixed_grad[rows, pair_lanes(pair, 256)] = low(key_grad * 0.125)
        value_grad = dot(jnp.concatenate(probabilities, axis=1), jnp.concatenate(outers, axis=0))
        mixed_grad[rows, pair_lanes(pair, 512)] = low(value_grad)
        if reduce:
            engine.turn(step)

    def last(tile, entry_grad):
        rows = rows_of(tile)
        mixed_grad[rows, 0:256] = low(flipped[:, rows].T * 0.125)
        norm_grad = dot_nt(mixed_grad[rows], attend[...])
        unit, inverse = standardize(start[rows])
        add_row(4, row_sum(norm_grad * unit))
        add_row(6, row_sum(norm_grad))
        grad = target[rows] + norm_back(unit, inverse, gains[0:1], norm_grad)
        spread = spread_of(tile)
        fill = validity(tile, TILE) * (1.0 - jnp.sum(spread, axis=1, keepdims=True))
        add_row(3, row_sum(fill * grad))
        if reduce:
            engine.turn(2 * tiles + tile)
        return entry_grad + dot_tn(low(spread), low(grad))

    entry_grad = lax.fori_loop(0, tiles, last, jnp.zeros((TILE, 512), F32))
    add_row(0, row_sum(entry_grad))
    entry_low = low(entry_grad)
    encoded_grad[...] = low(dot_nt(entry_low, entry_weight[...]))
    store_packed(put_rest, 0, ENTRY, dot_tn(sent[...], entry_low))

    @pl.loop(0, 3)
    def _(part):
        if reduce:
            engine.turn(3 * tiles + part)

        @pl.when(part < 2)
        def _():
            cols = aligned(part * 256, 256, 256)
            store_packed(put_rest, part * 16, DECODER_ATTEND, dot_tn(normed[:, cols], mixed_grad[...]))

    if reduce:
        engine.close()


def decoder_call(
    reduce, sizes, distance, slots, sent, cotangent, entry_weight, biases, mask_token,
    gains, shifts, attend, merging, expand, inner, shrink,
):
    length = cotangent.shape[1]
    width = 512
    frequency = np.exp(-np.log(10000.0) * np.arange(width // 4) / (width // 4)).astype(np.float32)
    if reduce:
        summed = jax.ShapeDtypeStruct((DECODER_PLAN.chunks, 16, DECODER_PLAN.span), F32)
        extra = reducer_scratch(DECODER_PLAN)
        params = dict(collective_id=1, has_side_effects=True)
    else:
        summed = jax.ShapeDtypeStruct((DECODER_PLAN.chunks, 2, 16, 16, DECODER_PLAN.span), BF16)
        extra = []
        params = dict()
    return pl.pallas_call(
        functools.partial(decoder_kernel, reduce),
        out_shape=(
            summed,
            jax.ShapeDtypeStruct((1, 2, 16, 16, UNIT), BF16),
            jax.ShapeDtypeStruct((24, width), F32),
            jax.ShapeDtypeStruct((256, 768), BF16),
        ),
        in_specs=[smem_spec()] * 2 + [vmem_spec()] * 8 + [any_spec()] * 6,
        out_specs=(vmem_spec(),) * 4,
        scratch_shapes=[
            pltpu.VMEM((2, 4, 32, 128), F32),
            pltpu.VMEM((length, width), F32),
            pltpu.VMEM((length, width), BF16),
            pltpu.VMEM((length, 768), BF16),
            pltpu.VMEM((512, length), BF16),
            pltpu.VMEM((4, length, length), BF16),
            pltpu.VMEM((256, length), F32),
            pltpu.VMEM((length, 256), BF16),
            pltpu.VMEM((length, width), BF16),
            pltpu.VMEM((length, 2048), BF16),
            pltpu.VMEM((length, 2048), BF16),
            pltpu.VMEM((length, width), BF16),
            pltpu.VMEM((length, width), BF16),
            pltpu.VMEM((length, 256), BF16),
            pltpu.VMEM((4, 1, length), F32),
            pltpu.VMEM((length, 768), BF16),
            pltpu.VMEM((length, width), F32),
            pltpu.VMEM((4, length, 128), BF16),
            pltpu.VMEM(entry_weight.shape, BF16),
            pltpu.VMEM(attend.shape, BF16),
            pltpu.VMEM(merging.shape, BF16),
            pltpu.VMEM(expand.shape, BF16),
            pltpu.VMEM(shrink.shape, BF16),
            pltpu.SemaphoreType.DMA((6,)),
        ]
        + extra,
        compiler_params=pltpu.CompilerParams(vmem_limit_bytes=63 * 2**20, **params),
        name="decoder_block",
    )(
        sizes, distance, slots, jnp.asarray(frequency)[None], sent, biases, mask_token[None], gains, shifts,
        inner[None], cotangent, entry_weight, attend, merging, expand, shrink,
    )


def encoder_backward_kernel(
    reduce, encoded_grad, sums, decoder_vectors, gains, tokens, rest, attend_far, merging_far, expand_far,
    shrink_far, normed_far, mixed_far, turned_far, probs_far, context_far, middle_far, normed_two_far, active_far,
    slope_far, summed, tail_summed, vectors, tokens_grad, *refs,
):
    if reduce:
        decoder_sums, arrived = refs[:2]
        refs = refs[2:]
    (
        hidden, attend, merging, expand, shrink, normed, mixed, turned, probs, context, middle, normed_two, active,
        slope, before_grad, norm_sum, attention_low, context_grad, key_grad, query_turned, mixed_grad, active_turned,
        flipped, inner_sum, load_sem, part_sem,
    ) = refs[:26]
    pack = lax.axis_index("section")

    def part_loads(part):
        cols = aligned(part * 1024, 1024, 1024)
        slot = part % 2
        return [
            pltpu.make_async_copy(expand_far.at[:, cols], expand.at[slot], part_sem.at[slot, 0]),
            pltpu.make_async_copy(shrink_far.at[cols], shrink.at[slot], part_sem.at[slot, 1]),
            pltpu.make_async_copy(slope_far.at[part], slope.at[slot], part_sem.at[slot, 2]),
        ]

    if reduce:
        (
            decoder_total, encoder_total, decoder_got, encoder_got, payload,
            own_sem, small_send, small_recv, pay_send, pay_recv, small_load,
        ) = refs[26:37]
        mine, partner = neighbours()
        greet(partner)
        engine = reducer(ENCODER_PLAN, mine, partner, summed, refs[37:68])
        tail = reducer(TAIL_PLAN, mine, partner, tail_summed, refs[68:])
        put, put_tail = engine.put, tail.put
        engine.release(UNIT)
        first_own = fetch(
            [
                pair
                for pair in (
                    (rest.at[0, 1 - mine["c"]], engine.staging.at[0]),
                    (rest.at[0, mine["c"]], engine.own.at[0]),
                )
            ],
            own_sem,
        )
        decoder_load = pltpu.make_async_copy(decoder_vectors, decoder_total.at[0], small_load)
        decoder_load.start()
    else:
        put, put_tail = put_into(summed), put_into(tail_summed)
    early = pltpu.make_async_copy(active_far, active, load_sem.at[10])
    early.start()
    for copy in part_loads(0):
        copy.start()
    if reduce:
        for copy in first_own:
            copy.wait()
        await_greetings()
        engine.send(UNIT)
    loads = fetch(
        [
            (normed_two_far, normed_two),
            (middle_far, middle),
            (merging_far, merging),
            (context_far, context),
            (mixed_far, mixed),
            (probs_far, probs),
            (turned_far.at[0:768], turned),
            (normed_far, normed),
            (attend_far, attend),
            (tokens.at[pack], hidden),
        ],
        load_sem,
    )
    for copy in part_loads(1):
        copy.start()
    vectors[...] = sums[...]
    go_low = encoded_grad[...]
    go = go_low.astype(F32)
    vectors[1:2, :768] = row_sum(go)
    norm_sum[...] = jnp.zeros_like(norm_sum)

    def send(unit):
        if reduce:
            engine.send((unit + 1) * UNIT)

    def release(unit):
        if reduce:
            engine.release((unit + 1) * UNIT)

    def shrink_start():
        early.wait()
        for piece in range(4):
            rows = slice(piece * 768, piece * 768 + 768)
            active_turned[rows] = active[:, rows].T

    def shrink_grad(part):
        release(1 + part)
        cols = slice(part * 256, part * 256 + 256)
        for piece in range(4):
            rows = slice(piece * 768, piece * 768 + 768)
            store_packed(put, piece * 8, ENCODER_SHRINK[part], dot(active_turned[rows], encoded_grad[:, cols]))
        send(1 + part)

    def hidden_layer(part):
        for copy in part_loads(part):
            copy.wait()
        slot = part % 2
        grad = low(slope[slot] * dot_nt(encoded_grad[...], shrink[slot]))
        before_grad[...] = grad
        inner_sum[part] = row_sum(grad.astype(F32))
        norm_sum[...] += dot_nt(grad, expand[slot])

        @pl.when(part == 0)
        def _():
            for copy in part_loads(2):
                copy.start()

    def expand_grad(part):
        release(4 + part)
        if part == 0:
            loads[0].wait()
            flipped[...] = normed_two[...].T
        store_packed(put, 0, ENCODER_EXPAND[part], dot(flipped[...], before_grad[...]))
        send(4 + part)

    def middle_layer():
        loads[1].wait()
        loads[2].wait()
        for part in range(3):
            vectors[6 + part : 7 + part] = inner_sum[part]
        unit, inverse = standardize(middle[...])
        norm_grad = norm_sum[...]
        vectors[3:4, :768] = row_sum(norm_grad * unit)
        vectors[5:6, :768] = row_sum(norm_grad)
        grad = encoded_grad[...].astype(F32) + norm_back(unit, inverse, gains[1:2], norm_grad)
        vectors[0:1, :768] = row_sum(grad)
        tokens_grad[...] = grad
        below = low(grad)
        attention_low[...] = below
        context_grad[...] = low(dot_nt(below, merging[...]))
        for copy in loads[3:7]:
            copy.wait()

    def attention(first):
        @pl.loop(first, first + 2)
        def _(pair):
            lanes = pair_lanes(pair)
            values = mixed[:, pair_lanes(pair, 1536)]
            keys_total = jnp.zeros((TILE, 128), F32)
            values_total = jnp.zeros((TILE, 128), F32)
            for half in range(2):
                prob = probs[pair * 2 + half]
                outer = only(context_grad[:, lanes], half)
                query = only(mixed[:, lanes], half)
                wide = prob.astype(F32)
                grad = dot_nt(values, outer)
                raw = low(wide * (grad - jnp.sum(wide * grad, axis=0, keepdims=True)))
                keys_total = keys_total + dot(raw, query)
                values_total = values_total + dot(prob, outer)
                rows = head_rows(pair, half)
                query_turned[rows] = dot(turned[rows], raw)
            key_grad[0, :, lanes] = keys_total
            key_grad[1, :, lanes] = values_total

    def mixing():
        mixed_grad[:, 0:768] = low(query_turned[...].T * 0.125)
        mixed_grad[:, 768:1536] = low(key_grad[0] * 0.125)
        mixed_grad[:, 1536:2304] = low(key_grad[1])

    def attend_grad(part):
        if part == 0:
            loads[7].wait()
            flipped[...] = normed[...].T
        wide = slice(part * 1024, min(part * 1024 + 1024, 2304))
        value = dot(flipped[...], mixed_grad[:, wide])
        if part < 2:
            release(7 + part)
            store_packed(put, 0, ENCODER_ATTEND[part], value)
            send(7 + part)
            return
        store_packed(put_tail, 0, ENCODER_ATTEND[part], value)
        store_packed(put_tail, 0, ENCODER_MERGE, dot_tn(attention_low[...], context[...]))
        if reduce:
            tail.send(UNIT)

    def input_layer():
        loads[8].wait()
        loads[9].wait()
        norm_grad = dot_nt(mixed_grad[...], attend[...])
        unit, inverse = standardize(hidden[...])
        vectors[2:3, :768] = row_sum(norm_grad * unit)
        vectors[4:5, :768] = row_sum(norm_grad)
        grad = tokens_grad[...] + norm_back(unit, inverse, gains[0:1], norm_grad)
        tokens_grad[...] = grad
        if reduce:
            payload[...] = low(grad)

    if not reduce:
        shrink_start()
        for part in range(3):
            shrink_grad(part)
        for part in range(3):
            hidden_layer(part)
            expand_grad(part)
        middle_layer()
        for first in (0, 2, 4):
            attention(first)
        mixing()
        for part in range(3):
            attend_grad(part)
        input_layer()
        return

    def exchange(source, piece):
        rows = aligned(piece * 32, 32, 32)
        return remote(source.at[rows], arrived.at[rows], pay_send.at[piece], pay_recv.at[piece], partner["x"])

    small_route = ("c",) + ROUTES[0]
    totals = ((decoder_total, decoder_got), (encoder_total, encoder_got))

    def small_copy(stage, kind):
        source, target = totals[kind]
        return remote(
            source.at[stage],
            target.at[stage],
            small_send.at[stage, kind],
            small_recv.at[stage, kind],
            partner[small_route[stage]],
        )

    def small_advance(stage):
        if stage == 0:
            encoder_total[0] = vectors[...]
        for kind in range(2):
            source, target = totals[kind]
            if stage > 0:
                small_copy(stage - 1, kind).wait_recv()
                source[stage] = source[stage - 1] + target[stage - 1]
            if stage < 5:
                small_copy(stage, kind).start()

    shrink_start()
    shrink_grad(0)
    decoder_load.wait()

    def expand_end():
        expand_grad(2)
        middle_layer()

    def attention_all():
        @pl.loop(0, 3)
        def _(step):
            attention(2 * step)

        mixing()

    def attend_start():
        attend_grad(0)
        attend_grad(1)

    def attend_end():
        attend_grad(2)
        input_layer()

    part = functools.partial
    works = {
        0: part(shrink_grad, 1),
        1: part(shrink_grad, 2),
        2: part(expand_grad, 0),
        3: part(expand_grad, 1),
        4: expand_end,
        5: attention_all,
        6: attend_start,
        7: attend_end,
    }
    turns = ENCODER_PLAN.chunks + TAIL_PLAN.chunks + 4 * LAG
    works.update({8 + stage + max(0, stage - 1): part(small_advance, stage) for stage in range(6)})

    @pl.loop(0, turns)
    def _(number):
        engine.turn(number)
        tail.turn(number - ENCODER_PLAN.chunks)

        for position, work in works.items():
            pl.when(number == position)(work)

        @pl.when((number >= 1) & (number <= 3))
        def _():
            hidden_layer(number - 1)

        @pl.when((pack == 0) & (number < 8))
        def _():
            exchange(encoded_grad, number).start()

        @pl.when((pack == 1) & (number >= 8) & (number < 16))
        def _():
            exchange(payload, number - 8).start()

    for stage in range(5):
        for kind in range(2):
            small_copy(stage, kind).wait_send()
    for piece in range(8):
        exchange(payload, piece).wait()
    engine.close()
    tail.close()
    vectors[...] = encoder_total[5]
    decoder_sums[...] = decoder_total[5]


def encoder_backward_call(reduce, tokens, encoded_grad, sums, decoder_vectors, rest, kept, gains, attend, merging, expand, shrink):
    if reduce:
        summed = tuple(
            jax.ShapeDtypeStruct((plan.chunks, 16, plan.span), F32) for plan in (ENCODER_PLAN, TAIL_PLAN)
        )
        more = (
            jax.ShapeDtypeStruct(decoder_vectors.shape, F32),
            jax.ShapeDtypeStruct((256, 768), BF16),
        )
        more_specs = (vmem_spec(), any_spec())
        extra = [
            pltpu.VMEM((6,) + decoder_vectors.shape, F32),
            pltpu.VMEM((6,) + sums.shape, F32),
            pltpu.VMEM((5,) + decoder_vectors.shape, F32),
            pltpu.VMEM((5,) + sums.shape, F32),
            pltpu.VMEM((256, 768), BF16),
            pltpu.SemaphoreType.DMA((2,)),
            pltpu.SemaphoreType.DMA((5, 2)),
            pltpu.SemaphoreType.DMA((5, 2)),
            pltpu.SemaphoreType.DMA((8,)),
            pltpu.SemaphoreType.DMA((8,)),
            pltpu.SemaphoreType.DMA,
        ] + reducer_scratch(ENCODER_PLAN) + reducer_scratch(TAIL_PLAN)
        params = dict(collective_id=2, has_side_effects=True)
    else:
        summed = tuple(
            jax.ShapeDtypeStruct((plan.chunks, 2, 16, 16, plan.span), BF16) for plan in (ENCODER_PLAN, TAIL_PLAN)
        )
        more, more_specs, extra, params = (), (), [], dict()
    return pl.pallas_call(
        functools.partial(encoder_backward_kernel, reduce),
        out_shape=summed
        + (
            jax.ShapeDtypeStruct(sums.shape, F32),
            jax.ShapeDtypeStruct((256, 768), F32),
        )
        + more,
        in_specs=[vmem_spec()] * 2 + [any_spec(), vmem_spec()] + [any_spec()] * 15,
        out_specs=(vmem_spec(),) * 4 + more_specs,
        scratch_shapes=[
            pltpu.VMEM((256, 768), F32),
            pltpu.VMEM(attend.shape, BF16),
            pltpu.VMEM(merging.shape, BF16),
            pltpu.VMEM((2, 768, 1024), BF16),
            pltpu.VMEM((2, 1024, 768), BF16),
            pltpu.VMEM((256, 768), BF16),
            pltpu.VMEM((256, 2304), BF16),
            pltpu.VMEM((768, 256), BF16),
            pltpu.VMEM((12, 256, 256), BF16),
            pltpu.VMEM((256, 768), BF16),
            pltpu.VMEM((256, 768), F32),
            pltpu.VMEM((256, 768), BF16),
            pltpu.VMEM((256, 3072), BF16),
            pltpu.VMEM((2, 256, 1024), F32),
            pltpu.VMEM((256, 1024), BF16),
            pltpu.VMEM((256, 768), F32),
            pltpu.VMEM((256, 768), BF16),
            pltpu.VMEM((256, 768), BF16),
            pltpu.VMEM((2, 256, 768), F32),
            pltpu.VMEM((768, 256), F32),
            pltpu.VMEM((256, 2304), BF16),
            pltpu.VMEM((3072, 256), BF16),
            pltpu.VMEM((768, 256), BF16),
            pltpu.VMEM((3, 1, 1024), F32),
            pltpu.SemaphoreType.DMA((11,)),
            pltpu.SemaphoreType.DMA((2, 3)),
        ]
        + extra,
        compiler_params=pltpu.CompilerParams(vmem_limit_bytes=62 * 2**20, **params),
        name="encoder_backward",
    )(encoded_grad, sums, decoder_vectors, gains, tokens, rest, attend, merging, expand, shrink, *kept)


def unpack(packed, place):
    span = packed.shape[-1]

    def take(start, size):
        pieces = []
        while size:
            chunk, first = divmod(start, span)
            length = min(size, span - first)
            pieces.append(packed[chunk, ..., first : first + length])
            start, size = start + length, size - length
        return pieces[0] if len(pieces) == 1 else jnp.concatenate(pieces, axis=-1)

    offset, count, width = place
    pieces = [take(offset + i * width, width) for i in range(count // 16)]
    if count % 16:
        rest = take(offset + count // 16 * width, width // 2)
        pieces.append(jnp.concatenate([rest[..., :8, :], rest[..., 8:, :]], axis=-1))
    return pieces[0] if len(pieces) == 1 else jnp.concatenate(pieces, axis=-2)


def finish_kernel(
    decoder_summed_far, decoder_sums_far, encoder_sums_far, summed_far, tail_far, arrived_far, tokens_grad_far, encoded_grad_far,
    boundary, statistics, e_gains, e_shifts, e_biases, e_attend, e_merge, e_expand, e_inner, e_shrink,
    d_entry, d_biases, mask_grad, d_gains, d_shifts, d_attend, d_merge, d_expand, d_inner, d_shrink,
    decoder_summed, decoder_sums, encoder_sums, summed, tail, arrived, tokens_grad, encoded_grad, load_sem,
):
    section = lax.axis_index("section")
    loads = fetch(
        [
            (decoder_summed_far, decoder_summed),
            (decoder_sums_far, decoder_sums),
            (encoder_sums_far, encoder_sums),
            (summed_far, summed),
            (tail_far, tail),
            (arrived_far, arrived),
            (tokens_grad_far, tokens_grad),
            (encoded_grad_far, encoded_grad),
        ],
        load_sem,
    )
    number = section * lax.axis_size("dp") + lax.axis_index("dp")

    def own(rows, count):
        width = rows.shape[1]
        return pltpu.roll(rows, (width - number * count) % width, axis=1)[:, :count]

    def own_line(rows, count):
        return own(jnp.concatenate([rows[i : i + 1] for i in range(rows.shape[0])], axis=1), count)

    for copy in loads[:3]:
        copy.wait()
    lane = iota((1, 128), 1)
    values = jnp.zeros((1, 128), F32)
    for sums, width, first, count_row, base in ((encoder_sums, DE, 10, 14, 0), (decoder_sums, DD, 12, 16, 4)):
        scale = 1.0 / (sums[count_row : count_row + 1, 0:1] * width)
        for i in range(4):
            value = jnp.sum(sums[first + i : first + i + 1, :], axis=1, keepdims=True) * scale
            values = jnp.where(lane == base + i, value, values)
    statistics[...] = jnp.sqrt(values)[:, :8]
    rows = own(encoder_sums[0:8, :DE], 24)
    e_biases[...] = rows[0:2]
    e_gains[...] = rows[2:4]
    e_shifts[...] = rows[4:6]
    e_inner[...] = own_line(encoder_sums[6:9], 96)
    rows = own(decoder_sums[0:8], 16)
    d_biases[...] = rows[0:3]
    mask_grad[...] = rows[3:4]
    d_gains[...] = rows[4:6]
    d_shifts[...] = rows[6:8]
    d_inner[...] = own_line(decoder_sums[8:12], 64)

    d_merge[...] = unpack(decoder_summed, DECODER_MERGE)
    d_expand[...] = unpack(decoder_summed, DECODER_EXPAND)
    d_shrink[...] = unpack(decoder_summed, DECODER_SHRINK)
    loads[3].wait()
    loads[4].wait()
    d_entry[...] = unpack(summed, ENTRY)
    d_attend[...] = unpack(summed, DECODER_ATTEND)
    for target, places in ((e_expand, ENCODER_EXPAND), (e_attend, ENCODER_ATTEND), (e_shrink, ENCODER_SHRINK)):
        start = 0
        for place in places:
            source = tail if place is ENCODER_ATTEND[2] else summed
            target[:, start : start + place[2]] = unpack(source, place)
            start += place[2]
    e_merge[...] = unpack(tail, ENCODER_MERGE)
    for copy in loads[5:]:
        copy.wait()

    @pl.when(section == 0)
    def _():
        boundary[0, 0] = tokens_grad[...]
        boundary[0, 1] = arrived[...].astype(F32)

    @pl.when(section == 1)
    def _():
        boundary[0, 0] = arrived[...].astype(F32)
        boundary[0, 1] = encoded_grad[...].astype(F32)


def finish_call(*operands):
    shapes = (
        (1, 2, 256, 768), (1, 8), (2, 24), (2, 24), (2, 24), (24, 2304), (24, 768), (24, 3072), (1, 96), (96, 768),
        (24, 512), (3, 16), (1, 16), (2, 16), (2, 16), (16, 768), (16, 256), (16, 2048), (1, 64), (64, 512),
    )
    outs = list(
        pl.pallas_call(
            finish_kernel,
            out_shape=tuple(jax.ShapeDtypeStruct(shape, F32) for shape in shapes),
            in_specs=[any_spec()] * len(operands),
            out_specs=(vmem_spec(),) * len(shapes),
            scratch_shapes=[pltpu.VMEM(operand.shape, operand.dtype) for operand in operands]
            + [pltpu.SemaphoreType.DMA((len(operands),))],
            compiler_params=pltpu.CompilerParams(vmem_limit_bytes=60 * 2**20),
            name="finish",
        )(*operands)
    )
    for line in (1, 8, 12, 18):
        outs[line] = outs[line].reshape(-1)
    for turned in (6, 16):
        outs[turned] = outs[turned].T
    return tuple(outs)


def scatter_sum(member, share_dim):
    return lax.psum_scatter(
        member, ("section", "dp"), scatter_dimension=share_dim, tiled=True
    )


def finish_generic(decoder_part, part, tail, decoder_sums, encoder_sums, tokens_grad, encoded_grad):
    section = lax.axis_index("section")
    payload = jnp.where(section == 0, encoded_grad, low(tokens_grad))

    def whole(packed, *places):
        packed = jnp.swapaxes(packed, 1, 2).reshape(-1, 32, 16, packed.shape[-1])
        blocks = [unpack(packed, place).reshape(32 * place[1], place[2]) for place in places]
        return scatter_sum(jnp.concatenate(blocks, axis=1).astype(F32), 0)

    def line(value):
        return scatter_sum(value, value.ndim - 1)

    arrived = lax.ppermute(payload, "section", [(0, 1), (1, 0)]).astype(F32)
    boundary = jnp.where(
        section == 0,
        jnp.stack([tokens_grad, arrived]),
        jnp.stack([arrived, encoded_grad.astype(F32)]),
    )
    sums = jnp.concatenate(
        [jnp.sum(encoder_sums[10:14], axis=1), jnp.sum(decoder_sums[12:16], axis=1)]
    )
    sums, counts = lax.psum((sums, (encoder_sums[14, 0], decoder_sums[16, 0])), ("section", "dp"))
    scales = jnp.concatenate([jnp.full((4,), counts[0] * DE), jnp.full((4,), counts[1] * DD)])
    return (
        boundary[None],
        jnp.sqrt(sums / scales),
        line(encoder_sums[2:4, :DE]),
        line(encoder_sums[4:6, :DE]),
        line(encoder_sums[0:2, :DE]),
        jnp.concatenate([whole(part, *ENCODER_ATTEND[:2]), whole(tail, ENCODER_ATTEND[2])], axis=1),
        whole(tail, ENCODER_MERGE).T,
        whole(part, *ENCODER_EXPAND),
        line(encoder_sums[6:9].reshape(-1)),
        whole(part, *ENCODER_SHRINK),
        whole(decoder_part[1], ENTRY),
        line(decoder_sums[0:3]),
        line(decoder_sums[3]),
        line(decoder_sums[4:6]),
        line(decoder_sums[6:8]),
        whole(decoder_part[1], DECODER_ATTEND),
        whole(decoder_part[0], DECODER_MERGE).T,
        whole(decoder_part[0], DECODER_EXPAND),
        line(decoder_sums[8:12].reshape(-1)),
        whole(decoder_part[0], DECODER_SHRINK),
    )


def body(
    visible_tokens,
    cotangent,
    chip_sizes,
    ground_distance,
    visible_slots,
    encoder_gains,
    encoder_shifts,
    encoder_biases,
    encoder_attend,
    encoder_merge,
    encoder_expand,
    encoder_inner,
    encoder_shrink,
    decoder_entry,
    decoder_biases,
    mask_token,
    decoder_gains,
    decoder_shifts,
    decoder_attend,
    decoder_merge,
    decoder_widen_weight,
    decoder_inner,
    decoder_shrink,
):
    reduce = (lax.axis_size("section"), lax.axis_size("dp")) == (2, 16)
    sent, sums, *kept = encoder_forward_call(
        chip_sizes, visible_tokens, encoder_gains, encoder_shifts, encoder_biases,
        encoder_attend, encoder_merge, encoder_expand, encoder_inner, encoder_shrink,
    )
    decoder_summed, rest, decoder_vectors, encoded_grad = decoder_call(
        reduce, chip_sizes, ground_distance, visible_slots, sent, cotangent, decoder_entry, decoder_biases, mask_token,
        decoder_gains, decoder_shifts, decoder_attend, decoder_merge, decoder_widen_weight, decoder_inner,
        decoder_shrink,
    )
    summed, tail, encoder_sums, tokens_grad, *more = encoder_backward_call(
        reduce, visible_tokens, encoded_grad, sums, decoder_vectors, rest, kept,
        encoder_gains, encoder_attend, encoder_merge, encoder_expand, encoder_shrink,
    )
    if reduce:
        decoder_sums, arrived = more
        return finish_call(
            decoder_summed, decoder_sums, encoder_sums, summed, tail, arrived, tokens_grad, encoded_grad
        )
    return finish_generic(
        (decoder_summed, rest), summed, tail, decoder_vectors, encoder_sums, tokens_grad, encoded_grad
    )


def solution(mesh):
    in_specs = (
        P("dp", None, None),
        P("dp", None, None),
        P("dp", None),
        P("dp", None),
        P("dp", None),
        P(),
        P(),
        P(),
        P(),
        P(),
        P(),
        P(),
        P(),
        P(),
        P(),
        P(),
        P(),
        P(),
        P(),
        P(),
        P(),
        P(),
        P(),
    )
    out_specs = (
        P("section", "dp", None, None),
        P(),
        P(None, ("section", "dp")),
        P(None, ("section", "dp")),
        P(None, ("section", "dp")),
        P(("section", "dp"), None),
        P(None, ("section", "dp")),
        P(("section", "dp"), None),
        P(("section", "dp")),
        P(("section", "dp"), None),
        P(("section", "dp"), None),
        P(None, ("section", "dp")),
        P(("section", "dp")),
        P(None, ("section", "dp")),
        P(None, ("section", "dp")),
        P(("section", "dp"), None),
        P(None, ("section", "dp")),
        P(("section", "dp"), None),
        P(("section", "dp")),
        P(("section", "dp"), None),
    )
    return jax.shard_map(body, mesh=mesh, in_specs=in_specs, out_specs=out_specs, check_vma=False)
```

```python
import functools
import types

import jax
import jax.numpy as jnp
import numpy as np
from jax import lax
from jax.experimental import pallas as pl
from jax.experimental.pallas import tpu as pltpu
from jax.sharding import PartitionSpec as P

DE = 768
DD = 512
TILE = 256
BLOCK = 512
NEGATIVE = -1e30
F32, BF16 = jnp.float32, jnp.bfloat16
MESH_ID = pl.DeviceIdType.MESH

CANON = ("x", "z2", "z1", "y")
ROUTES = (("x", "y", "z1", "z2"), ("y", "x", "z1", "z2"), ("z1", "z2", "x", "y"))
UNIT = 1536
LAG = 2
DECODER_PLAN = types.SimpleNamespace(widths=(2, 2, 1), chunks=7, slots=7, ring=3, span=640)
ENCODER_PLAN = types.SimpleNamespace(widths=(3, 6, 3), chunks=9, slots=3, ring=3, span=1536)
TAIL_PLAN = types.SimpleNamespace(widths=(2, 3, 1), chunks=2, slots=2, ring=2, span=768)

DECODER_EXPAND, DECODER_SHRINK, DECODER_MERGE = (0, 16, 2048), (2048, 64, 512), (4096, 16, 256)
ENTRY, DECODER_ATTEND = (0, 24, 512), (768, 16, 768)
ENCODER_SHRINK = tuple((UNIT * (1 + part), 96, 256) for part in range(3))
ENCODER_EXPAND = tuple((UNIT * (4 + part), 24, 1024) for part in range(3))
ENCODER_ATTEND = ((UNIT * 7, 24, 1024), (UNIT * 8, 24, 1024), (0, 24, 256))
ENCODER_MERGE = (384, 24, 768)


def dot(a, b):
    return jnp.dot(a, b, preferred_element_type=F32)


def dot_nt(a, b):
    return lax.dot_general(a, b, (((1,), (1,)), ((), ())), preferred_element_type=F32)


def dot_tn(a, b):
    return lax.dot_general(a, b, (((0,), (0,)), ((), ())), preferred_element_type=F32)


def low(value):
    return value.astype(BF16)


def standardize(values):
    centered = values - jnp.mean(values, axis=-1, keepdims=True)
    inverse = lax.rsqrt(jnp.mean(centered * centered, axis=-1, keepdims=True) + 1e-05)
    return centered * inverse, inverse


def norm_back(unit, inverse, gain, grad):
    inner = grad * gain
    return inverse * (
        inner
        - jnp.mean(inner, axis=-1, keepdims=True)
        - unit * jnp.mean(inner * unit, axis=-1, keepdims=True)
    )


def row_sum(values):
    return jnp.sum(values, axis=0, keepdims=True)


def gelu_pair(before):
    half = 0.5 * (1.0 + lax.erf(before * 0.7071067811865476))
    density = jnp.exp(-0.5 * before * before) * 0.3989422804014327
    return before * half, half + before * density


def chip_of(places, sizes, pack):
    end = sizes[pack, 0]
    chip = (places >= end).astype(jnp.int32)
    for slot in range(1, 4):
        end = end + sizes[pack, slot]
        chip = chip + (places >= end).astype(jnp.int32)
    return chip


def iota(shape, dimension):
    return lax.broadcasted_iota(jnp.int32, shape, dimension)


def aligned(start, size, unit):
    if isinstance(start, int):
        return slice(start, start + size)
    return pl.ds(pl.multiple_of(start, unit), size)


def pair_lanes(pair, base=0):
    return aligned(base + pair * 128, 128, 128)


def head_rows(pair, half, base=0):
    return aligned(base + pair * 128 + half * 64, 64, 64)


def rows_of(tile, size=TILE):
    return aligned(tile * size, size, size)


def only(values, half):
    return jnp.where(iota((1, 128), 1) // 64 == half, values, jnp.zeros_like(values))


def fetch(pairs, sems):
    copies = [
        pltpu.make_async_copy(source, target, sems.at[i]) for i, (source, target) in enumerate(pairs)
    ]
    for copy in copies:
        copy.start()
    return copies


def store_packed(put, first, place, value):
    offset, count, width = place
    value = value.reshape(-1, count, width)
    shards = slice(first, first + value.shape[0]) if isinstance(first, int) else pl.ds(first, value.shape[0])
    for piece in range(count // 16):
        put(shards, offset + piece * width, value[:, piece * 16 : piece * 16 + 16])
    if count % 16:
        half = width // 2
        rest = value[:, count - 8 :]
        rest = jnp.concatenate([rest[:, :, :half], rest[:, :, half:]], axis=1)
        put(shards, offset + count // 16 * width, rest)


def halves(shards, value):
    pairs = value.reshape(value.shape[0] // 2, 2, *value.shape[1:])
    if isinstance(shards, slice):
        return slice(shards.start // 2, shards.stop // 2), pairs[:, 0], pairs[:, 1]
    return pl.ds(shards.start // 2, shards.size // 2), pairs[:, 0], pairs[:, 1]


def place_of(names, bits):
    index = 0
    for name in names:
        index = index * 2 + bits[name]
    return index


def left_after(route, stage):
    return tuple(name for name in CANON if name not in route[:stage])


def choices(names):
    for number in range(2 ** len(names)):
        yield {name: (number >> (len(names) - 1 - i)) & 1 for i, name in enumerate(names)}


def neighbours():
    section = lax.axis_index("section")
    data = lax.axis_index("dp")
    mine = {"x": section, "c": data % 2, "y": data // 2 % 2, "z1": data // 4 % 2, "z2": data // 8 % 2}
    partner = {"x": (1 - section, data)}
    for name, step in {"c": 1, "y": 2, "z1": 4, "z2": 8}.items():
        partner[name] = (section, data + step * (1 - 2 * mine[name]))
    return mine, partner


def greet(partner):
    barrier = pltpu.get_barrier_semaphore()
    for name in ("c",) + CANON:
        pl.semaphore_signal(barrier, inc=1, device_id=partner[name], device_id_type=MESH_ID)


def await_greetings():
    pl.semaphore_wait(pltpu.get_barrier_semaphore(), 5)


def remote(source, target, send, recv, device):
    return pltpu.make_async_remote_copy(
        src_ref=source,
        dst_ref=target,
        send_sem=send,
        recv_sem=recv,
        device_id=device,
        device_id_type=MESH_ID,
    )


def reducer(plan, mine, partner, out, refs):
    chunks, slots, span, ring = plan.chunks, plan.slots, plan.span, plan.ring
    progress = types.SimpleNamespace(sent=0)
    own, staging, first = refs[:3]
    sent, got = refs[3:15], refs[15:27]
    first_send, first_recv, send_sem, recv_sem = refs[27:31]

    def first_copy(chunk):
        return remote(staging.at[chunk % slots], first.at[chunk], first_send.at[chunk], first_recv.at[chunk], partner["c"])

    def stage_copy(route, stage, chunk):
        return remote(
            sent[route * 4 + stage].at[chunk % ring],
            got[route * 4 + stage].at[chunk],
            send_sem.at[route, stage, chunk],
            recv_sem.at[route, stage, chunk],
            partner[ROUTES[route][stage]],
        )

    def total(route, stage, chunk, bits):
        spot = place_of(CANON, bits)
        cols = slice(sum(plan.widths[:route]) * 128, sum(plan.widths[: route + 1]) * 128)
        value = own[chunk, spot, :, cols].astype(F32) + first[chunk, spot, :, cols].astype(F32)
        for earlier in range(stage):
            names = left_after(ROUTES[route], earlier + 1)
            value = value + got[route * 4 + earlier][chunk, place_of(names, bits)].astype(F32)
        return value

    def advance(stage, chunk):
        for route in range(3):
            if stage:
                stage_copy(route, stage - 1, chunk).wait_recv()
            else:
                first_copy(chunk).wait_recv() if route == 0 else None
            if stage < 4:

                @pl.when(chunk >= ring)
                def _(route=route):
                    stage_copy(route, stage, chunk - ring).wait_send()

        values = []
        for route in range(3):
            path = ROUTES[route]
            if stage == 4:
                values.append(total(route, 4, chunk, mine))
                continue
            names = left_after(path, stage + 1)
            for free in choices(names):
                bits = dict(mine)
                bits[path[stage]] = 1 - mine[path[stage]]
                bits.update(free)
                values.append((route, place_of(names, free), low(total(route, stage, chunk, bits))))
        if stage == 4:
            out[chunk] = jnp.concatenate(values, axis=1)
            return
        for route, spot, value in values:
            sent[route * 4 + stage][chunk % ring, spot] = value
        for route in range(3):
            stage_copy(route, stage, chunk).start()

    def turn(number):
        for stage in range(4, -1, -1):
            chunk = number - LAG * stage
            pl.when((chunk >= 0) & (chunk < chunks))(functools.partial(advance, stage, chunk))

    def put(shards, column, value):
        shards, even, odd = halves(shards, value)
        kept = low(jnp.where(mine["c"] == 0, even, odd))
        given = low(jnp.where(mine["c"] == 0, odd, even))
        width = value.shape[2]
        done = 0
        while done < width:
            chunk, start = divmod(column + done, span)
            size = min(width - done, span - start)
            own[chunk, shards, :, start : start + size] = kept[:, :, done : done + size]
            staging[chunk % slots, shards, :, start : start + size] = given[:, :, done : done + size]
            done += size

    def put_unit(unit):
        def put(shards, column, value):
            shards, even, odd = halves(shards, value)
            cols = slice(column, column + value.shape[2])
            own[unit, shards, :, cols] = low(jnp.where(mine["c"] == 0, even, odd))
            staging[unit % slots, shards, :, cols] = low(jnp.where(mine["c"] == 0, odd, even))

        @pl.when(unit >= slots)
        def _():
            first_copy(unit - slots).wait_send()

        return put

    def send(column):
        while (progress.sent + 1) * span <= column:
            first_copy(progress.sent).start()
            progress.sent += 1

    def close():
        for chunk in range(max(0, chunks - slots), chunks):
            first_copy(chunk).wait_send()
        for chunk in range(chunks - ring, chunks):
            for route in range(3):
                for stage in range(4):
                    stage_copy(route, stage, chunk).wait_send()

    return types.SimpleNamespace(
        own=own, staging=staging, turn=turn, put=put, put_unit=put_unit, first_copy=first_copy, send=send, close=close
    )


def reducer_scratch(plan):
    stages = [(width, block) for width in plan.widths for block in (8, 4, 2, 1)]
    return (
        [
            pltpu.VMEM((plan.chunks, 16, 16, plan.span), BF16),
            pltpu.VMEM((plan.slots, 16, 16, plan.span), BF16),
            pltpu.VMEM((plan.chunks, 16, 16, plan.span), BF16),
        ]
        + [pltpu.VMEM((plan.ring, block, 16, width * 128), BF16) for width, block in stages]
        + [pltpu.VMEM((plan.chunks, block, 16, width * 128), BF16) for width, block in stages]
        + [
            pltpu.SemaphoreType.DMA((plan.chunks,)),
            pltpu.SemaphoreType.DMA((plan.chunks,)),
            pltpu.SemaphoreType.DMA((3, 4, plan.chunks)),
            pltpu.SemaphoreType.DMA((3, 4, plan.chunks)),
        ]
    )


def put_into(parts):
    span = parts.shape[-1]

    def put(shards, column, value):
        shards, *pair = halves(shards, value)
        width = value.shape[2]
        done = 0
        while done < width:
            chunk, start = divmod(column + done, span)
            size = min(width - done, span - start)
            for core in range(2):
                parts[chunk, core, shards, :, start : start + size] = low(pair[core][:, :, done : done + size])
            done += size

    return put


def put_unit_into(parts, unit):
    def put(shards, column, value):
        shards, *pair = halves(shards, value)
        for core in range(2):
            parts[unit, core, shards, :, column : column + value.shape[2]] = low(pair[core])

    return put


def vmem_spec():
    return pl.BlockSpec(memory_space=pltpu.VMEM)


def any_spec():
    return pl.BlockSpec(memory_space=pl.ANY)


def smem_spec():
    return pl.BlockSpec(memory_space=pltpu.SMEM)


def encoder_forward_kernel(
    sizes, gains, shifts, biases, inner, tokens, attend_far, merging_far, expand_far, shrink_far,
    sent, vectors, *refs,
):
    far = refs[:9]
    normed, mixed, turned, probs, context, middle, normed_two, active, slope = refs[9:18]
    hidden, attend, merging, expand, shrink, context_turned, load_sem, save_sem = refs[18:]
    pack = lax.axis_index("section")
    loads = fetch(
        [
            (tokens.at[pack], hidden),
            *[(attend_far.at[:, i * 768 : i * 768 + 768], attend.at[:, i * 768 : i * 768 + 768]) for i in range(3)],
            (merging_far, merging),
            *[(expand_far.at[:, i * 1024 : i * 1024 + 1024], expand.at[:, i * 1024 : i * 1024 + 1024]) for i in range(3)],
            *[(shrink_far.at[i * 1024 : i * 1024 + 1024], shrink.at[i * 1024 : i * 1024 + 1024]) for i in range(3)],
        ],
        load_sem,
    )
    saves = []

    def save(*numbers):
        for number in numbers:
            copy = pltpu.make_async_copy(refs[9 + number], far[number], save_sem.at[number])
            copy.start()
            saves.append(copy)

    vectors[...] = jnp.zeros_like(vectors)
    key_chip = chip_of(4 * iota((TILE, 1), 0), sizes, pack)
    own_chip = chip_of(4 * iota((1, TILE), 1), sizes, pack)
    valid = (key_chip < 4).astype(F32)
    loads[0].wait()
    values = hidden[...]
    vectors[10:11, :768] = row_sum(valid * values * values)
    unit, _ = standardize(values)
    norm = low(unit * gains[0:1] + shifts[0:1])
    normed[...] = norm
    for part in range(3):
        cols = slice(part * 768, part * 768 + 768)
        loads[1 + part].wait()
        mix = dot(norm, attend[:, cols])
        mixed[:, cols] = low(mix)
        if part:
            turned[(part - 1) * 768 : part * 768] = low(mix.T)
    save(0, 1, 2)

    def score(head):
        pair, half = divmod(head, 2)
        query = only(mixed[:, pair_lanes(pair)], half) * BF16(0.125)
        return dot_nt(mixed[:, pair_lanes(pair, 768)], query)

    ready = [score(0), score(1)]
    for head in range(12):
        if head + 2 < 12:
            ready.append(score(head + 2))
        scores = jnp.where(key_chip == own_chip, ready[head], NEGATIVE)
        expos = jnp.exp(scores - jnp.max(scores, axis=0, keepdims=True))
        prob = low(expos * (1.0 / jnp.sum(expos, axis=0, keepdims=True)))
        probs[head] = prob
        context_turned[head * 64 : head * 64 + 64] = dot(turned[768 + head * 64 : 832 + head * 64], prob)

    mingled = low(context_turned[...].T)
    context[...] = mingled
    save(3, 4)
    loads[4].wait()
    attention = dot(mingled, merging[...]) + biases[0:1]
    vectors[11:12, :768] = row_sum(valid * attention * attention)
    center = hidden[...] + attention
    middle[...] = center
    unit, _ = standardize(center)
    norm = low(unit * gains[1:2] + shifts[1:2])
    normed_two[...] = norm
    save(5, 6)
    feed = jnp.zeros_like(center)
    def widened(part):
        if part % 2 == 0:
            loads[5 + part // 2].wait()
        cols = slice(part * 512, part * 512 + 512)
        return dot(norm, expand[:, cols]) + inner[:, cols]

    ready = [widened(0)]
    for part in range(6):
        if part < 5:
            ready.append(widened(part + 1))
        cols = slice(part * 512, part * 512 + 512)
        value, slant = gelu_pair(ready[part])
        value = low(value)
        active[:, cols] = value
        slope[part // 2, :, part % 2 * 512 : part % 2 * 512 + 512] = slant
        if part % 2 == 0:
            loads[8 + part // 2].wait()
        feed = feed + dot(value, shrink[cols])
    save(7, 8)
    feed = feed + biases[1:2]
    vectors[12:13, :768] = row_sum(valid * feed * feed)
    output = center + feed
    vectors[13:14, :768] = row_sum(valid * output * output)
    vectors[14:15, :768] = jnp.broadcast_to(row_sum(valid), (1, 768))
    sent[...] = low(output)
    for copy in saves:
        copy.wait()


def encoder_forward_call(sizes, tokens, gains, shifts, biases, attend, merging, expand, inner, shrink):
    shapes = (
        ((256, 768), BF16),
        ((256, 2304), BF16),
        ((1536, 256), BF16),
        ((12, 256, 256), BF16),
        ((256, 768), BF16),
        ((256, 768), F32),
        ((256, 768), BF16),
        ((256, 3072), BF16),
        ((3, 256, 1024), F32),
    )
    return pl.pallas_call(
        encoder_forward_kernel,
        out_shape=(jax.ShapeDtypeStruct((256, 768), BF16), jax.ShapeDtypeStruct((16, 1024), F32))
        + tuple(jax.ShapeDtypeStruct(*shape) for shape in shapes),
        in_specs=[smem_spec()] + [vmem_spec()] * 4 + [any_spec()] * 5,
        out_specs=(vmem_spec(),) * 2 + (any_spec(),) * len(shapes),
        scratch_shapes=[pltpu.VMEM(*shape) for shape in shapes]
        + [
            pltpu.VMEM((256, 768), F32),
            pltpu.VMEM(attend.shape, BF16),
            pltpu.VMEM(merging.shape, BF16),
            pltpu.VMEM(expand.shape, BF16),
            pltpu.VMEM(shrink.shape, BF16),
            pltpu.VMEM((768, 256), F32),
            pltpu.SemaphoreType.DMA((11,)),
            pltpu.SemaphoreType.DMA((len(shapes),)),
        ],
        compiler_params=pltpu.CompilerParams(vmem_limit_bytes=60 * 2**20),
        name="encoder_forward",
    )(sizes, gains, shifts, biases, inner[None], tokens, attend, merging, expand, shrink)


def decoder_kernel(
    reduce, sizes, distance, slots, frequency, sent, biases, mask_token, gains, shifts, inner,
    cotangent, entry_far, attend_far, merging_far, expand_far, shrink_far,
    summed, rest, vectors, encoded_grad, *refs,
):
    (
        table, start, normed, mixed, turned, probs, flipped, context, normed_two, active,
        before_grad, go_low, attention_low, context_grad, delta, mixed_grad, target, masked_keys,
        entry_weight, attend, merging, expand, shrink, load_sem,
    ) = refs[:24]
    pack = lax.axis_index("section")
    if reduce:
        mine, partner = neighbours()
        greet(partner)
        engine = reducer(DECODER_PLAN, mine, partner, summed, refs[24:])
        put = engine.put
    else:
        put = put_into(summed)
    put_rest = put_into(rest)
    loads = fetch(
        [
            (entry_far, entry_weight),
            (attend_far, attend),
            (cotangent.at[pack], target),
            (merging_far, merging),
            (expand_far, expand),
            (shrink_far, shrink),
        ],
        load_sem,
    )
    tiles = start.shape[0] // TILE
    vectors[...] = jnp.zeros_like(vectors)
    large = sizes[pack, 0] == 1024

    def add_row(row, value):
        vectors[row : row + 1, :] += value

    positions = iota((32, 128), 0).astype(F32)
    for chip in range(4):
        spacing = distance[pack, chip].astype(F32) / 16.0
        angle = positions * (spacing * frequency[...])
        table[0, chip] = jnp.sin(angle)
        table[1, chip] = jnp.cos(angle)
    loads[0].wait()
    entry = low(dot(sent[...], entry_weight[...]) + biases[0:1])
    loads[1].wait()

    blocks = start.shape[0] // BLOCK

    def slot_chip(tile, size):
        return chip_of(iota((size, 1), 0) + tile * size, sizes, pack)

    def validity(tile, size):
        return (slot_chip(tile, size) < 4).astype(F32)

    def spread_of(tile):
        return (slots[pl.ds(pack, 1)] == iota((TILE, TILE), 0) + tile * TILE).astype(F32)

    def encoding_of(tile):
        pieces = []
        for kind in range(2):
            wave = table[kind, 0, aligned(tile * 8, 8, 8)]
            big = jnp.broadcast_to(wave[:, None], (8, 32, 128)).reshape(TILE, 128)
            wave = table[kind, tile, 0:16]
            own = jnp.broadcast_to(wave[:, None], (16, 16, 128)).reshape(TILE, 128)
            pieces.append(jnp.where(large, big, own))
        for kind in range(2):
            wave = table[kind, 0]
            big = jnp.broadcast_to(wave[None], (8, 32, 128)).reshape(TILE, 128)
            wave = table[kind, tile, 0:16]
            own = jnp.broadcast_to(wave[None], (16, 16, 128)).reshape(TILE, 128)
            pieces.append(jnp.where(large, big, own))
        return jnp.concatenate(pieces, axis=1)

    @pl.loop(0, tiles)
    def _(tile):
        rows = rows_of(tile)
        valid = validity(tile, TILE)
        spread = spread_of(tile)
        fill = valid * (1.0 - jnp.sum(spread, axis=1, keepdims=True))
        hidden = dot(low(spread), entry) + fill * mask_token[...] + encoding_of(tile) * valid
        start[rows] = hidden
        add_row(12, row_sum(valid * hidden * hidden))
        add_row(16, row_sum(valid))
        unit, _ = standardize(hidden)
        norm = low(unit * gains[0:1] + shifts[0:1])
        normed[rows] = norm
        mix = dot(norm, attend[...])
        mix_low = low(mix)
        mixed[rows] = mix_low
        turned[:, rows] = low(mix[:, 256:].T)
        lane = iota((TILE, 128), 1)
        other = (lane % 64 < 5) & (lane % 64 != slot_chip(tile, TILE))
        other = jnp.where(other, NEGATIVE, 0.0).astype(BF16)
        for head in range(4):
            lanes = slice(256 + head // 2 * 128, 384 + head // 2 * 128)
            masked_keys[head, rows] = jnp.where(lane // 64 == head % 2, mix_low[:, lanes], other)

    @pl.loop(0, 2 * tiles)
    def _(step):
        pair, tile = step // tiles, step % tiles
        rows = rows_of(tile)
        lane = iota((TILE, 128), 1)
        chosen = (lane % 64 == slot_chip(tile, TILE)).astype(F32).astype(BF16)
        for half in range(2):
            query = jnp.where(lane // 64 == half, mixed[rows, pair_lanes(pair)] * BF16(0.125), chosen)
            scores = dot_nt(masked_keys[pair * 2 + half], query)
            expos = jnp.exp(scores - jnp.max(scores, axis=0, keepdims=True))
            prob = low(expos * (1.0 / jnp.sum(expos, axis=0, keepdims=True)))
            probs[pair * 2 + half, :, rows] = prob
            flipped[head_rows(pair, half), rows] = dot(turned[head_rows(pair, half, 256)], prob)

    for copy in loads[2:]:
        copy.wait()

    @pl.loop(0, blocks)
    def _(tile):
        rows = rows_of(tile, BLOCK)
        valid = validity(tile, BLOCK)
        mingled = low(flipped[:, rows].T)
        context[rows] = mingled
        attention = dot(mingled, merging[...]) + biases[1:2]
        add_row(13, row_sum(valid * attention * attention))
        unit, _ = standardize(start[rows] + attention)
        norm = low(unit * gains[1:2] + shifts[1:2])
        normed_two[rows] = norm
        go = target[rows] * valid
        go_below = low(go)
        go_low[rows] = go_below
        add_row(2, row_sum(go))
        for part in range(8):
            cols = slice(part * 256, part * 256 + 256)
            value, slope = gelu_pair(dot(norm, expand[:, cols]) + inner[:, cols])
            active[rows, cols] = low(value)
            grad = low(slope * dot_nt(go_below, shrink[cols]))
            before_grad[rows, cols] = grad
            lanes = slice(part % 2 * 256, part % 2 * 256 + 256)
            vectors[8 + part // 2 : 9 + part // 2, lanes] += row_sum(grad.astype(F32))

    if reduce:
        await_greetings()
    for part in range(2):
        cols = slice(part * 256, part * 256 + 256)
        store_packed(put, part * 16, DECODER_EXPAND, dot_tn(normed_two[:, cols], before_grad[...]))
    if reduce:
        engine.send(2048)

    @pl.loop(0, 8)
    def _(part):
        cols = aligned(part * 256, 256, 256)
        store_packed(put, part * 4, DECODER_SHRINK, dot_tn(active[:, cols], go_low[...]))

    if reduce:
        engine.send(4096)

    @pl.loop(0, tiles)
    def _(tile):
        rows = rows_of(tile)
        valid = validity(tile, TILE)
        center = start[rows] + (dot(context[rows], merging[...]) + biases[1:2])
        unit, inverse = standardize(center)
        feed = dot(active[rows], shrink[...]) + biases[2:3]
        add_row(14, row_sum(valid * feed * feed))
        output = center + feed
        add_row(15, row_sum(valid * output * output))
        norm_grad = dot_nt(before_grad[rows], expand[...])
        add_row(5, row_sum(norm_grad * unit))
        add_row(7, row_sum(norm_grad))
        grad = target[rows] * valid + norm_back(unit, inverse, gains[1:2], norm_grad)
        target[rows] = grad
        add_row(1, row_sum(grad))
        below = low(grad)
        attention_low[rows] = below
        outer = low(dot_nt(below, merging[...]))
        context_grad[rows] = outer
        product = (outer.astype(F32) * flipped[:, rows].T).T
        for head in range(4):
            delta[head, :, rows] = row_sum(product[head * 64 : head * 64 + 64])
        if reduce:
            engine.turn(tile)

    for part in range(2):
        cols = slice(part * 256, part * 256 + 256)
        store_packed(put, part * 16, DECODER_MERGE, dot_tn(attention_low[:, cols], context[...]))
        shards = slice(part * 16, part * 16 + 16)
        put(shards, 4352, jnp.zeros((16, 16, DECODER_PLAN.chunks * DECODER_PLAN.span - 4352), F32))
    if reduce:
        engine.send(DECODER_PLAN.chunks * DECODER_PLAN.span)

    flipped[...] = jnp.zeros_like(flipped)

    @pl.loop(0, 2 * tiles)
    def _(step):
        pair, tile = step // tiles, step % tiles
        rows = rows_of(tile)
        lanes = pair_lanes(pair)
        values = mixed[rows, pair_lanes(pair, 512)]
        raws, probabilities, queries, outers = [], [], [], []
        for half in range(2):
            prob = probs[pair * 2 + half, rows]
            outer = only(context_grad[:, lanes], half)
            raw = low(prob.astype(F32) * (dot_nt(values, outer) - delta[pair * 2 + half]))
            flipped[head_rows(pair, half)] += dot(turned[head_rows(pair, half), rows], raw)
            raws.append(raw)
            probabilities.append(prob)
            outers.append(outer)
            queries.append(only(mixed[:, lanes], half))
        key_grad = dot(jnp.concatenate(raws, axis=1), jnp.concatenate(queries, axis=0))
        mixed_grad[rows, pair_lanes(pair, 256)] = low(key_grad * 0.125)
        value_grad = dot(jnp.concatenate(probabilities, axis=1), jnp.concatenate(outers, axis=0))
        mixed_grad[rows, pair_lanes(pair, 512)] = low(value_grad)
        if reduce:
            engine.turn(tiles + step)

    def last(tile, entry_grad):
        rows = rows_of(tile)
        mixed_grad[rows, 0:256] = low(flipped[:, rows].T * 0.125)
        norm_grad = dot_nt(mixed_grad[rows], attend[...])
        unit, inverse = standardize(start[rows])
        add_row(4, row_sum(norm_grad * unit))
        add_row(6, row_sum(norm_grad))
        grad = target[rows] + norm_back(unit, inverse, gains[0:1], norm_grad)
        spread = spread_of(tile)
        fill = validity(tile, TILE) * (1.0 - jnp.sum(spread, axis=1, keepdims=True))
        add_row(3, row_sum(fill * grad))
        if reduce:
            engine.turn(3 * tiles + tile)
        return entry_grad + dot_tn(low(spread), low(grad))

    entry_grad = lax.fori_loop(0, tiles, last, jnp.zeros((TILE, 512), F32))
    add_row(0, row_sum(entry_grad))
    entry_low = low(entry_grad)
    encoded_grad[...] = low(dot_nt(entry_low, entry_weight[...]))
    store_packed(put_rest, 0, ENTRY, dot_tn(sent[...], entry_low))

    @pl.loop(0, 2)
    def _(part):
        cols = aligned(part * 256, 256, 256)
        store_packed(put_rest, part * 16, DECODER_ATTEND, dot_tn(normed[:, cols], mixed_grad[...]))

    if reduce:
        engine.close()


def decoder_call(
    reduce, sizes, distance, slots, sent, cotangent, entry_weight, biases, mask_token,
    gains, shifts, attend, merging, expand, inner, shrink,
):
    length = cotangent.shape[1]
    width = 512
    frequency = np.exp(-np.log(10000.0) * np.arange(width // 4) / (width // 4)).astype(np.float32)
    if reduce:
        summed = jax.ShapeDtypeStruct((DECODER_PLAN.chunks, 16, DECODER_PLAN.span), F32)
        extra = reducer_scratch(DECODER_PLAN)
        params = dict(collective_id=1, has_side_effects=True)
    else:
        summed = jax.ShapeDtypeStruct((DECODER_PLAN.chunks, 2, 16, 16, DECODER_PLAN.span), BF16)
        extra = []
        params = dict()
    return pl.pallas_call(
        functools.partial(decoder_kernel, reduce),
        out_shape=(
            summed,
            jax.ShapeDtypeStruct((1, 2, 16, 16, UNIT), BF16),
            jax.ShapeDtypeStruct((24, width), F32),
            jax.ShapeDtypeStruct((256, 768), BF16),
        ),
        in_specs=[smem_spec()] * 2 + [vmem_spec()] * 8 + [any_spec()] * 6,
        out_specs=(vmem_spec(),) * 4,
        scratch_shapes=[
            pltpu.VMEM((2, 4, 32, 128), F32),
            pltpu.VMEM((length, width), F32),
            pltpu.VMEM((length, width), BF16),
            pltpu.VMEM((length, 768), BF16),
            pltpu.VMEM((512, length), BF16),
            pltpu.VMEM((4, length, length), BF16),
            pltpu.VMEM((256, length), F32),
            pltpu.VMEM((length, 256), BF16),
            pltpu.VMEM((length, width), BF16),
            pltpu.VMEM((length, 2048), BF16),
            pltpu.VMEM((length, 2048), BF16),
            pltpu.VMEM((length, width), BF16),
            pltpu.VMEM((length, width), BF16),
            pltpu.VMEM((length, 256), BF16),
            pltpu.VMEM((4, 1, length), F32),
            pltpu.VMEM((length, 768), BF16),
            pltpu.VMEM((length, width), F32),
            pltpu.VMEM((4, length, 128), BF16),
            pltpu.VMEM(entry_weight.shape, BF16),
            pltpu.VMEM(attend.shape, BF16),
            pltpu.VMEM(merging.shape, BF16),
            pltpu.VMEM(expand.shape, BF16),
            pltpu.VMEM(shrink.shape, BF16),
            pltpu.SemaphoreType.DMA((6,)),
        ]
        + extra,
        compiler_params=pltpu.CompilerParams(vmem_limit_bytes=63 * 2**20, **params),
        name="decoder_block",
    )(
        sizes, distance, slots, jnp.asarray(frequency)[None], sent, biases, mask_token[None], gains, shifts,
        inner[None], cotangent, entry_weight, attend, merging, expand, shrink,
    )


def encoder_backward_kernel(
    reduce, encoded_grad, sums, decoder_vectors, gains, tokens, rest, attend_far, merging_far, expand_far,
    shrink_far, normed_far, mixed_far, turned_far, probs_far, context_far, middle_far, normed_two_far, active_far,
    slope_far, summed, tail_summed, vectors, tokens_grad, *refs,
):
    if reduce:
        decoder_sums, arrived = refs[:2]
        refs = refs[2:]
    (
        hidden, attend, merging, expand, shrink, normed, mixed, turned, probs, context, middle, normed_two, active,
        slope, before_grad, norm_sum, attention_low, context_grad, key_grad, query_turned, mixed_grad, active_turned,
        flipped, inner_sum, load_sem, part_sem,
    ) = refs[:26]
    pack = lax.axis_index("section")

    def part_loads(part):
        cols = aligned(part * 1024, 1024, 1024)
        slot = part % 2
        return [
            pltpu.make_async_copy(expand_far.at[:, cols], expand.at[slot], part_sem.at[slot, 0]),
            pltpu.make_async_copy(shrink_far.at[cols], shrink.at[slot], part_sem.at[slot, 1]),
            pltpu.make_async_copy(slope_far.at[part], slope.at[slot], part_sem.at[slot, 2]),
        ]

    if reduce:
        (
            decoder_total, encoder_total, decoder_got, encoder_got, payload,
            own_sem, small_send, small_recv, pay_send, pay_recv, small_load,
        ) = refs[26:37]
        mine, partner = neighbours()
        greet(partner)
        engine = reducer(ENCODER_PLAN, mine, partner, summed, refs[37:68])
        tail = reducer(TAIL_PLAN, mine, partner, tail_summed, refs[68:])
        put_tail = tail.put
        first_own = fetch(
            [
                pair
                for pair in (
                    (rest.at[0, 1 - mine["c"]], engine.staging.at[0]),
                    (rest.at[0, mine["c"]], engine.own.at[0]),
                )
            ],
            own_sem,
        )
        decoder_load = pltpu.make_async_copy(decoder_vectors, decoder_total.at[0], small_load)
        decoder_load.start()
    else:
        put_tail = put_into(tail_summed)
    early = pltpu.make_async_copy(active_far, active, load_sem.at[10])
    early.start()
    for copy in part_loads(0):
        copy.start()
    if reduce:
        for copy in first_own:
            copy.wait()
        await_greetings()
        engine.first_copy(0).start()
    loads = fetch(
        [
            (normed_two_far, normed_two),
            (middle_far, middle),
            (merging_far, merging),
            (context_far, context),
            (mixed_far, mixed),
            (probs_far, probs),
            (turned_far.at[0:768], turned),
            (normed_far, normed),
            (attend_far, attend),
            (tokens.at[pack], hidden),
        ],
        load_sem,
    )
    for copy in part_loads(1):
        copy.start()
    vectors[...] = sums[...]
    go_low = encoded_grad[...]
    go = go_low.astype(F32)
    vectors[1:2, :768] = row_sum(go)
    norm_sum[...] = jnp.zeros_like(norm_sum)

    def unit_grad(unit, place, pieces):
        put = engine.put_unit(unit) if reduce else put_unit_into(summed, unit)
        for first, value in pieces:
            store_packed(put, first, (0,) + place[1:], value)
        if reduce:
            engine.first_copy(unit).start()

    def shrink_start():
        early.wait()
        for piece in range(4):
            rows = slice(piece * 768, piece * 768 + 768)
            active_turned[rows] = active[:, rows].T

    def shrink_grad(part):
        cols = aligned(part * 256, 256, 256)
        pieces = []
        for piece in range(4):
            rows = slice(piece * 768, piece * 768 + 768)
            pieces.append((piece * 8, dot(active_turned[rows], encoded_grad[:, cols])))
        unit_grad(1 + part, ENCODER_SHRINK[0], pieces)

    def hidden_layer(part):
        for copy in part_loads(part):
            copy.wait()
        slot = part % 2
        grad = low(slope[slot] * dot_nt(encoded_grad[...], shrink[slot]))
        before_grad[...] = grad
        inner_sum[part] = row_sum(grad.astype(F32))
        norm_sum[...] += dot_nt(grad, expand[slot])

        @pl.when(part == 0)
        def _():
            for copy in part_loads(2):
                copy.start()

    def expand_grad(part):
        @pl.when(part == 0)
        def _():
            loads[0].wait()
            flipped[...] = normed_two[...].T

        unit_grad(4 + part, ENCODER_EXPAND[0], [(0, dot(flipped[...], before_grad[...]))])

    def middle_layer():
        loads[1].wait()
        loads[2].wait()
        for part in range(3):
            vectors[6 + part : 7 + part] = inner_sum[part]
        unit, inverse = standardize(middle[...])
        norm_grad = norm_sum[...]
        vectors[3:4, :768] = row_sum(norm_grad * unit)
        vectors[5:6, :768] = row_sum(norm_grad)
        grad = encoded_grad[...].astype(F32) + norm_back(unit, inverse, gains[1:2], norm_grad)
        vectors[0:1, :768] = row_sum(grad)
        tokens_grad[...] = grad
        below = low(grad)
        attention_low[...] = below
        context_grad[...] = low(dot_nt(below, merging[...]))
        for copy in loads[3:7]:
            copy.wait()

    def attention(first):
        @pl.loop(first, first + 2)
        def _(pair):
            lanes = pair_lanes(pair)
            values = mixed[:, pair_lanes(pair, 1536)]
            keys_total = jnp.zeros((TILE, 128), F32)
            values_total = jnp.zeros((TILE, 128), F32)
            for half in range(2):
                prob = probs[pair * 2 + half]
                outer = only(context_grad[:, lanes], half)
                query = only(mixed[:, lanes], half)
                wide = prob.astype(F32)
                grad = dot_nt(values, outer)
                raw = low(wide * (grad - jnp.sum(wide * grad, axis=0, keepdims=True)))
                keys_total = keys_total + dot(raw, query)
                values_total = values_total + dot(prob, outer)
                rows = head_rows(pair, half)
                query_turned[rows] = dot(turned[rows], raw)
            key_grad[0, :, lanes] = keys_total
            key_grad[1, :, lanes] = values_total

    def mixing():
        mixed_grad[:, 0:768] = low(query_turned[...].T * 0.125)
        mixed_grad[:, 768:1536] = low(key_grad[0] * 0.125)
        mixed_grad[:, 1536:2304] = low(key_grad[1])

    def attend_grad(part):
        @pl.when(part == 0)
        def _():
            loads[7].wait()
            flipped[...] = normed[...].T

        wide = aligned(part * 1024, 1024, 1024)
        unit_grad(7 + part, ENCODER_ATTEND[0], [(0, dot(flipped[...], mixed_grad[:, wide]))])

    def tail_grad():
        store_packed(put_tail, 0, ENCODER_ATTEND[2], dot(flipped[...], mixed_grad[:, 2048:2304]))
        store_packed(put_tail, 0, ENCODER_MERGE, dot_tn(attention_low[...], context[...]))
        if reduce:
            tail.send(UNIT)

    def input_layer():
        loads[8].wait()
        loads[9].wait()
        norm_grad = dot_nt(mixed_grad[...], attend[...])
        unit, inverse = standardize(hidden[...])
        vectors[2:3, :768] = row_sum(norm_grad * unit)
        vectors[4:5, :768] = row_sum(norm_grad)
        grad = tokens_grad[...] + norm_back(unit, inverse, gains[0:1], norm_grad)
        tokens_grad[...] = grad
        if reduce:
            payload[...] = low(grad)

    if not reduce:
        shrink_start()
        for part in range(3):
            shrink_grad(part)
        for part in range(3):
            hidden_layer(part)
            expand_grad(part)
        middle_layer()
        for first in (0, 2, 4):
            attention(first)
        mixing()
        for part in range(2):
            attend_grad(part)
        tail_grad()
        input_layer()
        return

    def exchange(source, piece):
        rows = aligned(piece * 32, 32, 32)
        return remote(source.at[rows], arrived.at[rows], pay_send.at[piece], pay_recv.at[piece], partner["x"])

    small_route = ("c",) + ROUTES[0]
    totals = ((decoder_total, decoder_got), (encoder_total, encoder_got))

    def small_copy(stage, kind):
        source, target = totals[kind]
        return remote(
            source.at[stage],
            target.at[stage],
            small_send.at[stage, kind],
            small_recv.at[stage, kind],
            partner[small_route[stage]],
        )

    def small_advance(stage):
        if stage == 0:
            encoder_total[0] = vectors[...]
        for kind in range(2):
            source, target = totals[kind]
            if stage > 0:
                small_copy(stage - 1, kind).wait_recv()
                source[stage] = source[stage - 1] + target[stage - 1]
            if stage < 5:
                small_copy(stage, kind).start()

    shrink_start()
    shrink_grad(0)
    decoder_load.wait()

    def attention_all():
        @pl.loop(0, 3)
        def _(step):
            attention(2 * step)

        mixing()

    def ending():
        tail_grad()
        input_layer()

    part = functools.partial
    works = {4: middle_layer, 5: attention_all, 7: ending}
    turns = ENCODER_PLAN.chunks + TAIL_PLAN.chunks + 4 * LAG
    works.update({8 + stage + max(0, stage - 1): part(small_advance, stage) for stage in range(6)})

    @pl.loop(0, turns)
    def _(number):
        engine.turn(number)
        tail.turn(number - ENCODER_PLAN.chunks)

        @pl.when(number <= 1)
        def _():
            shrink_grad(number + 1)

        @pl.when((number >= 2) & (number <= 4))
        def _():
            expand_grad(number - 2)

        @pl.when((number >= 1) & (number <= 3))
        def _():
            hidden_layer(number - 1)

        for position, work in works.items():
            pl.when(number == position)(work)

        @pl.when(number == 6)
        def _():
            @pl.loop(0, 2)
            def _(part):
                attend_grad(part)

        @pl.when((pack == 0) & (number < 8))
        def _():
            exchange(encoded_grad, number).start()

        @pl.when((pack == 1) & (number >= 8) & (number < 16))
        def _():
            exchange(payload, number - 8).start()

    for stage in range(5):
        for kind in range(2):
            small_copy(stage, kind).wait_send()
    for piece in range(8):
        exchange(payload, piece).wait()
    engine.close()
    tail.close()
    vectors[...] = encoder_total[5]
    decoder_sums[...] = decoder_total[5]


def encoder_backward_call(reduce, tokens, encoded_grad, sums, decoder_vectors, rest, kept, gains, attend, merging, expand, shrink):
    if reduce:
        summed = tuple(
            jax.ShapeDtypeStruct((plan.chunks, 16, plan.span), F32) for plan in (ENCODER_PLAN, TAIL_PLAN)
        )
        more = (
            jax.ShapeDtypeStruct(decoder_vectors.shape, F32),
            jax.ShapeDtypeStruct((256, 768), BF16),
        )
        more_specs = (vmem_spec(), any_spec())
        extra = [
            pltpu.VMEM((6,) + decoder_vectors.shape, F32),
            pltpu.VMEM((6,) + sums.shape, F32),
            pltpu.VMEM((5,) + decoder_vectors.shape, F32),
            pltpu.VMEM((5,) + sums.shape, F32),
            pltpu.VMEM((256, 768), BF16),
            pltpu.SemaphoreType.DMA((2,)),
            pltpu.SemaphoreType.DMA((5, 2)),
            pltpu.SemaphoreType.DMA((5, 2)),
            pltpu.SemaphoreType.DMA((8,)),
            pltpu.SemaphoreType.DMA((8,)),
            pltpu.SemaphoreType.DMA,
        ] + reducer_scratch(ENCODER_PLAN) + reducer_scratch(TAIL_PLAN)
        params = dict(collective_id=2, has_side_effects=True)
    else:
        summed = tuple(
            jax.ShapeDtypeStruct((plan.chunks, 2, 16, 16, plan.span), BF16) for plan in (ENCODER_PLAN, TAIL_PLAN)
        )
        more, more_specs, extra, params = (), (), [], dict()
    return pl.pallas_call(
        functools.partial(encoder_backward_kernel, reduce),
        out_shape=summed
        + (
            jax.ShapeDtypeStruct(sums.shape, F32),
            jax.ShapeDtypeStruct((256, 768), F32),
        )
        + more,
        in_specs=[vmem_spec()] * 2 + [any_spec(), vmem_spec()] + [any_spec()] * 15,
        out_specs=(vmem_spec(),) * 4 + more_specs,
        scratch_shapes=[
            pltpu.VMEM((256, 768), F32),
            pltpu.VMEM(attend.shape, BF16),
            pltpu.VMEM(merging.shape, BF16),
            pltpu.VMEM((2, 768, 1024), BF16),
            pltpu.VMEM((2, 1024, 768), BF16),
            pltpu.VMEM((256, 768), BF16),
            pltpu.VMEM((256, 2304), BF16),
            pltpu.VMEM((768, 256), BF16),
            pltpu.VMEM((12, 256, 256), BF16),
            pltpu.VMEM((256, 768), BF16),
            pltpu.VMEM((256, 768), F32),
            pltpu.VMEM((256, 768), BF16),
            pltpu.VMEM((256, 3072), BF16),
            pltpu.VMEM((2, 256, 1024), F32),
            pltpu.VMEM((256, 1024), BF16),
            pltpu.VMEM((256, 768), F32),
            pltpu.VMEM((256, 768), BF16),
            pltpu.VMEM((256, 768), BF16),
            pltpu.VMEM((2, 256, 768), F32),
            pltpu.VMEM((768, 256), F32),
            pltpu.VMEM((256, 2304), BF16),
            pltpu.VMEM((3072, 256), BF16),
            pltpu.VMEM((768, 256), BF16),
            pltpu.VMEM((3, 1, 1024), F32),
            pltpu.SemaphoreType.DMA((11,)),
            pltpu.SemaphoreType.DMA((2, 3)),
        ]
        + extra,
        compiler_params=pltpu.CompilerParams(vmem_limit_bytes=62 * 2**20, **params),
        name="encoder_backward",
    )(encoded_grad, sums, decoder_vectors, gains, tokens, rest, attend, merging, expand, shrink, *kept)


def unpack(packed, place):
    span = packed.shape[-1]

    def take(start, size):
        pieces = []
        while size:
            chunk, first = divmod(start, span)
            length = min(size, span - first)
            pieces.append(packed[chunk, ..., first : first + length])
            start, size = start + length, size - length
        return pieces[0] if len(pieces) == 1 else jnp.concatenate(pieces, axis=-1)

    offset, count, width = place
    pieces = [take(offset + i * width, width) for i in range(count // 16)]
    if count % 16:
        rest = take(offset + count // 16 * width, width // 2)
        pieces.append(jnp.concatenate([rest[..., :8, :], rest[..., 8:, :]], axis=-1))
    return pieces[0] if len(pieces) == 1 else jnp.concatenate(pieces, axis=-2)


def finish_kernel(
    decoder_summed_far, decoder_sums_far, encoder_sums_far, summed_far, tail_far, arrived_far, tokens_grad_far, encoded_grad_far,
    boundary, statistics, e_gains, e_shifts, e_biases, e_attend, e_merge, e_expand, e_inner, e_shrink,
    d_entry, d_biases, mask_grad, d_gains, d_shifts, d_attend, d_merge, d_expand, d_inner, d_shrink,
    decoder_summed, decoder_sums, encoder_sums, summed, tail, arrived, tokens_grad, encoded_grad, load_sem,
):
    section = lax.axis_index("section")
    loads = fetch(
        [
            (decoder_summed_far, decoder_summed),
            (decoder_sums_far, decoder_sums),
            (encoder_sums_far, encoder_sums),
            (summed_far, summed),
            (tail_far, tail),
            (arrived_far, arrived),
            (tokens_grad_far, tokens_grad),
            (encoded_grad_far, encoded_grad),
        ],
        load_sem,
    )
    number = section * lax.axis_size("dp") + lax.axis_index("dp")

    def own(rows, count):
        width = rows.shape[1]
        return pltpu.roll(rows, (width - number * count) % width, axis=1)[:, :count]

    def own_line(rows, count):
        return own(jnp.concatenate([rows[i : i + 1] for i in range(rows.shape[0])], axis=1), count)

    for copy in loads[:3]:
        copy.wait()
    lane = iota((1, 128), 1)
    values = jnp.zeros((1, 128), F32)
    for sums, width, first, count_row, base in ((encoder_sums, DE, 10, 14, 0), (decoder_sums, DD, 12, 16, 4)):
        scale = 1.0 / (sums[count_row : count_row + 1, 0:1] * width)
        for i in range(4):
            value = jnp.sum(sums[first + i : first + i + 1, :], axis=1, keepdims=True) * scale
            values = jnp.where(lane == base + i, value, values)
    statistics[...] = jnp.sqrt(values)[:, :8]
    rows = own(encoder_sums[0:8, :DE], 24)
    e_biases[...] = rows[0:2]
    e_gains[...] = rows[2:4]
    e_shifts[...] = rows[4:6]
    e_inner[...] = own_line(encoder_sums[6:9], 96)
    rows = own(decoder_sums[0:8], 16)
    d_biases[...] = rows[0:3]
    mask_grad[...] = rows[3:4]
    d_gains[...] = rows[4:6]
    d_shifts[...] = rows[6:8]
    d_inner[...] = own_line(decoder_sums[8:12], 64)

    d_merge[...] = unpack(decoder_summed, DECODER_MERGE)
    d_expand[...] = unpack(decoder_summed, DECODER_EXPAND)
    d_shrink[...] = unpack(decoder_summed, DECODER_SHRINK)
    loads[3].wait()
    loads[4].wait()
    d_entry[...] = unpack(summed, ENTRY)
    d_attend[...] = unpack(summed, DECODER_ATTEND)
    for target, places in ((e_expand, ENCODER_EXPAND), (e_attend, ENCODER_ATTEND), (e_shrink, ENCODER_SHRINK)):
        start = 0
        for place in places:
            source = tail if place is ENCODER_ATTEND[2] else summed
            target[:, start : start + place[2]] = unpack(source, place)
            start += place[2]
    e_merge[...] = unpack(tail, ENCODER_MERGE)
    for copy in loads[5:]:
        copy.wait()

    @pl.when(section == 0)
    def _():
        boundary[0, 0] = tokens_grad[...]
        boundary[0, 1] = arrived[...].astype(F32)

    @pl.when(section == 1)
    def _():
        boundary[0, 0] = arrived[...].astype(F32)
        boundary[0, 1] = encoded_grad[...].astype(F32)


def finish_call(*operands):
    shapes = (
        (1, 2, 256, 768), (1, 8), (2, 24), (2, 24), (2, 24), (24, 2304), (24, 768), (24, 3072), (1, 96), (96, 768),
        (24, 512), (3, 16), (1, 16), (2, 16), (2, 16), (16, 768), (16, 256), (16, 2048), (1, 64), (64, 512),
    )
    outs = list(
        pl.pallas_call(
            finish_kernel,
            out_shape=tuple(jax.ShapeDtypeStruct(shape, F32) for shape in shapes),
            in_specs=[any_spec()] * len(operands),
            out_specs=(vmem_spec(),) * len(shapes),
            scratch_shapes=[pltpu.VMEM(operand.shape, operand.dtype) for operand in operands]
            + [pltpu.SemaphoreType.DMA((len(operands),))],
            compiler_params=pltpu.CompilerParams(vmem_limit_bytes=60 * 2**20),
            name="finish",
        )(*operands)
    )
    for line in (1, 8, 12, 18):
        outs[line] = outs[line].reshape(-1)
    for turned in (6, 16):
        outs[turned] = outs[turned].T
    return tuple(outs)


def scatter_sum(member, share_dim):
    return lax.psum_scatter(
        member, ("section", "dp"), scatter_dimension=share_dim, tiled=True
    )


def finish_generic(decoder_part, part, tail, decoder_sums, encoder_sums, tokens_grad, encoded_grad):
    section = lax.axis_index("section")
    payload = jnp.where(section == 0, encoded_grad, low(tokens_grad))

    def whole(packed, *places):
        packed = jnp.swapaxes(packed, 1, 2).reshape(-1, 32, 16, packed.shape[-1])
        blocks = [unpack(packed, place).reshape(32 * place[1], place[2]) for place in places]
        return scatter_sum(jnp.concatenate(blocks, axis=1).astype(F32), 0)

    def line(value):
        return scatter_sum(value, value.ndim - 1)

    arrived = lax.ppermute(payload, "section", [(0, 1), (1, 0)]).astype(F32)
    boundary = jnp.where(
        section == 0,
        jnp.stack([tokens_grad, arrived]),
        jnp.stack([arrived, encoded_grad.astype(F32)]),
    )
    sums = jnp.concatenate(
        [jnp.sum(encoder_sums[10:14], axis=1), jnp.sum(decoder_sums[12:16], axis=1)]
    )
    sums, counts = lax.psum((sums, (encoder_sums[14, 0], decoder_sums[16, 0])), ("section", "dp"))
    scales = jnp.concatenate([jnp.full((4,), counts[0] * DE), jnp.full((4,), counts[1] * DD)])
    return (
        boundary[None],
        jnp.sqrt(sums / scales),
        line(encoder_sums[2:4, :DE]),
        line(encoder_sums[4:6, :DE]),
        line(encoder_sums[0:2, :DE]),
        jnp.concatenate([whole(part, *ENCODER_ATTEND[:2]), whole(tail, ENCODER_ATTEND[2])], axis=1),
        whole(tail, ENCODER_MERGE).T,
        whole(part, *ENCODER_EXPAND),
        line(encoder_sums[6:9].reshape(-1)),
        whole(part, *ENCODER_SHRINK),
        whole(decoder_part[1], ENTRY),
        line(decoder_sums[0:3]),
        line(decoder_sums[3]),
        line(decoder_sums[4:6]),
        line(decoder_sums[6:8]),
        whole(decoder_part[1], DECODER_ATTEND),
        whole(decoder_part[0], DECODER_MERGE).T,
        whole(decoder_part[0], DECODER_EXPAND),
        line(decoder_sums[8:12].reshape(-1)),
        whole(decoder_part[0], DECODER_SHRINK),
    )


def body(
    visible_tokens,
    cotangent,
    chip_sizes,
    ground_distance,
    visible_slots,
    encoder_gains,
    encoder_shifts,
    encoder_biases,
    encoder_attend,
    encoder_merge,
    encoder_expand,
    encoder_inner,
    encoder_shrink,
    decoder_entry,
    decoder_biases,
    mask_token,
    decoder_gains,
    decoder_shifts,
    decoder_attend,
    decoder_merge,
    decoder_widen_weight,
    decoder_inner,
    decoder_shrink,
):
    reduce = (lax.axis_size("section"), lax.axis_size("dp")) == (2, 16)
    sent, sums, *kept = encoder_forward_call(
        chip_sizes, visible_tokens, encoder_gains, encoder_shifts, encoder_biases,
        encoder_attend, encoder_merge, encoder_expand, encoder_inner, encoder_shrink,
    )
    decoder_summed, rest, decoder_vectors, encoded_grad = decoder_call(
        reduce, chip_sizes, ground_distance, visible_slots, sent, cotangent, decoder_entry, decoder_biases, mask_token,
        decoder_gains, decoder_shifts, decoder_attend, decoder_merge, decoder_widen_weight, decoder_inner,
        decoder_shrink,
    )
    summed, tail, encoder_sums, tokens_grad, *more = encoder_backward_call(
        reduce, visible_tokens, encoded_grad, sums, decoder_vectors, rest, kept,
        encoder_gains, encoder_attend, encoder_merge, encoder_expand, encoder_shrink,
    )
    if reduce:
        decoder_sums, arrived = more
        return finish_call(
            decoder_summed, decoder_sums, encoder_sums, summed, tail, arrived, tokens_grad, encoded_grad
        )
    return finish_generic(
        (decoder_summed, rest), summed, tail, decoder_vectors, encoder_sums, tokens_grad, encoded_grad
    )


def solution(mesh):
    in_specs = (
        P("dp", None, None),
        P("dp", None, None),
        P("dp", None),
        P("dp", None),
        P("dp", None),
        P(),
        P(),
        P(),
        P(),
        P(),
        P(),
        P(),
        P(),
        P(),
        P(),
        P(),
        P(),
        P(),
        P(),
        P(),
        P(),
        P(),
        P(),
    )
    out_specs = (
        P("section", "dp", None, None),
        P(),
        P(None, ("section", "dp")),
        P(None, ("section", "dp")),
        P(None, ("section", "dp")),
        P(("section", "dp"), None),
        P(None, ("section", "dp")),
        P(("section", "dp"), None),
        P(("section", "dp")),
        P(("section", "dp"), None),
        P(("section", "dp"), None),
        P(None, ("section", "dp")),
        P(("section", "dp")),
        P(None, ("section", "dp")),
        P(None, ("section", "dp")),
        P(("section", "dp"), None),
        P(None, ("section", "dp")),
        P(("section", "dp"), None),
        P(("section", "dp")),
        P(("section", "dp"), None),
    )
    return jax.shard_map(body, mesh=mesh, in_specs=in_specs, out_specs=out_specs, check_vma=False)
```

```python
import functools
import types

import jax
import jax.numpy as jnp
import numpy as np
from jax import lax
from jax.experimental import pallas as pl
from jax.experimental.pallas import tpu as pltpu
from jax.sharding import PartitionSpec as P

DE = 768
DD = 512
TILE = 256
BLOCK = 512
NEGATIVE = -1e30
F32, BF16 = jnp.float32, jnp.bfloat16
MESH_ID = pl.DeviceIdType.MESH

CANON = ("x", "z2", "z1", "y")
ROUTES = (("x", "y", "z1", "z2"), ("y", "x", "z1", "z2"), ("z1", "z2", "x", "y"))
UNIT = 1536
LAG = 2
DECODER_PLAN = types.SimpleNamespace(widths=(2, 2, 1), chunks=7, slots=7, ring=3, span=640)
ENCODER_PLAN = types.SimpleNamespace(widths=(3, 6, 3), chunks=9, slots=3, ring=3, span=1536)
TAIL_PLAN = types.SimpleNamespace(widths=(2, 3, 1), chunks=2, slots=2, ring=2, span=768)

DECODER_EXPAND, DECODER_SHRINK, DECODER_MERGE = (0, 16, 2048), (2048, 64, 512), (4096, 16, 256)
ENTRY, DECODER_ATTEND = (0, 24, 512), (768, 16, 768)
ENCODER_SHRINK = tuple((UNIT * (1 + part), 96, 256) for part in range(3))
ENCODER_EXPAND = tuple((UNIT * (4 + part), 24, 1024) for part in range(3))
ENCODER_ATTEND = ((UNIT * 7, 24, 1024), (UNIT * 8, 24, 1024), (0, 24, 256))
ENCODER_MERGE = (384, 24, 768)


def dot(a, b):
    return jnp.dot(a, b, preferred_element_type=F32)


def dot_nt(a, b):
    return lax.dot_general(a, b, (((1,), (1,)), ((), ())), preferred_element_type=F32)


def dot_tn(a, b):
    return lax.dot_general(a, b, (((0,), (0,)), ((), ())), preferred_element_type=F32)


def low(value):
    return value.astype(BF16)


def standardize(values):
    centered = values - jnp.mean(values, axis=-1, keepdims=True)
    inverse = lax.rsqrt(jnp.mean(centered * centered, axis=-1, keepdims=True) + 1e-05)
    return centered * inverse, inverse


def norm_back(unit, inverse, gain, grad):
    inner = grad * gain
    return inverse * (
        inner
        - jnp.mean(inner, axis=-1, keepdims=True)
        - unit * jnp.mean(inner * unit, axis=-1, keepdims=True)
    )


def row_sum(values):
    return jnp.sum(values, axis=0, keepdims=True)


def gelu_pair(before):
    half = 0.5 * (1.0 + lax.erf(before * 0.7071067811865476))
    density = jnp.exp(-0.5 * before * before) * 0.3989422804014327
    return before * half, half + before * density


def chip_of(places, sizes, pack):
    end = sizes[pack, 0]
    chip = (places >= end).astype(jnp.int32)
    for slot in range(1, 4):
        end = end + sizes[pack, slot]
        chip = chip + (places >= end).astype(jnp.int32)
    return chip


def iota(shape, dimension):
    return lax.broadcasted_iota(jnp.int32, shape, dimension)


def aligned(start, size, unit):
    if isinstance(start, int):
        return slice(start, start + size)
    return pl.ds(pl.multiple_of(start, unit), size)


def pair_lanes(pair, base=0):
    return aligned(base + pair * 128, 128, 128)


def head_rows(pair, half, base=0):
    return aligned(base + pair * 128 + half * 64, 64, 64)


def rows_of(tile, size=TILE):
    return aligned(tile * size, size, size)


def only(values, half):
    return jnp.where(iota((1, 128), 1) // 64 == half, values, jnp.zeros_like(values))


def fetch(pairs, sems):
    copies = [
        pltpu.make_async_copy(source, target, sems.at[i]) for i, (source, target) in enumerate(pairs)
    ]
    for copy in copies:
        copy.start()
    return copies


def store_packed(put, first, place, value):
    offset, count, width = place
    value = value.reshape(-1, count, width)
    shards = slice(first, first + value.shape[0]) if isinstance(first, int) else pl.ds(first, value.shape[0])
    for piece in range(count // 16):
        put(shards, offset + piece * width, value[:, piece * 16 : piece * 16 + 16])
    if count % 16:
        half = width // 2
        rest = value[:, count - 8 :]
        rest = jnp.concatenate([rest[:, :, :half], rest[:, :, half:]], axis=1)
        put(shards, offset + count // 16 * width, rest)


def halves(shards, value):
    pairs = value.reshape(value.shape[0] // 2, 2, *value.shape[1:])
    if isinstance(shards, slice):
        return slice(shards.start // 2, shards.stop // 2), pairs[:, 0], pairs[:, 1]
    return pl.ds(shards.start // 2, shards.size // 2), pairs[:, 0], pairs[:, 1]


def place_of(names, bits):
    index = 0
    for name in names:
        index = index * 2 + bits[name]
    return index


def left_after(route, stage):
    return tuple(name for name in CANON if name not in route[:stage])


def choices(names):
    for number in range(2 ** len(names)):
        yield {name: (number >> (len(names) - 1 - i)) & 1 for i, name in enumerate(names)}


def neighbours():
    section = lax.axis_index("section")
    data = lax.axis_index("dp")
    mine = {"x": section, "c": data % 2, "y": data // 2 % 2, "z1": data // 4 % 2, "z2": data // 8 % 2}
    partner = {"x": (1 - section, data)}
    for name, step in {"c": 1, "y": 2, "z1": 4, "z2": 8}.items():
        partner[name] = (section, data + step * (1 - 2 * mine[name]))
    return mine, partner


def greet(partner):
    barrier = pltpu.get_barrier_semaphore()
    for name in ("c",) + CANON:
        pl.semaphore_signal(barrier, inc=1, device_id=partner[name], device_id_type=MESH_ID)


def await_greetings():
    pl.semaphore_wait(pltpu.get_barrier_semaphore(), 5)


def remote(source, target, send, recv, device):
    return pltpu.make_async_remote_copy(
        src_ref=source,
        dst_ref=target,
        send_sem=send,
        recv_sem=recv,
        device_id=device,
        device_id_type=MESH_ID,
    )


def reducer(plan, mine, partner, out, refs):
    chunks, slots, span, ring = plan.chunks, plan.slots, plan.span, plan.ring
    progress = types.SimpleNamespace(sent=0)
    own, staging, first = refs[:3]
    sent, got = refs[3:15], refs[15:27]
    first_send, first_recv, send_sem, recv_sem = refs[27:31]

    def first_copy(chunk):
        return remote(staging.at[chunk % slots], first.at[chunk], first_send.at[chunk], first_recv.at[chunk], partner["c"])

    def stage_copy(route, stage, chunk):
        return remote(
            sent[route * 4 + stage].at[chunk % ring],
            got[route * 4 + stage].at[chunk],
            send_sem.at[route, stage, chunk],
            recv_sem.at[route, stage, chunk],
            partner[ROUTES[route][stage]],
        )

    def total(route, stage, chunk, bits):
        spot = place_of(CANON, bits)
        cols = slice(sum(plan.widths[:route]) * 128, sum(plan.widths[: route + 1]) * 128)
        value = own[chunk, spot, :, cols].astype(F32) + first[chunk, spot, :, cols].astype(F32)
        for earlier in range(stage):
            names = left_after(ROUTES[route], earlier + 1)
            value = value + got[route * 4 + earlier][chunk, place_of(names, bits)].astype(F32)
        return value

    def advance(stage, chunk):
        for route in range(3):
            if stage:
                stage_copy(route, stage - 1, chunk).wait_recv()
            else:
                first_copy(chunk).wait_recv() if route == 0 else None
            if stage < 4:

                @pl.when(chunk >= ring)
                def _(route=route):
                    stage_copy(route, stage, chunk - ring).wait_send()

        values = []
        for route in range(3):
            path = ROUTES[route]
            if stage == 4:
                values.append(total(route, 4, chunk, mine))
                continue
            names = left_after(path, stage + 1)
            for free in choices(names):
                bits = dict(mine)
                bits[path[stage]] = 1 - mine[path[stage]]
                bits.update(free)
                values.append((route, place_of(names, free), low(total(route, stage, chunk, bits))))
        if stage == 4:
            out[chunk] = jnp.concatenate(values, axis=1)
            return
        for route, spot, value in values:
            sent[route * 4 + stage][chunk % ring, spot] = value
        for route in range(3):
            stage_copy(route, stage, chunk).start()

    def turn(number):
        for stage in range(4, -1, -1):
            chunk = number - LAG * stage
            pl.when((chunk >= 0) & (chunk < chunks))(functools.partial(advance, stage, chunk))

    def put(shards, column, value):
        shards, even, odd = halves(shards, value)
        kept = low(jnp.where(mine["c"] == 0, even, odd))
        given = low(jnp.where(mine["c"] == 0, odd, even))
        width = value.shape[2]
        done = 0
        while done < width:
            chunk, start = divmod(column + done, span)
            size = min(width - done, span - start)
            own[chunk, shards, :, start : start + size] = kept[:, :, done : done + size]
            staging[chunk % slots, shards, :, start : start + size] = given[:, :, done : done + size]
            done += size

    def put_unit(unit):
        def put(shards, column, value):
            shards, even, odd = halves(shards, value)
            cols = slice(column, column + value.shape[2])
            own[unit, shards, :, cols] = low(jnp.where(mine["c"] == 0, even, odd))
            staging[unit % slots, shards, :, cols] = low(jnp.where(mine["c"] == 0, odd, even))

        @pl.when(unit >= slots)
        def _():
            first_copy(unit - slots).wait_send()

        return put

    def send(column):
        while (progress.sent + 1) * span <= column:
            first_copy(progress.sent).start()
            progress.sent += 1

    def close():
        for chunk in range(max(0, chunks - slots), chunks):
            first_copy(chunk).wait_send()
        for chunk in range(chunks - ring, chunks):
            for route in range(3):
                for stage in range(4):
                    stage_copy(route, stage, chunk).wait_send()

    return types.SimpleNamespace(
        own=own, staging=staging, turn=turn, put=put, put_unit=put_unit, first_copy=first_copy, send=send, close=close
    )


def reducer_scratch(plan):
    stages = [(width, block) for width in plan.widths for block in (8, 4, 2, 1)]
    return (
        [
            pltpu.VMEM((plan.chunks, 16, 16, plan.span), BF16),
            pltpu.VMEM((plan.slots, 16, 16, plan.span), BF16),
            pltpu.VMEM((plan.chunks, 16, 16, plan.span), BF16),
        ]
        + [pltpu.VMEM((plan.ring, block, 16, width * 128), BF16) for width, block in stages]
        + [pltpu.VMEM((plan.chunks, block, 16, width * 128), BF16) for width, block in stages]
        + [
            pltpu.SemaphoreType.DMA((plan.chunks,)),
            pltpu.SemaphoreType.DMA((plan.chunks,)),
            pltpu.SemaphoreType.DMA((3, 4, plan.chunks)),
            pltpu.SemaphoreType.DMA((3, 4, plan.chunks)),
        ]
    )


def put_into(parts):
    span = parts.shape[-1]

    def put(shards, column, value):
        shards, *pair = halves(shards, value)
        width = value.shape[2]
        done = 0
        while done < width:
            chunk, start = divmod(column + done, span)
            size = min(width - done, span - start)
            for core in range(2):
                parts[chunk, core, shards, :, start : start + size] = low(pair[core][:, :, done : done + size])
            done += size

    return put


def put_unit_into(parts, unit):
    def put(shards, column, value):
        shards, *pair = halves(shards, value)
        for core in range(2):
            parts[unit, core, shards, :, column : column + value.shape[2]] = low(pair[core])

    return put


def vmem_spec():
    return pl.BlockSpec(memory_space=pltpu.VMEM)


def any_spec():
    return pl.BlockSpec(memory_space=pl.ANY)


def smem_spec():
    return pl.BlockSpec(memory_space=pltpu.SMEM)


def encoder_forward_kernel(
    sizes, distance, frequency, gains, shifts, biases, inner, tokens, attend_far, merging_far, expand_far,
    shrink_far, sent, vectors, table, *refs,
):
    far = refs[:9]
    normed, mixed, turned, probs, context, middle, normed_two, active, slope = refs[9:18]
    hidden, attend, merging, expand, shrink, context_turned, load_sem, save_sem = refs[18:]
    pack = lax.axis_index("section")
    loads = fetch(
        [
            (tokens.at[pack], hidden),
            *[(attend_far.at[:, i * 768 : i * 768 + 768], attend.at[:, i * 768 : i * 768 + 768]) for i in range(3)],
            (merging_far, merging),
            *[(expand_far.at[:, i * 1024 : i * 1024 + 1024], expand.at[:, i * 1024 : i * 1024 + 1024]) for i in range(3)],
            *[(shrink_far.at[i * 1024 : i * 1024 + 1024], shrink.at[i * 1024 : i * 1024 + 1024]) for i in range(3)],
        ],
        load_sem,
    )
    saves = []

    def save(*numbers):
        for number in numbers:
            copy = pltpu.make_async_copy(refs[9 + number], far[number], save_sem.at[number])
            copy.start()
            saves.append(copy)

    vectors[...] = jnp.zeros_like(vectors)
    positions = iota((32, 128), 0).astype(F32)
    for chip in range(4):
        spacing = distance[pack, chip].astype(F32) / 16.0
        angle = positions * (spacing * frequency[...])
        table[0, chip] = jnp.sin(angle)
        table[1, chip] = jnp.cos(angle)
    key_chip = chip_of(4 * iota((TILE, 1), 0), sizes, pack)
    own_chip = chip_of(4 * iota((1, TILE), 1), sizes, pack)
    valid = (key_chip < 4).astype(F32)
    loads[0].wait()
    values = hidden[...]
    vectors[10:11, :768] = row_sum(valid * values * values)
    unit, _ = standardize(values)
    norm = low(unit * gains[0:1] + shifts[0:1])
    normed[...] = norm
    for part in range(3):
        cols = slice(part * 768, part * 768 + 768)
        loads[1 + part].wait()
        mix = dot(norm, attend[:, cols])
        mixed[:, cols] = low(mix)
        if part:
            turned[(part - 1) * 768 : part * 768] = low(mix.T)
    save(0, 1, 2)

    def score(head):
        pair, half = divmod(head, 2)
        query = only(mixed[:, pair_lanes(pair)], half) * BF16(0.125)
        return dot_nt(mixed[:, pair_lanes(pair, 768)], query)

    ready = [score(0), score(1)]
    for head in range(12):
        if head + 2 < 12:
            ready.append(score(head + 2))
        scores = jnp.where(key_chip == own_chip, ready[head], NEGATIVE)
        expos = jnp.exp(scores - jnp.max(scores, axis=0, keepdims=True))
        prob = low(expos * (1.0 / jnp.sum(expos, axis=0, keepdims=True)))
        probs[head] = prob
        context_turned[head * 64 : head * 64 + 64] = dot(turned[768 + head * 64 : 832 + head * 64], prob)

    mingled = low(context_turned[...].T)
    context[...] = mingled
    save(3, 4)
    loads[4].wait()
    attention = dot(mingled, merging[...]) + biases[0:1]
    vectors[11:12, :768] = row_sum(valid * attention * attention)
    center = hidden[...] + attention
    middle[...] = center
    unit, _ = standardize(center)
    norm = low(unit * gains[1:2] + shifts[1:2])
    normed_two[...] = norm
    save(5, 6)
    feed = jnp.zeros_like(center)
    def widened(part):
        if part % 2 == 0:
            loads[5 + part // 2].wait()
        cols = slice(part * 512, part * 512 + 512)
        return dot(norm, expand[:, cols]) + inner[:, cols]

    ready = [widened(0)]
    for part in range(6):
        if part < 5:
            ready.append(widened(part + 1))
        cols = slice(part * 512, part * 512 + 512)
        value, slant = gelu_pair(ready[part])
        value = low(value)
        active[:, cols] = value
        slope[part // 2, :, part % 2 * 512 : part % 2 * 512 + 512] = slant
        if part % 2 == 0:
            loads[8 + part // 2].wait()
        feed = feed + dot(value, shrink[cols])
    save(7, 8)
    feed = feed + biases[1:2]
    vectors[12:13, :768] = row_sum(valid * feed * feed)
    output = center + feed
    vectors[13:14, :768] = row_sum(valid * output * output)
    vectors[14:15, :768] = jnp.broadcast_to(row_sum(valid), (1, 768))
    sent[...] = low(output)
    for copy in saves:
        copy.wait()


def encoder_forward_call(sizes, distance, tokens, gains, shifts, biases, attend, merging, expand, inner, shrink):
    frequency = np.exp(-np.log(10000.0) * np.arange(DD // 4) / (DD // 4)).astype(np.float32)
    shapes = (
        ((256, 768), BF16),
        ((256, 2304), BF16),
        ((1536, 256), BF16),
        ((12, 256, 256), BF16),
        ((256, 768), BF16),
        ((256, 768), F32),
        ((256, 768), BF16),
        ((256, 3072), BF16),
        ((3, 256, 1024), F32),
    )
    return pl.pallas_call(
        encoder_forward_kernel,
        out_shape=(
            jax.ShapeDtypeStruct((256, 768), BF16),
            jax.ShapeDtypeStruct((16, 1024), F32),
            jax.ShapeDtypeStruct((2, 4, 32, 128), F32),
        )
        + tuple(jax.ShapeDtypeStruct(*shape) for shape in shapes),
        in_specs=[smem_spec()] * 2 + [vmem_spec()] * 5 + [any_spec()] * 5,
        out_specs=(vmem_spec(),) * 3 + (any_spec(),) * len(shapes),
        scratch_shapes=[pltpu.VMEM(*shape) for shape in shapes]
        + [
            pltpu.VMEM((256, 768), F32),
            pltpu.VMEM(attend.shape, BF16),
            pltpu.VMEM(merging.shape, BF16),
            pltpu.VMEM(expand.shape, BF16),
            pltpu.VMEM(shrink.shape, BF16),
            pltpu.VMEM((768, 256), F32),
            pltpu.SemaphoreType.DMA((11,)),
            pltpu.SemaphoreType.DMA((len(shapes),)),
        ],
        compiler_params=pltpu.CompilerParams(vmem_limit_bytes=60 * 2**20),
        name="encoder_forward",
    )(
        sizes, distance, jnp.asarray(frequency)[None], gains, shifts, biases, inner[None], tokens, attend, merging,
        expand, shrink,
    )


def decoder_kernel(
    reduce, sizes, slots, table, sent, biases, mask_token, gains, shifts, inner,
    cotangent, entry_far, attend_far, merging_far, expand_far, shrink_far,
    summed, rest, vectors, encoded_grad, *refs,
):
    (
        start, normed, mixed, turned, probs, flipped, context, normed_two, active,
        before_grad, go_low, attention_low, context_grad, delta, mixed_grad, target, masked_keys,
        entry_weight, attend, merging, expand, shrink, inner_sum, load_sem,
    ) = refs[:24]
    inner_sum[...] = jnp.zeros_like(inner_sum)
    pack = lax.axis_index("section")
    if reduce:
        mine, partner = neighbours()
        greet(partner)
        engine = reducer(DECODER_PLAN, mine, partner, summed, refs[24:])
        put = engine.put
    else:
        put = put_into(summed)
    put_rest = put_into(rest)
    loads = fetch(
        [
            (entry_far, entry_weight),
            (attend_far, attend),
            (cotangent.at[pack], target),
            (merging_far, merging),
            (expand_far, expand),
            (shrink_far, shrink),
        ],
        load_sem,
    )
    tiles = start.shape[0] // TILE
    vectors[...] = jnp.zeros_like(vectors)
    large = sizes[pack, 0] == 1024

    def add_row(row, value):
        vectors[row : row + 1, :] += value

    loads[0].wait()
    entry = low(dot(sent[...], entry_weight[...]) + biases[0:1])
    loads[1].wait()

    blocks = start.shape[0] // BLOCK

    def turns(first):
        if reduce:

            @pl.loop(first, first + 2)
            def _(number):
                engine.turn(number)

    def slot_chip(tile, size):
        return chip_of(iota((size, 1), 0) + tile * size, sizes, pack)

    def validity(tile, size):
        return (slot_chip(tile, size) < 4).astype(F32)

    def spread_of(tile):
        return (slots[pl.ds(pack, 1)] == iota((BLOCK, TILE), 0) + tile * BLOCK).astype(F32)

    def encoding_of(tile):
        pieces = []
        for kind in range(2):
            wave = table[kind, 0, aligned(tile * 8, 8, 8)]
            big = jnp.broadcast_to(wave[:, None], (8, 32, 128)).reshape(TILE, 128)
            wave = table[kind, tile, 0:16]
            own = jnp.broadcast_to(wave[:, None], (16, 16, 128)).reshape(TILE, 128)
            pieces.append(jnp.where(large, big, own))
        for kind in range(2):
            wave = table[kind, 0]
            big = jnp.broadcast_to(wave[None], (8, 32, 128)).reshape(TILE, 128)
            wave = table[kind, tile, 0:16]
            own = jnp.broadcast_to(wave[None], (16, 16, 128)).reshape(TILE, 128)
            pieces.append(jnp.where(large, big, own))
        return jnp.concatenate(pieces, axis=1)

    @pl.loop(0, tiles)
    def _(tile):
        start[rows_of(tile)] = encoding_of(tile)

    @pl.loop(0, blocks)
    def _(tile):
        rows = rows_of(tile, BLOCK)
        valid = validity(tile, BLOCK)
        spread = spread_of(tile)
        fill = valid * (1.0 - jnp.sum(spread, axis=1, keepdims=True))
        hidden = dot(low(spread), entry) + fill * mask_token[...] + start[rows] * valid
        start[rows] = hidden
        add_row(12, row_sum(valid * hidden * hidden))
        add_row(16, row_sum(valid))
        unit, _ = standardize(hidden)
        norm = low(unit * gains[0:1] + shifts[0:1])
        normed[rows] = norm
        mix = dot(norm, attend[...])
        mix_low = low(mix)
        mixed[rows] = mix_low
        turned[:, rows] = low(mix[:, 256:].T)
        lane = iota((BLOCK, 128), 1)
        other = (lane % 64 < 5) & (lane % 64 != slot_chip(tile, BLOCK))
        other = jnp.where(other, NEGATIVE, 0.0).astype(BF16)
        for head in range(4):
            lanes = slice(256 + head // 2 * 128, 384 + head // 2 * 128)
            masked_keys[head, rows] = jnp.where(lane // 64 == head % 2, mix_low[:, lanes], other)

    @pl.loop(0, 2 * tiles)
    def _(step):
        pair, tile = step // tiles, step % tiles
        rows = rows_of(tile)
        lane = iota((TILE, 128), 1)
        chosen = (lane % 64 == slot_chip(tile, TILE)).astype(F32).astype(BF16)
        for half in range(2):
            query = jnp.where(lane // 64 == half, mixed[rows, pair_lanes(pair)] * BF16(0.125), chosen)
            scores = dot_nt(masked_keys[pair * 2 + half], query)
            expos = jnp.exp(scores - jnp.max(scores, axis=0, keepdims=True))
            prob = low(expos * (1.0 / jnp.sum(expos, axis=0, keepdims=True)))
            probs[pair * 2 + half, :, rows] = prob
            flipped[head_rows(pair, half), rows] = dot(turned[head_rows(pair, half, 256)], prob)

    for copy in loads[2:]:
        copy.wait()

    @pl.loop(0, blocks)
    def _(tile):
        rows = rows_of(tile, BLOCK)
        valid = validity(tile, BLOCK)
        mingled = low(flipped[:, rows].T)
        context[rows] = mingled
        attention = dot(mingled, merging[...]) + biases[1:2]
        add_row(13, row_sum(valid * attention * attention))
        unit, _ = standardize(start[rows] + attention)
        norm = low(unit * gains[1:2] + shifts[1:2])
        normed_two[rows] = norm
        go = target[rows] * valid
        go_low[rows] = low(go)
        add_row(2, row_sum(go))

        @pl.loop(0, 4)
        def _(pair):
            for part in (2 * pair, 2 * pair + 1):
                cols = aligned(part * 256, 256, 256)
                value, slope = gelu_pair(dot(normed_two[rows], expand[:, cols]) + inner[:, cols])
                active[rows, cols] = low(value)
                grad = low(slope * dot_nt(go_low[rows], shrink[cols]))
                before_grad[rows, cols] = grad
                inner_sum[part] += row_sum(grad.astype(F32))

    for part in range(8):
        lanes = slice(part % 2 * 256, part % 2 * 256 + 256)
        vectors[8 + part // 2 : 9 + part // 2, lanes] = inner_sum[part]
    if reduce:
        await_greetings()
    for part in range(2):
        cols = slice(part * 256, part * 256 + 256)
        store_packed(put, part * 16, DECODER_EXPAND, dot_tn(normed_two[:, cols], before_grad[...]))
    if reduce:
        engine.send(2048)

    @pl.loop(0, 8)
    def _(part):
        cols = aligned(part * 256, 256, 256)
        store_packed(put, part * 4, DECODER_SHRINK, dot_tn(active[:, cols], go_low[...]))

    if reduce:
        engine.send(4096)

    @pl.loop(0, blocks)
    def _(tile):
        rows = rows_of(tile, BLOCK)
        valid = validity(tile, BLOCK)
        center = start[rows] + (dot(context[rows], merging[...]) + biases[1:2])
        unit, inverse = standardize(center)
        feed = dot(active[rows], shrink[...]) + biases[2:3]
        add_row(14, row_sum(valid * feed * feed))
        output = center + feed
        add_row(15, row_sum(valid * output * output))
        norm_grad = dot_nt(before_grad[rows], expand[...])
        add_row(5, row_sum(norm_grad * unit))
        add_row(7, row_sum(norm_grad))
        grad = target[rows] * valid + norm_back(unit, inverse, gains[1:2], norm_grad)
        target[rows] = grad
        add_row(1, row_sum(grad))
        below = low(grad)
        attention_low[rows] = below
        outer = low(dot_nt(below, merging[...]))
        context_grad[rows] = outer
        product = (outer.astype(F32) * flipped[:, rows].T).T
        for head in range(4):
            delta[head, :, rows] = row_sum(product[head * 64 : head * 64 + 64])
        turns(2 * tile)

    for part in range(2):
        cols = slice(part * 256, part * 256 + 256)
        store_packed(put, part * 16, DECODER_MERGE, dot_tn(attention_low[:, cols], context[...]))
        shards = slice(part * 16, part * 16 + 16)
        put(shards, 4352, jnp.zeros((16, 16, DECODER_PLAN.chunks * DECODER_PLAN.span - 4352), F32))
    if reduce:
        engine.send(DECODER_PLAN.chunks * DECODER_PLAN.span)

    flipped[...] = jnp.zeros_like(flipped)

    @pl.loop(0, 2 * tiles)
    def _(step):
        pair, tile = step // tiles, step % tiles
        rows = rows_of(tile)
        lanes = pair_lanes(pair)
        values = mixed[rows, pair_lanes(pair, 512)]
        raws, probabilities, queries, outers = [], [], [], []
        for half in range(2):
            prob = probs[pair * 2 + half, rows]
            outer = only(context_grad[:, lanes], half)
            raw = low(prob.astype(F32) * (dot_nt(values, outer) - delta[pair * 2 + half]))
            flipped[head_rows(pair, half)] += dot(turned[head_rows(pair, half), rows], raw)
            raws.append(raw)
            probabilities.append(prob)
            outers.append(outer)
            queries.append(only(mixed[:, lanes], half))
        key_grad = dot(jnp.concatenate(raws, axis=1), jnp.concatenate(queries, axis=0))
        mixed_grad[rows, pair_lanes(pair, 256)] = low(key_grad * 0.125)
        value_grad = dot(jnp.concatenate(probabilities, axis=1), jnp.concatenate(outers, axis=0))
        mixed_grad[rows, pair_lanes(pair, 512)] = low(value_grad)
        if reduce:
            engine.turn(tiles + step)

    def last(tile, entry_grad):
        rows = rows_of(tile, BLOCK)
        mixed_grad[rows, 0:256] = low(flipped[:, rows].T * 0.125)
        norm_grad = dot_nt(mixed_grad[rows], attend[...])
        unit, inverse = standardize(start[rows])
        add_row(4, row_sum(norm_grad * unit))
        add_row(6, row_sum(norm_grad))
        grad = target[rows] + norm_back(unit, inverse, gains[0:1], norm_grad)
        spread = spread_of(tile)
        fill = validity(tile, BLOCK) * (1.0 - jnp.sum(spread, axis=1, keepdims=True))
        add_row(3, row_sum(fill * grad))
        turns(3 * tiles + 2 * tile)
        return entry_grad + dot_tn(low(spread), low(grad))

    entry_grad = lax.fori_loop(0, blocks, last, jnp.zeros((TILE, 512), F32))
    add_row(0, row_sum(entry_grad))
    entry_low = low(entry_grad)
    encoded_grad[...] = low(dot_nt(entry_low, entry_weight[...]))
    store_packed(put_rest, 0, ENTRY, dot_tn(sent[...], entry_low))

    @pl.loop(0, 2)
    def _(part):
        cols = aligned(part * 256, 256, 256)
        store_packed(put_rest, part * 16, DECODER_ATTEND, dot_tn(normed[:, cols], mixed_grad[...]))

    if reduce:
        engine.close()


def decoder_call(
    reduce, sizes, slots, table, sent, cotangent, entry_weight, biases, mask_token,
    gains, shifts, attend, merging, expand, inner, shrink,
):
    length = cotangent.shape[1]
    width = 512
    if reduce:
        summed = jax.ShapeDtypeStruct((DECODER_PLAN.chunks, 16, DECODER_PLAN.span), F32)
        extra = reducer_scratch(DECODER_PLAN)
        params = dict(collective_id=1, has_side_effects=True)
    else:
        summed = jax.ShapeDtypeStruct((DECODER_PLAN.chunks, 2, 16, 16, DECODER_PLAN.span), BF16)
        extra = []
        params = dict()
    return pl.pallas_call(
        functools.partial(decoder_kernel, reduce),
        out_shape=(
            summed,
            jax.ShapeDtypeStruct((1, 2, 16, 16, UNIT), BF16),
            jax.ShapeDtypeStruct((24, width), F32),
            jax.ShapeDtypeStruct((256, 768), BF16),
        ),
        in_specs=[smem_spec()] + [vmem_spec()] * 8 + [any_spec()] * 6,
        out_specs=(vmem_spec(),) * 4,
        scratch_shapes=[
            pltpu.VMEM((length, width), F32),
            pltpu.VMEM((length, width), BF16),
            pltpu.VMEM((length, 768), BF16),
            pltpu.VMEM((512, length), BF16),
            pltpu.VMEM((4, length, length), BF16),
            pltpu.VMEM((256, length), F32),
            pltpu.VMEM((length, 256), BF16),
            pltpu.VMEM((length, width), BF16),
            pltpu.VMEM((length, 2048), BF16),
            pltpu.VMEM((length, 2048), BF16),
            pltpu.VMEM((length, width), BF16),
            pltpu.VMEM((length, width), BF16),
            pltpu.VMEM((length, 256), BF16),
            pltpu.VMEM((4, 1, length), F32),
            pltpu.VMEM((length, 768), BF16),
            pltpu.VMEM((length, width), F32),
            pltpu.VMEM((4, length, 128), BF16),
            pltpu.VMEM(entry_weight.shape, BF16),
            pltpu.VMEM(attend.shape, BF16),
            pltpu.VMEM(merging.shape, BF16),
            pltpu.VMEM(expand.shape, BF16),
            pltpu.VMEM(shrink.shape, BF16),
            pltpu.VMEM((8, 1, 256), F32),
            pltpu.SemaphoreType.DMA((6,)),
        ]
        + extra,
        compiler_params=pltpu.CompilerParams(vmem_limit_bytes=63 * 2**20, **params),
        name="decoder_block",
    )(
        sizes, slots, table, sent, biases, mask_token[None], gains, shifts,
        inner[None], cotangent, entry_weight, attend, merging, expand, shrink,
    )


def encoder_backward_kernel(
    reduce, encoded_grad, sums, decoder_vectors, gains, tokens, rest, attend_far, merging_far, expand_far,
    shrink_far, normed_far, mixed_far, turned_far, probs_far, context_far, middle_far, normed_two_far, active_far,
    slope_far, summed, tail_summed, vectors, tokens_grad, *refs,
):
    if reduce:
        decoder_sums, arrived = refs[:2]
        refs = refs[2:]
    (
        hidden, attend, merging, expand, shrink, normed, mixed, turned, probs, context, middle, normed_two, active,
        slope, before_grad, norm_sum, attention_low, context_grad, key_grad, query_turned, mixed_grad, active_turned,
        flipped, inner_sum, load_sem, part_sem,
    ) = refs[:26]
    pack = lax.axis_index("section")

    def part_loads(part):
        cols = aligned(part * 1024, 1024, 1024)
        slot = part % 2
        return [
            pltpu.make_async_copy(expand_far.at[:, cols], expand.at[slot], part_sem.at[slot, 0]),
            pltpu.make_async_copy(shrink_far.at[cols], shrink.at[slot], part_sem.at[slot, 1]),
            pltpu.make_async_copy(slope_far.at[part], slope.at[slot], part_sem.at[slot, 2]),
        ]

    if reduce:
        (
            decoder_total, encoder_total, decoder_got, encoder_got, payload,
            own_sem, small_send, small_recv, pay_send, pay_recv, small_load,
        ) = refs[26:37]
        mine, partner = neighbours()
        greet(partner)
        engine = reducer(ENCODER_PLAN, mine, partner, summed, refs[37:68])
        tail = reducer(TAIL_PLAN, mine, partner, tail_summed, refs[68:])
        put_tail = tail.put
        first_own = fetch(
            [
                pair
                for pair in (
                    (rest.at[0, 1 - mine["c"]], engine.staging.at[0]),
                    (rest.at[0, mine["c"]], engine.own.at[0]),
                )
            ],
            own_sem,
        )
        decoder_load = pltpu.make_async_copy(decoder_vectors, decoder_total.at[0], small_load)
        decoder_load.start()
    else:
        put_tail = put_into(tail_summed)
    early = pltpu.make_async_copy(active_far, active, load_sem.at[10])
    early.start()
    for copy in part_loads(0):
        copy.start()
    if reduce:
        for copy in first_own:
            copy.wait()
        await_greetings()
        engine.first_copy(0).start()
    loads = fetch(
        [
            (normed_two_far, normed_two),
            (middle_far, middle),
            (merging_far, merging),
            (context_far, context),
            (mixed_far, mixed),
            (probs_far, probs),
            (turned_far.at[0:768], turned),
            (normed_far, normed),
            (attend_far, attend),
            (tokens.at[pack], hidden),
        ],
        load_sem,
    )
    for copy in part_loads(1):
        copy.start()
    vectors[...] = sums[...]
    go_low = encoded_grad[...]
    go = go_low.astype(F32)
    vectors[1:2, :768] = row_sum(go)
    norm_sum[...] = jnp.zeros_like(norm_sum)

    def unit_grad(unit, place, pieces):
        put = engine.put_unit(unit) if reduce else put_unit_into(summed, unit)
        for first, value in pieces:
            store_packed(put, first, (0,) + place[1:], value)
        if reduce:
            engine.first_copy(unit).start()

    def shrink_start():
        early.wait()
        for piece in range(4):
            rows = slice(piece * 768, piece * 768 + 768)
            active_turned[rows] = active[:, rows].T

    def shrink_grad(part):
        cols = aligned(part * 256, 256, 256)
        pieces = []
        for piece in range(4):
            rows = slice(piece * 768, piece * 768 + 768)
            pieces.append((piece * 8, dot(active_turned[rows], encoded_grad[:, cols])))
        unit_grad(1 + part, ENCODER_SHRINK[0], pieces)

    def hidden_layer(part):
        for copy in part_loads(part):
            copy.wait()
        slot = part % 2
        grad = low(slope[slot] * dot_nt(encoded_grad[...], shrink[slot]))
        before_grad[...] = grad
        inner_sum[part] = row_sum(grad.astype(F32))
        norm_sum[...] += dot_nt(grad, expand[slot])

        @pl.when(part == 0)
        def _():
            for copy in part_loads(2):
                copy.start()

    def expand_grad(part):
        @pl.when(part == 0)
        def _():
            loads[0].wait()
            flipped[...] = normed_two[...].T

        unit_grad(4 + part, ENCODER_EXPAND[0], [(0, dot(flipped[...], before_grad[...]))])

    def middle_layer():
        loads[1].wait()
        loads[2].wait()
        for part in range(3):
            vectors[6 + part : 7 + part] = inner_sum[part]
        unit, inverse = standardize(middle[...])
        norm_grad = norm_sum[...]
        vectors[3:4, :768] = row_sum(norm_grad * unit)
        vectors[5:6, :768] = row_sum(norm_grad)
        grad = encoded_grad[...].astype(F32) + norm_back(unit, inverse, gains[1:2], norm_grad)
        vectors[0:1, :768] = row_sum(grad)
        tokens_grad[...] = grad
        below = low(grad)
        attention_low[...] = below
        context_grad[...] = low(dot_nt(below, merging[...]))
        for copy in loads[3:7]:
            copy.wait()

    def attention(first):
        @pl.loop(first, first + 2)
        def _(pair):
            lanes = pair_lanes(pair)
            values = mixed[:, pair_lanes(pair, 1536)]
            keys_total = jnp.zeros((TILE, 128), F32)
            values_total = jnp.zeros((TILE, 128), F32)
            for half in range(2):
                prob = probs[pair * 2 + half]
                outer = only(context_grad[:, lanes], half)
                query = only(mixed[:, lanes], half)
                wide = prob.astype(F32)
                grad = dot_nt(values, outer)
                raw = low(wide * (grad - jnp.sum(wide * grad, axis=0, keepdims=True)))
                keys_total = keys_total + dot(raw, query)
                values_total = values_total + dot(prob, outer)
                rows = head_rows(pair, half)
                query_turned[rows] = dot(turned[rows], raw)
            key_grad[0, :, lanes] = keys_total
            key_grad[1, :, lanes] = values_total

    def mixing():
        mixed_grad[:, 0:768] = low(query_turned[...].T * 0.125)
        mixed_grad[:, 768:1536] = low(key_grad[0] * 0.125)
        mixed_grad[:, 1536:2304] = low(key_grad[1])

    def attend_grad(part):
        @pl.when(part == 0)
        def _():
            loads[7].wait()
            flipped[...] = normed[...].T

        wide = aligned(part * 1024, 1024, 1024)
        unit_grad(7 + part, ENCODER_ATTEND[0], [(0, dot(flipped[...], mixed_grad[:, wide]))])

    def tail_grad():
        store_packed(put_tail, 0, ENCODER_ATTEND[2], dot(flipped[...], mixed_grad[:, 2048:2304]))
        store_packed(put_tail, 0, ENCODER_MERGE, dot_tn(attention_low[...], context[...]))
        if reduce:
            tail.send(UNIT)

    def input_layer():
        loads[8].wait()
        loads[9].wait()
        norm_grad = dot_nt(mixed_grad[...], attend[...])
        unit, inverse = standardize(hidden[...])
        vectors[2:3, :768] = row_sum(norm_grad * unit)
        vectors[4:5, :768] = row_sum(norm_grad)
        grad = tokens_grad[...] + norm_back(unit, inverse, gains[0:1], norm_grad)
        tokens_grad[...] = grad
        if reduce:
            payload[...] = low(grad)

    if not reduce:
        shrink_start()
        for part in range(3):
            shrink_grad(part)
        for part in range(3):
            hidden_layer(part)
            expand_grad(part)
        middle_layer()
        for first in (0, 2, 4):
            attention(first)
        mixing()
        for part in range(2):
            attend_grad(part)
        tail_grad()
        input_layer()
        return

    def exchange(source, piece):
        rows = aligned(piece * 32, 32, 32)
        return remote(source.at[rows], arrived.at[rows], pay_send.at[piece], pay_recv.at[piece], partner["x"])

    small_route = ("c",) + ROUTES[0]
    totals = ((decoder_total, decoder_got), (encoder_total, encoder_got))

    def small_copy(stage, kind):
        source, target = totals[kind]
        return remote(
            source.at[stage],
            target.at[stage],
            small_send.at[stage, kind],
            small_recv.at[stage, kind],
            partner[small_route[stage]],
        )

    def small_advance(stage):
        if stage == 0:
            encoder_total[0] = vectors[...]
        for kind in range(2):
            source, target = totals[kind]
            if stage > 0:
                small_copy(stage - 1, kind).wait_recv()
                source[stage] = source[stage - 1] + target[stage - 1]
            if stage < 5:
                small_copy(stage, kind).start()

    shrink_start()
    shrink_grad(0)
    decoder_load.wait()

    def attention_all():
        @pl.loop(0, 3)
        def _(step):
            attention(2 * step)

        mixing()

    def ending():
        tail_grad()
        input_layer()

    part = functools.partial
    works = {4: middle_layer, 5: attention_all, 7: ending}
    turns = ENCODER_PLAN.chunks + TAIL_PLAN.chunks + 4 * LAG
    works.update({8 + stage + max(0, stage - 1): part(small_advance, stage) for stage in range(6)})

    @pl.loop(0, turns)
    def _(number):
        engine.turn(number)
        tail.turn(number - ENCODER_PLAN.chunks)

        @pl.when(number <= 1)
        def _():
            shrink_grad(number + 1)

        @pl.when((number >= 2) & (number <= 4))
        def _():
            expand_grad(number - 2)

        @pl.when((number >= 1) & (number <= 3))
        def _():
            hidden_layer(number - 1)

        for position, work in works.items():
            pl.when(number == position)(work)

        @pl.when(number == 6)
        def _():
            @pl.loop(0, 2)
            def _(part):
                attend_grad(part)

        @pl.when((pack == 0) & (number < 8))
        def _():
            exchange(encoded_grad, number).start()

        @pl.when((pack == 1) & (number >= 8) & (number < 16))
        def _():
            exchange(payload, number - 8).start()

    for stage in range(5):
        for kind in range(2):
            small_copy(stage, kind).wait_send()
    for piece in range(8):
        exchange(payload, piece).wait()
    engine.close()
    tail.close()
    vectors[...] = encoder_total[5]
    decoder_sums[...] = decoder_total[5]


def encoder_backward_call(reduce, tokens, encoded_grad, sums, decoder_vectors, rest, kept, gains, attend, merging, expand, shrink):
    if reduce:
        summed = tuple(
            jax.ShapeDtypeStruct((plan.chunks, 16, plan.span), F32) for plan in (ENCODER_PLAN, TAIL_PLAN)
        )
        more = (
            jax.ShapeDtypeStruct(decoder_vectors.shape, F32),
            jax.ShapeDtypeStruct((256, 768), BF16),
        )
        more_specs = (vmem_spec(), any_spec())
        extra = [
            pltpu.VMEM((6,) + decoder_vectors.shape, F32),
            pltpu.VMEM((6,) + sums.shape, F32),
            pltpu.VMEM((5,) + decoder_vectors.shape, F32),
            pltpu.VMEM((5,) + sums.shape, F32),
            pltpu.VMEM((256, 768), BF16),
            pltpu.SemaphoreType.DMA((2,)),
            pltpu.SemaphoreType.DMA((5, 2)),
            pltpu.SemaphoreType.DMA((5, 2)),
            pltpu.SemaphoreType.DMA((8,)),
            pltpu.SemaphoreType.DMA((8,)),
            pltpu.SemaphoreType.DMA,
        ] + reducer_scratch(ENCODER_PLAN) + reducer_scratch(TAIL_PLAN)
        params = dict(collective_id=2, has_side_effects=True)
    else:
        summed = tuple(
            jax.ShapeDtypeStruct((plan.chunks, 2, 16, 16, plan.span), BF16) for plan in (ENCODER_PLAN, TAIL_PLAN)
        )
        more, more_specs, extra, params = (), (), [], dict()
    return pl.pallas_call(
        functools.partial(encoder_backward_kernel, reduce),
        out_shape=summed
        + (
            jax.ShapeDtypeStruct(sums.shape, F32),
            jax.ShapeDtypeStruct((256, 768), F32),
        )
        + more,
        in_specs=[vmem_spec()] * 2 + [any_spec(), vmem_spec()] + [any_spec()] * 15,
        out_specs=(vmem_spec(),) * 4 + more_specs,
        scratch_shapes=[
            pltpu.VMEM((256, 768), F32),
            pltpu.VMEM(attend.shape, BF16),
            pltpu.VMEM(merging.shape, BF16),
            pltpu.VMEM((2, 768, 1024), BF16),
            pltpu.VMEM((2, 1024, 768), BF16),
            pltpu.VMEM((256, 768), BF16),
            pltpu.VMEM((256, 2304), BF16),
            pltpu.VMEM((768, 256), BF16),
            pltpu.VMEM((12, 256, 256), BF16),
            pltpu.VMEM((256, 768), BF16),
            pltpu.VMEM((256, 768), F32),
            pltpu.VMEM((256, 768), BF16),
            pltpu.VMEM((256, 3072), BF16),
            pltpu.VMEM((2, 256, 1024), F32),
            pltpu.VMEM((256, 1024), BF16),
            pltpu.VMEM((256, 768), F32),
            pltpu.VMEM((256, 768), BF16),
            pltpu.VMEM((256, 768), BF16),
            pltpu.VMEM((2, 256, 768), F32),
            pltpu.VMEM((768, 256), F32),
            pltpu.VMEM((256, 2304), BF16),
            pltpu.VMEM((3072, 256), BF16),
            pltpu.VMEM((768, 256), BF16),
            pltpu.VMEM((3, 1, 1024), F32),
            pltpu.SemaphoreType.DMA((11,)),
            pltpu.SemaphoreType.DMA((2, 3)),
        ]
        + extra,
        compiler_params=pltpu.CompilerParams(vmem_limit_bytes=62 * 2**20, **params),
        name="encoder_backward",
    )(encoded_grad, sums, decoder_vectors, gains, tokens, rest, attend, merging, expand, shrink, *kept)


def unpack(packed, place):
    span = packed.shape[-1]

    def take(start, size):
        pieces = []
        while size:
            chunk, first = divmod(start, span)
            length = min(size, span - first)
            pieces.append(packed[chunk, ..., first : first + length])
            start, size = start + length, size - length
        return pieces[0] if len(pieces) == 1 else jnp.concatenate(pieces, axis=-1)

    offset, count, width = place
    pieces = [take(offset + i * width, width) for i in range(count // 16)]
    if count % 16:
        rest = take(offset + count // 16 * width, width // 2)
        pieces.append(jnp.concatenate([rest[..., :8, :], rest[..., 8:, :]], axis=-1))
    return pieces[0] if len(pieces) == 1 else jnp.concatenate(pieces, axis=-2)


def finish_kernel(
    decoder_summed_far, decoder_sums_far, encoder_sums_far, summed_far, tail_far, arrived_far, tokens_grad_far, encoded_grad_far,
    boundary, statistics, e_gains, e_shifts, e_biases, e_attend, e_merge, e_expand, e_inner, e_shrink,
    d_entry, d_biases, mask_grad, d_gains, d_shifts, d_attend, d_merge, d_expand, d_inner, d_shrink,
    decoder_summed, decoder_sums, encoder_sums, summed, tail, arrived, tokens_grad, encoded_grad, load_sem,
):
    section = lax.axis_index("section")
    loads = fetch(
        [
            (decoder_summed_far, decoder_summed),
            (decoder_sums_far, decoder_sums),
            (encoder_sums_far, encoder_sums),
            (summed_far, summed),
            (tail_far, tail),
            (arrived_far, arrived),
            (tokens_grad_far, tokens_grad),
            (encoded_grad_far, encoded_grad),
        ],
        load_sem,
    )
    number = section * lax.axis_size("dp") + lax.axis_index("dp")

    def own(rows, count):
        width = rows.shape[1]
        return pltpu.roll(rows, (width - number * count) % width, axis=1)[:, :count]

    def own_line(rows, count):
        return own(jnp.concatenate([rows[i : i + 1] for i in range(rows.shape[0])], axis=1), count)

    for copy in loads[:3]:
        copy.wait()
    lane = iota((1, 128), 1)
    values = jnp.zeros((1, 128), F32)
    for sums, width, first, count_row, base in ((encoder_sums, DE, 10, 14, 0), (decoder_sums, DD, 12, 16, 4)):
        scale = 1.0 / (sums[count_row : count_row + 1, 0:1] * width)
        for i in range(4):
            value = jnp.sum(sums[first + i : first + i + 1, :], axis=1, keepdims=True) * scale
            values = jnp.where(lane == base + i, value, values)
    statistics[...] = jnp.sqrt(values)[:, :8]
    rows = own(encoder_sums[0:8, :DE], 24)
    e_biases[...] = rows[0:2]
    e_gains[...] = rows[2:4]
    e_shifts[...] = rows[4:6]
    e_inner[...] = own_line(encoder_sums[6:9], 96)
    rows = own(decoder_sums[0:8], 16)
    d_biases[...] = rows[0:3]
    mask_grad[...] = rows[3:4]
    d_gains[...] = rows[4:6]
    d_shifts[...] = rows[6:8]
    d_inner[...] = own_line(decoder_sums[8:12], 64)

    d_merge[...] = unpack(decoder_summed, DECODER_MERGE)
    d_expand[...] = unpack(decoder_summed, DECODER_EXPAND)
    d_shrink[...] = unpack(decoder_summed, DECODER_SHRINK)
    loads[3].wait()
    loads[4].wait()
    d_entry[...] = unpack(summed, ENTRY)
    d_attend[...] = unpack(summed, DECODER_ATTEND)
    for target, places in ((e_expand, ENCODER_EXPAND), (e_attend, ENCODER_ATTEND), (e_shrink, ENCODER_SHRINK)):
        start = 0
        for place in places:
            source = tail if place is ENCODER_ATTEND[2] else summed
            target[:, start : start + place[2]] = unpack(source, place)
            start += place[2]
    e_merge[...] = unpack(tail, ENCODER_MERGE)
    for copy in loads[5:]:
        copy.wait()

    @pl.when(section == 0)
    def _():
        boundary[0, 0] = tokens_grad[...]
        boundary[0, 1] = arrived[...].astype(F32)

    @pl.when(section == 1)
    def _():
        boundary[0, 0] = arrived[...].astype(F32)
        boundary[0, 1] = encoded_grad[...].astype(F32)


def finish_call(*operands):
    shapes = (
        (1, 2, 256, 768), (1, 8), (2, 24), (2, 24), (2, 24), (24, 2304), (24, 768), (24, 3072), (1, 96), (96, 768),
        (24, 512), (3, 16), (1, 16), (2, 16), (2, 16), (16, 768), (16, 256), (16, 2048), (1, 64), (64, 512),
    )
    outs = list(
        pl.pallas_call(
            finish_kernel,
            out_shape=tuple(jax.ShapeDtypeStruct(shape, F32) for shape in shapes),
            in_specs=[any_spec()] * len(operands),
            out_specs=(vmem_spec(),) * len(shapes),
            scratch_shapes=[pltpu.VMEM(operand.shape, operand.dtype) for operand in operands]
            + [pltpu.SemaphoreType.DMA((len(operands),))],
            compiler_params=pltpu.CompilerParams(vmem_limit_bytes=60 * 2**20),
            name="finish",
        )(*operands)
    )
    for line in (1, 8, 12, 18):
        outs[line] = outs[line].reshape(-1)
    for turned in (6, 16):
        outs[turned] = outs[turned].T
    return tuple(outs)


def scatter_sum(member, share_dim):
    return lax.psum_scatter(
        member, ("section", "dp"), scatter_dimension=share_dim, tiled=True
    )


def finish_generic(decoder_part, part, tail, decoder_sums, encoder_sums, tokens_grad, encoded_grad):
    section = lax.axis_index("section")
    payload = jnp.where(section == 0, encoded_grad, low(tokens_grad))

    def whole(packed, *places):
        packed = jnp.swapaxes(packed, 1, 2).reshape(-1, 32, 16, packed.shape[-1])
        blocks = [unpack(packed, place).reshape(32 * place[1], place[2]) for place in places]
        return scatter_sum(jnp.concatenate(blocks, axis=1).astype(F32), 0)

    def line(value):
        return scatter_sum(value, value.ndim - 1)

    arrived = lax.ppermute(payload, "section", [(0, 1), (1, 0)]).astype(F32)
    boundary = jnp.where(
        section == 0,
        jnp.stack([tokens_grad, arrived]),
        jnp.stack([arrived, encoded_grad.astype(F32)]),
    )
    sums = jnp.concatenate(
        [jnp.sum(encoder_sums[10:14], axis=1), jnp.sum(decoder_sums[12:16], axis=1)]
    )
    sums, counts = lax.psum((sums, (encoder_sums[14, 0], decoder_sums[16, 0])), ("section", "dp"))
    scales = jnp.concatenate([jnp.full((4,), counts[0] * DE), jnp.full((4,), counts[1] * DD)])
    return (
        boundary[None],
        jnp.sqrt(sums / scales),
        line(encoder_sums[2:4, :DE]),
        line(encoder_sums[4:6, :DE]),
        line(encoder_sums[0:2, :DE]),
        jnp.concatenate([whole(part, *ENCODER_ATTEND[:2]), whole(tail, ENCODER_ATTEND[2])], axis=1),
        whole(tail, ENCODER_MERGE).T,
        whole(part, *ENCODER_EXPAND),
        line(encoder_sums[6:9].reshape(-1)),
        whole(part, *ENCODER_SHRINK),
        whole(decoder_part[1], ENTRY),
        line(decoder_sums[0:3]),
        line(decoder_sums[3]),
        line(decoder_sums[4:6]),
        line(decoder_sums[6:8]),
        whole(decoder_part[1], DECODER_ATTEND),
        whole(decoder_part[0], DECODER_MERGE).T,
        whole(decoder_part[0], DECODER_EXPAND),
        line(decoder_sums[8:12].reshape(-1)),
        whole(decoder_part[0], DECODER_SHRINK),
    )


def body(
    visible_tokens,
    cotangent,
    chip_sizes,
    ground_distance,
    visible_slots,
    encoder_gains,
    encoder_shifts,
    encoder_biases,
    encoder_attend,
    encoder_merge,
    encoder_expand,
    encoder_inner,
    encoder_shrink,
    decoder_entry,
    decoder_biases,
    mask_token,
    decoder_gains,
    decoder_shifts,
    decoder_attend,
    decoder_merge,
    decoder_widen_weight,
    decoder_inner,
    decoder_shrink,
):
    reduce = (lax.axis_size("section"), lax.axis_size("dp")) == (2, 16)
    sent, sums, table, *kept = encoder_forward_call(
        chip_sizes, ground_distance, visible_tokens, encoder_gains, encoder_shifts, encoder_biases,
        encoder_attend, encoder_merge, encoder_expand, encoder_inner, encoder_shrink,
    )
    decoder_summed, rest, decoder_vectors, encoded_grad = decoder_call(
        reduce, chip_sizes, visible_slots, table, sent, cotangent, decoder_entry, decoder_biases, mask_token,
        decoder_gains, decoder_shifts, decoder_attend, decoder_merge, decoder_widen_weight, decoder_inner,
        decoder_shrink,
    )
    summed, tail, encoder_sums, tokens_grad, *more = encoder_backward_call(
        reduce, visible_tokens, encoded_grad, sums, decoder_vectors, rest, kept,
        encoder_gains, encoder_attend, encoder_merge, encoder_expand, encoder_shrink,
    )
    if reduce:
        decoder_sums, arrived = more
        return finish_call(
            decoder_summed, decoder_sums, encoder_sums, summed, tail, arrived, tokens_grad, encoded_grad
        )
    return finish_generic(
        (decoder_summed, rest), summed, tail, decoder_vectors, encoder_sums, tokens_grad, encoded_grad
    )


def solution(mesh):
    in_specs = (
        P("dp", None, None),
        P("dp", None, None),
        P("dp", None),
        P("dp", None),
        P("dp", None),
        P(),
        P(),
        P(),
        P(),
        P(),
        P(),
        P(),
        P(),
        P(),
        P(),
        P(),
        P(),
        P(),
        P(),
        P(),
        P(),
        P(),
        P(),
    )
    out_specs = (
        P("section", "dp", None, None),
        P(),
        P(None, ("section", "dp")),
        P(None, ("section", "dp")),
        P(None, ("section", "dp")),
        P(("section", "dp"), None),
        P(None, ("section", "dp")),
        P(("section", "dp"), None),
        P(("section", "dp")),
        P(("section", "dp"), None),
        P(("section", "dp"), None),
        P(None, ("section", "dp")),
        P(("section", "dp")),
        P(None, ("section", "dp")),
        P(None, ("section", "dp")),
        P(("section", "dp"), None),
        P(None, ("section", "dp")),
        P(("section", "dp"), None),
        P(("section", "dp")),
        P(("section", "dp"), None),
    )
    return jax.shard_map(body, mesh=mesh, in_specs=in_specs, out_specs=out_specs, check_vma=False)
```

```python
import functools
import types

import jax
import jax.numpy as jnp
import numpy as np
from jax import lax
from jax.experimental import pallas as pl
from jax.experimental.pallas import tpu as pltpu
from jax.sharding import PartitionSpec as P

DE = 768
DD = 512
TILE = 256
BLOCK = 512
NEGATIVE = -1e30
F32, BF16 = jnp.float32, jnp.bfloat16
MESH_ID = pl.DeviceIdType.MESH

CANON = ("x", "z2", "z1", "y")
ROUTES = (("x", "y", "z1", "z2"), ("y", "x", "z1", "z2"), ("z1", "z2", "x", "y"))
UNIT = 1536
LAG = 2
DECODER_PLAN = types.SimpleNamespace(widths=(3, 4, 2), chunks=4, slots=4, ring=3, span=1152)
ENCODER_PLAN = types.SimpleNamespace(widths=(3, 6, 3), chunks=9, slots=3, ring=3, span=1536)
TAIL_PLAN = types.SimpleNamespace(widths=(2, 3, 1), chunks=2, slots=2, ring=2, span=768)

DECODER_EXPAND, DECODER_SHRINK, DECODER_MERGE = (0, 16, 2048), (2048, 64, 512), (4096, 16, 256)
ENTRY, DECODER_ATTEND = (0, 24, 512), (768, 16, 768)
ENCODER_SHRINK = tuple((UNIT * (1 + part), 96, 256) for part in range(3))
ENCODER_EXPAND = tuple((UNIT * (4 + part), 24, 1024) for part in range(3))
ENCODER_ATTEND = ((UNIT * 7, 24, 1024), (UNIT * 8, 24, 1024), (0, 24, 256))
ENCODER_MERGE = (384, 24, 768)


def dot(a, b):
    return jnp.dot(a, b, preferred_element_type=F32)


def dot_nt(a, b):
    return lax.dot_general(a, b, (((1,), (1,)), ((), ())), preferred_element_type=F32)


def dot_tn(a, b):
    return lax.dot_general(a, b, (((0,), (0,)), ((), ())), preferred_element_type=F32)


def low(value):
    return value.astype(BF16)


def standardize(values):
    centered = values - jnp.mean(values, axis=-1, keepdims=True)
    inverse = lax.rsqrt(jnp.mean(centered * centered, axis=-1, keepdims=True) + 1e-05)
    return centered * inverse, inverse


def norm_back(unit, inverse, gain, grad):
    inner = grad * gain
    return inverse * (
        inner
        - jnp.mean(inner, axis=-1, keepdims=True)
        - unit * jnp.mean(inner * unit, axis=-1, keepdims=True)
    )


def row_sum(values):
    return jnp.sum(values, axis=0, keepdims=True)


def gelu_pair(before):
    half = 0.5 * (1.0 + lax.erf(before * 0.7071067811865476))
    density = jnp.exp(-0.5 * before * before) * 0.3989422804014327
    return before * half, half + before * density


def chip_of(places, sizes, pack):
    end = sizes[pack, 0]
    chip = (places >= end).astype(jnp.int32)
    for slot in range(1, 4):
        end = end + sizes[pack, slot]
        chip = chip + (places >= end).astype(jnp.int32)
    return chip


def iota(shape, dimension):
    return lax.broadcasted_iota(jnp.int32, shape, dimension)


def aligned(start, size, unit):
    if isinstance(start, int):
        return slice(start, start + size)
    return pl.ds(pl.multiple_of(start, unit), size)


def pair_lanes(pair, base=0):
    return aligned(base + pair * 128, 128, 128)


def head_rows(pair, half, base=0):
    return aligned(base + pair * 128 + half * 64, 64, 64)


def rows_of(tile, size=TILE):
    return aligned(tile * size, size, size)


def only(values, half):
    return jnp.where(iota((1, 128), 1) // 64 == half, values, jnp.zeros_like(values))


def fetch(pairs, sems):
    copies = [
        pltpu.make_async_copy(source, target, sems.at[i]) for i, (source, target) in enumerate(pairs)
    ]
    for copy in copies:
        copy.start()
    return copies


def store_packed(put, first, place, value):
    offset, count, width = place
    value = value.reshape(-1, count, width)
    shards = slice(first, first + value.shape[0]) if isinstance(first, int) else pl.ds(first, value.shape[0])
    for piece in range(count // 16):
        put(shards, offset + piece * width, value[:, piece * 16 : piece * 16 + 16])
    if count % 16:
        half = width // 2
        rest = value[:, count - 8 :]
        rest = jnp.concatenate([rest[:, :, :half], rest[:, :, half:]], axis=1)
        put(shards, offset + count // 16 * width, rest)


def halves(shards, value):
    pairs = value.reshape(value.shape[0] // 2, 2, *value.shape[1:])
    if isinstance(shards, slice):
        return slice(shards.start // 2, shards.stop // 2), pairs[:, 0], pairs[:, 1]
    return pl.ds(shards.start // 2, shards.size // 2), pairs[:, 0], pairs[:, 1]


def place_of(names, bits):
    index = 0
    for name in names:
        index = index * 2 + bits[name]
    return index


def left_after(route, stage):
    return tuple(name for name in CANON if name not in route[:stage])


def choices(names):
    for number in range(2 ** len(names)):
        yield {name: (number >> (len(names) - 1 - i)) & 1 for i, name in enumerate(names)}


def neighbours():
    section = lax.axis_index("section")
    data = lax.axis_index("dp")
    mine = {"x": section, "c": data % 2, "y": data // 2 % 2, "z1": data // 4 % 2, "z2": data // 8 % 2}
    partner = {"x": (1 - section, data)}
    for name, step in {"c": 1, "y": 2, "z1": 4, "z2": 8}.items():
        partner[name] = (section, data + step * (1 - 2 * mine[name]))
    return mine, partner


def greet(partner):
    barrier = pltpu.get_barrier_semaphore()
    for name in ("c",) + CANON:
        pl.semaphore_signal(barrier, inc=1, device_id=partner[name], device_id_type=MESH_ID)


def await_greetings():
    pl.semaphore_wait(pltpu.get_barrier_semaphore(), 5)


def remote(source, target, send, recv, device):
    return pltpu.make_async_remote_copy(
        src_ref=source,
        dst_ref=target,
        send_sem=send,
        recv_sem=recv,
        device_id=device,
        device_id_type=MESH_ID,
    )


def reducer(plan, mine, partner, out, refs):
    chunks, slots, span, ring = plan.chunks, plan.slots, plan.span, plan.ring
    progress = types.SimpleNamespace(sent=0)
    own, staging, first = refs[:3]
    sent, got = refs[3:15], refs[15:27]
    first_send, first_recv, send_sem, recv_sem = refs[27:31]

    def first_copy(chunk):
        return remote(staging.at[chunk % slots], first.at[chunk], first_send.at[chunk], first_recv.at[chunk], partner["c"])

    def stage_copy(route, stage, chunk):
        return remote(
            sent[route * 4 + stage].at[chunk % ring],
            got[route * 4 + stage].at[chunk],
            send_sem.at[route, stage, chunk],
            recv_sem.at[route, stage, chunk],
            partner[ROUTES[route][stage]],
        )

    def total(route, stage, chunk, bits):
        spot = place_of(CANON, bits)
        cols = slice(sum(plan.widths[:route]) * 128, sum(plan.widths[: route + 1]) * 128)
        value = own[chunk, spot, :, cols].astype(F32) + first[chunk, spot, :, cols].astype(F32)
        for earlier in range(stage):
            names = left_after(ROUTES[route], earlier + 1)
            value = value + got[route * 4 + earlier][chunk, place_of(names, bits)].astype(F32)
        return value

    def advance(stage, chunk):
        for route in range(3):
            if stage:
                stage_copy(route, stage - 1, chunk).wait_recv()
            else:
                first_copy(chunk).wait_recv() if route == 0 else None
            if stage < 4:

                @pl.when(chunk >= ring)
                def _(route=route):
                    stage_copy(route, stage, chunk - ring).wait_send()

        values = []
        for route in range(3):
            path = ROUTES[route]
            if stage == 4:
                values.append(total(route, 4, chunk, mine))
                continue
            names = left_after(path, stage + 1)
            for free in choices(names):
                bits = dict(mine)
                bits[path[stage]] = 1 - mine[path[stage]]
                bits.update(free)
                values.append((route, place_of(names, free), low(total(route, stage, chunk, bits))))
        if stage == 4:
            out[chunk] = jnp.concatenate(values, axis=1)
            return
        for route, spot, value in values:
            sent[route * 4 + stage][chunk % ring, spot] = value
        for route in range(3):
            stage_copy(route, stage, chunk).start()

    def turn(number):
        for stage in range(4, -1, -1):
            chunk = number - LAG * stage
            pl.when((chunk >= 0) & (chunk < chunks))(functools.partial(advance, stage, chunk))

    def put(shards, column, value):
        shards, even, odd = halves(shards, value)
        kept = low(jnp.where(mine["c"] == 0, even, odd))
        given = low(jnp.where(mine["c"] == 0, odd, even))
        width = value.shape[2]
        done = 0
        while done < width:
            chunk, start = divmod(column + done, span)
            size = min(width - done, span - start)
            own[chunk, shards, :, start : start + size] = kept[:, :, done : done + size]
            staging[chunk % slots, shards, :, start : start + size] = given[:, :, done : done + size]
            done += size

    def put_unit(unit):
        def put(shards, column, value):
            shards, even, odd = halves(shards, value)
            cols = slice(column, column + value.shape[2])
            own[unit, shards, :, cols] = low(jnp.where(mine["c"] == 0, even, odd))
            staging[unit % slots, shards, :, cols] = low(jnp.where(mine["c"] == 0, odd, even))

        @pl.when(unit >= slots)
        def _():
            first_copy(unit - slots).wait_send()

        return put

    def send(column):
        while (progress.sent + 1) * span <= column:
            first_copy(progress.sent).start()
            progress.sent += 1

    def close():
        for chunk in range(max(0, chunks - slots), chunks):
            first_copy(chunk).wait_send()
        for chunk in range(chunks - ring, chunks):
            for route in range(3):
                for stage in range(4):
                    stage_copy(route, stage, chunk).wait_send()

    return types.SimpleNamespace(
        own=own, staging=staging, turn=turn, put=put, put_unit=put_unit, first_copy=first_copy, send=send, close=close
    )


def reducer_scratch(plan):
    stages = [(width, block) for width in plan.widths for block in (8, 4, 2, 1)]
    return (
        [
            pltpu.VMEM((plan.chunks, 16, 16, plan.span), BF16),
            pltpu.VMEM((plan.slots, 16, 16, plan.span), BF16),
            pltpu.VMEM((plan.chunks, 16, 16, plan.span), BF16),
        ]
        + [pltpu.VMEM((plan.ring, block, 16, width * 128), BF16) for width, block in stages]
        + [pltpu.VMEM((plan.chunks, block, 16, width * 128), BF16) for width, block in stages]
        + [
            pltpu.SemaphoreType.DMA((plan.chunks,)),
            pltpu.SemaphoreType.DMA((plan.chunks,)),
            pltpu.SemaphoreType.DMA((3, 4, plan.chunks)),
            pltpu.SemaphoreType.DMA((3, 4, plan.chunks)),
        ]
    )


def put_into(parts):
    span = parts.shape[-1]

    def put(shards, column, value):
        shards, *pair = halves(shards, value)
        width = value.shape[2]
        done = 0
        while done < width:
            chunk, start = divmod(column + done, span)
            size = min(width - done, span - start)
            for core in range(2):
                parts[chunk, core, shards, :, start : start + size] = low(pair[core][:, :, done : done + size])
            done += size

    return put


def put_unit_into(parts, unit):
    def put(shards, column, value):
        shards, *pair = halves(shards, value)
        for core in range(2):
            parts[unit, core, shards, :, column : column + value.shape[2]] = low(pair[core])

    return put


def vmem_spec():
    return pl.BlockSpec(memory_space=pltpu.VMEM)


def any_spec():
    return pl.BlockSpec(memory_space=pl.ANY)


def smem_spec():
    return pl.BlockSpec(memory_space=pltpu.SMEM)


def encoder_forward_kernel(
    sizes, distance, frequency, gains, shifts, biases, inner, tokens, attend_far, merging_far, expand_far,
    shrink_far, sent, vectors, table, *refs,
):
    far = refs[:9]
    normed, mixed, turned, probs, context, middle, normed_two, active, slope = refs[9:18]
    hidden, attend, merging, expand, shrink, context_turned, load_sem, save_sem = refs[18:]
    pack = lax.axis_index("section")
    loads = fetch(
        [
            (tokens.at[pack], hidden),
            *[(attend_far.at[:, i * 768 : i * 768 + 768], attend.at[:, i * 768 : i * 768 + 768]) for i in range(3)],
            (merging_far, merging),
            *[(expand_far.at[:, i * 1024 : i * 1024 + 1024], expand.at[:, i * 1024 : i * 1024 + 1024]) for i in range(3)],
            *[(shrink_far.at[i * 1024 : i * 1024 + 1024], shrink.at[i * 1024 : i * 1024 + 1024]) for i in range(3)],
        ],
        load_sem,
    )
    saves = []

    def save(*numbers):
        for number in numbers:
            copy = pltpu.make_async_copy(refs[9 + number], far[number], save_sem.at[number])
            copy.start()
            saves.append(copy)

    vectors[...] = jnp.zeros_like(vectors)
    positions = iota((32, 128), 0).astype(F32)
    for chip in range(4):
        spacing = distance[pack, chip].astype(F32) / 16.0
        angle = positions * (spacing * frequency[...])
        table[0, chip] = jnp.sin(angle)
        table[1, chip] = jnp.cos(angle)
    key_chip = chip_of(4 * iota((TILE, 1), 0), sizes, pack)
    own_chip = chip_of(4 * iota((1, TILE), 1), sizes, pack)
    valid = (key_chip < 4).astype(F32)
    loads[0].wait()
    values = hidden[...]
    vectors[10:11, :768] = row_sum(valid * values * values)
    unit, _ = standardize(values)
    norm = low(unit * gains[0:1] + shifts[0:1])
    normed[...] = norm
    for part in range(3):
        cols = slice(part * 768, part * 768 + 768)
        loads[1 + part].wait()
        mix = dot(norm, attend[:, cols])
        mixed[:, cols] = low(mix)
        if part:
            turned[(part - 1) * 768 : part * 768] = low(mix.T)
    save(0, 1, 2)

    def score(head):
        pair, half = divmod(head, 2)
        query = only(mixed[:, pair_lanes(pair)], half) * BF16(0.125)
        return dot_nt(mixed[:, pair_lanes(pair, 768)], query)

    ready = [score(0), score(1)]
    for head in range(12):
        if head + 2 < 12:
            ready.append(score(head + 2))
        scores = jnp.where(key_chip == own_chip, ready[head], NEGATIVE)
        expos = jnp.exp(scores - jnp.max(scores, axis=0, keepdims=True))
        prob = low(expos * (1.0 / jnp.sum(expos, axis=0, keepdims=True)))
        probs[head] = prob
        context_turned[head * 64 : head * 64 + 64] = dot(turned[768 + head * 64 : 832 + head * 64], prob)

    mingled = low(context_turned[...].T)
    context[...] = mingled
    save(3, 4)
    loads[4].wait()
    attention = dot(mingled, merging[...]) + biases[0:1]
    vectors[11:12, :768] = row_sum(valid * attention * attention)
    center = hidden[...] + attention
    middle[...] = center
    unit, _ = standardize(center)
    norm = low(unit * gains[1:2] + shifts[1:2])
    normed_two[...] = norm
    save(5, 6)
    feed = jnp.zeros_like(center)
    def widened(part):
        if part % 2 == 0:
            loads[5 + part // 2].wait()
        cols = slice(part * 512, part * 512 + 512)
        return dot(norm, expand[:, cols]) + inner[:, cols]

    ready = [widened(0)]
    for part in range(6):
        if part < 5:
            ready.append(widened(part + 1))
        cols = slice(part * 512, part * 512 + 512)
        value, slant = gelu_pair(ready[part])
        value = low(value)
        active[:, cols] = value
        slope[part // 2, :, part % 2 * 512 : part % 2 * 512 + 512] = slant
        if part % 2 == 0:
            loads[8 + part // 2].wait()
        feed = feed + dot(value, shrink[cols])
    save(7, 8)
    feed = feed + biases[1:2]
    vectors[12:13, :768] = row_sum(valid * feed * feed)
    output = center + feed
    vectors[13:14, :768] = row_sum(valid * output * output)
    vectors[14:15, :768] = jnp.broadcast_to(row_sum(valid), (1, 768))
    sent[...] = low(output)
    for copy in saves:
        copy.wait()


def encoder_forward_call(sizes, distance, tokens, gains, shifts, biases, attend, merging, expand, inner, shrink):
    frequency = np.exp(-np.log(10000.0) * np.arange(DD // 4) / (DD // 4)).astype(np.float32)
    shapes = (
        ((256, 768), BF16),
        ((256, 2304), BF16),
        ((1536, 256), BF16),
        ((12, 256, 256), BF16),
        ((256, 768), BF16),
        ((256, 768), F32),
        ((256, 768), BF16),
        ((256, 3072), BF16),
        ((3, 256, 1024), F32),
    )
    return pl.pallas_call(
        encoder_forward_kernel,
        out_shape=(
            jax.ShapeDtypeStruct((256, 768), BF16),
            jax.ShapeDtypeStruct((16, 1024), F32),
            jax.ShapeDtypeStruct((2, 4, 32, 128), F32),
        )
        + tuple(jax.ShapeDtypeStruct(*shape) for shape in shapes),
        in_specs=[smem_spec()] * 2 + [vmem_spec()] * 5 + [any_spec()] * 5,
        out_specs=(vmem_spec(),) * 3 + (any_spec(),) * len(shapes),
        scratch_shapes=[pltpu.VMEM(*shape) for shape in shapes]
        + [
            pltpu.VMEM((256, 768), F32),
            pltpu.VMEM(attend.shape, BF16),
            pltpu.VMEM(merging.shape, BF16),
            pltpu.VMEM(expand.shape, BF16),
            pltpu.VMEM(shrink.shape, BF16),
            pltpu.VMEM((768, 256), F32),
            pltpu.SemaphoreType.DMA((11,)),
            pltpu.SemaphoreType.DMA((len(shapes),)),
        ],
        compiler_params=pltpu.CompilerParams(vmem_limit_bytes=60 * 2**20),
        name="encoder_forward",
    )(
        sizes, distance, jnp.asarray(frequency)[None], gains, shifts, biases, inner[None], tokens, attend, merging,
        expand, shrink,
    )


def decoder_kernel(
    reduce, sizes, slots, table, sent, biases, mask_token, gains, shifts, inner,
    cotangent, entry_far, attend_far, merging_far, expand_far, shrink_far,
    summed, rest, vectors, encoded_grad, *refs,
):
    (
        start, normed, mixed, turned, probs, flipped, context, normed_two, active,
        before_grad, go_low, attention_low, context_grad, delta, mixed_grad, target, masked_keys,
        entry_weight, attend, merging, expand, shrink, load_sem,
    ) = refs[:23]
    pack = lax.axis_index("section")
    if reduce:
        mine, partner = neighbours()
        greet(partner)
        engine = reducer(DECODER_PLAN, mine, partner, summed, refs[23:])
        put = engine.put
    else:
        put = put_into(summed)
    put_rest = put_into(rest)
    loads = fetch(
        [
            (entry_far, entry_weight),
            (attend_far, attend),
            (cotangent.at[pack], target),
            (merging_far, merging),
            (expand_far, expand),
            (shrink_far, shrink),
        ],
        load_sem,
    )
    tiles = start.shape[0] // TILE
    vectors[...] = jnp.zeros_like(vectors)
    large = sizes[pack, 0] == 1024

    def add_row(row, value):
        vectors[row : row + 1, :] += value

    loads[0].wait()
    entry = low(dot(sent[...], entry_weight[...]) + biases[0:1])
    loads[1].wait()

    blocks = start.shape[0] // BLOCK

    def slot_chip(tile, size):
        return chip_of(iota((size, 1), 0) + tile * size, sizes, pack)

    def validity(tile, size):
        return (slot_chip(tile, size) < 4).astype(F32)

    def spread_of(tile):
        return (slots[pl.ds(pack, 1)] == iota((TILE, TILE), 0) + tile * TILE).astype(F32)

    def encoding_of(tile):
        pieces = []
        for kind in range(2):
            wave = table[kind, 0, aligned(tile * 8, 8, 8)]
            big = jnp.broadcast_to(wave[:, None], (8, 32, 128)).reshape(TILE, 128)
            wave = table[kind, tile, 0:16]
            own = jnp.broadcast_to(wave[:, None], (16, 16, 128)).reshape(TILE, 128)
            pieces.append(jnp.where(large, big, own))
        for kind in range(2):
            wave = table[kind, 0]
            big = jnp.broadcast_to(wave[None], (8, 32, 128)).reshape(TILE, 128)
            wave = table[kind, tile, 0:16]
            own = jnp.broadcast_to(wave[None], (16, 16, 128)).reshape(TILE, 128)
            pieces.append(jnp.where(large, big, own))
        return jnp.concatenate(pieces, axis=1)

    @pl.loop(0, tiles)
    def _(tile):
        rows = rows_of(tile)
        valid = validity(tile, TILE)
        spread = spread_of(tile)
        fill = valid * (1.0 - jnp.sum(spread, axis=1, keepdims=True))
        hidden = dot(low(spread), entry) + fill * mask_token[...] + encoding_of(tile) * valid
        start[rows] = hidden
        add_row(12, row_sum(valid * hidden * hidden))
        add_row(16, row_sum(valid))
        unit, _ = standardize(hidden)
        norm = low(unit * gains[0:1] + shifts[0:1])
        normed[rows] = norm
        mix = dot(norm, attend[...])
        mix_low = low(mix)
        mixed[rows] = mix_low
        turned[:, rows] = low(mix[:, 256:].T)
        lane = iota((TILE, 128), 1)
        other = (lane % 64 < 5) & (lane % 64 != slot_chip(tile, TILE))
        other = jnp.where(other, NEGATIVE, 0.0).astype(BF16)
        for head in range(4):
            lanes = slice(256 + head // 2 * 128, 384 + head // 2 * 128)
            masked_keys[head, rows] = jnp.where(lane // 64 == head % 2, mix_low[:, lanes], other)

    @pl.loop(0, 2 * tiles)
    def _(step):
        pair, tile = step // tiles, step % tiles
        rows = rows_of(tile)
        lane = iota((TILE, 128), 1)
        chosen = (lane % 64 == slot_chip(tile, TILE)).astype(F32).astype(BF16)
        for half in range(2):
            query = jnp.where(lane // 64 == half, mixed[rows, pair_lanes(pair)] * BF16(0.125), chosen)
            scores = dot_nt(masked_keys[pair * 2 + half], query)
            expos = jnp.exp(scores - jnp.max(scores, axis=0, keepdims=True))
            prob = low(expos * (1.0 / jnp.sum(expos, axis=0, keepdims=True)))
            probs[pair * 2 + half, :, rows] = prob
            flipped[head_rows(pair, half), rows] = dot(turned[head_rows(pair, half, 256)], prob)

    for copy in loads[2:]:
        copy.wait()

    @pl.loop(0, blocks)
    def _(tile):
        rows = rows_of(tile, BLOCK)
        valid = validity(tile, BLOCK)
        mingled = low(flipped[:, rows].T)
        context[rows] = mingled
        attention = dot(mingled, merging[...]) + biases[1:2]
        add_row(13, row_sum(valid * attention * attention))
        unit, _ = standardize(start[rows] + attention)
        norm = low(unit * gains[1:2] + shifts[1:2])
        normed_two[rows] = norm
        go = target[rows] * valid
        go_below = low(go)
        go_low[rows] = go_below
        add_row(2, row_sum(go))
        for part in range(8):
            cols = slice(part * 256, part * 256 + 256)
            value, slope = gelu_pair(dot(norm, expand[:, cols]) + inner[:, cols])
            active[rows, cols] = low(value)
            grad = low(slope * dot_nt(go_below, shrink[cols]))
            before_grad[rows, cols] = grad
            lanes = slice(part % 2 * 256, part % 2 * 256 + 256)
            vectors[8 + part // 2 : 9 + part // 2, lanes] += row_sum(grad.astype(F32))

    if reduce:
        await_greetings()
    for part in range(2):
        cols = slice(part * 256, part * 256 + 256)
        store_packed(put, part * 16, DECODER_EXPAND, dot_tn(normed_two[:, cols], before_grad[...]))
    if reduce:
        engine.send(2048)

    @pl.loop(0, 8)
    def _(part):
        cols = aligned(part * 256, 256, 256)
        store_packed(put, part * 4, DECODER_SHRINK, dot_tn(active[:, cols], go_low[...]))

    if reduce:
        engine.send(4096)

    @pl.loop(0, tiles)
    def _(tile):
        rows = rows_of(tile)
        valid = validity(tile, TILE)
        center = start[rows] + (dot(context[rows], merging[...]) + biases[1:2])
        unit, inverse = standardize(center)
        feed = dot(active[rows], shrink[...]) + biases[2:3]
        add_row(14, row_sum(valid * feed * feed))
        output = center + feed
        add_row(15, row_sum(valid * output * output))
        norm_grad = dot_nt(before_grad[rows], expand[...])
        add_row(5, row_sum(norm_grad * unit))
        add_row(7, row_sum(norm_grad))
        grad = target[rows] * valid + norm_back(unit, inverse, gains[1:2], norm_grad)
        target[rows] = grad
        add_row(1, row_sum(grad))
        below = low(grad)
        attention_low[rows] = below
        outer = low(dot_nt(below, merging[...]))
        context_grad[rows] = outer
        product = (outer.astype(F32) * flipped[:, rows].T).T
        for head in range(4):
            delta[head, :, rows] = row_sum(product[head * 64 : head * 64 + 64])
        if reduce:
            engine.turn(tile - 1)

    for part in range(2):
        cols = slice(part * 256, part * 256 + 256)
        store_packed(put, part * 16, DECODER_MERGE, dot_tn(attention_low[:, cols], context[...]))
        shards = slice(part * 16, part * 16 + 16)
        put(shards, 4352, jnp.zeros((16, 16, DECODER_PLAN.chunks * DECODER_PLAN.span - 4352), F32))
    if reduce:
        engine.send(DECODER_PLAN.chunks * DECODER_PLAN.span)

    flipped[...] = jnp.zeros_like(flipped)

    @pl.loop(0, 2 * tiles)
    def _(step):
        pair, tile = step // tiles, step % tiles
        rows = rows_of(tile)
        lanes = pair_lanes(pair)
        values = mixed[rows, pair_lanes(pair, 512)]
        raws, probabilities, queries, outers = [], [], [], []
        for half in range(2):
            prob = probs[pair * 2 + half, rows]
            outer = only(context_grad[:, lanes], half)
            raw = low(prob.astype(F32) * (dot_nt(values, outer) - delta[pair * 2 + half]))
            flipped[head_rows(pair, half)] += dot(turned[head_rows(pair, half), rows], raw)
            raws.append(raw)
            probabilities.append(prob)
            outers.append(outer)
            queries.append(only(mixed[:, lanes], half))
        key_grad = dot(jnp.concatenate(raws, axis=1), jnp.concatenate(queries, axis=0))
        mixed_grad[rows, pair_lanes(pair, 256)] = low(key_grad * 0.125)
        value_grad = dot(jnp.concatenate(probabilities, axis=1), jnp.concatenate(outers, axis=0))
        mixed_grad[rows, pair_lanes(pair, 512)] = low(value_grad)
        if reduce:
            engine.turn(tiles - 1 + step)

    def last(tile, entry_grad):
        rows = rows_of(tile)
        mixed_grad[rows, 0:256] = low(flipped[:, rows].T * 0.125)
        norm_grad = dot_nt(mixed_grad[rows], attend[...])
        unit, inverse = standardize(start[rows])
        add_row(4, row_sum(norm_grad * unit))
        add_row(6, row_sum(norm_grad))
        grad = target[rows] + norm_back(unit, inverse, gains[0:1], norm_grad)
        spread = spread_of(tile)
        fill = validity(tile, TILE) * (1.0 - jnp.sum(spread, axis=1, keepdims=True))
        add_row(3, row_sum(fill * grad))
        if reduce:
            engine.turn(3 * tiles - 1 + tile)
        return entry_grad + dot_tn(low(spread), low(grad))

    entry_grad = lax.fori_loop(0, tiles, last, jnp.zeros((TILE, 512), F32))
    add_row(0, row_sum(entry_grad))
    entry_low = low(entry_grad)
    encoded_grad[...] = low(dot_nt(entry_low, entry_weight[...]))
    store_packed(put_rest, 0, ENTRY, dot_tn(sent[...], entry_low))

    @pl.loop(0, 2)
    def _(part):
        cols = aligned(part * 256, 256, 256)
        store_packed(put_rest, part * 16, DECODER_ATTEND, dot_tn(normed[:, cols], mixed_grad[...]))

    if reduce:
        engine.close()


def decoder_call(
    reduce, sizes, slots, table, sent, cotangent, entry_weight, biases, mask_token,
    gains, shifts, attend, merging, expand, inner, shrink,
):
    length = cotangent.shape[1]
    width = 512
    if reduce:
        summed = jax.ShapeDtypeStruct((DECODER_PLAN.chunks, 16, DECODER_PLAN.span), F32)
        extra = reducer_scratch(DECODER_PLAN)
        params = dict(collective_id=1, has_side_effects=True)
    else:
        summed = jax.ShapeDtypeStruct((DECODER_PLAN.chunks, 2, 16, 16, DECODER_PLAN.span), BF16)
        extra = []
        params = dict()
    return pl.pallas_call(
        functools.partial(decoder_kernel, reduce),
        out_shape=(
            summed,
            jax.ShapeDtypeStruct((1, 2, 16, 16, UNIT), BF16),
            jax.ShapeDtypeStruct((24, width), F32),
            jax.ShapeDtypeStruct((256, 768), BF16),
        ),
        in_specs=[smem_spec()] + [vmem_spec()] * 8 + [any_spec()] * 6,
        out_specs=(vmem_spec(),) * 4,
        scratch_shapes=[
            pltpu.VMEM((length, width), F32),
            pltpu.VMEM((length, width), BF16),
            pltpu.VMEM((length, 768), BF16),
            pltpu.VMEM((512, length), BF16),
            pltpu.VMEM((4, length, length), BF16),
            pltpu.VMEM((256, length), F32),
            pltpu.VMEM((length, 256), BF16),
            pltpu.VMEM((length, width), BF16),
            pltpu.VMEM((length, 2048), BF16),
            pltpu.VMEM((length, 2048), BF16),
            pltpu.VMEM((length, width), BF16),
            pltpu.VMEM((length, width), BF16),
            pltpu.VMEM((length, 256), BF16),
            pltpu.VMEM((4, 1, length), F32),
            pltpu.VMEM((length, 768), BF16),
            pltpu.VMEM((length, width), F32),
            pltpu.VMEM((4, length, 128), BF16),
            pltpu.VMEM(entry_weight.shape, BF16),
            pltpu.VMEM(attend.shape, BF16),
            pltpu.VMEM(merging.shape, BF16),
            pltpu.VMEM(expand.shape, BF16),
            pltpu.VMEM(shrink.shape, BF16),
            pltpu.SemaphoreType.DMA((6,)),
        ]
        + extra,
        compiler_params=pltpu.CompilerParams(vmem_limit_bytes=63 * 2**20, **params),
        name="decoder_block",
    )(
        sizes, slots, table, sent, biases, mask_token[None], gains, shifts,
        inner[None], cotangent, entry_weight, attend, merging, expand, shrink,
    )


def encoder_backward_kernel(
    reduce, encoded_grad, sums, decoder_vectors, gains, tokens, rest, attend_far, merging_far, expand_far,
    shrink_far, normed_far, mixed_far, turned_far, probs_far, context_far, middle_far, normed_two_far, active_far,
    slope_far, summed, tail_summed, vectors, tokens_grad, *refs,
):
    if reduce:
        decoder_sums, arrived = refs[:2]
        refs = refs[2:]
    (
        hidden, attend, merging, expand, shrink, normed, mixed, turned, probs, context, middle, normed_two, active,
        slope, before_grad, norm_sum, attention_low, context_grad, key_grad, query_turned, mixed_grad, active_turned,
        flipped, inner_sum, load_sem, part_sem,
    ) = refs[:26]
    pack = lax.axis_index("section")

    def part_loads(part):
        cols = aligned(part * 1024, 1024, 1024)
        slot = part % 2
        return [
            pltpu.make_async_copy(expand_far.at[:, cols], expand.at[slot], part_sem.at[slot, 0]),
            pltpu.make_async_copy(shrink_far.at[cols], shrink.at[slot], part_sem.at[slot, 1]),
            pltpu.make_async_copy(slope_far.at[part], slope.at[slot], part_sem.at[slot, 2]),
        ]

    if reduce:
        (
            decoder_total, encoder_total, decoder_got, encoder_got, payload,
            own_sem, small_send, small_recv, pay_send, pay_recv, small_load,
        ) = refs[26:37]
        mine, partner = neighbours()
        greet(partner)
        engine = reducer(ENCODER_PLAN, mine, partner, summed, refs[37:68])
        tail = reducer(TAIL_PLAN, mine, partner, tail_summed, refs[68:])
        put_tail = tail.put
        first_own = fetch(
            [
                pair
                for pair in (
                    (rest.at[0, 1 - mine["c"]], engine.staging.at[0]),
                    (rest.at[0, mine["c"]], engine.own.at[0]),
                )
            ],
            own_sem,
        )
        decoder_load = pltpu.make_async_copy(decoder_vectors, decoder_total.at[0], small_load)
        decoder_load.start()
    else:
        put_tail = put_into(tail_summed)
    early = pltpu.make_async_copy(active_far, active, load_sem.at[10])
    early.start()
    for copy in part_loads(0):
        copy.start()
    if reduce:
        for copy in first_own:
            copy.wait()
        await_greetings()
        engine.first_copy(0).start()
    loads = fetch(
        [
            (normed_two_far, normed_two),
            (middle_far, middle),
            (merging_far, merging),
            (context_far, context),
            (mixed_far, mixed),
            (probs_far, probs),
            (turned_far.at[0:768], turned),
            (normed_far, normed),
            (attend_far, attend),
            (tokens.at[pack], hidden),
        ],
        load_sem,
    )
    for copy in part_loads(1):
        copy.start()
    vectors[...] = sums[...]
    go_low = encoded_grad[...]
    go = go_low.astype(F32)
    vectors[1:2, :768] = row_sum(go)
    norm_sum[...] = jnp.zeros_like(norm_sum)

    def unit_grad(unit, place, pieces):
        put = engine.put_unit(unit) if reduce else put_unit_into(summed, unit)
        for first, value in pieces:
            store_packed(put, first, (0,) + place[1:], value)
        if reduce:
            engine.first_copy(unit).start()

    def shrink_start():
        early.wait()
        for piece in range(4):
            rows = slice(piece * 768, piece * 768 + 768)
            active_turned[rows] = active[:, rows].T

    def shrink_grad(part):
        cols = aligned(part * 256, 256, 256)
        pieces = []
        for piece in range(4):
            rows = slice(piece * 768, piece * 768 + 768)
            pieces.append((piece * 8, dot(active_turned[rows], encoded_grad[:, cols])))
        unit_grad(1 + part, ENCODER_SHRINK[0], pieces)

    def hidden_layer(part):
        for copy in part_loads(part):
            copy.wait()
        slot = part % 2
        grad = low(slope[slot] * dot_nt(encoded_grad[...], shrink[slot]))
        before_grad[...] = grad
        inner_sum[part] = row_sum(grad.astype(F32))
        norm_sum[...] += dot_nt(grad, expand[slot])

        @pl.when(part == 0)
        def _():
            for copy in part_loads(2):
                copy.start()

    def expand_grad(part):
        @pl.when(part == 0)
        def _():
            loads[0].wait()
            flipped[...] = normed_two[...].T

        unit_grad(4 + part, ENCODER_EXPAND[0], [(0, dot(flipped[...], before_grad[...]))])

    def middle_layer():
        loads[1].wait()
        loads[2].wait()
        for part in range(3):
            vectors[6 + part : 7 + part] = inner_sum[part]
        unit, inverse = standardize(middle[...])
        norm_grad = norm_sum[...]
        vectors[3:4, :768] = row_sum(norm_grad * unit)
        vectors[5:6, :768] = row_sum(norm_grad)
        grad = encoded_grad[...].astype(F32) + norm_back(unit, inverse, gains[1:2], norm_grad)
        vectors[0:1, :768] = row_sum(grad)
        tokens_grad[...] = grad
        below = low(grad)
        attention_low[...] = below
        context_grad[...] = low(dot_nt(below, merging[...]))
        for copy in loads[3:7]:
            copy.wait()

    def attention(first):
        @pl.loop(first, first + 2)
        def _(pair):
            lanes = pair_lanes(pair)
            values = mixed[:, pair_lanes(pair, 1536)]
            keys_total = jnp.zeros((TILE, 128), F32)
            values_total = jnp.zeros((TILE, 128), F32)
            for half in range(2):
                prob = probs[pair * 2 + half]
                outer = only(context_grad[:, lanes], half)
                query = only(mixed[:, lanes], half)
                wide = prob.astype(F32)
                grad = dot_nt(values, outer)
                raw = low(wide * (grad - jnp.sum(wide * grad, axis=0, keepdims=True)))
                keys_total = keys_total + dot(raw, query)
                values_total = values_total + dot(prob, outer)
                rows = head_rows(pair, half)
                query_turned[rows] = dot(turned[rows], raw)
            key_grad[0, :, lanes] = keys_total
            key_grad[1, :, lanes] = values_total

    def mixing():
        mixed_grad[:, 0:768] = low(query_turned[...].T * 0.125)
        mixed_grad[:, 768:1536] = low(key_grad[0] * 0.125)
        mixed_grad[:, 1536:2304] = low(key_grad[1])

    def attend_grad(part):
        @pl.when(part == 0)
        def _():
            loads[7].wait()
            flipped[...] = normed[...].T

        wide = aligned(part * 1024, 1024, 1024)
        unit_grad(7 + part, ENCODER_ATTEND[0], [(0, dot(flipped[...], mixed_grad[:, wide]))])

    def tail_grad():
        store_packed(put_tail, 0, ENCODER_ATTEND[2], dot(flipped[...], mixed_grad[:, 2048:2304]))
        store_packed(put_tail, 0, ENCODER_MERGE, dot_tn(attention_low[...], context[...]))
        if reduce:
            tail.send(UNIT)

    def input_layer():
        loads[8].wait()
        loads[9].wait()
        norm_grad = dot_nt(mixed_grad[...], attend[...])
        unit, inverse = standardize(hidden[...])
        vectors[2:3, :768] = row_sum(norm_grad * unit)
        vectors[4:5, :768] = row_sum(norm_grad)
        grad = tokens_grad[...] + norm_back(unit, inverse, gains[0:1], norm_grad)
        tokens_grad[...] = grad
        if reduce:
            payload[...] = low(grad)

    if not reduce:
        shrink_start()
        for part in range(3):
            shrink_grad(part)
        for part in range(3):
            hidden_layer(part)
            expand_grad(part)
        middle_layer()
        for first in (0, 2, 4):
            attention(first)
        mixing()
        for part in range(2):
            attend_grad(part)
        tail_grad()
        input_layer()
        return

    def exchange(source, piece):
        rows = aligned(piece * 32, 32, 32)
        return remote(source.at[rows], arrived.at[rows], pay_send.at[piece], pay_recv.at[piece], partner["x"])

    small_route = ("c",) + ROUTES[0]
    totals = ((decoder_total, decoder_got), (encoder_total, encoder_got))

    def small_copy(stage, kind):
        source, target = totals[kind]
        return remote(
            source.at[stage],
            target.at[stage],
            small_send.at[stage, kind],
            small_recv.at[stage, kind],
            partner[small_route[stage]],
        )

    def small_advance(stage):
        if stage == 0:
            encoder_total[0] = vectors[...]
        for kind in range(2):
            source, target = totals[kind]
            if stage > 0:
                small_copy(stage - 1, kind).wait_recv()
                source[stage] = source[stage - 1] + target[stage - 1]
            if stage < 5:
                small_copy(stage, kind).start()

    shrink_start()
    shrink_grad(0)
    decoder_load.wait()

    def attention_all():
        @pl.loop(0, 3)
        def _(step):
            attention(2 * step)

        mixing()

    def ending():
        tail_grad()
        input_layer()

    part = functools.partial
    works = {4: middle_layer, 5: attention_all, 7: ending}
    turns = ENCODER_PLAN.chunks + TAIL_PLAN.chunks + 4 * LAG
    works.update({8 + stage + max(0, stage - 1): part(small_advance, stage) for stage in range(6)})

    @pl.loop(0, turns)
    def _(number):
        engine.turn(number)
        tail.turn(number - ENCODER_PLAN.chunks)

        @pl.when(number <= 1)
        def _():
            shrink_grad(number + 1)

        @pl.when((number >= 2) & (number <= 4))
        def _():
            expand_grad(number - 2)

        @pl.when((number >= 1) & (number <= 3))
        def _():
            hidden_layer(number - 1)

        for position, work in works.items():
            pl.when(number == position)(work)

        @pl.when(number == 6)
        def _():
            @pl.loop(0, 2)
            def _(part):
                attend_grad(part)

        @pl.when((pack == 0) & (number < 8))
        def _():
            exchange(encoded_grad, number).start()

        @pl.when((pack == 1) & (number >= 8) & (number < 16))
        def _():
            exchange(payload, number - 8).start()

    for stage in range(5):
        for kind in range(2):
            small_copy(stage, kind).wait_send()
    for piece in range(8):
        exchange(payload, piece).wait()
    engine.close()
    tail.close()
    vectors[...] = encoder_total[5]
    decoder_sums[...] = decoder_total[5]


def encoder_backward_call(reduce, tokens, encoded_grad, sums, decoder_vectors, rest, kept, gains, attend, merging, expand, shrink):
    if reduce:
        summed = tuple(
            jax.ShapeDtypeStruct((plan.chunks, 16, plan.span), F32) for plan in (ENCODER_PLAN, TAIL_PLAN)
        )
        more = (
            jax.ShapeDtypeStruct(decoder_vectors.shape, F32),
            jax.ShapeDtypeStruct((256, 768), BF16),
        )
        more_specs = (vmem_spec(), any_spec())
        extra = [
            pltpu.VMEM((6,) + decoder_vectors.shape, F32),
            pltpu.VMEM((6,) + sums.shape, F32),
            pltpu.VMEM((5,) + decoder_vectors.shape, F32),
            pltpu.VMEM((5,) + sums.shape, F32),
            pltpu.VMEM((256, 768), BF16),
            pltpu.SemaphoreType.DMA((2,)),
            pltpu.SemaphoreType.DMA((5, 2)),
            pltpu.SemaphoreType.DMA((5, 2)),
            pltpu.SemaphoreType.DMA((8,)),
            pltpu.SemaphoreType.DMA((8,)),
            pltpu.SemaphoreType.DMA,
        ] + reducer_scratch(ENCODER_PLAN) + reducer_scratch(TAIL_PLAN)
        params = dict(collective_id=2, has_side_effects=True)
    else:
        summed = tuple(
            jax.ShapeDtypeStruct((plan.chunks, 2, 16, 16, plan.span), BF16) for plan in (ENCODER_PLAN, TAIL_PLAN)
        )
        more, more_specs, extra, params = (), (), [], dict()
    return pl.pallas_call(
        functools.partial(encoder_backward_kernel, reduce),
        out_shape=summed
        + (
            jax.ShapeDtypeStruct(sums.shape, F32),
            jax.ShapeDtypeStruct((256, 768), F32),
        )
        + more,
        in_specs=[vmem_spec()] * 2 + [any_spec(), vmem_spec()] + [any_spec()] * 15,
        out_specs=(vmem_spec(),) * 4 + more_specs,
        scratch_shapes=[
            pltpu.VMEM((256, 768), F32),
            pltpu.VMEM(attend.shape, BF16),
            pltpu.VMEM(merging.shape, BF16),
            pltpu.VMEM((2, 768, 1024), BF16),
            pltpu.VMEM((2, 1024, 768), BF16),
            pltpu.VMEM((256, 768), BF16),
            pltpu.VMEM((256, 2304), BF16),
            pltpu.VMEM((768, 256), BF16),
            pltpu.VMEM((12, 256, 256), BF16),
            pltpu.VMEM((256, 768), BF16),
            pltpu.VMEM((256, 768), F32),
            pltpu.VMEM((256, 768), BF16),
            pltpu.VMEM((256, 3072), BF16),
            pltpu.VMEM((2, 256, 1024), F32),
            pltpu.VMEM((256, 1024), BF16),
            pltpu.VMEM((256, 768), F32),
            pltpu.VMEM((256, 768), BF16),
            pltpu.VMEM((256, 768), BF16),
            pltpu.VMEM((2, 256, 768), F32),
            pltpu.VMEM((768, 256), F32),
            pltpu.VMEM((256, 2304), BF16),
            pltpu.VMEM((3072, 256), BF16),
            pltpu.VMEM((768, 256), BF16),
            pltpu.VMEM((3, 1, 1024), F32),
            pltpu.SemaphoreType.DMA((11,)),
            pltpu.SemaphoreType.DMA((2, 3)),
        ]
        + extra,
        compiler_params=pltpu.CompilerParams(vmem_limit_bytes=62 * 2**20, **params),
        name="encoder_backward",
    )(encoded_grad, sums, decoder_vectors, gains, tokens, rest, attend, merging, expand, shrink, *kept)


def unpack(packed, place):
    span = packed.shape[-1]

    def take(start, size):
        pieces = []
        while size:
            chunk, first = divmod(start, span)
            length = min(size, span - first)
            pieces.append(packed[chunk, ..., first : first + length])
            start, size = start + length, size - length
        return pieces[0] if len(pieces) == 1 else jnp.concatenate(pieces, axis=-1)

    offset, count, width = place
    pieces = [take(offset + i * width, width) for i in range(count // 16)]
    if count % 16:
        rest = take(offset + count // 16 * width, width // 2)
        pieces.append(jnp.concatenate([rest[..., :8, :], rest[..., 8:, :]], axis=-1))
    return pieces[0] if len(pieces) == 1 else jnp.concatenate(pieces, axis=-2)


def finish_kernel(
    decoder_summed_far, decoder_sums_far, encoder_sums_far, summed_far, tail_far, arrived_far, tokens_grad_far, encoded_grad_far,
    boundary, statistics, e_gains, e_shifts, e_biases, e_attend, e_merge, e_expand, e_inner, e_shrink,
    d_entry, d_biases, mask_grad, d_gains, d_shifts, d_attend, d_merge, d_expand, d_inner, d_shrink,
    decoder_summed, decoder_sums, encoder_sums, summed, tail, arrived, tokens_grad, encoded_grad, load_sem,
):
    section = lax.axis_index("section")
    loads = fetch(
        [
            (decoder_summed_far, decoder_summed),
            (decoder_sums_far, decoder_sums),
            (encoder_sums_far, encoder_sums),
            (summed_far, summed),
            (tail_far, tail),
            (arrived_far, arrived),
            (tokens_grad_far, tokens_grad),
            (encoded_grad_far, encoded_grad),
        ],
        load_sem,
    )
    number = section * lax.axis_size("dp") + lax.axis_index("dp")

    def own(rows, count):
        width = rows.shape[1]
        return pltpu.roll(rows, (width - number * count) % width, axis=1)[:, :count]

    def own_line(rows, count):
        return own(jnp.concatenate([rows[i : i + 1] for i in range(rows.shape[0])], axis=1), count)

    for copy in loads[:3]:
        copy.wait()
    lane = iota((1, 128), 1)
    values = jnp.zeros((1, 128), F32)
    for sums, width, first, count_row, base in ((encoder_sums, DE, 10, 14, 0), (decoder_sums, DD, 12, 16, 4)):
        scale = 1.0 / (sums[count_row : count_row + 1, 0:1] * width)
        for i in range(4):
            value = jnp.sum(sums[first + i : first + i + 1, :], axis=1, keepdims=True) * scale
            values = jnp.where(lane == base + i, value, values)
    statistics[...] = jnp.sqrt(values)[:, :8]
    rows = own(encoder_sums[0:8, :DE], 24)
    e_biases[...] = rows[0:2]
    e_gains[...] = rows[2:4]
    e_shifts[...] = rows[4:6]
    e_inner[...] = own_line(encoder_sums[6:9], 96)
    rows = own(decoder_sums[0:8], 16)
    d_biases[...] = rows[0:3]
    mask_grad[...] = rows[3:4]
    d_gains[...] = rows[4:6]
    d_shifts[...] = rows[6:8]
    d_inner[...] = own_line(decoder_sums[8:12], 64)

    d_merge[...] = unpack(decoder_summed, DECODER_MERGE)
    d_expand[...] = unpack(decoder_summed, DECODER_EXPAND)
    d_shrink[...] = unpack(decoder_summed, DECODER_SHRINK)
    loads[3].wait()
    loads[4].wait()
    d_entry[...] = unpack(summed, ENTRY)
    d_attend[...] = unpack(summed, DECODER_ATTEND)
    for target, places in ((e_expand, ENCODER_EXPAND), (e_attend, ENCODER_ATTEND), (e_shrink, ENCODER_SHRINK)):
        start = 0
        for place in places:
            source = tail if place is ENCODER_ATTEND[2] else summed
            target[:, start : start + place[2]] = unpack(source, place)
            start += place[2]
    e_merge[...] = unpack(tail, ENCODER_MERGE)
    for copy in loads[5:]:
        copy.wait()

    @pl.when(section == 0)
    def _():
        boundary[0, 0] = tokens_grad[...]
        boundary[0, 1] = arrived[...].astype(F32)

    @pl.when(section == 1)
    def _():
        boundary[0, 0] = arrived[...].astype(F32)
        boundary[0, 1] = encoded_grad[...].astype(F32)


def finish_call(*operands):
    shapes = (
        (1, 2, 256, 768), (1, 8), (2, 24), (2, 24), (2, 24), (24, 2304), (24, 768), (24, 3072), (1, 96), (96, 768),
        (24, 512), (3, 16), (1, 16), (2, 16), (2, 16), (16, 768), (16, 256), (16, 2048), (1, 64), (64, 512),
    )
    outs = list(
        pl.pallas_call(
            finish_kernel,
            out_shape=tuple(jax.ShapeDtypeStruct(shape, F32) for shape in shapes),
            in_specs=[any_spec()] * len(operands),
            out_specs=(vmem_spec(),) * len(shapes),
            scratch_shapes=[pltpu.VMEM(operand.shape, operand.dtype) for operand in operands]
            + [pltpu.SemaphoreType.DMA((len(operands),))],
            compiler_params=pltpu.CompilerParams(vmem_limit_bytes=60 * 2**20),
            name="finish",
        )(*operands)
    )
    for line in (1, 8, 12, 18):
        outs[line] = outs[line].reshape(-1)
    for turned in (6, 16):
        outs[turned] = outs[turned].T
    return tuple(outs)


def scatter_sum(member, share_dim):
    return lax.psum_scatter(
        member, ("section", "dp"), scatter_dimension=share_dim, tiled=True
    )


def finish_generic(decoder_part, part, tail, decoder_sums, encoder_sums, tokens_grad, encoded_grad):
    section = lax.axis_index("section")
    payload = jnp.where(section == 0, encoded_grad, low(tokens_grad))

    def whole(packed, *places):
        packed = jnp.swapaxes(packed, 1, 2).reshape(-1, 32, 16, packed.shape[-1])
        blocks = [unpack(packed, place).reshape(32 * place[1], place[2]) for place in places]
        return scatter_sum(jnp.concatenate(blocks, axis=1).astype(F32), 0)

    def line(value):
        return scatter_sum(value, value.ndim - 1)

    arrived = lax.ppermute(payload, "section", [(0, 1), (1, 0)]).astype(F32)
    boundary = jnp.where(
        section == 0,
        jnp.stack([tokens_grad, arrived]),
        jnp.stack([arrived, encoded_grad.astype(F32)]),
    )
    sums = jnp.concatenate(
        [jnp.sum(encoder_sums[10:14], axis=1), jnp.sum(decoder_sums[12:16], axis=1)]
    )
    sums, counts = lax.psum((sums, (encoder_sums[14, 0], decoder_sums[16, 0])), ("section", "dp"))
    scales = jnp.concatenate([jnp.full((4,), counts[0] * DE), jnp.full((4,), counts[1] * DD)])
    return (
        boundary[None],
        jnp.sqrt(sums / scales),
        line(encoder_sums[2:4, :DE]),
        line(encoder_sums[4:6, :DE]),
        line(encoder_sums[0:2, :DE]),
        jnp.concatenate([whole(part, *ENCODER_ATTEND[:2]), whole(tail, ENCODER_ATTEND[2])], axis=1),
        whole(tail, ENCODER_MERGE).T,
        whole(part, *ENCODER_EXPAND),
        line(encoder_sums[6:9].reshape(-1)),
        whole(part, *ENCODER_SHRINK),
        whole(decoder_part[1], ENTRY),
        line(decoder_sums[0:3]),
        line(decoder_sums[3]),
        line(decoder_sums[4:6]),
        line(decoder_sums[6:8]),
        whole(decoder_part[1], DECODER_ATTEND),
        whole(decoder_part[0], DECODER_MERGE).T,
        whole(decoder_part[0], DECODER_EXPAND),
        line(decoder_sums[8:12].reshape(-1)),
        whole(decoder_part[0], DECODER_SHRINK),
    )


def body(
    visible_tokens,
    cotangent,
    chip_sizes,
    ground_distance,
    visible_slots,
    encoder_gains,
    encoder_shifts,
    encoder_biases,
    encoder_attend,
    encoder_merge,
    encoder_expand,
    encoder_inner,
    encoder_shrink,
    decoder_entry,
    decoder_biases,
    mask_token,
    decoder_gains,
    decoder_shifts,
    decoder_attend,
    decoder_merge,
    decoder_widen_weight,
    decoder_inner,
    decoder_shrink,
):
    reduce = (lax.axis_size("section"), lax.axis_size("dp")) == (2, 16)
    sent, sums, table, *kept = encoder_forward_call(
        chip_sizes, ground_distance, visible_tokens, encoder_gains, encoder_shifts, encoder_biases,
        encoder_attend, encoder_merge, encoder_expand, encoder_inner, encoder_shrink,
    )
    decoder_summed, rest, decoder_vectors, encoded_grad = decoder_call(
        reduce, chip_sizes, visible_slots, table, sent, cotangent, decoder_entry, decoder_biases, mask_token,
        decoder_gains, decoder_shifts, decoder_attend, decoder_merge, decoder_widen_weight, decoder_inner,
        decoder_shrink,
    )
    summed, tail, encoder_sums, tokens_grad, *more = encoder_backward_call(
        reduce, visible_tokens, encoded_grad, sums, decoder_vectors, rest, kept,
        encoder_gains, encoder_attend, encoder_merge, encoder_expand, encoder_shrink,
    )
    if reduce:
        decoder_sums, arrived = more
        return finish_call(
            decoder_summed, decoder_sums, encoder_sums, summed, tail, arrived, tokens_grad, encoded_grad
        )
    return finish_generic(
        (decoder_summed, rest), summed, tail, decoder_vectors, encoder_sums, tokens_grad, encoded_grad
    )


def solution(mesh):
    in_specs = (
        P("dp", None, None),
        P("dp", None, None),
        P("dp", None),
        P("dp", None),
        P("dp", None),
        P(),
        P(),
        P(),
        P(),
        P(),
        P(),
        P(),
        P(),
        P(),
        P(),
        P(),
        P(),
        P(),
        P(),
        P(),
        P(),
        P(),
        P(),
    )
    out_specs = (
        P("section", "dp", None, None),
        P(),
        P(None, ("section", "dp")),
        P(None, ("section", "dp")),
        P(None, ("section", "dp")),
        P(("section", "dp"), None),
        P(None, ("section", "dp")),
        P(("section", "dp"), None),
        P(("section", "dp")),
        P(("section", "dp"), None),
        P(("section", "dp"), None),
        P(None, ("section", "dp")),
        P(("section", "dp")),
        P(None, ("section", "dp")),
        P(None, ("section", "dp")),
        P(("section", "dp"), None),
        P(None, ("section", "dp")),
        P(("section", "dp"), None),
        P(("section", "dp")),
        P(("section", "dp"), None),
    )
    return jax.shard_map(body, mesh=mesh, in_specs=in_specs, out_specs=out_specs, check_vma=False)
```

```python
import functools
import types

import jax
import jax.numpy as jnp
import numpy as np
from jax import lax
from jax.experimental import pallas as pl
from jax.experimental.pallas import tpu as pltpu
from jax.sharding import PartitionSpec as P

DE = 768
DD = 512
TILE = 256
BLOCK = 512
NEGATIVE = -1e30
F32, BF16 = jnp.float32, jnp.bfloat16
MESH_ID = pl.DeviceIdType.MESH

CANON = ("x", "z2", "z1", "y")
ROUTES = (("x", "y", "z1", "z2"), ("y", "x", "z1", "z2"), ("z1", "z2", "x", "y"))
UNIT = 1536
LAG = 2
DECODER_PLAN = types.SimpleNamespace(widths=(2, 2, 1), chunks=7, slots=7, ring=3, span=640)
ENCODER_PLAN = types.SimpleNamespace(widths=(3, 6, 3), chunks=9, slots=3, ring=3, span=1536)
TAIL_PLAN = types.SimpleNamespace(widths=(2, 3, 1), chunks=2, slots=2, ring=2, span=768)

DECODER_EXPAND, DECODER_SHRINK, DECODER_MERGE = (0, 16, 2048), (2048, 64, 512), (4096, 16, 256)
ENTRY, DECODER_ATTEND = (0, 24, 512), (768, 16, 768)
ENCODER_SHRINK = tuple((UNIT * (1 + part), 96, 256) for part in range(3))
ENCODER_EXPAND = tuple((UNIT * (4 + part), 24, 1024) for part in range(3))
ENCODER_ATTEND = ((UNIT * 7, 24, 1024), (UNIT * 8, 24, 1024), (0, 24, 256))
ENCODER_MERGE = (384, 24, 768)


def dot(a, b):
    return jnp.dot(a, b, preferred_element_type=F32)


def dot_nt(a, b):
    return lax.dot_general(a, b, (((1,), (1,)), ((), ())), preferred_element_type=F32)


def dot_tn(a, b):
    return lax.dot_general(a, b, (((0,), (0,)), ((), ())), preferred_element_type=F32)


def low(value):
    return value.astype(BF16)


def standardize(values):
    centered = values - jnp.mean(values, axis=-1, keepdims=True)
    inverse = lax.rsqrt(jnp.mean(centered * centered, axis=-1, keepdims=True) + 1e-05)
    return centered * inverse, inverse


def norm_back(unit, inverse, gain, grad):
    inner = grad * gain
    return inverse * (
        inner
        - jnp.mean(inner, axis=-1, keepdims=True)
        - unit * jnp.mean(inner * unit, axis=-1, keepdims=True)
    )


def row_sum(values):
    return jnp.sum(values, axis=0, keepdims=True)


def gelu_pair(before):
    half = 0.5 * (1.0 + lax.erf(before * 0.7071067811865476))
    density = jnp.exp(-0.5 * before * before) * 0.3989422804014327
    return before * half, half + before * density


def chip_of(places, sizes, pack):
    end = sizes[pack, 0]
    chip = (places >= end).astype(jnp.int32)
    for slot in range(1, 4):
        end = end + sizes[pack, slot]
        chip = chip + (places >= end).astype(jnp.int32)
    return chip


def iota(shape, dimension):
    return lax.broadcasted_iota(jnp.int32, shape, dimension)


def aligned(start, size, unit):
    if isinstance(start, int):
        return slice(start, start + size)
    return pl.ds(pl.multiple_of(start, unit), size)


def pair_lanes(pair, base=0):
    return aligned(base + pair * 128, 128, 128)


def head_rows(pair, half, base=0):
    return aligned(base + pair * 128 + half * 64, 64, 64)


def rows_of(tile, size=TILE):
    return aligned(tile * size, size, size)


def only(values, half):
    return jnp.where(iota((1, 128), 1) // 64 == half, values, jnp.zeros_like(values))


def fetch(pairs, sems):
    copies = [
        pltpu.make_async_copy(source, target, sems.at[i]) for i, (source, target) in enumerate(pairs)
    ]
    for copy in copies:
        copy.start()
    return copies


def store_packed(put, first, place, value):
    offset, count, width = place
    value = value.reshape(-1, count, width)
    shards = slice(first, first + value.shape[0]) if isinstance(first, int) else pl.ds(first, value.shape[0])
    for piece in range(count // 16):
        put(shards, offset + piece * width, value[:, piece * 16 : piece * 16 + 16])
    if count % 16:
        half = width // 2
        rest = value[:, count - 8 :]
        rest = jnp.concatenate([rest[:, :, :half], rest[:, :, half:]], axis=1)
        put(shards, offset + count // 16 * width, rest)


def halves(shards, value):
    pairs = value.reshape(value.shape[0] // 2, 2, *value.shape[1:])
    if isinstance(shards, slice):
        return slice(shards.start // 2, shards.stop // 2), pairs[:, 0], pairs[:, 1]
    return pl.ds(shards.start // 2, shards.size // 2), pairs[:, 0], pairs[:, 1]


def place_of(names, bits):
    index = 0
    for name in names:
        index = index * 2 + bits[name]
    return index


def left_after(route, stage):
    return tuple(name for name in CANON if name not in route[:stage])


def choices(names):
    for number in range(2 ** len(names)):
        yield {name: (number >> (len(names) - 1 - i)) & 1 for i, name in enumerate(names)}


def neighbours():
    section = lax.axis_index("section")
    data = lax.axis_index("dp")
    mine = {"x": section, "c": data % 2, "y": data // 2 % 2, "z1": data // 4 % 2, "z2": data // 8 % 2}
    partner = {"x": (1 - section, data)}
    for name, step in {"c": 1, "y": 2, "z1": 4, "z2": 8}.items():
        partner[name] = (section, data + step * (1 - 2 * mine[name]))
    return mine, partner


def greet(partner):
    barrier = pltpu.get_barrier_semaphore()
    for name in ("c",) + CANON:
        pl.semaphore_signal(barrier, inc=1, device_id=partner[name], device_id_type=MESH_ID)


def await_greetings():
    pl.semaphore_wait(pltpu.get_barrier_semaphore(), 5)


def remote(source, target, send, recv, device):
    return pltpu.make_async_remote_copy(
        src_ref=source,
        dst_ref=target,
        send_sem=send,
        recv_sem=recv,
        device_id=device,
        device_id_type=MESH_ID,
    )


def reducer(plan, mine, partner, out, refs):
    chunks, slots, span, ring = plan.chunks, plan.slots, plan.span, plan.ring
    progress = types.SimpleNamespace(sent=0)
    own, staging, first = refs[:3]
    sent, got = refs[3:15], refs[15:27]
    first_send, first_recv, send_sem, recv_sem = refs[27:31]

    def first_copy(chunk):
        return remote(staging.at[chunk % slots], first.at[chunk], first_send.at[chunk], first_recv.at[chunk], partner["c"])

    def stage_copy(route, stage, chunk):
        return remote(
            sent[route * 4 + stage].at[chunk % ring],
            got[route * 4 + stage].at[chunk],
            send_sem.at[route, stage, chunk],
            recv_sem.at[route, stage, chunk],
            partner[ROUTES[route][stage]],
        )

    def total(route, stage, chunk, bits):
        spot = place_of(CANON, bits)
        cols = slice(sum(plan.widths[:route]) * 128, sum(plan.widths[: route + 1]) * 128)
        value = own[chunk, spot, :, cols].astype(F32) + first[chunk, spot, :, cols].astype(F32)
        for earlier in range(stage):
            names = left_after(ROUTES[route], earlier + 1)
            value = value + got[route * 4 + earlier][chunk, place_of(names, bits)].astype(F32)
        return value

    def advance(stage, chunk):
        for route in range(3):
            if stage:
                stage_copy(route, stage - 1, chunk).wait_recv()
            else:
                first_copy(chunk).wait_recv() if route == 0 else None
            if stage < 4:

                @pl.when(chunk >= ring)
                def _(route=route):
                    stage_copy(route, stage, chunk - ring).wait_send()

        values = []
        for route in range(3):
            path = ROUTES[route]
            if stage == 4:
                values.append(total(route, 4, chunk, mine))
                continue
            names = left_after(path, stage + 1)
            for free in choices(names):
                bits = dict(mine)
                bits[path[stage]] = 1 - mine[path[stage]]
                bits.update(free)
                values.append((route, place_of(names, free), low(total(route, stage, chunk, bits))))
        if stage == 4:
            out[chunk] = jnp.concatenate(values, axis=1)
            return
        for route, spot, value in values:
            sent[route * 4 + stage][chunk % ring, spot] = value
        for route in range(3):
            stage_copy(route, stage, chunk).start()

    def turn(number):
        for stage in range(4, -1, -1):
            chunk = number - LAG * stage
            pl.when((chunk >= 0) & (chunk < chunks))(functools.partial(advance, stage, chunk))

    def put(shards, column, value):
        shards, even, odd = halves(shards, value)
        kept = low(jnp.where(mine["c"] == 0, even, odd))
        given = low(jnp.where(mine["c"] == 0, odd, even))
        width = value.shape[2]
        done = 0
        while done < width:
            chunk, start = divmod(column + done, span)
            size = min(width - done, span - start)
            own[chunk, shards, :, start : start + size] = kept[:, :, done : done + size]
            staging[chunk % slots, shards, :, start : start + size] = given[:, :, done : done + size]
            done += size

    def put_unit(unit):
        def put(shards, column, value):
            shards, even, odd = halves(shards, value)
            cols = slice(column, column + value.shape[2])
            own[unit, shards, :, cols] = low(jnp.where(mine["c"] == 0, even, odd))
            staging[unit % slots, shards, :, cols] = low(jnp.where(mine["c"] == 0, odd, even))

        @pl.when(unit >= slots)
        def _():
            first_copy(unit - slots).wait_send()

        return put

    def send(column):
        while (progress.sent + 1) * span <= column:
            first_copy(progress.sent).start()
            progress.sent += 1

    def close():
        for chunk in range(max(0, chunks - slots), chunks):
            first_copy(chunk).wait_send()
        for chunk in range(chunks - ring, chunks):
            for route in range(3):
                for stage in range(4):
                    stage_copy(route, stage, chunk).wait_send()

    return types.SimpleNamespace(
        own=own, staging=staging, turn=turn, put=put, put_unit=put_unit, first_copy=first_copy, send=send, close=close
    )


def reducer_scratch(plan):
    stages = [(width, block) for width in plan.widths for block in (8, 4, 2, 1)]
    return (
        [
            pltpu.VMEM((plan.chunks, 16, 16, plan.span), BF16),
            pltpu.VMEM((plan.slots, 16, 16, plan.span), BF16),
            pltpu.VMEM((plan.chunks, 16, 16, plan.span), BF16),
        ]
        + [pltpu.VMEM((plan.ring, block, 16, width * 128), BF16) for width, block in stages]
        + [pltpu.VMEM((plan.chunks, block, 16, width * 128), BF16) for width, block in stages]
        + [
            pltpu.SemaphoreType.DMA((plan.chunks,)),
            pltpu.SemaphoreType.DMA((plan.chunks,)),
            pltpu.SemaphoreType.DMA((3, 4, plan.chunks)),
            pltpu.SemaphoreType.DMA((3, 4, plan.chunks)),
        ]
    )


def put_into(parts):
    span = parts.shape[-1]

    def put(shards, column, value):
        shards, *pair = halves(shards, value)
        width = value.shape[2]
        done = 0
        while done < width:
            chunk, start = divmod(column + done, span)
            size = min(width - done, span - start)
            for core in range(2):
                parts[chunk, core, shards, :, start : start + size] = low(pair[core][:, :, done : done + size])
            done += size

    return put


def put_unit_into(parts, unit):
    def put(shards, column, value):
        shards, *pair = halves(shards, value)
        for core in range(2):
            parts[unit, core, shards, :, column : column + value.shape[2]] = low(pair[core])

    return put


def vmem_spec():
    return pl.BlockSpec(memory_space=pltpu.VMEM)


def any_spec():
    return pl.BlockSpec(memory_space=pl.ANY)


def smem_spec():
    return pl.BlockSpec(memory_space=pltpu.SMEM)


def encoder_forward_kernel(
    sizes, distance, frequency, gains, shifts, biases, inner, tokens, attend_far, merging_far, expand_far,
    shrink_far, sent, vectors, table, *refs,
):
    far = refs[:9]
    normed, mixed, turned, probs, context, middle, normed_two, active, slope = refs[9:18]
    hidden, attend, merging, expand, shrink, context_turned, load_sem, save_sem = refs[18:]
    pack = lax.axis_index("section")
    loads = fetch(
        [
            (tokens.at[pack], hidden),
            *[(attend_far.at[:, i * 768 : i * 768 + 768], attend.at[:, i * 768 : i * 768 + 768]) for i in range(3)],
            (merging_far, merging),
            *[(expand_far.at[:, i * 1024 : i * 1024 + 1024], expand.at[:, i * 1024 : i * 1024 + 1024]) for i in range(3)],
            *[(shrink_far.at[i * 1024 : i * 1024 + 1024], shrink.at[i * 1024 : i * 1024 + 1024]) for i in range(3)],
        ],
        load_sem,
    )
    saves = []

    def save(*numbers):
        for number in numbers:
            copy = pltpu.make_async_copy(refs[9 + number], far[number], save_sem.at[number])
            copy.start()
            saves.append(copy)

    vectors[...] = jnp.zeros_like(vectors)
    positions = iota((32, 128), 0).astype(F32)
    for chip in range(4):
        spacing = distance[pack, chip].astype(F32) / 16.0
        angle = positions * (spacing * frequency[...])
        table[0, chip] = jnp.sin(angle)
        table[1, chip] = jnp.cos(angle)
    key_chip = chip_of(4 * iota((TILE, 1), 0), sizes, pack)
    own_chip = chip_of(4 * iota((1, TILE), 1), sizes, pack)
    valid = (key_chip < 4).astype(F32)
    loads[0].wait()
    values = hidden[...]
    vectors[10:11, :768] = row_sum(valid * values * values)
    unit, _ = standardize(values)
    norm = low(unit * gains[0:1] + shifts[0:1])
    normed[...] = norm
    for part in range(3):
        cols = slice(part * 768, part * 768 + 768)
        loads[1 + part].wait()
        mix = dot(norm, attend[:, cols])
        mixed[:, cols] = low(mix)
        if part:
            turned[(part - 1) * 768 : part * 768] = low(mix.T)
    save(0, 1, 2)

    def score(head):
        pair, half = divmod(head, 2)
        query = only(mixed[:, pair_lanes(pair)], half) * BF16(0.125)
        return dot_nt(mixed[:, pair_lanes(pair, 768)], query)

    ready = [score(0), score(1)]
    for head in range(12):
        if head + 2 < 12:
            ready.append(score(head + 2))
        scores = jnp.where(key_chip == own_chip, ready[head], NEGATIVE)
        expos = jnp.exp(scores - jnp.max(scores, axis=0, keepdims=True))
        prob = low(expos * (1.0 / jnp.sum(expos, axis=0, keepdims=True)))
        probs[head] = prob
        context_turned[head * 64 : head * 64 + 64] = dot(turned[768 + head * 64 : 832 + head * 64], prob)

    mingled = low(context_turned[...].T)
    context[...] = mingled
    save(3, 4)
    loads[4].wait()
    attention = dot(mingled, merging[...]) + biases[0:1]
    vectors[11:12, :768] = row_sum(valid * attention * attention)
    center = hidden[...] + attention
    middle[...] = center
    unit, _ = standardize(center)
    norm = low(unit * gains[1:2] + shifts[1:2])
    normed_two[...] = norm
    save(5, 6)
    feed = jnp.zeros_like(center)
    def widened(part):
        if part % 2 == 0:
            loads[5 + part // 2].wait()
        cols = slice(part * 512, part * 512 + 512)
        return dot(norm, expand[:, cols]) + inner[:, cols]

    ready = [widened(0)]
    for part in range(6):
        if part < 5:
            ready.append(widened(part + 1))
        cols = slice(part * 512, part * 512 + 512)
        value, slant = gelu_pair(ready[part])
        value = low(value)
        active[:, cols] = value
        slope[part // 2, :, part % 2 * 512 : part % 2 * 512 + 512] = slant
        if part % 2 == 0:
            loads[8 + part // 2].wait()
        feed = feed + dot(value, shrink[cols])
    save(7, 8)
    feed = feed + biases[1:2]
    vectors[12:13, :768] = row_sum(valid * feed * feed)
    output = center + feed
    vectors[13:14, :768] = row_sum(valid * output * output)
    vectors[14:15, :768] = jnp.broadcast_to(row_sum(valid), (1, 768))
    sent[...] = low(output)
    for copy in saves:
        copy.wait()


def encoder_forward_call(sizes, distance, tokens, gains, shifts, biases, attend, merging, expand, inner, shrink):
    frequency = np.exp(-np.log(10000.0) * np.arange(DD // 4) / (DD // 4)).astype(np.float32)
    shapes = (
        ((256, 768), BF16),
        ((256, 2304), BF16),
        ((1536, 256), BF16),
        ((12, 256, 256), BF16),
        ((256, 768), BF16),
        ((256, 768), F32),
        ((256, 768), BF16),
        ((256, 3072), BF16),
        ((3, 256, 1024), F32),
    )
    return pl.pallas_call(
        encoder_forward_kernel,
        out_shape=(
            jax.ShapeDtypeStruct((256, 768), BF16),
            jax.ShapeDtypeStruct((16, 1024), F32),
            jax.ShapeDtypeStruct((2, 4, 32, 128), F32),
        )
        + tuple(jax.ShapeDtypeStruct(*shape) for shape in shapes),
        in_specs=[smem_spec()] * 2 + [vmem_spec()] * 5 + [any_spec()] * 5,
        out_specs=(vmem_spec(),) * 3 + (any_spec(),) * len(shapes),
        scratch_shapes=[pltpu.VMEM(*shape) for shape in shapes]
        + [
            pltpu.VMEM((256, 768), F32),
            pltpu.VMEM(attend.shape, BF16),
            pltpu.VMEM(merging.shape, BF16),
            pltpu.VMEM(expand.shape, BF16),
            pltpu.VMEM(shrink.shape, BF16),
            pltpu.VMEM((768, 256), F32),
            pltpu.SemaphoreType.DMA((11,)),
            pltpu.SemaphoreType.DMA((len(shapes),)),
        ],
        compiler_params=pltpu.CompilerParams(vmem_limit_bytes=60 * 2**20),
        name="encoder_forward",
    )(
        sizes, distance, jnp.asarray(frequency)[None], gains, shifts, biases, inner[None], tokens, attend, merging,
        expand, shrink,
    )


def decoder_kernel(
    reduce, sizes, slots, table, sent, biases, mask_token, gains, shifts, inner,
    cotangent, entry_far, attend_far, merging_far, expand_far, shrink_far,
    summed, rest, vectors, encoded_grad, *refs,
):
    (
        start, normed, mixed, turned, probs, flipped, context, normed_two, active,
        before_grad, go_low, attention_low, context_grad, delta, mixed_grad, target, masked_keys,
        entry_weight, attend, merging, expand, shrink, load_sem,
    ) = refs[:23]
    pack = lax.axis_index("section")
    if reduce:
        mine, partner = neighbours()
        greet(partner)
        engine = reducer(DECODER_PLAN, mine, partner, summed, refs[23:])
        put = engine.put
    else:
        put = put_into(summed)
    put_rest = put_into(rest)
    loads = fetch(
        [
            (entry_far, entry_weight),
            (attend_far, attend),
            (cotangent.at[pack], target),
            (merging_far, merging),
            (expand_far, expand),
            (shrink_far, shrink),
        ],
        load_sem,
    )
    tiles = start.shape[0] // TILE
    vectors[...] = jnp.zeros_like(vectors)
    large = sizes[pack, 0] == 1024

    def add_row(row, value):
        vectors[row : row + 1, :] += value

    loads[0].wait()
    entry = low(dot(sent[...], entry_weight[...]) + biases[0:1])
    loads[1].wait()

    blocks = start.shape[0] // BLOCK

    def slot_chip(tile, size):
        return chip_of(iota((size, 1), 0) + tile * size, sizes, pack)

    def validity(tile, size):
        return (slot_chip(tile, size) < 4).astype(F32)

    def spread_of(tile):
        return (slots[pl.ds(pack, 1)] == iota((TILE, TILE), 0) + tile * TILE).astype(F32)

    def encoding_of(tile):
        pieces = []
        for kind in range(2):
            wave = table[kind, 0, aligned(tile * 8, 8, 8)]
            big = jnp.broadcast_to(wave[:, None], (8, 32, 128)).reshape(TILE, 128)
            wave = table[kind, tile, 0:16]
            own = jnp.broadcast_to(wave[:, None], (16, 16, 128)).reshape(TILE, 128)
            pieces.append(jnp.where(large, big, own))
        for kind in range(2):
            wave = table[kind, 0]
            big = jnp.broadcast_to(wave[None], (8, 32, 128)).reshape(TILE, 128)
            wave = table[kind, tile, 0:16]
            own = jnp.broadcast_to(wave[None], (16, 16, 128)).reshape(TILE, 128)
            pieces.append(jnp.where(large, big, own))
        return jnp.concatenate(pieces, axis=1)

    @pl.loop(0, tiles)
    def _(tile):
        rows = rows_of(tile)
        valid = validity(tile, TILE)
        spread = spread_of(tile)
        fill = valid * (1.0 - jnp.sum(spread, axis=1, keepdims=True))
        hidden = dot(low(spread), entry) + fill * mask_token[...] + encoding_of(tile) * valid
        start[rows] = hidden
        add_row(12, row_sum(valid * hidden * hidden))
        add_row(16, row_sum(valid))
        unit, _ = standardize(hidden)
        norm = low(unit * gains[0:1] + shifts[0:1])
        normed[rows] = norm
        mix = dot(norm, attend[...])
        mix_low = low(mix)
        mixed[rows] = mix_low
        turned[:, rows] = low(mix[:, 256:].T)
        lane = iota((TILE, 128), 1)
        other = (lane % 64 < 5) & (lane % 64 != slot_chip(tile, TILE))
        other = jnp.where(other, NEGATIVE, 0.0).astype(BF16)
        for head in range(4):
            lanes = slice(256 + head // 2 * 128, 384 + head // 2 * 128)
            masked_keys[head, rows] = jnp.where(lane // 64 == head % 2, mix_low[:, lanes], other)

    @pl.loop(0, 2 * tiles)
    def _(step):
        pair, tile = step // tiles, step % tiles
        rows = rows_of(tile)
        lane = iota((TILE, 128), 1)
        chosen = (lane % 64 == slot_chip(tile, TILE)).astype(F32).astype(BF16)
        for half in range(2):
            query = jnp.where(lane // 64 == half, mixed[rows, pair_lanes(pair)] * BF16(0.125), chosen)
            scores = dot_nt(masked_keys[pair * 2 + half], query)
            expos = jnp.exp(scores - jnp.max(scores, axis=0, keepdims=True))
            prob = low(expos * (1.0 / jnp.sum(expos, axis=0, keepdims=True)))
            probs[pair * 2 + half, :, rows] = prob
            flipped[head_rows(pair, half), rows] = dot(turned[head_rows(pair, half, 256)], prob)

    for copy in loads[2:]:
        copy.wait()

    @pl.loop(0, blocks)
    def _(tile):
        rows = rows_of(tile, BLOCK)
        valid = validity(tile, BLOCK)
        mingled = low(flipped[:, rows].T)
        context[rows] = mingled
        attention = dot(mingled, merging[...]) + biases[1:2]
        add_row(13, row_sum(valid * attention * attention))
        unit, _ = standardize(start[rows] + attention)
        norm = low(unit * gains[1:2] + shifts[1:2])
        normed_two[rows] = norm
        go = target[rows] * valid
        go_below = low(go)
        go_low[rows] = go_below
        add_row(2, row_sum(go))
        for part in range(8):
            cols = slice(part * 256, part * 256 + 256)
            value, slope = gelu_pair(dot(norm, expand[:, cols]) + inner[:, cols])
            active[rows, cols] = low(value)
            grad = low(slope * dot_nt(go_below, shrink[cols]))
            before_grad[rows, cols] = grad
            lanes = slice(part % 2 * 256, part % 2 * 256 + 256)
            vectors[8 + part // 2 : 9 + part // 2, lanes] += row_sum(grad.astype(F32))

    if reduce:
        await_greetings()
    for part in range(2):
        cols = slice(part * 256, part * 256 + 256)
        store_packed(put, part * 16, DECODER_EXPAND, dot_tn(normed_two[:, cols], before_grad[...]))
    if reduce:
        engine.send(2048)

    @pl.loop(0, 8)
    def _(part):
        cols = aligned(part * 256, 256, 256)
        store_packed(put, part * 4, DECODER_SHRINK, dot_tn(active[:, cols], go_low[...]))

    if reduce:
        engine.send(4096)

    @pl.loop(0, tiles)
    def _(tile):
        rows = rows_of(tile)
        valid = validity(tile, TILE)
        center = start[rows] + (dot(context[rows], merging[...]) + biases[1:2])
        unit, inverse = standardize(center)
        feed = dot(active[rows], shrink[...]) + biases[2:3]
        add_row(14, row_sum(valid * feed * feed))
        output = center + feed
        add_row(15, row_sum(valid * output * output))
        norm_grad = dot_nt(before_grad[rows], expand[...])
        add_row(5, row_sum(norm_grad * unit))
        add_row(7, row_sum(norm_grad))
        grad = target[rows] * valid + norm_back(unit, inverse, gains[1:2], norm_grad)
        target[rows] = grad
        add_row(1, row_sum(grad))
        below = low(grad)
        attention_low[rows] = below
        outer = low(dot_nt(below, merging[...]))
        context_grad[rows] = outer
        product = (outer.astype(F32) * flipped[:, rows].T).T
        for head in range(4):
            delta[head, :, rows] = row_sum(product[head * 64 : head * 64 + 64])
        if reduce:
            engine.turn(tile)

    for part in range(2):
        cols = slice(part * 256, part * 256 + 256)
        store_packed(put, part * 16, DECODER_MERGE, dot_tn(attention_low[:, cols], context[...]))
        shards = slice(part * 16, part * 16 + 16)
        put(shards, 4352, jnp.zeros((16, 16, DECODER_PLAN.chunks * DECODER_PLAN.span - 4352), F32))
    if reduce:
        engine.send(DECODER_PLAN.chunks * DECODER_PLAN.span)

    flipped[...] = jnp.zeros_like(flipped)

    @pl.loop(0, 2 * tiles)
    def _(step):
        pair, tile = step // tiles, step % tiles
        rows = rows_of(tile)
        lanes = pair_lanes(pair)
        values = mixed[rows, pair_lanes(pair, 512)]
        raws, probabilities, queries, outers = [], [], [], []
        for half in range(2):
            prob = probs[pair * 2 + half, rows]
            outer = only(context_grad[:, lanes], half)
            raw = low(prob.astype(F32) * (dot_nt(values, outer) - delta[pair * 2 + half]))
            flipped[head_rows(pair, half)] += dot(turned[head_rows(pair, half), rows], raw)
            raws.append(raw)
            probabilities.append(prob)
            outers.append(outer)
            queries.append(only(mixed[:, lanes], half))
        key_grad = dot(jnp.concatenate(raws, axis=1), jnp.concatenate(queries, axis=0))
        mixed_grad[rows, pair_lanes(pair, 256)] = low(key_grad * 0.125)
        value_grad = dot(jnp.concatenate(probabilities, axis=1), jnp.concatenate(outers, axis=0))
        mixed_grad[rows, pair_lanes(pair, 512)] = low(value_grad)
        if reduce:
            engine.turn(tiles + step)

    def last(tile, entry_grad):
        rows = rows_of(tile)
        mixed_grad[rows, 0:256] = low(flipped[:, rows].T * 0.125)
        norm_grad = dot_nt(mixed_grad[rows], attend[...])
        unit, inverse = standardize(start[rows])
        add_row(4, row_sum(norm_grad * unit))
        add_row(6, row_sum(norm_grad))
        grad = target[rows] + norm_back(unit, inverse, gains[0:1], norm_grad)
        spread = spread_of(tile)
        fill = validity(tile, TILE) * (1.0 - jnp.sum(spread, axis=1, keepdims=True))
        add_row(3, row_sum(fill * grad))
        if reduce:
            engine.turn(3 * tiles + tile)
        return entry_grad + dot_tn(low(spread), low(grad))

    entry_grad = lax.fori_loop(0, tiles, last, jnp.zeros((TILE, 512), F32))
    add_row(0, row_sum(entry_grad))
    entry_low = low(entry_grad)
    encoded_grad[...] = low(dot_nt(entry_low, entry_weight[...]))
    store_packed(put_rest, 0, ENTRY, dot_tn(sent[...], entry_low))

    @pl.loop(0, 2)
    def _(part):
        cols = aligned(part * 256, 256, 256)
        store_packed(put_rest, part * 16, DECODER_ATTEND, dot_tn(normed[:, cols], mixed_grad[...]))

    if reduce:
        engine.close()


def decoder_call(
    reduce, sizes, slots, table, sent, cotangent, entry_weight, biases, mask_token,
    gains, shifts, attend, merging, expand, inner, shrink,
):
    length = cotangent.shape[1]
    width = 512
    if reduce:
        summed = jax.ShapeDtypeStruct((DECODER_PLAN.chunks, 16, DECODER_PLAN.span), F32)
        extra = reducer_scratch(DECODER_PLAN)
        params = dict(collective_id=1, has_side_effects=True)
    else:
        summed = jax.ShapeDtypeStruct((DECODER_PLAN.chunks, 2, 16, 16, DECODER_PLAN.span), BF16)
        extra = []
        params = dict()
    return pl.pallas_call(
        functools.partial(decoder_kernel, reduce),
        out_shape=(
            summed,
            jax.ShapeDtypeStruct((1, 2, 16, 16, UNIT), BF16),
            jax.ShapeDtypeStruct((24, width), F32),
            jax.ShapeDtypeStruct((256, 768), BF16),
        ),
        in_specs=[smem_spec()] + [vmem_spec()] * 8 + [any_spec()] * 6,
        out_specs=(vmem_spec(),) * 4,
        scratch_shapes=[
            pltpu.VMEM((length, width), F32),
            pltpu.VMEM((length, width), BF16),
            pltpu.VMEM((length, 768), BF16),
            pltpu.VMEM((512, length), BF16),
            pltpu.VMEM((4, length, length), BF16),
            pltpu.VMEM((256, length), F32),
            pltpu.VMEM((length, 256), BF16),
            pltpu.VMEM((length, width), BF16),
            pltpu.VMEM((length, 2048), BF16),
            pltpu.VMEM((length, 2048), BF16),
            pltpu.VMEM((length, width), BF16),
            pltpu.VMEM((length, width), BF16),
            pltpu.VMEM((length, 256), BF16),
            pltpu.VMEM((4, 1, length), F32),
            pltpu.VMEM((length, 768), BF16),
            pltpu.VMEM((length, width), F32),
            pltpu.VMEM((4, length, 128), BF16),
            pltpu.VMEM(entry_weight.shape, BF16),
            pltpu.VMEM(attend.shape, BF16),
            pltpu.VMEM(merging.shape, BF16),
            pltpu.VMEM(expand.shape, BF16),
            pltpu.VMEM(shrink.shape, BF16),
            pltpu.SemaphoreType.DMA((6,)),
        ]
        + extra,
        compiler_params=pltpu.CompilerParams(vmem_limit_bytes=63 * 2**20, **params),
        name="decoder_block",
    )(
        sizes, slots, table, sent, biases, mask_token[None], gains, shifts,
        inner[None], cotangent, entry_weight, attend, merging, expand, shrink,
    )


def encoder_backward_kernel(
    reduce, encoded_grad, sums, decoder_vectors, gains, tokens, rest, attend_far, merging_far, expand_far,
    shrink_far, normed_far, mixed_far, turned_far, probs_far, context_far, middle_far, normed_two_far, active_far,
    slope_far, summed, tail_summed, vectors, tokens_grad, *refs,
):
    if reduce:
        decoder_sums, arrived = refs[:2]
        refs = refs[2:]
    (
        hidden, attend, merging, expand, shrink, normed, mixed, turned, probs, context, middle, normed_two, active,
        slope, before_grad, norm_sum, attention_low, context_grad, key_grad, query_turned, mixed_grad, active_turned,
        flipped, inner_sum, load_sem, part_sem,
    ) = refs[:26]
    pack = lax.axis_index("section")

    def part_loads(part):
        cols = aligned(part * 1024, 1024, 1024)
        slot = part % 2
        return [
            pltpu.make_async_copy(expand_far.at[:, cols], expand.at[slot], part_sem.at[slot, 0]),
            pltpu.make_async_copy(shrink_far.at[cols], shrink.at[slot], part_sem.at[slot, 1]),
            pltpu.make_async_copy(slope_far.at[part], slope.at[slot], part_sem.at[slot, 2]),
        ]

    if reduce:
        (
            decoder_total, encoder_total, decoder_got, encoder_got, payload,
            own_sem, small_send, small_recv, pay_send, pay_recv, small_load,
        ) = refs[26:37]
        mine, partner = neighbours()
        greet(partner)
        engine = reducer(ENCODER_PLAN, mine, partner, summed, refs[37:68])
        tail = reducer(TAIL_PLAN, mine, partner, tail_summed, refs[68:])
        put_tail = tail.put
        first_own = fetch(
            [
                pair
                for pair in (
                    (rest.at[0, 1 - mine["c"]], engine.staging.at[0]),
                    (rest.at[0, mine["c"]], engine.own.at[0]),
                )
            ],
            own_sem,
        )
        decoder_load = pltpu.make_async_copy(decoder_vectors, decoder_total.at[0], small_load)
        decoder_load.start()
    else:
        put_tail = put_into(tail_summed)
    early = pltpu.make_async_copy(active_far, active, load_sem.at[10])
    early.start()
    for copy in part_loads(0):
        copy.start()
    if reduce:
        for copy in first_own:
            copy.wait()
        await_greetings()
        engine.first_copy(0).start()
    loads = fetch(
        [
            (normed_two_far, normed_two),
            (middle_far, middle),
            (merging_far, merging),
            (context_far, context),
            (mixed_far, mixed),
            (probs_far, probs),
            (turned_far.at[0:768], turned),
            (normed_far, normed),
            (attend_far, attend),
            (tokens.at[pack], hidden),
        ],
        load_sem,
    )
    for copy in part_loads(1):
        copy.start()
    vectors[...] = sums[...]
    go_low = encoded_grad[...]
    go = go_low.astype(F32)
    vectors[1:2, :768] = row_sum(go)
    norm_sum[...] = jnp.zeros_like(norm_sum)

    def unit_grad(unit, place, pieces):
        put = engine.put_unit(unit) if reduce else put_unit_into(summed, unit)
        for first, value in pieces:
            store_packed(put, first, (0,) + place[1:], value)
        if reduce:
            engine.first_copy(unit).start()

    def shrink_start():
        early.wait()
        for piece in range(4):
            rows = slice(piece * 768, piece * 768 + 768)
            active_turned[rows] = active[:, rows].T

    def shrink_grad(part):
        cols = aligned(part * 256, 256, 256)
        pieces = []
        for piece in range(4):
            rows = slice(piece * 768, piece * 768 + 768)
            pieces.append((piece * 8, dot(active_turned[rows], encoded_grad[:, cols])))
        unit_grad(1 + part, ENCODER_SHRINK[0], pieces)

    def hidden_layer(part):
        for copy in part_loads(part):
            copy.wait()
        slot = part % 2
        grad = low(slope[slot] * dot_nt(encoded_grad[...], shrink[slot]))
        before_grad[...] = grad
        inner_sum[part] = row_sum(grad.astype(F32))
        norm_sum[...] += dot_nt(grad, expand[slot])

        @pl.when(part == 0)
        def _():
            for copy in part_loads(2):
                copy.start()

    def expand_grad(part):
        @pl.when(part == 0)
        def _():
            loads[0].wait()
            flipped[...] = normed_two[...].T

        unit_grad(4 + part, ENCODER_EXPAND[0], [(0, dot(flipped[...], before_grad[...]))])

    def middle_layer():
        loads[1].wait()
        loads[2].wait()
        for part in range(3):
            vectors[6 + part : 7 + part] = inner_sum[part]
        unit, inverse = standardize(middle[...])
        norm_grad = norm_sum[...]
        vectors[3:4, :768] = row_sum(norm_grad * unit)
        vectors[5:6, :768] = row_sum(norm_grad)
        grad = encoded_grad[...].astype(F32) + norm_back(unit, inverse, gains[1:2], norm_grad)
        vectors[0:1, :768] = row_sum(grad)
        tokens_grad[...] = grad
        below = low(grad)
        attention_low[...] = below
        context_grad[...] = low(dot_nt(below, merging[...]))
        for copy in loads[3:7]:
            copy.wait()

    def attention(first):
        @pl.loop(first, first + 2)
        def _(pair):
            lanes = pair_lanes(pair)
            values = mixed[:, pair_lanes(pair, 1536)]
            keys_total = jnp.zeros((TILE, 128), F32)
            values_total = jnp.zeros((TILE, 128), F32)
            for half in range(2):
                prob = probs[pair * 2 + half]
                outer = only(context_grad[:, lanes], half)
                query = only(mixed[:, lanes], half)
                wide = prob.astype(F32)
                grad = dot_nt(values, outer)
                raw = low(wide * (grad - jnp.sum(wide * grad, axis=0, keepdims=True)))
                keys_total = keys_total + dot(raw, query)
                values_total = values_total + dot(prob, outer)
                rows = head_rows(pair, half)
                query_turned[rows] = dot(turned[rows], raw)
            key_grad[0, :, lanes] = keys_total
            key_grad[1, :, lanes] = values_total

    def mixing():
        mixed_grad[:, 0:768] = low(query_turned[...].T * 0.125)
        mixed_grad[:, 768:1536] = low(key_grad[0] * 0.125)
        mixed_grad[:, 1536:2304] = low(key_grad[1])

    def attend_grad(part):
        @pl.when(part == 0)
        def _():
            loads[7].wait()
            flipped[...] = normed[...].T

        wide = aligned(part * 1024, 1024, 1024)
        unit_grad(7 + part, ENCODER_ATTEND[0], [(0, dot(flipped[...], mixed_grad[:, wide]))])

    def tail_grad():
        store_packed(put_tail, 0, ENCODER_ATTEND[2], dot(flipped[...], mixed_grad[:, 2048:2304]))
        store_packed(put_tail, 0, ENCODER_MERGE, dot_tn(attention_low[...], context[...]))
        if reduce:
            tail.send(UNIT)

    def input_layer():
        loads[8].wait()
        loads[9].wait()
        norm_grad = dot_nt(mixed_grad[...], attend[...])
        unit, inverse = standardize(hidden[...])
        vectors[2:3, :768] = row_sum(norm_grad * unit)
        vectors[4:5, :768] = row_sum(norm_grad)
        grad = tokens_grad[...] + norm_back(unit, inverse, gains[0:1], norm_grad)
        tokens_grad[...] = grad
        if reduce:
            payload[...] = low(grad)

    if not reduce:
        shrink_start()
        for part in range(3):
            shrink_grad(part)
        for part in range(3):
            hidden_layer(part)
            expand_grad(part)
        middle_layer()
        for first in (0, 2, 4):
            attention(first)
        mixing()
        for part in range(2):
            attend_grad(part)
        tail_grad()
        input_layer()
        return

    def exchange(source, piece):
        rows = aligned(piece * 32, 32, 32)
        return remote(source.at[rows], arrived.at[rows], pay_send.at[piece], pay_recv.at[piece], partner["x"])

    small_route = ("c",) + ROUTES[0]
    totals = ((decoder_total, decoder_got), (encoder_total, encoder_got))

    def small_copy(stage, kind):
        source, target = totals[kind]
        return remote(
            source.at[stage],
            target.at[stage],
            small_send.at[stage, kind],
            small_recv.at[stage, kind],
            partner[small_route[stage]],
        )

    def small_advance(stage):
        if stage == 0:
            encoder_total[0] = vectors[...]
        for kind in range(2):
            source, target = totals[kind]
            if stage > 0:
                small_copy(stage - 1, kind).wait_recv()
                source[stage] = source[stage - 1] + target[stage - 1]
            if stage < 5:
                small_copy(stage, kind).start()

    shrink_start()
    shrink_grad(0)
    decoder_load.wait()

    def attention_all():
        @pl.loop(0, 3)
        def _(step):
            attention(2 * step)

        mixing()

    def ending():
        tail_grad()
        input_layer()

    part = functools.partial
    works = {4: middle_layer, 5: attention_all, 7: ending}
    turns = ENCODER_PLAN.chunks + TAIL_PLAN.chunks + 4 * LAG
    works.update({8 + stage + max(0, stage - 1): part(small_advance, stage) for stage in range(6)})

    @pl.loop(0, turns)
    def _(number):
        engine.turn(number)
        tail.turn(number - ENCODER_PLAN.chunks)

        @pl.when(number <= 1)
        def _():
            shrink_grad(number + 1)

        @pl.when((number >= 2) & (number <= 4))
        def _():
            expand_grad(number - 2)

        @pl.when((number >= 1) & (number <= 3))
        def _():
            hidden_layer(number - 1)

        for position, work in works.items():
            pl.when(number == position)(work)

        @pl.when(number == 6)
        def _():
            @pl.loop(0, 2)
            def _(part):
                attend_grad(part)

        @pl.when((pack == 0) & (number < 8))
        def _():
            exchange(encoded_grad, number).start()

        @pl.when((pack == 1) & (number >= 8) & (number < 16))
        def _():
            exchange(payload, number - 8).start()

    for stage in range(5):
        for kind in range(2):
            small_copy(stage, kind).wait_send()
    for piece in range(8):
        exchange(payload, piece).wait()
    engine.close()
    tail.close()
    vectors[...] = encoder_total[5]
    decoder_sums[...] = decoder_total[5]


def encoder_backward_call(reduce, tokens, encoded_grad, sums, decoder_vectors, rest, kept, gains, attend, merging, expand, shrink):
    if reduce:
        summed = tuple(
            jax.ShapeDtypeStruct((plan.chunks, 16, plan.span), F32) for plan in (ENCODER_PLAN, TAIL_PLAN)
        )
        more = (
            jax.ShapeDtypeStruct(decoder_vectors.shape, F32),
            jax.ShapeDtypeStruct((256, 768), BF16),
        )
        more_specs = (vmem_spec(), any_spec())
        extra = [
            pltpu.VMEM((6,) + decoder_vectors.shape, F32),
            pltpu.VMEM((6,) + sums.shape, F32),
            pltpu.VMEM((5,) + decoder_vectors.shape, F32),
            pltpu.VMEM((5,) + sums.shape, F32),
            pltpu.VMEM((256, 768), BF16),
            pltpu.SemaphoreType.DMA((2,)),
            pltpu.SemaphoreType.DMA((5, 2)),
            pltpu.SemaphoreType.DMA((5, 2)),
            pltpu.SemaphoreType.DMA((8,)),
            pltpu.SemaphoreType.DMA((8,)),
            pltpu.SemaphoreType.DMA,
        ] + reducer_scratch(ENCODER_PLAN) + reducer_scratch(TAIL_PLAN)
        params = dict(collective_id=2, has_side_effects=True)
    else:
        summed = tuple(
            jax.ShapeDtypeStruct((plan.chunks, 2, 16, 16, plan.span), BF16) for plan in (ENCODER_PLAN, TAIL_PLAN)
        )
        more, more_specs, extra, params = (), (), [], dict()
    return pl.pallas_call(
        functools.partial(encoder_backward_kernel, reduce),
        out_shape=summed
        + (
            jax.ShapeDtypeStruct(sums.shape, F32),
            jax.ShapeDtypeStruct((256, 768), F32),
        )
        + more,
        in_specs=[vmem_spec()] * 2 + [any_spec(), vmem_spec()] + [any_spec()] * 15,
        out_specs=(vmem_spec(),) * 4 + more_specs,
        scratch_shapes=[
            pltpu.VMEM((256, 768), F32),
            pltpu.VMEM(attend.shape, BF16),
            pltpu.VMEM(merging.shape, BF16),
            pltpu.VMEM((2, 768, 1024), BF16),
            pltpu.VMEM((2, 1024, 768), BF16),
            pltpu.VMEM((256, 768), BF16),
            pltpu.VMEM((256, 2304), BF16),
            pltpu.VMEM((768, 256), BF16),
            pltpu.VMEM((12, 256, 256), BF16),
            pltpu.VMEM((256, 768), BF16),
            pltpu.VMEM((256, 768), F32),
            pltpu.VMEM((256, 768), BF16),
            pltpu.VMEM((256, 3072), BF16),
            pltpu.VMEM((2, 256, 1024), F32),
            pltpu.VMEM((256, 1024), BF16),
            pltpu.VMEM((256, 768), F32),
            pltpu.VMEM((256, 768), BF16),
            pltpu.VMEM((256, 768), BF16),
            pltpu.VMEM((2, 256, 768), F32),
            pltpu.VMEM((768, 256), F32),
            pltpu.VMEM((256, 2304), BF16),
            pltpu.VMEM((3072, 256), BF16),
            pltpu.VMEM((768, 256), BF16),
            pltpu.VMEM((3, 1, 1024), F32),
            pltpu.SemaphoreType.DMA((11,)),
            pltpu.SemaphoreType.DMA((2, 3)),
        ]
        + extra,
        compiler_params=pltpu.CompilerParams(vmem_limit_bytes=62 * 2**20, **params),
        name="encoder_backward",
    )(encoded_grad, sums, decoder_vectors, gains, tokens, rest, attend, merging, expand, shrink, *kept)


def unpack(packed, place):
    span = packed.shape[-1]

    def take(start, size):
        pieces = []
        while size:
            chunk, first = divmod(start, span)
            length = min(size, span - first)
            pieces.append(packed[chunk, ..., first : first + length])
            start, size = start + length, size - length
        return pieces[0] if len(pieces) == 1 else jnp.concatenate(pieces, axis=-1)

    offset, count, width = place
    pieces = [take(offset + i * width, width) for i in range(count // 16)]
    if count % 16:
        rest = take(offset + count // 16 * width, width // 2)
        pieces.append(jnp.concatenate([rest[..., :8, :], rest[..., 8:, :]], axis=-1))
    return pieces[0] if len(pieces) == 1 else jnp.concatenate(pieces, axis=-2)


def finish_kernel(
    decoder_summed_far, decoder_sums_far, encoder_sums_far, summed_far, tail_far, arrived_far, tokens_grad_far, encoded_grad_far,
    boundary, statistics, e_gains, e_shifts, e_biases, e_attend, e_merge, e_expand, e_inner, e_shrink,
    d_entry, d_biases, mask_grad, d_gains, d_shifts, d_attend, d_merge, d_expand, d_inner, d_shrink,
    decoder_summed, decoder_sums, encoder_sums, summed, tail, arrived, tokens_grad, encoded_grad, load_sem,
):
    section = lax.axis_index("section")
    loads = fetch(
        [
            (decoder_summed_far, decoder_summed),
            (decoder_sums_far, decoder_sums),
            (encoder_sums_far, encoder_sums),
            (summed_far, summed),
            (tail_far, tail),
            (arrived_far, arrived),
            (tokens_grad_far, tokens_grad),
            (encoded_grad_far, encoded_grad),
        ],
        load_sem,
    )
    number = section * lax.axis_size("dp") + lax.axis_index("dp")

    def own(rows, count):
        width = rows.shape[1]
        return pltpu.roll(rows, (width - number * count) % width, axis=1)[:, :count]

    def own_line(rows, count):
        return own(jnp.concatenate([rows[i : i + 1] for i in range(rows.shape[0])], axis=1), count)

    for copy in loads[:3]:
        copy.wait()
    lane = iota((1, 128), 1)
    values = jnp.zeros((1, 128), F32)
    for sums, width, first, count_row, base in ((encoder_sums, DE, 10, 14, 0), (decoder_sums, DD, 12, 16, 4)):
        scale = 1.0 / (sums[count_row : count_row + 1, 0:1] * width)
        for i in range(4):
            value = jnp.sum(sums[first + i : first + i + 1, :], axis=1, keepdims=True) * scale
            values = jnp.where(lane == base + i, value, values)
    statistics[...] = jnp.sqrt(values)[:, :8]
    rows = own(encoder_sums[0:8, :DE], 24)
    e_biases[...] = rows[0:2]
    e_gains[...] = rows[2:4]
    e_shifts[...] = rows[4:6]
    e_inner[...] = own_line(encoder_sums[6:9], 96)
    rows = own(decoder_sums[0:8], 16)
    d_biases[...] = rows[0:3]
    mask_grad[...] = rows[3:4]
    d_gains[...] = rows[4:6]
    d_shifts[...] = rows[6:8]
    d_inner[...] = own_line(decoder_sums[8:12], 64)

    d_merge[...] = unpack(decoder_summed, DECODER_MERGE)
    d_expand[...] = unpack(decoder_summed, DECODER_EXPAND)
    d_shrink[...] = unpack(decoder_summed, DECODER_SHRINK)
    loads[3].wait()
    loads[4].wait()
    d_entry[...] = unpack(summed, ENTRY)
    d_attend[...] = unpack(summed, DECODER_ATTEND)
    for target, places in ((e_expand, ENCODER_EXPAND), (e_attend, ENCODER_ATTEND), (e_shrink, ENCODER_SHRINK)):
        start = 0
        for place in places:
            source = tail if place is ENCODER_ATTEND[2] else summed
            target[:, start : start + place[2]] = unpack(source, place)
            start += place[2]
    e_merge[...] = unpack(tail, ENCODER_MERGE)
    for copy in loads[5:]:
        copy.wait()

    @pl.when(section == 0)
    def _():
        boundary[0, 0] = tokens_grad[...]
        boundary[0, 1] = arrived[...].astype(F32)

    @pl.when(section == 1)
    def _():
        boundary[0, 0] = arrived[...].astype(F32)
        boundary[0, 1] = encoded_grad[...].astype(F32)


def finish_call(*operands):
    shapes = (
        (1, 2, 256, 768), (1, 8), (2, 24), (2, 24), (2, 24), (24, 2304), (24, 768), (24, 3072), (1, 96), (96, 768),
        (24, 512), (3, 16), (1, 16), (2, 16), (2, 16), (16, 768), (16, 256), (16, 2048), (1, 64), (64, 512),
    )
    outs = list(
        pl.pallas_call(
            finish_kernel,
            out_shape=tuple(jax.ShapeDtypeStruct(shape, F32) for shape in shapes),
            in_specs=[any_spec()] * len(operands),
            out_specs=(vmem_spec(),) * len(shapes),
            scratch_shapes=[pltpu.VMEM(operand.shape, operand.dtype) for operand in operands]
            + [pltpu.SemaphoreType.DMA((len(operands),))],
            compiler_params=pltpu.CompilerParams(vmem_limit_bytes=60 * 2**20),
            name="finish",
        )(*operands)
    )
    for line in (1, 8, 12, 18):
        outs[line] = outs[line].reshape(-1)
    for turned in (6, 16):
        outs[turned] = outs[turned].T
    return tuple(outs)


def scatter_sum(member, share_dim):
    return lax.psum_scatter(
        member, ("section", "dp"), scatter_dimension=share_dim, tiled=True
    )


def finish_generic(decoder_part, part, tail, decoder_sums, encoder_sums, tokens_grad, encoded_grad):
    section = lax.axis_index("section")
    payload = jnp.where(section == 0, encoded_grad, low(tokens_grad))

    def whole(packed, *places):
        packed = jnp.swapaxes(packed, 1, 2).reshape(-1, 32, 16, packed.shape[-1])
        blocks = [unpack(packed, place).reshape(32 * place[1], place[2]) for place in places]
        return scatter_sum(jnp.concatenate(blocks, axis=1).astype(F32), 0)

    def line(value):
        return scatter_sum(value, value.ndim - 1)

    arrived = lax.ppermute(payload, "section", [(0, 1), (1, 0)]).astype(F32)
    boundary = jnp.where(
        section == 0,
        jnp.stack([tokens_grad, arrived]),
        jnp.stack([arrived, encoded_grad.astype(F32)]),
    )
    sums = jnp.concatenate(
        [jnp.sum(encoder_sums[10:14], axis=1), jnp.sum(decoder_sums[12:16], axis=1)]
    )
    sums, counts = lax.psum((sums, (encoder_sums[14, 0], decoder_sums[16, 0])), ("section", "dp"))
    scales = jnp.concatenate([jnp.full((4,), counts[0] * DE), jnp.full((4,), counts[1] * DD)])
    return (
        boundary[None],
        jnp.sqrt(sums / scales),
        line(encoder_sums[2:4, :DE]),
        line(encoder_sums[4:6, :DE]),
        line(encoder_sums[0:2, :DE]),
        jnp.concatenate([whole(part, *ENCODER_ATTEND[:2]), whole(tail, ENCODER_ATTEND[2])], axis=1),
        whole(tail, ENCODER_MERGE).T,
        whole(part, *ENCODER_EXPAND),
        line(encoder_sums[6:9].reshape(-1)),
        whole(part, *ENCODER_SHRINK),
        whole(decoder_part[1], ENTRY),
        line(decoder_sums[0:3]),
        line(decoder_sums[3]),
        line(decoder_sums[4:6]),
        line(decoder_sums[6:8]),
        whole(decoder_part[1], DECODER_ATTEND),
        whole(decoder_part[0], DECODER_MERGE).T,
        whole(decoder_part[0], DECODER_EXPAND),
        line(decoder_sums[8:12].reshape(-1)),
        whole(decoder_part[0], DECODER_SHRINK),
    )


def body(
    visible_tokens,
    cotangent,
    chip_sizes,
    ground_distance,
    visible_slots,
    encoder_gains,
    encoder_shifts,
    encoder_biases,
    encoder_attend,
    encoder_merge,
    encoder_expand,
    encoder_inner,
    encoder_shrink,
    decoder_entry,
    decoder_biases,
    mask_token,
    decoder_gains,
    decoder_shifts,
    decoder_attend,
    decoder_merge,
    decoder_widen_weight,
    decoder_inner,
    decoder_shrink,
):
    reduce = (lax.axis_size("section"), lax.axis_size("dp")) == (2, 16)
    sent, sums, table, *kept = encoder_forward_call(
        chip_sizes, ground_distance, visible_tokens, encoder_gains, encoder_shifts, encoder_biases,
        encoder_attend, encoder_merge, encoder_expand, encoder_inner, encoder_shrink,
    )
    decoder_summed, rest, decoder_vectors, encoded_grad = decoder_call(
        reduce, chip_sizes, visible_slots, table, sent, cotangent, decoder_entry, decoder_biases, mask_token,
        decoder_gains, decoder_shifts, decoder_attend, decoder_merge, decoder_widen_weight, decoder_inner,
        decoder_shrink,
    )
    summed, tail, encoder_sums, tokens_grad, *more = encoder_backward_call(
        reduce, visible_tokens, encoded_grad, sums, decoder_vectors, rest, kept,
        encoder_gains, encoder_attend, encoder_merge, encoder_expand, encoder_shrink,
    )
    if reduce:
        decoder_sums, arrived = more
        return finish_call(
            decoder_summed, decoder_sums, encoder_sums, summed, tail, arrived, tokens_grad, encoded_grad
        )
    return finish_generic(
        (decoder_summed, rest), summed, tail, decoder_vectors, encoder_sums, tokens_grad, encoded_grad
    )


def solution(mesh):
    in_specs = (
        P("dp", None, None),
        P("dp", None, None),
        P("dp", None),
        P("dp", None),
        P("dp", None),
        P(),
        P(),
        P(),
        P(),
        P(),
        P(),
        P(),
        P(),
        P(),
        P(),
        P(),
        P(),
        P(),
        P(),
        P(),
        P(),
        P(),
        P(),
    )
    out_specs = (
        P("section", "dp", None, None),
        P(),
        P(None, ("section", "dp")),
        P(None, ("section", "dp")),
        P(None, ("section", "dp")),
        P(("section", "dp"), None),
        P(None, ("section", "dp")),
        P(("section", "dp"), None),
        P(("section", "dp")),
        P(("section", "dp"), None),
        P(("section", "dp"), None),
        P(None, ("section", "dp")),
        P(("section", "dp")),
        P(None, ("section", "dp")),
        P(None, ("section", "dp")),
        P(("section", "dp"), None),
        P(None, ("section", "dp")),
        P(("section", "dp"), None),
        P(("section", "dp")),
        P(("section", "dp"), None),
    )
    return jax.shard_map(body, mesh=mesh, in_specs=in_specs, out_specs=out_specs, check_vma=False)
```

```python
import functools
import types

import jax
import jax.numpy as jnp
import numpy as np
from jax import lax
from jax.experimental import pallas as pl
from jax.experimental.pallas import tpu as pltpu
from jax.sharding import PartitionSpec as P

DE = 768
DD = 512
TILE = 256
BLOCK = 512
NEGATIVE = -1e30
F32, BF16 = jnp.float32, jnp.bfloat16
MESH_ID = pl.DeviceIdType.MESH

CANON = ("x", "z2", "z1", "y")
ROUTES = (("x", "y", "z1", "z2"), ("y", "x", "z1", "z2"), ("z1", "z2", "x", "y"))
UNIT = 1536
STARTS = (0, 2, 4, 5, 6)
DECODER_PLAN = types.SimpleNamespace(widths=(2, 2, 1), chunks=7, slots=7, ring=3, span=640)
ENCODER_PLAN = types.SimpleNamespace(widths=(3, 6, 3), chunks=9, slots=3, ring=3, span=1536)
TAIL_PLAN = types.SimpleNamespace(widths=(2, 3, 1), chunks=2, slots=2, ring=2, span=768)

DECODER_EXPAND, DECODER_SHRINK, DECODER_MERGE = (0, 16, 2048), (2048, 64, 512), (4096, 16, 256)
ENTRY, DECODER_ATTEND = (0, 24, 512), (768, 16, 768)
ENCODER_SHRINK = tuple((UNIT * (1 + part), 96, 256) for part in range(3))
ENCODER_EXPAND = tuple((UNIT * (4 + part), 24, 1024) for part in range(3))
ENCODER_ATTEND = ((UNIT * 7, 24, 1024), (UNIT * 8, 24, 1024), (0, 24, 256))
ENCODER_MERGE = (384, 24, 768)


def dot(a, b):
    return jnp.dot(a, b, preferred_element_type=F32)


def dot_nt(a, b):
    return lax.dot_general(a, b, (((1,), (1,)), ((), ())), preferred_element_type=F32)


def dot_tn(a, b):
    return lax.dot_general(a, b, (((0,), (0,)), ((), ())), preferred_element_type=F32)


def low(value):
    return value.astype(BF16)


def standardize(values):
    centered = values - jnp.mean(values, axis=-1, keepdims=True)
    inverse = lax.rsqrt(jnp.mean(centered * centered, axis=-1, keepdims=True) + 1e-05)
    return centered * inverse, inverse


def norm_back(unit, inverse, gain, grad):
    inner = grad * gain
    return inverse * (
        inner
        - jnp.mean(inner, axis=-1, keepdims=True)
        - unit * jnp.mean(inner * unit, axis=-1, keepdims=True)
    )


def row_sum(values):
    return jnp.sum(values, axis=0, keepdims=True)


def gelu_pair(before):
    half = 0.5 * (1.0 + lax.erf(before * 0.7071067811865476))
    density = jnp.exp(-0.5 * before * before) * 0.3989422804014327
    return before * half, half + before * density


def chip_of(places, sizes, pack):
    end = sizes[pack, 0]
    chip = (places >= end).astype(jnp.int32)
    for slot in range(1, 4):
        end = end + sizes[pack, slot]
        chip = chip + (places >= end).astype(jnp.int32)
    return chip


def iota(shape, dimension):
    return lax.broadcasted_iota(jnp.int32, shape, dimension)


def aligned(start, size, unit):
    if isinstance(start, int):
        return slice(start, start + size)
    return pl.ds(pl.multiple_of(start, unit), size)


def pair_lanes(pair, base=0):
    return aligned(base + pair * 128, 128, 128)


def head_rows(pair, half, base=0):
    return aligned(base + pair * 128 + half * 64, 64, 64)


def rows_of(tile, size=TILE):
    return aligned(tile * size, size, size)


def only(values, half):
    return jnp.where(iota((1, 128), 1) // 64 == half, values, jnp.zeros_like(values))


def fetch(pairs, sems):
    copies = [
        pltpu.make_async_copy(source, target, sems.at[i]) for i, (source, target) in enumerate(pairs)
    ]
    for copy in copies:
        copy.start()
    return copies


def store_packed(put, first, place, value):
    offset, count, width = place
    value = value.reshape(-1, count, width)
    shards = slice(first, first + value.shape[0]) if isinstance(first, int) else pl.ds(first, value.shape[0])
    for piece in range(count // 16):
        put(shards, offset + piece * width, value[:, piece * 16 : piece * 16 + 16])
    if count % 16:
        half = width // 2
        rest = value[:, count - 8 :]
        rest = jnp.concatenate([rest[:, :, :half], rest[:, :, half:]], axis=1)
        put(shards, offset + count // 16 * width, rest)


def halves(shards, value):
    pairs = value.reshape(value.shape[0] // 2, 2, *value.shape[1:])
    if isinstance(shards, slice):
        return slice(shards.start // 2, shards.stop // 2), pairs[:, 0], pairs[:, 1]
    return pl.ds(shards.start // 2, shards.size // 2), pairs[:, 0], pairs[:, 1]


def place_of(names, bits):
    index = 0
    for name in names:
        index = index * 2 + bits[name]
    return index


def left_after(route, stage):
    return tuple(name for name in CANON if name not in route[:stage])


def choices(names):
    for number in range(2 ** len(names)):
        yield {name: (number >> (len(names) - 1 - i)) & 1 for i, name in enumerate(names)}


def neighbours():
    section = lax.axis_index("section")
    data = lax.axis_index("dp")
    mine = {"x": section, "c": data % 2, "y": data // 2 % 2, "z1": data // 4 % 2, "z2": data // 8 % 2}
    partner = {"x": (1 - section, data)}
    for name, step in {"c": 1, "y": 2, "z1": 4, "z2": 8}.items():
        partner[name] = (section, data + step * (1 - 2 * mine[name]))
    return mine, partner


def greet(partner):
    barrier = pltpu.get_barrier_semaphore()
    for name in ("c",) + CANON:
        pl.semaphore_signal(barrier, inc=1, device_id=partner[name], device_id_type=MESH_ID)


def await_greetings():
    pl.semaphore_wait(pltpu.get_barrier_semaphore(), 5)


def remote(source, target, send, recv, device):
    return pltpu.make_async_remote_copy(
        src_ref=source,
        dst_ref=target,
        send_sem=send,
        recv_sem=recv,
        device_id=device,
        device_id_type=MESH_ID,
    )


def reducer(plan, mine, partner, out, refs):
    chunks, slots, span, ring = plan.chunks, plan.slots, plan.span, plan.ring
    progress = types.SimpleNamespace(sent=0)
    own, staging, first = refs[:3]
    sent, got = refs[3:15], refs[15:27]
    first_send, first_recv, send_sem, recv_sem = refs[27:31]

    def first_copy(chunk):
        return remote(staging.at[chunk % slots], first.at[chunk], first_send.at[chunk], first_recv.at[chunk], partner["c"])

    def stage_copy(route, stage, chunk):
        return remote(
            sent[route * 4 + stage].at[chunk % ring],
            got[route * 4 + stage].at[chunk],
            send_sem.at[route, stage, chunk],
            recv_sem.at[route, stage, chunk],
            partner[ROUTES[route][stage]],
        )

    def total(route, stage, chunk, bits):
        spot = place_of(CANON, bits)
        cols = slice(sum(plan.widths[:route]) * 128, sum(plan.widths[: route + 1]) * 128)
        value = own[chunk, spot, :, cols].astype(F32) + first[chunk, spot, :, cols].astype(F32)
        for earlier in range(stage):
            names = left_after(ROUTES[route], earlier + 1)
            value = value + got[route * 4 + earlier][chunk, place_of(names, bits)].astype(F32)
        return value

    def advance(stage, chunk):
        for route in range(3):
            if stage:
                stage_copy(route, stage - 1, chunk).wait_recv()
            else:
                first_copy(chunk).wait_recv() if route == 0 else None
            if stage < 4:

                @pl.when(chunk >= ring)
                def _(route=route):
                    stage_copy(route, stage, chunk - ring).wait_send()

        values = []
        for route in range(3):
            path = ROUTES[route]
            if stage == 4:
                values.append(total(route, 4, chunk, mine))
                continue
            names = left_after(path, stage + 1)
            for free in choices(names):
                bits = dict(mine)
                bits[path[stage]] = 1 - mine[path[stage]]
                bits.update(free)
                values.append((route, place_of(names, free), low(total(route, stage, chunk, bits))))
        if stage == 4:
            out[chunk] = jnp.concatenate(values, axis=1)
            return
        for route, spot, value in values:
            sent[route * 4 + stage][chunk % ring, spot] = value
        for route in range(3):
            stage_copy(route, stage, chunk).start()

    def turn(number):
        for stage in range(4, -1, -1):
            chunk = number - STARTS[stage]
            pl.when((chunk >= 0) & (chunk < chunks))(functools.partial(advance, stage, chunk))

    def put(shards, column, value):
        shards, even, odd = halves(shards, value)
        kept = low(jnp.where(mine["c"] == 0, even, odd))
        given = low(jnp.where(mine["c"] == 0, odd, even))
        width = value.shape[2]
        done = 0
        while done < width:
            chunk, start = divmod(column + done, span)
            size = min(width - done, span - start)
            own[chunk, shards, :, start : start + size] = kept[:, :, done : done + size]
            staging[chunk % slots, shards, :, start : start + size] = given[:, :, done : done + size]
            done += size

    def put_unit(unit):
        def put(shards, column, value):
            shards, even, odd = halves(shards, value)
            cols = slice(column, column + value.shape[2])
            own[unit, shards, :, cols] = low(jnp.where(mine["c"] == 0, even, odd))
            staging[unit % slots, shards, :, cols] = low(jnp.where(mine["c"] == 0, odd, even))

        @pl.when(unit >= slots)
        def _():
            first_copy(unit - slots).wait_send()

        return put

    def send(column):
        while (progress.sent + 1) * span <= column:
            first_copy(progress.sent).start()
            progress.sent += 1

    def close():
        for chunk in range(max(0, chunks - slots), chunks):
            first_copy(chunk).wait_send()
        for chunk in range(chunks - ring, chunks):
            for route in range(3):
                for stage in range(4):
                    stage_copy(route, stage, chunk).wait_send()

    return types.SimpleNamespace(
        own=own, staging=staging, turn=turn, put=put, put_unit=put_unit, first_copy=first_copy, send=send, close=close
    )


def reducer_scratch(plan):
    stages = [(width, block) for width in plan.widths for block in (8, 4, 2, 1)]
    return (
        [
            pltpu.VMEM((plan.chunks, 16, 16, plan.span), BF16),
            pltpu.VMEM((plan.slots, 16, 16, plan.span), BF16),
            pltpu.VMEM((plan.chunks, 16, 16, plan.span), BF16),
        ]
        + [pltpu.VMEM((plan.ring, block, 16, width * 128), BF16) for width, block in stages]
        + [pltpu.VMEM((plan.chunks, block, 16, width * 128), BF16) for width, block in stages]
        + [
            pltpu.SemaphoreType.DMA((plan.chunks,)),
            pltpu.SemaphoreType.DMA((plan.chunks,)),
            pltpu.SemaphoreType.DMA((3, 4, plan.chunks)),
            pltpu.SemaphoreType.DMA((3, 4, plan.chunks)),
        ]
    )


def put_into(parts):
    span = parts.shape[-1]

    def put(shards, column, value):
        shards, *pair = halves(shards, value)
        width = value.shape[2]
        done = 0
        while done < width:
            chunk, start = divmod(column + done, span)
            size = min(width - done, span - start)
            for core in range(2):
                parts[chunk, core, shards, :, start : start + size] = low(pair[core][:, :, done : done + size])
            done += size

    return put


def put_unit_into(parts, unit):
    def put(shards, column, value):
        shards, *pair = halves(shards, value)
        for core in range(2):
            parts[unit, core, shards, :, column : column + value.shape[2]] = low(pair[core])

    return put


def vmem_spec():
    return pl.BlockSpec(memory_space=pltpu.VMEM)


def any_spec():
    return pl.BlockSpec(memory_space=pl.ANY)


def smem_spec():
    return pl.BlockSpec(memory_space=pltpu.SMEM)


def encoder_forward_kernel(
    sizes, distance, frequency, gains, shifts, biases, inner, tokens, attend_far, merging_far, expand_far,
    shrink_far, sent, vectors, table, *refs,
):
    far = refs[:9]
    normed, mixed, turned, probs, context, middle, normed_two, active, slope = refs[9:18]
    hidden, attend, merging, expand, shrink, context_turned, load_sem, save_sem = refs[18:]
    pack = lax.axis_index("section")
    loads = fetch(
        [
            (tokens.at[pack], hidden),
            *[(attend_far.at[:, i * 768 : i * 768 + 768], attend.at[:, i * 768 : i * 768 + 768]) for i in range(3)],
            (merging_far, merging),
            *[(expand_far.at[:, i * 1024 : i * 1024 + 1024], expand.at[:, i * 1024 : i * 1024 + 1024]) for i in range(3)],
            *[(shrink_far.at[i * 1024 : i * 1024 + 1024], shrink.at[i * 1024 : i * 1024 + 1024]) for i in range(3)],
        ],
        load_sem,
    )
    saves = []

    def save(*numbers):
        for number in numbers:
            copy = pltpu.make_async_copy(refs[9 + number], far[number], save_sem.at[number])
            copy.start()
            saves.append(copy)

    vectors[...] = jnp.zeros_like(vectors)
    positions = iota((32, 128), 0).astype(F32)
    for chip in range(4):
        spacing = distance[pack, chip].astype(F32) / 16.0
        angle = positions * (spacing * frequency[...])
        table[0, chip] = jnp.sin(angle)
        table[1, chip] = jnp.cos(angle)
    key_chip = chip_of(4 * iota((TILE, 1), 0), sizes, pack)
    own_chip = chip_of(4 * iota((1, TILE), 1), sizes, pack)
    valid = (key_chip < 4).astype(F32)
    loads[0].wait()
    values = hidden[...]
    vectors[10:11, :768] = row_sum(valid * values * values)
    unit, _ = standardize(values)
    norm = low(unit * gains[0:1] + shifts[0:1])
    normed[...] = norm
    for part in range(3):
        cols = slice(part * 768, part * 768 + 768)
        loads[1 + part].wait()
        mix = dot(norm, attend[:, cols])
        mixed[:, cols] = low(mix)
        if part:
            turned[(part - 1) * 768 : part * 768] = low(mix.T)
    save(0, 1, 2)

    def score(head):
        pair, half = divmod(head, 2)
        query = only(mixed[:, pair_lanes(pair)], half) * BF16(0.125)
        return dot_nt(mixed[:, pair_lanes(pair, 768)], query)

    ready = [score(0), score(1)]
    for head in range(12):
        if head + 2 < 12:
            ready.append(score(head + 2))
        scores = jnp.where(key_chip == own_chip, ready[head], NEGATIVE)
        expos = jnp.exp(scores - jnp.max(scores, axis=0, keepdims=True))
        prob = low(expos * (1.0 / jnp.sum(expos, axis=0, keepdims=True)))
        probs[head] = prob
        context_turned[head * 64 : head * 64 + 64] = dot(turned[768 + head * 64 : 832 + head * 64], prob)

    mingled = low(context_turned[...].T)
    context[...] = mingled
    save(3, 4)
    loads[4].wait()
    attention = dot(mingled, merging[...]) + biases[0:1]
    vectors[11:12, :768] = row_sum(valid * attention * attention)
    center = hidden[...] + attention
    middle[...] = center
    unit, _ = standardize(center)
    norm = low(unit * gains[1:2] + shifts[1:2])
    normed_two[...] = norm
    save(5, 6)
    feed = jnp.zeros_like(center)
    def widened(part):
        if part % 2 == 0:
            loads[5 + part // 2].wait()
        cols = slice(part * 512, part * 512 + 512)
        return dot(norm, expand[:, cols]) + inner[:, cols]

    ready = [widened(0)]
    for part in range(6):
        if part < 5:
            ready.append(widened(part + 1))
        cols = slice(part * 512, part * 512 + 512)
        value, slant = gelu_pair(ready[part])
        value = low(value)
        active[:, cols] = value
        slope[part // 2, :, part % 2 * 512 : part % 2 * 512 + 512] = slant
        if part % 2 == 0:
            loads[8 + part // 2].wait()
        feed = feed + dot(value, shrink[cols])
    save(7, 8)
    feed = feed + biases[1:2]
    vectors[12:13, :768] = row_sum(valid * feed * feed)
    output = center + feed
    vectors[13:14, :768] = row_sum(valid * output * output)
    vectors[14:15, :768] = jnp.broadcast_to(row_sum(valid), (1, 768))
    sent[...] = low(output)
    for copy in saves:
        copy.wait()


def encoder_forward_call(sizes, distance, tokens, gains, shifts, biases, attend, merging, expand, inner, shrink):
    frequency = np.exp(-np.log(10000.0) * np.arange(DD // 4) / (DD // 4)).astype(np.float32)
    shapes = (
        ((256, 768), BF16),
        ((256, 2304), BF16),
        ((1536, 256), BF16),
        ((12, 256, 256), BF16),
        ((256, 768), BF16),
        ((256, 768), F32),
        ((256, 768), BF16),
        ((256, 3072), BF16),
        ((3, 256, 1024), F32),
    )
    return pl.pallas_call(
        encoder_forward_kernel,
        out_shape=(
            jax.ShapeDtypeStruct((256, 768), BF16),
            jax.ShapeDtypeStruct((16, 1024), F32),
            jax.ShapeDtypeStruct((2, 4, 32, 128), F32),
        )
        + tuple(jax.ShapeDtypeStruct(*shape) for shape in shapes),
        in_specs=[smem_spec()] * 2 + [vmem_spec()] * 5 + [any_spec()] * 5,
        out_specs=(vmem_spec(),) * 3 + (any_spec(),) * len(shapes),
        scratch_shapes=[pltpu.VMEM(*shape) for shape in shapes]
        + [
            pltpu.VMEM((256, 768), F32),
            pltpu.VMEM(attend.shape, BF16),
            pltpu.VMEM(merging.shape, BF16),
            pltpu.VMEM(expand.shape, BF16),
            pltpu.VMEM(shrink.shape, BF16),
            pltpu.VMEM((768, 256), F32),
            pltpu.SemaphoreType.DMA((11,)),
            pltpu.SemaphoreType.DMA((len(shapes),)),
        ],
        compiler_params=pltpu.CompilerParams(vmem_limit_bytes=60 * 2**20),
        name="encoder_forward",
    )(
        sizes, distance, jnp.asarray(frequency)[None], gains, shifts, biases, inner[None], tokens, attend, merging,
        expand, shrink,
    )


def decoder_kernel(
    reduce, sizes, slots, table, sent, biases, mask_token, gains, shifts, inner,
    cotangent, entry_far, attend_far, merging_far, expand_far, shrink_far,
    summed, rest, vectors, encoded_grad, *refs,
):
    (
        start, normed, mixed, turned, probs, flipped, context, normed_two, active,
        before_grad, go_low, attention_low, context_grad, delta, mixed_grad, target, masked_keys,
        entry_weight, attend, merging, expand, shrink, load_sem,
    ) = refs[:23]
    pack = lax.axis_index("section")
    if reduce:
        mine, partner = neighbours()
        greet(partner)
        engine = reducer(DECODER_PLAN, mine, partner, summed, refs[23:])
        put = engine.put
    else:
        put = put_into(summed)
    put_rest = put_into(rest)
    loads = fetch(
        [
            (entry_far, entry_weight),
            (attend_far, attend),
            (cotangent.at[pack], target),
            (merging_far, merging),
            (expand_far, expand),
            (shrink_far, shrink),
        ],
        load_sem,
    )
    tiles = start.shape[0] // TILE
    vectors[...] = jnp.zeros_like(vectors)
    large = sizes[pack, 0] == 1024

    def add_row(row, value):
        vectors[row : row + 1, :] += value

    loads[0].wait()
    entry = low(dot(sent[...], entry_weight[...]) + biases[0:1])
    loads[1].wait()

    blocks = start.shape[0] // BLOCK

    def slot_chip(tile, size):
        return chip_of(iota((size, 1), 0) + tile * size, sizes, pack)

    def validity(tile, size):
        return (slot_chip(tile, size) < 4).astype(F32)

    def spread_of(tile):
        return (slots[pl.ds(pack, 1)] == iota((TILE, TILE), 0) + tile * TILE).astype(F32)

    def encoding_of(tile):
        pieces = []
        for kind in range(2):
            wave = table[kind, 0, aligned(tile * 8, 8, 8)]
            big = jnp.broadcast_to(wave[:, None], (8, 32, 128)).reshape(TILE, 128)
            wave = table[kind, tile, 0:16]
            own = jnp.broadcast_to(wave[:, None], (16, 16, 128)).reshape(TILE, 128)
            pieces.append(jnp.where(large, big, own))
        for kind in range(2):
            wave = table[kind, 0]
            big = jnp.broadcast_to(wave[None], (8, 32, 128)).reshape(TILE, 128)
            wave = table[kind, tile, 0:16]
            own = jnp.broadcast_to(wave[None], (16, 16, 128)).reshape(TILE, 128)
            pieces.append(jnp.where(large, big, own))
        return jnp.concatenate(pieces, axis=1)

    @pl.loop(0, tiles)
    def _(tile):
        rows = rows_of(tile)
        valid = validity(tile, TILE)
        spread = spread_of(tile)
        fill = valid * (1.0 - jnp.sum(spread, axis=1, keepdims=True))
        hidden = dot(low(spread), entry) + fill * mask_token[...] + encoding_of(tile) * valid
        start[rows] = hidden
        add_row(12, row_sum(valid * hidden * hidden))
        add_row(16, row_sum(valid))
        unit, _ = standardize(hidden)
        norm = low(unit * gains[0:1] + shifts[0:1])
        normed[rows] = norm
        mix = dot(norm, attend[...])
        mix_low = low(mix)
        mixed[rows] = mix_low
        turned[:, rows] = low(mix[:, 256:].T)
        lane = iota((TILE, 128), 1)
        other = (lane % 64 < 5) & (lane % 64 != slot_chip(tile, TILE))
        other = jnp.where(other, NEGATIVE, 0.0).astype(BF16)
        for head in range(4):
            lanes = slice(256 + head // 2 * 128, 384 + head // 2 * 128)
            masked_keys[head, rows] = jnp.where(lane // 64 == head % 2, mix_low[:, lanes], other)

    @pl.loop(0, 2 * tiles)
    def _(step):
        pair, tile = step // tiles, step % tiles
        rows = rows_of(tile)
        lane = iota((TILE, 128), 1)
        chosen = (lane % 64 == slot_chip(tile, TILE)).astype(F32).astype(BF16)
        for half in range(2):
            query = jnp.where(lane // 64 == half, mixed[rows, pair_lanes(pair)] * BF16(0.125), chosen)
            scores = dot_nt(masked_keys[pair * 2 + half], query)
            expos = jnp.exp(scores - jnp.max(scores, axis=0, keepdims=True))
            prob = low(expos * (1.0 / jnp.sum(expos, axis=0, keepdims=True)))
            probs[pair * 2 + half, :, rows] = prob
            flipped[head_rows(pair, half), rows] = dot(turned[head_rows(pair, half, 256)], prob)

    for copy in loads[2:]:
        copy.wait()

    @pl.loop(0, blocks)
    def _(tile):
        rows = rows_of(tile, BLOCK)
        valid = validity(tile, BLOCK)
        mingled = low(flipped[:, rows].T)
        context[rows] = mingled
        attention = dot(mingled, merging[...]) + biases[1:2]
        add_row(13, row_sum(valid * attention * attention))
        unit, _ = standardize(start[rows] + attention)
        norm = low(unit * gains[1:2] + shifts[1:2])
        normed_two[rows] = norm
        go = target[rows] * valid
        go_below = low(go)
        go_low[rows] = go_below
        add_row(2, row_sum(go))
        for part in range(8):
            cols = slice(part * 256, part * 256 + 256)
            value, slope = gelu_pair(dot(norm, expand[:, cols]) + inner[:, cols])
            active[rows, cols] = low(value)
            grad = low(slope * dot_nt(go_below, shrink[cols]))
            before_grad[rows, cols] = grad
            lanes = slice(part % 2 * 256, part % 2 * 256 + 256)
            vectors[8 + part // 2 : 9 + part // 2, lanes] += row_sum(grad.astype(F32))

    if reduce:
        await_greetings()
    for part in range(2):
        cols = slice(part * 256, part * 256 + 256)
        store_packed(put, part * 16, DECODER_EXPAND, dot_tn(normed_two[:, cols], before_grad[...]))
    if reduce:
        engine.send(2048)

    @pl.loop(0, 8)
    def _(part):
        cols = aligned(part * 256, 256, 256)
        store_packed(put, part * 4, DECODER_SHRINK, dot_tn(active[:, cols], go_low[...]))

    if reduce:
        engine.send(4096)

    @pl.loop(0, tiles)
    def _(tile):
        rows = rows_of(tile)
        valid = validity(tile, TILE)
        center = start[rows] + (dot(context[rows], merging[...]) + biases[1:2])
        unit, inverse = standardize(center)
        feed = dot(active[rows], shrink[...]) + biases[2:3]
        add_row(14, row_sum(valid * feed * feed))
        output = center + feed
        add_row(15, row_sum(valid * output * output))
        norm_grad = dot_nt(before_grad[rows], expand[...])
        add_row(5, row_sum(norm_grad * unit))
        add_row(7, row_sum(norm_grad))
        grad = target[rows] * valid + norm_back(unit, inverse, gains[1:2], norm_grad)
        target[rows] = grad
        add_row(1, row_sum(grad))
        below = low(grad)
        attention_low[rows] = below
        outer = low(dot_nt(below, merging[...]))
        context_grad[rows] = outer
        product = (outer.astype(F32) * flipped[:, rows].T).T
        for head in range(4):
            delta[head, :, rows] = row_sum(product[head * 64 : head * 64 + 64])
        if reduce:
            engine.turn(tile)

    for part in range(2):
        cols = slice(part * 256, part * 256 + 256)
        store_packed(put, part * 16, DECODER_MERGE, dot_tn(attention_low[:, cols], context[...]))
        shards = slice(part * 16, part * 16 + 16)
        put(shards, 4352, jnp.zeros((16, 16, DECODER_PLAN.chunks * DECODER_PLAN.span - 4352), F32))
    if reduce:
        engine.send(DECODER_PLAN.chunks * DECODER_PLAN.span)

    flipped[...] = jnp.zeros_like(flipped)

    @pl.loop(0, 2 * tiles)
    def _(step):
        pair, tile = step // tiles, step % tiles
        rows = rows_of(tile)
        lanes = pair_lanes(pair)
        values = mixed[rows, pair_lanes(pair, 512)]
        raws, probabilities, queries, outers = [], [], [], []
        for half in range(2):
            prob = probs[pair * 2 + half, rows]
            outer = only(context_grad[:, lanes], half)
            raw = low(prob.astype(F32) * (dot_nt(values, outer) - delta[pair * 2 + half]))
            flipped[head_rows(pair, half)] += dot(turned[head_rows(pair, half), rows], raw)
            raws.append(raw)
            probabilities.append(prob)
            outers.append(outer)
            queries.append(only(mixed[:, lanes], half))
        key_grad = dot(jnp.concatenate(raws, axis=1), jnp.concatenate(queries, axis=0))
        mixed_grad[rows, pair_lanes(pair, 256)] = low(key_grad * 0.125)
        value_grad = dot(jnp.concatenate(probabilities, axis=1), jnp.concatenate(outers, axis=0))
        mixed_grad[rows, pair_lanes(pair, 512)] = low(value_grad)
        if reduce:
            engine.turn(tiles + step)

    def last(tile, entry_grad):
        rows = rows_of(tile)
        mixed_grad[rows, 0:256] = low(flipped[:, rows].T * 0.125)
        norm_grad = dot_nt(mixed_grad[rows], attend[...])
        unit, inverse = standardize(start[rows])
        add_row(4, row_sum(norm_grad * unit))
        add_row(6, row_sum(norm_grad))
        grad = target[rows] + norm_back(unit, inverse, gains[0:1], norm_grad)
        spread = spread_of(tile)
        fill = validity(tile, TILE) * (1.0 - jnp.sum(spread, axis=1, keepdims=True))
        add_row(3, row_sum(fill * grad))
        if reduce:
            engine.turn(3 * tiles + tile)
        return entry_grad + dot_tn(low(spread), low(grad))

    entry_grad = lax.fori_loop(0, tiles, last, jnp.zeros((TILE, 512), F32))
    add_row(0, row_sum(entry_grad))
    entry_low = low(entry_grad)
    encoded_grad[...] = low(dot_nt(entry_low, entry_weight[...]))
    store_packed(put_rest, 0, ENTRY, dot_tn(sent[...], entry_low))

    @pl.loop(0, 2)
    def _(part):
        cols = aligned(part * 256, 256, 256)
        store_packed(put_rest, part * 16, DECODER_ATTEND, dot_tn(normed[:, cols], mixed_grad[...]))

    if reduce:
        engine.close()


def decoder_call(
    reduce, sizes, slots, table, sent, cotangent, entry_weight, biases, mask_token,
    gains, shifts, attend, merging, expand, inner, shrink,
):
    length = cotangent.shape[1]
    width = 512
    if reduce:
        summed = jax.ShapeDtypeStruct((DECODER_PLAN.chunks, 16, DECODER_PLAN.span), F32)
        extra = reducer_scratch(DECODER_PLAN)
        params = dict(collective_id=1, has_side_effects=True)
    else:
        summed = jax.ShapeDtypeStruct((DECODER_PLAN.chunks, 2, 16, 16, DECODER_PLAN.span), BF16)
        extra = []
        params = dict()
    return pl.pallas_call(
        functools.partial(decoder_kernel, reduce),
        out_shape=(
            summed,
            jax.ShapeDtypeStruct((1, 2, 16, 16, UNIT), BF16),
            jax.ShapeDtypeStruct((24, width), F32),
            jax.ShapeDtypeStruct((256, 768), BF16),
        ),
        in_specs=[smem_spec()] + [vmem_spec()] * 8 + [any_spec()] * 6,
        out_specs=(vmem_spec(),) * 4,
        scratch_shapes=[
            pltpu.VMEM((length, width), F32),
            pltpu.VMEM((length, width), BF16),
            pltpu.VMEM((length, 768), BF16),
            pltpu.VMEM((512, length), BF16),
            pltpu.VMEM((4, length, length), BF16),
            pltpu.VMEM((256, length), F32),
            pltpu.VMEM((length, 256), BF16),
            pltpu.VMEM((length, width), BF16),
            pltpu.VMEM((length, 2048), BF16),
            pltpu.VMEM((length, 2048), BF16),
            pltpu.VMEM((length, width), BF16),
            pltpu.VMEM((length, width), BF16),
            pltpu.VMEM((length, 256), BF16),
            pltpu.VMEM((4, 1, length), F32),
            pltpu.VMEM((length, 768), BF16),
            pltpu.VMEM((length, width), F32),
            pltpu.VMEM((4, length, 128), BF16),
            pltpu.VMEM(entry_weight.shape, BF16),
            pltpu.VMEM(attend.shape, BF16),
            pltpu.VMEM(merging.shape, BF16),
            pltpu.VMEM(expand.shape, BF16),
            pltpu.VMEM(shrink.shape, BF16),
            pltpu.SemaphoreType.DMA((6,)),
        ]
        + extra,
        compiler_params=pltpu.CompilerParams(vmem_limit_bytes=63 * 2**20, **params),
        name="decoder_block",
    )(
        sizes, slots, table, sent, biases, mask_token[None], gains, shifts,
        inner[None], cotangent, entry_weight, attend, merging, expand, shrink,
    )


def encoder_backward_kernel(
    reduce, encoded_grad, sums, decoder_vectors, gains, tokens, rest, attend_far, merging_far, expand_far,
    shrink_far, normed_far, mixed_far, turned_far, probs_far, context_far, middle_far, normed_two_far, active_far,
    slope_far, summed, tail_summed, vectors, tokens_grad, *refs,
):
    if reduce:
        decoder_sums, arrived = refs[:2]
        refs = refs[2:]
    (
        hidden, attend, merging, expand, shrink, normed, mixed, turned, probs, context, middle, normed_two, active,
        slope, before_grad, norm_sum, attention_low, context_grad, key_grad, query_turned, mixed_grad, active_turned,
        flipped, inner_sum, load_sem, part_sem,
    ) = refs[:26]
    pack = lax.axis_index("section")

    def part_loads(part):
        cols = aligned(part * 1024, 1024, 1024)
        slot = part % 2
        return [
            pltpu.make_async_copy(expand_far.at[:, cols], expand.at[slot], part_sem.at[slot, 0]),
            pltpu.make_async_copy(shrink_far.at[cols], shrink.at[slot], part_sem.at[slot, 1]),
            pltpu.make_async_copy(slope_far.at[part], slope.at[slot], part_sem.at[slot, 2]),
        ]

    if reduce:
        (
            decoder_total, encoder_total, decoder_got, encoder_got, payload,
            own_sem, small_send, small_recv, pay_send, pay_recv, small_load,
        ) = refs[26:37]
        mine, partner = neighbours()
        greet(partner)
        engine = reducer(ENCODER_PLAN, mine, partner, summed, refs[37:68])
        tail = reducer(TAIL_PLAN, mine, partner, tail_summed, refs[68:])
        put_tail = tail.put
        first_own = fetch(
            [
                pair
                for pair in (
                    (rest.at[0, 1 - mine["c"]], engine.staging.at[0]),
                    (rest.at[0, mine["c"]], engine.own.at[0]),
                )
            ],
            own_sem,
        )
        decoder_load = pltpu.make_async_copy(decoder_vectors, decoder_total.at[0], small_load)
        decoder_load.start()
    else:
        put_tail = put_into(tail_summed)
    early = pltpu.make_async_copy(active_far, active, load_sem.at[10])
    early.start()
    for copy in part_loads(0):
        copy.start()
    if reduce:
        for copy in first_own:
            copy.wait()
        await_greetings()
        engine.first_copy(0).start()
    loads = fetch(
        [
            (normed_two_far, normed_two),
            (middle_far, middle),
            (merging_far, merging),
            (context_far, context),
            (mixed_far, mixed),
            (probs_far, probs),
            (turned_far.at[0:768], turned),
            (normed_far, normed),
            (attend_far, attend),
            (tokens.at[pack], hidden),
        ],
        load_sem,
    )
    for copy in part_loads(1):
        copy.start()
    vectors[...] = sums[...]
    go_low = encoded_grad[...]
    go = go_low.astype(F32)
    vectors[1:2, :768] = row_sum(go)
    norm_sum[...] = jnp.zeros_like(norm_sum)

    def unit_grad(unit, place, pieces):
        put = engine.put_unit(unit) if reduce else put_unit_into(summed, unit)
        for first, value in pieces:
            store_packed(put, first, (0,) + place[1:], value)
        if reduce:
            engine.first_copy(unit).start()

    def shrink_start():
        early.wait()
        for piece in range(4):
            rows = slice(piece * 768, piece * 768 + 768)
            active_turned[rows] = active[:, rows].T

    def shrink_grad(part):
        cols = aligned(part * 256, 256, 256)
        pieces = []
        for piece in range(4):
            rows = slice(piece * 768, piece * 768 + 768)
            pieces.append((piece * 8, dot(active_turned[rows], encoded_grad[:, cols])))
        unit_grad(1 + part, ENCODER_SHRINK[0], pieces)

    def hidden_layer(part):
        for copy in part_loads(part):
            copy.wait()
        slot = part % 2
        grad = low(slope[slot] * dot_nt(encoded_grad[...], shrink[slot]))
        before_grad[...] = grad
        inner_sum[part] = row_sum(grad.astype(F32))
        norm_sum[...] += dot_nt(grad, expand[slot])

        @pl.when(part == 0)
        def _():
            for copy in part_loads(2):
                copy.start()

    def expand_grad(part):
        @pl.when(part == 0)
        def _():
            loads[0].wait()
            flipped[...] = normed_two[...].T

        unit_grad(4 + part, ENCODER_EXPAND[0], [(0, dot(flipped[...], before_grad[...]))])

    def middle_layer():
        loads[1].wait()
        loads[2].wait()
        for part in range(3):
            vectors[6 + part : 7 + part] = inner_sum[part]
        unit, inverse = standardize(middle[...])
        norm_grad = norm_sum[...]
        vectors[3:4, :768] = row_sum(norm_grad * unit)
        vectors[5:6, :768] = row_sum(norm_grad)
        grad = encoded_grad[...].astype(F32) + norm_back(unit, inverse, gains[1:2], norm_grad)
        vectors[0:1, :768] = row_sum(grad)
        tokens_grad[...] = grad
        below = low(grad)
        attention_low[...] = below
        context_grad[...] = low(dot_nt(below, merging[...]))
        for copy in loads[3:7]:
            copy.wait()

    def attention(first):
        @pl.loop(first, first + 2)
        def _(pair):
            lanes = pair_lanes(pair)
            values = mixed[:, pair_lanes(pair, 1536)]
            keys_total = jnp.zeros((TILE, 128), F32)
            values_total = jnp.zeros((TILE, 128), F32)
            for half in range(2):
                prob = probs[pair * 2 + half]
                outer = only(context_grad[:, lanes], half)
                query = only(mixed[:, lanes], half)
                wide = prob.astype(F32)
                grad = dot_nt(values, outer)
                raw = low(wide * (grad - jnp.sum(wide * grad, axis=0, keepdims=True)))
                keys_total = keys_total + dot(raw, query)
                values_total = values_total + dot(prob, outer)
                rows = head_rows(pair, half)
                query_turned[rows] = dot(turned[rows], raw)
            key_grad[0, :, lanes] = keys_total
            key_grad[1, :, lanes] = values_total

    def mixing():
        mixed_grad[:, 0:768] = low(query_turned[...].T * 0.125)
        mixed_grad[:, 768:1536] = low(key_grad[0] * 0.125)
        mixed_grad[:, 1536:2304] = low(key_grad[1])

    def attend_grad(part):
        @pl.when(part == 0)
        def _():
            loads[7].wait()
            flipped[...] = normed[...].T

        wide = aligned(part * 1024, 1024, 1024)
        unit_grad(7 + part, ENCODER_ATTEND[0], [(0, dot(flipped[...], mixed_grad[:, wide]))])

    def tail_grad():
        store_packed(put_tail, 0, ENCODER_ATTEND[2], dot(flipped[...], mixed_grad[:, 2048:2304]))
        store_packed(put_tail, 0, ENCODER_MERGE, dot_tn(attention_low[...], context[...]))
        if reduce:
            tail.send(UNIT)

    def input_layer():
        loads[8].wait()
        loads[9].wait()
        norm_grad = dot_nt(mixed_grad[...], attend[...])
        unit, inverse = standardize(hidden[...])
        vectors[2:3, :768] = row_sum(norm_grad * unit)
        vectors[4:5, :768] = row_sum(norm_grad)
        grad = tokens_grad[...] + norm_back(unit, inverse, gains[0:1], norm_grad)
        tokens_grad[...] = grad
        if reduce:
            payload[...] = low(grad)

    if not reduce:
        shrink_start()
        for part in range(3):
            shrink_grad(part)
        for part in range(3):
            hidden_layer(part)
            expand_grad(part)
        middle_layer()
        for first in (0, 2, 4):
            attention(first)
        mixing()
        for part in range(2):
            attend_grad(part)
        tail_grad()
        input_layer()
        return

    def exchange(source, piece):
        rows = aligned(piece * 32, 32, 32)
        return remote(source.at[rows], arrived.at[rows], pay_send.at[piece], pay_recv.at[piece], partner["x"])

    small_route = ("c",) + ROUTES[0]
    totals = ((decoder_total, decoder_got), (encoder_total, encoder_got))

    def small_copy(stage, kind):
        source, target = totals[kind]
        return remote(
            source.at[stage],
            target.at[stage],
            small_send.at[stage, kind],
            small_recv.at[stage, kind],
            partner[small_route[stage]],
        )

    def small_advance(stage):
        if stage == 0:
            encoder_total[0] = vectors[...]
        for kind in range(2):
            source, target = totals[kind]
            if stage > 0:
                small_copy(stage - 1, kind).wait_recv()
                source[stage] = source[stage - 1] + target[stage - 1]
            if stage < 5:
                small_copy(stage, kind).start()

    shrink_start()
    shrink_grad(0)
    decoder_load.wait()

    def attention_all():
        @pl.loop(0, 3)
        def _(step):
            attention(2 * step)

        mixing()

    def ending():
        tail_grad()
        input_layer()

    part = functools.partial
    works = {4: middle_layer, 5: attention_all, 7: ending}
    turns = ENCODER_PLAN.chunks + TAIL_PLAN.chunks + STARTS[4]
    works.update({8 + stage + max(0, stage - 2): part(small_advance, stage) for stage in range(6)})

    @pl.loop(0, turns)
    def _(number):
        engine.turn(number)
        tail.turn(number - ENCODER_PLAN.chunks)

        @pl.when(number <= 1)
        def _():
            shrink_grad(number + 1)

        @pl.when((number >= 2) & (number <= 4))
        def _():
            expand_grad(number - 2)

        @pl.when((number >= 1) & (number <= 3))
        def _():
            hidden_layer(number - 1)

        for position, work in works.items():
            pl.when(number == position)(work)

        @pl.when(number == 6)
        def _():
            @pl.loop(0, 2)
            def _(part):
                attend_grad(part)

        @pl.when((pack == 0) & (number < 8))
        def _():
            exchange(encoded_grad, number).start()

        @pl.when((pack == 1) & (number >= 8) & (number < 16))
        def _():
            exchange(payload, number - 8).start()

    for stage in range(5):
        for kind in range(2):
            small_copy(stage, kind).wait_send()
    for piece in range(8):
        exchange(payload, piece).wait()
    engine.close()
    tail.close()
    vectors[...] = encoder_total[5]
    decoder_sums[...] = decoder_total[5]


def encoder_backward_call(reduce, tokens, encoded_grad, sums, decoder_vectors, rest, kept, gains, attend, merging, expand, shrink):
    if reduce:
        summed = tuple(
            jax.ShapeDtypeStruct((plan.chunks, 16, plan.span), F32) for plan in (ENCODER_PLAN, TAIL_PLAN)
        )
        more = (
            jax.ShapeDtypeStruct(decoder_vectors.shape, F32),
            jax.ShapeDtypeStruct((256, 768), BF16),
        )
        more_specs = (vmem_spec(), any_spec())
        extra = [
            pltpu.VMEM((6,) + decoder_vectors.shape, F32),
            pltpu.VMEM((6,) + sums.shape, F32),
            pltpu.VMEM((5,) + decoder_vectors.shape, F32),
            pltpu.VMEM((5,) + sums.shape, F32),
            pltpu.VMEM((256, 768), BF16),
            pltpu.SemaphoreType.DMA((2,)),
            pltpu.SemaphoreType.DMA((5, 2)),
            pltpu.SemaphoreType.DMA((5, 2)),
            pltpu.SemaphoreType.DMA((8,)),
            pltpu.SemaphoreType.DMA((8,)),
            pltpu.SemaphoreType.DMA,
        ] + reducer_scratch(ENCODER_PLAN) + reducer_scratch(TAIL_PLAN)
        params = dict(collective_id=2, has_side_effects=True)
    else:
        summed = tuple(
            jax.ShapeDtypeStruct((plan.chunks, 2, 16, 16, plan.span), BF16) for plan in (ENCODER_PLAN, TAIL_PLAN)
        )
        more, more_specs, extra, params = (), (), [], dict()
    return pl.pallas_call(
        functools.partial(encoder_backward_kernel, reduce),
        out_shape=summed
        + (
            jax.ShapeDtypeStruct(sums.shape, F32),
            jax.ShapeDtypeStruct((256, 768), F32),
        )
        + more,
        in_specs=[vmem_spec()] * 2 + [any_spec(), vmem_spec()] + [any_spec()] * 15,
        out_specs=(vmem_spec(),) * 4 + more_specs,
        scratch_shapes=[
            pltpu.VMEM((256, 768), F32),
            pltpu.VMEM(attend.shape, BF16),
            pltpu.VMEM(merging.shape, BF16),
            pltpu.VMEM((2, 768, 1024), BF16),
            pltpu.VMEM((2, 1024, 768), BF16),
            pltpu.VMEM((256, 768), BF16),
            pltpu.VMEM((256, 2304), BF16),
            pltpu.VMEM((768, 256), BF16),
            pltpu.VMEM((12, 256, 256), BF16),
            pltpu.VMEM((256, 768), BF16),
            pltpu.VMEM((256, 768), F32),
            pltpu.VMEM((256, 768), BF16),
            pltpu.VMEM((256, 3072), BF16),
            pltpu.VMEM((2, 256, 1024), F32),
            pltpu.VMEM((256, 1024), BF16),
            pltpu.VMEM((256, 768), F32),
            pltpu.VMEM((256, 768), BF16),
            pltpu.VMEM((256, 768), BF16),
            pltpu.VMEM((2, 256, 768), F32),
            pltpu.VMEM((768, 256), F32),
            pltpu.VMEM((256, 2304), BF16),
            pltpu.VMEM((3072, 256), BF16),
            pltpu.VMEM((768, 256), BF16),
            pltpu.VMEM((3, 1, 1024), F32),
            pltpu.SemaphoreType.DMA((11,)),
            pltpu.SemaphoreType.DMA((2, 3)),
        ]
        + extra,
        compiler_params=pltpu.CompilerParams(vmem_limit_bytes=62 * 2**20, **params),
        name="encoder_backward",
    )(encoded_grad, sums, decoder_vectors, gains, tokens, rest, attend, merging, expand, shrink, *kept)


def unpack(packed, place):
    span = packed.shape[-1]

    def take(start, size):
        pieces = []
        while size:
            chunk, first = divmod(start, span)
            length = min(size, span - first)
            pieces.append(packed[chunk, ..., first : first + length])
            start, size = start + length, size - length
        return pieces[0] if len(pieces) == 1 else jnp.concatenate(pieces, axis=-1)

    offset, count, width = place
    pieces = [take(offset + i * width, width) for i in range(count // 16)]
    if count % 16:
        rest = take(offset + count // 16 * width, width // 2)
        pieces.append(jnp.concatenate([rest[..., :8, :], rest[..., 8:, :]], axis=-1))
    return pieces[0] if len(pieces) == 1 else jnp.concatenate(pieces, axis=-2)


def finish_kernel(
    decoder_summed_far, decoder_sums_far, encoder_sums_far, summed_far, tail_far, arrived_far, tokens_grad_far, encoded_grad_far,
    boundary, statistics, e_gains, e_shifts, e_biases, e_attend, e_merge, e_expand, e_inner, e_shrink,
    d_entry, d_biases, mask_grad, d_gains, d_shifts, d_attend, d_merge, d_expand, d_inner, d_shrink,
    decoder_summed, decoder_sums, encoder_sums, summed, tail, arrived, tokens_grad, encoded_grad, load_sem,
):
    section = lax.axis_index("section")
    loads = fetch(
        [
            (decoder_summed_far, decoder_summed),
            (decoder_sums_far, decoder_sums),
            (encoder_sums_far, encoder_sums),
            (summed_far, summed),
            (tail_far, tail),
            (arrived_far, arrived),
            (tokens_grad_far, tokens_grad),
            (encoded_grad_far, encoded_grad),
        ],
        load_sem,
    )
    number = section * lax.axis_size("dp") + lax.axis_index("dp")

    def own(rows, count):
        width = rows.shape[1]
        return pltpu.roll(rows, (width - number * count) % width, axis=1)[:, :count]

    def own_line(rows, count):
        return own(jnp.concatenate([rows[i : i + 1] for i in range(rows.shape[0])], axis=1), count)

    for copy in loads[:3]:
        copy.wait()
    lane = iota((1, 128), 1)
    values = jnp.zeros((1, 128), F32)
    for sums, width, first, count_row, base in ((encoder_sums, DE, 10, 14, 0), (decoder_sums, DD, 12, 16, 4)):
        scale = 1.0 / (sums[count_row : count_row + 1, 0:1] * width)
        for i in range(4):
            value = jnp.sum(sums[first + i : first + i + 1, :], axis=1, keepdims=True) * scale
            values = jnp.where(lane == base + i, value, values)
    statistics[...] = jnp.sqrt(values)[:, :8]
    rows = own(encoder_sums[0:8, :DE], 24)
    e_biases[...] = rows[0:2]
    e_gains[...] = rows[2:4]
    e_shifts[...] = rows[4:6]
    e_inner[...] = own_line(encoder_sums[6:9], 96)
    rows = own(decoder_sums[0:8], 16)
    d_biases[...] = rows[0:3]
    mask_grad[...] = rows[3:4]
    d_gains[...] = rows[4:6]
    d_shifts[...] = rows[6:8]
    d_inner[...] = own_line(decoder_sums[8:12], 64)

    d_merge[...] = unpack(decoder_summed, DECODER_MERGE)
    d_expand[...] = unpack(decoder_summed, DECODER_EXPAND)
    d_shrink[...] = unpack(decoder_summed, DECODER_SHRINK)
    loads[3].wait()
    loads[4].wait()
    d_entry[...] = unpack(summed, ENTRY)
    d_attend[...] = unpack(summed, DECODER_ATTEND)
    for target, places in ((e_expand, ENCODER_EXPAND), (e_attend, ENCODER_ATTEND), (e_shrink, ENCODER_SHRINK)):
        start = 0
        for place in places:
            source = tail if place is ENCODER_ATTEND[2] else summed
            target[:, start : start + place[2]] = unpack(source, place)
            start += place[2]
    e_merge[...] = unpack(tail, ENCODER_MERGE)
    for copy in loads[5:]:
        copy.wait()

    @pl.when(section == 0)
    def _():
        boundary[0, 0] = tokens_grad[...]
        boundary[0, 1] = arrived[...].astype(F32)

    @pl.when(section == 1)
    def _():
        boundary[0, 0] = arrived[...].astype(F32)
        boundary[0, 1] = encoded_grad[...].astype(F32)


def finish_call(*operands):
    shapes = (
        (1, 2, 256, 768), (1, 8), (2, 24), (2, 24), (2, 24), (24, 2304), (24, 768), (24, 3072), (1, 96), (96, 768),
        (24, 512), (3, 16), (1, 16), (2, 16), (2, 16), (16, 768), (16, 256), (16, 2048), (1, 64), (64, 512),
    )
    outs = list(
        pl.pallas_call(
            finish_kernel,
            out_shape=tuple(jax.ShapeDtypeStruct(shape, F32) for shape in shapes),
            in_specs=[any_spec()] * len(operands),
            out_specs=(vmem_spec(),) * len(shapes),
            scratch_shapes=[pltpu.VMEM(operand.shape, operand.dtype) for operand in operands]
            + [pltpu.SemaphoreType.DMA((len(operands),))],
            compiler_params=pltpu.CompilerParams(vmem_limit_bytes=60 * 2**20),
            name="finish",
        )(*operands)
    )
    for line in (1, 8, 12, 18):
        outs[line] = outs[line].reshape(-1)
    for turned in (6, 16):
        outs[turned] = outs[turned].T
    return tuple(outs)


def scatter_sum(member, share_dim):
    return lax.psum_scatter(
        member, ("section", "dp"), scatter_dimension=share_dim, tiled=True
    )


def finish_generic(decoder_part, part, tail, decoder_sums, encoder_sums, tokens_grad, encoded_grad):
    section = lax.axis_index("section")
    payload = jnp.where(section == 0, encoded_grad, low(tokens_grad))

    def whole(packed, *places):
        packed = jnp.swapaxes(packed, 1, 2).reshape(-1, 32, 16, packed.shape[-1])
        blocks = [unpack(packed, place).reshape(32 * place[1], place[2]) for place in places]
        return scatter_sum(jnp.concatenate(blocks, axis=1).astype(F32), 0)

    def line(value):
        return scatter_sum(value, value.ndim - 1)

    arrived = lax.ppermute(payload, "section", [(0, 1), (1, 0)]).astype(F32)
    boundary = jnp.where(
        section == 0,
        jnp.stack([tokens_grad, arrived]),
        jnp.stack([arrived, encoded_grad.astype(F32)]),
    )
    sums = jnp.concatenate(
        [jnp.sum(encoder_sums[10:14], axis=1), jnp.sum(decoder_sums[12:16], axis=1)]
    )
    sums, counts = lax.psum((sums, (encoder_sums[14, 0], decoder_sums[16, 0])), ("section", "dp"))
    scales = jnp.concatenate([jnp.full((4,), counts[0] * DE), jnp.full((4,), counts[1] * DD)])
    return (
        boundary[None],
        jnp.sqrt(sums / scales),
        line(encoder_sums[2:4, :DE]),
        line(encoder_sums[4:6, :DE]),
        line(encoder_sums[0:2, :DE]),
        jnp.concatenate([whole(part, *ENCODER_ATTEND[:2]), whole(tail, ENCODER_ATTEND[2])], axis=1),
        whole(tail, ENCODER_MERGE).T,
        whole(part, *ENCODER_EXPAND),
        line(encoder_sums[6:9].reshape(-1)),
        whole(part, *ENCODER_SHRINK),
        whole(decoder_part[1], ENTRY),
        line(decoder_sums[0:3]),
        line(decoder_sums[3]),
        line(decoder_sums[4:6]),
        line(decoder_sums[6:8]),
        whole(decoder_part[1], DECODER_ATTEND),
        whole(decoder_part[0], DECODER_MERGE).T,
        whole(decoder_part[0], DECODER_EXPAND),
        line(decoder_sums[8:12].reshape(-1)),
        whole(decoder_part[0], DECODER_SHRINK),
    )


def body(
    visible_tokens,
    cotangent,
    chip_sizes,
    ground_distance,
    visible_slots,
    encoder_gains,
    encoder_shifts,
    encoder_biases,
    encoder_attend,
    encoder_merge,
    encoder_expand,
    encoder_inner,
    encoder_shrink,
    decoder_entry,
    decoder_biases,
    mask_token,
    decoder_gains,
    decoder_shifts,
    decoder_attend,
    decoder_merge,
    decoder_widen_weight,
    decoder_inner,
    decoder_shrink,
):
    reduce = (lax.axis_size("section"), lax.axis_size("dp")) == (2, 16)
    sent, sums, table, *kept = encoder_forward_call(
        chip_sizes, ground_distance, visible_tokens, encoder_gains, encoder_shifts, encoder_biases,
        encoder_attend, encoder_merge, encoder_expand, encoder_inner, encoder_shrink,
    )
    decoder_summed, rest, decoder_vectors, encoded_grad = decoder_call(
        reduce, chip_sizes, visible_slots, table, sent, cotangent, decoder_entry, decoder_biases, mask_token,
        decoder_gains, decoder_shifts, decoder_attend, decoder_merge, decoder_widen_weight, decoder_inner,
        decoder_shrink,
    )
    summed, tail, encoder_sums, tokens_grad, *more = encoder_backward_call(
        reduce, visible_tokens, encoded_grad, sums, decoder_vectors, rest, kept,
        encoder_gains, encoder_attend, encoder_merge, encoder_expand, encoder_shrink,
    )
    if reduce:
        decoder_sums, arrived = more
        return finish_call(
            decoder_summed, decoder_sums, encoder_sums, summed, tail, arrived, tokens_grad, encoded_grad
        )
    return finish_generic(
        (decoder_summed, rest), summed, tail, decoder_vectors, encoder_sums, tokens_grad, encoded_grad
    )


def solution(mesh):
    in_specs = (
        P("dp", None, None),
        P("dp", None, None),
        P("dp", None),
        P("dp", None),
        P("dp", None),
        P(),
        P(),
        P(),
        P(),
        P(),
        P(),
        P(),
        P(),
        P(),
        P(),
        P(),
        P(),
        P(),
        P(),
        P(),
        P(),
        P(),
        P(),
    )
    out_specs = (
        P("section", "dp", None, None),
        P(),
        P(None, ("section", "dp")),
        P(None, ("section", "dp")),
        P(None, ("section", "dp")),
        P(("section", "dp"), None),
        P(None, ("section", "dp")),
        P(("section", "dp"), None),
        P(("section", "dp")),
        P(("section", "dp"), None),
        P(("section", "dp"), None),
        P(None, ("section", "dp")),
        P(("section", "dp")),
        P(None, ("section", "dp")),
        P(None, ("section", "dp")),
        P(("section", "dp"), None),
        P(None, ("section", "dp")),
        P(("section", "dp"), None),
        P(("section", "dp")),
        P(("section", "dp"), None),
    )
    return jax.shard_map(body, mesh=mesh, in_specs=in_specs, out_specs=out_specs, check_vma=False)
```
